32 devices in a mesh: ctx: 8 (over z, x), fsdp: 4 (over y, core).
Axes of the slice: x: 2, y: 2, z: 4, core: 2. Of those that a mesh axis runs over, the one named last changes fastest.
Arguments:
- hidden_in: bfloat16 [4, 1024, 2048], P('fsdp', 'ctx'), may hold values from -6 to 6
- block_of: int32 [4, 16], P('fsdp', 'ctx'), may hold values from 0 to 15, as said below
- in_gain: bfloat16 [2048], P(('ctx', 'fsdp')), may hold values from 0.25 to 1.75
- w_query: bfloat16 [2048, 2048], P(('ctx', 'fsdp')), may hold values from -0.125 to 0.125
- w_key: bfloat16 [2048, 1024], P(('ctx', 'fsdp')), may hold values from -0.125 to 0.125
- w_value: bfloat16 [2048, 1024], P(('ctx', 'fsdp')), may hold values from -0.125 to 0.125
- w_output: bfloat16 [2048, 2048], P(('ctx', 'fsdp')), may hold values from -2 to 2
- q_gain: bfloat16 [128], replicated, may hold values from 0.25 to 1.75
- k_gain: bfloat16 [128], replicated, may hold values from 0.25 to 1.75
- post_gain: bfloat16 [2048], P(('ctx', 'fsdp')), may hold values from 0.25 to 1.75
- w_gate: bfloat16 [2048, 6144], P(('ctx', 'fsdp')), may hold values from -0.125 to 0.125
- w_up: bfloat16 [2048, 6144], P(('ctx', 'fsdp')), may hold values from -0.125 to 0.125
- w_down: bfloat16 [6144, 2048], P(('ctx', 'fsdp')), may hold values from -0.078125 to 0.078125
- cotangent: bfloat16 [4, 1024, 2048], P('fsdp', 'ctx'), may hold values from -6 to 6
Outputs:
- out_hidden: bfloat16 [4, 1024, 2048], P('fsdp', 'ctx')
- grad_hidden_in: float32 [4, 1024, 2048], P('fsdp', 'ctx')
- grad_in_gain: float32 [2048], P(('ctx', 'fsdp'))
- grad_w_query: float32 [2048, 2048], P(('ctx', 'fsdp'))
- grad_w_key: float32 [2048, 1024], P(('ctx', 'fsdp'))
- grad_w_value: float32 [2048, 1024], P(('ctx', 'fsdp'))
- grad_w_output: float32 [2048, 2048], P(('ctx', 'fsdp'))
- grad_q_gain: float32 [128], replicated
- grad_k_gain: float32 [128], replicated
- grad_post_gain: float32 [2048], P(('ctx', 'fsdp'))
- grad_w_gate: float32 [2048, 6144], P(('ctx', 'fsdp'))
- grad_w_up: float32 [2048, 6144], P(('ctx', 'fsdp'))
- grad_w_down: float32 [6144, 2048], P(('ctx', 'fsdp'))
The draws below stay inside these ranges and needn't reach their ends.
Inputs may be any that keep to these rules, and one draw needn't show every extreme that they name: `block_of`: each row is a permutation of the blocks of its sequence in which slots 2c and 2c + 1 hold a mirrored pair b and 15 - b.
All inputs are finite; a program needn't handle non-finite values.
Results may differ from the reference program's by a relative error of at most 0.019.
Values may be sent and summed in bfloat16 or wider, within the bound.
A program may use at most 512 MiB of HBM per device.

```python
import jax
import jax.numpy as jnp
from jax import lax

D = 2048
QH = 16
KVH = 8
HD = 128
FF = 6144
BLK = 64
BLOCKS = 16
LEN = 1024
SEQS = 4


def draw_block_of(key, part):
    key = jax.random.fold_in(key, 7)
    keys_all = jax.random.split(key, SEQS + 1)
    orders = jax.vmap(lambda single: jax.random.permutation(single, BLOCKS // 2))(keys_all[:SEQS])
    flips = jax.random.randint(keys_all[SEQS], (SEQS, BLOCKS // 2), 0, 2)
    mirror = BLOCKS - 1 - orders
    first = jnp.where(flips == 1, mirror, orders)
    second = jnp.where(flips == 1, orders, mirror)
    return jnp.stack([first, second], axis=-1).reshape(SEQS, BLOCKS).astype(jnp.int32)


def raised(values, stream_key, source, target, shards_of, factor):
    def block_of(axis_at):
        return (jnp.arange(values.shape[axis_at]) // (values.shape[axis_at] // shards_of)).reshape((-1,) + (1,) * (values.ndim - 1 - axis_at))

    near = jax.random.permutation(stream_key, shards_of)[block_of(target)]
    second = (block_of(target) + shards_of // 2) % shards_of
    return jnp.where((block_of(source) == near) | (block_of(source) == second), factor * values, values)


def block_levels(rng, extent, pieces, least, largest):
    def one(position, blocks):
        heights = jax.random.uniform(jax.random.fold_in(jax.random.fold_in(rng, 6), position), (blocks,), jnp.float32, least / len(pieces), largest / len(pieces))
        return jnp.repeat(jnp.exp(heights), extent[position] // blocks).reshape((-1,) + (1,) * (len(extent) - position - 1))

    loudness = one(*pieces[0])
    for cut in pieces[1:]:
        loudness = loudness * one(*cut)
    return loudness


def normal_values(stream_key, dims, scale, limit, cuts=(), kind=jnp.bfloat16):
    values = jax.random.normal(stream_key, dims, jnp.float32) * scale
    if len(cuts) > 0:
        values = block_levels(stream_key, dims, cuts, -0.22, 0.18) * values
    return jnp.clip(values, min=-limit, max=limit).astype(kind)


def heavy_noise(stream_key, dims, scale, bound, pieces, heavy, held_as=jnp.bfloat16):
    values = scale * jax.random.normal(stream_key, dims, jnp.float32)
    if pieces:
        values = values * block_levels(stream_key, dims, pieces, -0.22, 0.18)
    return jnp.clip(raised(values, jax.random.fold_in(stream_key, 3), *heavy), -bound, bound).astype(held_as)


def setup_inputs(seed: int = 0) -> dict:
    arg_keys = jax.random.split(jax.random.key(seed), 15)
    return {
        "hidden_in": heavy_noise(arg_keys[0], (SEQS, LEN, D), 1.0, 6.0, ((0, 4), (1, 8)), (1, 2, 8, 2.0)),
        "block_of": draw_block_of(jax.random.fold_in(arg_keys[14], 71), 0),
        "in_gain": jnp.clip(1.0 + 0.15 * jax.random.normal(arg_keys[2], (D,), jnp.float32), 0.25, 1.75).astype(jnp.bfloat16),
        "w_query": normal_values(arg_keys[3], (D, QH * HD), D ** -0.5, 0.125, ((0, 32),)),
        "w_key": normal_values(arg_keys[4], (D, KVH * HD), D ** -0.5, 0.125, ((0, 32),)),
        "w_value": normal_values(arg_keys[5], (D, KVH * HD), D ** -0.5, 0.125, ((0, 32),)),
        "w_output": normal_values(arg_keys[6], (QH * HD, D), (max(1, 4 * QH * HD // LEN)) ** -0.5, 2.0, ((0, 32),)),
        "q_gain": jnp.clip(1.0 + 0.15 * jax.random.normal(arg_keys[7], (HD,), jnp.float32), 0.25, 1.75).astype(jnp.bfloat16),
        "k_gain": jnp.clip(1.0 + 0.15 * jax.random.normal(arg_keys[8], (HD,), jnp.float32), 0.25, 1.75).astype(jnp.bfloat16),
        "post_gain": jnp.clip(1.0 + 0.15 * jax.random.normal(arg_keys[9], (D,), jnp.float32), 0.25, 1.75).astype(jnp.bfloat16),
        "w_gate": normal_values(arg_keys[10], (D, FF), D ** -0.5, 0.125, ((0, 32),)),
        "w_up": normal_values(arg_keys[11], (D, FF), D ** -0.5, 0.125, ((0, 32),)),
        "w_down": normal_values(arg_keys[12], (FF, D), FF ** -0.5, 0.078125, ((0, 32),)),
        "cotangent": normal_values(arg_keys[13], (SEQS, LEN, D), 1.0, 6.0, ((0, 4), (1, 8))),
    }


EPS = 1e-06
THETA = 1000000.0
HIGHEST = lax.Precision.HIGHEST

@jax.custom_vjp
def low(v):
    return lax.optimization_barrier(v.astype(jnp.bfloat16)).astype(jnp.float32)

@jax.custom_vjp
def low_back(v):
    return v

def low_keep(v):
    return (low(v), None)

def low_pass(kept, grad):
    return (grad,)

def back_keep(v):
    return (v, None)

def back_low(kept, grad):
    return (low(grad),)
low.defvjp(low_keep, low_pass)
low_back.defvjp(back_keep, back_low)

def rms_norm(values, gain):
    return values * lax.rsqrt(lax.optimization_barrier(jnp.mean(values * values, axis=-1, keepdims=True)) + EPS) * gain

def rope_tables(positions, width):
    half_width = width // 2
    inverse = THETA ** (-(jnp.arange(half_width, dtype=jnp.float32) * 2.0 / width))
    angles = positions.astype(jnp.float32)[:, None] * inverse[None, :]
    return (jnp.cos(angles), jnp.sin(angles))

def rotate(values, cosine, sine):
    half_width = values.shape[-1] // 2
    first = values[..., :half_width]
    second = values[..., half_width:]
    cos_wide = cosine[:, None, :]
    sin_wide = sine[:, None, :]
    return jnp.concatenate([first * cos_wide - second * sin_wide, second * cos_wide + first * sin_wide], axis=-1)

def attend(queries, keys, values, positions):
    seq_len = queries.shape[0]
    query_rows = min(512, seq_len)
    block_count = seq_len // query_rows

    def one_block(pair):
        query_block, query_pos = pair
        scores = low_back(jnp.einsum('qhgd,khd->hgqk', query_block, keys, precision=HIGHEST))
        visible = positions[None, None, None, :] <= query_pos[None, None, :, None]
        scores = jnp.where(visible, scores, -1e+30)
        peak = lax.optimization_barrier(jnp.max(scores, axis=-1, keepdims=True))
        weights = jnp.exp(scores - peak)
        probs = low(weights / lax.optimization_barrier(jnp.sum(weights, axis=-1, keepdims=True)))
        return jnp.einsum('hgqk,khd->qhgd', probs, values, precision=HIGHEST)
    shaped = queries.reshape((block_count, query_rows) + queries.shape[1:])
    outputs = lax.map(jax.checkpoint(one_block), (shaped, positions.reshape(block_count, query_rows)))
    return outputs.reshape(queries.shape)

def decoder_layer(tokens_in, positions, params):
    in_gain, w_query, w_key, w_value, w_output, q_gain, k_gain, post_gain, w_gate, w_up, w_down = params
    seq_len = tokens_in.shape[0]
    attn_in = low(rms_norm(tokens_in, in_gain))
    q_raw = low_back(jnp.dot(attn_in, w_query, precision=HIGHEST)).reshape(seq_len, QH, HD)
    k_raw = low_back(jnp.dot(attn_in, w_key, precision=HIGHEST)).reshape(seq_len, KVH, HD)
    v_all = low(low_back(jnp.dot(attn_in, w_value, precision=HIGHEST))).reshape(seq_len, KVH, HD)
    cosine, sine = rope_tables(positions, HD)
    queries = low(rotate(rms_norm(q_raw, q_gain), cosine, sine) * HD ** (-0.5)).reshape(seq_len, KVH, QH // KVH, HD)
    keys = low(rotate(rms_norm(k_raw, k_gain), cosine, sine))
    mixed = low(low_back(attend(queries, keys, v_all, positions))).reshape(seq_len, QH * HD)
    hidden_mid = tokens_in + low_back(jnp.dot(mixed, w_output, precision=HIGHEST))
    mlp_in = low(rms_norm(hidden_mid, post_gain))
    gate_pre = low_back(jnp.dot(mlp_in, w_gate, precision=HIGHEST))
    up_pre = low_back(jnp.dot(mlp_in, w_up, precision=HIGHEST))
    inner = low(jax.nn.silu(gate_pre) * up_pre)
    return hidden_mid + jnp.dot(inner, w_down, precision=HIGHEST)

def reference(hidden_in, block_of, in_gain, w_query, w_key, w_value, w_output, q_gain, k_gain, post_gain, w_gate, w_up, w_down, cotangent):
    offsets = jnp.arange(BLK, dtype=jnp.int32)
    positions = (block_of[:, :, None] * BLK + offsets[None, None, :]).reshape(SEQS, LEN).astype(jnp.int32)
    params = tuple((weight.astype(jnp.float32) for weight in (in_gain, w_query, w_key, w_value, w_output, q_gain, k_gain, post_gain, w_gate, w_up, w_down)))

    def forward(tokens, *weights):

        def one_sequence(pair):
            return decoder_layer(pair[0], pair[1], weights)
        return lax.map(jax.checkpoint(one_sequence), (tokens, positions))
    result, pullback = jax.vjp(forward, hidden_in.astype(jnp.float32), *params)
    gradients = pullback(cotangent.astype(jnp.float32))
    return (result.astype(jnp.bfloat16), gradients[0], gradients[1], gradients[2], gradients[3], gradients[4], gradients[5], gradients[6], gradients[7], gradients[8], gradients[9], gradients[10], gradients[11])
```

```python
import math

import jax
import jax.numpy as jnp
from jax import lax
from jax.sharding import PartitionSpec as P

EPS = 1e-06
THETA = 1000000.0
KV_HEADS = 8


def rope_tables(positions, width):
    half_width = width // 2
    inverse = THETA ** (-(jnp.arange(half_width, dtype=jnp.float32) * 2.0 / width))
    angles = positions.astype(jnp.float32)[:, None] * inverse[None, :]
    return (jnp.cos(angles), jnp.sin(angles))


def rotate(values, cosine, sine):
    half_width = values.shape[-1] // 2
    first = values[..., :half_width]
    second = values[..., half_width:]
    cos_wide = cosine[:, None, :]
    sin_wide = sine[:, None, :]
    return jnp.concatenate(
        [first * cos_wide - second * sin_wide, second * cos_wide + first * sin_wide], axis=-1
    )


def norm_back(grad_normed, normed, scale):
    return scale * (grad_normed - normed * jnp.mean(grad_normed * normed, axis=-1, keepdims=True))


def gathered_weights_body(
    hidden_in,
    block_of,
    in_gain,
    w_query,
    w_key,
    w_value,
    w_output,
    q_gain,
    k_gain,
    post_gain,
    w_gate,
    w_up,
    w_down,
    cotangent,
):
    seq_count = hidden_in.shape[0]
    tok_rows = hidden_in.shape[1]
    flat_rows = seq_count * tok_rows
    model_width = hidden_in.shape[2]
    block_rows = tok_rows // 2
    block_total = 2 * lax.axis_size("ctx")
    seq_len = block_total * block_rows
    head_dim = q_gain.shape[0]
    q_heads = w_query.shape[1] // head_dim
    kv_heads = w_key.shape[1] // head_dim
    group_size = q_heads // kv_heads
    tile_blocks = math.gcd(block_total, max(1, 512 // block_rows))
    tile_rows = tile_blocks * block_rows
    q_scale = head_dim ** (-0.5)
    contract_rows = (((0,), (0,)), ((), ()))
    contract_cols = (((1,), (1,)), ((), ()))
    offsets = jnp.arange(block_rows, dtype=jnp.int32)
    positions = (block_of[:, :, None] * block_rows + offsets[None, None, :]).reshape(flat_rows)
    cosine, sine = rope_tables(positions, head_dim)
    residual = hidden_in.reshape(flat_rows, model_width).astype(jnp.float32)
    full_in_gain, full_query, full_key, full_value, full_output = (
        lax.all_gather(in_gain, ("ctx", "fsdp"), axis=0, tiled=True),
        lax.all_gather(w_query, ("ctx", "fsdp"), axis=0, tiled=True),
        lax.all_gather(w_key, ("ctx", "fsdp"), axis=0, tiled=True),
        lax.all_gather(w_value, ("ctx", "fsdp"), axis=0, tiled=True),
        lax.all_gather(w_output, ("ctx", "fsdp"), axis=0, tiled=True),
    )
    in_scale = lax.rsqrt(jnp.mean(residual * residual, axis=-1, keepdims=True) + EPS)
    in_normed = residual * in_scale
    attn_in = (in_normed * full_in_gain.astype(jnp.float32)).astype(jnp.bfloat16)
    q_raw = jnp.dot(attn_in, full_query, preferred_element_type=jnp.float32).reshape(
        flat_rows, q_heads, head_dim
    )
    k_raw = jnp.dot(attn_in, full_key, preferred_element_type=jnp.float32).reshape(
        flat_rows, kv_heads, head_dim
    )
    v_local = jnp.dot(attn_in, full_value, preferred_element_type=jnp.float32).astype(jnp.bfloat16)
    q_rms = lax.rsqrt(jnp.mean(q_raw * q_raw, axis=-1, keepdims=True) + EPS)
    q_unit = q_raw * q_rms
    queries = (rotate(q_unit * q_gain.astype(jnp.float32), cosine, sine) * q_scale).astype(
        jnp.bfloat16
    )
    k_rms = lax.rsqrt(jnp.mean(k_raw * k_raw, axis=-1, keepdims=True) + EPS)
    k_unit = k_raw * k_rms
    keys_local = rotate(k_unit * k_gain.astype(jnp.float32), cosine, sine).astype(jnp.bfloat16)
    all_keys, all_values, all_slots = (
        lax.all_gather(
            keys_local.reshape(seq_count, tok_rows, kv_heads * head_dim), "ctx", axis=1, tiled=True
        ),
        lax.all_gather(
            v_local.reshape(seq_count, tok_rows, kv_heads * head_dim), "ctx", axis=1, tiled=True
        ),
        lax.all_gather(block_of, "ctx", axis=1, tiled=True),
    )

    def tile_scores(query_tile, key_tile, query_pos, step):
        scores = jnp.einsum(
            "qhgd,khd->hgqk", query_tile, key_tile, preferred_element_type=jnp.float32
        )
        key_pos = step * tile_rows + jnp.arange(tile_rows, dtype=jnp.int32)
        visible = key_pos[None, :] <= query_pos[:, None]
        return (scores, visible)

    def sequence_tables(seq):
        key_blocks = all_keys[seq].reshape(block_total, block_rows, kv_heads, head_dim)
        value_blocks = all_values[seq].reshape(block_total, block_rows, kv_heads, head_dim)
        block_index = (
            jnp.zeros((block_total,), jnp.int32)
            .at[all_slots[seq]]
            .set(jnp.arange(block_total, dtype=jnp.int32))
        )
        return (key_blocks, value_blocks, block_index)

    def tile_index(block_index, step):
        return lax.dynamic_slice_in_dim(block_index, step * tile_blocks, tile_blocks)

    def fetch(table, block_index, step):
        return jnp.take(table, tile_index(block_index, step), axis=0).reshape(
            tile_rows, kv_heads, head_dim
        )

    log_totals = []
    attn_parts = []
    seq = 0
    key_blocks, value_blocks, block_index = sequence_tables(seq)
    for which in range(2):
        slot = 2 * seq + which
        query_tile = queries[slot * block_rows : (slot + 1) * block_rows].reshape(
            block_rows, kv_heads, group_size, head_dim
        )
        query_pos = positions[slot * block_rows : (slot + 1) * block_rows]
        tile_count = block_of[seq, which] // tile_blocks + 1

        def max_step(step, carry):
            running_max, running_sum = carry
            scores, visible = tile_scores(
                query_tile, fetch(key_blocks, block_index, step), query_pos, step
            )
            scores = jnp.where(visible, scores, -1e30)
            new_max = jnp.maximum(running_max, jnp.max(scores, axis=-1))
            running_sum = running_sum * jnp.exp(running_max - new_max) + jnp.sum(
                jnp.exp(scores - new_max[..., None]), axis=-1
            )
            return (new_max, running_sum)

        start_max = jnp.full((kv_heads, group_size, block_rows), -1e30, jnp.float32)
        start_sum = jnp.zeros((kv_heads, group_size, block_rows), jnp.float32)
        running_max, running_sum = lax.fori_loop(0, tile_count, max_step, (start_max, start_sum))
        log_total = running_max + jnp.log(running_sum)

        def value_step(step, total):
            scores, visible = tile_scores(
                query_tile, fetch(key_blocks, block_index, step), query_pos, step
            )
            probs = jnp.where(visible, jnp.exp(scores - log_total[..., None]), 0.0)
            return total + jnp.einsum(
                "hgqk,khd->qhgd",
                probs.astype(jnp.bfloat16),
                fetch(value_blocks, block_index, step),
                preferred_element_type=jnp.float32,
            )

        attn_part = lax.fori_loop(
            0,
            tile_count,
            value_step,
            jnp.zeros((block_rows, kv_heads, group_size, head_dim), jnp.float32),
        )
        log_totals.append(log_total)
        attn_parts.append(attn_part)
    attn_full = jnp.concatenate(attn_parts, axis=0)
    attn_bf = attn_full.reshape(flat_rows, q_heads * head_dim).astype(jnp.bfloat16)
    branch = jnp.dot(attn_bf, full_output, preferred_element_type=jnp.float32)
    hidden_mid = residual + branch
    full_post, full_gate, full_up, full_down = (
        lax.all_gather(post_gain, ("ctx", "fsdp"), axis=0, tiled=True),
        lax.all_gather(w_gate, ("ctx", "fsdp"), axis=0, tiled=True),
        lax.all_gather(w_up, ("ctx", "fsdp"), axis=0, tiled=True),
        lax.all_gather(w_down, ("ctx", "fsdp"), axis=0, tiled=True),
    )
    post_scale = lax.rsqrt(jnp.mean(hidden_mid * hidden_mid, axis=-1, keepdims=True) + EPS)
    post_normed = hidden_mid * post_scale
    mlp_in = (post_normed * full_post.astype(jnp.float32)).astype(jnp.bfloat16)
    gate_pre = jnp.dot(mlp_in, full_gate, preferred_element_type=jnp.float32)
    up_pre = jnp.dot(mlp_in, full_up, preferred_element_type=jnp.float32)
    sigmoid_gate = jax.nn.sigmoid(gate_pre)
    activated = gate_pre * sigmoid_gate
    inner = (activated * up_pre).astype(jnp.bfloat16)
    mlp_out = jnp.dot(inner, full_down, preferred_element_type=jnp.float32)
    output = (hidden_mid + mlp_out).astype(jnp.bfloat16)
    full_post, full_gate, full_up, full_down = (
        lax.all_gather(post_gain, ("ctx", "fsdp"), axis=0, tiled=True),
        lax.all_gather(w_gate, ("ctx", "fsdp"), axis=0, tiled=True),
        lax.all_gather(w_up, ("ctx", "fsdp"), axis=0, tiled=True),
        lax.all_gather(w_down, ("ctx", "fsdp"), axis=0, tiled=True),
    )
    grad_out = cotangent.reshape(flat_rows, model_width)
    grad_down = lax.dot_general(inner, grad_out, contract_rows, preferred_element_type=jnp.float32)
    part_down = lax.psum_scatter(grad_down, ("ctx", "fsdp"), scatter_dimension=0, tiled=True)
    grad_inner = lax.dot_general(
        grad_out, full_down, contract_cols, preferred_element_type=jnp.float32
    )
    grad_gate_pre = (
        grad_inner * up_pre * sigmoid_gate * (1.0 + gate_pre * (1.0 - sigmoid_gate))
    ).astype(jnp.bfloat16)
    grad_up_pre = (grad_inner * activated).astype(jnp.bfloat16)
    grad_gate = lax.dot_general(
        mlp_in, grad_gate_pre, contract_rows, preferred_element_type=jnp.float32
    )
    grad_up = lax.dot_general(
        mlp_in, grad_up_pre, contract_rows, preferred_element_type=jnp.float32
    )
    grad_mlp_in = lax.dot_general(
        grad_gate_pre, full_gate, contract_cols, preferred_element_type=jnp.float32
    ) + lax.dot_general(grad_up_pre, full_up, contract_cols, preferred_element_type=jnp.float32)
    grad_post_gain = jnp.sum(grad_mlp_in * post_normed, axis=0)
    grad_mid = grad_out.astype(jnp.float32) + norm_back(
        grad_mlp_in * full_post.astype(jnp.float32), post_normed, post_scale
    )
    part_post, part_gate, part_up = (
        lax.psum_scatter(grad_post_gain, ("ctx", "fsdp"), scatter_dimension=0, tiled=True),
        lax.psum_scatter(grad_gate, ("ctx", "fsdp"), scatter_dimension=0, tiled=True),
        lax.psum_scatter(grad_up, ("ctx", "fsdp"), scatter_dimension=0, tiled=True),
    )
    full_in_gain, full_query, full_key, full_value, full_output = (
        lax.all_gather(in_gain, ("ctx", "fsdp"), axis=0, tiled=True),
        lax.all_gather(w_query, ("ctx", "fsdp"), axis=0, tiled=True),
        lax.all_gather(w_key, ("ctx", "fsdp"), axis=0, tiled=True),
        lax.all_gather(w_value, ("ctx", "fsdp"), axis=0, tiled=True),
        lax.all_gather(w_output, ("ctx", "fsdp"), axis=0, tiled=True),
    )
    grad_branch = grad_mid.astype(jnp.bfloat16)
    grad_output = lax.dot_general(
        attn_bf, grad_branch, contract_rows, preferred_element_type=jnp.float32
    )
    grad_attn = lax.dot_general(
        grad_branch, full_output, contract_cols, preferred_element_type=jnp.float32
    ).astype(jnp.bfloat16)
    grad_attn = grad_attn.reshape(flat_rows, kv_heads, group_size, head_dim)
    query_grads = []
    seq = 0
    key_blocks, value_blocks, block_index = sequence_tables(seq)
    key_grads = jnp.zeros((block_total, block_rows, kv_heads, head_dim), jnp.float32)
    value_grads = jnp.zeros((block_total, block_rows, kv_heads, head_dim), jnp.float32)
    for which in range(2):
        slot = 2 * seq + which
        query_tile = queries[slot * block_rows : (slot + 1) * block_rows].reshape(
            block_rows, kv_heads, group_size, head_dim
        )
        query_pos = positions[slot * block_rows : (slot + 1) * block_rows]
        grad_tile = grad_attn[slot * block_rows : (slot + 1) * block_rows]
        tile_count = block_of[seq, which] // tile_blocks + 1
        delta = jnp.einsum("qhgd,qhgd->hgq", grad_tile.astype(jnp.float32), attn_parts[slot])
        log_total = log_totals[slot]

        def grad_step(step, carry):
            grad_query, keys_acc, values_acc = carry
            key_tile = fetch(key_blocks, block_index, step)
            scores, visible = tile_scores(query_tile, key_tile, query_pos, step)
            probs = jnp.where(visible, jnp.exp(scores - log_total[..., None]), 0.0)
            grad_probs = jnp.einsum(
                "qhgd,khd->hgqk",
                grad_tile,
                fetch(value_blocks, block_index, step),
                preferred_element_type=jnp.float32,
            )
            grad_scores = (probs * (grad_probs - delta[..., None])).astype(jnp.bfloat16)
            grad_query = grad_query + jnp.einsum(
                "hgqk,khd->qhgd", grad_scores, key_tile, preferred_element_type=jnp.float32
            )
            key_part = jnp.einsum(
                "hgqk,qhgd->khd", grad_scores, query_tile, preferred_element_type=jnp.float32
            )
            value_part = jnp.einsum(
                "hgqk,qhgd->khd",
                probs.astype(jnp.bfloat16),
                grad_tile,
                preferred_element_type=jnp.float32,
            )
            places = tile_index(block_index, step)
            keys_acc = keys_acc.at[places].add(
                key_part.reshape(tile_blocks, block_rows, kv_heads, head_dim)
            )
            values_acc = values_acc.at[places].add(
                value_part.reshape(tile_blocks, block_rows, kv_heads, head_dim)
            )
            return (grad_query, keys_acc, values_acc)

        start_query = jnp.zeros((block_rows, kv_heads, group_size, head_dim), jnp.float32)
        grad_query, key_grads, value_grads = lax.fori_loop(
            0, tile_count, grad_step, (start_query, key_grads, value_grads)
        )
        query_grads.append(grad_query)
    key_grad_list = [key_grads.reshape(seq_len, kv_heads * head_dim)]
    value_grad_list = [value_grads.reshape(seq_len, kv_heads * head_dim)]
    grad_keys, grad_values = (
        lax.psum_scatter(
            jnp.stack(key_grad_list, axis=0).astype(jnp.bfloat16),
            "ctx",
            scatter_dimension=1,
            tiled=True,
        ).astype(jnp.float32),
        lax.psum_scatter(
            jnp.stack(value_grad_list, axis=0).astype(jnp.bfloat16),
            "ctx",
            scatter_dimension=1,
            tiled=True,
        ).astype(jnp.float32),
    )
    grad_q_rot = (
        jnp.concatenate(query_grads, axis=0).reshape(flat_rows, q_heads, head_dim) * q_scale
    )
    grad_q_normed = rotate(grad_q_rot, cosine, -sine)
    grad_q_gain = jnp.sum(grad_q_normed * q_unit, axis=(0, 1))
    grad_q_raw = (
        norm_back(grad_q_normed * q_gain.astype(jnp.float32), q_unit, q_rms)
        .astype(jnp.bfloat16)
        .reshape(flat_rows, q_heads * head_dim)
    )
    grad_k_normed = rotate(grad_keys.reshape(flat_rows, kv_heads, head_dim), cosine, -sine)
    grad_k_gain = jnp.sum(grad_k_normed * k_unit, axis=(0, 1))
    grad_k_raw = (
        norm_back(grad_k_normed * k_gain.astype(jnp.float32), k_unit, k_rms)
        .astype(jnp.bfloat16)
        .reshape(flat_rows, kv_heads * head_dim)
    )
    grad_v_local = grad_values.reshape(flat_rows, kv_heads * head_dim).astype(jnp.bfloat16)
    grad_query_w = lax.dot_general(
        attn_in, grad_q_raw, contract_rows, preferred_element_type=jnp.float32
    )
    grad_key_w = lax.dot_general(
        attn_in, grad_k_raw, contract_rows, preferred_element_type=jnp.float32
    )
    grad_value_w = lax.dot_general(
        attn_in, grad_v_local, contract_rows, preferred_element_type=jnp.float32
    )
    grad_attn_in = lax.dot_general(
        grad_q_raw, full_query, contract_cols, preferred_element_type=jnp.float32
    )
    grad_attn_in = grad_attn_in + lax.dot_general(
        grad_k_raw, full_key, contract_cols, preferred_element_type=jnp.float32
    )
    grad_attn_in = grad_attn_in + lax.dot_general(
        grad_v_local, full_value, contract_cols, preferred_element_type=jnp.float32
    )
    grad_in_gain = jnp.sum(grad_attn_in * in_normed, axis=0)
    grad_input = grad_mid + norm_back(
        grad_attn_in * full_in_gain.astype(jnp.float32), in_normed, in_scale
    )
    part_in, part_query, part_key, part_value, part_output = (
        lax.psum_scatter(grad_in_gain, ("ctx", "fsdp"), scatter_dimension=0, tiled=True),
        lax.psum_scatter(grad_query_w, ("ctx", "fsdp"), scatter_dimension=0, tiled=True),
        lax.psum_scatter(grad_key_w, ("ctx", "fsdp"), scatter_dimension=0, tiled=True),
        lax.psum_scatter(grad_value_w, ("ctx", "fsdp"), scatter_dimension=0, tiled=True),
        lax.psum_scatter(grad_output, ("ctx", "fsdp"), scatter_dimension=0, tiled=True),
    )
    sum_q_gain, sum_k_gain = lax.psum((grad_q_gain, grad_k_gain), ("ctx", "fsdp"))
    return (
        output.reshape(seq_count, tok_rows, model_width),
        grad_input.reshape(seq_count, tok_rows, model_width),
        part_in,
        part_query,
        part_key,
        part_value,
        part_output,
        sum_q_gain,
        sum_k_gain,
        part_post,
        part_gate,
        part_up,
        part_down,
    )


def tp_body(
    hidden_in,
    block_of,
    in_gain,
    w_query,
    w_key,
    w_value,
    w_output,
    q_gain,
    k_gain,
    post_gain,
    w_gate,
    w_up,
    w_down,
    cotangent,
):
    seq_count, tok_rows, model_width = hidden_in.shape
    n_ctx = lax.axis_size("ctx")
    n_fsdp = lax.axis_size("fsdp")
    block_rows = tok_rows // 2
    rows = seq_count * tok_rows
    seq_rows = n_ctx * rows
    head_dim = q_gain.shape[0]
    q_heads = w_query.shape[1] // head_dim // n_ctx
    kv_heads = w_key.shape[1] // head_dim // n_ctx
    group = q_heads // kv_heads
    q_scale = head_dim ** (-0.5)
    f32, bf16 = jnp.float32, jnp.bfloat16
    contract_rows = (((0,), (0,)), ((), ()))
    contract_cols = (((1,), (1,)), ((), ()))

    def take_columns(weight):
        depth, width = weight.shape
        parts = weight.reshape(depth, n_ctx, width // n_ctx).transpose(1, 0, 2)
        mine = lax.all_to_all(parts, "ctx", 0, 0, tiled=False)
        whole = lax.all_gather(mine, "fsdp", axis=1, tiled=False)
        return whole.reshape(n_ctx * n_fsdp * depth, width // n_ctx)

    def give_columns(grad):
        width = grad.shape[1]
        depth = grad.shape[0] // (n_ctx * n_fsdp)
        parts = grad.astype(bf16).reshape(n_ctx, n_fsdp, depth, width).transpose(1, 0, 2, 3)
        parts = parts.reshape(n_fsdp * n_ctx * depth, width)
        mine = lax.psum_scatter(parts, "fsdp", scatter_dimension=0, tiled=True)
        parts = lax.all_to_all(mine.reshape(n_ctx, depth, width), "ctx", 0, 0, tiled=False)
        return parts.transpose(1, 0, 2).reshape(depth, n_ctx * width).astype(f32)

    def take_rows(weight):
        return lax.all_gather(weight, "fsdp", axis=0, tiled=True)

    def give_rows(grad):
        return lax.psum_scatter(grad.astype(bf16), "fsdp", scatter_dimension=0, tiled=True).astype(f32)

    def gather(local):
        return lax.all_gather(local, "ctx", axis=0, tiled=True)

    def scatter_sum(partial):
        return lax.psum_scatter(partial.astype(bf16), "ctx", scatter_dimension=0, tiled=True).astype(f32)

    full_in_gain = lax.all_gather(in_gain, ("ctx", "fsdp"), axis=0, tiled=True).astype(f32)
    full_post = lax.all_gather(post_gain, ("ctx", "fsdp"), axis=0, tiled=True).astype(f32)
    all_blocks = lax.all_gather(block_of[0], "ctx", axis=0, tiled=True)
    offsets = jnp.arange(block_rows, dtype=jnp.int32)
    positions = (all_blocks[:, None] * block_rows + offsets[None, :]).reshape(seq_rows)
    cosine, sine = rope_tables(positions, head_dim)

    residual = hidden_in.reshape(rows, model_width).astype(f32)
    in_scale = lax.rsqrt(jnp.mean(residual * residual, axis=-1, keepdims=True) + EPS)
    in_normed = residual * in_scale
    attn_in = gather((in_normed * full_in_gain).astype(bf16))

    mine_query, mine_key, mine_value = take_columns(w_query), take_columns(w_key), take_columns(w_value)
    q_raw = jnp.dot(attn_in, mine_query, preferred_element_type=f32).reshape(seq_rows, q_heads, head_dim)
    k_raw = jnp.dot(attn_in, mine_key, preferred_element_type=f32).reshape(seq_rows, kv_heads, head_dim)
    values = jnp.dot(attn_in, mine_value, preferred_element_type=f32).astype(bf16).reshape(seq_rows, kv_heads, head_dim)
    q_rms = lax.rsqrt(jnp.mean(q_raw * q_raw, axis=-1, keepdims=True) + EPS)
    q_unit = q_raw * q_rms
    queries = (rotate(q_unit * q_gain.astype(f32), cosine, sine) * q_scale).astype(bf16)
    queries = queries.reshape(seq_rows, kv_heads, group, head_dim)
    k_rms = lax.rsqrt(jnp.mean(k_raw * k_raw, axis=-1, keepdims=True) + EPS)
    k_unit = k_raw * k_rms
    keys = rotate(k_unit * k_gain.astype(f32), cosine, sine).astype(bf16)

    visible = positions[None, :] <= positions[:, None]

    def exact_probs():
        scores = jnp.einsum("qhgd,khd->hgqk", queries, keys, preferred_element_type=f32)
        scores = jnp.where(visible, scores, -1e30)
        peak = jnp.max(scores, axis=-1, keepdims=True)
        weights = jnp.exp(scores - peak)
        return weights / jnp.sum(weights, axis=-1, keepdims=True)

    probs = exact_probs()
    attn = jnp.einsum("hgqk,khd->qhgd", probs.astype(bf16), values, preferred_element_type=f32)
    attn_bf = attn.reshape(seq_rows, q_heads * head_dim).astype(bf16)
    mine_output = take_rows(w_output)
    branch = scatter_sum(jnp.dot(attn_bf, mine_output, preferred_element_type=f32))
    hidden_mid = residual + branch

    post_scale = lax.rsqrt(jnp.mean(hidden_mid * hidden_mid, axis=-1, keepdims=True) + EPS)
    post_normed = hidden_mid * post_scale
    mlp_in = gather((post_normed * full_post).astype(bf16))
    mine_gate, mine_up, mine_down = take_columns(w_gate), take_columns(w_up), take_rows(w_down)
    gate_pre = jnp.dot(mlp_in, mine_gate, preferred_element_type=f32)
    up_pre = jnp.dot(mlp_in, mine_up, preferred_element_type=f32)
    sigmoid_gate = jax.nn.sigmoid(gate_pre)
    activated = gate_pre * sigmoid_gate
    inner = (activated * up_pre).astype(bf16)
    mlp_out = scatter_sum(jnp.dot(inner, mine_down, preferred_element_type=f32))
    output = (hidden_mid + mlp_out).astype(bf16)

    cot_local = cotangent.reshape(rows, model_width)
    grad_out = gather(cot_local)
    part_down = give_rows(lax.dot_general(inner, grad_out, contract_rows, preferred_element_type=f32))
    grad_inner = lax.dot_general(grad_out, mine_down, contract_cols, preferred_element_type=f32)
    grad_gate_pre = (grad_inner * up_pre * sigmoid_gate * (1.0 + gate_pre * (1.0 - sigmoid_gate))).astype(bf16)
    grad_up_pre = (grad_inner * activated).astype(bf16)
    part_gate = give_columns(lax.dot_general(mlp_in, grad_gate_pre, contract_rows, preferred_element_type=f32))
    part_up = give_columns(lax.dot_general(mlp_in, grad_up_pre, contract_rows, preferred_element_type=f32))
    grad_mlp_in = scatter_sum(
        lax.dot_general(grad_gate_pre, mine_gate, contract_cols, preferred_element_type=f32)
        + lax.dot_general(grad_up_pre, mine_up, contract_cols, preferred_element_type=f32)
    )
    grad_post_gain = jnp.sum(grad_mlp_in * post_normed, axis=0)
    grad_mid = cot_local.astype(f32) + norm_back(grad_mlp_in * full_post, post_normed, post_scale)

    grad_branch = gather(grad_mid.astype(bf16))
    part_output = give_rows(lax.dot_general(attn_bf, grad_branch, contract_rows, preferred_element_type=f32))
    grad_attn = lax.dot_general(grad_branch, mine_output, contract_cols, preferred_element_type=f32).astype(bf16)
    grad_attn = grad_attn.reshape(seq_rows, kv_heads, group, head_dim)
    delta = jnp.einsum("qhgd,qhgd->hgq", grad_attn.astype(f32), attn)
    grad_probs = jnp.einsum("qhgd,khd->hgqk", grad_attn, values, preferred_element_type=f32)
    grad_scores = (probs * (grad_probs - delta[..., None])).astype(bf16)
    grad_queries = jnp.einsum("hgqk,khd->qhgd", grad_scores, keys, preferred_element_type=f32)
    grad_keys = jnp.einsum("hgqk,qhgd->khd", grad_scores, queries, preferred_element_type=f32)
    grad_values = jnp.einsum("hgqk,qhgd->khd", probs.astype(bf16), grad_attn, preferred_element_type=f32)

    grad_q_normed = rotate(grad_queries.reshape(seq_rows, q_heads, head_dim) * q_scale, cosine, -sine)
    grad_q_gain = jnp.sum(grad_q_normed * q_unit, axis=(0, 1))
    grad_q_raw = norm_back(grad_q_normed * q_gain.astype(f32), q_unit, q_rms).astype(bf16).reshape(seq_rows, q_heads * head_dim)
    grad_k_normed = rotate(grad_keys, cosine, -sine)
    grad_k_gain = jnp.sum(grad_k_normed * k_unit, axis=(0, 1))
    grad_k_raw = norm_back(grad_k_normed * k_gain.astype(f32), k_unit, k_rms).astype(bf16).reshape(seq_rows, kv_heads * head_dim)
    grad_v = grad_values.astype(bf16).reshape(seq_rows, kv_heads * head_dim)
    part_query = give_columns(lax.dot_general(attn_in, grad_q_raw, contract_rows, preferred_element_type=f32))
    part_key = give_columns(lax.dot_general(attn_in, grad_k_raw, contract_rows, preferred_element_type=f32))
    part_value = give_columns(lax.dot_general(attn_in, grad_v, contract_rows, preferred_element_type=f32))
    grad_attn_in = scatter_sum(
        lax.dot_general(grad_q_raw, mine_query, contract_cols, preferred_element_type=f32)
        + lax.dot_general(grad_k_raw, mine_key, contract_cols, preferred_element_type=f32)
        + lax.dot_general(grad_v, mine_value, contract_cols, preferred_element_type=f32)
    )
    grad_in_gain = jnp.sum(grad_attn_in * in_normed, axis=0)
    grad_input = grad_mid + norm_back(grad_attn_in * full_in_gain, in_normed, in_scale)

    part_in = lax.psum_scatter(grad_in_gain, ("ctx", "fsdp"), scatter_dimension=0, tiled=True)
    part_post = lax.psum_scatter(grad_post_gain, ("ctx", "fsdp"), scatter_dimension=0, tiled=True)
    sum_q_gain, sum_k_gain = lax.psum((grad_q_gain, grad_k_gain), ("ctx", "fsdp"))
    return (
        output.reshape(seq_count, tok_rows, model_width),
        grad_input.reshape(seq_count, tok_rows, model_width),
        part_in,
        part_query,
        part_key,
        part_value,
        part_output,
        sum_q_gain,
        sum_k_gain,
        part_post,
        part_gate,
        part_up,
        part_down,
    )


def solution(mesh):
    body = tp_body if KV_HEADS % mesh.shape["ctx"] == 0 else gathered_weights_body
    return jax.shard_map(
        body,
        mesh=mesh,
        in_specs=(
            P("fsdp", "ctx", None),
            P("fsdp", "ctx"),
            P(("ctx", "fsdp")),
            P(("ctx", "fsdp"), None),
            P(("ctx", "fsdp"), None),
            P(("ctx", "fsdp"), None),
            P(("ctx", "fsdp"), None),
            P(),
            P(),
            P(("ctx", "fsdp")),
            P(("ctx", "fsdp"), None),
            P(("ctx", "fsdp"), None),
            P(("ctx", "fsdp"), None),
            P("fsdp", "ctx", None),
        ),
        out_specs=(
            P("fsdp", "ctx", None),
            P("fsdp", "ctx", None),
            P(("ctx", "fsdp")),
            P(("ctx", "fsdp"), None),
            P(("ctx", "fsdp"), None),
            P(("ctx", "fsdp"), None),
            P(("ctx", "fsdp"), None),
            P(),
            P(),
            P(("ctx", "fsdp")),
            P(("ctx", "fsdp"), None),
            P(("ctx", "fsdp"), None),
            P(("ctx", "fsdp"), None),
        ),
        check_vma=False,
    )
```

```python
import functools
import math

import jax
import jax.numpy as jnp
from jax import lax
from jax.experimental import pallas as pl
from jax.experimental.pallas import tpu as pltpu
from jax.sharding import PartitionSpec as P

EPS = 1e-06
THETA = 1000000.0
KV_HEADS = 8


def rope_tables(positions, width):
    half_width = width // 2
    inverse = THETA ** (-(jnp.arange(half_width, dtype=jnp.float32) * 2.0 / width))
    angles = positions.astype(jnp.float32)[:, None] * inverse[None, :]
    return (jnp.cos(angles), jnp.sin(angles))


def rotate(values, cosine, sine):
    half_width = values.shape[-1] // 2
    first = values[..., :half_width]
    second = values[..., half_width:]
    cos_wide = cosine[:, None, :]
    sin_wide = sine[:, None, :]
    return jnp.concatenate(
        [first * cos_wide - second * sin_wide, second * cos_wide + first * sin_wide], axis=-1
    )


def norm_back(grad_normed, normed, scale):
    return scale * (grad_normed - normed * jnp.mean(grad_normed * normed, axis=-1, keepdims=True))


def gathered_weights_body(
    hidden_in,
    block_of,
    in_gain,
    w_query,
    w_key,
    w_value,
    w_output,
    q_gain,
    k_gain,
    post_gain,
    w_gate,
    w_up,
    w_down,
    cotangent,
):
    seq_count = hidden_in.shape[0]
    tok_rows = hidden_in.shape[1]
    flat_rows = seq_count * tok_rows
    model_width = hidden_in.shape[2]
    block_rows = tok_rows // 2
    block_total = 2 * lax.axis_size("ctx")
    seq_len = block_total * block_rows
    head_dim = q_gain.shape[0]
    q_heads = w_query.shape[1] // head_dim
    kv_heads = w_key.shape[1] // head_dim
    group_size = q_heads // kv_heads
    tile_blocks = math.gcd(block_total, max(1, 512 // block_rows))
    tile_rows = tile_blocks * block_rows
    q_scale = head_dim ** (-0.5)
    contract_rows = (((0,), (0,)), ((), ()))
    contract_cols = (((1,), (1,)), ((), ()))
    offsets = jnp.arange(block_rows, dtype=jnp.int32)
    positions = (block_of[:, :, None] * block_rows + offsets[None, None, :]).reshape(flat_rows)
    cosine, sine = rope_tables(positions, head_dim)
    residual = hidden_in.reshape(flat_rows, model_width).astype(jnp.float32)
    full_in_gain, full_query, full_key, full_value, full_output = (
        lax.all_gather(in_gain, ("ctx", "fsdp"), axis=0, tiled=True),
        lax.all_gather(w_query, ("ctx", "fsdp"), axis=0, tiled=True),
        lax.all_gather(w_key, ("ctx", "fsdp"), axis=0, tiled=True),
        lax.all_gather(w_value, ("ctx", "fsdp"), axis=0, tiled=True),
        lax.all_gather(w_output, ("ctx", "fsdp"), axis=0, tiled=True),
    )
    in_scale = lax.rsqrt(jnp.mean(residual * residual, axis=-1, keepdims=True) + EPS)
    in_normed = residual * in_scale
    attn_in = (in_normed * full_in_gain.astype(jnp.float32)).astype(jnp.bfloat16)
    q_raw = jnp.dot(attn_in, full_query, preferred_element_type=jnp.float32).reshape(
        flat_rows, q_heads, head_dim
    )
    k_raw = jnp.dot(attn_in, full_key, preferred_element_type=jnp.float32).reshape(
        flat_rows, kv_heads, head_dim
    )
    v_local = jnp.dot(attn_in, full_value, preferred_element_type=jnp.float32).astype(jnp.bfloat16)
    q_rms = lax.rsqrt(jnp.mean(q_raw * q_raw, axis=-1, keepdims=True) + EPS)
    q_unit = q_raw * q_rms
    queries = (rotate(q_unit * q_gain.astype(jnp.float32), cosine, sine) * q_scale).astype(
        jnp.bfloat16
    )
    k_rms = lax.rsqrt(jnp.mean(k_raw * k_raw, axis=-1, keepdims=True) + EPS)
    k_unit = k_raw * k_rms
    keys_local = rotate(k_unit * k_gain.astype(jnp.float32), cosine, sine).astype(jnp.bfloat16)
    all_keys, all_values, all_slots = (
        lax.all_gather(
            keys_local.reshape(seq_count, tok_rows, kv_heads * head_dim), "ctx", axis=1, tiled=True
        ),
        lax.all_gather(
            v_local.reshape(seq_count, tok_rows, kv_heads * head_dim), "ctx", axis=1, tiled=True
        ),
        lax.all_gather(block_of, "ctx", axis=1, tiled=True),
    )

    def tile_scores(query_tile, key_tile, query_pos, step):
        scores = jnp.einsum(
            "qhgd,khd->hgqk", query_tile, key_tile, preferred_element_type=jnp.float32
        )
        key_pos = step * tile_rows + jnp.arange(tile_rows, dtype=jnp.int32)
        visible = key_pos[None, :] <= query_pos[:, None]
        return (scores, visible)

    def sequence_tables(seq):
        key_blocks = all_keys[seq].reshape(block_total, block_rows, kv_heads, head_dim)
        value_blocks = all_values[seq].reshape(block_total, block_rows, kv_heads, head_dim)
        block_index = (
            jnp.zeros((block_total,), jnp.int32)
            .at[all_slots[seq]]
            .set(jnp.arange(block_total, dtype=jnp.int32))
        )
        return (key_blocks, value_blocks, block_index)

    def tile_index(block_index, step):
        return lax.dynamic_slice_in_dim(block_index, step * tile_blocks, tile_blocks)

    def fetch(table, block_index, step):
        return jnp.take(table, tile_index(block_index, step), axis=0).reshape(
            tile_rows, kv_heads, head_dim
        )

    log_totals = []
    attn_parts = []
    seq = 0
    key_blocks, value_blocks, block_index = sequence_tables(seq)
    for which in range(2):
        slot = 2 * seq + which
        query_tile = queries[slot * block_rows : (slot + 1) * block_rows].reshape(
            block_rows, kv_heads, group_size, head_dim
        )
        query_pos = positions[slot * block_rows : (slot + 1) * block_rows]
        tile_count = block_of[seq, which] // tile_blocks + 1

        def max_step(step, carry):
            running_max, running_sum = carry
            scores, visible = tile_scores(
                query_tile, fetch(key_blocks, block_index, step), query_pos, step
            )
            scores = jnp.where(visible, scores, -1e30)
            new_max = jnp.maximum(running_max, jnp.max(scores, axis=-1))
            running_sum = running_sum * jnp.exp(running_max - new_max) + jnp.sum(
                jnp.exp(scores - new_max[..., None]), axis=-1
            )
            return (new_max, running_sum)

        start_max = jnp.full((kv_heads, group_size, block_rows), -1e30, jnp.float32)
        start_sum = jnp.zeros((kv_heads, group_size, block_rows), jnp.float32)
        running_max, running_sum = lax.fori_loop(0, tile_count, max_step, (start_max, start_sum))
        log_total = running_max + jnp.log(running_sum)

        def value_step(step, total):
            scores, visible = tile_scores(
                query_tile, fetch(key_blocks, block_index, step), query_pos, step
            )
            probs = jnp.where(visible, jnp.exp(scores - log_total[..., None]), 0.0)
            return total + jnp.einsum(
                "hgqk,khd->qhgd",
                probs.astype(jnp.bfloat16),
                fetch(value_blocks, block_index, step),
                preferred_element_type=jnp.float32,
            )

        attn_part = lax.fori_loop(
            0,
            tile_count,
            value_step,
            jnp.zeros((block_rows, kv_heads, group_size, head_dim), jnp.float32),
        )
        log_totals.append(log_total)
        attn_parts.append(attn_part)
    attn_full = jnp.concatenate(attn_parts, axis=0)
    attn_bf = attn_full.reshape(flat_rows, q_heads * head_dim).astype(jnp.bfloat16)
    branch = jnp.dot(attn_bf, full_output, preferred_element_type=jnp.float32)
    hidden_mid = residual + branch
    full_post, full_gate, full_up, full_down = (
        lax.all_gather(post_gain, ("ctx", "fsdp"), axis=0, tiled=True),
        lax.all_gather(w_gate, ("ctx", "fsdp"), axis=0, tiled=True),
        lax.all_gather(w_up, ("ctx", "fsdp"), axis=0, tiled=True),
        lax.all_gather(w_down, ("ctx", "fsdp"), axis=0, tiled=True),
    )
    post_scale = lax.rsqrt(jnp.mean(hidden_mid * hidden_mid, axis=-1, keepdims=True) + EPS)
    post_normed = hidden_mid * post_scale
    mlp_in = (post_normed * full_post.astype(jnp.float32)).astype(jnp.bfloat16)
    gate_pre = jnp.dot(mlp_in, full_gate, preferred_element_type=jnp.float32)
    up_pre = jnp.dot(mlp_in, full_up, preferred_element_type=jnp.float32)
    sigmoid_gate = jax.nn.sigmoid(gate_pre)
    activated = gate_pre * sigmoid_gate
    inner = (activated * up_pre).astype(jnp.bfloat16)
    mlp_out = jnp.dot(inner, full_down, preferred_element_type=jnp.float32)
    output = (hidden_mid + mlp_out).astype(jnp.bfloat16)
    full_post, full_gate, full_up, full_down = (
        lax.all_gather(post_gain, ("ctx", "fsdp"), axis=0, tiled=True),
        lax.all_gather(w_gate, ("ctx", "fsdp"), axis=0, tiled=True),
        lax.all_gather(w_up, ("ctx", "fsdp"), axis=0, tiled=True),
        lax.all_gather(w_down, ("ctx", "fsdp"), axis=0, tiled=True),
    )
    grad_out = cotangent.reshape(flat_rows, model_width)
    grad_down = lax.dot_general(inner, grad_out, contract_rows, preferred_element_type=jnp.float32)
    part_down = lax.psum_scatter(grad_down, ("ctx", "fsdp"), scatter_dimension=0, tiled=True)
    grad_inner = lax.dot_general(
        grad_out, full_down, contract_cols, preferred_element_type=jnp.float32
    )
    grad_gate_pre = (
        grad_inner * up_pre * sigmoid_gate * (1.0 + gate_pre * (1.0 - sigmoid_gate))
    ).astype(jnp.bfloat16)
    grad_up_pre = (grad_inner * activated).astype(jnp.bfloat16)
    grad_gate = lax.dot_general(
        mlp_in, grad_gate_pre, contract_rows, preferred_element_type=jnp.float32
    )
    grad_up = lax.dot_general(
        mlp_in, grad_up_pre, contract_rows, preferred_element_type=jnp.float32
    )
    grad_mlp_in = lax.dot_general(
        grad_gate_pre, full_gate, contract_cols, preferred_element_type=jnp.float32
    ) + lax.dot_general(grad_up_pre, full_up, contract_cols, preferred_element_type=jnp.float32)
    grad_post_gain = jnp.sum(grad_mlp_in * post_normed, axis=0)
    grad_mid = grad_out.astype(jnp.float32) + norm_back(
        grad_mlp_in * full_post.astype(jnp.float32), post_normed, post_scale
    )
    part_post, part_gate, part_up = (
        lax.psum_scatter(grad_post_gain, ("ctx", "fsdp"), scatter_dimension=0, tiled=True),
        lax.psum_scatter(grad_gate, ("ctx", "fsdp"), scatter_dimension=0, tiled=True),
        lax.psum_scatter(grad_up, ("ctx", "fsdp"), scatter_dimension=0, tiled=True),
    )
    full_in_gain, full_query, full_key, full_value, full_output = (
        lax.all_gather(in_gain, ("ctx", "fsdp"), axis=0, tiled=True),
        lax.all_gather(w_query, ("ctx", "fsdp"), axis=0, tiled=True),
        lax.all_gather(w_key, ("ctx", "fsdp"), axis=0, tiled=True),
        lax.all_gather(w_value, ("ctx", "fsdp"), axis=0, tiled=True),
        lax.all_gather(w_output, ("ctx", "fsdp"), axis=0, tiled=True),
    )
    grad_branch = grad_mid.astype(jnp.bfloat16)
    grad_output = lax.dot_general(
        attn_bf, grad_branch, contract_rows, preferred_element_type=jnp.float32
    )
    grad_attn = lax.dot_general(
        grad_branch, full_output, contract_cols, preferred_element_type=jnp.float32
    ).astype(jnp.bfloat16)
    grad_attn = grad_attn.reshape(flat_rows, kv_heads, group_size, head_dim)
    query_grads = []
    seq = 0
    key_blocks, value_blocks, block_index = sequence_tables(seq)
    key_grads = jnp.zeros((block_total, block_rows, kv_heads, head_dim), jnp.float32)
    value_grads = jnp.zeros((block_total, block_rows, kv_heads, head_dim), jnp.float32)
    for which in range(2):
        slot = 2 * seq + which
        query_tile = queries[slot * block_rows : (slot + 1) * block_rows].reshape(
            block_rows, kv_heads, group_size, head_dim
        )
        query_pos = positions[slot * block_rows : (slot + 1) * block_rows]
        grad_tile = grad_attn[slot * block_rows : (slot + 1) * block_rows]
        tile_count = block_of[seq, which] // tile_blocks + 1
        delta = jnp.einsum("qhgd,qhgd->hgq", grad_tile.astype(jnp.float32), attn_parts[slot])
        log_total = log_totals[slot]

        def grad_step(step, carry):
            grad_query, keys_acc, values_acc = carry
            key_tile = fetch(key_blocks, block_index, step)
            scores, visible = tile_scores(query_tile, key_tile, query_pos, step)
            probs = jnp.where(visible, jnp.exp(scores - log_total[..., None]), 0.0)
            grad_probs = jnp.einsum(
                "qhgd,khd->hgqk",
                grad_tile,
                fetch(value_blocks, block_index, step),
                preferred_element_type=jnp.float32,
            )
            grad_scores = (probs * (grad_probs - delta[..., None])).astype(jnp.bfloat16)
            grad_query = grad_query + jnp.einsum(
                "hgqk,khd->qhgd", grad_scores, key_tile, preferred_element_type=jnp.float32
            )
            key_part = jnp.einsum(
                "hgqk,qhgd->khd", grad_scores, query_tile, preferred_element_type=jnp.float32
            )
            value_part = jnp.einsum(
                "hgqk,qhgd->khd",
                probs.astype(jnp.bfloat16),
                grad_tile,
                preferred_element_type=jnp.float32,
            )
            places = tile_index(block_index, step)
            keys_acc = keys_acc.at[places].add(
                key_part.reshape(tile_blocks, block_rows, kv_heads, head_dim)
            )
            values_acc = values_acc.at[places].add(
                value_part.reshape(tile_blocks, block_rows, kv_heads, head_dim)
            )
            return (grad_query, keys_acc, values_acc)

        start_query = jnp.zeros((block_rows, kv_heads, group_size, head_dim), jnp.float32)
        grad_query, key_grads, value_grads = lax.fori_loop(
            0, tile_count, grad_step, (start_query, key_grads, value_grads)
        )
        query_grads.append(grad_query)
    key_grad_list = [key_grads.reshape(seq_len, kv_heads * head_dim)]
    value_grad_list = [value_grads.reshape(seq_len, kv_heads * head_dim)]
    grad_keys, grad_values = (
        lax.psum_scatter(
            jnp.stack(key_grad_list, axis=0).astype(jnp.bfloat16),
            "ctx",
            scatter_dimension=1,
            tiled=True,
        ).astype(jnp.float32),
        lax.psum_scatter(
            jnp.stack(value_grad_list, axis=0).astype(jnp.bfloat16),
            "ctx",
            scatter_dimension=1,
            tiled=True,
        ).astype(jnp.float32),
    )
    grad_q_rot = (
        jnp.concatenate(query_grads, axis=0).reshape(flat_rows, q_heads, head_dim) * q_scale
    )
    grad_q_normed = rotate(grad_q_rot, cosine, -sine)
    grad_q_gain = jnp.sum(grad_q_normed * q_unit, axis=(0, 1))
    grad_q_raw = (
        norm_back(grad_q_normed * q_gain.astype(jnp.float32), q_unit, q_rms)
        .astype(jnp.bfloat16)
        .reshape(flat_rows, q_heads * head_dim)
    )
    grad_k_normed = rotate(grad_keys.reshape(flat_rows, kv_heads, head_dim), cosine, -sine)
    grad_k_gain = jnp.sum(grad_k_normed * k_unit, axis=(0, 1))
    grad_k_raw = (
        norm_back(grad_k_normed * k_gain.astype(jnp.float32), k_unit, k_rms)
        .astype(jnp.bfloat16)
        .reshape(flat_rows, kv_heads * head_dim)
    )
    grad_v_local = grad_values.reshape(flat_rows, kv_heads * head_dim).astype(jnp.bfloat16)
    grad_query_w = lax.dot_general(
        attn_in, grad_q_raw, contract_rows, preferred_element_type=jnp.float32
    )
    grad_key_w = lax.dot_general(
        attn_in, grad_k_raw, contract_rows, preferred_element_type=jnp.float32
    )
    grad_value_w = lax.dot_general(
        attn_in, grad_v_local, contract_rows, preferred_element_type=jnp.float32
    )
    grad_attn_in = lax.dot_general(
        grad_q_raw, full_query, contract_cols, preferred_element_type=jnp.float32
    )
    grad_attn_in = grad_attn_in + lax.dot_general(
        grad_k_raw, full_key, contract_cols, preferred_element_type=jnp.float32
    )
    grad_attn_in = grad_attn_in + lax.dot_general(
        grad_v_local, full_value, contract_cols, preferred_element_type=jnp.float32
    )
    grad_in_gain = jnp.sum(grad_attn_in * in_normed, axis=0)
    grad_input = grad_mid + norm_back(
        grad_attn_in * full_in_gain.astype(jnp.float32), in_normed, in_scale
    )
    part_in, part_query, part_key, part_value, part_output = (
        lax.psum_scatter(grad_in_gain, ("ctx", "fsdp"), scatter_dimension=0, tiled=True),
        lax.psum_scatter(grad_query_w, ("ctx", "fsdp"), scatter_dimension=0, tiled=True),
        lax.psum_scatter(grad_key_w, ("ctx", "fsdp"), scatter_dimension=0, tiled=True),
        lax.psum_scatter(grad_value_w, ("ctx", "fsdp"), scatter_dimension=0, tiled=True),
        lax.psum_scatter(grad_output, ("ctx", "fsdp"), scatter_dimension=0, tiled=True),
    )
    sum_q_gain, sum_k_gain = lax.psum((grad_q_gain, grad_k_gain), ("ctx", "fsdp"))
    return (
        output.reshape(seq_count, tok_rows, model_width),
        grad_input.reshape(seq_count, tok_rows, model_width),
        part_in,
        part_query,
        part_key,
        part_value,
        part_output,
        sum_q_gain,
        sum_k_gain,
        part_post,
        part_gate,
        part_up,
        part_down,
    )


MESH = pl.DeviceIdType.MESH
SUBS = 2


def ring_position(index, size):
    column, line = lax.rem(index, 2), lax.div(index, 2)
    return column * (line + 1) + (1 - column) * lax.rem(size - line, size)


def ring_member(position, size):
    late = lax.div(position + size // 2 - 1, size)
    beyond = lax.div(position + size - 1, size)
    return beyond * (1 - late) * (2 * position - 1) + late * 2 * (size - position)


class Ring:
    def __init__(self, size):
        self.size = size
        self.me = lax.axis_index("ctx")
        self.row = lax.axis_index("fsdp")
        self.position = ring_position(self.me, size)

    def member(self, way, steps):
        ahead = self.size - steps if way == 0 else steps
        return ring_member(lax.rem(self.position + ahead, self.size), self.size)

    def target(self, way):
        return (self.member(way, self.size - 1), self.row)

    def barrier(self):
        barrier = pltpu.get_barrier_semaphore()
        for way in range(2):
            pl.semaphore_signal(barrier, inc=1, device_id=self.target(way), device_id_type=MESH)
        pl.semaphore_wait(barrier, 2)


class GatherRing:
    def __init__(self, ring, own, out, send_sems, recv_sems):
        self.ring, self.own, self.out, self.send_sems, self.recv_sems = ring, own, out, send_sems, recv_sems
        self.half = own.shape[0] // 2
        self.sub = self.half // SUBS

    def copy(self, way, step, part, first=False):
        place = pl.ds(way * self.half + part * self.sub, self.sub)
        owner = self.ring.me if first else self.ring.member(way, step)
        source = self.own.at[place] if first else self.out.at[owner, place]
        return pltpu.make_async_remote_copy(
            src_ref=source,
            dst_ref=self.out.at[owner, place],
            send_sem=self.send_sems.at[way, step, part],
            recv_sem=self.recv_sems.at[way, step, part],
            device_id=self.ring.target(way),
            device_id_type=MESH,
        )

    def start(self, way):
        for part in range(SUBS):
            self.copy(way, 0, part, first=True).start()

    def step(self, step):
        for part in range(SUBS):
            for way in range(2):
                self.copy(way, step - 1, part).wait_recv()
                self.copy(way, step, part).start()

    def finish(self):
        last = self.ring.size - 2
        for part in range(SUBS):
            for way in range(2):
                self.copy(way, last, part).wait_recv()

        @pl.loop(0, last + 1)
        def _(step):
            for part in range(SUBS):
                for way in range(2):
                    self.copy(way, step, part).wait_send()

    def run(self):
        for way in range(2):
            self.start(way)

        @pl.loop(1, self.ring.size - 1)
        def _(step):
            self.step(step)

        self.finish()


def gather_sems(size):
    return [pltpu.SemaphoreType.DMA((2, size - 1, SUBS)), pltpu.SemaphoreType.DMA((2, size - 1, SUBS))]


class SumRing:
    def __init__(self, ring, compute, terms, outgoing, incoming, send_sems, recv_sems):
        self.ring, self.compute, self.terms = ring, compute, terms
        self.outgoing, self.incoming, self.send_sems, self.recv_sems = outgoing, incoming, send_sems, recv_sems
        self.half = terms.shape[1]
        self.sub = self.half // SUBS

    def copy(self, way, step, part):
        place = pl.ds(part * self.sub, self.sub)
        return pltpu.make_async_remote_copy(
            src_ref=self.outgoing.at[way, step, place],
            dst_ref=self.incoming.at[way, step, place],
            send_sem=self.send_sems.at[way, step, part],
            recv_sem=self.recv_sems.at[way, step, part],
            device_id=self.ring.target(way),
            device_id_type=MESH,
        )

    def terms_of(self, step):
        self.compute([self.ring.member(way, step + 1) for way in range(2)])

    def begin(self):
        self.terms_of(0)
        for part in range(SUBS):
            place = pl.ds(part * self.sub, self.sub)
            for way in range(2):
                self.outgoing[way, 0, place] = self.terms[way, place].astype(jnp.bfloat16)
                self.copy(way, 0, part).start()

    def step(self, step):
        self.terms_of(step)
        for part in range(SUBS):
            place = pl.ds(part * self.sub, self.sub)
            for way in range(2):
                self.copy(way, step - 1, part).wait_recv()
                total = self.terms[way, place] + self.incoming[way, step - 1, place].astype(jnp.float32)
                self.outgoing[way, step, place] = total.astype(jnp.bfloat16)
                self.copy(way, step, part).start()

    def last_terms(self):
        self.compute([self.ring.me, self.ring.me])

    def result(self, way):
        last = self.ring.size - 2
        for part in range(SUBS):
            self.copy(way, last, part).wait_recv()
        return self.terms[way] + self.incoming[way, last].astype(jnp.float32)

    def finish(self):
        @pl.loop(0, self.ring.size - 1)
        def _(step):
            for part in range(SUBS):
                for way in range(2):
                    self.copy(way, step, part).wait_send()

    def run(self):
        self.begin()

        @pl.loop(1, self.ring.size - 1)
        def _(step):
            self.step(step)

        self.last_terms()


def sum_scratch(size, rows, width):
    half = rows // 2
    return [
        pltpu.VMEM((2, half, width), jnp.float32),
        pltpu.VMEM((2, size - 1, half, width), jnp.bfloat16),
        pltpu.VMEM((2, size - 1, half, width), jnp.bfloat16),
        pltpu.SemaphoreType.DMA((2, size - 1, SUBS)),
        pltpu.SemaphoreType.DMA((2, size - 1, SUBS)),
    ]


TILE = 512


def row_terms(left, weight, terms):
    half = terms.shape[1]

    def compute(members):
        lines = jnp.concatenate([left[members[way], way * half : (way + 1) * half] for way in range(2)], axis=0)

        @pl.loop(0, weight.shape[1] // TILE)
        def _(tile):
            columns = pl.ds(pl.multiple_of(tile * TILE, TILE), TILE)
            product = jnp.dot(lines, weight[:, columns], preferred_element_type=jnp.float32)
            for way in range(2):
                terms[way, :, columns] = product[way * half : (way + 1) * half]

    return compute


def row_terms_t(left, weight, terms):
    half = terms.shape[1]

    def compute(members):
        lines = jnp.concatenate([left[members[way], way * half : (way + 1) * half] for way in range(2)], axis=0)

        @pl.loop(0, weight.shape[0] // TILE)
        def _(tile):
            columns = pl.ds(pl.multiple_of(tile * TILE, TILE), TILE)
            product = lax.dot_general(
                lines, weight[columns, :], (((1,), (1,)), ((), ())), preferred_element_type=jnp.float32
            )
            for way in range(2):
                terms[way, :, columns] = product[way * half : (way + 1) * half]

    return compute


VMEM_SPEC = pl.BlockSpec(memory_space=pltpu.VMEM)
ANY_SPEC = pl.BlockSpec(memory_space=pl.ANY)


def attention_out_kernel(size, attn, weight, residual, gain, mid_out, gathered, own, *scratch):
    sums, (gather_send, gather_recv, own_sem) = scratch[:5], scratch[5:]
    ring = Ring(size)
    ring.barrier()
    half = own.shape[0] // 2
    summing = SumRing(ring, row_terms(attn, weight, sums[0]), *sums)
    gathering = GatherRing(ring, own, gathered, gather_send, gather_recv)
    summing.run()
    for way in range(2):
        place = slice(way * half, (way + 1) * half)
        mid = summing.result(way) + residual[place].astype(jnp.float32)
        mid_out[place] = mid
        scale = lax.rsqrt(jnp.mean(mid * mid, axis=-1, keepdims=True) + EPS)
        own[place] = (mid * scale * gain[...]).astype(jnp.bfloat16)
        gathering.start(way)
    keep = pltpu.make_async_copy(own, gathered.at[ring.me], own_sem)
    keep.start()

    @pl.loop(1, size - 1)
    def _(step):
        gathering.step(step)

    gathering.finish()
    summing.finish()
    keep.wait()


def attention_out(attn, weight, residual, gain):
    size = lax.axis_size("ctx")
    rows, width = residual.shape
    return pl.pallas_call(
        functools.partial(attention_out_kernel, size),
        out_shape=[
            jax.ShapeDtypeStruct((rows, width), jnp.float32),
            jax.ShapeDtypeStruct((size, rows, width), jnp.bfloat16),
        ],
        in_specs=[VMEM_SPEC] * 4,
        out_specs=[VMEM_SPEC, ANY_SPEC],
        scratch_shapes=[pltpu.VMEM((rows, width), jnp.bfloat16)]
        + sum_scratch(size, rows, width)
        + gather_sems(size)
        + [pltpu.SemaphoreType.DMA],
        compiler_params=pltpu.CompilerParams(
            collective_id=1, has_side_effects=True, vmem_limit_bytes=56 * 1024 * 1024
        ),
    )(attn.reshape(size, rows, -1), weight, residual, gain.reshape(1, width))


def ctx_peer(ring, ahead):
    return lax.rem(ring.me + ahead, ring.size)


def across(row, n_fsdp):
    return lax.rem(row + n_fsdp // 2, n_fsdp)


def beside(row):
    return row + 1 - 2 * lax.rem(row, 2)


def remote(source, target, send_sem, recv_sem, device):
    return pltpu.make_async_remote_copy(
        src_ref=source,
        dst_ref=target,
        send_sem=send_sem,
        recv_sem=recv_sem,
        device_id=device,
        device_id_type=MESH,
    )


def greet(devices):
    barrier = pltpu.get_barrier_semaphore()
    for device in devices:
        pl.semaphore_signal(barrier, inc=1, device_id=device, device_id_type=MESH)
    pl.semaphore_wait(barrier, len(devices))


def near_devices(ring, n_fsdp):
    return [(ctx_peer(ring, ahead), ring.row) for ahead in range(1, ring.size)] + [
        (ring.me, across(ring.row, n_fsdp)),
        (ring.me, beside(ring.row)),
    ]


class Others:
    def __init__(self, ring, n_fsdp):
        self.ring, self.n_fsdp, self.count = ring, n_fsdp, ring.size * n_fsdp
        self.index = ring.me * n_fsdp + ring.row

    def each(self, act):
        @pl.loop(0, self.count)
        def _(other):
            @pl.when(other != self.index)
            def _():
                act(other, (lax.div(other, self.n_fsdp), lax.rem(other, self.n_fsdp)))

    def greet(self):
        barrier = pltpu.get_barrier_semaphore()
        self.each(lambda other, device: pl.semaphore_signal(barrier, inc=1, device_id=device, device_id_type=MESH))
        pl.semaphore_wait(barrier, self.count - 1)


class Rows:
    def __init__(self, ring, n_fsdp, shard, out, send_sems, recv_sems):
        own, far, twin = ring.row, across(ring.row, n_fsdp), beside(ring.row)
        self.keep = pltpu.make_async_copy(shard, out.at[own], send_sems.at[3])
        self.to_far = remote(shard, out.at[own], send_sems.at[0], recv_sems.at[0], (ring.me, far))
        self.to_twin = remote(shard, out.at[own], send_sems.at[1], recv_sems.at[1], (ring.me, twin))
        self.pass_on = remote(out.at[far], out.at[far], send_sems.at[2], recv_sems.at[2], (ring.me, twin))

    def begin(self):
        self.keep.start()
        self.to_far.start()
        self.to_twin.start()

    def relay(self):
        self.to_far.wait_recv()
        self.pass_on.start()

    def finish(self):
        self.keep.wait()
        self.to_far.wait_send()
        self.to_twin.wait()
        self.pass_on.wait()


def rows_sems():
    return [pltpu.SemaphoreType.DMA((4,)), pltpu.SemaphoreType.DMA((3,))]


class Columns:
    def __init__(self, ring, n_fsdp, shards, out, send_sems, recv_sems, link_send, link_recv):
        self.ring, self.shards, self.out, self.send_sems, self.recv_sems = ring, shards, out, send_sems, recv_sems
        own, far, twin = ring.row, across(ring.row, n_fsdp), beside(ring.row)
        self.widths = [shard.shape[1] // ring.size for shard in shards]
        self.to_far = remote(out.at[:, own], out.at[:, own], link_send.at[0], link_recv.at[0], (ring.me, far))
        self.to_twin = remote(out.at[:, own], out.at[:, own], link_send.at[1], link_recv.at[1], (ring.me, twin))
        self.pass_on = remote(out.at[:, far], out.at[:, far], link_send.at[2], link_recv.at[2], (ring.me, twin))

    def piece(self, which, ahead):
        member = ctx_peer(self.ring, ahead)
        width = self.widths[which]
        start = sum(self.widths[:which])
        source = self.shards[which].at[:, pl.ds(pl.multiple_of(member * width, width), width)]
        target = self.out.at[self.ring.me, self.ring.row, :, pl.ds(start, width)]
        if ahead == 0:
            return pltpu.make_async_copy(source, target, self.send_sems.at[which, 0])
        return remote(
            source, target, self.send_sems.at[which, ahead], self.recv_sems.at[which, ahead], (member, self.ring.row)
        )

    def begin(self):
        for ahead in range(self.ring.size):
            for which in range(len(self.shards)):
                self.piece(which, ahead).start()

    def spread(self):
        for ahead in range(self.ring.size):
            for which in range(len(self.shards)):
                if ahead:
                    self.piece(which, ahead).wait_recv()
                else:
                    self.piece(which, ahead).wait()
        self.to_far.start()
        self.to_twin.start()

    def relay(self):
        self.to_far.wait_recv()
        self.pass_on.start()

    def finish(self):
        for ahead in range(1, self.ring.size):
            for which in range(len(self.shards)):
                self.piece(which, ahead).wait_send()
        self.to_far.wait_send()
        self.to_twin.wait()
        self.pass_on.wait()


def columns_sems(size, count):
    return [
        pltpu.SemaphoreType.DMA((count, size)),
        pltpu.SemaphoreType.DMA((count, size)),
        pltpu.SemaphoreType.DMA((3,)),
        pltpu.SemaphoreType.DMA((3,)),
    ]


class RowGrads:
    def __init__(self, ring, n_fsdp, part, from_twin, to_far, from_far, send_sems, recv_sems):
        own, far, twin = ring.row, across(ring.row, n_fsdp), beside(ring.row)
        self.part, self.from_twin, self.to_far, self.from_far = part, from_twin, to_far, from_far
        self.own, self.far = own, far
        twin_far = across(twin, n_fsdp)
        self.first = [
            remote(part.at[twin], from_twin.at[0], send_sems.at[0], recv_sems.at[0], (ring.me, twin)),
            remote(part.at[twin_far], from_twin.at[1], send_sems.at[1], recv_sems.at[1], (ring.me, twin)),
        ]
        self.second = remote(to_far, from_far, send_sems.at[2], recv_sems.at[2], (ring.me, far))

    def begin(self):
        self.first[1].start()
        self.first[0].start()

    def cross(self):
        self.first[1].wait_recv()
        self.to_far[...] = (
            self.part[self.far].astype(jnp.float32) + self.from_twin[1].astype(jnp.float32)
        ).astype(jnp.bfloat16)
        self.second.start()

    def result(self):
        self.first[0].wait_recv()
        self.second.wait_recv()
        return (
            self.part[self.own].astype(jnp.float32)
            + self.from_twin[0].astype(jnp.float32)
            + self.from_far[...].astype(jnp.float32)
        )

    def finish(self):
        for copy in self.first + [self.second]:
            copy.wait_send()


def row_grads_scratch(shape):
    return [
        pltpu.VMEM((2,) + shape, jnp.bfloat16),
        pltpu.VMEM(shape, jnp.bfloat16),
        pltpu.VMEM(shape, jnp.bfloat16),
        pltpu.SemaphoreType.DMA((3,)),
        pltpu.SemaphoreType.DMA((3,)),
    ]


class ColumnGrads:
    def __init__(self, ring, summing, total, arrived, send_sems, recv_sems):
        self.ring, self.summing, self.total, self.arrived = ring, summing, total, arrived
        self.send_sems, self.recv_sems = send_sems, recv_sems

    def piece(self, ahead):
        member = ctx_peer(self.ring, ahead)
        return remote(
            self.total.at[member],
            self.arrived.at[self.ring.me],
            self.send_sems.at[ahead],
            self.recv_sems.at[ahead],
            (member, self.ring.row),
        )

    def begin(self):
        self.summing.begin()

    def cross(self):
        self.summing.cross()

    def deal(self):
        self.total[...] = self.summing.result().astype(jnp.bfloat16)
        for ahead in range(1, self.ring.size):
            self.piece(ahead).start()
        self.arrived[self.ring.me] = self.total[self.ring.me]

    def collect(self, outs):
        for ahead in range(1, self.ring.size):
            self.piece(ahead).wait_recv()
        start = 0
        for out in outs:
            width = out.shape[1] // self.ring.size
            for member in range(self.ring.size):
                out[:, member * width : (member + 1) * width] = self.arrived[member, :, start : start + width].astype(
                    jnp.float32
                )
            start += width

    def finish(self):
        self.summing.finish()
        for ahead in range(1, self.ring.size):
            self.piece(ahead).wait_send()


def column_grads_scratch(shape):
    return row_grads_scratch(shape) + [
        pltpu.VMEM(shape, jnp.bfloat16),
        pltpu.VMEM(shape, jnp.bfloat16),
        pltpu.SemaphoreType.DMA((shape[0],)),
        pltpu.SemaphoreType.DMA((shape[0],)),
    ]


def params(collective_id):
    return pltpu.CompilerParams(
        collective_id=collective_id, has_side_effects=True, vmem_limit_bytes=60 * 1024 * 1024
    )


def front_kernel(size, n_fsdp, hidden, small, w_query, w_key, w_value, w_output, attn_in, all_small, columns_out, rows_out, *scratch):
    own, gain, gather_send, gather_recv, own_sem, small_send, small_recv = scratch[:7]
    ring = Ring(size)
    others = Others(ring, n_fsdp)
    columns = Columns(ring, n_fsdp, [w_query, w_key, w_value], columns_out, *scratch[7:11])
    rows = Rows(ring, n_fsdp, w_output, rows_out, *scratch[11:13])
    gathering = GatherRing(ring, own, attn_in, gather_send, gather_recv)
    others.greet()

    def tiny(other, device):
        return remote(small, all_small.at[others.index], small_send.at[other], small_recv.at[others.index], device)

    others.each(lambda other, device: tiny(other, device).start())
    columns.begin()
    rows.begin()
    all_small[others.index] = small[...]
    others.each(
        lambda other, device: remote(
            small, all_small.at[other], small_send.at[other], small_recv.at[other], device
        ).wait_recv()
    )
    for pair in range(others.count // 2):
        gain[:, pair * 128 : (pair + 1) * 128] = all_small[2 * pair, 0:1] + all_small[2 * pair + 1, 0:1]
    half = own.shape[0] // 2
    for way in range(2):
        place = slice(way * half, (way + 1) * half)
        values = hidden[place].astype(jnp.float32)
        scale = lax.rsqrt(jnp.mean(values * values, axis=-1, keepdims=True) + EPS)
        own[place] = (values * scale * gain[...]).astype(jnp.bfloat16)
        gathering.start(way)
    keep = pltpu.make_async_copy(own, attn_in.at[ring.me], own_sem)
    keep.start()
    gathering.step(1)
    gathering.step(2)
    columns.spread()
    gathering.step(3)
    gathering.step(4)
    rows.relay()

    @pl.loop(5, size - 1)
    def _(step):
        gathering.step(step)

    columns.relay()
    gathering.finish()
    others.each(lambda other, device: tiny(other, device).wait_send())
    columns.finish()
    rows.finish()
    keep.wait()


def front(hidden, small, w_query, w_key, w_value, w_output):
    size, n_fsdp = lax.axis_size("ctx"), lax.axis_size("fsdp")
    rows, width = hidden.shape
    depth = w_query.shape[0]
    share = (w_query.shape[1] + w_key.shape[1] + w_value.shape[1]) // size
    return pl.pallas_call(
        functools.partial(front_kernel, size, n_fsdp),
        out_shape=[
            jax.ShapeDtypeStruct((size, rows, width), jnp.bfloat16),
            jax.ShapeDtypeStruct((size * n_fsdp,) + small.shape, jnp.float32),
            jax.ShapeDtypeStruct((size, n_fsdp, depth, share), jnp.bfloat16),
            jax.ShapeDtypeStruct((n_fsdp,) + w_output.shape, jnp.bfloat16),
        ],
        in_specs=[VMEM_SPEC, VMEM_SPEC] + [ANY_SPEC] * 4,
        out_specs=[ANY_SPEC, VMEM_SPEC, ANY_SPEC, ANY_SPEC],
        scratch_shapes=[pltpu.VMEM((rows, width), jnp.bfloat16), pltpu.VMEM((1, width), jnp.float32)]
        + gather_sems(size)
        + [
            pltpu.SemaphoreType.DMA,
            pltpu.SemaphoreType.DMA((size * n_fsdp,)),
            pltpu.SemaphoreType.DMA((size * n_fsdp,)),
        ]
        + columns_sems(size, 3)
        + rows_sems(),
        compiler_params=params(2),
    )(hidden, small, w_query, w_key, w_value, w_output)


def second_kernel(size, n_fsdp, cotangent, w_gate, w_up, w_down, grad_out, columns_out, rows_out, *scratch):
    gather_send, gather_recv, own_sem = scratch[:3]
    ring = Ring(size)
    columns = Columns(ring, n_fsdp, [w_gate, w_up], columns_out, *scratch[3:7])
    rows = Rows(ring, n_fsdp, w_down, rows_out, *scratch[7:9])
    gathering = GatherRing(ring, cotangent, grad_out, gather_send, gather_recv)
    greet(near_devices(ring, n_fsdp))
    columns.begin()
    rows.begin()
    for way in range(2):
        gathering.start(way)
    keep = pltpu.make_async_copy(cotangent, grad_out.at[ring.me], own_sem)
    keep.start()
    gathering.step(1)
    gathering.step(2)
    gathering.step(3)
    columns.spread()
    rows.relay()

    @pl.loop(4, size - 1)
    def _(step):
        gathering.step(step)

    gathering.finish()
    columns.relay()
    columns.finish()
    rows.finish()
    keep.wait()


def second(cotangent, w_gate, w_up, w_down):
    size, n_fsdp = lax.axis_size("ctx"), lax.axis_size("fsdp")
    rows, width = cotangent.shape
    depth = w_gate.shape[0]
    share = (w_gate.shape[1] + w_up.shape[1]) // size
    return pl.pallas_call(
        functools.partial(second_kernel, size, n_fsdp),
        out_shape=[
            jax.ShapeDtypeStruct((size, rows, width), jnp.bfloat16),
            jax.ShapeDtypeStruct((size, n_fsdp, depth, share), jnp.bfloat16),
            jax.ShapeDtypeStruct((n_fsdp,) + w_down.shape, jnp.bfloat16),
        ],
        in_specs=[ANY_SPEC] * 4,
        out_specs=[ANY_SPEC] * 3,
        scratch_shapes=gather_sems(size) + [pltpu.SemaphoreType.DMA] + columns_sems(size, 2) + rows_sems(),
        compiler_params=params(3),
    )(cotangent, w_gate, w_up, w_down)


def layer_out_kernel(size, inner, weight, mid, out, *sums):
    ring = Ring(size)
    ring.barrier()
    summing = SumRing(ring, row_terms(inner, weight, sums[0]), *sums)
    summing.run()
    half = out.shape[0] // 2
    for way in range(2):
        place = slice(way * half, (way + 1) * half)
        out[place] = (mid[place] + summing.result(way)).astype(jnp.bfloat16)
    summing.finish()


def layer_out(inner, weight, mid):
    size = lax.axis_size("ctx")
    rows, width = mid.shape
    return pl.pallas_call(
        functools.partial(layer_out_kernel, size),
        out_shape=jax.ShapeDtypeStruct((rows, width), jnp.bfloat16),
        in_specs=[VMEM_SPEC] * 3,
        out_specs=VMEM_SPEC,
        scratch_shapes=sum_scratch(size, rows, width),
        compiler_params=params(4),
    )(inner.reshape(size, rows, -1), weight, mid)


def norm_pull(grad_normed, normed, scale):
    return scale * (grad_normed - normed * jnp.mean(grad_normed * normed, axis=-1, keepdims=True))


def middle_kernel(
    size,
    n_fsdp,
    grads,
    weight,
    mid,
    cotangent,
    gain,
    column_part,
    row_part,
    grad_mid,
    grad_gain,
    gathered,
    gate_out,
    up_out,
    down_out,
    own,
    *scratch,
):
    sums, (gather_send, gather_recv, own_sem) = scratch[:5], scratch[5:8]
    ring = Ring(size)
    greet(near_devices(ring, n_fsdp))
    half = own.shape[0] // 2
    columns = ColumnGrads(ring, RowGrads(ring, n_fsdp, column_part, *scratch[8:13]), *scratch[13:17])
    rows = RowGrads(ring, n_fsdp, row_part, *scratch[17:22])
    columns.begin()
    rows.begin()
    summing = SumRing(ring, row_terms_t(grads, weight, sums[0]), *sums)
    gathering = GatherRing(ring, own, gathered, gather_send, gather_recv)
    summing.begin()
    summing.step(1)
    columns.cross()
    rows.cross()

    @pl.loop(2, size - 1)
    def _(step):
        summing.step(step)

    summing.last_terms()
    gain_sum = jnp.zeros_like(grad_gain)
    for way in range(2):
        place = slice(way * half, (way + 1) * half)
        pulled = summing.result(way)
        values = mid[place]
        scale = lax.rsqrt(jnp.mean(values * values, axis=-1, keepdims=True) + EPS)
        normed = values * scale
        gain_sum = gain_sum + jnp.sum(pulled * normed, axis=0, keepdims=True)
        total = cotangent[place].astype(jnp.float32) + norm_pull(pulled * gain[...], normed, scale)
        grad_mid[place] = total
        own[place] = total.astype(jnp.bfloat16)
        gathering.start(way)
    grad_gain[...] = gain_sum
    keep = pltpu.make_async_copy(own, gathered.at[ring.me], own_sem)
    keep.start()
    gathering.step(1)
    columns.deal()
    gathering.step(2)
    down_out[...] = rows.result()

    @pl.loop(3, size - 1)
    def _(step):
        gathering.step(step)

    gathering.finish()
    columns.collect([gate_out, up_out])
    summing.finish()
    columns.finish()
    rows.finish()
    keep.wait()


def middle(grads, weight, mid, cotangent, gain, column_part, row_part):
    size, n_fsdp = lax.axis_size("ctx"), lax.axis_size("fsdp")
    rows, width = mid.shape
    share = column_part.shape[3]
    depth = column_part.shape[2]
    return pl.pallas_call(
        functools.partial(middle_kernel, size, n_fsdp),
        out_shape=[
            jax.ShapeDtypeStruct((rows, width), jnp.float32),
            jax.ShapeDtypeStruct((1, width), jnp.float32),
            jax.ShapeDtypeStruct((size, rows, width), jnp.bfloat16),
            jax.ShapeDtypeStruct((depth, share // 2 * size), jnp.float32),
            jax.ShapeDtypeStruct((depth, share // 2 * size), jnp.float32),
            jax.ShapeDtypeStruct(row_part.shape[1:], jnp.float32),
        ],
        in_specs=[VMEM_SPEC] * 7,
        out_specs=[VMEM_SPEC, VMEM_SPEC, ANY_SPEC, VMEM_SPEC, VMEM_SPEC, VMEM_SPEC],
        scratch_shapes=[pltpu.VMEM((rows, width), jnp.bfloat16)]
        + sum_scratch(size, rows, width)
        + gather_sems(size)
        + [pltpu.SemaphoreType.DMA]
        + column_grads_scratch((size, depth, share))
        + row_grads_scratch(row_part.shape[1:]),
        compiler_params=params(5),
    )(grads.reshape(size, rows, -1), weight, mid, cotangent, gain.reshape(1, width), column_part, row_part)


def back_kernel(
    size,
    n_fsdp,
    grads,
    weight,
    hidden,
    grad_mid,
    gain,
    post_sum,
    q_sum,
    k_sum,
    column_part,
    row_part,
    grad_hidden,
    gains_out,
    query_out,
    key_out,
    value_out,
    output_out,
    small,
    all_small,
    small_send,
    small_recv,
    *scratch,
):
    sums = scratch[:5]
    ring = Ring(size)
    others = Others(ring, n_fsdp)
    others.greet()
    half = hidden.shape[0] // 2
    columns = ColumnGrads(ring, RowGrads(ring, n_fsdp, column_part, *scratch[5:10]), *scratch[10:14])
    rows = RowGrads(ring, n_fsdp, row_part, *scratch[14:19])
    columns.begin()
    rows.begin()
    summing = SumRing(ring, row_terms_t(grads, weight, sums[0]), *sums)
    summing.begin()
    summing.step(1)
    columns.cross()
    rows.cross()
    summing.step(2)
    summing.step(3)
    columns.deal()

    @pl.loop(4, size - 1)
    def _(step):
        summing.step(step)

    output_out[...] = rows.result()
    summing.last_terms()
    gain_sum = jnp.zeros_like(post_sum)
    for way in range(2):
        place = slice(way * half, (way + 1) * half)
        pulled = summing.result(way)
        values = hidden[place].astype(jnp.float32)
        scale = lax.rsqrt(jnp.mean(values * values, axis=-1, keepdims=True) + EPS)
        normed = values * scale
        gain_sum = gain_sum + jnp.sum(pulled * normed, axis=0, keepdims=True)
        grad_hidden[place] = grad_mid[place] + norm_pull(pulled * gain[...], normed, scale)
    for pair in range(others.count // 2):
        lanes = slice(pair * 128, (pair + 1) * 128)
        small[pair, 0:1] = gain_sum[:, lanes]
        small[pair, 1:2] = post_sum[:, lanes]
        small[pair, 2:3] = q_sum[...]
        small[pair, 3:4] = k_sum[...]
        small[pair, 4:8] = jnp.zeros((4, 128), jnp.float32)

    def tiny(other, device):
        return remote(
            small.at[lax.div(other, 2)],
            all_small.at[others.index],
            small_send.at[other],
            small_recv.at[others.index],
            device,
        )

    others.each(lambda other, device: tiny(other, device).start())
    all_small[others.index] = small[lax.div(others.index, 2)]
    columns.collect([query_out, key_out, value_out])
    others.each(
        lambda other, device: remote(
            small.at[0], all_small.at[other], small_send.at[other], small_recv.at[other], device
        ).wait_recv()
    )
    gains_out[...] = jnp.sum(all_small[...], axis=0)
    others.each(lambda other, device: tiny(other, device).wait_send())
    summing.finish()
    columns.finish()
    rows.finish()


def back(grads, weight, hidden, grad_mid, gain, post_sum, q_sum, k_sum, column_part, row_part, widths):
    size, n_fsdp = lax.axis_size("ctx"), lax.axis_size("fsdp")
    rows, width = hidden.shape
    share = column_part.shape[3]
    depth = column_part.shape[2]
    count = size * n_fsdp
    return pl.pallas_call(
        functools.partial(back_kernel, size, n_fsdp),
        out_shape=[
            jax.ShapeDtypeStruct((rows, width), jnp.float32),
            jax.ShapeDtypeStruct((8, 128), jnp.float32),
        ]
        + [jax.ShapeDtypeStruct((depth, full), jnp.float32) for full in widths]
        + [jax.ShapeDtypeStruct(row_part.shape[1:], jnp.float32)],
        in_specs=[VMEM_SPEC] * 10,
        out_specs=[VMEM_SPEC] * 6,
        scratch_shapes=[
            pltpu.VMEM((count // 2, 8, 128), jnp.float32),
            pltpu.VMEM((count, 8, 128), jnp.float32),
            pltpu.SemaphoreType.DMA((count,)),
            pltpu.SemaphoreType.DMA((count,)),
        ]
        + sum_scratch(size, rows, width)
        + column_grads_scratch((size, depth, share))
        + row_grads_scratch(row_part.shape[1:]),
        compiler_params=params(6),
    )(
        grads.reshape(size, rows, -1),
        weight,
        hidden,
        grad_mid,
        gain.reshape(1, width),
        post_sum.reshape(1, width),
        q_sum.reshape(1, -1),
        k_sum.reshape(1, -1),
        column_part,
        row_part,
    )


def tp_body(
    hidden_in,
    block_of,
    in_gain,
    w_query,
    w_key,
    w_value,
    w_output,
    q_gain,
    k_gain,
    post_gain,
    w_gate,
    w_up,
    w_down,
    cotangent,
):
    seq_count, tok_rows, model_width = hidden_in.shape
    n_ctx = lax.axis_size("ctx")
    n_fsdp = lax.axis_size("fsdp")
    block_rows = tok_rows // 2
    rows = seq_count * tok_rows
    seq_rows = n_ctx * rows
    head_dim = q_gain.shape[0]
    q_heads = w_query.shape[1] // head_dim // n_ctx
    kv_heads = w_key.shape[1] // head_dim // n_ctx
    group = q_heads // kv_heads
    q_scale = head_dim ** (-0.5)
    f32, bf16 = jnp.float32, jnp.bfloat16
    contract_rows = (((0,), (0,)), ((), ()))
    contract_cols = (((1,), (1,)), ((), ()))
    hidden = hidden_in.reshape(rows, model_width)
    cot_local = cotangent.reshape(rows, model_width)
    depth = w_query.shape[0]

    side = lax.rem(lax.axis_index("fsdp"), 2)
    lanes = jnp.arange(2 * depth, dtype=jnp.int32)
    pair_mask = lax.div(lanes, depth) == side
    small = jnp.zeros((8, 2 * depth), f32)
    small = small.at[0].set(jnp.where(pair_mask, jnp.tile(in_gain.astype(f32), 2), 0.0))
    small = small.at[1].set(jnp.where(pair_mask, jnp.tile(post_gain.astype(f32), 2), 0.0))
    small = small.at[2, :2].set(block_of[0].astype(f32))

    attn_in, all_small, mine_qkv, mine_output = front(hidden, small, w_query, w_key, w_value, w_output)
    attn_in = attn_in.reshape(seq_rows, model_width)
    mine_qkv = mine_qkv.reshape(model_width, -1)
    mine_output = mine_output.reshape(-1, model_width)
    paired = all_small.reshape(n_ctx * n_fsdp // 2, 2, 8, 2 * depth).sum(axis=1)
    full_in_gain, full_post = paired[:, 0].reshape(model_width), paired[:, 1].reshape(model_width)
    own_row = lax.dynamic_index_in_dim(
        all_small.reshape(n_ctx, n_fsdp, 8, 2 * depth), lax.axis_index("fsdp"), axis=1, keepdims=False
    )
    all_blocks = own_row[:, 2, :2].reshape(2 * n_ctx).astype(jnp.int32)
    offsets = jnp.arange(block_rows, dtype=jnp.int32)
    positions = (all_blocks[:, None] * block_rows + offsets[None, :]).reshape(seq_rows)
    cosine, sine = rope_tables(positions, head_dim)

    grad_out, mine_gu, mine_down = second(cot_local, w_gate, w_up, w_down)
    grad_out = grad_out.reshape(seq_rows, model_width)
    mine_gu = mine_gu.reshape(model_width, -1)
    mine_down = mine_down.reshape(-1, model_width)
    ff = mine_down.shape[0]

    qkv = jnp.dot(attn_in, mine_qkv, preferred_element_type=f32)
    q_width, k_width = q_heads * head_dim, kv_heads * head_dim
    q_raw = qkv[:, :q_width].reshape(seq_rows, q_heads, head_dim)
    k_raw = qkv[:, q_width : q_width + k_width].reshape(seq_rows, kv_heads, head_dim)
    values = qkv[:, q_width + k_width :].astype(bf16).reshape(seq_rows, kv_heads, head_dim)
    q_rms = lax.rsqrt(jnp.mean(q_raw * q_raw, axis=-1, keepdims=True) + EPS)
    q_unit = q_raw * q_rms
    queries = (rotate(q_unit * q_gain.astype(f32), cosine, sine) * q_scale).astype(bf16)
    queries = queries.reshape(seq_rows, kv_heads, group, head_dim)
    k_rms = lax.rsqrt(jnp.mean(k_raw * k_raw, axis=-1, keepdims=True) + EPS)
    k_unit = k_raw * k_rms
    keys = rotate(k_unit * k_gain.astype(f32), cosine, sine).astype(bf16)

    visible = positions[None, :] <= positions[:, None]
    scores = jnp.einsum("qhgd,khd->hgqk", queries, keys, preferred_element_type=f32)
    scores = jnp.where(visible, scores, -1e30)
    peak = jnp.max(scores, axis=-1, keepdims=True)
    weights = jnp.exp(scores - peak)
    probs = weights / jnp.sum(weights, axis=-1, keepdims=True)
    attn = jnp.einsum("hgqk,khd->qhgd", probs.astype(bf16), values, preferred_element_type=f32)
    attn_bf = attn.reshape(seq_rows, q_heads * head_dim).astype(bf16)

    hidden_mid, mlp_in = attention_out(attn_bf, mine_output, hidden, full_post)
    mlp_in = mlp_in.reshape(seq_rows, model_width)

    gate_up = jnp.dot(mlp_in, mine_gu, preferred_element_type=f32)
    gate_pre, up_pre = gate_up[:, :ff], gate_up[:, ff:]
    sigmoid_gate = jax.nn.sigmoid(gate_pre)
    activated = gate_pre * sigmoid_gate
    inner = (activated * up_pre).astype(bf16)
    grad_inner = lax.dot_general(grad_out, mine_down, contract_cols, preferred_element_type=f32)
    grad_gate_pre = (grad_inner * up_pre * sigmoid_gate * (1.0 + gate_pre * (1.0 - sigmoid_gate))).astype(bf16)
    grad_up_pre = (grad_inner * activated).astype(bf16)
    grad_gu = jnp.concatenate([grad_gate_pre, grad_up_pre], axis=1)
    output = layer_out(inner, mine_down, hidden_mid)
    down_part = lax.dot_general(inner, grad_out, contract_rows, preferred_element_type=f32).astype(bf16)

    def by_owner(part):
        return part.reshape(n_ctx, n_fsdp, depth, -1).transpose(1, 0, 2, 3)

    gu_part = lax.dot_general(mlp_in, grad_gu, contract_rows, preferred_element_type=f32).astype(bf16)
    grad_mid, post_sum, grad_branch, part_gate, part_up, part_down = middle(
        grad_gu,
        mine_gu,
        hidden_mid,
        cot_local,
        full_post,
        by_owner(gu_part),
        down_part.reshape(n_fsdp, -1, model_width),
    )
    grad_branch = grad_branch.reshape(seq_rows, model_width)

    output_part = lax.dot_general(attn_bf, grad_branch, contract_rows, preferred_element_type=f32).astype(bf16)
    grad_attn = lax.dot_general(grad_branch, mine_output, contract_cols, preferred_element_type=f32).astype(bf16)
    grad_attn = grad_attn.reshape(seq_rows, kv_heads, group, head_dim)
    delta = jnp.einsum("qhgd,qhgd->hgq", grad_attn.astype(f32), attn)
    grad_probs = jnp.einsum("qhgd,khd->hgqk", grad_attn, values, preferred_element_type=f32)
    grad_scores = (probs * (grad_probs - delta[..., None])).astype(bf16)
    grad_queries = jnp.einsum("hgqk,khd->qhgd", grad_scores, keys, preferred_element_type=f32)
    grad_keys = jnp.einsum("hgqk,qhgd->khd", grad_scores, queries, preferred_element_type=f32)
    grad_values = jnp.einsum("hgqk,qhgd->khd", probs.astype(bf16), grad_attn, preferred_element_type=f32)

    grad_q_normed = rotate(grad_queries.reshape(seq_rows, q_heads, head_dim) * q_scale, cosine, -sine)
    q_sum = jnp.sum(grad_q_normed * q_unit, axis=(0, 1))
    grad_q_raw = norm_back(grad_q_normed * q_gain.astype(f32), q_unit, q_rms).astype(bf16).reshape(seq_rows, q_width)
    grad_k_normed = rotate(grad_keys, cosine, -sine)
    k_sum = jnp.sum(grad_k_normed * k_unit, axis=(0, 1))
    grad_k_raw = norm_back(grad_k_normed * k_gain.astype(f32), k_unit, k_rms).astype(bf16).reshape(seq_rows, k_width)
    grad_v = grad_values.astype(bf16).reshape(seq_rows, k_width)
    grad_qkv = jnp.concatenate([grad_q_raw, grad_k_raw, grad_v], axis=1)
    qkv_part = lax.dot_general(attn_in, grad_qkv, contract_rows, preferred_element_type=f32).astype(bf16)
    grad_input, gains, part_query, part_key, part_value, part_output = back(
        grad_qkv,
        mine_qkv,
        hidden,
        grad_mid,
        full_in_gain,
        post_sum,
        q_sum,
        k_sum,
        by_owner(qkv_part),
        output_part.reshape(n_fsdp, -1, model_width),
        [w_query.shape[1], w_key.shape[1], w_value.shape[1]],
    )
    part_in = lax.dynamic_slice_in_dim(gains[0], side * depth, depth)
    part_post = lax.dynamic_slice_in_dim(gains[1], side * depth, depth)
    return (
        output.reshape(seq_count, tok_rows, model_width),
        grad_input.reshape(seq_count, tok_rows, model_width),
        part_in,
        part_query,
        part_key,
        part_value,
        part_output,
        gains[2],
        gains[3],
        part_post,
        part_gate,
        part_up,
        part_down,
    )


def solution(mesh):
    body = tp_body if KV_HEADS % mesh.shape["ctx"] == 0 else gathered_weights_body
    return jax.shard_map(
        body,
        mesh=mesh,
        in_specs=(
            P("fsdp", "ctx", None),
            P("fsdp", "ctx"),
            P(("ctx", "fsdp")),
            P(("ctx", "fsdp"), None),
            P(("ctx", "fsdp"), None),
            P(("ctx", "fsdp"), None),
            P(("ctx", "fsdp"), None),
            P(),
            P(),
            P(("ctx", "fsdp")),
            P(("ctx", "fsdp"), None),
            P(("ctx", "fsdp"), None),
            P(("ctx", "fsdp"), None),
            P("fsdp", "ctx", None),
        ),
        out_specs=(
            P("fsdp", "ctx", None),
            P("fsdp", "ctx", None),
            P(("ctx", "fsdp")),
            P(("ctx", "fsdp"), None),
            P(("ctx", "fsdp"), None),
            P(("ctx", "fsdp"), None),
            P(("ctx", "fsdp"), None),
            P(),
            P(),
            P(("ctx", "fsdp")),
            P(("ctx", "fsdp"), None),
            P(("ctx", "fsdp"), None),
            P(("ctx", "fsdp"), None),
        ),
        check_vma=False,
    )
```

```python
import functools
import math

import jax
import jax.numpy as jnp
from jax import lax
from jax.experimental import pallas as pl
from jax.experimental.pallas import tpu as pltpu
from jax.sharding import PartitionSpec as P

EPS = 1e-06
THETA = 1000000.0
KV_HEADS = 8


def rope_tables(positions, width):
    half_width = width // 2
    inverse = THETA ** (-(jnp.arange(half_width, dtype=jnp.float32) * 2.0 / width))
    angles = positions.astype(jnp.float32)[:, None] * inverse[None, :]
    return (jnp.cos(angles), jnp.sin(angles))


def rotate(values, cosine, sine):
    half_width = values.shape[-1] // 2
    first = values[..., :half_width]
    second = values[..., half_width:]
    cos_wide = cosine[:, None, :]
    sin_wide = sine[:, None, :]
    return jnp.concatenate(
        [first * cos_wide - second * sin_wide, second * cos_wide + first * sin_wide], axis=-1
    )


def norm_back(grad_normed, normed, scale):
    return scale * (grad_normed - normed * jnp.mean(grad_normed * normed, axis=-1, keepdims=True))


def gathered_weights_body(
    hidden_in,
    block_of,
    in_gain,
    w_query,
    w_key,
    w_value,
    w_output,
    q_gain,
    k_gain,
    post_gain,
    w_gate,
    w_up,
    w_down,
    cotangent,
):
    seq_count = hidden_in.shape[0]
    tok_rows = hidden_in.shape[1]
    flat_rows = seq_count * tok_rows
    model_width = hidden_in.shape[2]
    block_rows = tok_rows // 2
    block_total = 2 * lax.axis_size("ctx")
    seq_len = block_total * block_rows
    head_dim = q_gain.shape[0]
    q_heads = w_query.shape[1] // head_dim
    kv_heads = w_key.shape[1] // head_dim
    group_size = q_heads // kv_heads
    tile_blocks = math.gcd(block_total, max(1, 512 // block_rows))
    tile_rows = tile_blocks * block_rows
    q_scale = head_dim ** (-0.5)
    contract_rows = (((0,), (0,)), ((), ()))
    contract_cols = (((1,), (1,)), ((), ()))
    offsets = jnp.arange(block_rows, dtype=jnp.int32)
    positions = (block_of[:, :, None] * block_rows + offsets[None, None, :]).reshape(flat_rows)
    cosine, sine = rope_tables(positions, head_dim)
    residual = hidden_in.reshape(flat_rows, model_width).astype(jnp.float32)
    full_in_gain, full_query, full_key, full_value, full_output = (
        lax.all_gather(in_gain, ("ctx", "fsdp"), axis=0, tiled=True),
        lax.all_gather(w_query, ("ctx", "fsdp"), axis=0, tiled=True),
        lax.all_gather(w_key, ("ctx", "fsdp"), axis=0, tiled=True),
        lax.all_gather(w_value, ("ctx", "fsdp"), axis=0, tiled=True),
        lax.all_gather(w_output, ("ctx", "fsdp"), axis=0, tiled=True),
    )
    in_scale = lax.rsqrt(jnp.mean(residual * residual, axis=-1, keepdims=True) + EPS)
    in_normed = residual * in_scale
    attn_in = (in_normed * full_in_gain.astype(jnp.float32)).astype(jnp.bfloat16)
    q_raw = jnp.dot(attn_in, full_query, preferred_element_type=jnp.float32).reshape(
        flat_rows, q_heads, head_dim
    )
    k_raw = jnp.dot(attn_in, full_key, preferred_element_type=jnp.float32).reshape(
        flat_rows, kv_heads, head_dim
    )
    v_local = jnp.dot(attn_in, full_value, preferred_element_type=jnp.float32).astype(jnp.bfloat16)
    q_rms = lax.rsqrt(jnp.mean(q_raw * q_raw, axis=-1, keepdims=True) + EPS)
    q_unit = q_raw * q_rms
    queries = (rotate(q_unit * q_gain.astype(jnp.float32), cosine, sine) * q_scale).astype(
        jnp.bfloat16
    )
    k_rms = lax.rsqrt(jnp.mean(k_raw * k_raw, axis=-1, keepdims=True) + EPS)
    k_unit = k_raw * k_rms
    keys_local = rotate(k_unit * k_gain.astype(jnp.float32), cosine, sine).astype(jnp.bfloat16)
    all_keys, all_values, all_slots = (
        lax.all_gather(
            keys_local.reshape(seq_count, tok_rows, kv_heads * head_dim), "ctx", axis=1, tiled=True
        ),
        lax.all_gather(
            v_local.reshape(seq_count, tok_rows, kv_heads * head_dim), "ctx", axis=1, tiled=True
        ),
        lax.all_gather(block_of, "ctx", axis=1, tiled=True),
    )

    def tile_scores(query_tile, key_tile, query_pos, step):
        scores = jnp.einsum(
            "qhgd,khd->hgqk", query_tile, key_tile, preferred_element_type=jnp.float32
        )
        key_pos = step * tile_rows + jnp.arange(tile_rows, dtype=jnp.int32)
        visible = key_pos[None, :] <= query_pos[:, None]
        return (scores, visible)

    def sequence_tables(seq):
        key_blocks = all_keys[seq].reshape(block_total, block_rows, kv_heads, head_dim)
        value_blocks = all_values[seq].reshape(block_total, block_rows, kv_heads, head_dim)
        block_index = (
            jnp.zeros((block_total,), jnp.int32)
            .at[all_slots[seq]]
            .set(jnp.arange(block_total, dtype=jnp.int32))
        )
        return (key_blocks, value_blocks, block_index)

    def tile_index(block_index, step):
        return lax.dynamic_slice_in_dim(block_index, step * tile_blocks, tile_blocks)

    def fetch(table, block_index, step):
        return jnp.take(table, tile_index(block_index, step), axis=0).reshape(
            tile_rows, kv_heads, head_dim
        )

    log_totals = []
    attn_parts = []
    seq = 0
    key_blocks, value_blocks, block_index = sequence_tables(seq)
    for which in range(2):
        slot = 2 * seq + which
        query_tile = queries[slot * block_rows : (slot + 1) * block_rows].reshape(
            block_rows, kv_heads, group_size, head_dim
        )
        query_pos = positions[slot * block_rows : (slot + 1) * block_rows]
        tile_count = block_of[seq, which] // tile_blocks + 1

        def max_step(step, carry):
            running_max, running_sum = carry
            scores, visible = tile_scores(
                query_tile, fetch(key_blocks, block_index, step), query_pos, step
            )
            scores = jnp.where(visible, scores, -1e30)
            new_max = jnp.maximum(running_max, jnp.max(scores, axis=-1))
            running_sum = running_sum * jnp.exp(running_max - new_max) + jnp.sum(
                jnp.exp(scores - new_max[..., None]), axis=-1
            )
            return (new_max, running_sum)

        start_max = jnp.full((kv_heads, group_size, block_rows), -1e30, jnp.float32)
        start_sum = jnp.zeros((kv_heads, group_size, block_rows), jnp.float32)
        running_max, running_sum = lax.fori_loop(0, tile_count, max_step, (start_max, start_sum))
        log_total = running_max + jnp.log(running_sum)

        def value_step(step, total):
            scores, visible = tile_scores(
                query_tile, fetch(key_blocks, block_index, step), query_pos, step
            )
            probs = jnp.where(visible, jnp.exp(scores - log_total[..., None]), 0.0)
            return total + jnp.einsum(
                "hgqk,khd->qhgd",
                probs.astype(jnp.bfloat16),
                fetch(value_blocks, block_index, step),
                preferred_element_type=jnp.float32,
            )

        attn_part = lax.fori_loop(
            0,
            tile_count,
            value_step,
            jnp.zeros((block_rows, kv_heads, group_size, head_dim), jnp.float32),
        )
        log_totals.append(log_total)
        attn_parts.append(attn_part)
    attn_full = jnp.concatenate(attn_parts, axis=0)
    attn_bf = attn_full.reshape(flat_rows, q_heads * head_dim).astype(jnp.bfloat16)
    branch = jnp.dot(attn_bf, full_output, preferred_element_type=jnp.float32)
    hidden_mid = residual + branch
    full_post, full_gate, full_up, full_down = (
        lax.all_gather(post_gain, ("ctx", "fsdp"), axis=0, tiled=True),
        lax.all_gather(w_gate, ("ctx", "fsdp"), axis=0, tiled=True),
        lax.all_gather(w_up, ("ctx", "fsdp"), axis=0, tiled=True),
        lax.all_gather(w_down, ("ctx", "fsdp"), axis=0, tiled=True),
    )
    post_scale = lax.rsqrt(jnp.mean(hidden_mid * hidden_mid, axis=-1, keepdims=True) + EPS)
    post_normed = hidden_mid * post_scale
    mlp_in = (post_normed * full_post.astype(jnp.float32)).astype(jnp.bfloat16)
    gate_pre = jnp.dot(mlp_in, full_gate, preferred_element_type=jnp.float32)
    up_pre = jnp.dot(mlp_in, full_up, preferred_element_type=jnp.float32)
    sigmoid_gate = jax.nn.sigmoid(gate_pre)
    activated = gate_pre * sigmoid_gate
    inner = (activated * up_pre).astype(jnp.bfloat16)
    mlp_out = jnp.dot(inner, full_down, preferred_element_type=jnp.float32)
    output = (hidden_mid + mlp_out).astype(jnp.bfloat16)
    full_post, full_gate, full_up, full_down = (
        lax.all_gather(post_gain, ("ctx", "fsdp"), axis=0, tiled=True),
        lax.all_gather(w_gate, ("ctx", "fsdp"), axis=0, tiled=True),
        lax.all_gather(w_up, ("ctx", "fsdp"), axis=0, tiled=True),
        lax.all_gather(w_down, ("ctx", "fsdp"), axis=0, tiled=True),
    )
    grad_out = cotangent.reshape(flat_rows, model_width)
    grad_down = lax.dot_general(inner, grad_out, contract_rows, preferred_element_type=jnp.float32)
    part_down = lax.psum_scatter(grad_down, ("ctx", "fsdp"), scatter_dimension=0, tiled=True)
    grad_inner = lax.dot_general(
        grad_out, full_down, contract_cols, preferred_element_type=jnp.float32
    )
    grad_gate_pre = (
        grad_inner * up_pre * sigmoid_gate * (1.0 + gate_pre * (1.0 - sigmoid_gate))
    ).astype(jnp.bfloat16)
    grad_up_pre = (grad_inner * activated).astype(jnp.bfloat16)
    grad_gate = lax.dot_general(
        mlp_in, grad_gate_pre, contract_rows, preferred_element_type=jnp.float32
    )
    grad_up = lax.dot_general(
        mlp_in, grad_up_pre, contract_rows, preferred_element_type=jnp.float32
    )
    grad_mlp_in = lax.dot_general(
        grad_gate_pre, full_gate, contract_cols, preferred_element_type=jnp.float32
    ) + lax.dot_general(grad_up_pre, full_up, contract_cols, preferred_element_type=jnp.float32)
    grad_post_gain = jnp.sum(grad_mlp_in * post_normed, axis=0)
    grad_mid = grad_out.astype(jnp.float32) + norm_back(
        grad_mlp_in * full_post.astype(jnp.float32), post_normed, post_scale
    )
    part_post, part_gate, part_up = (
        lax.psum_scatter(grad_post_gain, ("ctx", "fsdp"), scatter_dimension=0, tiled=True),
        lax.psum_scatter(grad_gate, ("ctx", "fsdp"), scatter_dimension=0, tiled=True),
        lax.psum_scatter(grad_up, ("ctx", "fsdp"), scatter_dimension=0, tiled=True),
    )
    full_in_gain, full_query, full_key, full_value, full_output = (
        lax.all_gather(in_gain, ("ctx", "fsdp"), axis=0, tiled=True),
        lax.all_gather(w_query, ("ctx", "fsdp"), axis=0, tiled=True),
        lax.all_gather(w_key, ("ctx", "fsdp"), axis=0, tiled=True),
        lax.all_gather(w_value, ("ctx", "fsdp"), axis=0, tiled=True),
        lax.all_gather(w_output, ("ctx", "fsdp"), axis=0, tiled=True),
    )
    grad_branch = grad_mid.astype(jnp.bfloat16)
    grad_output = lax.dot_general(
        attn_bf, grad_branch, contract_rows, preferred_element_type=jnp.float32
    )
    grad_attn = lax.dot_general(
        grad_branch, full_output, contract_cols, preferred_element_type=jnp.float32
    ).astype(jnp.bfloat16)
    grad_attn = grad_attn.reshape(flat_rows, kv_heads, group_size, head_dim)
    query_grads = []
    seq = 0
    key_blocks, value_blocks, block_index = sequence_tables(seq)
    key_grads = jnp.zeros((block_total, block_rows, kv_heads, head_dim), jnp.float32)
    value_grads = jnp.zeros((block_total, block_rows, kv_heads, head_dim), jnp.float32)
    for which in range(2):
        slot = 2 * seq + which
        query_tile = queries[slot * block_rows : (slot + 1) * block_rows].reshape(
            block_rows, kv_heads, group_size, head_dim
        )
        query_pos = positions[slot * block_rows : (slot + 1) * block_rows]
        grad_tile = grad_attn[slot * block_rows : (slot + 1) * block_rows]
        tile_count = block_of[seq, which] // tile_blocks + 1
        delta = jnp.einsum("qhgd,qhgd->hgq", grad_tile.astype(jnp.float32), attn_parts[slot])
        log_total = log_totals[slot]

        def grad_step(step, carry):
            grad_query, keys_acc, values_acc = carry
            key_tile = fetch(key_blocks, block_index, step)
            scores, visible = tile_scores(query_tile, key_tile, query_pos, step)
            probs = jnp.where(visible, jnp.exp(scores - log_total[..., None]), 0.0)
            grad_probs = jnp.einsum(
                "qhgd,khd->hgqk",
                grad_tile,
                fetch(value_blocks, block_index, step),
                preferred_element_type=jnp.float32,
            )
            grad_scores = (probs * (grad_probs - delta[..., None])).astype(jnp.bfloat16)
            grad_query = grad_query + jnp.einsum(
                "hgqk,khd->qhgd", grad_scores, key_tile, preferred_element_type=jnp.float32
            )
            key_part = jnp.einsum(
                "hgqk,qhgd->khd", grad_scores, query_tile, preferred_element_type=jnp.float32
            )
            value_part = jnp.einsum(
                "hgqk,qhgd->khd",
                probs.astype(jnp.bfloat16),
                grad_tile,
                preferred_element_type=jnp.float32,
            )
            places = tile_index(block_index, step)
            keys_acc = keys_acc.at[places].add(
                key_part.reshape(tile_blocks, block_rows, kv_heads, head_dim)
            )
            values_acc = values_acc.at[places].add(
                value_part.reshape(tile_blocks, block_rows, kv_heads, head_dim)
            )
            return (grad_query, keys_acc, values_acc)

        start_query = jnp.zeros((block_rows, kv_heads, group_size, head_dim), jnp.float32)
        grad_query, key_grads, value_grads = lax.fori_loop(
            0, tile_count, grad_step, (start_query, key_grads, value_grads)
        )
        query_grads.append(grad_query)
    key_grad_list = [key_grads.reshape(seq_len, kv_heads * head_dim)]
    value_grad_list = [value_grads.reshape(seq_len, kv_heads * head_dim)]
    grad_keys, grad_values = (
        lax.psum_scatter(
            jnp.stack(key_grad_list, axis=0).astype(jnp.bfloat16),
            "ctx",
            scatter_dimension=1,
            tiled=True,
        ).astype(jnp.float32),
        lax.psum_scatter(
            jnp.stack(value_grad_list, axis=0).astype(jnp.bfloat16),
            "ctx",
            scatter_dimension=1,
            tiled=True,
        ).astype(jnp.float32),
    )
    grad_q_rot = (
        jnp.concatenate(query_grads, axis=0).reshape(flat_rows, q_heads, head_dim) * q_scale
    )
    grad_q_normed = rotate(grad_q_rot, cosine, -sine)
    grad_q_gain = jnp.sum(grad_q_normed * q_unit, axis=(0, 1))
    grad_q_raw = (
        norm_back(grad_q_normed * q_gain.astype(jnp.float32), q_unit, q_rms)
        .astype(jnp.bfloat16)
        .reshape(flat_rows, q_heads * head_dim)
    )
    grad_k_normed = rotate(grad_keys.reshape(flat_rows, kv_heads, head_dim), cosine, -sine)
    grad_k_gain = jnp.sum(grad_k_normed * k_unit, axis=(0, 1))
    grad_k_raw = (
        norm_back(grad_k_normed * k_gain.astype(jnp.float32), k_unit, k_rms)
        .astype(jnp.bfloat16)
        .reshape(flat_rows, kv_heads * head_dim)
    )
    grad_v_local = grad_values.reshape(flat_rows, kv_heads * head_dim).astype(jnp.bfloat16)
    grad_query_w = lax.dot_general(
        attn_in, grad_q_raw, contract_rows, preferred_element_type=jnp.float32
    )
    grad_key_w = lax.dot_general(
        attn_in, grad_k_raw, contract_rows, preferred_element_type=jnp.float32
    )
    grad_value_w = lax.dot_general(
        attn_in, grad_v_local, contract_rows, preferred_element_type=jnp.float32
    )
    grad_attn_in = lax.dot_general(
        grad_q_raw, full_query, contract_cols, preferred_element_type=jnp.float32
    )
    grad_attn_in = grad_attn_in + lax.dot_general(
        grad_k_raw, full_key, contract_cols, preferred_element_type=jnp.float32
    )
    grad_attn_in = grad_attn_in + lax.dot_general(
        grad_v_local, full_value, contract_cols, preferred_element_type=jnp.float32
    )
    grad_in_gain = jnp.sum(grad_attn_in * in_normed, axis=0)
    grad_input = grad_mid + norm_back(
        grad_attn_in * full_in_gain.astype(jnp.float32), in_normed, in_scale
    )
    part_in, part_query, part_key, part_value, part_output = (
        lax.psum_scatter(grad_in_gain, ("ctx", "fsdp"), scatter_dimension=0, tiled=True),
        lax.psum_scatter(grad_query_w, ("ctx", "fsdp"), scatter_dimension=0, tiled=True),
        lax.psum_scatter(grad_key_w, ("ctx", "fsdp"), scatter_dimension=0, tiled=True),
        lax.psum_scatter(grad_value_w, ("ctx", "fsdp"), scatter_dimension=0, tiled=True),
        lax.psum_scatter(grad_output, ("ctx", "fsdp"), scatter_dimension=0, tiled=True),
    )
    sum_q_gain, sum_k_gain = lax.psum((grad_q_gain, grad_k_gain), ("ctx", "fsdp"))
    return (
        output.reshape(seq_count, tok_rows, model_width),
        grad_input.reshape(seq_count, tok_rows, model_width),
        part_in,
        part_query,
        part_key,
        part_value,
        part_output,
        sum_q_gain,
        sum_k_gain,
        part_post,
        part_gate,
        part_up,
        part_down,
    )


MESH = pl.DeviceIdType.MESH
SUBS = 2


def ring_position(index, size):
    column, line = lax.rem(index, 2), lax.div(index, 2)
    return column * (line + 1) + (1 - column) * lax.rem(size - line, size)


def ring_member(position, size):
    late = lax.div(position + size // 2 - 1, size)
    beyond = lax.div(position + size - 1, size)
    return beyond * (1 - late) * (2 * position - 1) + late * 2 * (size - position)


class Ring:
    def __init__(self, size):
        self.size = size
        self.me = lax.axis_index("ctx")
        self.row = lax.axis_index("fsdp")
        self.position = ring_position(self.me, size)

    def member(self, way, steps):
        ahead = self.size - steps if way == 0 else steps
        return ring_member(lax.rem(self.position + ahead, self.size), self.size)

    def target(self, way):
        return (self.member(way, self.size - 1), self.row)

    def barrier(self):
        barrier = pltpu.get_barrier_semaphore()
        for way in range(2):
            pl.semaphore_signal(barrier, inc=1, device_id=self.target(way), device_id_type=MESH)
        pl.semaphore_wait(barrier, 2)


class GatherRing:
    def __init__(self, ring, own, out, send_sems, recv_sems):
        self.ring, self.own, self.out, self.send_sems, self.recv_sems = ring, own, out, send_sems, recv_sems
        self.half = own.shape[0] // 2
        self.sub = self.half // SUBS

    def copy(self, way, step, part, first=False):
        place = pl.ds(way * self.half + part * self.sub, self.sub)
        owner = self.ring.me if first else self.ring.member(way, step)
        source = self.own.at[place] if first else self.out.at[owner, place]
        return pltpu.make_async_remote_copy(
            src_ref=source,
            dst_ref=self.out.at[owner, place],
            send_sem=self.send_sems.at[way, step, part],
            recv_sem=self.recv_sems.at[way, step, part],
            device_id=self.ring.target(way),
            device_id_type=MESH,
        )

    def start(self, way):
        for part in range(SUBS):
            self.copy(way, 0, part, first=True).start()

    def step(self, step):
        for part in range(SUBS):
            for way in range(2):
                self.copy(way, step - 1, part).wait_recv()
                self.copy(way, step, part).start()

    def finish(self):
        last = self.ring.size - 2
        for part in range(SUBS):
            for way in range(2):
                self.copy(way, last, part).wait_recv()

        @pl.loop(0, last + 1)
        def _(step):
            for part in range(SUBS):
                for way in range(2):
                    self.copy(way, step, part).wait_send()

    def run(self):
        for way in range(2):
            self.start(way)

        @pl.loop(1, self.ring.size - 1)
        def _(step):
            self.step(step)

        self.finish()


def gather_sems(size):
    return [pltpu.SemaphoreType.DMA((2, size - 1, SUBS)), pltpu.SemaphoreType.DMA((2, size - 1, SUBS))]


class SumRing:
    def __init__(self, ring, compute, terms, outgoing, incoming, send_sems, recv_sems):
        self.ring, self.compute, self.terms = ring, compute, terms
        self.outgoing, self.incoming, self.send_sems, self.recv_sems = outgoing, incoming, send_sems, recv_sems
        self.half = terms.shape[1]
        self.sub = self.half // SUBS

    def copy(self, way, step, part):
        place = pl.ds(part * self.sub, self.sub)
        return pltpu.make_async_remote_copy(
            src_ref=self.outgoing.at[way, lax.rem(step, 2), place],
            dst_ref=self.incoming.at[way, step, place],
            send_sem=self.send_sems.at[way, step, part],
            recv_sem=self.recv_sems.at[way, step, part],
            device_id=self.ring.target(way),
            device_id_type=MESH,
        )

    def terms_of(self, step):
        self.compute([self.ring.member(way, step + 1) for way in range(2)])

    def begin(self):
        self.terms_of(0)
        for part in range(SUBS):
            place = pl.ds(part * self.sub, self.sub)
            for way in range(2):
                self.outgoing[way, 0, place] = self.terms[way, place].astype(jnp.bfloat16)
                self.copy(way, 0, part).start()

    def second(self):
        self.step(1, fresh=True)

    def step(self, step, fresh=False):
        self.terms_of(step)
        for part in range(SUBS):
            place = pl.ds(part * self.sub, self.sub)
            for way in range(2):
                self.copy(way, step - 1, part).wait_recv()
                total = self.terms[way, place] + self.incoming[way, step - 1, place].astype(jnp.float32)
                if not fresh:
                    self.copy(way, step - 2, part).wait_send()
                self.outgoing[way, lax.rem(step, 2), place] = total.astype(jnp.bfloat16)
                self.copy(way, step, part).start()

    def last_terms(self):
        self.compute([self.ring.me, self.ring.me])

    def result(self, way):
        last = self.ring.size - 2
        for part in range(SUBS):
            self.copy(way, last, part).wait_recv()
        return self.terms[way] + self.incoming[way, last].astype(jnp.float32)

    def finish(self):
        for step in (self.ring.size - 3, self.ring.size - 2):
            for part in range(SUBS):
                for way in range(2):
                    self.copy(way, step, part).wait_send()

    def run(self):
        self.begin()
        self.second()

        @pl.loop(2, self.ring.size - 1)
        def _(step):
            self.step(step)

        self.last_terms()


def sum_scratch(size, rows, width):
    half = rows // 2
    return [
        pltpu.VMEM((2, half, width), jnp.float32),
        pltpu.VMEM((2, 2, half, width), jnp.bfloat16),
        pltpu.VMEM((2, size - 1, half, width), jnp.bfloat16),
        pltpu.SemaphoreType.DMA((2, size - 1, SUBS)),
        pltpu.SemaphoreType.DMA((2, size - 1, SUBS)),
    ]


TILE = 512


def row_terms(left, weight, terms):
    half = terms.shape[1]

    def compute(members):
        lines = jnp.concatenate([left[members[way], way * half : (way + 1) * half] for way in range(2)], axis=0)

        @pl.loop(0, weight.shape[1] // TILE)
        def _(tile):
            columns = pl.ds(pl.multiple_of(tile * TILE, TILE), TILE)
            product = jnp.dot(lines, weight[:, columns], preferred_element_type=jnp.float32)
            for way in range(2):
                terms[way, :, columns] = product[way * half : (way + 1) * half]

    return compute


def row_terms_t(left, weight, terms):
    half = terms.shape[1]

    def compute(members):
        lines = jnp.concatenate([left[members[way], way * half : (way + 1) * half] for way in range(2)], axis=0)

        @pl.loop(0, weight.shape[0] // TILE)
        def _(tile):
            columns = pl.ds(pl.multiple_of(tile * TILE, TILE), TILE)
            product = lax.dot_general(
                lines, weight[columns, :], (((1,), (1,)), ((), ())), preferred_element_type=jnp.float32
            )
            for way in range(2):
                terms[way, :, columns] = product[way * half : (way + 1) * half]

    return compute


VMEM_SPEC = pl.BlockSpec(memory_space=pltpu.VMEM)
ANY_SPEC = pl.BlockSpec(memory_space=pl.ANY)


def ctx_peer(ring, ahead):
    return lax.rem(ring.me + ahead, ring.size)


def across(row, n_fsdp):
    return lax.rem(row + n_fsdp // 2, n_fsdp)


def beside(row):
    return row + 1 - 2 * lax.rem(row, 2)


def remote(source, target, send_sem, recv_sem, device):
    return pltpu.make_async_remote_copy(
        src_ref=source,
        dst_ref=target,
        send_sem=send_sem,
        recv_sem=recv_sem,
        device_id=device,
        device_id_type=MESH,
    )


def greet(devices):
    barrier = pltpu.get_barrier_semaphore()
    for device in devices:
        pl.semaphore_signal(barrier, inc=1, device_id=device, device_id_type=MESH)
    pl.semaphore_wait(barrier, len(devices))


def near_devices(ring, n_fsdp):
    return [(ctx_peer(ring, ahead), ring.row) for ahead in range(1, ring.size)] + [
        (ring.me, across(ring.row, n_fsdp)),
        (ring.me, beside(ring.row)),
    ]


class Others:
    def __init__(self, ring, n_fsdp):
        self.ring, self.n_fsdp, self.count = ring, n_fsdp, ring.size * n_fsdp
        self.index = ring.me * n_fsdp + ring.row

    def each(self, act):
        @pl.loop(0, self.count)
        def _(other):
            @pl.when(other != self.index)
            def _():
                act(other, (lax.div(other, self.n_fsdp), lax.rem(other, self.n_fsdp)))

    def greet(self):
        barrier = pltpu.get_barrier_semaphore()
        self.each(lambda other, device: pl.semaphore_signal(barrier, inc=1, device_id=device, device_id_type=MESH))
        pl.semaphore_wait(barrier, self.count - 1)


class Rows:
    def __init__(self, ring, n_fsdp, shard, out, send_sems, recv_sems):
        own, far, twin = ring.row, across(ring.row, n_fsdp), beside(ring.row)
        self.keep = pltpu.make_async_copy(shard, out.at[own], send_sems.at[3])
        self.to_far = remote(shard, out.at[own], send_sems.at[0], recv_sems.at[0], (ring.me, far))
        self.to_twin = remote(shard, out.at[own], send_sems.at[1], recv_sems.at[1], (ring.me, twin))
        self.pass_on = remote(out.at[far], out.at[far], send_sems.at[2], recv_sems.at[2], (ring.me, twin))

    def begin(self):
        self.keep.start()
        self.to_far.start()
        self.to_twin.start()

    def relay(self):
        self.to_far.wait_recv()
        self.pass_on.start()

    def finish(self):
        self.keep.wait()
        self.to_far.wait_send()
        self.to_twin.wait()
        self.pass_on.wait()


def rows_sems():
    return [pltpu.SemaphoreType.DMA((4,)), pltpu.SemaphoreType.DMA((3,))]


class Columns:
    def __init__(self, ring, n_fsdp, shards, out, send_sems, recv_sems, link_send, link_recv):
        self.ring, self.shards, self.out, self.send_sems, self.recv_sems = ring, shards, out, send_sems, recv_sems
        own, far, twin = ring.row, across(ring.row, n_fsdp), beside(ring.row)
        self.widths = [shard.shape[1] // ring.size for shard in shards]
        self.to_far = remote(out.at[:, own], out.at[:, own], link_send.at[0], link_recv.at[0], (ring.me, far))
        self.to_twin = remote(out.at[:, own], out.at[:, own], link_send.at[1], link_recv.at[1], (ring.me, twin))
        self.pass_on = remote(out.at[:, far], out.at[:, far], link_send.at[2], link_recv.at[2], (ring.me, twin))

    def piece(self, which, ahead):
        member = ctx_peer(self.ring, ahead)
        width = self.widths[which]
        start = sum(self.widths[:which])
        source = self.shards[which].at[:, pl.ds(pl.multiple_of(member * width, width), width)]
        target = self.out.at[self.ring.me, self.ring.row, :, pl.ds(start, width)]
        if ahead == 0:
            return pltpu.make_async_copy(source, target, self.send_sems.at[which, 0])
        return remote(
            source, target, self.send_sems.at[which, ahead], self.recv_sems.at[which, ahead], (member, self.ring.row)
        )

    def begin(self):
        for ahead in range(self.ring.size):
            for which in range(len(self.shards)):
                self.piece(which, ahead).start()

    def spread(self):
        for ahead in range(self.ring.size):
            for which in range(len(self.shards)):
                if ahead:
                    self.piece(which, ahead).wait_recv()
                else:
                    self.piece(which, ahead).wait()
        self.to_far.start()
        self.to_twin.start()

    def relay(self):
        self.to_far.wait_recv()
        self.pass_on.start()

    def finish(self):
        for ahead in range(1, self.ring.size):
            for which in range(len(self.shards)):
                self.piece(which, ahead).wait_send()
        self.to_far.wait_send()
        self.to_twin.wait()
        self.pass_on.wait()


def columns_sems(size, count):
    return [
        pltpu.SemaphoreType.DMA((count, size)),
        pltpu.SemaphoreType.DMA((count, size)),
        pltpu.SemaphoreType.DMA((3,)),
        pltpu.SemaphoreType.DMA((3,)),
    ]


class RowGrads:
    def __init__(self, ring, n_fsdp, part, from_twin, to_far, from_far, send_sems, recv_sems):
        own, far, twin = ring.row, across(ring.row, n_fsdp), beside(ring.row)
        self.part, self.from_twin, self.to_far, self.from_far = part, from_twin, to_far, from_far
        self.own, self.far = own, far
        twin_far = across(twin, n_fsdp)
        self.first = [
            remote(part.at[twin], from_twin.at[0], send_sems.at[0], recv_sems.at[0], (ring.me, twin)),
            remote(part.at[twin_far], from_twin.at[1], send_sems.at[1], recv_sems.at[1], (ring.me, twin)),
        ]
        if to_far is None:
            self.to_far = part.at[far]
        self.second = remote(self.to_far, from_far, send_sems.at[2], recv_sems.at[2], (ring.me, far))

    def begin(self):
        self.first[1].start()
        self.first[0].start()

    def cross(self):
        self.first[1].wait_recv()
        self.to_far[...] = (
            self.part[self.far].astype(jnp.float32) + self.from_twin[1].astype(jnp.float32)
        ).astype(jnp.bfloat16)
        self.second.start()

    def result(self):
        self.first[0].wait_recv()
        self.second.wait_recv()
        return (
            self.part[self.own].astype(jnp.float32)
            + self.from_twin[0].astype(jnp.float32)
            + self.from_far[...].astype(jnp.float32)
        )

    def finish(self):
        for copy in self.first + [self.second]:
            copy.wait_send()


def row_grads_sems():
    return [pltpu.SemaphoreType.DMA((3,)), pltpu.SemaphoreType.DMA((3,))]


def row_grads_scratch(shape):
    return [
        pltpu.VMEM((2,) + shape, jnp.bfloat16),
        pltpu.VMEM(shape, jnp.bfloat16),
        pltpu.VMEM(shape, jnp.bfloat16),
    ] + row_grads_sems()


class Deal:
    def __init__(self, ring, total, arrived, send_sems, recv_sems):
        self.ring, self.total, self.arrived = ring, total, arrived
        self.send_sems, self.recv_sems = send_sems, recv_sems

    def piece(self, ahead):
        member = ctx_peer(self.ring, ahead)
        return remote(
            self.total.at[member],
            self.arrived.at[self.ring.me],
            self.send_sems.at[ahead],
            self.recv_sems.at[ahead],
            (member, self.ring.row),
        )

    def begin(self):
        for ahead in range(1, self.ring.size):
            self.piece(ahead).start()
        self.arrived[self.ring.me] = self.total[self.ring.me]

    def collect(self, outs):
        for ahead in range(1, self.ring.size):
            self.piece(ahead).wait_recv()
        start = 0
        for out in outs:
            width = out.shape[1] // self.ring.size
            for member in range(self.ring.size):
                out[:, member * width : (member + 1) * width] = self.arrived[member, :, start : start + width].astype(
                    jnp.float32
                )
            start += width

    def finish(self):
        for ahead in range(1, self.ring.size):
            self.piece(ahead).wait_send()


def deal_scratch(shape):
    return [
        pltpu.VMEM(shape, jnp.bfloat16),
        pltpu.SemaphoreType.DMA((shape[0],)),
        pltpu.SemaphoreType.DMA((shape[0],)),
    ]


def params(collective_id):
    return pltpu.CompilerParams(
        collective_id=collective_id, has_side_effects=True, vmem_limit_bytes=62 * 1024 * 1024
    )


def front_kernel(size, n_fsdp, hidden, small, w_query, w_key, w_value, w_output, attn_in, all_small, columns_out, rows_out, *scratch):
    own, gain, gather_send, gather_recv, own_sem, small_send, small_recv = scratch[:7]
    ring = Ring(size)
    others = Others(ring, n_fsdp)
    columns = Columns(ring, n_fsdp, [w_query, w_key, w_value], columns_out, *scratch[7:11])
    rows = Rows(ring, n_fsdp, w_output, rows_out, *scratch[11:13])
    gathering = GatherRing(ring, own, attn_in, gather_send, gather_recv)
    others.greet()

    def tiny(other, device):
        return remote(small, all_small.at[others.index], small_send.at[other], small_recv.at[others.index], device)

    others.each(lambda other, device: tiny(other, device).start())
    columns.begin()
    rows.begin()
    all_small[others.index] = small[...]
    others.each(
        lambda other, device: remote(
            small, all_small.at[other], small_send.at[other], small_recv.at[other], device
        ).wait_recv()
    )
    for pair in range(others.count // 2):
        gain[:, pair * 128 : (pair + 1) * 128] = all_small[2 * pair, 0:1] + all_small[2 * pair + 1, 0:1]
    half = own.shape[0] // 2
    for way in range(2):
        place = slice(way * half, (way + 1) * half)
        values = hidden[place].astype(jnp.float32)
        scale = lax.rsqrt(jnp.mean(values * values, axis=-1, keepdims=True) + EPS)
        own[place] = (values * scale * gain[...]).astype(jnp.bfloat16)
        gathering.start(way)
    keep = pltpu.make_async_copy(own, attn_in.at[ring.me], own_sem)
    keep.start()
    gathering.step(1)
    gathering.step(2)
    columns.spread()
    gathering.step(3)
    gathering.step(4)
    rows.relay()

    @pl.loop(5, size - 1)
    def _(step):
        gathering.step(step)

    columns.relay()
    gathering.finish()
    others.each(lambda other, device: tiny(other, device).wait_send())
    columns.finish()
    rows.finish()
    keep.wait()


def front(hidden, small, w_query, w_key, w_value, w_output):
    size, n_fsdp = lax.axis_size("ctx"), lax.axis_size("fsdp")
    rows, width = hidden.shape
    depth = w_query.shape[0]
    share = (w_query.shape[1] + w_key.shape[1] + w_value.shape[1]) // size
    return pl.pallas_call(
        functools.partial(front_kernel, size, n_fsdp),
        out_shape=[
            jax.ShapeDtypeStruct((size, rows, width), jnp.bfloat16),
            jax.ShapeDtypeStruct((size * n_fsdp,) + small.shape, jnp.float32),
            jax.ShapeDtypeStruct((size, n_fsdp, depth, share), jnp.bfloat16),
            jax.ShapeDtypeStruct((n_fsdp,) + w_output.shape, jnp.bfloat16),
        ],
        in_specs=[VMEM_SPEC, VMEM_SPEC] + [ANY_SPEC] * 4,
        out_specs=[ANY_SPEC, VMEM_SPEC, ANY_SPEC, ANY_SPEC],
        scratch_shapes=[pltpu.VMEM((rows, width), jnp.bfloat16), pltpu.VMEM((1, width), jnp.float32)]
        + gather_sems(size)
        + [
            pltpu.SemaphoreType.DMA,
            pltpu.SemaphoreType.DMA((size * n_fsdp,)),
            pltpu.SemaphoreType.DMA((size * n_fsdp,)),
        ]
        + columns_sems(size, 3)
        + rows_sems(),
        compiler_params=params(2),
    )(hidden, small, w_query, w_key, w_value, w_output)


def second_kernel(size, n_fsdp, cotangent, w_gate, w_up, w_down, grad_out, columns_out, rows_out, *scratch):
    gather_send, gather_recv, own_sem = scratch[:3]
    ring = Ring(size)
    columns = Columns(ring, n_fsdp, [w_gate, w_up], columns_out, *scratch[3:7])
    rows = Rows(ring, n_fsdp, w_down, rows_out, *scratch[7:9])
    gathering = GatherRing(ring, cotangent, grad_out, gather_send, gather_recv)
    greet(near_devices(ring, n_fsdp))
    columns.begin()
    rows.begin()
    for way in range(2):
        gathering.start(way)
    keep = pltpu.make_async_copy(cotangent, grad_out.at[ring.me], own_sem)
    keep.start()
    gathering.step(1)
    gathering.step(2)
    gathering.step(3)
    columns.spread()
    rows.relay()

    @pl.loop(4, size - 1)
    def _(step):
        gathering.step(step)

    gathering.finish()
    columns.relay()
    columns.finish()
    rows.finish()
    keep.wait()


def second(cotangent, w_gate, w_up, w_down):
    size, n_fsdp = lax.axis_size("ctx"), lax.axis_size("fsdp")
    rows, width = cotangent.shape
    depth = w_gate.shape[0]
    share = (w_gate.shape[1] + w_up.shape[1]) // size
    return pl.pallas_call(
        functools.partial(second_kernel, size, n_fsdp),
        out_shape=[
            jax.ShapeDtypeStruct((size, rows, width), jnp.bfloat16),
            jax.ShapeDtypeStruct((size, n_fsdp, depth, share), jnp.bfloat16),
            jax.ShapeDtypeStruct((n_fsdp,) + w_down.shape, jnp.bfloat16),
        ],
        in_specs=[ANY_SPEC] * 4,
        out_specs=[ANY_SPEC] * 3,
        scratch_shapes=gather_sems(size) + [pltpu.SemaphoreType.DMA] + columns_sems(size, 2) + rows_sems(),
        compiler_params=params(3),
    )(cotangent, w_gate, w_up, w_down)


def norm_pull(grad_normed, normed, scale):
    return scale * (grad_normed - normed * jnp.mean(grad_normed * normed, axis=-1, keepdims=True))


def feed_forward_kernel(
    size,
    n_fsdp,
    attn,
    w_output,
    hidden,
    gain,
    w_gu_in,
    w_down_in,
    cot_in,
    out_hidden,
    grad_mid,
    grad_gain,
    grad_branch,
    gu_total,
    down_out,
    w_gu,
    w_down,
    cot,
    load_sems,
    mid,
    own,
    mlp_in,
    inner,
    grad_gu,
    gu_part,
    down_part,
    *scratch,
):
    loads = [
        pltpu.make_async_copy(source, target, load_sems.at[which])
        for which, (source, target) in enumerate(((w_gu_in, w_gu), (w_down_in, w_down), (cot_in, cot)))
    ]
    for load in loads:
        load.start()
    ring = Ring(size)
    greet(near_devices(ring, n_fsdp))
    half = own.shape[0] // 2
    ff = w_down.shape[0]
    out_sums, gather_sems_in = scratch[:5], scratch[5:7]
    layer_sums = (scratch[0],) + tuple(scratch[7:11])
    gather_sems_out, keep_sems = scratch[11:13], scratch[13]
    column_scratch = (scratch[14], None, gu_total, scratch[15], scratch[16])
    row_scratch = (scratch[17], None, scratch[18], scratch[19], scratch[20])

    first = SumRing(ring, row_terms(attn, w_output, out_sums[0]), *out_sums)
    first.run()
    gathering = GatherRing(ring, own, mlp_in, *gather_sems_in)
    for way in range(2):
        place = slice(way * half, (way + 1) * half)
        total = first.result(way) + hidden[place].astype(jnp.float32)
        mid[place] = total
        scale = lax.rsqrt(jnp.mean(total * total, axis=-1, keepdims=True) + EPS)
        own[place] = (total * scale * gain[...]).astype(jnp.bfloat16)
        gathering.start(way)
    first.finish()
    keep = pltpu.make_async_copy(own, mlp_in.at[ring.me], keep_sems.at[0])
    keep.start()
    for load in loads:
        load.wait()

    def units(lines, members):
        cot_lines = jnp.concatenate([cot[members[way], way * half : (way + 1) * half] for way in range(2)], axis=0)

        @pl.loop(0, ff // UNITS)
        def _(tile):
            at = pl.multiple_of(tile * UNITS, UNITS)
            here, there = pl.ds(at, UNITS), pl.ds(pl.multiple_of(ff + at, UNITS), UNITS)
            gate = jnp.dot(lines, w_gu[:, here], preferred_element_type=jnp.float32)
            up = jnp.dot(lines, w_gu[:, there], preferred_element_type=jnp.float32)
            pulled = lax.dot_general(
                cot_lines, w_down[here, :], (((1,), (1,)), ((), ())), preferred_element_type=jnp.float32
            )
            sigmoid = 1.0 / (1.0 + jnp.exp(-gate))
            active = gate * sigmoid
            inner_new = (active * up).astype(jnp.bfloat16)
            gate_new = (pulled * up * sigmoid * (1.0 + gate * (1.0 - sigmoid))).astype(jnp.bfloat16)
            up_new = (pulled * active).astype(jnp.bfloat16)
            for way in range(2):
                place = slice(way * half, (way + 1) * half)
                inner[members[way], place, here] = inner_new[place]
                grad_gu[members[way], place, here] = gate_new[place]
                grad_gu[members[way], place, there] = up_new[place]

    def units_of(step):
        members = [ring.member(way, step) for way in range(2)]
        units(
            jnp.concatenate([mlp_in[members[way], way * half : (way + 1) * half] for way in range(2)], axis=0), members
        )

    units(own[...], [ring.me, ring.me])

    @pl.loop(1, size - 1)
    def _(step):
        gathering.step(step)
        units_of(step)

    gathering.finish()
    keep.wait()
    units_of(size - 1)

    second = SumRing(ring, row_terms(inner, w_down, layer_sums[0]), *layer_sums)
    rows_all = size * 2 * half
    width = w_gu.shape[0]
    block = width // size

    def gu_tile(member):
        columns = pl.ds(pl.multiple_of(member * block, block), block)
        lines = mlp_in[:, :, columns].reshape(rows_all, block)

        @pl.loop(0, 2 * ff // TILE)
        def _(tile):
            there = pl.ds(pl.multiple_of(tile * TILE, TILE), TILE)
            product = lax.dot_general(
                lines,
                grad_gu[:, :, there].reshape(rows_all, TILE),
                (((0,), (0,)), ((), ())),
                preferred_element_type=jnp.float32,
            ).astype(jnp.bfloat16)
            for row in range(n_fsdp):
                gu_part[row, member, :, there] = product[row * (block // n_fsdp) : (row + 1) * (block // n_fsdp)]

    share = ff // n_fsdp

    def down_tile(tile):
        columns = pl.ds(pl.multiple_of(tile * UNITS, UNITS), UNITS)
        lines = cot[:, :, columns].reshape(rows_all, UNITS)
        product = lax.dot_general(
            inner[...].reshape(rows_all, ff), lines, (((0,), (0,)), ((), ())), preferred_element_type=jnp.float32
        ).astype(jnp.bfloat16)
        for row in range(n_fsdp):
            down_part[row, :, columns] = product[row * share : (row + 1) * share]

    second.begin()
    gu_tile(0)
    second.second()
    gu_tile(1)

    @pl.loop(2, size - 1)
    def _(step):
        second.step(step)
        gu_tile(step)

        @pl.when(step < 2 + width // UNITS // 2)
        def _():
            down_tile(2 * step - 4)
            down_tile(2 * step - 3)

    gu_tile(size - 1)
    columns = RowGrads(ring, n_fsdp, gu_part, *column_scratch)
    rows = RowGrads(ring, n_fsdp, down_part, *row_scratch)
    columns.begin()
    rows.begin()
    second.last_terms()
    for way in range(2):
        place = slice(way * half, (way + 1) * half)
        out_hidden[place] = (mid[place] + second.result(way)).astype(jnp.bfloat16)

    third = SumRing(ring, row_terms_t(grad_gu, w_gu, out_sums[0]), *out_sums)
    third.begin()
    second.finish()
    third.second()
    columns.cross()
    rows.cross()

    @pl.loop(2, size - 1)
    def _(step):
        third.step(step)

    third.last_terms()
    gathering = GatherRing(ring, own, grad_branch, *gather_sems_out)
    gain_sum = jnp.zeros_like(grad_gain)
    for way in range(2):
        place = slice(way * half, (way + 1) * half)
        pulled = third.result(way)
        values = mid[place]
        scale = lax.rsqrt(jnp.mean(values * values, axis=-1, keepdims=True) + EPS)
        normed = values * scale
        gain_sum = gain_sum + jnp.sum(pulled * normed, axis=0, keepdims=True)
        total = cot[ring.me, place].astype(jnp.float32) + norm_pull(pulled * gain[...], normed, scale)
        grad_mid[place] = total
        own[place] = total.astype(jnp.bfloat16)
        gathering.start(way)
    grad_gain[...] = gain_sum
    keep = pltpu.make_async_copy(own, grad_branch.at[ring.me], keep_sems.at[1])
    keep.start()
    third.finish()
    gathering.step(1)
    gathering.step(2)
    down_out[...] = rows.result()
    gathering.step(3)
    gu_total[...] = columns.result().astype(jnp.bfloat16)

    @pl.loop(4, size - 1)
    def _(step):
        gathering.step(step)

    gathering.finish()
    columns.finish()
    rows.finish()
    keep.wait()


UNITS = 256


def feed_forward(attn, w_output, hidden, gain, w_gu, w_down, cotangent):
    size, n_fsdp = lax.axis_size("ctx"), lax.axis_size("fsdp")
    rows, width = hidden.shape
    ff = w_down.shape[0]
    depth = width // size // n_fsdp
    sums = sum_scratch(size, rows, width)
    return pl.pallas_call(
        functools.partial(feed_forward_kernel, size, n_fsdp),
        out_shape=[
            jax.ShapeDtypeStruct((rows, width), jnp.bfloat16),
            jax.ShapeDtypeStruct((rows, width), jnp.float32),
            jax.ShapeDtypeStruct((1, width), jnp.float32),
            jax.ShapeDtypeStruct((size, rows, width), jnp.bfloat16),
            jax.ShapeDtypeStruct((size, depth, 2 * ff), jnp.bfloat16),
            jax.ShapeDtypeStruct((ff // n_fsdp, width), jnp.float32),
        ],
        in_specs=[VMEM_SPEC] * 4 + [ANY_SPEC] * 3,
        out_specs=[VMEM_SPEC, VMEM_SPEC, VMEM_SPEC, ANY_SPEC, VMEM_SPEC, VMEM_SPEC],
        scratch_shapes=[
            pltpu.VMEM(w_gu.shape, jnp.bfloat16),
            pltpu.VMEM(w_down.shape, jnp.bfloat16),
            pltpu.VMEM((size, rows, width), jnp.bfloat16),
            pltpu.SemaphoreType.DMA((3,)),
            pltpu.VMEM((rows, width), jnp.float32),
            pltpu.VMEM((rows, width), jnp.bfloat16),
            pltpu.VMEM((size, rows, width), jnp.bfloat16),
            pltpu.VMEM((size, rows, ff), jnp.bfloat16),
            pltpu.VMEM((size, rows, 2 * ff), jnp.bfloat16),
            pltpu.VMEM((n_fsdp, size, depth, 2 * ff), jnp.bfloat16),
            pltpu.VMEM((n_fsdp, ff // n_fsdp, width), jnp.bfloat16),
        ]
        + sums
        + gather_sems(size)
        + sums[1:]
        + gather_sems(size)
        + [pltpu.SemaphoreType.DMA((2,))]
        + [pltpu.VMEM((2, size, depth, 2 * ff), jnp.bfloat16)]
        + row_grads_sems()
        + [pltpu.VMEM((2, ff // n_fsdp, width), jnp.bfloat16), pltpu.VMEM((ff // n_fsdp, width), jnp.bfloat16)]
        + row_grads_sems(),
        compiler_params=params(5),
    )(
        attn.reshape(size, rows, -1),
        w_output,
        hidden,
        gain.reshape(1, width),
        w_gu,
        w_down,
        cotangent.reshape(size, rows, width),
    )


def back_kernel(
    size,
    n_fsdp,
    grads,
    weight,
    hidden,
    grad_mid,
    gain,
    post_sum,
    q_sum,
    k_sum,
    column_part,
    row_part,
    gu_total,
    grad_hidden,
    gains_out,
    query_out,
    key_out,
    value_out,
    output_out,
    gate_out,
    up_out,
    small,
    all_small,
    small_send,
    small_recv,
    *scratch,
):
    sums = scratch[:5]
    ring = Ring(size)
    others = Others(ring, n_fsdp)
    others.greet()
    half = hidden.shape[0] // 2
    total = scratch[10]
    columns = RowGrads(ring, n_fsdp, column_part, *scratch[5:10])
    dealing = Deal(ring, total, *scratch[11:14])
    rows = RowGrads(ring, n_fsdp, row_part, *scratch[14:19])
    gu_dealing = Deal(ring, gu_total, *scratch[19:22])
    columns.begin()
    rows.begin()
    gu_dealing.begin()
    summing = SumRing(ring, row_terms_t(grads, weight, sums[0]), *sums)
    summing.begin()
    summing.second()
    columns.cross()
    rows.cross()
    summing.step(2)
    summing.step(3)
    total[...] = columns.result().astype(jnp.bfloat16)
    dealing.begin()

    @pl.loop(4, size - 1)
    def _(step):
        summing.step(step)

    output_out[...] = rows.result()
    summing.last_terms()
    gain_sum = jnp.zeros_like(post_sum)
    for way in range(2):
        place = slice(way * half, (way + 1) * half)
        pulled = summing.result(way)
        values = hidden[place].astype(jnp.float32)
        scale = lax.rsqrt(jnp.mean(values * values, axis=-1, keepdims=True) + EPS)
        normed = values * scale
        gain_sum = gain_sum + jnp.sum(pulled * normed, axis=0, keepdims=True)
        grad_hidden[place] = grad_mid[place] + norm_pull(pulled * gain[...], normed, scale)
    for pair in range(others.count // 2):
        lanes = slice(pair * 128, (pair + 1) * 128)
        small[pair, 0:1] = gain_sum[:, lanes]
        small[pair, 1:2] = post_sum[:, lanes]
        small[pair, 2:3] = q_sum[...]
        small[pair, 3:4] = k_sum[...]
        small[pair, 4:8] = jnp.zeros((4, 128), jnp.float32)

    def tiny(other, device):
        return remote(
            small.at[lax.div(other, 2)],
            all_small.at[others.index],
            small_send.at[other],
            small_recv.at[others.index],
            device,
        )

    others.each(lambda other, device: tiny(other, device).start())
    all_small[others.index] = small[lax.div(others.index, 2)]
    gu_dealing.collect([gate_out, up_out])
    dealing.collect([query_out, key_out, value_out])
    others.each(
        lambda other, device: remote(
            small.at[0], all_small.at[other], small_send.at[other], small_recv.at[other], device
        ).wait_recv()
    )
    gains_out[...] = jnp.sum(all_small[...], axis=0)
    others.each(lambda other, device: tiny(other, device).wait_send())
    summing.finish()
    columns.finish()
    rows.finish()
    dealing.finish()
    gu_dealing.finish()


def back(grads, weight, hidden, grad_mid, gain, post_sum, q_sum, k_sum, column_part, row_part, gu_total, widths):
    size, n_fsdp = lax.axis_size("ctx"), lax.axis_size("fsdp")
    rows, width = hidden.shape
    share = column_part.shape[3]
    depth = column_part.shape[2]
    count = size * n_fsdp
    return pl.pallas_call(
        functools.partial(back_kernel, size, n_fsdp),
        out_shape=[
            jax.ShapeDtypeStruct((rows, width), jnp.float32),
            jax.ShapeDtypeStruct((8, 128), jnp.float32),
        ]
        + [jax.ShapeDtypeStruct((depth, full), jnp.float32) for full in widths]
        + [jax.ShapeDtypeStruct(row_part.shape[1:], jnp.float32)]
        + [jax.ShapeDtypeStruct((depth, gu_total.shape[2] // 2 * size), jnp.float32)] * 2,
        in_specs=[VMEM_SPEC] * 11,
        out_specs=[VMEM_SPEC] * 8,
        scratch_shapes=[
            pltpu.VMEM((count // 2, 8, 128), jnp.float32),
            pltpu.VMEM((count, 8, 128), jnp.float32),
            pltpu.SemaphoreType.DMA((count,)),
            pltpu.SemaphoreType.DMA((count,)),
        ]
        + sum_scratch(size, rows, width)
        + row_grads_scratch((size, depth, share))
        + [pltpu.VMEM((size, depth, share), jnp.bfloat16)]
        + deal_scratch((size, depth, share))
        + row_grads_scratch(row_part.shape[1:])
        + deal_scratch(gu_total.shape),
        compiler_params=params(6),
    )(
        grads.reshape(size, rows, -1),
        weight,
        hidden,
        grad_mid,
        gain.reshape(1, width),
        post_sum.reshape(1, width),
        q_sum.reshape(1, -1),
        k_sum.reshape(1, -1),
        column_part,
        row_part,
        gu_total,
    )


def tp_body(
    hidden_in,
    block_of,
    in_gain,
    w_query,
    w_key,
    w_value,
    w_output,
    q_gain,
    k_gain,
    post_gain,
    w_gate,
    w_up,
    w_down,
    cotangent,
):
    seq_count, tok_rows, model_width = hidden_in.shape
    n_ctx = lax.axis_size("ctx")
    n_fsdp = lax.axis_size("fsdp")
    block_rows = tok_rows // 2
    rows = seq_count * tok_rows
    seq_rows = n_ctx * rows
    head_dim = q_gain.shape[0]
    q_heads = w_query.shape[1] // head_dim // n_ctx
    kv_heads = w_key.shape[1] // head_dim // n_ctx
    group = q_heads // kv_heads
    q_scale = head_dim ** (-0.5)
    f32, bf16 = jnp.float32, jnp.bfloat16
    contract_rows = (((0,), (0,)), ((), ()))
    contract_cols = (((1,), (1,)), ((), ()))
    hidden = hidden_in.reshape(rows, model_width)
    cot_local = cotangent.reshape(rows, model_width)
    depth = w_query.shape[0]

    side = lax.rem(lax.axis_index("fsdp"), 2)
    lanes = jnp.arange(2 * depth, dtype=jnp.int32)
    pair_mask = lax.div(lanes, depth) == side
    small = jnp.zeros((8, 2 * depth), f32)
    small = small.at[0].set(jnp.where(pair_mask, jnp.tile(in_gain.astype(f32), 2), 0.0))
    small = small.at[1].set(jnp.where(pair_mask, jnp.tile(post_gain.astype(f32), 2), 0.0))
    small = small.at[2, :2].set(block_of[0].astype(f32))

    attn_in, all_small, mine_qkv, mine_output = front(hidden, small, w_query, w_key, w_value, w_output)
    attn_in = attn_in.reshape(seq_rows, model_width)
    mine_qkv = mine_qkv.reshape(model_width, -1)
    mine_output = mine_output.reshape(-1, model_width)
    paired = all_small.reshape(n_ctx * n_fsdp // 2, 2, 8, 2 * depth).sum(axis=1)
    full_in_gain, full_post = paired[:, 0].reshape(model_width), paired[:, 1].reshape(model_width)
    own_row = lax.dynamic_index_in_dim(
        all_small.reshape(n_ctx, n_fsdp, 8, 2 * depth), lax.axis_index("fsdp"), axis=1, keepdims=False
    )
    all_blocks = own_row[:, 2, :2].reshape(2 * n_ctx).astype(jnp.int32)
    offsets = jnp.arange(block_rows, dtype=jnp.int32)
    positions = (all_blocks[:, None] * block_rows + offsets[None, :]).reshape(seq_rows)
    cosine, sine = rope_tables(positions, head_dim)

    grad_out, mine_gu, mine_down = second(cot_local, w_gate, w_up, w_down)
    mine_gu = mine_gu.reshape(model_width, -1)
    mine_down = mine_down.reshape(-1, model_width)

    qkv = jnp.dot(attn_in, mine_qkv, preferred_element_type=f32)
    q_width, k_width = q_heads * head_dim, kv_heads * head_dim
    q_raw = qkv[:, :q_width].reshape(seq_rows, q_heads, head_dim)
    k_raw = qkv[:, q_width : q_width + k_width].reshape(seq_rows, kv_heads, head_dim)
    values = qkv[:, q_width + k_width :].astype(bf16).reshape(seq_rows, kv_heads, head_dim)
    q_rms = lax.rsqrt(jnp.mean(q_raw * q_raw, axis=-1, keepdims=True) + EPS)
    q_unit = q_raw * q_rms
    queries = (rotate(q_unit * q_gain.astype(f32), cosine, sine) * q_scale).astype(bf16)
    queries = queries.reshape(seq_rows, kv_heads, group, head_dim)
    k_rms = lax.rsqrt(jnp.mean(k_raw * k_raw, axis=-1, keepdims=True) + EPS)
    k_unit = k_raw * k_rms
    keys = rotate(k_unit * k_gain.astype(f32), cosine, sine).astype(bf16)

    visible = positions[None, :] <= positions[:, None]
    scores = jnp.einsum("qhgd,khd->hgqk", queries, keys, preferred_element_type=f32)
    scores = jnp.where(visible, scores, -1e30)
    peak = jnp.max(scores, axis=-1, keepdims=True)
    weights = jnp.exp(scores - peak)
    probs = weights / jnp.sum(weights, axis=-1, keepdims=True)
    attn = jnp.einsum("hgqk,khd->qhgd", probs.astype(bf16), values, preferred_element_type=f32)
    attn_bf = attn.reshape(seq_rows, q_heads * head_dim).astype(bf16)

    output, grad_mid, post_sum, grad_branch, gu_total, part_down = feed_forward(
        attn_bf, mine_output, hidden, full_post, mine_gu, mine_down, grad_out
    )
    grad_branch = grad_branch.reshape(seq_rows, model_width)

    def by_owner(part):
        return part.reshape(n_ctx, n_fsdp, depth, -1).transpose(1, 0, 2, 3)

    output_part = lax.dot_general(attn_bf, grad_branch, contract_rows, preferred_element_type=f32).astype(bf16)
    grad_attn = lax.dot_general(grad_branch, mine_output, contract_cols, preferred_element_type=f32).astype(bf16)
    grad_attn = grad_attn.reshape(seq_rows, kv_heads, group, head_dim)
    delta = jnp.einsum("qhgd,qhgd->hgq", grad_attn.astype(f32), attn)
    grad_probs = jnp.einsum("qhgd,khd->hgqk", grad_attn, values, preferred_element_type=f32)
    grad_scores = (probs * (grad_probs - delta[..., None])).astype(bf16)
    grad_queries = jnp.einsum("hgqk,khd->qhgd", grad_scores, keys, preferred_element_type=f32)
    grad_keys = jnp.einsum("hgqk,qhgd->khd", grad_scores, queries, preferred_element_type=f32)
    grad_values = jnp.einsum("hgqk,qhgd->khd", probs.astype(bf16), grad_attn, preferred_element_type=f32)

    grad_q_normed = rotate(grad_queries.reshape(seq_rows, q_heads, head_dim) * q_scale, cosine, -sine)
    q_sum = jnp.sum(grad_q_normed * q_unit, axis=(0, 1))
    grad_q_raw = norm_back(grad_q_normed * q_gain.astype(f32), q_unit, q_rms).astype(bf16).reshape(seq_rows, q_width)
    grad_k_normed = rotate(grad_keys, cosine, -sine)
    k_sum = jnp.sum(grad_k_normed * k_unit, axis=(0, 1))
    grad_k_raw = norm_back(grad_k_normed * k_gain.astype(f32), k_unit, k_rms).astype(bf16).reshape(seq_rows, k_width)
    grad_v = grad_values.astype(bf16).reshape(seq_rows, k_width)
    grad_qkv = jnp.concatenate([grad_q_raw, grad_k_raw, grad_v], axis=1)
    qkv_part = lax.dot_general(attn_in, grad_qkv, contract_rows, preferred_element_type=f32).astype(bf16)
    grad_input, gains, part_query, part_key, part_value, part_output, part_gate, part_up = back(
        grad_qkv,
        mine_qkv,
        hidden,
        grad_mid,
        full_in_gain,
        post_sum,
        q_sum,
        k_sum,
        by_owner(qkv_part),
        output_part.reshape(n_fsdp, -1, model_width),
        gu_total,
        [w_query.shape[1], w_key.shape[1], w_value.shape[1]],
    )
    part_in = lax.dynamic_slice_in_dim(gains[0], side * depth, depth)
    part_post = lax.dynamic_slice_in_dim(gains[1], side * depth, depth)
    return (
        output.reshape(seq_count, tok_rows, model_width),
        grad_input.reshape(seq_count, tok_rows, model_width),
        part_in,
        part_query,
        part_key,
        part_value,
        part_output,
        gains[2],
        gains[3],
        part_post,
        part_gate,
        part_up,
        part_down,
    )


def solution(mesh):
    body = tp_body if KV_HEADS % mesh.shape["ctx"] == 0 else gathered_weights_body
    return jax.shard_map(
        body,
        mesh=mesh,
        in_specs=(
            P("fsdp", "ctx", None),
            P("fsdp", "ctx"),
            P(("ctx", "fsdp")),
            P(("ctx", "fsdp"), None),
            P(("ctx", "fsdp"), None),
            P(("ctx", "fsdp"), None),
            P(("ctx", "fsdp"), None),
            P(),
            P(),
            P(("ctx", "fsdp")),
            P(("ctx", "fsdp"), None),
            P(("ctx", "fsdp"), None),
            P(("ctx", "fsdp"), None),
            P("fsdp", "ctx", None),
        ),
        out_specs=(
            P("fsdp", "ctx", None),
            P("fsdp", "ctx", None),
            P(("ctx", "fsdp")),
            P(("ctx", "fsdp"), None),
            P(("ctx", "fsdp"), None),
            P(("ctx", "fsdp"), None),
            P(("ctx", "fsdp"), None),
            P(),
            P(),
            P(("ctx", "fsdp")),
            P(("ctx", "fsdp"), None),
            P(("ctx", "fsdp"), None),
            P(("ctx", "fsdp"), None),
        ),
        check_vma=False,
    )
```

```python
import functools
import math

import jax
import jax.numpy as jnp
import numpy as np
from jax import lax
from jax.experimental import pallas as pl
from jax.experimental.pallas import tpu as pltpu
from jax.sharding import PartitionSpec as P

EPS = 1e-06
THETA = 1000000.0
KV_HEADS = 8


def rope_tables(positions, width):
    half_width = width // 2
    inverse = THETA ** (-(jnp.arange(half_width, dtype=jnp.float32) * 2.0 / width))
    angles = positions.astype(jnp.float32)[:, None] * inverse[None, :]
    return (jnp.cos(angles), jnp.sin(angles))


def rotate(values, cosine, sine):
    half_width = values.shape[-1] // 2
    first = values[..., :half_width]
    second = values[..., half_width:]
    cos_wide = cosine[:, None, :]
    sin_wide = sine[:, None, :]
    return jnp.concatenate(
        [first * cos_wide - second * sin_wide, second * cos_wide + first * sin_wide], axis=-1
    )


def norm_back(grad_normed, normed, scale):
    return scale * (grad_normed - normed * jnp.mean(grad_normed * normed, axis=-1, keepdims=True))


def gathered_weights_body(
    hidden_in,
    block_of,
    in_gain,
    w_query,
    w_key,
    w_value,
    w_output,
    q_gain,
    k_gain,
    post_gain,
    w_gate,
    w_up,
    w_down,
    cotangent,
):
    seq_count = hidden_in.shape[0]
    tok_rows = hidden_in.shape[1]
    flat_rows = seq_count * tok_rows
    model_width = hidden_in.shape[2]
    block_rows = tok_rows // 2
    block_total = 2 * lax.axis_size("ctx")
    seq_len = block_total * block_rows
    head_dim = q_gain.shape[0]
    q_heads = w_query.shape[1] // head_dim
    kv_heads = w_key.shape[1] // head_dim
    group_size = q_heads // kv_heads
    tile_blocks = math.gcd(block_total, max(1, 512 // block_rows))
    tile_rows = tile_blocks * block_rows
    q_scale = head_dim ** (-0.5)
    contract_rows = (((0,), (0,)), ((), ()))
    contract_cols = (((1,), (1,)), ((), ()))
    offsets = jnp.arange(block_rows, dtype=jnp.int32)
    positions = (block_of[:, :, None] * block_rows + offsets[None, None, :]).reshape(flat_rows)
    cosine, sine = rope_tables(positions, head_dim)
    residual = hidden_in.reshape(flat_rows, model_width).astype(jnp.float32)
    full_in_gain, full_query, full_key, full_value, full_output = (
        lax.all_gather(in_gain, ("ctx", "fsdp"), axis=0, tiled=True),
        lax.all_gather(w_query, ("ctx", "fsdp"), axis=0, tiled=True),
        lax.all_gather(w_key, ("ctx", "fsdp"), axis=0, tiled=True),
        lax.all_gather(w_value, ("ctx", "fsdp"), axis=0, tiled=True),
        lax.all_gather(w_output, ("ctx", "fsdp"), axis=0, tiled=True),
    )
    in_scale = lax.rsqrt(jnp.mean(residual * residual, axis=-1, keepdims=True) + EPS)
    in_normed = residual * in_scale
    attn_in = (in_normed * full_in_gain.astype(jnp.float32)).astype(jnp.bfloat16)
    q_raw = jnp.dot(attn_in, full_query, preferred_element_type=jnp.float32).reshape(
        flat_rows, q_heads, head_dim
    )
    k_raw = jnp.dot(attn_in, full_key, preferred_element_type=jnp.float32).reshape(
        flat_rows, kv_heads, head_dim
    )
    v_local = jnp.dot(attn_in, full_value, preferred_element_type=jnp.float32).astype(jnp.bfloat16)
    q_rms = lax.rsqrt(jnp.mean(q_raw * q_raw, axis=-1, keepdims=True) + EPS)
    q_unit = q_raw * q_rms
    queries = (rotate(q_unit * q_gain.astype(jnp.float32), cosine, sine) * q_scale).astype(
        jnp.bfloat16
    )
    k_rms = lax.rsqrt(jnp.mean(k_raw * k_raw, axis=-1, keepdims=True) + EPS)
    k_unit = k_raw * k_rms
    keys_local = rotate(k_unit * k_gain.astype(jnp.float32), cosine, sine).astype(jnp.bfloat16)
    all_keys, all_values, all_slots = (
        lax.all_gather(
            keys_local.reshape(seq_count, tok_rows, kv_heads * head_dim), "ctx", axis=1, tiled=True
        ),
        lax.all_gather(
            v_local.reshape(seq_count, tok_rows, kv_heads * head_dim), "ctx", axis=1, tiled=True
        ),
        lax.all_gather(block_of, "ctx", axis=1, tiled=True),
    )

    def tile_scores(query_tile, key_tile, query_pos, step):
        scores = jnp.einsum(
            "qhgd,khd->hgqk", query_tile, key_tile, preferred_element_type=jnp.float32
        )
        key_pos = step * tile_rows + jnp.arange(tile_rows, dtype=jnp.int32)
        visible = key_pos[None, :] <= query_pos[:, None]
        return (scores, visible)

    def sequence_tables(seq):
        key_blocks = all_keys[seq].reshape(block_total, block_rows, kv_heads, head_dim)
        value_blocks = all_values[seq].reshape(block_total, block_rows, kv_heads, head_dim)
        block_index = (
            jnp.zeros((block_total,), jnp.int32)
            .at[all_slots[seq]]
            .set(jnp.arange(block_total, dtype=jnp.int32))
        )
        return (key_blocks, value_blocks, block_index)

    def tile_index(block_index, step):
        return lax.dynamic_slice_in_dim(block_index, step * tile_blocks, tile_blocks)

    def fetch(table, block_index, step):
        return jnp.take(table, tile_index(block_index, step), axis=0).reshape(
            tile_rows, kv_heads, head_dim
        )

    log_totals = []
    attn_parts = []
    seq = 0
    key_blocks, value_blocks, block_index = sequence_tables(seq)
    for which in range(2):
        slot = 2 * seq + which
        query_tile = queries[slot * block_rows : (slot + 1) * block_rows].reshape(
            block_rows, kv_heads, group_size, head_dim
        )
        query_pos = positions[slot * block_rows : (slot + 1) * block_rows]
        tile_count = block_of[seq, which] // tile_blocks + 1

        def max_step(step, carry):
            running_max, running_sum = carry
            scores, visible = tile_scores(
                query_tile, fetch(key_blocks, block_index, step), query_pos, step
            )
            scores = jnp.where(visible, scores, -1e30)
            new_max = jnp.maximum(running_max, jnp.max(scores, axis=-1))
            running_sum = running_sum * jnp.exp(running_max - new_max) + jnp.sum(
                jnp.exp(scores - new_max[..., None]), axis=-1
            )
            return (new_max, running_sum)

        start_max = jnp.full((kv_heads, group_size, block_rows), -1e30, jnp.float32)
        start_sum = jnp.zeros((kv_heads, group_size, block_rows), jnp.float32)
        running_max, running_sum = lax.fori_loop(0, tile_count, max_step, (start_max, start_sum))
        log_total = running_max + jnp.log(running_sum)

        def value_step(step, total):
            scores, visible = tile_scores(
                query_tile, fetch(key_blocks, block_index, step), query_pos, step
            )
            probs = jnp.where(visible, jnp.exp(scores - log_total[..., None]), 0.0)
            return total + jnp.einsum(
                "hgqk,khd->qhgd",
                probs.astype(jnp.bfloat16),
                fetch(value_blocks, block_index, step),
                preferred_element_type=jnp.float32,
            )

        attn_part = lax.fori_loop(
            0,
            tile_count,
            value_step,
            jnp.zeros((block_rows, kv_heads, group_size, head_dim), jnp.float32),
        )
        log_totals.append(log_total)
        attn_parts.append(attn_part)
    attn_full = jnp.concatenate(attn_parts, axis=0)
    attn_bf = attn_full.reshape(flat_rows, q_heads * head_dim).astype(jnp.bfloat16)
    branch = jnp.dot(attn_bf, full_output, preferred_element_type=jnp.float32)
    hidden_mid = residual + branch
    full_post, full_gate, full_up, full_down = (
        lax.all_gather(post_gain, ("ctx", "fsdp"), axis=0, tiled=True),
        lax.all_gather(w_gate, ("ctx", "fsdp"), axis=0, tiled=True),
        lax.all_gather(w_up, ("ctx", "fsdp"), axis=0, tiled=True),
        lax.all_gather(w_down, ("ctx", "fsdp"), axis=0, tiled=True),
    )
    post_scale = lax.rsqrt(jnp.mean(hidden_mid * hidden_mid, axis=-1, keepdims=True) + EPS)
    post_normed = hidden_mid * post_scale
    mlp_in = (post_normed * full_post.astype(jnp.float32)).astype(jnp.bfloat16)
    gate_pre = jnp.dot(mlp_in, full_gate, preferred_element_type=jnp.float32)
    up_pre = jnp.dot(mlp_in, full_up, preferred_element_type=jnp.float32)
    sigmoid_gate = jax.nn.sigmoid(gate_pre)
    activated = gate_pre * sigmoid_gate
    inner = (activated * up_pre).astype(jnp.bfloat16)
    mlp_out = jnp.dot(inner, full_down, preferred_element_type=jnp.float32)
    output = (hidden_mid + mlp_out).astype(jnp.bfloat16)
    full_post, full_gate, full_up, full_down = (
        lax.all_gather(post_gain, ("ctx", "fsdp"), axis=0, tiled=True),
        lax.all_gather(w_gate, ("ctx", "fsdp"), axis=0, tiled=True),
        lax.all_gather(w_up, ("ctx", "fsdp"), axis=0, tiled=True),
        lax.all_gather(w_down, ("ctx", "fsdp"), axis=0, tiled=True),
    )
    grad_out = cotangent.reshape(flat_rows, model_width)
    grad_down = lax.dot_general(inner, grad_out, contract_rows, preferred_element_type=jnp.float32)
    part_down = lax.psum_scatter(grad_down, ("ctx", "fsdp"), scatter_dimension=0, tiled=True)
    grad_inner = lax.dot_general(
        grad_out, full_down, contract_cols, preferred_element_type=jnp.float32
    )
    grad_gate_pre = (
        grad_inner * up_pre * sigmoid_gate * (1.0 + gate_pre * (1.0 - sigmoid_gate))
    ).astype(jnp.bfloat16)
    grad_up_pre = (grad_inner * activated).astype(jnp.bfloat16)
    grad_gate = lax.dot_general(
        mlp_in, grad_gate_pre, contract_rows, preferred_element_type=jnp.float32
    )
    grad_up = lax.dot_general(
        mlp_in, grad_up_pre, contract_rows, preferred_element_type=jnp.float32
    )
    grad_mlp_in = lax.dot_general(
        grad_gate_pre, full_gate, contract_cols, preferred_element_type=jnp.float32
    ) + lax.dot_general(grad_up_pre, full_up, contract_cols, preferred_element_type=jnp.float32)
    grad_post_gain = jnp.sum(grad_mlp_in * post_normed, axis=0)
    grad_mid = grad_out.astype(jnp.float32) + norm_back(
        grad_mlp_in * full_post.astype(jnp.float32), post_normed, post_scale
    )
    part_post, part_gate, part_up = (
        lax.psum_scatter(grad_post_gain, ("ctx", "fsdp"), scatter_dimension=0, tiled=True),
        lax.psum_scatter(grad_gate, ("ctx", "fsdp"), scatter_dimension=0, tiled=True),
        lax.psum_scatter(grad_up, ("ctx", "fsdp"), scatter_dimension=0, tiled=True),
    )
    full_in_gain, full_query, full_key, full_value, full_output = (
        lax.all_gather(in_gain, ("ctx", "fsdp"), axis=0, tiled=True),
        lax.all_gather(w_query, ("ctx", "fsdp"), axis=0, tiled=True),
        lax.all_gather(w_key, ("ctx", "fsdp"), axis=0, tiled=True),
        lax.all_gather(w_value, ("ctx", "fsdp"), axis=0, tiled=True),
        lax.all_gather(w_output, ("ctx", "fsdp"), axis=0, tiled=True),
    )
    grad_branch = grad_mid.astype(jnp.bfloat16)
    grad_output = lax.dot_general(
        attn_bf, grad_branch, contract_rows, preferred_element_type=jnp.float32
    )
    grad_attn = lax.dot_general(
        grad_branch, full_output, contract_cols, preferred_element_type=jnp.float32
    ).astype(jnp.bfloat16)
    grad_attn = grad_attn.reshape(flat_rows, kv_heads, group_size, head_dim)
    query_grads = []
    seq = 0
    key_blocks, value_blocks, block_index = sequence_tables(seq)
    key_grads = jnp.zeros((block_total, block_rows, kv_heads, head_dim), jnp.float32)
    value_grads = jnp.zeros((block_total, block_rows, kv_heads, head_dim), jnp.float32)
    for which in range(2):
        slot = 2 * seq + which
        query_tile = queries[slot * block_rows : (slot + 1) * block_rows].reshape(
            block_rows, kv_heads, group_size, head_dim
        )
        query_pos = positions[slot * block_rows : (slot + 1) * block_rows]
        grad_tile = grad_attn[slot * block_rows : (slot + 1) * block_rows]
        tile_count = block_of[seq, which] // tile_blocks + 1
        delta = jnp.einsum("qhgd,qhgd->hgq", grad_tile.astype(jnp.float32), attn_parts[slot])
        log_total = log_totals[slot]

        def grad_step(step, carry):
            grad_query, keys_acc, values_acc = carry
            key_tile = fetch(key_blocks, block_index, step)
            scores, visible = tile_scores(query_tile, key_tile, query_pos, step)
            probs = jnp.where(visible, jnp.exp(scores - log_total[..., None]), 0.0)
            grad_probs = jnp.einsum(
                "qhgd,khd->hgqk",
                grad_tile,
                fetch(value_blocks, block_index, step),
                preferred_element_type=jnp.float32,
            )
            grad_scores = (probs * (grad_probs - delta[..., None])).astype(jnp.bfloat16)
            grad_query = grad_query + jnp.einsum(
                "hgqk,khd->qhgd", grad_scores, key_tile, preferred_element_type=jnp.float32
            )
            key_part = jnp.einsum(
                "hgqk,qhgd->khd", grad_scores, query_tile, preferred_element_type=jnp.float32
            )
            value_part = jnp.einsum(
                "hgqk,qhgd->khd",
                probs.astype(jnp.bfloat16),
                grad_tile,
                preferred_element_type=jnp.float32,
            )
            places = tile_index(block_index, step)
            keys_acc = keys_acc.at[places].add(
                key_part.reshape(tile_blocks, block_rows, kv_heads, head_dim)
            )
            values_acc = values_acc.at[places].add(
                value_part.reshape(tile_blocks, block_rows, kv_heads, head_dim)
            )
            return (grad_query, keys_acc, values_acc)

        start_query = jnp.zeros((block_rows, kv_heads, group_size, head_dim), jnp.float32)
        grad_query, key_grads, value_grads = lax.fori_loop(
            0, tile_count, grad_step, (start_query, key_grads, value_grads)
        )
        query_grads.append(grad_query)
    key_grad_list = [key_grads.reshape(seq_len, kv_heads * head_dim)]
    value_grad_list = [value_grads.reshape(seq_len, kv_heads * head_dim)]
    grad_keys, grad_values = (
        lax.psum_scatter(
            jnp.stack(key_grad_list, axis=0).astype(jnp.bfloat16),
            "ctx",
            scatter_dimension=1,
            tiled=True,
        ).astype(jnp.float32),
        lax.psum_scatter(
            jnp.stack(value_grad_list, axis=0).astype(jnp.bfloat16),
            "ctx",
            scatter_dimension=1,
            tiled=True,
        ).astype(jnp.float32),
    )
    grad_q_rot = (
        jnp.concatenate(query_grads, axis=0).reshape(flat_rows, q_heads, head_dim) * q_scale
    )
    grad_q_normed = rotate(grad_q_rot, cosine, -sine)
    grad_q_gain = jnp.sum(grad_q_normed * q_unit, axis=(0, 1))
    grad_q_raw = (
        norm_back(grad_q_normed * q_gain.astype(jnp.float32), q_unit, q_rms)
        .astype(jnp.bfloat16)
        .reshape(flat_rows, q_heads * head_dim)
    )
    grad_k_normed = rotate(grad_keys.reshape(flat_rows, kv_heads, head_dim), cosine, -sine)
    grad_k_gain = jnp.sum(grad_k_normed * k_unit, axis=(0, 1))
    grad_k_raw = (
        norm_back(grad_k_normed * k_gain.astype(jnp.float32), k_unit, k_rms)
        .astype(jnp.bfloat16)
        .reshape(flat_rows, kv_heads * head_dim)
    )
    grad_v_local = grad_values.reshape(flat_rows, kv_heads * head_dim).astype(jnp.bfloat16)
    grad_query_w = lax.dot_general(
        attn_in, grad_q_raw, contract_rows, preferred_element_type=jnp.float32
    )
    grad_key_w = lax.dot_general(
        attn_in, grad_k_raw, contract_rows, preferred_element_type=jnp.float32
    )
    grad_value_w = lax.dot_general(
        attn_in, grad_v_local, contract_rows, preferred_element_type=jnp.float32
    )
    grad_attn_in = lax.dot_general(
        grad_q_raw, full_query, contract_cols, preferred_element_type=jnp.float32
    )
    grad_attn_in = grad_attn_in + lax.dot_general(
        grad_k_raw, full_key, contract_cols, preferred_element_type=jnp.float32
    )
    grad_attn_in = grad_attn_in + lax.dot_general(
        grad_v_local, full_value, contract_cols, preferred_element_type=jnp.float32
    )
    grad_in_gain = jnp.sum(grad_attn_in * in_normed, axis=0)
    grad_input = grad_mid + norm_back(
        grad_attn_in * full_in_gain.astype(jnp.float32), in_normed, in_scale
    )
    part_in, part_query, part_key, part_value, part_output = (
        lax.psum_scatter(grad_in_gain, ("ctx", "fsdp"), scatter_dimension=0, tiled=True),
        lax.psum_scatter(grad_query_w, ("ctx", "fsdp"), scatter_dimension=0, tiled=True),
        lax.psum_scatter(grad_key_w, ("ctx", "fsdp"), scatter_dimension=0, tiled=True),
        lax.psum_scatter(grad_value_w, ("ctx", "fsdp"), scatter_dimension=0, tiled=True),
        lax.psum_scatter(grad_output, ("ctx", "fsdp"), scatter_dimension=0, tiled=True),
    )
    sum_q_gain, sum_k_gain = lax.psum((grad_q_gain, grad_k_gain), ("ctx", "fsdp"))
    return (
        output.reshape(seq_count, tok_rows, model_width),
        grad_input.reshape(seq_count, tok_rows, model_width),
        part_in,
        part_query,
        part_key,
        part_value,
        part_output,
        sum_q_gain,
        sum_k_gain,
        part_post,
        part_gate,
        part_up,
        part_down,
    )


MESH = pl.DeviceIdType.MESH
SUBS = 2


def ring_position(index, size):
    column, line = lax.rem(index, 2), lax.div(index, 2)
    return column * (line + 1) + (1 - column) * lax.rem(size - line, size)


def ring_member(position, size):
    late = lax.div(position + size // 2 - 1, size)
    beyond = lax.div(position + size - 1, size)
    return beyond * (1 - late) * (2 * position - 1) + late * 2 * (size - position)


class Ring:
    def __init__(self, size):
        self.size = size
        self.me = lax.axis_index("ctx")
        self.row = lax.axis_index("fsdp")
        self.position = ring_position(self.me, size)

    def member(self, way, steps):
        ahead = self.size - steps if way == 0 else steps
        return ring_member(lax.rem(self.position + ahead, self.size), self.size)

    def target(self, way):
        return (self.member(way, self.size - 1), self.row)

    def barrier(self):
        barrier = pltpu.get_barrier_semaphore()
        for way in range(2):
            pl.semaphore_signal(barrier, inc=1, device_id=self.target(way), device_id_type=MESH)
        pl.semaphore_wait(barrier, 2)


class GatherRing:
    def __init__(self, ring, own, out, send_sems, recv_sems):
        self.ring, self.own, self.out, self.send_sems, self.recv_sems = ring, own, out, send_sems, recv_sems
        self.half = own.shape[0] // 2
        self.sub = self.half // SUBS

    def copy(self, way, step, part, first=False):
        place = pl.ds(way * self.half + part * self.sub, self.sub)
        owner = self.ring.me if first else self.ring.member(way, step)
        source = self.own.at[place] if first else self.out.at[owner, place]
        return pltpu.make_async_remote_copy(
            src_ref=source,
            dst_ref=self.out.at[owner, place],
            send_sem=self.send_sems.at[way, step, part],
            recv_sem=self.recv_sems.at[way, step, part],
            device_id=self.ring.target(way),
            device_id_type=MESH,
        )

    def start(self, way):
        for part in range(SUBS):
            self.copy(way, 0, part, first=True).start()

    def step(self, step):
        for part in range(SUBS):
            for way in range(2):
                self.copy(way, step - 1, part).wait_recv()
                self.copy(way, step, part).start()

    def finish(self):
        last = self.ring.size - 2
        for part in range(SUBS):
            for way in range(2):
                self.copy(way, last, part).wait_recv()

        @pl.loop(0, last + 1)
        def _(step):
            for part in range(SUBS):
                for way in range(2):
                    self.copy(way, step, part).wait_send()

    def run(self):
        for way in range(2):
            self.start(way)

        @pl.loop(1, self.ring.size - 1)
        def _(step):
            self.step(step)

        self.finish()


def gather_sems(size):
    return [pltpu.SemaphoreType.DMA((2, size - 1, SUBS)), pltpu.SemaphoreType.DMA((2, size - 1, SUBS))]


class SumRing:
    def __init__(self, ring, compute, terms, outgoing, incoming, send_sems, recv_sems):
        self.ring, self.compute, self.terms = ring, compute, terms
        self.outgoing, self.incoming, self.send_sems, self.recv_sems = outgoing, incoming, send_sems, recv_sems
        self.half = terms.shape[1]
        self.sub = self.half // SUBS

    def copy(self, way, step, part):
        place = pl.ds(part * self.sub, self.sub)
        return pltpu.make_async_remote_copy(
            src_ref=self.outgoing.at[way, lax.rem(step, 2), place],
            dst_ref=self.incoming.at[way, step, place],
            send_sem=self.send_sems.at[way, step, part],
            recv_sem=self.recv_sems.at[way, step, part],
            device_id=self.ring.target(way),
            device_id_type=MESH,
        )

    def terms_of(self, step):
        self.compute([self.ring.member(way, step + 1) for way in range(2)])

    def begin(self):
        self.terms_of(0)
        for part in range(SUBS):
            place = pl.ds(part * self.sub, self.sub)
            for way in range(2):
                self.outgoing[way, 0, place] = self.terms[way, place].astype(jnp.bfloat16)
                self.copy(way, 0, part).start()

    def second(self):
        self.step(1, fresh=True)

    def step(self, step, fresh=False):
        self.terms_of(step)
        for part in range(SUBS):
            place = pl.ds(part * self.sub, self.sub)
            for way in range(2):
                self.copy(way, step - 1, part).wait_recv()
                total = self.terms[way, place] + self.incoming[way, step - 1, place].astype(jnp.float32)
                if not fresh:
                    self.copy(way, step - 2, part).wait_send()
                self.outgoing[way, lax.rem(step, 2), place] = total.astype(jnp.bfloat16)
                self.copy(way, step, part).start()

    def last_terms(self):
        self.compute([self.ring.me, self.ring.me])

    def result(self, way):
        last = self.ring.size - 2
        for part in range(SUBS):
            self.copy(way, last, part).wait_recv()
        return self.terms[way] + self.incoming[way, last].astype(jnp.float32)

    def finish(self):
        for step in (self.ring.size - 3, self.ring.size - 2):
            for part in range(SUBS):
                for way in range(2):
                    self.copy(way, step, part).wait_send()

    def run(self):
        self.begin()
        self.second()

        @pl.loop(2, self.ring.size - 1)
        def _(step):
            self.step(step)

        self.last_terms()


def sum_scratch(size, rows, width):
    half = rows // 2
    return [
        pltpu.VMEM((2, half, width), jnp.float32),
        pltpu.VMEM((2, 2, half, width), jnp.bfloat16),
        pltpu.VMEM((2, size - 1, half, width), jnp.bfloat16),
        pltpu.SemaphoreType.DMA((2, size - 1, SUBS)),
        pltpu.SemaphoreType.DMA((2, size - 1, SUBS)),
    ]


TILE = 512


def row_terms(left, weight, terms):
    half = terms.shape[1]

    def compute(members):
        lines = jnp.concatenate([left[members[way], way * half : (way + 1) * half] for way in range(2)], axis=0)

        @pl.loop(0, weight.shape[1] // TILE)
        def _(tile):
            columns = pl.ds(pl.multiple_of(tile * TILE, TILE), TILE)
            product = jnp.dot(lines, weight[:, columns], preferred_element_type=jnp.float32)
            for way in range(2):
                terms[way, :, columns] = product[way * half : (way + 1) * half]

    return compute


def row_terms_t(left, weight, terms):
    half = terms.shape[1]

    def compute(members):
        lines = jnp.concatenate([left[members[way], way * half : (way + 1) * half] for way in range(2)], axis=0)

        @pl.loop(0, weight.shape[0] // TILE)
        def _(tile):
            columns = pl.ds(pl.multiple_of(tile * TILE, TILE), TILE)
            product = lax.dot_general(
                lines, weight[columns, :], (((1,), (1,)), ((), ())), preferred_element_type=jnp.float32
            )
            for way in range(2):
                terms[way, :, columns] = product[way * half : (way + 1) * half]

    return compute


VMEM_SPEC = pl.BlockSpec(memory_space=pltpu.VMEM)
ANY_SPEC = pl.BlockSpec(memory_space=pl.ANY)


def ctx_peer(ring, ahead):
    return lax.rem(ring.me + ahead, ring.size)


def across(row, n_fsdp):
    return lax.rem(row + n_fsdp // 2, n_fsdp)


def beside(row):
    return row + 1 - 2 * lax.rem(row, 2)


def remote(source, target, send_sem, recv_sem, device):
    return pltpu.make_async_remote_copy(
        src_ref=source,
        dst_ref=target,
        send_sem=send_sem,
        recv_sem=recv_sem,
        device_id=device,
        device_id_type=MESH,
    )


def greet(devices):
    barrier = pltpu.get_barrier_semaphore()
    for device in devices:
        pl.semaphore_signal(barrier, inc=1, device_id=device, device_id_type=MESH)
    pl.semaphore_wait(barrier, len(devices))


def near_devices(ring, n_fsdp):
    return [(ctx_peer(ring, ahead), ring.row) for ahead in range(1, ring.size)] + [
        (ring.me, across(ring.row, n_fsdp)),
        (ring.me, beside(ring.row)),
    ]


class Others:
    def __init__(self, ring, n_fsdp):
        self.ring, self.n_fsdp, self.count = ring, n_fsdp, ring.size * n_fsdp
        self.index = ring.me * n_fsdp + ring.row

    def each(self, act):
        @pl.loop(0, self.count)
        def _(other):
            @pl.when(other != self.index)
            def _():
                act(other, (lax.div(other, self.n_fsdp), lax.rem(other, self.n_fsdp)))

    def greet(self):
        barrier = pltpu.get_barrier_semaphore()
        self.each(lambda other, device: pl.semaphore_signal(barrier, inc=1, device_id=device, device_id_type=MESH))
        pl.semaphore_wait(barrier, self.count - 1)


class Rows:
    def __init__(self, ring, n_fsdp, shard, out, send_sems, recv_sems):
        own, far, twin = ring.row, across(ring.row, n_fsdp), beside(ring.row)
        self.keep = pltpu.make_async_copy(shard, out.at[own], send_sems.at[3])
        self.to_far = remote(shard, out.at[own], send_sems.at[0], recv_sems.at[0], (ring.me, far))
        self.to_twin = remote(shard, out.at[own], send_sems.at[1], recv_sems.at[1], (ring.me, twin))
        self.pass_on = remote(out.at[far], out.at[far], send_sems.at[2], recv_sems.at[2], (ring.me, twin))

    def begin(self):
        self.keep.start()
        self.to_far.start()
        self.to_twin.start()

    def relay(self):
        self.to_far.wait_recv()
        self.pass_on.start()

    def finish(self):
        self.keep.wait()
        self.to_far.wait_send()
        self.to_twin.wait()
        self.pass_on.wait()


def rows_sems():
    return [pltpu.SemaphoreType.DMA((4,)), pltpu.SemaphoreType.DMA((3,))]


class Columns:
    def __init__(self, ring, n_fsdp, shards, out, send_sems, recv_sems, link_send, link_recv):
        self.ring, self.shards, self.out, self.send_sems, self.recv_sems = ring, shards, out, send_sems, recv_sems
        own, far, twin = ring.row, across(ring.row, n_fsdp), beside(ring.row)
        self.widths = [shard.shape[1] // ring.size for shard in shards]
        self.to_far = remote(out.at[:, own], out.at[:, own], link_send.at[0], link_recv.at[0], (ring.me, far))
        self.to_twin = remote(out.at[:, own], out.at[:, own], link_send.at[1], link_recv.at[1], (ring.me, twin))
        self.pass_on = remote(out.at[:, far], out.at[:, far], link_send.at[2], link_recv.at[2], (ring.me, twin))

    def piece(self, which, ahead):
        member = ctx_peer(self.ring, ahead)
        width = self.widths[which]
        start = sum(self.widths[:which])
        source = self.shards[which].at[:, pl.ds(pl.multiple_of(member * width, width), width)]
        target = self.out.at[self.ring.me, self.ring.row, :, pl.ds(start, width)]
        if ahead == 0:
            return pltpu.make_async_copy(source, target, self.send_sems.at[which, 0])
        return remote(
            source, target, self.send_sems.at[which, ahead], self.recv_sems.at[which, ahead], (member, self.ring.row)
        )

    def begin(self):
        for ahead in range(self.ring.size):
            for which in range(len(self.shards)):
                self.piece(which, ahead).start()

    def spread(self):
        for ahead in range(self.ring.size):
            for which in range(len(self.shards)):
                if ahead:
                    self.piece(which, ahead).wait_recv()
                else:
                    self.piece(which, ahead).wait()
        self.to_far.start()
        self.to_twin.start()

    def relay(self):
        self.to_far.wait_recv()
        self.pass_on.start()

    def finish(self):
        for ahead in range(1, self.ring.size):
            for which in range(len(self.shards)):
                self.piece(which, ahead).wait_send()
        self.to_far.wait_send()
        self.to_twin.wait()
        self.pass_on.wait()


def columns_sems(size, count):
    return [
        pltpu.SemaphoreType.DMA((count, size)),
        pltpu.SemaphoreType.DMA((count, size)),
        pltpu.SemaphoreType.DMA((3,)),
        pltpu.SemaphoreType.DMA((3,)),
    ]


class RowGrads:
    def __init__(self, ring, n_fsdp, part, from_twin, to_far, from_far, send_sems, recv_sems):
        own, far, twin = ring.row, across(ring.row, n_fsdp), beside(ring.row)
        self.part, self.from_twin, self.to_far, self.from_far = part, from_twin, to_far, from_far
        self.own, self.far = own, far
        twin_far = across(twin, n_fsdp)
        self.first = [
            remote(part.at[twin], from_twin.at[0], send_sems.at[0], recv_sems.at[0], (ring.me, twin)),
            remote(part.at[twin_far], from_twin.at[1], send_sems.at[1], recv_sems.at[1], (ring.me, twin)),
        ]
        if to_far is None:
            self.to_far = part.at[far]
        self.second = remote(self.to_far, from_far, send_sems.at[2], recv_sems.at[2], (ring.me, far))

    def begin(self):
        self.first[1].start()
        self.first[0].start()

    def cross(self):
        self.first[1].wait_recv()
        self.to_far[...] = (
            self.part[self.far].astype(jnp.float32) + self.from_twin[1].astype(jnp.float32)
        ).astype(jnp.bfloat16)
        self.second.start()

    def result(self):
        self.first[0].wait_recv()
        self.second.wait_recv()
        return (
            self.part[self.own].astype(jnp.float32)
            + self.from_twin[0].astype(jnp.float32)
            + self.from_far[...].astype(jnp.float32)
        )

    def finish(self):
        for copy in self.first + [self.second]:
            copy.wait_send()


def row_grads_sems():
    return [pltpu.SemaphoreType.DMA((3,)), pltpu.SemaphoreType.DMA((3,))]


def row_grads_scratch(shape):
    return [
        pltpu.VMEM((2,) + shape, jnp.bfloat16),
        pltpu.VMEM(shape, jnp.bfloat16),
        pltpu.VMEM(shape, jnp.bfloat16),
    ] + row_grads_sems()


class Deal:
    def __init__(self, ring, total, arrived, send_sems, recv_sems):
        self.ring, self.total, self.arrived = ring, total, arrived
        self.send_sems, self.recv_sems = send_sems, recv_sems

    def piece(self, ahead):
        member = ctx_peer(self.ring, ahead)
        return remote(
            self.total.at[member],
            self.arrived.at[self.ring.me],
            self.send_sems.at[ahead],
            self.recv_sems.at[ahead],
            (member, self.ring.row),
        )

    def begin(self):
        for ahead in range(1, self.ring.size):
            self.piece(ahead).start()
        self.arrived[self.ring.me] = self.total[self.ring.me]

    def collect(self, outs):
        for ahead in range(1, self.ring.size):
            self.piece(ahead).wait_recv()
        start = 0
        for out in outs:
            width = out.shape[1] // self.ring.size
            for member in range(self.ring.size):
                out[:, member * width : (member + 1) * width] = self.arrived[member, :, start : start + width].astype(
                    jnp.float32
                )
            start += width

    def finish(self):
        for ahead in range(1, self.ring.size):
            self.piece(ahead).wait_send()


def deal_scratch(shape):
    return [
        pltpu.VMEM(shape, jnp.bfloat16),
        pltpu.SemaphoreType.DMA((shape[0],)),
        pltpu.SemaphoreType.DMA((shape[0],)),
    ]


def params(collective_id):
    return pltpu.CompilerParams(
        collective_id=collective_id, has_side_effects=True, vmem_limit_bytes=62 * 1024 * 1024
    )


def front_kernel(size, n_fsdp, hidden, small, w_query, w_key, w_value, w_output, attn_in, all_small, columns_out, rows_out, *scratch):
    own, gain, gather_send, gather_recv, own_sem, small_send, small_recv = scratch[:7]
    ring = Ring(size)
    others = Others(ring, n_fsdp)
    columns = Columns(ring, n_fsdp, [w_query, w_key, w_value], columns_out, *scratch[7:11])
    rows = Rows(ring, n_fsdp, w_output, rows_out, *scratch[11:13])
    gathering = GatherRing(ring, own, attn_in, gather_send, gather_recv)
    others.greet()

    def tiny(other, device):
        return remote(small, all_small.at[others.index], small_send.at[other], small_recv.at[others.index], device)

    others.each(lambda other, device: tiny(other, device).start())
    columns.begin()
    rows.begin()
    all_small[others.index] = small[...]
    others.each(
        lambda other, device: remote(
            small, all_small.at[other], small_send.at[other], small_recv.at[other], device
        ).wait_recv()
    )
    for pair in range(others.count // 2):
        gain[:, pair * 128 : (pair + 1) * 128] = all_small[2 * pair, 0:1] + all_small[2 * pair + 1, 0:1]
    half = own.shape[0] // 2
    for way in range(2):
        place = slice(way * half, (way + 1) * half)
        values = hidden[place].astype(jnp.float32)
        scale = lax.rsqrt(jnp.mean(values * values, axis=-1, keepdims=True) + EPS)
        own[place] = (values * scale * gain[...]).astype(jnp.bfloat16)
        gathering.start(way)
    keep = pltpu.make_async_copy(own, attn_in.at[ring.me], own_sem)
    keep.start()
    gathering.step(1)
    gathering.step(2)
    columns.spread()
    gathering.step(3)
    gathering.step(4)
    rows.relay()

    @pl.loop(5, size - 1)
    def _(step):
        gathering.step(step)

    columns.relay()
    gathering.finish()
    others.each(lambda other, device: tiny(other, device).wait_send())
    columns.finish()
    rows.finish()
    keep.wait()


def front(hidden, small, w_query, w_key, w_value, w_output):
    size, n_fsdp = lax.axis_size("ctx"), lax.axis_size("fsdp")
    rows, width = hidden.shape
    depth = w_query.shape[0]
    share = (w_query.shape[1] + w_key.shape[1] + w_value.shape[1]) // size
    return pl.pallas_call(
        functools.partial(front_kernel, size, n_fsdp),
        out_shape=[
            jax.ShapeDtypeStruct((size, rows, width), jnp.bfloat16),
            jax.ShapeDtypeStruct((size * n_fsdp,) + small.shape, jnp.float32),
            jax.ShapeDtypeStruct((size, n_fsdp, depth, share), jnp.bfloat16),
            jax.ShapeDtypeStruct((n_fsdp,) + w_output.shape, jnp.bfloat16),
        ],
        in_specs=[VMEM_SPEC, VMEM_SPEC] + [ANY_SPEC] * 4,
        out_specs=[ANY_SPEC, VMEM_SPEC, ANY_SPEC, ANY_SPEC],
        scratch_shapes=[pltpu.VMEM((rows, width), jnp.bfloat16), pltpu.VMEM((1, width), jnp.float32)]
        + gather_sems(size)
        + [
            pltpu.SemaphoreType.DMA,
            pltpu.SemaphoreType.DMA((size * n_fsdp,)),
            pltpu.SemaphoreType.DMA((size * n_fsdp,)),
        ]
        + columns_sems(size, 3)
        + rows_sems(),
        compiler_params=params(2),
    )(hidden, small, w_query, w_key, w_value, w_output)


def head_norm(raw):
    return lax.rsqrt(jnp.mean(raw * raw, axis=-1, keepdims=True) + EPS)


def turn(values, cosine, sine):
    return values * cosine + pltpu.roll(values, values.shape[-1] // 2, 1) * sine


def fill_tables(blocks, cos_table, sin_table, cosine, sine, places):
    block_rows = cos_table.shape[1]
    offsets = lax.broadcasted_iota(jnp.int32, (block_rows, places.shape[1]), 0)
    for slot in range(places.shape[0] // block_rows):
        at = slice(slot * block_rows, (slot + 1) * block_rows)
        cosine[at] = cos_table[blocks[slot]]
        sine[at] = sin_table[blocks[slot]]
        places[at] = offsets + blocks[slot] * block_rows


def query_places(blocks, member, block_rows, width):
    lane = lax.broadcasted_iota(jnp.int32, (1, width), 1)
    first = blocks[2 * member] * block_rows
    second = blocks[2 * member + 1] * block_rows - block_rows
    return lane + jnp.where(lane < block_rows, first, second)


def attend_kernel(
    size,
    n_fsdp,
    q_heads,
    blocks,
    cos_table,
    sin_table,
    q_gain,
    k_gain,
    attn_in_hbm,
    w_qkv_hbm,
    cotangent,
    w_gate,
    w_up,
    w_down,
    raw,
    queries,
    keys,
    values,
    attn,
    log_totals,
    grad_out,
    columns_out,
    rows_out,
    attn_in,
    w_qkv,
    cosine,
    sine,
    places,
    values_t,
    load_sems,
    *scratch,
):
    gather_send, gather_recv, own_sem = scratch[:3]
    ring = Ring(size)
    columns = Columns(ring, n_fsdp, [w_gate, w_up], columns_out, *scratch[3:7])
    rows = Rows(ring, n_fsdp, w_down, rows_out, *scratch[7:9])
    gathering = GatherRing(ring, cotangent, grad_out, gather_send, gather_recv)
    loads = [
        pltpu.make_async_copy(attn_in_hbm, attn_in, load_sems.at[0]),
        pltpu.make_async_copy(w_qkv_hbm, w_qkv, load_sems.at[1]),
    ]
    for load in loads:
        load.start()
    greet(near_devices(ring, n_fsdp))
    columns.begin()
    rows.begin()
    keep = pltpu.make_async_copy(cotangent, grad_out.at[ring.me], own_sem)
    keep.start()
    fill_tables(blocks, cos_table, sin_table, cosine, sine, places)
    head = q_gain.shape[1]
    tokens = attn_in.shape[1]
    block_rows = cos_table.shape[1]
    for load in loads:
        load.wait()

    @pl.loop(0, size)
    def _(member):
        at = pl.ds(pl.multiple_of(member * tokens, tokens), tokens)
        product = jnp.dot(attn_in[member], w_qkv[...], preferred_element_type=jnp.float32)
        raw[at, :] = product[:, : (q_heads + 1) * head]
        for which in range(q_heads + 1):
            values_raw = product[:, which * head : (which + 1) * head]
            gain = q_gain if which < q_heads else k_gain
            turned = turn(values_raw * head_norm(values_raw) * gain[...], cosine[at, :], sine[at, :])
            if which < q_heads:
                queries[member, which] = (turned * head**-0.5).astype(jnp.bfloat16)
            else:
                keys[at, :] = turned.astype(jnp.bfloat16)
        fresh = product[:, (q_heads + 1) * head :]
        values[at, :] = fresh.astype(jnp.bfloat16)
        values_t[:, at] = fresh.T.astype(jnp.bfloat16)

    @pl.loop(0, size)
    def _(member):
        visible = places[...] <= query_places(blocks, member, block_rows, tokens)
        for which in range(q_heads):
            scores = lax.dot_general(
                keys[...], queries[member, which], (((1,), (1,)), ((), ())), preferred_element_type=jnp.float32
            )
            scores = jnp.where(visible, scores, -1e30)
            peak = jnp.max(scores, axis=0, keepdims=True)
            weights = jnp.exp(scores - peak)
            total = jnp.sum(weights, axis=0, keepdims=True)
            probs = (weights * (1.0 / total)).astype(jnp.bfloat16)
            mixed = jnp.dot(values_t[...], probs, preferred_element_type=jnp.float32)
            attn[member, :, which * head : (which + 1) * head] = mixed.T.astype(jnp.bfloat16)
            log_totals[member, which : which + 1, :] = peak + jnp.log(total)

    columns.spread()
    for way in range(2):
        gathering.start(way)
    rows.relay()

    @pl.loop(1, size - 1)
    def _(step):
        gathering.step(step)

    columns.relay()
    gathering.finish()
    columns.finish()
    rows.finish()
    keep.wait()


def attend(blocks, tables, q_gain, k_gain, attn_in, w_qkv, q_heads, cotangent, w_gate, w_up, w_down):
    size, n_fsdp = lax.axis_size("ctx"), lax.axis_size("fsdp")
    rows, width = cotangent.shape
    depth = w_gate.shape[0]
    share = (w_gate.shape[1] + w_up.shape[1]) // size
    head = q_gain.shape[0]
    everyone = size * rows
    return pl.pallas_call(
        functools.partial(attend_kernel, size, n_fsdp, q_heads),
        out_shape=[
            jax.ShapeDtypeStruct((everyone, (q_heads + 1) * head), jnp.float32),
            jax.ShapeDtypeStruct((size, q_heads, rows, head), jnp.bfloat16),
            jax.ShapeDtypeStruct((everyone, head), jnp.bfloat16),
            jax.ShapeDtypeStruct((everyone, head), jnp.bfloat16),
            jax.ShapeDtypeStruct((size, rows, q_heads * head), jnp.bfloat16),
            jax.ShapeDtypeStruct((size, q_heads, rows), jnp.float32),
            jax.ShapeDtypeStruct((size, rows, width), jnp.bfloat16),
            jax.ShapeDtypeStruct((size, n_fsdp, depth, share), jnp.bfloat16),
            jax.ShapeDtypeStruct((n_fsdp,) + w_down.shape, jnp.bfloat16),
        ],
        in_specs=[pl.BlockSpec(memory_space=pltpu.SMEM)] + [VMEM_SPEC] * 4 + [ANY_SPEC] * 6,
        out_specs=[VMEM_SPEC] * 6 + [ANY_SPEC] * 3,
        scratch_shapes=[
            pltpu.VMEM((size, rows, width), jnp.bfloat16),
            pltpu.VMEM(w_qkv.shape, jnp.bfloat16),
            pltpu.VMEM((everyone, head), jnp.float32),
            pltpu.VMEM((everyone, head), jnp.float32),
            pltpu.VMEM((everyone, head), jnp.int32),
            pltpu.VMEM((head, everyone), jnp.bfloat16),
            pltpu.SemaphoreType.DMA((2,)),
        ]
        + gather_sems(size)
        + [pltpu.SemaphoreType.DMA]
        + columns_sems(size, 2)
        + rows_sems(),
        compiler_params=params(3),
    )(
        blocks,
        *tables,
        q_gain.reshape(1, head).astype(jnp.float32),
        k_gain.reshape(1, head).astype(jnp.float32),
        attn_in,
        w_qkv,
        cotangent,
        w_gate,
        w_up,
        w_down,
    )


def norm_pull(grad_normed, normed, scale):
    return scale * (grad_normed - normed * jnp.mean(grad_normed * normed, axis=-1, keepdims=True))


def feed_forward_kernel(
    size,
    n_fsdp,
    attn,
    w_output,
    hidden,
    gain,
    w_gu_in,
    w_down_in,
    cot_in,
    out_hidden,
    grad_mid,
    grad_gain,
    grad_branch,
    gu_total,
    down_out,
    w_gu,
    w_down,
    cot,
    load_sems,
    mid,
    own,
    mlp_in,
    inner,
    grad_gu,
    gu_part,
    down_part,
    *scratch,
):
    loads = [
        pltpu.make_async_copy(source, target, load_sems.at[which])
        for which, (source, target) in enumerate(((w_gu_in, w_gu), (w_down_in, w_down), (cot_in, cot)))
    ]
    for load in loads:
        load.start()
    ring = Ring(size)
    greet(near_devices(ring, n_fsdp))
    half = own.shape[0] // 2
    ff = w_down.shape[0]
    out_sums, gather_sems_in = scratch[:5], scratch[5:7]
    layer_sums = (scratch[0],) + tuple(scratch[7:11])
    gather_sems_out, keep_sems = scratch[11:13], scratch[13]
    column_scratch = (scratch[14], None, gu_total, scratch[15], scratch[16])
    row_scratch = (scratch[17], None, scratch[18], scratch[19], scratch[20])

    first = SumRing(ring, row_terms(attn, w_output, out_sums[0]), *out_sums)
    first.run()
    gathering = GatherRing(ring, own, mlp_in, *gather_sems_in)
    for way in range(2):
        place = slice(way * half, (way + 1) * half)
        total = first.result(way) + hidden[place].astype(jnp.float32)
        mid[place] = total
        scale = lax.rsqrt(jnp.mean(total * total, axis=-1, keepdims=True) + EPS)
        own[place] = (total * scale * gain[...]).astype(jnp.bfloat16)
        gathering.start(way)
    first.finish()
    keep = pltpu.make_async_copy(own, mlp_in.at[ring.me], keep_sems.at[0])
    keep.start()
    for load in loads:
        load.wait()

    def units(lines, members):
        cot_lines = jnp.concatenate([cot[members[way], way * half : (way + 1) * half] for way in range(2)], axis=0)

        @pl.loop(0, ff // UNITS)
        def _(tile):
            at = pl.multiple_of(tile * UNITS, UNITS)
            here, there = pl.ds(at, UNITS), pl.ds(pl.multiple_of(ff + at, UNITS), UNITS)
            gate = jnp.dot(lines, w_gu[:, here], preferred_element_type=jnp.float32)
            up = jnp.dot(lines, w_gu[:, there], preferred_element_type=jnp.float32)
            pulled = lax.dot_general(
                cot_lines, w_down[here, :], (((1,), (1,)), ((), ())), preferred_element_type=jnp.float32
            )
            sigmoid = 1.0 / (1.0 + jnp.exp(-gate))
            active = gate * sigmoid
            inner_new = (active * up).astype(jnp.bfloat16)
            gate_new = (pulled * up * sigmoid * (1.0 + gate * (1.0 - sigmoid))).astype(jnp.bfloat16)
            up_new = (pulled * active).astype(jnp.bfloat16)
            for way in range(2):
                place = slice(way * half, (way + 1) * half)
                inner[members[way], place, here] = inner_new[place]
                grad_gu[members[way], place, here] = gate_new[place]
                grad_gu[members[way], place, there] = up_new[place]

    def units_of(step):
        members = [ring.member(way, step) for way in range(2)]
        units(
            jnp.concatenate([mlp_in[members[way], way * half : (way + 1) * half] for way in range(2)], axis=0), members
        )

    units(own[...], [ring.me, ring.me])

    @pl.loop(1, size - 1)
    def _(step):
        gathering.step(step)
        units_of(step)

    gathering.finish()
    keep.wait()
    units_of(size - 1)

    second = SumRing(ring, row_terms(inner, w_down, layer_sums[0]), *layer_sums)
    rows_all = size * 2 * half
    width = w_gu.shape[0]
    block = width // size

    def gu_tile(member):
        columns = pl.ds(pl.multiple_of(member * block, block), block)
        lines = mlp_in[:, :, columns].reshape(rows_all, block)

        @pl.loop(0, 2 * ff // TILE)
        def _(tile):
            there = pl.ds(pl.multiple_of(tile * TILE, TILE), TILE)
            product = lax.dot_general(
                lines,
                grad_gu[:, :, there].reshape(rows_all, TILE),
                (((0,), (0,)), ((), ())),
                preferred_element_type=jnp.float32,
            ).astype(jnp.bfloat16)
            for row in range(n_fsdp):
                gu_part[row, member, :, there] = product[row * (block // n_fsdp) : (row + 1) * (block // n_fsdp)]

    share = ff // n_fsdp

    def down_tile(tile):
        columns = pl.ds(pl.multiple_of(tile * UNITS, UNITS), UNITS)
        lines = cot[:, :, columns].reshape(rows_all, UNITS)
        product = lax.dot_general(
            inner[...].reshape(rows_all, ff), lines, (((0,), (0,)), ((), ())), preferred_element_type=jnp.float32
        ).astype(jnp.bfloat16)
        for row in range(n_fsdp):
            down_part[row, :, columns] = product[row * share : (row + 1) * share]

    second.begin()
    gu_tile(0)
    second.second()
    gu_tile(1)

    @pl.loop(2, size - 1)
    def _(step):
        second.step(step)
        gu_tile(step)

        @pl.when(step < 2 + width // UNITS // 2)
        def _():
            down_tile(2 * step - 4)
            down_tile(2 * step - 3)

    gu_tile(size - 1)
    columns = RowGrads(ring, n_fsdp, gu_part, *column_scratch)
    rows = RowGrads(ring, n_fsdp, down_part, *row_scratch)
    columns.begin()
    rows.begin()
    second.last_terms()
    for way in range(2):
        place = slice(way * half, (way + 1) * half)
        out_hidden[place] = (mid[place] + second.result(way)).astype(jnp.bfloat16)

    third = SumRing(ring, row_terms_t(grad_gu, w_gu, out_sums[0]), *out_sums)
    third.begin()
    second.finish()
    third.second()
    columns.cross()
    rows.cross()

    @pl.loop(2, size - 1)
    def _(step):
        third.step(step)

    third.last_terms()
    gathering = GatherRing(ring, own, grad_branch, *gather_sems_out)
    gain_sum = jnp.zeros_like(grad_gain)
    for way in range(2):
        place = slice(way * half, (way + 1) * half)
        pulled = third.result(way)
        values = mid[place]
        scale = lax.rsqrt(jnp.mean(values * values, axis=-1, keepdims=True) + EPS)
        normed = values * scale
        gain_sum = gain_sum + jnp.sum(pulled * normed, axis=0, keepdims=True)
        total = cot[ring.me, place].astype(jnp.float32) + norm_pull(pulled * gain[...], normed, scale)
        grad_mid[place] = total
        own[place] = total.astype(jnp.bfloat16)
        gathering.start(way)
    grad_gain[...] = gain_sum
    keep = pltpu.make_async_copy(own, grad_branch.at[ring.me], keep_sems.at[1])
    keep.start()
    third.finish()
    gathering.step(1)
    gathering.step(2)
    down_out[...] = rows.result()
    gathering.step(3)
    gu_total[...] = columns.result().astype(jnp.bfloat16)

    @pl.loop(4, size - 1)
    def _(step):
        gathering.step(step)

    gathering.finish()
    columns.finish()
    rows.finish()
    keep.wait()


UNITS = 256


def feed_forward(attn, w_output, hidden, gain, w_gu, w_down, cotangent):
    size, n_fsdp = lax.axis_size("ctx"), lax.axis_size("fsdp")
    rows, width = hidden.shape
    ff = w_down.shape[0]
    depth = width // size // n_fsdp
    sums = sum_scratch(size, rows, width)
    return pl.pallas_call(
        functools.partial(feed_forward_kernel, size, n_fsdp),
        out_shape=[
            jax.ShapeDtypeStruct((rows, width), jnp.bfloat16),
            jax.ShapeDtypeStruct((rows, width), jnp.float32),
            jax.ShapeDtypeStruct((1, width), jnp.float32),
            jax.ShapeDtypeStruct((size, rows, width), jnp.bfloat16),
            jax.ShapeDtypeStruct((size, depth, 2 * ff), jnp.bfloat16),
            jax.ShapeDtypeStruct((ff // n_fsdp, width), jnp.float32),
        ],
        in_specs=[VMEM_SPEC] * 4 + [ANY_SPEC] * 3,
        out_specs=[VMEM_SPEC, VMEM_SPEC, VMEM_SPEC, ANY_SPEC, VMEM_SPEC, VMEM_SPEC],
        scratch_shapes=[
            pltpu.VMEM(w_gu.shape, jnp.bfloat16),
            pltpu.VMEM(w_down.shape, jnp.bfloat16),
            pltpu.VMEM((size, rows, width), jnp.bfloat16),
            pltpu.SemaphoreType.DMA((3,)),
            pltpu.VMEM((rows, width), jnp.float32),
            pltpu.VMEM((rows, width), jnp.bfloat16),
            pltpu.VMEM((size, rows, width), jnp.bfloat16),
            pltpu.VMEM((size, rows, ff), jnp.bfloat16),
            pltpu.VMEM((size, rows, 2 * ff), jnp.bfloat16),
            pltpu.VMEM((n_fsdp, size, depth, 2 * ff), jnp.bfloat16),
            pltpu.VMEM((n_fsdp, ff // n_fsdp, width), jnp.bfloat16),
        ]
        + sums
        + gather_sems(size)
        + sums[1:]
        + gather_sems(size)
        + [pltpu.SemaphoreType.DMA((2,))]
        + [pltpu.VMEM((2, size, depth, 2 * ff), jnp.bfloat16)]
        + row_grads_sems()
        + [pltpu.VMEM((2, ff // n_fsdp, width), jnp.bfloat16), pltpu.VMEM((ff // n_fsdp, width), jnp.bfloat16)]
        + row_grads_sems(),
        compiler_params=params(5),
    )(
        attn.reshape(size, rows, -1),
        w_output,
        hidden,
        gain.reshape(1, width),
        w_gu,
        w_down,
        cotangent.reshape(size, rows, width),
    )


def back_kernel(
    size,
    n_fsdp,
    grads,
    weight,
    hidden,
    grad_mid,
    gain,
    post_sum,
    q_sum,
    k_sum,
    column_part,
    row_part,
    gu_total,
    grad_hidden,
    gains_out,
    query_out,
    key_out,
    value_out,
    output_out,
    gate_out,
    up_out,
    small,
    all_small,
    small_send,
    small_recv,
    *scratch,
):
    sums = scratch[:5]
    ring = Ring(size)
    others = Others(ring, n_fsdp)
    others.greet()
    half = hidden.shape[0] // 2
    total = scratch[10]
    columns = RowGrads(ring, n_fsdp, column_part, *scratch[5:10])
    dealing = Deal(ring, total, *scratch[11:14])
    rows = RowGrads(ring, n_fsdp, row_part, *scratch[14:19])
    gu_dealing = Deal(ring, gu_total, *scratch[19:22])
    columns.begin()
    rows.begin()
    gu_dealing.begin()
    summing = SumRing(ring, row_terms_t(grads, weight, sums[0]), *sums)
    summing.begin()
    summing.second()
    columns.cross()
    rows.cross()
    summing.step(2)
    summing.step(3)
    total[...] = columns.result().astype(jnp.bfloat16)
    dealing.begin()

    @pl.loop(4, size - 1)
    def _(step):
        summing.step(step)

    output_out[...] = rows.result()
    summing.last_terms()
    gain_sum = jnp.zeros_like(post_sum)
    for way in range(2):
        place = slice(way * half, (way + 1) * half)
        pulled = summing.result(way)
        values = hidden[place].astype(jnp.float32)
        scale = lax.rsqrt(jnp.mean(values * values, axis=-1, keepdims=True) + EPS)
        normed = values * scale
        gain_sum = gain_sum + jnp.sum(pulled * normed, axis=0, keepdims=True)
        grad_hidden[place] = grad_mid[place] + norm_pull(pulled * gain[...], normed, scale)
    for pair in range(others.count // 2):
        lanes = slice(pair * 128, (pair + 1) * 128)
        small[pair, 0:1] = gain_sum[:, lanes]
        small[pair, 1:2] = post_sum[:, lanes]
        small[pair, 2:3] = q_sum[...]
        small[pair, 3:4] = k_sum[...]
        small[pair, 4:8] = jnp.zeros((4, 128), jnp.float32)

    def tiny(other, device):
        return remote(
            small.at[lax.div(other, 2)],
            all_small.at[others.index],
            small_send.at[other],
            small_recv.at[others.index],
            device,
        )

    others.each(lambda other, device: tiny(other, device).start())
    all_small[others.index] = small[lax.div(others.index, 2)]
    gu_dealing.collect([gate_out, up_out])
    dealing.collect([query_out, key_out, value_out])
    others.each(
        lambda other, device: remote(
            small.at[0], all_small.at[other], small_send.at[other], small_recv.at[other], device
        ).wait_recv()
    )
    gains_out[...] = jnp.sum(all_small[...], axis=0)
    others.each(lambda other, device: tiny(other, device).wait_send())
    summing.finish()
    columns.finish()
    rows.finish()
    dealing.finish()
    gu_dealing.finish()


def back(grads, weight, hidden, grad_mid, gain, post_sum, q_sum, k_sum, column_part, row_part, gu_total, widths):
    size, n_fsdp = lax.axis_size("ctx"), lax.axis_size("fsdp")
    rows, width = hidden.shape
    share = column_part.shape[3]
    depth = column_part.shape[2]
    count = size * n_fsdp
    return pl.pallas_call(
        functools.partial(back_kernel, size, n_fsdp),
        out_shape=[
            jax.ShapeDtypeStruct((rows, width), jnp.float32),
            jax.ShapeDtypeStruct((8, 128), jnp.float32),
        ]
        + [jax.ShapeDtypeStruct((depth, full), jnp.float32) for full in widths]
        + [jax.ShapeDtypeStruct(row_part.shape[1:], jnp.float32)]
        + [jax.ShapeDtypeStruct((depth, gu_total.shape[2] // 2 * size), jnp.float32)] * 2,
        in_specs=[VMEM_SPEC] * 11,
        out_specs=[VMEM_SPEC] * 8,
        scratch_shapes=[
            pltpu.VMEM((count // 2, 8, 128), jnp.float32),
            pltpu.VMEM((count, 8, 128), jnp.float32),
            pltpu.SemaphoreType.DMA((count,)),
            pltpu.SemaphoreType.DMA((count,)),
        ]
        + sum_scratch(size, rows, width)
        + row_grads_scratch((size, depth, share))
        + [pltpu.VMEM((size, depth, share), jnp.bfloat16)]
        + deal_scratch((size, depth, share))
        + row_grads_scratch(row_part.shape[1:])
        + deal_scratch(gu_total.shape),
        compiler_params=params(6),
    )(
        grads.reshape(size, rows, -1),
        weight,
        hidden,
        grad_mid,
        gain.reshape(1, width),
        post_sum.reshape(1, width),
        q_sum.reshape(1, -1),
        k_sum.reshape(1, -1),
        column_part,
        row_part,
        gu_total,
    )


def tp_body(
    hidden_in,
    block_of,
    in_gain,
    w_query,
    w_key,
    w_value,
    w_output,
    q_gain,
    k_gain,
    post_gain,
    w_gate,
    w_up,
    w_down,
    cotangent,
):
    seq_count, tok_rows, model_width = hidden_in.shape
    n_ctx = lax.axis_size("ctx")
    n_fsdp = lax.axis_size("fsdp")
    block_rows = tok_rows // 2
    rows = seq_count * tok_rows
    seq_rows = n_ctx * rows
    head_dim = q_gain.shape[0]
    q_heads = w_query.shape[1] // head_dim // n_ctx
    kv_heads = w_key.shape[1] // head_dim // n_ctx
    group = q_heads // kv_heads
    q_scale = head_dim ** (-0.5)
    f32, bf16 = jnp.float32, jnp.bfloat16
    contract_rows = (((0,), (0,)), ((), ()))
    contract_cols = (((1,), (1,)), ((), ()))
    hidden = hidden_in.reshape(rows, model_width)
    cot_local = cotangent.reshape(rows, model_width)
    depth = w_query.shape[0]

    side = lax.rem(lax.axis_index("fsdp"), 2)
    lanes = jnp.arange(2 * depth, dtype=jnp.int32)
    pair_mask = lax.div(lanes, depth) == side
    small = jnp.zeros((8, 2 * depth), f32)
    small = small.at[0].set(jnp.where(pair_mask, jnp.tile(in_gain.astype(f32), 2), 0.0))
    small = small.at[1].set(jnp.where(pair_mask, jnp.tile(post_gain.astype(f32), 2), 0.0))
    small = small.at[2, :2].set(block_of[0].astype(f32))

    attn_in, all_small, mine_qkv, mine_output = front(hidden, small, w_query, w_key, w_value, w_output)
    attn_in = attn_in.reshape(seq_rows, model_width)
    mine_qkv = mine_qkv.reshape(model_width, -1)
    mine_output = mine_output.reshape(-1, model_width)
    paired = all_small.reshape(n_ctx * n_fsdp // 2, 2, 8, 2 * depth).sum(axis=1)
    full_in_gain, full_post = paired[:, 0].reshape(model_width), paired[:, 1].reshape(model_width)
    own_row = lax.dynamic_index_in_dim(
        all_small.reshape(n_ctx, n_fsdp, 8, 2 * depth), lax.axis_index("fsdp"), axis=1, keepdims=False
    )
    all_blocks = own_row[:, 2, :2].reshape(2 * n_ctx).astype(jnp.int32)
    offsets = jnp.arange(block_rows, dtype=jnp.int32)
    positions = (all_blocks[:, None] * block_rows + offsets[None, :]).reshape(seq_rows)
    cosine, sine = rope_tables(positions, head_dim)

    q_width, k_width = q_heads * head_dim, kv_heads * head_dim
    half_width = head_dim // 2
    inverse = (THETA ** (-(np.arange(half_width, dtype=np.float32) * np.float32(2.0) / head_dim))).astype(np.float32)
    angles = np.arange(seq_rows, dtype=np.float32)[:, None] * inverse[None, :]
    cos_half, sin_half = np.cos(angles.astype(np.float64)), np.sin(angles.astype(np.float64))
    shape = (2 * n_ctx, block_rows, head_dim)
    tables = (
        jnp.asarray(np.concatenate([cos_half, cos_half], axis=1).astype(np.float32).reshape(shape)),
        jnp.asarray(np.concatenate([-sin_half, sin_half], axis=1).astype(np.float32).reshape(shape)),
    )
    raw, queries, keys, values, attn_bf, log_totals, grad_out, mine_gu, mine_down = attend(
        all_blocks,
        tables,
        q_gain,
        k_gain,
        attn_in.reshape(n_ctx, rows, model_width),
        mine_qkv,
        q_heads,
        cot_local,
        w_gate,
        w_up,
        w_down,
    )
    mine_gu = mine_gu.reshape(model_width, -1)
    mine_down = mine_down.reshape(-1, model_width)

    attn_bf = attn_bf.reshape(seq_rows, q_width)
    q_raw = raw[:, :q_width].reshape(seq_rows, q_heads, head_dim)
    k_raw = raw[:, q_width:].reshape(seq_rows, kv_heads, head_dim)
    q_rms = lax.rsqrt(jnp.mean(q_raw * q_raw, axis=-1, keepdims=True) + EPS)
    q_unit = q_raw * q_rms
    k_rms = lax.rsqrt(jnp.mean(k_raw * k_raw, axis=-1, keepdims=True) + EPS)
    k_unit = k_raw * k_rms
    queries = queries.transpose(0, 2, 1, 3).reshape(seq_rows, kv_heads, group, head_dim)
    keys = keys.reshape(seq_rows, kv_heads, head_dim)
    values = values.reshape(seq_rows, kv_heads, head_dim)
    visible = positions[None, :] <= positions[:, None]
    scores = jnp.einsum("qhgd,khd->hgqk", queries, keys, preferred_element_type=f32)
    log_rows = log_totals.transpose(1, 0, 2).reshape(kv_heads, group, seq_rows)
    probs = jnp.where(visible, jnp.exp(scores - log_rows[..., None]), 0.0)
    attn = jnp.einsum("hgqk,khd->qhgd", probs.astype(bf16), values, preferred_element_type=f32)

    output, grad_mid, post_sum, grad_branch, gu_total, part_down = feed_forward(
        attn_bf, mine_output, hidden, full_post, mine_gu, mine_down, grad_out
    )
    grad_branch = grad_branch.reshape(seq_rows, model_width)

    def by_owner(part):
        return part.reshape(n_ctx, n_fsdp, depth, -1).transpose(1, 0, 2, 3)

    output_part = lax.dot_general(attn_bf, grad_branch, contract_rows, preferred_element_type=f32).astype(bf16)
    grad_attn = lax.dot_general(grad_branch, mine_output, contract_cols, preferred_element_type=f32).astype(bf16)
    grad_attn = grad_attn.reshape(seq_rows, kv_heads, group, head_dim)
    delta = jnp.einsum("qhgd,qhgd->hgq", grad_attn.astype(f32), attn)
    grad_probs = jnp.einsum("qhgd,khd->hgqk", grad_attn, values, preferred_element_type=f32)
    grad_scores = (probs * (grad_probs - delta[..., None])).astype(bf16)
    grad_queries = jnp.einsum("hgqk,khd->qhgd", grad_scores, keys, preferred_element_type=f32)
    grad_keys = jnp.einsum("hgqk,qhgd->khd", grad_scores, queries, preferred_element_type=f32)
    grad_values = jnp.einsum("hgqk,qhgd->khd", probs.astype(bf16), grad_attn, preferred_element_type=f32)

    grad_q_normed = rotate(grad_queries.reshape(seq_rows, q_heads, head_dim) * q_scale, cosine, -sine)
    q_sum = jnp.sum(grad_q_normed * q_unit, axis=(0, 1))
    grad_q_raw = norm_back(grad_q_normed * q_gain.astype(f32), q_unit, q_rms).astype(bf16).reshape(seq_rows, q_width)
    grad_k_normed = rotate(grad_keys, cosine, -sine)
    k_sum = jnp.sum(grad_k_normed * k_unit, axis=(0, 1))
    grad_k_raw = norm_back(grad_k_normed * k_gain.astype(f32), k_unit, k_rms).astype(bf16).reshape(seq_rows, k_width)
    grad_v = grad_values.astype(bf16).reshape(seq_rows, k_width)
    grad_qkv = jnp.concatenate([grad_q_raw, grad_k_raw, grad_v], axis=1)
    qkv_part = lax.dot_general(attn_in, grad_qkv, contract_rows, preferred_element_type=f32).astype(bf16)
    grad_input, gains, part_query, part_key, part_value, part_output, part_gate, part_up = back(
        grad_qkv,
        mine_qkv,
        hidden,
        grad_mid,
        full_in_gain,
        post_sum,
        q_sum,
        k_sum,
        by_owner(qkv_part),
        output_part.reshape(n_fsdp, -1, model_width),
        gu_total,
        [w_query.shape[1], w_key.shape[1], w_value.shape[1]],
    )
    part_in = lax.dynamic_slice_in_dim(gains[0], side * depth, depth)
    part_post = lax.dynamic_slice_in_dim(gains[1], side * depth, depth)
    return (
        output.reshape(seq_count, tok_rows, model_width),
        grad_input.reshape(seq_count, tok_rows, model_width),
        part_in,
        part_query,
        part_key,
        part_value,
        part_output,
        gains[2],
        gains[3],
        part_post,
        part_gate,
        part_up,
        part_down,
    )


def solution(mesh):
    body = tp_body if KV_HEADS % mesh.shape["ctx"] == 0 else gathered_weights_body
    return jax.shard_map(
        body,
        mesh=mesh,
        in_specs=(
            P("fsdp", "ctx", None),
            P("fsdp", "ctx"),
            P(("ctx", "fsdp")),
            P(("ctx", "fsdp"), None),
            P(("ctx", "fsdp"), None),
            P(("ctx", "fsdp"), None),
            P(("ctx", "fsdp"), None),
            P(),
            P(),
            P(("ctx", "fsdp")),
            P(("ctx", "fsdp"), None),
            P(("ctx", "fsdp"), None),
            P(("ctx", "fsdp"), None),
            P("fsdp", "ctx", None),
        ),
        out_specs=(
            P("fsdp", "ctx", None),
            P("fsdp", "ctx", None),
            P(("ctx", "fsdp")),
            P(("ctx", "fsdp"), None),
            P(("ctx", "fsdp"), None),
            P(("ctx", "fsdp"), None),
            P(("ctx", "fsdp"), None),
            P(),
            P(),
            P(("ctx", "fsdp")),
            P(("ctx", "fsdp"), None),
            P(("ctx", "fsdp"), None),
            P(("ctx", "fsdp"), None),
        ),
        check_vma=False,
    )
```

```python
import functools
import math

import jax
import jax.numpy as jnp
import numpy as np
from jax import lax
from jax.experimental import pallas as pl
from jax.experimental.pallas import tpu as pltpu
from jax.sharding import PartitionSpec as P

EPS = 1e-06
THETA = 1000000.0
KV_HEADS = 8


def rope_tables(positions, width):
    half_width = width // 2
    inverse = THETA ** (-(jnp.arange(half_width, dtype=jnp.float32) * 2.0 / width))
    angles = positions.astype(jnp.float32)[:, None] * inverse[None, :]
    return (jnp.cos(angles), jnp.sin(angles))


def rotate(values, cosine, sine):
    half_width = values.shape[-1] // 2
    first = values[..., :half_width]
    second = values[..., half_width:]
    cos_wide = cosine[:, None, :]
    sin_wide = sine[:, None, :]
    return jnp.concatenate(
        [first * cos_wide - second * sin_wide, second * cos_wide + first * sin_wide], axis=-1
    )


def norm_back(grad_normed, normed, scale):
    return scale * (grad_normed - normed * jnp.mean(grad_normed * normed, axis=-1, keepdims=True))


def gathered_weights_body(
    hidden_in,
    block_of,
    in_gain,
    w_query,
    w_key,
    w_value,
    w_output,
    q_gain,
    k_gain,
    post_gain,
    w_gate,
    w_up,
    w_down,
    cotangent,
):
    seq_count = hidden_in.shape[0]
    tok_rows = hidden_in.shape[1]
    flat_rows = seq_count * tok_rows
    model_width = hidden_in.shape[2]
    block_rows = tok_rows // 2
    block_total = 2 * lax.axis_size("ctx")
    seq_len = block_total * block_rows
    head_dim = q_gain.shape[0]
    q_heads = w_query.shape[1] // head_dim
    kv_heads = w_key.shape[1] // head_dim
    group_size = q_heads // kv_heads
    tile_blocks = math.gcd(block_total, max(1, 512 // block_rows))
    tile_rows = tile_blocks * block_rows
    q_scale = head_dim ** (-0.5)
    contract_rows = (((0,), (0,)), ((), ()))
    contract_cols = (((1,), (1,)), ((), ()))
    offsets = jnp.arange(block_rows, dtype=jnp.int32)
    positions = (block_of[:, :, None] * block_rows + offsets[None, None, :]).reshape(flat_rows)
    cosine, sine = rope_tables(positions, head_dim)
    residual = hidden_in.reshape(flat_rows, model_width).astype(jnp.float32)
    full_in_gain, full_query, full_key, full_value, full_output = (
        lax.all_gather(in_gain, ("ctx", "fsdp"), axis=0, tiled=True),
        lax.all_gather(w_query, ("ctx", "fsdp"), axis=0, tiled=True),
        lax.all_gather(w_key, ("ctx", "fsdp"), axis=0, tiled=True),
        lax.all_gather(w_value, ("ctx", "fsdp"), axis=0, tiled=True),
        lax.all_gather(w_output, ("ctx", "fsdp"), axis=0, tiled=True),
    )
    in_scale = lax.rsqrt(jnp.mean(residual * residual, axis=-1, keepdims=True) + EPS)
    in_normed = residual * in_scale
    attn_in = (in_normed * full_in_gain.astype(jnp.float32)).astype(jnp.bfloat16)
    q_raw = jnp.dot(attn_in, full_query, preferred_element_type=jnp.float32).reshape(
        flat_rows, q_heads, head_dim
    )
    k_raw = jnp.dot(attn_in, full_key, preferred_element_type=jnp.float32).reshape(
        flat_rows, kv_heads, head_dim
    )
    v_local = jnp.dot(attn_in, full_value, preferred_element_type=jnp.float32).astype(jnp.bfloat16)
    q_rms = lax.rsqrt(jnp.mean(q_raw * q_raw, axis=-1, keepdims=True) + EPS)
    q_unit = q_raw * q_rms
    queries = (rotate(q_unit * q_gain.astype(jnp.float32), cosine, sine) * q_scale).astype(
        jnp.bfloat16
    )
    k_rms = lax.rsqrt(jnp.mean(k_raw * k_raw, axis=-1, keepdims=True) + EPS)
    k_unit = k_raw * k_rms
    keys_local = rotate(k_unit * k_gain.astype(jnp.float32), cosine, sine).astype(jnp.bfloat16)
    all_keys, all_values, all_slots = (
        lax.all_gather(
            keys_local.reshape(seq_count, tok_rows, kv_heads * head_dim), "ctx", axis=1, tiled=True
        ),
        lax.all_gather(
            v_local.reshape(seq_count, tok_rows, kv_heads * head_dim), "ctx", axis=1, tiled=True
        ),
        lax.all_gather(block_of, "ctx", axis=1, tiled=True),
    )

    def tile_scores(query_tile, key_tile, query_pos, step):
        scores = jnp.einsum(
            "qhgd,khd->hgqk", query_tile, key_tile, preferred_element_type=jnp.float32
        )
        key_pos = step * tile_rows + jnp.arange(tile_rows, dtype=jnp.int32)
        visible = key_pos[None, :] <= query_pos[:, None]
        return (scores, visible)

    def sequence_tables(seq):
        key_blocks = all_keys[seq].reshape(block_total, block_rows, kv_heads, head_dim)
        value_blocks = all_values[seq].reshape(block_total, block_rows, kv_heads, head_dim)
        block_index = (
            jnp.zeros((block_total,), jnp.int32)
            .at[all_slots[seq]]
            .set(jnp.arange(block_total, dtype=jnp.int32))
        )
        return (key_blocks, value_blocks, block_index)

    def tile_index(block_index, step):
        return lax.dynamic_slice_in_dim(block_index, step * tile_blocks, tile_blocks)

    def fetch(table, block_index, step):
        return jnp.take(table, tile_index(block_index, step), axis=0).reshape(
            tile_rows, kv_heads, head_dim
        )

    log_totals = []
    attn_parts = []
    seq = 0
    key_blocks, value_blocks, block_index = sequence_tables(seq)
    for which in range(2):
        slot = 2 * seq + which
        query_tile = queries[slot * block_rows : (slot + 1) * block_rows].reshape(
            block_rows, kv_heads, group_size, head_dim
        )
        query_pos = positions[slot * block_rows : (slot + 1) * block_rows]
        tile_count = block_of[seq, which] // tile_blocks + 1

        def max_step(step, carry):
            running_max, running_sum = carry
            scores, visible = tile_scores(
                query_tile, fetch(key_blocks, block_index, step), query_pos, step
            )
            scores = jnp.where(visible, scores, -1e30)
            new_max = jnp.maximum(running_max, jnp.max(scores, axis=-1))
            running_sum = running_sum * jnp.exp(running_max - new_max) + jnp.sum(
                jnp.exp(scores - new_max[..., None]), axis=-1
            )
            return (new_max, running_sum)

        start_max = jnp.full((kv_heads, group_size, block_rows), -1e30, jnp.float32)
        start_sum = jnp.zeros((kv_heads, group_size, block_rows), jnp.float32)
        running_max, running_sum = lax.fori_loop(0, tile_count, max_step, (start_max, start_sum))
        log_total = running_max + jnp.log(running_sum)

        def value_step(step, total):
            scores, visible = tile_scores(
                query_tile, fetch(key_blocks, block_index, step), query_pos, step
            )
            probs = jnp.where(visible, jnp.exp(scores - log_total[..., None]), 0.0)
            return total + jnp.einsum(
                "hgqk,khd->qhgd",
                probs.astype(jnp.bfloat16),
                fetch(value_blocks, block_index, step),
                preferred_element_type=jnp.float32,
            )

        attn_part = lax.fori_loop(
            0,
            tile_count,
            value_step,
            jnp.zeros((block_rows, kv_heads, group_size, head_dim), jnp.float32),
        )
        log_totals.append(log_total)
        attn_parts.append(attn_part)
    attn_full = jnp.concatenate(attn_parts, axis=0)
    attn_bf = attn_full.reshape(flat_rows, q_heads * head_dim).astype(jnp.bfloat16)
    branch = jnp.dot(attn_bf, full_output, preferred_element_type=jnp.float32)
    hidden_mid = residual + branch
    full_post, full_gate, full_up, full_down = (
        lax.all_gather(post_gain, ("ctx", "fsdp"), axis=0, tiled=True),
        lax.all_gather(w_gate, ("ctx", "fsdp"), axis=0, tiled=True),
        lax.all_gather(w_up, ("ctx", "fsdp"), axis=0, tiled=True),
        lax.all_gather(w_down, ("ctx", "fsdp"), axis=0, tiled=True),
    )
    post_scale = lax.rsqrt(jnp.mean(hidden_mid * hidden_mid, axis=-1, keepdims=True) + EPS)
    post_normed = hidden_mid * post_scale
    mlp_in = (post_normed * full_post.astype(jnp.float32)).astype(jnp.bfloat16)
    gate_pre = jnp.dot(mlp_in, full_gate, preferred_element_type=jnp.float32)
    up_pre = jnp.dot(mlp_in, full_up, preferred_element_type=jnp.float32)
    sigmoid_gate = jax.nn.sigmoid(gate_pre)
    activated = gate_pre * sigmoid_gate
    inner = (activated * up_pre).astype(jnp.bfloat16)
    mlp_out = jnp.dot(inner, full_down, preferred_element_type=jnp.float32)
    output = (hidden_mid + mlp_out).astype(jnp.bfloat16)
    full_post, full_gate, full_up, full_down = (
        lax.all_gather(post_gain, ("ctx", "fsdp"), axis=0, tiled=True),
        lax.all_gather(w_gate, ("ctx", "fsdp"), axis=0, tiled=True),
        lax.all_gather(w_up, ("ctx", "fsdp"), axis=0, tiled=True),
        lax.all_gather(w_down, ("ctx", "fsdp"), axis=0, tiled=True),
    )
    grad_out = cotangent.reshape(flat_rows, model_width)
    grad_down = lax.dot_general(inner, grad_out, contract_rows, preferred_element_type=jnp.float32)
    part_down = lax.psum_scatter(grad_down, ("ctx", "fsdp"), scatter_dimension=0, tiled=True)
    grad_inner = lax.dot_general(
        grad_out, full_down, contract_cols, preferred_element_type=jnp.float32
    )
    grad_gate_pre = (
        grad_inner * up_pre * sigmoid_gate * (1.0 + gate_pre * (1.0 - sigmoid_gate))
    ).astype(jnp.bfloat16)
    grad_up_pre = (grad_inner * activated).astype(jnp.bfloat16)
    grad_gate = lax.dot_general(
        mlp_in, grad_gate_pre, contract_rows, preferred_element_type=jnp.float32
    )
    grad_up = lax.dot_general(
        mlp_in, grad_up_pre, contract_rows, preferred_element_type=jnp.float32
    )
    grad_mlp_in = lax.dot_general(
        grad_gate_pre, full_gate, contract_cols, preferred_element_type=jnp.float32
    ) + lax.dot_general(grad_up_pre, full_up, contract_cols, preferred_element_type=jnp.float32)
    grad_post_gain = jnp.sum(grad_mlp_in * post_normed, axis=0)
    grad_mid = grad_out.astype(jnp.float32) + norm_back(
        grad_mlp_in * full_post.astype(jnp.float32), post_normed, post_scale
    )
    part_post, part_gate, part_up = (
        lax.psum_scatter(grad_post_gain, ("ctx", "fsdp"), scatter_dimension=0, tiled=True),
        lax.psum_scatter(grad_gate, ("ctx", "fsdp"), scatter_dimension=0, tiled=True),
        lax.psum_scatter(grad_up, ("ctx", "fsdp"), scatter_dimension=0, tiled=True),
    )
    full_in_gain, full_query, full_key, full_value, full_output = (
        lax.all_gather(in_gain, ("ctx", "fsdp"), axis=0, tiled=True),
        lax.all_gather(w_query, ("ctx", "fsdp"), axis=0, tiled=True),
        lax.all_gather(w_key, ("ctx", "fsdp"), axis=0, tiled=True),
        lax.all_gather(w_value, ("ctx", "fsdp"), axis=0, tiled=True),
        lax.all_gather(w_output, ("ctx", "fsdp"), axis=0, tiled=True),
    )
    grad_branch = grad_mid.astype(jnp.bfloat16)
    grad_output = lax.dot_general(
        attn_bf, grad_branch, contract_rows, preferred_element_type=jnp.float32
    )
    grad_attn = lax.dot_general(
        grad_branch, full_output, contract_cols, preferred_element_type=jnp.float32
    ).astype(jnp.bfloat16)
    grad_attn = grad_attn.reshape(flat_rows, kv_heads, group_size, head_dim)
    query_grads = []
    seq = 0
    key_blocks, value_blocks, block_index = sequence_tables(seq)
    key_grads = jnp.zeros((block_total, block_rows, kv_heads, head_dim), jnp.float32)
    value_grads = jnp.zeros((block_total, block_rows, kv_heads, head_dim), jnp.float32)
    for which in range(2):
        slot = 2 * seq + which
        query_tile = queries[slot * block_rows : (slot + 1) * block_rows].reshape(
            block_rows, kv_heads, group_size, head_dim
        )
        query_pos = positions[slot * block_rows : (slot + 1) * block_rows]
        grad_tile = grad_attn[slot * block_rows : (slot + 1) * block_rows]
        tile_count = block_of[seq, which] // tile_blocks + 1
        delta = jnp.einsum("qhgd,qhgd->hgq", grad_tile.astype(jnp.float32), attn_parts[slot])
        log_total = log_totals[slot]

        def grad_step(step, carry):
            grad_query, keys_acc, values_acc = carry
            key_tile = fetch(key_blocks, block_index, step)
            scores, visible = tile_scores(query_tile, key_tile, query_pos, step)
            probs = jnp.where(visible, jnp.exp(scores - log_total[..., None]), 0.0)
            grad_probs = jnp.einsum(
                "qhgd,khd->hgqk",
                grad_tile,
                fetch(value_blocks, block_index, step),
                preferred_element_type=jnp.float32,
            )
            grad_scores = (probs * (grad_probs - delta[..., None])).astype(jnp.bfloat16)
            grad_query = grad_query + jnp.einsum(
                "hgqk,khd->qhgd", grad_scores, key_tile, preferred_element_type=jnp.float32
            )
            key_part = jnp.einsum(
                "hgqk,qhgd->khd", grad_scores, query_tile, preferred_element_type=jnp.float32
            )
            value_part = jnp.einsum(
                "hgqk,qhgd->khd",
                probs.astype(jnp.bfloat16),
                grad_tile,
                preferred_element_type=jnp.float32,
            )
            places = tile_index(block_index, step)
            keys_acc = keys_acc.at[places].add(
                key_part.reshape(tile_blocks, block_rows, kv_heads, head_dim)
            )
            values_acc = values_acc.at[places].add(
                value_part.reshape(tile_blocks, block_rows, kv_heads, head_dim)
            )
            return (grad_query, keys_acc, values_acc)

        start_query = jnp.zeros((block_rows, kv_heads, group_size, head_dim), jnp.float32)
        grad_query, key_grads, value_grads = lax.fori_loop(
            0, tile_count, grad_step, (start_query, key_grads, value_grads)
        )
        query_grads.append(grad_query)
    key_grad_list = [key_grads.reshape(seq_len, kv_heads * head_dim)]
    value_grad_list = [value_grads.reshape(seq_len, kv_heads * head_dim)]
    grad_keys, grad_values = (
        lax.psum_scatter(
            jnp.stack(key_grad_list, axis=0).astype(jnp.bfloat16),
            "ctx",
            scatter_dimension=1,
            tiled=True,
        ).astype(jnp.float32),
        lax.psum_scatter(
            jnp.stack(value_grad_list, axis=0).astype(jnp.bfloat16),
            "ctx",
            scatter_dimension=1,
            tiled=True,
        ).astype(jnp.float32),
    )
    grad_q_rot = (
        jnp.concatenate(query_grads, axis=0).reshape(flat_rows, q_heads, head_dim) * q_scale
    )
    grad_q_normed = rotate(grad_q_rot, cosine, -sine)
    grad_q_gain = jnp.sum(grad_q_normed * q_unit, axis=(0, 1))
    grad_q_raw = (
        norm_back(grad_q_normed * q_gain.astype(jnp.float32), q_unit, q_rms)
        .astype(jnp.bfloat16)
        .reshape(flat_rows, q_heads * head_dim)
    )
    grad_k_normed = rotate(grad_keys.reshape(flat_rows, kv_heads, head_dim), cosine, -sine)
    grad_k_gain = jnp.sum(grad_k_normed * k_unit, axis=(0, 1))
    grad_k_raw = (
        norm_back(grad_k_normed * k_gain.astype(jnp.float32), k_unit, k_rms)
        .astype(jnp.bfloat16)
        .reshape(flat_rows, kv_heads * head_dim)
    )
    grad_v_local = grad_values.reshape(flat_rows, kv_heads * head_dim).astype(jnp.bfloat16)
    grad_query_w = lax.dot_general(
        attn_in, grad_q_raw, contract_rows, preferred_element_type=jnp.float32
    )
    grad_key_w = lax.dot_general(
        attn_in, grad_k_raw, contract_rows, preferred_element_type=jnp.float32
    )
    grad_value_w = lax.dot_general(
        attn_in, grad_v_local, contract_rows, preferred_element_type=jnp.float32
    )
    grad_attn_in = lax.dot_general(
        grad_q_raw, full_query, contract_cols, preferred_element_type=jnp.float32
    )
    grad_attn_in = grad_attn_in + lax.dot_general(
        grad_k_raw, full_key, contract_cols, preferred_element_type=jnp.float32
    )
    grad_attn_in = grad_attn_in + lax.dot_general(
        grad_v_local, full_value, contract_cols, preferred_element_type=jnp.float32
    )
    grad_in_gain = jnp.sum(grad_attn_in * in_normed, axis=0)
    grad_input = grad_mid + norm_back(
        grad_attn_in * full_in_gain.astype(jnp.float32), in_normed, in_scale
    )
    part_in, part_query, part_key, part_value, part_output = (
        lax.psum_scatter(grad_in_gain, ("ctx", "fsdp"), scatter_dimension=0, tiled=True),
        lax.psum_scatter(grad_query_w, ("ctx", "fsdp"), scatter_dimension=0, tiled=True),
        lax.psum_scatter(grad_key_w, ("ctx", "fsdp"), scatter_dimension=0, tiled=True),
        lax.psum_scatter(grad_value_w, ("ctx", "fsdp"), scatter_dimension=0, tiled=True),
        lax.psum_scatter(grad_output, ("ctx", "fsdp"), scatter_dimension=0, tiled=True),
    )
    sum_q_gain, sum_k_gain = lax.psum((grad_q_gain, grad_k_gain), ("ctx", "fsdp"))
    return (
        output.reshape(seq_count, tok_rows, model_width),
        grad_input.reshape(seq_count, tok_rows, model_width),
        part_in,
        part_query,
        part_key,
        part_value,
        part_output,
        sum_q_gain,
        sum_k_gain,
        part_post,
        part_gate,
        part_up,
        part_down,
    )


MESH = pl.DeviceIdType.MESH
SUBS = 2


def ring_position(index, size):
    column, line = lax.rem(index, 2), lax.div(index, 2)
    return column * (line + 1) + (1 - column) * lax.rem(size - line, size)


def ring_member(position, size):
    late = lax.div(position + size // 2 - 1, size)
    beyond = lax.div(position + size - 1, size)
    return beyond * (1 - late) * (2 * position - 1) + late * 2 * (size - position)


class Ring:
    def __init__(self, size):
        self.size = size
        self.me = lax.axis_index("ctx")
        self.row = lax.axis_index("fsdp")
        self.position = ring_position(self.me, size)

    def member(self, way, steps):
        ahead = self.size - steps if way == 0 else steps
        return ring_member(lax.rem(self.position + ahead, self.size), self.size)

    def target(self, way):
        return (self.member(way, self.size - 1), self.row)

    def barrier(self):
        barrier = pltpu.get_barrier_semaphore()
        for way in range(2):
            pl.semaphore_signal(barrier, inc=1, device_id=self.target(way), device_id_type=MESH)
        pl.semaphore_wait(barrier, 2)


class GatherRing:
    def __init__(self, ring, own, out, send_sems, recv_sems):
        self.ring, self.own, self.out, self.send_sems, self.recv_sems = ring, own, out, send_sems, recv_sems
        self.half = own.shape[0] // 2
        self.sub = self.half // SUBS

    def copy(self, way, step, part, first=False):
        place = pl.ds(way * self.half + part * self.sub, self.sub)
        owner = self.ring.me if first else self.ring.member(way, step)
        source = self.own.at[place] if first else self.out.at[owner, place]
        return pltpu.make_async_remote_copy(
            src_ref=source,
            dst_ref=self.out.at[owner, place],
            send_sem=self.send_sems.at[way, step, part],
            recv_sem=self.recv_sems.at[way, step, part],
            device_id=self.ring.target(way),
            device_id_type=MESH,
        )

    def start(self, way):
        for part in range(SUBS):
            self.copy(way, 0, part, first=True).start()

    def step(self, step):
        for part in range(SUBS):
            for way in range(2):
                self.copy(way, step - 1, part).wait_recv()
                self.copy(way, step, part).start()

    def finish(self):
        last = self.ring.size - 2
        for part in range(SUBS):
            for way in range(2):
                self.copy(way, last, part).wait_recv()

        @pl.loop(0, last + 1)
        def _(step):
            for part in range(SUBS):
                for way in range(2):
                    self.copy(way, step, part).wait_send()

    def run(self):
        for way in range(2):
            self.start(way)

        @pl.loop(1, self.ring.size - 1)
        def _(step):
            self.step(step)

        self.finish()


def gather_sems(size):
    return [pltpu.SemaphoreType.DMA((2, size - 1, SUBS)), pltpu.SemaphoreType.DMA((2, size - 1, SUBS))]


class SumRing:
    def __init__(self, ring, compute, terms, outgoing, incoming, send_sems, recv_sems):
        self.ring, self.compute, self.terms = ring, compute, terms
        self.outgoing, self.incoming, self.send_sems, self.recv_sems = outgoing, incoming, send_sems, recv_sems
        self.half = terms.shape[1]
        self.sub = self.half // SUBS

    def copy(self, way, step, part):
        place = pl.ds(part * self.sub, self.sub)
        return pltpu.make_async_remote_copy(
            src_ref=self.outgoing.at[way, lax.rem(step, 2), place],
            dst_ref=self.incoming.at[way, step, place],
            send_sem=self.send_sems.at[way, step, part],
            recv_sem=self.recv_sems.at[way, step, part],
            device_id=self.ring.target(way),
            device_id_type=MESH,
        )

    def terms_of(self, step):
        self.compute([self.ring.member(way, step + 1) for way in range(2)])

    def begin(self):
        self.terms_of(0)
        for part in range(SUBS):
            place = pl.ds(part * self.sub, self.sub)
            for way in range(2):
                self.outgoing[way, 0, place] = self.terms[way, place].astype(jnp.bfloat16)
                self.copy(way, 0, part).start()

    def second(self):
        self.step(1, fresh=True)

    def step(self, step, fresh=False):
        self.terms_of(step)
        for part in range(SUBS):
            place = pl.ds(part * self.sub, self.sub)
            for way in range(2):
                self.copy(way, step - 1, part).wait_recv()
                total = self.terms[way, place] + self.incoming[way, step - 1, place].astype(jnp.float32)
                if not fresh:
                    self.copy(way, step - 2, part).wait_send()
                self.outgoing[way, lax.rem(step, 2), place] = total.astype(jnp.bfloat16)
                self.copy(way, step, part).start()

    def last_terms(self):
        self.compute([self.ring.me, self.ring.me])

    def result(self, way):
        last = self.ring.size - 2
        for part in range(SUBS):
            self.copy(way, last, part).wait_recv()
        return self.terms[way] + self.incoming[way, last].astype(jnp.float32)

    def finish(self):
        for step in (self.ring.size - 3, self.ring.size - 2):
            for part in range(SUBS):
                for way in range(2):
                    self.copy(way, step, part).wait_send()

    def run(self):
        self.begin()
        self.second()

        @pl.loop(2, self.ring.size - 1)
        def _(step):
            self.step(step)

        self.last_terms()


def sum_scratch(size, rows, width):
    half = rows // 2
    return [
        pltpu.VMEM((2, half, width), jnp.float32),
        pltpu.VMEM((2, 2, half, width), jnp.bfloat16),
        pltpu.VMEM((2, size - 1, half, width), jnp.bfloat16),
        pltpu.SemaphoreType.DMA((2, size - 1, SUBS)),
        pltpu.SemaphoreType.DMA((2, size - 1, SUBS)),
    ]


TILE = 512


def row_terms(left, weight, terms):
    half = terms.shape[1]

    def compute(members):
        lines = jnp.concatenate([left[members[way], way * half : (way + 1) * half] for way in range(2)], axis=0)

        @pl.loop(0, weight.shape[1] // TILE)
        def _(tile):
            columns = pl.ds(pl.multiple_of(tile * TILE, TILE), TILE)
            product = jnp.dot(lines, weight[:, columns], preferred_element_type=jnp.float32)
            for way in range(2):
                terms[way, :, columns] = product[way * half : (way + 1) * half]

    return compute


def row_terms_t(left, weight, terms):
    half = terms.shape[1]

    def compute(members):
        lines = jnp.concatenate([left[members[way], way * half : (way + 1) * half] for way in range(2)], axis=0)

        @pl.loop(0, weight.shape[0] // TILE)
        def _(tile):
            columns = pl.ds(pl.multiple_of(tile * TILE, TILE), TILE)
            product = lax.dot_general(
                lines, weight[columns, :], (((1,), (1,)), ((), ())), preferred_element_type=jnp.float32
            )
            for way in range(2):
                terms[way, :, columns] = product[way * half : (way + 1) * half]

    return compute


VMEM_SPEC = pl.BlockSpec(memory_space=pltpu.VMEM)
ANY_SPEC = pl.BlockSpec(memory_space=pl.ANY)


def ctx_peer(ring, ahead):
    return lax.rem(ring.me + ahead, ring.size)


def across(row, n_fsdp):
    return lax.rem(row + n_fsdp // 2, n_fsdp)


def beside(row):
    return row + 1 - 2 * lax.rem(row, 2)


def remote(source, target, send_sem, recv_sem, device):
    return pltpu.make_async_remote_copy(
        src_ref=source,
        dst_ref=target,
        send_sem=send_sem,
        recv_sem=recv_sem,
        device_id=device,
        device_id_type=MESH,
    )


def greet(devices):
    barrier = pltpu.get_barrier_semaphore()
    for device in devices:
        pl.semaphore_signal(barrier, inc=1, device_id=device, device_id_type=MESH)
    pl.semaphore_wait(barrier, len(devices))


def near_devices(ring, n_fsdp):
    return [(ctx_peer(ring, ahead), ring.row) for ahead in range(1, ring.size)] + [
        (ring.me, across(ring.row, n_fsdp)),
        (ring.me, beside(ring.row)),
    ]


class Others:
    def __init__(self, ring, n_fsdp):
        self.ring, self.n_fsdp, self.count = ring, n_fsdp, ring.size * n_fsdp
        self.index = ring.me * n_fsdp + ring.row

    def each(self, act):
        @pl.loop(0, self.count)
        def _(other):
            @pl.when(other != self.index)
            def _():
                act(other, (lax.div(other, self.n_fsdp), lax.rem(other, self.n_fsdp)))

    def greet(self):
        barrier = pltpu.get_barrier_semaphore()
        self.each(lambda other, device: pl.semaphore_signal(barrier, inc=1, device_id=device, device_id_type=MESH))
        pl.semaphore_wait(barrier, self.count - 1)


class Rows:
    def __init__(self, ring, n_fsdp, shard, out, send_sems, recv_sems):
        own, far, twin = ring.row, across(ring.row, n_fsdp), beside(ring.row)
        self.keep = pltpu.make_async_copy(shard, out.at[own], send_sems.at[3])
        self.to_far = remote(shard, out.at[own], send_sems.at[0], recv_sems.at[0], (ring.me, far))
        self.to_twin = remote(shard, out.at[own], send_sems.at[1], recv_sems.at[1], (ring.me, twin))
        self.pass_on = remote(out.at[far], out.at[far], send_sems.at[2], recv_sems.at[2], (ring.me, twin))

    def begin(self):
        self.keep.start()
        self.to_far.start()
        self.to_twin.start()

    def relay(self):
        self.to_far.wait_recv()
        self.pass_on.start()

    def finish(self):
        self.keep.wait()
        self.to_far.wait_send()
        self.to_twin.wait()
        self.pass_on.wait()


def rows_sems():
    return [pltpu.SemaphoreType.DMA((4,)), pltpu.SemaphoreType.DMA((3,))]


class Columns:
    def __init__(self, ring, n_fsdp, shards, out, send_sems, recv_sems, link_send, link_recv):
        self.ring, self.shards, self.out, self.send_sems, self.recv_sems = ring, shards, out, send_sems, recv_sems
        own, far, twin = ring.row, across(ring.row, n_fsdp), beside(ring.row)
        self.widths = [shard.shape[1] // ring.size for shard in shards]
        self.to_far = remote(out.at[:, own], out.at[:, own], link_send.at[0], link_recv.at[0], (ring.me, far))
        self.to_twin = remote(out.at[:, own], out.at[:, own], link_send.at[1], link_recv.at[1], (ring.me, twin))
        self.pass_on = remote(out.at[:, far], out.at[:, far], link_send.at[2], link_recv.at[2], (ring.me, twin))

    def piece(self, which, ahead):
        member = ctx_peer(self.ring, ahead)
        width = self.widths[which]
        start = sum(self.widths[:which])
        source = self.shards[which].at[:, pl.ds(pl.multiple_of(member * width, width), width)]
        target = self.out.at[self.ring.me, self.ring.row, :, pl.ds(start, width)]
        if ahead == 0:
            return pltpu.make_async_copy(source, target, self.send_sems.at[which, 0])
        return remote(
            source, target, self.send_sems.at[which, ahead], self.recv_sems.at[which, ahead], (member, self.ring.row)
        )

    def begin(self):
        for ahead in range(self.ring.size):
            for which in range(len(self.shards)):
                self.piece(which, ahead).start()

    def spread(self):
        for ahead in range(self.ring.size):
            for which in range(len(self.shards)):
                if ahead:
                    self.piece(which, ahead).wait_recv()
                else:
                    self.piece(which, ahead).wait()
        self.to_far.start()
        self.to_twin.start()

    def relay(self):
        self.to_far.wait_recv()
        self.pass_on.start()

    def finish(self):
        for ahead in range(1, self.ring.size):
            for which in range(len(self.shards)):
                self.piece(which, ahead).wait_send()
        self.to_far.wait_send()
        self.to_twin.wait()
        self.pass_on.wait()


def columns_sems(size, count):
    return [
        pltpu.SemaphoreType.DMA((count, size)),
        pltpu.SemaphoreType.DMA((count, size)),
        pltpu.SemaphoreType.DMA((3,)),
        pltpu.SemaphoreType.DMA((3,)),
    ]


class RowGrads:
    def __init__(self, ring, n_fsdp, part, from_twin, to_far, from_far, send_sems, recv_sems):
        own, far, twin = ring.row, across(ring.row, n_fsdp), beside(ring.row)
        self.part, self.from_twin, self.to_far, self.from_far = part, from_twin, to_far, from_far
        self.own, self.far = own, far
        twin_far = across(twin, n_fsdp)
        self.first = [
            remote(part.at[twin], from_twin.at[0], send_sems.at[0], recv_sems.at[0], (ring.me, twin)),
            remote(part.at[twin_far], from_twin.at[1], send_sems.at[1], recv_sems.at[1], (ring.me, twin)),
        ]
        if to_far is None:
            self.to_far = part.at[far]
        self.second = remote(self.to_far, from_far, send_sems.at[2], recv_sems.at[2], (ring.me, far))

    def begin(self):
        self.first[1].start()
        self.first[0].start()

    def cross(self):
        self.first[1].wait_recv()
        self.to_far[...] = (
            self.part[self.far].astype(jnp.float32) + self.from_twin[1].astype(jnp.float32)
        ).astype(jnp.bfloat16)
        self.second.start()

    def result(self):
        self.first[0].wait_recv()
        self.second.wait_recv()
        return (
            self.part[self.own].astype(jnp.float32)
            + self.from_twin[0].astype(jnp.float32)
            + self.from_far[...].astype(jnp.float32)
        )

    def finish(self):
        for copy in self.first + [self.second]:
            copy.wait_send()


def row_grads_sems():
    return [pltpu.SemaphoreType.DMA((3,)), pltpu.SemaphoreType.DMA((3,))]


def row_grads_scratch(shape):
    return [
        pltpu.VMEM((2,) + shape, jnp.bfloat16),
        pltpu.VMEM(shape, jnp.bfloat16),
        pltpu.VMEM(shape, jnp.bfloat16),
    ] + row_grads_sems()


class Deal:
    def __init__(self, ring, total, arrived, send_sems, recv_sems):
        self.ring, self.total, self.arrived = ring, total, arrived
        self.send_sems, self.recv_sems = send_sems, recv_sems

    def piece(self, ahead):
        member = ctx_peer(self.ring, ahead)
        return remote(
            self.total.at[member],
            self.arrived.at[self.ring.me],
            self.send_sems.at[ahead],
            self.recv_sems.at[ahead],
            (member, self.ring.row),
        )

    def begin(self):
        for ahead in range(1, self.ring.size):
            self.piece(ahead).start()
        self.arrived[self.ring.me] = self.total[self.ring.me]

    def collect(self, outs):
        for ahead in range(1, self.ring.size):
            self.piece(ahead).wait_recv()
        start = 0
        for out in outs:
            width = out.shape[1] // self.ring.size
            for member in range(self.ring.size):
                out[:, member * width : (member + 1) * width] = self.arrived[member, :, start : start + width].astype(
                    jnp.float32
                )
            start += width

    def finish(self):
        for ahead in range(1, self.ring.size):
            self.piece(ahead).wait_send()


def deal_scratch(shape):
    return [
        pltpu.VMEM(shape, jnp.bfloat16),
        pltpu.SemaphoreType.DMA((shape[0],)),
        pltpu.SemaphoreType.DMA((shape[0],)),
    ]


def params(collective_id):
    return pltpu.CompilerParams(
        collective_id=collective_id, has_side_effects=True, vmem_limit_bytes=62 * 1024 * 1024
    )


def front_kernel(size, n_fsdp, hidden, small, w_query, w_key, w_value, w_output, attn_in, all_small, columns_out, rows_out, *scratch):
    own, gain, gather_send, gather_recv, own_sem, small_send, small_recv = scratch[:7]
    ring = Ring(size)
    others = Others(ring, n_fsdp)
    columns = Columns(ring, n_fsdp, [w_query, w_key, w_value], columns_out, *scratch[7:11])
    rows = Rows(ring, n_fsdp, w_output, rows_out, *scratch[11:13])
    gathering = GatherRing(ring, own, attn_in, gather_send, gather_recv)
    others.greet()

    def tiny(other, device):
        return remote(small, all_small.at[others.index], small_send.at[other], small_recv.at[others.index], device)

    others.each(lambda other, device: tiny(other, device).start())
    columns.begin()
    rows.begin()
    all_small[others.index] = small[...]
    others.each(
        lambda other, device: remote(
            small, all_small.at[other], small_send.at[other], small_recv.at[other], device
        ).wait_recv()
    )
    for pair in range(others.count // 2):
        gain[:, pair * 128 : (pair + 1) * 128] = all_small[2 * pair, 0:1] + all_small[2 * pair + 1, 0:1]
    half = own.shape[0] // 2
    for way in range(2):
        place = slice(way * half, (way + 1) * half)
        values = hidden[place].astype(jnp.float32)
        scale = lax.rsqrt(jnp.mean(values * values, axis=-1, keepdims=True) + EPS)
        own[place] = (values * scale * gain[...]).astype(jnp.bfloat16)
        gathering.start(way)
    keep = pltpu.make_async_copy(own, attn_in.at[ring.me], own_sem)
    keep.start()
    gathering.step(1)
    gathering.step(2)
    columns.spread()
    gathering.step(3)
    gathering.step(4)
    rows.relay()

    @pl.loop(5, size - 1)
    def _(step):
        gathering.step(step)

    columns.relay()
    gathering.finish()
    others.each(lambda other, device: tiny(other, device).wait_send())
    columns.finish()
    rows.finish()
    keep.wait()


def front(hidden, small, w_query, w_key, w_value, w_output):
    size, n_fsdp = lax.axis_size("ctx"), lax.axis_size("fsdp")
    rows, width = hidden.shape
    depth = w_query.shape[0]
    share = (w_query.shape[1] + w_key.shape[1] + w_value.shape[1]) // size
    return pl.pallas_call(
        functools.partial(front_kernel, size, n_fsdp),
        out_shape=[
            jax.ShapeDtypeStruct((size, rows, width), jnp.bfloat16),
            jax.ShapeDtypeStruct((size * n_fsdp,) + small.shape, jnp.float32),
            jax.ShapeDtypeStruct((size, n_fsdp, depth, share), jnp.bfloat16),
            jax.ShapeDtypeStruct((n_fsdp,) + w_output.shape, jnp.bfloat16),
        ],
        in_specs=[VMEM_SPEC, VMEM_SPEC] + [ANY_SPEC] * 4,
        out_specs=[ANY_SPEC, VMEM_SPEC, ANY_SPEC, ANY_SPEC],
        scratch_shapes=[pltpu.VMEM((rows, width), jnp.bfloat16), pltpu.VMEM((1, width), jnp.float32)]
        + gather_sems(size)
        + [
            pltpu.SemaphoreType.DMA,
            pltpu.SemaphoreType.DMA((size * n_fsdp,)),
            pltpu.SemaphoreType.DMA((size * n_fsdp,)),
        ]
        + columns_sems(size, 3)
        + rows_sems(),
        compiler_params=params(2),
    )(hidden, small, w_query, w_key, w_value, w_output)


def head_norm(raw):
    return lax.rsqrt(jnp.mean(raw * raw, axis=-1, keepdims=True) + EPS)


def turn(values, cosine, sine):
    return values * cosine + pltpu.roll(values, values.shape[-1] // 2, 1) * sine


def fill_tables(blocks, cos_table, sin_table, cosine, sine, places):
    block_rows = cos_table.shape[1]
    offsets = lax.broadcasted_iota(jnp.int32, (block_rows, places.shape[1]), 0)
    for slot in range(places.shape[0] // block_rows):
        at = slice(slot * block_rows, (slot + 1) * block_rows)
        cosine[at] = cos_table[blocks[slot]]
        sine[at] = sin_table[blocks[slot]]
        places[at] = offsets + blocks[slot] * block_rows


def query_places(blocks, member, block_rows, width):
    lane = lax.broadcasted_iota(jnp.int32, (1, width), 1)
    first = blocks[2 * member] * block_rows
    second = blocks[2 * member + 1] * block_rows - block_rows
    return lane + jnp.where(lane < block_rows, first, second)


def attend_kernel(
    size,
    n_fsdp,
    q_heads,
    blocks,
    cos_table,
    sin_table,
    q_gain,
    k_gain,
    attn_in_hbm,
    w_qkv_hbm,
    cotangent,
    w_gate,
    w_up,
    w_down,
    raw,
    queries,
    keys,
    values,
    attn,
    log_totals,
    grad_out,
    columns_out,
    rows_out,
    attn_in,
    w_qkv,
    cosine,
    sine,
    places,
    values_t,
    load_sems,
    *scratch,
):
    gather_send, gather_recv, own_sem = scratch[:3]
    ring = Ring(size)
    columns = Columns(ring, n_fsdp, [w_gate, w_up], columns_out, *scratch[3:7])
    rows = Rows(ring, n_fsdp, w_down, rows_out, *scratch[7:9])
    gathering = GatherRing(ring, cotangent, grad_out, gather_send, gather_recv)
    loads = [
        pltpu.make_async_copy(attn_in_hbm, attn_in, load_sems.at[0]),
        pltpu.make_async_copy(w_qkv_hbm, w_qkv, load_sems.at[1]),
    ]
    for load in loads:
        load.start()
    greet(near_devices(ring, n_fsdp))
    columns.begin()
    rows.begin()
    keep = pltpu.make_async_copy(cotangent, grad_out.at[ring.me], own_sem)
    keep.start()
    fill_tables(blocks, cos_table, sin_table, cosine, sine, places)
    head = q_gain.shape[1]
    tokens = attn_in.shape[1]
    block_rows = cos_table.shape[1]
    for load in loads:
        load.wait()

    @pl.loop(0, size)
    def _(member):
        at = pl.ds(pl.multiple_of(member * tokens, tokens), tokens)
        product = jnp.dot(attn_in[member], w_qkv[...], preferred_element_type=jnp.float32)
        raw[at, :] = product[:, : (q_heads + 1) * head]
        for which in range(q_heads + 1):
            values_raw = product[:, which * head : (which + 1) * head]
            gain = q_gain if which < q_heads else k_gain
            turned = turn(values_raw * head_norm(values_raw) * gain[...], cosine[at, :], sine[at, :])
            if which < q_heads:
                queries[member, which] = (turned * head**-0.5).astype(jnp.bfloat16)
            else:
                keys[at, :] = turned.astype(jnp.bfloat16)
        fresh = product[:, (q_heads + 1) * head :]
        values[at, :] = fresh.astype(jnp.bfloat16)
        values_t[:, at] = fresh.T.astype(jnp.bfloat16)

    @pl.loop(0, size)
    def _(member):
        visible = places[...] <= query_places(blocks, member, block_rows, tokens)
        for which in range(q_heads):
            scores = lax.dot_general(
                keys[...], queries[member, which], (((1,), (1,)), ((), ())), preferred_element_type=jnp.float32
            )
            scores = jnp.where(visible, scores, -1e30)
            peak = jnp.max(scores, axis=0, keepdims=True)
            weights = jnp.exp(scores - peak)
            total = jnp.sum(weights, axis=0, keepdims=True)
            probs = (weights * (1.0 / total)).astype(jnp.bfloat16)
            mixed = jnp.dot(values_t[...], probs, preferred_element_type=jnp.float32)
            attn[member, :, which * head : (which + 1) * head] = mixed.T.astype(jnp.bfloat16)
            log_totals[member, which : which + 1, :] = peak + jnp.log(total)

    columns.spread()
    for way in range(2):
        gathering.start(way)
    rows.relay()

    @pl.loop(1, size - 1)
    def _(step):
        gathering.step(step)

    columns.relay()
    gathering.finish()
    columns.finish()
    rows.finish()
    keep.wait()


def attend(blocks, tables, q_gain, k_gain, attn_in, w_qkv, q_heads, cotangent, w_gate, w_up, w_down):
    size, n_fsdp = lax.axis_size("ctx"), lax.axis_size("fsdp")
    rows, width = cotangent.shape
    depth = w_gate.shape[0]
    share = (w_gate.shape[1] + w_up.shape[1]) // size
    head = q_gain.shape[0]
    everyone = size * rows
    return pl.pallas_call(
        functools.partial(attend_kernel, size, n_fsdp, q_heads),
        out_shape=[
            jax.ShapeDtypeStruct((everyone, (q_heads + 1) * head), jnp.float32),
            jax.ShapeDtypeStruct((size, q_heads, rows, head), jnp.bfloat16),
            jax.ShapeDtypeStruct((everyone, head), jnp.bfloat16),
            jax.ShapeDtypeStruct((everyone, head), jnp.bfloat16),
            jax.ShapeDtypeStruct((size, rows, q_heads * head), jnp.bfloat16),
            jax.ShapeDtypeStruct((size, q_heads, rows), jnp.float32),
            jax.ShapeDtypeStruct((size, rows, width), jnp.bfloat16),
            jax.ShapeDtypeStruct((size, n_fsdp, depth, share), jnp.bfloat16),
            jax.ShapeDtypeStruct((n_fsdp,) + w_down.shape, jnp.bfloat16),
        ],
        in_specs=[pl.BlockSpec(memory_space=pltpu.SMEM)] + [VMEM_SPEC] * 4 + [ANY_SPEC] * 6,
        out_specs=[VMEM_SPEC] * 6 + [ANY_SPEC] * 3,
        scratch_shapes=[
            pltpu.VMEM((size, rows, width), jnp.bfloat16),
            pltpu.VMEM(w_qkv.shape, jnp.bfloat16),
            pltpu.VMEM((everyone, head), jnp.float32),
            pltpu.VMEM((everyone, head), jnp.float32),
            pltpu.VMEM((everyone, head), jnp.int32),
            pltpu.VMEM((head, everyone), jnp.bfloat16),
            pltpu.SemaphoreType.DMA((2,)),
        ]
        + gather_sems(size)
        + [pltpu.SemaphoreType.DMA]
        + columns_sems(size, 2)
        + rows_sems(),
        compiler_params=params(3),
    )(
        blocks,
        *tables,
        q_gain.reshape(1, head).astype(jnp.float32),
        k_gain.reshape(1, head).astype(jnp.float32),
        attn_in,
        w_qkv,
        cotangent,
        w_gate,
        w_up,
        w_down,
    )


def norm_pull(grad_normed, normed, scale):
    return scale * (grad_normed - normed * jnp.mean(grad_normed * normed, axis=-1, keepdims=True))


def feed_forward_kernel(
    size,
    n_fsdp,
    attn,
    w_output,
    hidden,
    gain,
    w_gu_in,
    w_down_in,
    cot_in,
    out_hidden,
    grad_mid,
    grad_gain,
    grad_branch,
    gu_total,
    down_out,
    w_gu,
    w_down,
    cot,
    load_sems,
    mid,
    own,
    mlp_in,
    inner,
    grad_gu,
    gu_part,
    down_part,
    *scratch,
):
    loads = [
        pltpu.make_async_copy(source, target, load_sems.at[which])
        for which, (source, target) in enumerate(((w_gu_in, w_gu), (w_down_in, w_down), (cot_in, cot)))
    ]
    for load in loads:
        load.start()
    ring = Ring(size)
    greet(near_devices(ring, n_fsdp))
    half = own.shape[0] // 2
    ff = w_down.shape[0]
    out_sums, gather_sems_in = scratch[:5], scratch[5:7]
    layer_sums = (scratch[0],) + tuple(scratch[7:11])
    gather_sems_out, keep_sems = scratch[11:13], scratch[13]
    column_scratch = (scratch[14], None, gu_total, scratch[15], scratch[16])
    row_scratch = (scratch[17], None, scratch[18], scratch[19], scratch[20])

    first = SumRing(ring, row_terms(attn, w_output, out_sums[0]), *out_sums)
    first.run()
    gathering = GatherRing(ring, own, mlp_in, *gather_sems_in)
    for way in range(2):
        place = slice(way * half, (way + 1) * half)
        total = first.result(way) + hidden[place].astype(jnp.float32)
        mid[place] = total
        scale = lax.rsqrt(jnp.mean(total * total, axis=-1, keepdims=True) + EPS)
        own[place] = (total * scale * gain[...]).astype(jnp.bfloat16)
        gathering.start(way)
    first.finish()
    keep = pltpu.make_async_copy(own, mlp_in.at[ring.me], keep_sems.at[0])
    keep.start()
    for load in loads:
        load.wait()

    def units(lines, members):
        cot_lines = jnp.concatenate([cot[members[way], way * half : (way + 1) * half] for way in range(2)], axis=0)

        @pl.loop(0, ff // UNITS)
        def _(tile):
            at = pl.multiple_of(tile * UNITS, UNITS)
            here, there = pl.ds(at, UNITS), pl.ds(pl.multiple_of(ff + at, UNITS), UNITS)
            gate = jnp.dot(lines, w_gu[:, here], preferred_element_type=jnp.float32)
            up = jnp.dot(lines, w_gu[:, there], preferred_element_type=jnp.float32)
            pulled = lax.dot_general(
                cot_lines, w_down[here, :], (((1,), (1,)), ((), ())), preferred_element_type=jnp.float32
            )
            sigmoid = 1.0 / (1.0 + jnp.exp(-gate))
            active = gate * sigmoid
            inner_new = (active * up).astype(jnp.bfloat16)
            gate_new = (pulled * up * sigmoid * (1.0 + gate * (1.0 - sigmoid))).astype(jnp.bfloat16)
            up_new = (pulled * active).astype(jnp.bfloat16)
            for way in range(2):
                place = slice(way * half, (way + 1) * half)
                inner[members[way], place, here] = inner_new[place]
                grad_gu[members[way], place, here] = gate_new[place]
                grad_gu[members[way], place, there] = up_new[place]

    def units_of(step):
        members = [ring.member(way, step) for way in range(2)]
        units(
            jnp.concatenate([mlp_in[members[way], way * half : (way + 1) * half] for way in range(2)], axis=0), members
        )

    units(own[...], [ring.me, ring.me])

    @pl.loop(1, size - 1)
    def _(step):
        gathering.step(step)
        units_of(step)

    gathering.finish()
    keep.wait()
    units_of(size - 1)

    second = SumRing(ring, row_terms(inner, w_down, layer_sums[0]), *layer_sums)
    rows_all = size * 2 * half
    width = w_gu.shape[0]
    block = width // size

    def gu_tile(member):
        columns = pl.ds(pl.multiple_of(member * block, block), block)
        lines = mlp_in[:, :, columns].reshape(rows_all, block)

        @pl.loop(0, 2 * ff // TILE)
        def _(tile):
            there = pl.ds(pl.multiple_of(tile * TILE, TILE), TILE)
            product = lax.dot_general(
                lines,
                grad_gu[:, :, there].reshape(rows_all, TILE),
                (((0,), (0,)), ((), ())),
                preferred_element_type=jnp.float32,
            ).astype(jnp.bfloat16)
            for row in range(n_fsdp):
                gu_part[row, member, :, there] = product[row * (block // n_fsdp) : (row + 1) * (block // n_fsdp)]

    share = ff // n_fsdp

    def down_tile(tile):
        columns = pl.ds(pl.multiple_of(tile * UNITS, UNITS), UNITS)
        lines = cot[:, :, columns].reshape(rows_all, UNITS)
        product = lax.dot_general(
            inner[...].reshape(rows_all, ff), lines, (((0,), (0,)), ((), ())), preferred_element_type=jnp.float32
        ).astype(jnp.bfloat16)
        for row in range(n_fsdp):
            down_part[row, :, columns] = product[row * share : (row + 1) * share]

    second.begin()
    gu_tile(0)
    second.second()
    gu_tile(1)

    @pl.loop(2, size - 1)
    def _(step):
        second.step(step)
        gu_tile(step)

        @pl.when(step < 2 + width // UNITS // 2)
        def _():
            down_tile(2 * step - 4)
            down_tile(2 * step - 3)

    gu_tile(size - 1)
    columns = RowGrads(ring, n_fsdp, gu_part, *column_scratch)
    rows = RowGrads(ring, n_fsdp, down_part, *row_scratch)
    columns.begin()
    rows.begin()
    second.last_terms()
    for way in range(2):
        place = slice(way * half, (way + 1) * half)
        out_hidden[place] = (mid[place] + second.result(way)).astype(jnp.bfloat16)

    third = SumRing(ring, row_terms_t(grad_gu, w_gu, out_sums[0]), *out_sums)
    third.begin()
    second.finish()
    third.second()
    columns.cross()
    rows.cross()

    @pl.loop(2, size - 1)
    def _(step):
        third.step(step)

    third.last_terms()
    gathering = GatherRing(ring, own, grad_branch, *gather_sems_out)
    gain_sum = jnp.zeros_like(grad_gain)
    for way in range(2):
        place = slice(way * half, (way + 1) * half)
        pulled = third.result(way)
        values = mid[place]
        scale = lax.rsqrt(jnp.mean(values * values, axis=-1, keepdims=True) + EPS)
        normed = values * scale
        gain_sum = gain_sum + jnp.sum(pulled * normed, axis=0, keepdims=True)
        total = cot[ring.me, place].astype(jnp.float32) + norm_pull(pulled * gain[...], normed, scale)
        grad_mid[place] = total
        own[place] = total.astype(jnp.bfloat16)
        gathering.start(way)
    grad_gain[...] = gain_sum
    keep = pltpu.make_async_copy(own, grad_branch.at[ring.me], keep_sems.at[1])
    keep.start()
    third.finish()
    gathering.step(1)
    gathering.step(2)
    down_out[...] = rows.result()
    gathering.step(3)
    gu_total[...] = columns.result().astype(jnp.bfloat16)

    @pl.loop(4, size - 1)
    def _(step):
        gathering.step(step)

    gathering.finish()
    columns.finish()
    rows.finish()
    keep.wait()


UNITS = 256


def feed_forward(attn, w_output, hidden, gain, w_gu, w_down, cotangent):
    size, n_fsdp = lax.axis_size("ctx"), lax.axis_size("fsdp")
    rows, width = hidden.shape
    ff = w_down.shape[0]
    depth = width // size // n_fsdp
    sums = sum_scratch(size, rows, width)
    return pl.pallas_call(
        functools.partial(feed_forward_kernel, size, n_fsdp),
        out_shape=[
            jax.ShapeDtypeStruct((rows, width), jnp.bfloat16),
            jax.ShapeDtypeStruct((rows, width), jnp.float32),
            jax.ShapeDtypeStruct((1, width), jnp.float32),
            jax.ShapeDtypeStruct((size, rows, width), jnp.bfloat16),
            jax.ShapeDtypeStruct((size, depth, 2 * ff), jnp.bfloat16),
            jax.ShapeDtypeStruct((ff // n_fsdp, width), jnp.float32),
        ],
        in_specs=[VMEM_SPEC] * 4 + [ANY_SPEC] * 3,
        out_specs=[VMEM_SPEC, VMEM_SPEC, VMEM_SPEC, ANY_SPEC, VMEM_SPEC, VMEM_SPEC],
        scratch_shapes=[
            pltpu.VMEM(w_gu.shape, jnp.bfloat16),
            pltpu.VMEM(w_down.shape, jnp.bfloat16),
            pltpu.VMEM((size, rows, width), jnp.bfloat16),
            pltpu.SemaphoreType.DMA((3,)),
            pltpu.VMEM((rows, width), jnp.float32),
            pltpu.VMEM((rows, width), jnp.bfloat16),
            pltpu.VMEM((size, rows, width), jnp.bfloat16),
            pltpu.VMEM((size, rows, ff), jnp.bfloat16),
            pltpu.VMEM((size, rows, 2 * ff), jnp.bfloat16),
            pltpu.VMEM((n_fsdp, size, depth, 2 * ff), jnp.bfloat16),
            pltpu.VMEM((n_fsdp, ff // n_fsdp, width), jnp.bfloat16),
        ]
        + sums
        + gather_sems(size)
        + sums[1:]
        + gather_sems(size)
        + [pltpu.SemaphoreType.DMA((2,))]
        + [pltpu.VMEM((2, size, depth, 2 * ff), jnp.bfloat16)]
        + row_grads_sems()
        + [pltpu.VMEM((2, ff // n_fsdp, width), jnp.bfloat16), pltpu.VMEM((ff // n_fsdp, width), jnp.bfloat16)]
        + row_grads_sems(),
        compiler_params=params(5),
    )(
        attn.reshape(size, rows, -1),
        w_output,
        hidden,
        gain.reshape(1, width),
        w_gu,
        w_down,
        cotangent.reshape(size, rows, width),
    )


def back_kernel(
    size,
    n_fsdp,
    blocks,
    cos_table,
    sin_table,
    q_gain,
    k_gain,
    raw,
    queries,
    keys,
    values,
    attn,
    log_totals,
    hidden,
    grad_mid,
    gain,
    post_sum,
    gu_total,
    grad_branch_hbm,
    w_output_hbm,
    attn_in_hbm,
    w_qkv_hbm,
    grad_hidden,
    gains_out,
    query_out,
    key_out,
    value_out,
    output_out,
    gate_out,
    up_out,
    grad_branch,
    w_output,
    attn_in,
    w_qkv,
    load_sems,
    cosine,
    sine,
    places,
    keys_t,
    grad_keys,
    grad_values,
    head_sums,
    grads,
    qkv_part,
    output_part,
    small,
    all_small,
    small_send,
    small_recv,
    *scratch,
):
    loads = [
        pltpu.make_async_copy(source, target, load_sems.at[which])
        for which, (source, target) in enumerate(
            (
                (grad_branch_hbm, grad_branch),
                (w_output_hbm, w_output),
                (attn_in_hbm, attn_in),
                (w_qkv_hbm, w_qkv),
            )
        )
    ]
    for load in loads:
        load.start()
    sums = scratch[:5]
    ring = Ring(size)
    others = Others(ring, n_fsdp)
    others.greet()
    half = hidden.shape[0] // 2
    total = scratch[8]
    columns = RowGrads(ring, n_fsdp, qkv_part, scratch[5], None, *scratch[6:8], scratch[9])
    dealing = Deal(ring, total, *scratch[10:13])
    rows = RowGrads(ring, n_fsdp, output_part, scratch[13], None, *scratch[14:17])
    gu_dealing = Deal(ring, gu_total, *scratch[17:20])
    gu_dealing.begin()
    fill_tables(blocks, cos_table, sin_table, cosine, sine, places)
    head = q_gain.shape[1]
    q_heads = queries.shape[1]
    tokens = attn_in.shape[1]
    block_rows = cos_table.shape[1]
    everyone = size * tokens
    width = attn_in.shape[2]
    q_width = q_heads * head
    keys_t[...] = keys[...].astype(jnp.float32).T.astype(jnp.bfloat16)
    grad_keys[...] = jnp.zeros_like(grad_keys)
    grad_values[...] = jnp.zeros_like(grad_values)
    head_sums[...] = jnp.zeros_like(head_sums)
    for load in loads:
        load.wait()

    def through_head(pulled, at, which, gain_here):
        turned = turn(pulled, cosine[at, :], -sine[at, :])
        values_raw = raw[at, which * head : (which + 1) * head]
        scale = head_norm(values_raw)
        unit = values_raw * scale
        kind = 0 if which < q_heads else 1
        head_sums[kind : kind + 1] = head_sums[kind : kind + 1] + jnp.sum(turned * unit, axis=0, keepdims=True)
        return norm_pull(turned * gain_here[...], unit, scale).astype(jnp.bfloat16)

    def output_tile(tile):
        there = pl.ds(pl.multiple_of(tile * TILE, TILE), TILE)
        product = lax.dot_general(
            attn[...].reshape(everyone, q_width),
            grad_branch[:, :, there].reshape(everyone, TILE),
            (((0,), (0,)), ((), ())),
            preferred_element_type=jnp.float32,
        ).astype(jnp.bfloat16)
        share = q_width // n_fsdp
        for row in range(n_fsdp):
            output_part[row, :, there] = product[row * share : (row + 1) * share]

    @pl.loop(0, width // TILE)
    def _(tile):
        output_tile(tile)

    rows.begin()

    @pl.loop(0, size)
    def _(member):
        at = pl.ds(pl.multiple_of(member * tokens, tokens), tokens)
        grad_attn = lax.dot_general(
            grad_branch[member], w_output[...], (((1,), (1,)), ((), ())), preferred_element_type=jnp.float32
        ).astype(jnp.bfloat16)
        visible = places[...] <= query_places(blocks, member, block_rows, tokens)
        for which in range(q_heads):
            lanes = slice(which * head, (which + 1) * head)
            pulled = grad_attn[:, lanes]
            query = queries[member, which]
            scores = lax.dot_general(keys[...], query, (((1,), (1,)), ((), ())), preferred_element_type=jnp.float32)
            probs = jnp.where(visible, jnp.exp(scores - log_totals[member, which : which + 1, :]), 0.0)
            grad_probs = lax.dot_general(
                values[...], pulled, (((1,), (1,)), ((), ())), preferred_element_type=jnp.float32
            )
            delta = jnp.sum(probs * grad_probs, axis=0, keepdims=True)
            grad_scores = (probs * (grad_probs - delta)).astype(jnp.bfloat16)
            grad_keys[...] = grad_keys[...] + jnp.dot(grad_scores, query, preferred_element_type=jnp.float32)
            grad_values[...] = grad_values[...] + jnp.dot(
                probs.astype(jnp.bfloat16), pulled, preferred_element_type=jnp.float32
            )
            grad_query = jnp.dot(keys_t[...], grad_scores, preferred_element_type=jnp.float32).T
            grads[member, :, lanes] = through_head(grad_query * head**-0.5, at, which, q_gain)

    rows.cross()

    @pl.loop(0, size)
    def _(member):
        at = pl.ds(pl.multiple_of(member * tokens, tokens), tokens)
        grads[member, :, q_width : q_width + head] = through_head(grad_keys[at, :], at, q_heads, k_gain)
        grads[member, :, q_width + head :] = grad_values[at, :].astype(jnp.bfloat16)

    block = width // size

    def qkv_tile(member):
        lines = attn_in[:, :, pl.ds(pl.multiple_of(member * block, block), block)].reshape(everyone, block)
        product = lax.dot_general(
            lines,
            grads[...].reshape(everyone, grads.shape[2]),
            (((0,), (0,)), ((), ())),
            preferred_element_type=jnp.float32,
        ).astype(jnp.bfloat16)
        for row in range(n_fsdp):
            qkv_part[row, member] = product[row * (block // n_fsdp) : (row + 1) * (block // n_fsdp)]

    summing = SumRing(ring, row_terms_t(grads, w_qkv, sums[0]), *sums)
    summing.begin()

    @pl.loop(0, size // 2)
    def _(member):
        qkv_tile(member)

    summing.second()

    @pl.loop(size // 2, size)
    def _(member):
        qkv_tile(member)

    columns.begin()
    summing.step(2)
    columns.cross()
    summing.step(3)
    summing.step(4)
    total[...] = columns.result().astype(jnp.bfloat16)
    dealing.begin()
    gu_dealing.collect([gate_out, up_out])

    @pl.loop(5, size - 1)
    def _(step):
        summing.step(step)

    output_out[...] = rows.result()
    summing.last_terms()
    gain_sum = jnp.zeros_like(post_sum)
    for way in range(2):
        place = slice(way * half, (way + 1) * half)
        pulled = summing.result(way)
        values_in = hidden[place].astype(jnp.float32)
        scale = lax.rsqrt(jnp.mean(values_in * values_in, axis=-1, keepdims=True) + EPS)
        normed = values_in * scale
        gain_sum = gain_sum + jnp.sum(pulled * normed, axis=0, keepdims=True)
        grad_hidden[place] = grad_mid[place] + norm_pull(pulled * gain[...], normed, scale)
    for pair in range(others.count // 2):
        lanes = slice(pair * 128, (pair + 1) * 128)
        small[pair, 0:1] = gain_sum[:, lanes]
        small[pair, 1:2] = post_sum[:, lanes]
        small[pair, 2:4] = head_sums[0:2]
        small[pair, 4:8] = jnp.zeros((4, 128), jnp.float32)

    def tiny(other, device):
        return remote(
            small.at[lax.div(other, 2)],
            all_small.at[others.index],
            small_send.at[other],
            small_recv.at[others.index],
            device,
        )

    others.each(lambda other, device: tiny(other, device).start())
    all_small[others.index] = small[lax.div(others.index, 2)]
    dealing.collect([query_out, key_out, value_out])
    others.each(
        lambda other, device: remote(
            small.at[0], all_small.at[other], small_send.at[other], small_recv.at[other], device
        ).wait_recv()
    )
    gains_out[...] = jnp.sum(all_small[...], axis=0)
    others.each(lambda other, device: tiny(other, device).wait_send())
    summing.finish()
    columns.finish()
    rows.finish()
    dealing.finish()
    gu_dealing.finish()


def back(
    blocks,
    tables,
    q_gain,
    k_gain,
    raw,
    queries,
    keys,
    values,
    attn,
    log_totals,
    hidden,
    grad_mid,
    gain,
    post_sum,
    gu_total,
    grad_branch,
    w_output,
    attn_in,
    w_qkv,
    widths,
):
    size, n_fsdp = lax.axis_size("ctx"), lax.axis_size("fsdp")
    rows, width = hidden.shape
    head = q_gain.shape[0]
    everyone = size * rows
    share = w_qkv.shape[1]
    depth = width // size // n_fsdp
    count = size * n_fsdp
    q_width = attn.shape[2]
    f32, bf16 = jnp.float32, jnp.bfloat16
    return pl.pallas_call(
        functools.partial(back_kernel, size, n_fsdp),
        out_shape=[
            jax.ShapeDtypeStruct((rows, width), f32),
            jax.ShapeDtypeStruct((8, 128), f32),
        ]
        + [jax.ShapeDtypeStruct((depth, full), f32) for full in widths]
        + [jax.ShapeDtypeStruct((q_width // n_fsdp, width), f32)]
        + [jax.ShapeDtypeStruct((depth, gu_total.shape[2] // 2 * size), f32)] * 2,
        in_specs=[pl.BlockSpec(memory_space=pltpu.SMEM)] + [VMEM_SPEC] * 15 + [ANY_SPEC] * 4,
        out_specs=[VMEM_SPEC] * 8,
        scratch_shapes=[
            pltpu.VMEM((size, rows, width), bf16),
            pltpu.VMEM(w_output.shape, bf16),
            pltpu.VMEM((size, rows, width), bf16),
            pltpu.VMEM(w_qkv.shape, bf16),
            pltpu.SemaphoreType.DMA((4,)),
            pltpu.VMEM((everyone, head), f32),
            pltpu.VMEM((everyone, head), f32),
            pltpu.VMEM((everyone, head), jnp.int32),
            pltpu.VMEM((head, everyone), bf16),
            pltpu.VMEM((everyone, head), f32),
            pltpu.VMEM((everyone, head), f32),
            pltpu.VMEM((8, head), f32),
            pltpu.VMEM((size, rows, share), bf16),
            pltpu.VMEM((n_fsdp, size, depth, share), bf16),
            pltpu.VMEM((n_fsdp, q_width // n_fsdp, width), bf16),
            pltpu.VMEM((count // 2, 8, 128), f32),
            pltpu.VMEM((count, 8, 128), f32),
            pltpu.SemaphoreType.DMA((count,)),
            pltpu.SemaphoreType.DMA((count,)),
        ]
        + sum_scratch(size, rows, width)
        + [
            pltpu.VMEM((2, size, depth, share), bf16),
            pltpu.VMEM((size, depth, share), bf16),
            pltpu.SemaphoreType.DMA((3,)),
            pltpu.VMEM((size, depth, share), bf16),
            pltpu.SemaphoreType.DMA((3,)),
        ]
        + deal_scratch((size, depth, share))
        + [
            pltpu.VMEM((2, q_width // n_fsdp, width), bf16),
            pltpu.VMEM((q_width // n_fsdp, width), bf16),
        ]
        + row_grads_sems()
        + deal_scratch(gu_total.shape),
        compiler_params=params(6),
    )(
        blocks,
        *tables,
        q_gain.reshape(1, head).astype(f32),
        k_gain.reshape(1, head).astype(f32),
        raw,
        queries,
        keys,
        values,
        attn,
        log_totals,
        hidden,
        grad_mid,
        gain.reshape(1, width),
        post_sum,
        gu_total,
        grad_branch,
        w_output,
        attn_in,
        w_qkv,
    )


def tp_body(
    hidden_in,
    block_of,
    in_gain,
    w_query,
    w_key,
    w_value,
    w_output,
    q_gain,
    k_gain,
    post_gain,
    w_gate,
    w_up,
    w_down,
    cotangent,
):
    seq_count, tok_rows, model_width = hidden_in.shape
    n_ctx = lax.axis_size("ctx")
    n_fsdp = lax.axis_size("fsdp")
    block_rows = tok_rows // 2
    rows = seq_count * tok_rows
    seq_rows = n_ctx * rows
    head_dim = q_gain.shape[0]
    q_heads = w_query.shape[1] // head_dim // n_ctx
    f32 = jnp.float32
    hidden = hidden_in.reshape(rows, model_width)
    cot_local = cotangent.reshape(rows, model_width)
    depth = w_query.shape[0]

    side = lax.rem(lax.axis_index("fsdp"), 2)
    lanes = jnp.arange(2 * depth, dtype=jnp.int32)
    pair_mask = lax.div(lanes, depth) == side
    small = jnp.zeros((8, 2 * depth), f32)
    small = small.at[0].set(jnp.where(pair_mask, jnp.tile(in_gain.astype(f32), 2), 0.0))
    small = small.at[1].set(jnp.where(pair_mask, jnp.tile(post_gain.astype(f32), 2), 0.0))
    small = small.at[2, :2].set(block_of[0].astype(f32))

    attn_in, all_small, mine_qkv, mine_output = front(hidden, small, w_query, w_key, w_value, w_output)
    mine_qkv = mine_qkv.reshape(model_width, -1)
    mine_output = mine_output.reshape(-1, model_width)
    paired = all_small.reshape(n_ctx * n_fsdp // 2, 2, 8, 2 * depth).sum(axis=1)
    full_in_gain, full_post = paired[:, 0].reshape(model_width), paired[:, 1].reshape(model_width)
    own_row = lax.dynamic_index_in_dim(
        all_small.reshape(n_ctx, n_fsdp, 8, 2 * depth), lax.axis_index("fsdp"), axis=1, keepdims=False
    )
    all_blocks = own_row[:, 2, :2].reshape(2 * n_ctx).astype(jnp.int32)

    half_width = head_dim // 2
    inverse = (THETA ** (-(np.arange(half_width, dtype=np.float32) * np.float32(2.0) / head_dim))).astype(np.float32)
    angles = np.arange(seq_rows, dtype=np.float32)[:, None] * inverse[None, :]
    cos_half, sin_half = np.cos(angles.astype(np.float64)), np.sin(angles.astype(np.float64))
    shape = (2 * n_ctx, block_rows, head_dim)
    tables = (
        jnp.asarray(np.concatenate([cos_half, cos_half], axis=1).astype(np.float32).reshape(shape)),
        jnp.asarray(np.concatenate([-sin_half, sin_half], axis=1).astype(np.float32).reshape(shape)),
    )
    raw, queries, keys, values, attn_bf, log_totals, grad_out, mine_gu, mine_down = attend(
        all_blocks,
        tables,
        q_gain,
        k_gain,
        attn_in,
        mine_qkv,
        q_heads,
        cot_local,
        w_gate,
        w_up,
        w_down,
    )
    mine_gu = mine_gu.reshape(model_width, -1)
    mine_down = mine_down.reshape(-1, model_width)

    output, grad_mid, post_sum, grad_branch, gu_total, part_down = feed_forward(
        attn_bf, mine_output, hidden, full_post, mine_gu, mine_down, grad_out
    )
    grad_input, gains, part_query, part_key, part_value, part_output, part_gate, part_up = back(
        all_blocks,
        tables,
        q_gain,
        k_gain,
        raw,
        queries,
        keys,
        values,
        attn_bf,
        log_totals,
        hidden,
        grad_mid,
        full_in_gain,
        post_sum,
        gu_total,
        grad_branch,
        mine_output,
        attn_in,
        mine_qkv,
        [w_query.shape[1], w_key.shape[1], w_value.shape[1]],
    )
    part_in = lax.dynamic_slice_in_dim(gains[0], side * depth, depth)
    part_post = lax.dynamic_slice_in_dim(gains[1], side * depth, depth)
    return (
        output.reshape(seq_count, tok_rows, model_width),
        grad_input.reshape(seq_count, tok_rows, model_width),
        part_in,
        part_query,
        part_key,
        part_value,
        part_output,
        gains[2],
        gains[3],
        part_post,
        part_gate,
        part_up,
        part_down,
    )


def solution(mesh):
    body = tp_body if KV_HEADS % mesh.shape["ctx"] == 0 else gathered_weights_body
    return jax.shard_map(
        body,
        mesh=mesh,
        in_specs=(
            P("fsdp", "ctx", None),
            P("fsdp", "ctx"),
            P(("ctx", "fsdp")),
            P(("ctx", "fsdp"), None),
            P(("ctx", "fsdp"), None),
            P(("ctx", "fsdp"), None),
            P(("ctx", "fsdp"), None),
            P(),
            P(),
            P(("ctx", "fsdp")),
            P(("ctx", "fsdp"), None),
            P(("ctx", "fsdp"), None),
            P(("ctx", "fsdp"), None),
            P("fsdp", "ctx", None),
        ),
        out_specs=(
            P("fsdp", "ctx", None),
            P("fsdp", "ctx", None),
            P(("ctx", "fsdp")),
            P(("ctx", "fsdp"), None),
            P(("ctx", "fsdp"), None),
            P(("ctx", "fsdp"), None),
            P(("ctx", "fsdp"), None),
            P(),
            P(),
            P(("ctx", "fsdp")),
            P(("ctx", "fsdp"), None),
            P(("ctx", "fsdp"), None),
            P(("ctx", "fsdp"), None),
        ),
        check_vma=False,
    )
```

```python
import functools
import math

import jax
import jax.numpy as jnp
import numpy as np
from jax import lax
from jax.experimental import pallas as pl
from jax.experimental.pallas import tpu as pltpu
from jax.sharding import PartitionSpec as P

EPS = 1e-06
THETA = 1000000.0
KV_HEADS = 8


def rope_tables(positions, width):
    half_width = width // 2
    inverse = THETA ** (-(jnp.arange(half_width, dtype=jnp.float32) * 2.0 / width))
    angles = positions.astype(jnp.float32)[:, None] * inverse[None, :]
    return (jnp.cos(angles), jnp.sin(angles))


def rotate(values, cosine, sine):
    half_width = values.shape[-1] // 2
    first = values[..., :half_width]
    second = values[..., half_width:]
    cos_wide = cosine[:, None, :]
    sin_wide = sine[:, None, :]
    return jnp.concatenate(
        [first * cos_wide - second * sin_wide, second * cos_wide + first * sin_wide], axis=-1
    )


def norm_back(grad_normed, normed, scale):
    return scale * (grad_normed - normed * jnp.mean(grad_normed * normed, axis=-1, keepdims=True))


def gathered_weights_body(
    hidden_in,
    block_of,
    in_gain,
    w_query,
    w_key,
    w_value,
    w_output,
    q_gain,
    k_gain,
    post_gain,
    w_gate,
    w_up,
    w_down,
    cotangent,
):
    seq_count = hidden_in.shape[0]
    tok_rows = hidden_in.shape[1]
    flat_rows = seq_count * tok_rows
    model_width = hidden_in.shape[2]
    block_rows = tok_rows // 2
    block_total = 2 * lax.axis_size("ctx")
    seq_len = block_total * block_rows
    head_dim = q_gain.shape[0]
    q_heads = w_query.shape[1] // head_dim
    kv_heads = w_key.shape[1] // head_dim
    group_size = q_heads // kv_heads
    tile_blocks = math.gcd(block_total, max(1, 512 // block_rows))
    tile_rows = tile_blocks * block_rows
    q_scale = head_dim ** (-0.5)
    contract_rows = (((0,), (0,)), ((), ()))
    contract_cols = (((1,), (1,)), ((), ()))
    offsets = jnp.arange(block_rows, dtype=jnp.int32)
    positions = (block_of[:, :, None] * block_rows + offsets[None, None, :]).reshape(flat_rows)
    cosine, sine = rope_tables(positions, head_dim)
    residual = hidden_in.reshape(flat_rows, model_width).astype(jnp.float32)
    full_in_gain, full_query, full_key, full_value, full_output = (
        lax.all_gather(in_gain, ("ctx", "fsdp"), axis=0, tiled=True),
        lax.all_gather(w_query, ("ctx", "fsdp"), axis=0, tiled=True),
        lax.all_gather(w_key, ("ctx", "fsdp"), axis=0, tiled=True),
        lax.all_gather(w_value, ("ctx", "fsdp"), axis=0, tiled=True),
        lax.all_gather(w_output, ("ctx", "fsdp"), axis=0, tiled=True),
    )
    in_scale = lax.rsqrt(jnp.mean(residual * residual, axis=-1, keepdims=True) + EPS)
    in_normed = residual * in_scale
    attn_in = (in_normed * full_in_gain.astype(jnp.float32)).astype(jnp.bfloat16)
    q_raw = jnp.dot(attn_in, full_query, preferred_element_type=jnp.float32).reshape(
        flat_rows, q_heads, head_dim
    )
    k_raw = jnp.dot(attn_in, full_key, preferred_element_type=jnp.float32).reshape(
        flat_rows, kv_heads, head_dim
    )
    v_local = jnp.dot(attn_in, full_value, preferred_element_type=jnp.float32).astype(jnp.bfloat16)
    q_rms = lax.rsqrt(jnp.mean(q_raw * q_raw, axis=-1, keepdims=True) + EPS)
    q_unit = q_raw * q_rms
    queries = (rotate(q_unit * q_gain.astype(jnp.float32), cosine, sine) * q_scale).astype(
        jnp.bfloat16
    )
    k_rms = lax.rsqrt(jnp.mean(k_raw * k_raw, axis=-1, keepdims=True) + EPS)
    k_unit = k_raw * k_rms
    keys_local = rotate(k_unit * k_gain.astype(jnp.float32), cosine, sine).astype(jnp.bfloat16)
    all_keys, all_values, all_slots = (
        lax.all_gather(
            keys_local.reshape(seq_count, tok_rows, kv_heads * head_dim), "ctx", axis=1, tiled=True
        ),
        lax.all_gather(
            v_local.reshape(seq_count, tok_rows, kv_heads * head_dim), "ctx", axis=1, tiled=True
        ),
        lax.all_gather(block_of, "ctx", axis=1, tiled=True),
    )

    def tile_scores(query_tile, key_tile, query_pos, step):
        scores = jnp.einsum(
            "qhgd,khd->hgqk", query_tile, key_tile, preferred_element_type=jnp.float32
        )
        key_pos = step * tile_rows + jnp.arange(tile_rows, dtype=jnp.int32)
        visible = key_pos[None, :] <= query_pos[:, None]
        return (scores, visible)

    def sequence_tables(seq):
        key_blocks = all_keys[seq].reshape(block_total, block_rows, kv_heads, head_dim)
        value_blocks = all_values[seq].reshape(block_total, block_rows, kv_heads, head_dim)
        block_index = (
            jnp.zeros((block_total,), jnp.int32)
            .at[all_slots[seq]]
            .set(jnp.arange(block_total, dtype=jnp.int32))
        )
        return (key_blocks, value_blocks, block_index)

    def tile_index(block_index, step):
        return lax.dynamic_slice_in_dim(block_index, step * tile_blocks, tile_blocks)

    def fetch(table, block_index, step):
        return jnp.take(table, tile_index(block_index, step), axis=0).reshape(
            tile_rows, kv_heads, head_dim
        )

    log_totals = []
    attn_parts = []
    seq = 0
    key_blocks, value_blocks, block_index = sequence_tables(seq)
    for which in range(2):
        slot = 2 * seq + which
        query_tile = queries[slot * block_rows : (slot + 1) * block_rows].reshape(
            block_rows, kv_heads, group_size, head_dim
        )
        query_pos = positions[slot * block_rows : (slot + 1) * block_rows]
        tile_count = block_of[seq, which] // tile_blocks + 1

        def max_step(step, carry):
            running_max, running_sum = carry
            scores, visible = tile_scores(
                query_tile, fetch(key_blocks, block_index, step), query_pos, step
            )
            scores = jnp.where(visible, scores, -1e30)
            new_max = jnp.maximum(running_max, jnp.max(scores, axis=-1))
            running_sum = running_sum * jnp.exp(running_max - new_max) + jnp.sum(
                jnp.exp(scores - new_max[..., None]), axis=-1
            )
            return (new_max, running_sum)

        start_max = jnp.full((kv_heads, group_size, block_rows), -1e30, jnp.float32)
        start_sum = jnp.zeros((kv_heads, group_size, block_rows), jnp.float32)
        running_max, running_sum = lax.fori_loop(0, tile_count, max_step, (start_max, start_sum))
        log_total = running_max + jnp.log(running_sum)

        def value_step(step, total):
            scores, visible = tile_scores(
                query_tile, fetch(key_blocks, block_index, step), query_pos, step
            )
            probs = jnp.where(visible, jnp.exp(scores - log_total[..., None]), 0.0)
            return total + jnp.einsum(
                "hgqk,khd->qhgd",
                probs.astype(jnp.bfloat16),
                fetch(value_blocks, block_index, step),
                preferred_element_type=jnp.float32,
            )

        attn_part = lax.fori_loop(
            0,
            tile_count,
            value_step,
            jnp.zeros((block_rows, kv_heads, group_size, head_dim), jnp.float32),
        )
        log_totals.append(log_total)
        attn_parts.append(attn_part)
    attn_full = jnp.concatenate(attn_parts, axis=0)
    attn_bf = attn_full.reshape(flat_rows, q_heads * head_dim).astype(jnp.bfloat16)
    branch = jnp.dot(attn_bf, full_output, preferred_element_type=jnp.float32)
    hidden_mid = residual + branch
    full_post, full_gate, full_up, full_down = (
        lax.all_gather(post_gain, ("ctx", "fsdp"), axis=0, tiled=True),
        lax.all_gather(w_gate, ("ctx", "fsdp"), axis=0, tiled=True),
        lax.all_gather(w_up, ("ctx", "fsdp"), axis=0, tiled=True),
        lax.all_gather(w_down, ("ctx", "fsdp"), axis=0, tiled=True),
    )
    post_scale = lax.rsqrt(jnp.mean(hidden_mid * hidden_mid, axis=-1, keepdims=True) + EPS)
    post_normed = hidden_mid * post_scale
    mlp_in = (post_normed * full_post.astype(jnp.float32)).astype(jnp.bfloat16)
    gate_pre = jnp.dot(mlp_in, full_gate, preferred_element_type=jnp.float32)
    up_pre = jnp.dot(mlp_in, full_up, preferred_element_type=jnp.float32)
    sigmoid_gate = jax.nn.sigmoid(gate_pre)
    activated = gate_pre * sigmoid_gate
    inner = (activated * up_pre).astype(jnp.bfloat16)
    mlp_out = jnp.dot(inner, full_down, preferred_element_type=jnp.float32)
    output = (hidden_mid + mlp_out).astype(jnp.bfloat16)
    full_post, full_gate, full_up, full_down = (
        lax.all_gather(post_gain, ("ctx", "fsdp"), axis=0, tiled=True),
        lax.all_gather(w_gate, ("ctx", "fsdp"), axis=0, tiled=True),
        lax.all_gather(w_up, ("ctx", "fsdp"), axis=0, tiled=True),
        lax.all_gather(w_down, ("ctx", "fsdp"), axis=0, tiled=True),
    )
    grad_out = cotangent.reshape(flat_rows, model_width)
    grad_down = lax.dot_general(inner, grad_out, contract_rows, preferred_element_type=jnp.float32)
    part_down = lax.psum_scatter(grad_down, ("ctx", "fsdp"), scatter_dimension=0, tiled=True)
    grad_inner = lax.dot_general(
        grad_out, full_down, contract_cols, preferred_element_type=jnp.float32
    )
    grad_gate_pre = (
        grad_inner * up_pre * sigmoid_gate * (1.0 + gate_pre * (1.0 - sigmoid_gate))
    ).astype(jnp.bfloat16)
    grad_up_pre = (grad_inner * activated).astype(jnp.bfloat16)
    grad_gate = lax.dot_general(
        mlp_in, grad_gate_pre, contract_rows, preferred_element_type=jnp.float32
    )
    grad_up = lax.dot_general(
        mlp_in, grad_up_pre, contract_rows, preferred_element_type=jnp.float32
    )
    grad_mlp_in = lax.dot_general(
        grad_gate_pre, full_gate, contract_cols, preferred_element_type=jnp.float32
    ) + lax.dot_general(grad_up_pre, full_up, contract_cols, preferred_element_type=jnp.float32)
    grad_post_gain = jnp.sum(grad_mlp_in * post_normed, axis=0)
    grad_mid = grad_out.astype(jnp.float32) + norm_back(
        grad_mlp_in * full_post.astype(jnp.float32), post_normed, post_scale
    )
    part_post, part_gate, part_up = (
        lax.psum_scatter(grad_post_gain, ("ctx", "fsdp"), scatter_dimension=0, tiled=True),
        lax.psum_scatter(grad_gate, ("ctx", "fsdp"), scatter_dimension=0, tiled=True),
        lax.psum_scatter(grad_up, ("ctx", "fsdp"), scatter_dimension=0, tiled=True),
    )
    full_in_gain, full_query, full_key, full_value, full_output = (
        lax.all_gather(in_gain, ("ctx", "fsdp"), axis=0, tiled=True),
        lax.all_gather(w_query, ("ctx", "fsdp"), axis=0, tiled=True),
        lax.all_gather(w_key, ("ctx", "fsdp"), axis=0, tiled=True),
        lax.all_gather(w_value, ("ctx", "fsdp"), axis=0, tiled=True),
        lax.all_gather(w_output, ("ctx", "fsdp"), axis=0, tiled=True),
    )
    grad_branch = grad_mid.astype(jnp.bfloat16)
    grad_output = lax.dot_general(
        attn_bf, grad_branch, contract_rows, preferred_element_type=jnp.float32
    )
    grad_attn = lax.dot_general(
        grad_branch, full_output, contract_cols, preferred_element_type=jnp.float32
    ).astype(jnp.bfloat16)
    grad_attn = grad_attn.reshape(flat_rows, kv_heads, group_size, head_dim)
    query_grads = []
    seq = 0
    key_blocks, value_blocks, block_index = sequence_tables(seq)
    key_grads = jnp.zeros((block_total, block_rows, kv_heads, head_dim), jnp.float32)
    value_grads = jnp.zeros((block_total, block_rows, kv_heads, head_dim), jnp.float32)
    for which in range(2):
        slot = 2 * seq + which
        query_tile = queries[slot * block_rows : (slot + 1) * block_rows].reshape(
            block_rows, kv_heads, group_size, head_dim
        )
        query_pos = positions[slot * block_rows : (slot + 1) * block_rows]
        grad_tile = grad_attn[slot * block_rows : (slot + 1) * block_rows]
        tile_count = block_of[seq, which] // tile_blocks + 1
        delta = jnp.einsum("qhgd,qhgd->hgq", grad_tile.astype(jnp.float32), attn_parts[slot])
        log_total = log_totals[slot]

        def grad_step(step, carry):
            grad_query, keys_acc, values_acc = carry
            key_tile = fetch(key_blocks, block_index, step)
            scores, visible = tile_scores(query_tile, key_tile, query_pos, step)
            probs = jnp.where(visible, jnp.exp(scores - log_total[..., None]), 0.0)
            grad_probs = jnp.einsum(
                "qhgd,khd->hgqk",
                grad_tile,
                fetch(value_blocks, block_index, step),
                preferred_element_type=jnp.float32,
            )
            grad_scores = (probs * (grad_probs - delta[..., None])).astype(jnp.bfloat16)
            grad_query = grad_query + jnp.einsum(
                "hgqk,khd->qhgd", grad_scores, key_tile, preferred_element_type=jnp.float32
            )
            key_part = jnp.einsum(
                "hgqk,qhgd->khd", grad_scores, query_tile, preferred_element_type=jnp.float32
            )
            value_part = jnp.einsum(
                "hgqk,qhgd->khd",
                probs.astype(jnp.bfloat16),
                grad_tile,
                preferred_element_type=jnp.float32,
            )
            places = tile_index(block_index, step)
            keys_acc = keys_acc.at[places].add(
                key_part.reshape(tile_blocks, block_rows, kv_heads, head_dim)
            )
            values_acc = values_acc.at[places].add(
                value_part.reshape(tile_blocks, block_rows, kv_heads, head_dim)
            )
            return (grad_query, keys_acc, values_acc)

        start_query = jnp.zeros((block_rows, kv_heads, group_size, head_dim), jnp.float32)
        grad_query, key_grads, value_grads = lax.fori_loop(
            0, tile_count, grad_step, (start_query, key_grads, value_grads)
        )
        query_grads.append(grad_query)
    key_grad_list = [key_grads.reshape(seq_len, kv_heads * head_dim)]
    value_grad_list = [value_grads.reshape(seq_len, kv_heads * head_dim)]
    grad_keys, grad_values = (
        lax.psum_scatter(
            jnp.stack(key_grad_list, axis=0).astype(jnp.bfloat16),
            "ctx",
            scatter_dimension=1,
            tiled=True,
        ).astype(jnp.float32),
        lax.psum_scatter(
            jnp.stack(value_grad_list, axis=0).astype(jnp.bfloat16),
            "ctx",
            scatter_dimension=1,
            tiled=True,
        ).astype(jnp.float32),
    )
    grad_q_rot = (
        jnp.concatenate(query_grads, axis=0).reshape(flat_rows, q_heads, head_dim) * q_scale
    )
    grad_q_normed = rotate(grad_q_rot, cosine, -sine)
    grad_q_gain = jnp.sum(grad_q_normed * q_unit, axis=(0, 1))
    grad_q_raw = (
        norm_back(grad_q_normed * q_gain.astype(jnp.float32), q_unit, q_rms)
        .astype(jnp.bfloat16)
        .reshape(flat_rows, q_heads * head_dim)
    )
    grad_k_normed = rotate(grad_keys.reshape(flat_rows, kv_heads, head_dim), cosine, -sine)
    grad_k_gain = jnp.sum(grad_k_normed * k_unit, axis=(0, 1))
    grad_k_raw = (
        norm_back(grad_k_normed * k_gain.astype(jnp.float32), k_unit, k_rms)
        .astype(jnp.bfloat16)
        .reshape(flat_rows, kv_heads * head_dim)
    )
    grad_v_local = grad_values.reshape(flat_rows, kv_heads * head_dim).astype(jnp.bfloat16)
    grad_query_w = lax.dot_general(
        attn_in, grad_q_raw, contract_rows, preferred_element_type=jnp.float32
    )
    grad_key_w = lax.dot_general(
        attn_in, grad_k_raw, contract_rows, preferred_element_type=jnp.float32
    )
    grad_value_w = lax.dot_general(
        attn_in, grad_v_local, contract_rows, preferred_element_type=jnp.float32
    )
    grad_attn_in = lax.dot_general(
        grad_q_raw, full_query, contract_cols, preferred_element_type=jnp.float32
    )
    grad_attn_in = grad_attn_in + lax.dot_general(
        grad_k_raw, full_key, contract_cols, preferred_element_type=jnp.float32
    )
    grad_attn_in = grad_attn_in + lax.dot_general(
        grad_v_local, full_value, contract_cols, preferred_element_type=jnp.float32
    )
    grad_in_gain = jnp.sum(grad_attn_in * in_normed, axis=0)
    grad_input = grad_mid + norm_back(
        grad_attn_in * full_in_gain.astype(jnp.float32), in_normed, in_scale
    )
    part_in, part_query, part_key, part_value, part_output = (
        lax.psum_scatter(grad_in_gain, ("ctx", "fsdp"), scatter_dimension=0, tiled=True),
        lax.psum_scatter(grad_query_w, ("ctx", "fsdp"), scatter_dimension=0, tiled=True),
        lax.psum_scatter(grad_key_w, ("ctx", "fsdp"), scatter_dimension=0, tiled=True),
        lax.psum_scatter(grad_value_w, ("ctx", "fsdp"), scatter_dimension=0, tiled=True),
        lax.psum_scatter(grad_output, ("ctx", "fsdp"), scatter_dimension=0, tiled=True),
    )
    sum_q_gain, sum_k_gain = lax.psum((grad_q_gain, grad_k_gain), ("ctx", "fsdp"))
    return (
        output.reshape(seq_count, tok_rows, model_width),
        grad_input.reshape(seq_count, tok_rows, model_width),
        part_in,
        part_query,
        part_key,
        part_value,
        part_output,
        sum_q_gain,
        sum_k_gain,
        part_post,
        part_gate,
        part_up,
        part_down,
    )


MESH = pl.DeviceIdType.MESH
SUBS = 2


def ring_position(index, size):
    column, line = lax.rem(index, 2), lax.div(index, 2)
    return column * (line + 1) + (1 - column) * lax.rem(size - line, size)


def ring_member(position, size):
    late = lax.div(position + size // 2 - 1, size)
    beyond = lax.div(position + size - 1, size)
    return beyond * (1 - late) * (2 * position - 1) + late * 2 * (size - position)


class Ring:
    def __init__(self, size):
        self.size = size
        self.me = lax.axis_index("ctx")
        self.row = lax.axis_index("fsdp")
        self.position = ring_position(self.me, size)

    def member(self, way, steps):
        ahead = self.size - steps if way == 0 else steps
        return ring_member(lax.rem(self.position + ahead, self.size), self.size)

    def target(self, way):
        return (self.member(way, self.size - 1), self.row)

    def barrier(self):
        barrier = pltpu.get_barrier_semaphore()
        for way in range(2):
            pl.semaphore_signal(barrier, inc=1, device_id=self.target(way), device_id_type=MESH)
        pl.semaphore_wait(barrier, 2)


class GatherRing:
    def __init__(self, ring, own, out, send_sems, recv_sems):
        self.ring, self.own, self.out, self.send_sems, self.recv_sems = ring, own, out, send_sems, recv_sems
        self.half = own.shape[0] // 2
        self.sub = self.half // SUBS

    def copy(self, way, step, part, first=False):
        place = pl.ds(way * self.half + part * self.sub, self.sub)
        owner = self.ring.me if first else self.ring.member(way, step)
        source = self.own.at[place] if first else self.out.at[owner, place]
        return pltpu.make_async_remote_copy(
            src_ref=source,
            dst_ref=self.out.at[owner, place],
            send_sem=self.send_sems.at[way, step, part],
            recv_sem=self.recv_sems.at[way, step, part],
            device_id=self.ring.target(way),
            device_id_type=MESH,
        )

    def start(self, way):
        for part in range(SUBS):
            self.copy(way, 0, part, first=True).start()

    def step(self, step):
        for part in range(SUBS):
            for way in range(2):
                self.copy(way, step - 1, part).wait_recv()
                self.copy(way, step, part).start()

    def finish(self):
        last = self.ring.size - 2
        for part in range(SUBS):
            for way in range(2):
                self.copy(way, last, part).wait_recv()

        @pl.loop(0, last + 1)
        def _(step):
            for part in range(SUBS):
                for way in range(2):
                    self.copy(way, step, part).wait_send()

    def run(self):
        for way in range(2):
            self.start(way)

        @pl.loop(1, self.ring.size - 1)
        def _(step):
            self.step(step)

        self.finish()


def gather_sems(size):
    return [pltpu.SemaphoreType.DMA((2, size - 1, SUBS)), pltpu.SemaphoreType.DMA((2, size - 1, SUBS))]


class SumRing:
    def __init__(self, ring, compute, terms, outgoing, incoming, send_sems, recv_sems):
        self.ring, self.compute, self.terms = ring, compute, terms
        self.outgoing, self.incoming, self.send_sems, self.recv_sems = outgoing, incoming, send_sems, recv_sems
        self.half = terms.shape[1]
        self.sub = self.half // SUBS

    def copy(self, way, step, part):
        place = pl.ds(part * self.sub, self.sub)
        return pltpu.make_async_remote_copy(
            src_ref=self.outgoing.at[way, lax.rem(step, 2), place],
            dst_ref=self.incoming.at[way, step, place],
            send_sem=self.send_sems.at[way, step, part],
            recv_sem=self.recv_sems.at[way, step, part],
            device_id=self.ring.target(way),
            device_id_type=MESH,
        )

    def terms_of(self, step):
        self.compute([self.ring.member(way, step + 1) for way in range(2)])

    def begin(self):
        self.terms_of(0)
        for part in range(SUBS):
            place = pl.ds(part * self.sub, self.sub)
            for way in range(2):
                self.outgoing[way, 0, place] = self.terms[way, place].astype(jnp.bfloat16)
                self.copy(way, 0, part).start()

    def second(self):
        self.step(1, fresh=True)

    def step(self, step, fresh=False):
        self.terms_of(step)
        for part in range(SUBS):
            place = pl.ds(part * self.sub, self.sub)
            for way in range(2):
                self.copy(way, step - 1, part).wait_recv()
                total = self.terms[way, place] + self.incoming[way, step - 1, place].astype(jnp.float32)
                if not fresh:
                    self.copy(way, step - 2, part).wait_send()
                self.outgoing[way, lax.rem(step, 2), place] = total.astype(jnp.bfloat16)
                self.copy(way, step, part).start()

    def last_terms(self):
        self.compute([self.ring.me, self.ring.me])

    def result(self, way):
        last = self.ring.size - 2
        for part in range(SUBS):
            self.copy(way, last, part).wait_recv()
        return self.terms[way] + self.incoming[way, last].astype(jnp.float32)

    def finish(self):
        for step in (self.ring.size - 3, self.ring.size - 2):
            for part in range(SUBS):
                for way in range(2):
                    self.copy(way, step, part).wait_send()

    def run(self):
        self.begin()
        self.second()

        @pl.loop(2, self.ring.size - 1)
        def _(step):
            self.step(step)

        self.last_terms()


def sum_scratch(size, rows, width):
    half = rows // 2
    return [
        pltpu.VMEM((2, half, width), jnp.float32),
        pltpu.VMEM((2, 2, half, width), jnp.bfloat16),
        pltpu.VMEM((2, size - 1, half, width), jnp.bfloat16),
        pltpu.SemaphoreType.DMA((2, size - 1, SUBS)),
        pltpu.SemaphoreType.DMA((2, size - 1, SUBS)),
    ]


TILE = 512


def row_terms(left, weight, terms):
    half = terms.shape[1]

    def compute(members):
        lines = jnp.concatenate([left[members[way], way * half : (way + 1) * half] for way in range(2)], axis=0)

        @pl.loop(0, weight.shape[1] // TILE)
        def _(tile):
            columns = pl.ds(pl.multiple_of(tile * TILE, TILE), TILE)
            product = jnp.dot(lines, weight[:, columns], preferred_element_type=jnp.float32)
            for way in range(2):
                terms[way, :, columns] = product[way * half : (way + 1) * half]

    return compute


def row_terms_t(left, weight, terms):
    half = terms.shape[1]

    def compute(members):
        lines = jnp.concatenate([left[members[way], way * half : (way + 1) * half] for way in range(2)], axis=0)

        @pl.loop(0, weight.shape[0] // TILE)
        def _(tile):
            columns = pl.ds(pl.multiple_of(tile * TILE, TILE), TILE)
            product = lax.dot_general(
                lines, weight[columns, :], (((1,), (1,)), ((), ())), preferred_element_type=jnp.float32
            )
            for way in range(2):
                terms[way, :, columns] = product[way * half : (way + 1) * half]

    return compute


VMEM_SPEC = pl.BlockSpec(memory_space=pltpu.VMEM)
ANY_SPEC = pl.BlockSpec(memory_space=pl.ANY)


def ctx_peer(ring, ahead):
    return lax.rem(ring.me + ahead, ring.size)


def across(row, n_fsdp):
    return lax.rem(row + n_fsdp // 2, n_fsdp)


def beside(row):
    return row + 1 - 2 * lax.rem(row, 2)


def remote(source, target, send_sem, recv_sem, device):
    return pltpu.make_async_remote_copy(
        src_ref=source,
        dst_ref=target,
        send_sem=send_sem,
        recv_sem=recv_sem,
        device_id=device,
        device_id_type=MESH,
    )


def greet(devices):
    barrier = pltpu.get_barrier_semaphore()
    for device in devices:
        pl.semaphore_signal(barrier, inc=1, device_id=device, device_id_type=MESH)
    pl.semaphore_wait(barrier, len(devices))


def near_devices(ring, n_fsdp):
    return [(ctx_peer(ring, ahead), ring.row) for ahead in range(1, ring.size)] + [
        (ring.me, lax.rem(ring.row + ahead, n_fsdp)) for ahead in range(1, n_fsdp)
    ]


class Spread:
    def __init__(self, ring, n_fsdp, block, out, send_sems, recv_sems):
        self.ring, self.n_fsdp, self.block, self.out = ring, n_fsdp, block, out
        self.send_sems, self.recv_sems = send_sems, recv_sems

    def along_ctx(self, ahead):
        return remote(
            self.block,
            self.out.at[self.ring.row, self.ring.me],
            self.send_sems.at[ahead],
            self.recv_sems.at[ahead],
            (ctx_peer(self.ring, ahead), self.ring.row),
        )

    def along_fsdp(self, ahead):
        line = self.out.at[self.ring.row]
        sem = self.ring.size + ahead
        row = lax.rem(self.ring.row + ahead, self.n_fsdp)
        return remote(line, line, self.send_sems.at[sem], self.recv_sems.at[sem], (self.ring.me, row))

    def begin(self):
        for ahead in range(1, self.ring.size):
            self.along_ctx(ahead).start()
        self.out[self.ring.row, self.ring.me] = self.block[...]

    def collect(self):
        for ahead in range(1, self.ring.size):
            self.along_ctx(ahead).wait_recv()
        for ahead in range(1, self.n_fsdp):
            self.along_fsdp(ahead).start()
        for ahead in range(1, self.n_fsdp):
            self.along_fsdp(ahead).wait_recv()

    def finish(self):
        for ahead in range(1, self.ring.size):
            self.along_ctx(ahead).wait_send()
        for ahead in range(1, self.n_fsdp):
            self.along_fsdp(ahead).wait_send()


class SmallSum:
    def __init__(self, ring, n_fsdp, blocks, by_ctx, part, by_fsdp, send_sems, recv_sems):
        self.ring, self.n_fsdp, self.blocks, self.by_ctx, self.part, self.by_fsdp = (
            ring,
            n_fsdp,
            blocks,
            by_ctx,
            part,
            by_fsdp,
        )
        self.send_sems, self.recv_sems = send_sems, recv_sems

    def along_ctx(self, ahead):
        member = ctx_peer(self.ring, ahead)
        return remote(
            self.blocks.at[member],
            self.by_ctx.at[self.ring.me],
            self.send_sems.at[ahead],
            self.recv_sems.at[ahead],
            (member, self.ring.row),
        )

    def along_fsdp(self, ahead):
        row = lax.rem(self.ring.row + ahead, self.n_fsdp)
        sem = self.ring.size + ahead
        return remote(
            self.part.at[lax.div(row, 2)],
            self.by_fsdp.at[self.ring.row],
            self.send_sems.at[sem],
            self.recv_sems.at[sem],
            (self.ring.me, row),
        )

    def begin(self):
        for ahead in range(1, self.ring.size):
            self.along_ctx(ahead).start()
        self.by_ctx[self.ring.me] = self.blocks[self.ring.me]

    def cross(self):
        for ahead in range(1, self.ring.size):
            self.along_ctx(ahead).wait_recv()
        self.part[...] = jnp.sum(self.by_ctx[...], axis=0)
        for ahead in range(1, self.n_fsdp):
            self.along_fsdp(ahead).start()
        self.by_fsdp[self.ring.row] = self.part[lax.div(self.ring.row, 2)]

    def result(self):
        for ahead in range(1, self.n_fsdp):
            self.along_fsdp(ahead).wait_recv()
        return jnp.sum(self.by_fsdp[...], axis=0)

    def finish(self):
        for ahead in range(1, self.ring.size):
            self.along_ctx(ahead).wait_send()
        for ahead in range(1, self.n_fsdp):
            self.along_fsdp(ahead).wait_send()


def small_sems(size, n_fsdp):
    return [pltpu.SemaphoreType.DMA((size + n_fsdp,)), pltpu.SemaphoreType.DMA((size + n_fsdp,))]


class Rows:
    def __init__(self, ring, n_fsdp, shard, out, send_sems, recv_sems):
        own, far, twin = ring.row, across(ring.row, n_fsdp), beside(ring.row)
        self.keep = pltpu.make_async_copy(shard, out.at[own], send_sems.at[3])
        self.to_far = remote(shard, out.at[own], send_sems.at[0], recv_sems.at[0], (ring.me, far))
        self.to_twin = remote(shard, out.at[own], send_sems.at[1], recv_sems.at[1], (ring.me, twin))
        self.pass_on = remote(out.at[far], out.at[far], send_sems.at[2], recv_sems.at[2], (ring.me, twin))

    def begin(self):
        self.keep.start()
        self.to_far.start()
        self.to_twin.start()

    def relay(self):
        self.to_far.wait_recv()
        self.pass_on.start()

    def finish(self):
        self.keep.wait()
        self.to_far.wait_send()
        self.to_twin.wait()
        self.pass_on.wait()


def rows_sems():
    return [pltpu.SemaphoreType.DMA((4,)), pltpu.SemaphoreType.DMA((3,))]


class Columns:
    def __init__(self, ring, n_fsdp, shard, out, start, send_sems, recv_sems):
        self.ring, self.shard, self.out, self.send_sems, self.recv_sems = ring, shard, out, send_sems, recv_sems
        self.width = shard.shape[1] // ring.size
        self.place = pl.ds(start, self.width)
        far, twin = across(ring.row, n_fsdp), beside(ring.row)
        self.to_far = self.link(0, ring.row, far)
        self.to_twin = self.link(1, ring.row, twin)
        self.pass_on = self.link(2, far, twin)

    def link(self, which, row, target):
        block = self.out.at[:, row, :, self.place]
        sem = self.ring.size + which
        return remote(block, block, self.send_sems.at[sem], self.recv_sems.at[sem], (self.ring.me, target))

    def piece(self, ahead):
        member = ctx_peer(self.ring, ahead)
        source = self.shard.at[:, pl.ds(pl.multiple_of(member * self.width, self.width), self.width)]
        target = self.out.at[self.ring.me, self.ring.row, :, self.place]
        if ahead == 0:
            return pltpu.make_async_copy(source, target, self.send_sems.at[0])
        return remote(source, target, self.send_sems.at[ahead], self.recv_sems.at[ahead], (member, self.ring.row))

    def begin(self):
        for ahead in range(self.ring.size):
            self.piece(ahead).start()

    def spread(self):
        self.piece(0).wait()
        for ahead in range(1, self.ring.size):
            self.piece(ahead).wait_recv()
        self.to_far.start()
        self.to_twin.start()

    def relay(self):
        self.to_far.wait_recv()
        self.pass_on.start()

    def arrive(self):
        self.to_twin.wait_recv()
        self.pass_on.wait_recv()

    def finish(self):
        for ahead in range(1, self.ring.size):
            self.piece(ahead).wait_send()
        self.to_far.wait_send()
        self.to_twin.wait_send()
        self.pass_on.wait_send()


def columns_sems(size):
    return [pltpu.SemaphoreType.DMA((size + 3,)), pltpu.SemaphoreType.DMA((size + 3,))]


class RowGrads:
    def __init__(self, ring, n_fsdp, part, from_twin, to_far, from_far, send_sems, recv_sems):
        own, far, twin = ring.row, across(ring.row, n_fsdp), beside(ring.row)
        self.part, self.from_twin, self.to_far, self.from_far = part, from_twin, to_far, from_far
        self.own, self.far = own, far
        twin_far = across(twin, n_fsdp)
        self.first = [
            remote(part.at[twin], from_twin.at[0], send_sems.at[0], recv_sems.at[0], (ring.me, twin)),
            remote(part.at[twin_far], from_twin.at[1], send_sems.at[1], recv_sems.at[1], (ring.me, twin)),
        ]
        if to_far is None:
            self.to_far = part.at[far]
        self.second = remote(self.to_far, from_far, send_sems.at[2], recv_sems.at[2], (ring.me, far))

    def begin(self):
        self.first[1].start()
        self.first[0].start()

    def cross(self):
        self.first[1].wait_recv()
        self.to_far[...] = (
            self.part[self.far].astype(jnp.float32) + self.from_twin[1].astype(jnp.float32)
        ).astype(jnp.bfloat16)
        self.second.start()

    def result(self):
        self.first[0].wait_recv()
        self.second.wait_recv()
        return (
            self.part[self.own].astype(jnp.float32)
            + self.from_twin[0].astype(jnp.float32)
            + self.from_far[...].astype(jnp.float32)
        )

    def finish(self):
        for copy in self.first + [self.second]:
            copy.wait_send()


def row_grads_sems():
    return [pltpu.SemaphoreType.DMA((3,)), pltpu.SemaphoreType.DMA((3,))]


def row_grads_scratch(shape):
    return [
        pltpu.VMEM((2,) + shape, jnp.bfloat16),
        pltpu.VMEM(shape, jnp.bfloat16),
        pltpu.VMEM(shape, jnp.bfloat16),
    ] + row_grads_sems()


class Deal:
    def __init__(self, ring, total, arrived, send_sems, recv_sems):
        self.ring, self.total, self.arrived = ring, total, arrived
        self.send_sems, self.recv_sems = send_sems, recv_sems

    def piece(self, ahead):
        member = ctx_peer(self.ring, ahead)
        source, target = self.total.at[member], self.arrived.at[self.ring.me]
        if ahead == 0:
            return pltpu.make_async_copy(source, target, self.send_sems.at[0])
        return remote(source, target, self.send_sems.at[ahead], self.recv_sems.at[ahead], (member, self.ring.row))

    def begin(self):
        for ahead in range(self.ring.size):
            self.piece(ahead).start()

    def finish(self):
        for ahead in range(self.ring.size):
            self.piece(ahead).wait()


def deal_sems(size):
    return [pltpu.SemaphoreType.DMA((size,)), pltpu.SemaphoreType.DMA((size,))]


def params(collective_id):
    return pltpu.CompilerParams(
        collective_id=collective_id, has_side_effects=True, vmem_limit_bytes=62 * 1024 * 1024
    )


def head_norm(raw):
    return lax.rsqrt(jnp.mean(raw * raw, axis=-1, keepdims=True) + EPS)


def turn(values, cosine, sine):
    return values * cosine + pltpu.roll(values, values.shape[-1] // 2, 1) * sine


class Places:
    def __init__(self, ring, n_fsdp, all_small, starts, offsets, cosine, sine, places):
        self.ring, self.n_fsdp, self.all_small = ring, n_fsdp, all_small
        self.starts, self.offsets, self.cosine, self.sine, self.places = starts, offsets, cosine, sine, places
        self.block_rows = offsets.shape[1]

    def block(self, member, which):
        return self.all_small[self.ring.row, member, 2:3, which : which + 1]

    def fill(self):
        count = self.starts.shape[1]
        numbers = lax.broadcasted_iota(jnp.int32, (count, 1), 0).astype(jnp.float32)
        offset = lax.broadcasted_iota(jnp.int32, (self.block_rows, self.places.shape[1]), 0).astype(jnp.float32)
        for slot in range(count):
            block = self.block(slot // 2, slot % 2)
            chosen = (numbers == block).astype(jnp.float32)
            cos_start = jnp.sum(chosen * self.starts[0], axis=0, keepdims=True)
            sin_start = jnp.sum(chosen * self.starts[1], axis=0, keepdims=True)
            at = slice(slot * self.block_rows, (slot + 1) * self.block_rows)
            self.cosine[at] = cos_start * self.offsets[0] - sin_start * self.offsets[1]
            self.sine[at] = sin_start * self.offsets[0] + cos_start * self.offsets[1]
            self.places[at] = offset + block * self.block_rows

    def visible(self, member):
        width = self.places.shape[1]
        lane = lax.broadcasted_iota(jnp.int32, (1, width), 1).astype(jnp.float32)
        rows = float(self.block_rows)
        query = lane + jnp.where(lane < rows, self.block(member, 0) * rows, self.block(member, 1) * rows - rows)
        return self.places[...] <= query


def rotation_tables(blocks, block_rows, head):
    inverse = (THETA ** (-(np.arange(head // 2, dtype=np.float32) * np.float32(2.0) / head))).astype(np.float64)

    def both(at):
        angles = at.astype(np.float64)[:, None] * inverse[None, :]
        cosine, sine = np.cos(angles), np.sin(angles)
        return jnp.asarray(
            np.stack(
                [np.concatenate([cosine, cosine], axis=1), np.concatenate([-sine, sine], axis=1)], axis=0
            ).astype(np.float32)
        )

    return both(np.arange(blocks) * block_rows), both(np.arange(block_rows))


def fore_kernel(
    size,
    n_fsdp,
    q_heads,
    blocks,
    in_gain,
    post_gain,
    starts,
    offsets,
    q_gain,
    k_gain,
    hidden,
    w_query,
    w_key,
    w_value,
    w_output,
    w_gate,
    w_up,
    w_down,
    cotangent,
    all_small,
    gains,
    log_totals,
    raw_out,
    queries_out,
    keys_out,
    values_out,
    attn_out,
    attn_in_out,
    w_qkv_out,
    output_out,
    gu_out,
    down_out,
    grad_out,
    small,
    own,
    attn_in,
    w_qkv,
    cosine,
    sine,
    places_ref,
    values_t,
    raw,
    queries,
    keys,
    values,
    attn,
    small_send,
    small_recv,
    local_sems,
    *scratch,
):
    ring = Ring(size)
    head = q_gain.shape[1]
    tokens = hidden.shape[0]
    depth = in_gain.shape[1]
    q_width = q_heads * head
    k_width = w_key.shape[1] // size
    ff = w_gate.shape[1] // size
    columns_q = Columns(ring, n_fsdp, w_query, w_qkv, 0, *scratch[0:2])
    columns_k = Columns(ring, n_fsdp, w_key, w_qkv, q_width, *scratch[2:4])
    columns_v = Columns(ring, n_fsdp, w_value, w_qkv, q_width + k_width, *scratch[4:6])
    columns_gate = Columns(ring, n_fsdp, w_gate, gu_out, 0, *scratch[6:8])
    columns_up = Columns(ring, n_fsdp, w_up, gu_out, ff, *scratch[8:10])
    rows_output = Rows(ring, n_fsdp, w_output, output_out, *scratch[10:12])
    rows_down = Rows(ring, n_fsdp, w_down, down_out, *scratch[12:14])
    gathering = GatherRing(ring, own, attn_in, *scratch[14:16])
    gathering_cot = GatherRing(ring, cotangent, grad_out, *scratch[16:18])
    places = Places(ring, n_fsdp, all_small, starts, offsets, cosine, sine, places_ref)

    side = lax.rem(ring.row, 2)
    lane = lax.broadcasted_iota(jnp.int32, (1, 2 * depth), 1)
    mine = lax.div(lane, depth) == side
    small[...] = jnp.zeros_like(small)
    for row, part in enumerate((in_gain, post_gain)):
        part_row = part[...].astype(jnp.float32)
        small[row : row + 1] = jnp.where(mine, jnp.concatenate([part_row, part_row], axis=1), 0.0)
    small[2:3] = jnp.where(lane == 0, blocks[0, 0], jnp.where(lane == 1, blocks[0, 1], 0)).astype(jnp.float32)
    greet(near_devices(ring, n_fsdp))
    sharing = Spread(ring, n_fsdp, small, all_small, small_send, small_recv)
    sharing.begin()
    for columns in (columns_q, columns_k, columns_v):
        columns.begin()
    half = tokens // 2
    sharing.collect()
    for pair in range(size * n_fsdp // 2):
        member, chip = pair // (n_fsdp // 2), pair % (n_fsdp // 2)
        gains[:, pair * 128 : (pair + 1) * 128] = all_small[2 * chip, member] + all_small[2 * chip + 1, member]
    for way in range(2):
        place = slice(way * half, (way + 1) * half)
        rows = hidden[place].astype(jnp.float32)
        scale = lax.rsqrt(jnp.mean(rows * rows, axis=-1, keepdims=True) + EPS)
        own[place] = (rows * scale * gains[0:1]).astype(jnp.bfloat16)
        gathering.start(way)
    rows_output.begin()
    rows_down.begin()
    keep = pltpu.make_async_copy(own, attn_in.at[ring.me], local_sems.at[0])
    keep.start()
    keep_cot = pltpu.make_async_copy(cotangent, grad_out.at[ring.me], local_sems.at[1])
    keep_cot.start()
    gathering.step(1)
    places.fill()
    gathering.step(2)
    for columns in (columns_q, columns_k, columns_v):
        columns.spread()
    gathering.step(3)
    rows_output.relay()
    gathering.step(4)
    for columns in (columns_q, columns_k, columns_v):
        columns.relay()

    @pl.loop(5, size - 1)
    def _(step):
        gathering.step(step)

    columns_gate.begin()
    columns_up.begin()
    rows_down.relay()
    for columns in (columns_q, columns_k, columns_v):
        columns.arrive()
    gathering.finish()
    keep.wait()
    save_in = pltpu.make_async_copy(attn_in, attn_in_out, local_sems.at[2])
    save_in.start()
    save_qkv = pltpu.make_async_copy(w_qkv, w_qkv_out, local_sems.at[3])
    save_qkv.start()
    width = hidden.shape[1]

    @pl.loop(0, size)
    def _(member):
        at = pl.ds(pl.multiple_of(member * tokens, tokens), tokens)
        product = jnp.dot(
            attn_in[member], w_qkv[...].reshape(width, w_qkv.shape[3]), preferred_element_type=jnp.float32
        )
        raw[at, :] = product[:, : q_width + head]
        for which in range(q_heads + 1):
            values_raw = product[:, which * head : (which + 1) * head]
            gain = q_gain if which < q_heads else k_gain
            turned = turn(values_raw * head_norm(values_raw) * gain[...].astype(jnp.float32), cosine[at, :], sine[at, :])
            if which < q_heads:
                queries[member, which] = (turned * head**-0.5).astype(jnp.bfloat16)
            else:
                keys[at, :] = turned.astype(jnp.bfloat16)
        fresh = product[:, q_width + head :]
        values[at, :] = fresh.astype(jnp.bfloat16)
        values_t[:, at] = fresh.T.astype(jnp.bfloat16)

    @pl.loop(0, size)
    def _(member):
        visible = places.visible(member)
        for which in range(q_heads):
            scores = lax.dot_general(
                keys[...], queries[member, which], (((1,), (1,)), ((), ())), preferred_element_type=jnp.float32
            )
            scores = jnp.where(visible, scores, -1e30)
            peak = jnp.max(scores, axis=0, keepdims=True)
            weights = jnp.exp(scores - peak)
            total = jnp.sum(weights, axis=0, keepdims=True)
            probs = (weights * (1.0 / total)).astype(jnp.bfloat16)
            mixed = jnp.dot(values_t[...], probs, preferred_element_type=jnp.float32)
            attn[member, :, which * head : (which + 1) * head] = mixed.T.astype(jnp.bfloat16)
            log_totals[member, which : which + 1, :] = peak + jnp.log(total)

    saves = [
        pltpu.make_async_copy(source, target, local_sems.at[4 + which])
        for which, (source, target) in enumerate(
            ((raw, raw_out), (queries, queries_out), (keys, keys_out), (values, values_out), (attn, attn_out))
        )
    ]
    for save in saves:
        save.start()
    columns_gate.spread()
    for way in range(2):
        gathering_cot.start(way)
    gathering_cot.step(1)
    gathering_cot.step(2)
    columns_up.spread()
    gathering_cot.step(3)
    columns_gate.relay()

    @pl.loop(4, size - 1)
    def _(step):
        gathering_cot.step(step)

    columns_up.relay()
    gathering_cot.finish()
    sharing.finish()
    columns_gate.arrive()
    columns_up.arrive()
    for columns in (columns_q, columns_k, columns_v, columns_gate, columns_up):
        columns.finish()
    rows_output.finish()
    rows_down.finish()
    keep_cot.wait()
    for save in saves + [save_in, save_qkv]:
        save.wait()


def fore(blocks, in_gain, post_gain, tables, q_gain, k_gain, hidden, w_query, w_key, w_value, w_output, w_gate, w_up, w_down, cotangent):
    size, n_fsdp = lax.axis_size("ctx"), lax.axis_size("fsdp")
    rows, width = hidden.shape
    depth = w_query.shape[0]
    head = q_gain.shape[0]
    q_heads = w_query.shape[1] // size // head
    everyone = size * rows
    qkv_share = (w_query.shape[1] + w_key.shape[1] + w_value.shape[1]) // size
    gu_share = (w_gate.shape[1] + w_up.shape[1]) // size
    f32, bf16 = jnp.float32, jnp.bfloat16
    return pl.pallas_call(
        functools.partial(fore_kernel, size, n_fsdp, q_heads),
        out_shape=[
            jax.ShapeDtypeStruct((n_fsdp, size, 8, 2 * depth), f32),
            jax.ShapeDtypeStruct((8, width), f32),
            jax.ShapeDtypeStruct((size, q_heads, rows), f32),
            jax.ShapeDtypeStruct((everyone, (q_heads + 1) * head), f32),
            jax.ShapeDtypeStruct((size, q_heads, rows, head), bf16),
            jax.ShapeDtypeStruct((everyone, head), bf16),
            jax.ShapeDtypeStruct((everyone, head), bf16),
            jax.ShapeDtypeStruct((size, rows, q_heads * head), bf16),
            jax.ShapeDtypeStruct((size, rows, width), bf16),
            jax.ShapeDtypeStruct((size, n_fsdp, depth, qkv_share), bf16),
            jax.ShapeDtypeStruct((n_fsdp,) + w_output.shape, bf16),
            jax.ShapeDtypeStruct((size, n_fsdp, depth, gu_share), bf16),
            jax.ShapeDtypeStruct((n_fsdp,) + w_down.shape, bf16),
            jax.ShapeDtypeStruct((size, rows, width), bf16),
        ],
        in_specs=[pl.BlockSpec(memory_space=pltpu.SMEM)] + [VMEM_SPEC] * 7 + [ANY_SPEC] * 8,
        out_specs=[VMEM_SPEC] * 3 + [ANY_SPEC] * 11,
        scratch_shapes=[
            pltpu.VMEM((8, 2 * depth), f32),
            pltpu.VMEM((rows, width), bf16),
            pltpu.VMEM((size, rows, width), bf16),
            pltpu.VMEM((size, n_fsdp, depth, qkv_share), bf16),
            pltpu.VMEM((everyone, head), f32),
            pltpu.VMEM((everyone, head), f32),
            pltpu.VMEM((everyone, head), f32),
            pltpu.VMEM((head, everyone), bf16),
            pltpu.VMEM((everyone, (q_heads + 1) * head), f32),
            pltpu.VMEM((size, q_heads, rows, head), bf16),
            pltpu.VMEM((everyone, head), bf16),
            pltpu.VMEM((everyone, head), bf16),
            pltpu.VMEM((size, rows, q_heads * head), bf16),
        ]
        + small_sems(size, n_fsdp)
        + [pltpu.SemaphoreType.DMA((9,))]
        + columns_sems(size) * 5
        + rows_sems() * 2
        + gather_sems(size) * 2,
        compiler_params=params(2),
    )(
        blocks,
        in_gain.reshape(1, depth),
        post_gain.reshape(1, depth),
        *tables,
        q_gain.reshape(1, head),
        k_gain.reshape(1, head),
        hidden,
        w_query,
        w_key,
        w_value,
        w_output,
        w_gate,
        w_up,
        w_down,
        cotangent,
    )


def norm_pull(grad_normed, normed, scale):
    return scale * (grad_normed - normed * jnp.mean(grad_normed * normed, axis=-1, keepdims=True))


def feed_forward_kernel(
    size,
    n_fsdp,
    attn,
    w_output,
    hidden,
    gains,
    w_gu_in,
    w_down_in,
    cot_in,
    out_hidden,
    grad_gain,
    grad_mid_out,
    grad_branch,
    gu_total_out,
    down_out,
    w_gu,
    w_down,
    cot,
    load_sems,
    mid,
    own,
    mlp_in,
    inner,
    grad_gu,
    gu_part,
    down_part,
    grad_mid,
    gu_total,
    down_total,
    layer_terms,
    *scratch,
):
    loads = [
        pltpu.make_async_copy(source, target, load_sems.at[which])
        for which, (source, target) in enumerate(((w_gu_in, w_gu), (w_down_in, w_down), (cot_in, cot)))
    ]
    for load in loads:
        load.start()
    ring = Ring(size)
    greet(near_devices(ring, n_fsdp))
    half = own.shape[0] // 2
    ff = w_down.shape[0]
    out_sums, gather_sems_in = scratch[:5], scratch[5:7]
    layer_sums = (layer_terms,) + tuple(scratch[7:11])
    gather_sems_out, keep_sems = scratch[11:13], scratch[13]
    column_scratch = (scratch[14], None, gu_total, scratch[15], scratch[16])
    row_scratch = (scratch[17], None, scratch[18], scratch[19], scratch[20])

    first = SumRing(ring, row_terms(attn, w_output, out_sums[0]), *out_sums)
    first.run()
    gathering = GatherRing(ring, own, mlp_in, *gather_sems_in)
    for way in range(2):
        place = slice(way * half, (way + 1) * half)
        total = first.result(way) + hidden[place].astype(jnp.float32)
        mid[place] = total
        scale = lax.rsqrt(jnp.mean(total * total, axis=-1, keepdims=True) + EPS)
        own[place] = (total * scale * gains[1:2]).astype(jnp.bfloat16)
        gathering.start(way)
    first.finish()
    keep = pltpu.make_async_copy(own, mlp_in.at[ring.me], keep_sems.at[0])
    keep.start()
    for load in loads:
        load.wait()

    def units(lines, members):
        cot_lines = jnp.concatenate([cot[members[way], way * half : (way + 1) * half] for way in range(2)], axis=0)

        @pl.loop(0, ff // UNITS)
        def _(tile):
            at = pl.multiple_of(tile * UNITS, UNITS)
            here, there = pl.ds(at, UNITS), pl.ds(pl.multiple_of(ff + at, UNITS), UNITS)
            gate = jnp.dot(lines, w_gu[:, here], preferred_element_type=jnp.float32)
            up = jnp.dot(lines, w_gu[:, there], preferred_element_type=jnp.float32)
            pulled = lax.dot_general(
                cot_lines, w_down[here, :], (((1,), (1,)), ((), ())), preferred_element_type=jnp.float32
            )
            sigmoid = 1.0 / (1.0 + jnp.exp(-gate))
            active = gate * sigmoid
            inner_new = (active * up).astype(jnp.bfloat16)
            gate_new = (pulled * up * sigmoid * (1.0 + gate * (1.0 - sigmoid))).astype(jnp.bfloat16)
            up_new = (pulled * active).astype(jnp.bfloat16)
            for way in range(2):
                place = slice(way * half, (way + 1) * half)
                inner[members[way], place, here] = inner_new[place]
                grad_gu[members[way], place, here] = gate_new[place]
                grad_gu[members[way], place, there] = up_new[place]

    def units_of(step):
        members = [ring.member(way, step) for way in range(2)]
        units(
            jnp.concatenate([mlp_in[members[way], way * half : (way + 1) * half] for way in range(2)], axis=0), members
        )

    units(own[...], [ring.me, ring.me])

    @pl.loop(1, size - 1)
    def _(step):
        gathering.step(step)
        units_of(step)

    third = SumRing(ring, row_terms_t(grad_gu, w_gu, out_sums[0]), *out_sums)
    third.begin()
    gathering.finish()
    keep.wait()
    units_of(size - 1)
    rows_all = size * 2 * half
    width = w_gu.shape[0]
    block = width // size

    def gu_tile(member):
        columns = pl.ds(pl.multiple_of(member * block, block), block)
        lines = mlp_in[:, :, columns].reshape(rows_all, block)

        @pl.loop(0, 2 * ff // TILE)
        def _(tile):
            there = pl.ds(pl.multiple_of(tile * TILE, TILE), TILE)
            product = lax.dot_general(
                lines,
                grad_gu[:, :, there].reshape(rows_all, TILE),
                (((0,), (0,)), ((), ())),
                preferred_element_type=jnp.float32,
            ).astype(jnp.bfloat16)
            for row in range(n_fsdp):
                gu_part[row, member, :, there] = product[row * (block // n_fsdp) : (row + 1) * (block // n_fsdp)]

    share = ff // n_fsdp

    def down_tile(tile):
        columns = pl.ds(pl.multiple_of(tile * UNITS, UNITS), UNITS)
        lines = cot[:, :, columns].reshape(rows_all, UNITS)
        product = lax.dot_general(
            inner[...].reshape(rows_all, ff), lines, (((0,), (0,)), ((), ())), preferred_element_type=jnp.float32
        ).astype(jnp.bfloat16)
        for row in range(n_fsdp):
            down_part[row, :, columns] = product[row * share : (row + 1) * share]

    gu_tile(0)
    third.second()
    gu_tile(1)

    @pl.loop(2, size - 1)
    def _(step):
        third.step(step)
        gu_tile(step)

        @pl.when(step < 2 + width // UNITS // 2)
        def _():
            down_tile(2 * step - 4)
            down_tile(2 * step - 3)

    second = SumRing(ring, row_terms(inner, w_down, layer_sums[0]), *layer_sums)
    second.begin()
    gu_tile(size - 1)
    columns = RowGrads(ring, n_fsdp, gu_part, *column_scratch)
    rows = RowGrads(ring, n_fsdp, down_part, *row_scratch)
    columns.begin()
    rows.begin()
    third.last_terms()
    gathering = GatherRing(ring, own, grad_branch, *gather_sems_out)
    gain_sum = jnp.zeros_like(grad_gain)
    for way in range(2):
        place = slice(way * half, (way + 1) * half)
        pulled = third.result(way)
        values = mid[place]
        scale = lax.rsqrt(jnp.mean(values * values, axis=-1, keepdims=True) + EPS)
        normed = values * scale
        gain_sum = gain_sum + jnp.sum(pulled * normed, axis=0, keepdims=True)
        total = cot[ring.me, place].astype(jnp.float32) + norm_pull(pulled * gains[1:2], normed, scale)
        grad_mid[place] = total
        own[place] = total.astype(jnp.bfloat16)
        gathering.start(way)
    grad_gain[...] = gain_sum
    keep = pltpu.make_async_copy(own, grad_branch.at[ring.me], keep_sems.at[1])
    keep.start()
    save_mid = pltpu.make_async_copy(grad_mid, grad_mid_out, keep_sems.at[2])
    save_mid.start()
    third.finish()
    second.second()
    gathering.step(1)
    columns.cross()
    rows.cross()

    @pl.loop(2, size - 1)
    def _(step):
        second.step(step)
        gathering.step(step)

    second.last_terms()
    down_total[...] = rows.result()
    save_down = pltpu.make_async_copy(down_total, down_out, keep_sems.at[3])
    save_down.start()
    gu_total[...] = columns.result().astype(jnp.bfloat16)
    save_gu = pltpu.make_async_copy(gu_total, gu_total_out, keep_sems.at[4])
    save_gu.start()
    for way in range(2):
        place = slice(way * half, (way + 1) * half)
        out_hidden[place] = (mid[place] + second.result(way)).astype(jnp.bfloat16)
    gathering.finish()
    second.finish()
    columns.finish()
    rows.finish()
    for copy in (keep, save_mid, save_down, save_gu):
        copy.wait()


UNITS = 256


def feed_forward(attn, w_output, hidden, gains, w_gu, w_down, cotangent):
    size, n_fsdp = lax.axis_size("ctx"), lax.axis_size("fsdp")
    rows, width = hidden.shape
    ff = w_down.shape[0]
    depth = width // size // n_fsdp
    sums = sum_scratch(size, rows, width)
    return pl.pallas_call(
        functools.partial(feed_forward_kernel, size, n_fsdp),
        out_shape=[
            jax.ShapeDtypeStruct((rows, width), jnp.bfloat16),
            jax.ShapeDtypeStruct((1, width), jnp.float32),
            jax.ShapeDtypeStruct((rows, width), jnp.float32),
            jax.ShapeDtypeStruct((size, rows, width), jnp.bfloat16),
            jax.ShapeDtypeStruct((size, depth, 2 * ff), jnp.bfloat16),
            jax.ShapeDtypeStruct((ff // n_fsdp, width), jnp.float32),
        ],
        in_specs=[VMEM_SPEC] * 4 + [ANY_SPEC] * 3,
        out_specs=[VMEM_SPEC] * 2 + [ANY_SPEC] * 4,
        scratch_shapes=[
            pltpu.VMEM(w_gu.shape, jnp.bfloat16),
            pltpu.VMEM(w_down.shape, jnp.bfloat16),
            pltpu.VMEM((size, rows, width), jnp.bfloat16),
            pltpu.SemaphoreType.DMA((3,)),
            pltpu.VMEM((rows, width), jnp.float32),
            pltpu.VMEM((rows, width), jnp.bfloat16),
            pltpu.VMEM((size, rows, width), jnp.bfloat16),
            pltpu.VMEM((size, rows, ff), jnp.bfloat16),
            pltpu.VMEM((size, rows, 2 * ff), jnp.bfloat16),
            pltpu.VMEM((n_fsdp, size, depth, 2 * ff), jnp.bfloat16),
            pltpu.VMEM((n_fsdp, ff // n_fsdp, width), jnp.bfloat16),
            pltpu.VMEM((rows, width), jnp.float32),
            pltpu.VMEM((size, depth, 2 * ff), jnp.bfloat16),
            pltpu.VMEM((ff // n_fsdp, width), jnp.float32),
            pltpu.VMEM((2, rows // 2, width), jnp.float32),
        ]
        + sums
        + gather_sems(size)
        + sums[1:]
        + gather_sems(size)
        + [pltpu.SemaphoreType.DMA((5,))]
        + [pltpu.VMEM((2, size, depth, 2 * ff), jnp.bfloat16)]
        + row_grads_sems()
        + [pltpu.VMEM((2, ff // n_fsdp, width), jnp.bfloat16), pltpu.VMEM((ff // n_fsdp, width), jnp.bfloat16)]
        + row_grads_sems(),
        compiler_params=params(5),
    )(
        attn,
        w_output,
        hidden,
        gains,
        w_gu,
        w_down,
        cotangent,
    )


def back_kernel(
    size,
    n_fsdp,
    all_blocks,
    starts,
    offsets,
    q_gain,
    k_gain,
    gains,
    post_sum,
    log_totals,
    *refs,
):
    sources, refs = refs[:11], refs[11:]
    gu_total = refs[0]
    grad_hidden, gains_out, output_out, gu_out, qkv_out = refs[1:6]
    targets, refs = refs[6:17], refs[17:]
    grad_branch, attn, w_output, queries, keys, values, raw, attn_in, w_qkv, hidden, grad_mid = targets
    load_sems, cosine, sine, places_ref, keys_t, grad_keys, grad_values, head_sums, grads, qkv_part, output_part = refs[:11]
    small, small_ctx, small_part, small_fsdp, small_send, small_recv = refs[11:17]
    scratch = refs[17:]
    loads = [
        pltpu.make_async_copy(source, target, load_sems.at[which])
        for which, (source, target) in enumerate(zip(sources, targets))
    ]
    for load in loads:
        load.start()
    sums = scratch[:5]
    ring = Ring(size)
    greet(near_devices(ring, n_fsdp))
    half = hidden.shape[0] // 2
    total = scratch[8]
    columns = RowGrads(ring, n_fsdp, qkv_part, scratch[5], None, *scratch[6:8], scratch[9])
    dealing = Deal(ring, total, qkv_out, *scratch[10:12])
    rows = RowGrads(ring, n_fsdp, output_part, scratch[12], None, *scratch[13:16])
    gu_dealing = Deal(ring, gu_total, gu_out, *scratch[16:18])
    gu_dealing.begin()
    places = Places(ring, n_fsdp, all_blocks, starts, offsets, cosine, sine, places_ref)
    places.fill()
    head = q_gain.shape[1]
    q_heads = queries.shape[1]
    tokens = attn_in.shape[1]
    everyone = size * tokens
    width = attn_in.shape[2]
    q_width = q_heads * head
    grad_keys[...] = jnp.zeros_like(grad_keys)
    grad_values[...] = jnp.zeros_like(grad_values)
    head_sums[...] = jnp.zeros_like(head_sums)
    for load in loads[:3]:
        load.wait()

    def through_head(pulled, at, which, gain_here):
        turned = turn(pulled, cosine[at, :], -sine[at, :])
        values_raw = raw[at, which * head : (which + 1) * head]
        scale = head_norm(values_raw)
        unit = values_raw * scale
        kind = 0 if which < q_heads else 1
        head_sums[kind : kind + 1] = head_sums[kind : kind + 1] + jnp.sum(turned * unit, axis=0, keepdims=True)
        return norm_pull(turned * gain_here[...].astype(jnp.float32), unit, scale).astype(jnp.bfloat16)

    def output_tile(tile):
        there = pl.ds(pl.multiple_of(tile * TILE, TILE), TILE)
        product = lax.dot_general(
            attn[...].reshape(everyone, q_width),
            grad_branch[:, :, there].reshape(everyone, TILE),
            (((0,), (0,)), ((), ())),
            preferred_element_type=jnp.float32,
        ).astype(jnp.bfloat16)
        share = q_width // n_fsdp
        for row in range(n_fsdp):
            output_part[row, :, there] = product[row * share : (row + 1) * share]

    @pl.loop(0, width // TILE)
    def _(tile):
        output_tile(tile)

    rows.begin()
    for load in loads[3:]:
        load.wait()
    keys_t[...] = keys[...].astype(jnp.float32).T.astype(jnp.bfloat16)

    @pl.loop(0, size)
    def _(member):
        at = pl.ds(pl.multiple_of(member * tokens, tokens), tokens)
        grad_attn = lax.dot_general(
            grad_branch[member], w_output[...], (((1,), (1,)), ((), ())), preferred_element_type=jnp.float32
        ).astype(jnp.bfloat16)
        visible = places.visible(member)
        for which in range(q_heads):
            lanes = slice(which * head, (which + 1) * head)
            pulled = grad_attn[:, lanes]
            query = queries[member, which]
            scores = lax.dot_general(keys[...], query, (((1,), (1,)), ((), ())), preferred_element_type=jnp.float32)
            probs = jnp.where(visible, jnp.exp(scores - log_totals[member, which : which + 1, :]), 0.0)
            grad_probs = lax.dot_general(
                values[...], pulled, (((1,), (1,)), ((), ())), preferred_element_type=jnp.float32
            )
            delta = jnp.sum(probs * grad_probs, axis=0, keepdims=True)
            grad_scores = (probs * (grad_probs - delta)).astype(jnp.bfloat16)
            grad_keys[...] = grad_keys[...] + jnp.dot(grad_scores, query, preferred_element_type=jnp.float32)
            grad_values[...] = grad_values[...] + jnp.dot(
                probs.astype(jnp.bfloat16), pulled, preferred_element_type=jnp.float32
            )
            grad_query = jnp.dot(keys_t[...], grad_scores, preferred_element_type=jnp.float32).T
            grads[member, :, lanes] = through_head(grad_query * head**-0.5, at, which, q_gain)

    rows.cross()

    @pl.loop(0, size)
    def _(member):
        at = pl.ds(pl.multiple_of(member * tokens, tokens), tokens)
        grads[member, :, q_width : q_width + head] = through_head(grad_keys[at, :], at, q_heads, k_gain)
        grads[member, :, q_width + head :] = grad_values[at, :].astype(jnp.bfloat16)

    block = width // size

    def qkv_tile(member):
        lines = attn_in[:, :, pl.ds(pl.multiple_of(member * block, block), block)].reshape(everyone, block)
        product = lax.dot_general(
            lines,
            grads[...].reshape(everyone, grads.shape[2]),
            (((0,), (0,)), ((), ())),
            preferred_element_type=jnp.float32,
        ).astype(jnp.bfloat16)
        for row in range(n_fsdp):
            qkv_part[row, member] = product[row * (block // n_fsdp) : (row + 1) * (block // n_fsdp)]

    summing = SumRing(ring, row_terms_t(grads, w_qkv, sums[0]), *sums)
    summing.begin()

    @pl.loop(0, size // 2)
    def _(member):
        qkv_tile(member)

    summing.second()

    @pl.loop(size // 2, size)
    def _(member):
        qkv_tile(member)

    columns.begin()
    summing.step(2)
    columns.cross()
    summing.step(3)
    summing.step(4)
    summing.step(5)
    total[...] = columns.result().astype(jnp.bfloat16)
    dealing.begin()
    summing.step(6)
    output_out[...] = rows.result()
    summing.last_terms()
    gain_sum = jnp.zeros_like(post_sum)
    for way in range(2):
        place = slice(way * half, (way + 1) * half)
        pulled = summing.result(way)
        values_in = hidden[place].astype(jnp.float32)
        scale = lax.rsqrt(jnp.mean(values_in * values_in, axis=-1, keepdims=True) + EPS)
        normed = values_in * scale
        gain_sum = gain_sum + jnp.sum(pulled * normed, axis=0, keepdims=True)
        grad_hidden[place] = grad_mid[place] + norm_pull(pulled * gains[0:1], normed, scale)
    chips = n_fsdp // 2
    for pair in range(size * chips):
        lanes = slice(pair * 128, (pair + 1) * 128)
        small[pair // chips, pair % chips, 0:1] = gain_sum[:, lanes]
        small[pair // chips, pair % chips, 1:2] = post_sum[:, lanes]
        small[pair // chips, pair % chips, 2:4] = head_sums[0:2]
        small[pair // chips, pair % chips, 4:8] = jnp.zeros((4, 128), jnp.float32)
    sharing = SmallSum(ring, n_fsdp, small, small_ctx, small_part, small_fsdp, small_send, small_recv)
    sharing.begin()
    sharing.cross()
    gains_out[...] = sharing.result()
    sharing.finish()
    summing.finish()
    columns.finish()
    rows.finish()
    dealing.finish()
    gu_dealing.finish()


def back(
    all_small,
    tables,
    q_gain,
    k_gain,
    raw,
    queries,
    keys,
    values,
    attn,
    log_totals,
    hidden,
    grad_mid,
    gains,
    post_sum,
    gu_total,
    grad_branch,
    w_output,
    attn_in,
    w_qkv,
):
    size, n_fsdp = lax.axis_size("ctx"), lax.axis_size("fsdp")
    rows, width = hidden.shape
    head = q_gain.shape[0]
    everyone = size * rows
    share = w_qkv.shape[1]
    depth = width // size // n_fsdp
    q_width = attn.shape[2]
    f32, bf16 = jnp.float32, jnp.bfloat16
    loaded = [grad_branch, attn, w_output, queries, keys, values, raw, attn_in, w_qkv, hidden, grad_mid]
    return pl.pallas_call(
        functools.partial(back_kernel, size, n_fsdp),
        out_shape=[
            jax.ShapeDtypeStruct((rows, width), f32),
            jax.ShapeDtypeStruct((8, 128), f32),
            jax.ShapeDtypeStruct((q_width // n_fsdp, width), f32),
            jax.ShapeDtypeStruct(gu_total.shape, bf16),
            jax.ShapeDtypeStruct((size, depth, share), bf16),
        ],
        in_specs=[VMEM_SPEC] * 8 + [ANY_SPEC] * 12,
        out_specs=[VMEM_SPEC] * 3 + [ANY_SPEC] * 2,
        scratch_shapes=[pltpu.VMEM(array.shape, array.dtype) for array in loaded]
        + [
            pltpu.SemaphoreType.DMA((len(loaded),)),
            pltpu.VMEM((everyone, head), f32),
            pltpu.VMEM((everyone, head), f32),
            pltpu.VMEM((everyone, head), f32),
            pltpu.VMEM((head, everyone), bf16),
            pltpu.VMEM((everyone, head), f32),
            pltpu.VMEM((everyone, head), f32),
            pltpu.VMEM((8, head), f32),
            pltpu.VMEM((size, rows, share), bf16),
            pltpu.VMEM((n_fsdp, size, depth, share), bf16),
            pltpu.VMEM((n_fsdp, q_width // n_fsdp, width), bf16),
            pltpu.VMEM((size, n_fsdp // 2, 8, 128), f32),
            pltpu.VMEM((size, n_fsdp // 2, 8, 128), f32),
            pltpu.VMEM((n_fsdp // 2, 8, 128), f32),
            pltpu.VMEM((n_fsdp, 8, 128), f32),
        ]
        + small_sems(size, n_fsdp)
        + sum_scratch(size, rows, width)
        + [
            pltpu.VMEM((2, size, depth, share), bf16),
            pltpu.VMEM((size, depth, share), bf16),
            pltpu.SemaphoreType.DMA((3,)),
            pltpu.VMEM((size, depth, share), bf16),
            pltpu.SemaphoreType.DMA((3,)),
        ]
        + deal_sems(size)
        + [
            pltpu.VMEM((2, q_width // n_fsdp, width), bf16),
            pltpu.VMEM((q_width // n_fsdp, width), bf16),
        ]
        + row_grads_sems()
        + deal_sems(size),
        compiler_params=params(6),
    )(
        all_small,
        *tables,
        q_gain.reshape(1, head),
        k_gain.reshape(1, head),
        gains,
        post_sum,
        log_totals,
        *loaded,
        gu_total,
    )


def finish_kernel(
    gu,
    qkv,
    grad_hidden,
    hidden,
    down,
    output,
    gain_sums,
    gate_out,
    up_out,
    query_out,
    key_out,
    value_out,
    grad_hidden_out,
    hidden_out,
    down_out,
    output_out,
    in_gain_out,
    post_gain_out,
    q_gain_out,
    k_gain_out,
):
    start = 0
    for arrived, outs in ((gu, (gate_out, up_out)), (qkv, (query_out, key_out, value_out))):
        start = 0
        for out in outs:
            width = out.shape[1]
            out[...] = arrived[0, :, start : start + width].astype(jnp.float32)
            start += width
    grad_hidden_out[...] = grad_hidden[...]
    hidden_out[...] = hidden[...]
    down_out[...] = down[...]
    output_out[...] = output[...]
    side = lax.rem(lax.axis_index("fsdp"), 2)
    depth = in_gain_out.shape[1]
    for row, out in enumerate((in_gain_out, post_gain_out)):
        out[...] = jnp.where(side == 0, gain_sums[row : row + 1, :depth], gain_sums[row : row + 1, depth:])
    q_gain_out[...] = gain_sums[2:3]
    k_gain_out[...] = gain_sums[3:4]


def finish(gu, qkv, grad_hidden, hidden, down, output, gain_sums, ff, q_width, k_width):
    size = lax.axis_size("ctx")
    depth = gu.shape[1]
    f32 = jnp.float32

    def lines(array):
        return pl.BlockSpec((array.shape[0] // size, array.shape[1]), lambda step: (step, 0))

    def columns(width):
        return pl.BlockSpec((depth, width), lambda step: (0, step))

    def blocks(array):
        return pl.BlockSpec((1,) + array.shape[1:], lambda step: (step, 0, 0))

    def whole(shape):
        return pl.BlockSpec(shape, lambda step: (0, 0))

    widths = (ff, ff, q_width, k_width, k_width)
    kept = (grad_hidden, hidden, down, output)
    return pl.pallas_call(
        finish_kernel,
        grid=(size,),
        out_shape=[jax.ShapeDtypeStruct((depth, size * width), f32) for width in widths]
        + [jax.ShapeDtypeStruct(array.shape, array.dtype) for array in kept]
        + [jax.ShapeDtypeStruct((1, depth), f32)] * 2
        + [jax.ShapeDtypeStruct((1, 128), f32)] * 2,
        in_specs=[blocks(gu), blocks(qkv)] + [lines(array) for array in kept] + [whole(gain_sums.shape)],
        out_specs=[columns(width) for width in widths]
        + [lines(array) for array in kept]
        + [whole((1, depth))] * 2
        + [whole((1, 128))] * 2,
    )(gu, qkv, *kept, gain_sums)


def tp_body(
    hidden_in,
    block_of,
    in_gain,
    w_query,
    w_key,
    w_value,
    w_output,
    q_gain,
    k_gain,
    post_gain,
    w_gate,
    w_up,
    w_down,
    cotangent,
):
    seq_count, tok_rows, model_width = hidden_in.shape
    n_ctx = lax.axis_size("ctx")
    block_rows = tok_rows // 2
    rows = seq_count * tok_rows
    head_dim = q_gain.shape[0]
    hidden = hidden_in.reshape(rows, model_width)
    cot_local = cotangent.reshape(rows, model_width)
    depth = w_query.shape[0]

    tables = rotation_tables(2 * n_ctx, block_rows, head_dim)
    (
        all_small,
        gains,
        log_totals,
        raw,
        queries,
        keys,
        values,
        attn,
        attn_in,
        mine_qkv,
        mine_output,
        mine_gu,
        mine_down,
        grad_out,
    ) = fore(
        block_of,
        in_gain,
        post_gain,
        tables,
        q_gain,
        k_gain,
        hidden,
        w_query,
        w_key,
        w_value,
        w_output,
        w_gate,
        w_up,
        w_down,
        cot_local,
    )
    mine_qkv = mine_qkv.reshape(model_width, -1)
    mine_output = mine_output.reshape(-1, model_width)
    output, post_sum, grad_mid, grad_branch, gu_total, part_down = feed_forward(
        attn, mine_output, hidden, gains, mine_gu.reshape(model_width, -1), mine_down.reshape(-1, model_width), grad_out
    )
    grad_hidden, gain_sums, part_output, gu_sums, qkv_sums = back(
        all_small,
        tables,
        q_gain,
        k_gain,
        raw,
        queries,
        keys,
        values,
        attn,
        log_totals,
        hidden,
        grad_mid,
        gains,
        post_sum,
        gu_total,
        grad_branch,
        mine_output,
        attn_in,
        mine_qkv,
    )
    (
        part_gate,
        part_up,
        part_query,
        part_key,
        part_value,
        grad_hidden,
        output,
        part_down,
        part_output,
        part_in,
        part_post,
        sum_q_gain,
        sum_k_gain,
    ) = finish(
        gu_sums,
        qkv_sums,
        grad_hidden,
        output,
        part_down,
        part_output,
        gain_sums,
        w_gate.shape[1] // n_ctx,
        w_query.shape[1] // n_ctx,
        w_key.shape[1] // n_ctx,
    )
    return (
        output.reshape(seq_count, tok_rows, model_width),
        grad_hidden.reshape(seq_count, tok_rows, model_width),
        part_in.reshape(-1),
        part_query,
        part_key,
        part_value,
        part_output,
        sum_q_gain.reshape(-1),
        sum_k_gain.reshape(-1),
        part_post.reshape(-1),
        part_gate,
        part_up,
        part_down,
    )


def solution(mesh):
    body = tp_body if KV_HEADS % mesh.shape["ctx"] == 0 else gathered_weights_body
    return jax.shard_map(
        body,
        mesh=mesh,
        in_specs=(
            P("fsdp", "ctx", None),
            P("fsdp", "ctx"),
            P(("ctx", "fsdp")),
            P(("ctx", "fsdp"), None),
            P(("ctx", "fsdp"), None),
            P(("ctx", "fsdp"), None),
            P(("ctx", "fsdp"), None),
            P(),
            P(),
            P(("ctx", "fsdp")),
            P(("ctx", "fsdp"), None),
            P(("ctx", "fsdp"), None),
            P(("ctx", "fsdp"), None),
            P("fsdp", "ctx", None),
        ),
        out_specs=(
            P("fsdp", "ctx", None),
            P("fsdp", "ctx", None),
            P(("ctx", "fsdp")),
            P(("ctx", "fsdp"), None),
            P(("ctx", "fsdp"), None),
            P(("ctx", "fsdp"), None),
            P(("ctx", "fsdp"), None),
            P(),
            P(),
            P(("ctx", "fsdp")),
            P(("ctx", "fsdp"), None),
            P(("ctx", "fsdp"), None),
            P(("ctx", "fsdp"), None),
        ),
        check_vma=False,
    )
```

```python
import functools
import math

import jax
import jax.numpy as jnp
import numpy as np
from jax import lax
from jax.experimental import pallas as pl
from jax.experimental.pallas import tpu as pltpu
from jax.sharding import PartitionSpec as P

EPS = 1e-06
THETA = 1000000.0


def rope_tables(positions, width):
    half_width = width // 2
    inverse = THETA ** (-(jnp.arange(half_width, dtype=jnp.float32) * 2.0 / width))
    angles = positions.astype(jnp.float32)[:, None] * inverse[None, :]
    return (jnp.cos(angles), jnp.sin(angles))


def rotate(values, cosine, sine):
    half_width = values.shape[-1] // 2
    first = values[..., :half_width]
    second = values[..., half_width:]
    cos_wide = cosine[:, None, :]
    sin_wide = sine[:, None, :]
    return jnp.concatenate(
        [first * cos_wide - second * sin_wide, second * cos_wide + first * sin_wide], axis=-1
    )


def norm_back(grad_normed, normed, scale):
    return scale * (grad_normed - normed * jnp.mean(grad_normed * normed, axis=-1, keepdims=True))


def gathered_weights_body(
    hidden_in,
    block_of,
    in_gain,
    w_query,
    w_key,
    w_value,
    w_output,
    q_gain,
    k_gain,
    post_gain,
    w_gate,
    w_up,
    w_down,
    cotangent,
):
    seq_count = hidden_in.shape[0]
    tok_rows = hidden_in.shape[1]
    flat_rows = seq_count * tok_rows
    model_width = hidden_in.shape[2]
    block_rows = tok_rows // 2
    block_total = 2 * lax.axis_size("ctx")
    seq_len = block_total * block_rows
    head_dim = q_gain.shape[0]
    q_heads = w_query.shape[1] // head_dim
    kv_heads = w_key.shape[1] // head_dim
    group_size = q_heads // kv_heads
    tile_blocks = math.gcd(block_total, max(1, 512 // block_rows))
    tile_rows = tile_blocks * block_rows
    q_scale = head_dim ** (-0.5)
    contract_rows = (((0,), (0,)), ((), ()))
    contract_cols = (((1,), (1,)), ((), ()))
    offsets = jnp.arange(block_rows, dtype=jnp.int32)
    positions = (block_of[:, :, None] * block_rows + offsets[None, None, :]).reshape(flat_rows)
    cosine, sine = rope_tables(positions, head_dim)
    residual = hidden_in.reshape(flat_rows, model_width).astype(jnp.float32)
    full_in_gain, full_query, full_key, full_value, full_output = (
        lax.all_gather(in_gain, ("ctx", "fsdp"), axis=0, tiled=True),
        lax.all_gather(w_query, ("ctx", "fsdp"), axis=0, tiled=True),
        lax.all_gather(w_key, ("ctx", "fsdp"), axis=0, tiled=True),
        lax.all_gather(w_value, ("ctx", "fsdp"), axis=0, tiled=True),
        lax.all_gather(w_output, ("ctx", "fsdp"), axis=0, tiled=True),
    )
    in_scale = lax.rsqrt(jnp.mean(residual * residual, axis=-1, keepdims=True) + EPS)
    in_normed = residual * in_scale
    attn_in = (in_normed * full_in_gain.astype(jnp.float32)).astype(jnp.bfloat16)
    q_raw = jnp.dot(attn_in, full_query, preferred_element_type=jnp.float32).reshape(
        flat_rows, q_heads, head_dim
    )
    k_raw = jnp.dot(attn_in, full_key, preferred_element_type=jnp.float32).reshape(
        flat_rows, kv_heads, head_dim
    )
    v_local = jnp.dot(attn_in, full_value, preferred_element_type=jnp.float32).astype(jnp.bfloat16)
    q_rms = lax.rsqrt(jnp.mean(q_raw * q_raw, axis=-1, keepdims=True) + EPS)
    q_unit = q_raw * q_rms
    queries = (rotate(q_unit * q_gain.astype(jnp.float32), cosine, sine) * q_scale).astype(
        jnp.bfloat16
    )
    k_rms = lax.rsqrt(jnp.mean(k_raw * k_raw, axis=-1, keepdims=True) + EPS)
    k_unit = k_raw * k_rms
    keys_local = rotate(k_unit * k_gain.astype(jnp.float32), cosine, sine).astype(jnp.bfloat16)
    all_keys, all_values, all_slots = (
        lax.all_gather(
            keys_local.reshape(seq_count, tok_rows, kv_heads * head_dim), "ctx", axis=1, tiled=True
        ),
        lax.all_gather(
            v_local.reshape(seq_count, tok_rows, kv_heads * head_dim), "ctx", axis=1, tiled=True
        ),
        lax.all_gather(block_of, "ctx", axis=1, tiled=True),
    )

    def tile_scores(query_tile, key_tile, query_pos, step):
        scores = jnp.einsum(
            "qhgd,khd->hgqk", query_tile, key_tile, preferred_element_type=jnp.float32
        )
        key_pos = step * tile_rows + jnp.arange(tile_rows, dtype=jnp.int32)
        visible = key_pos[None, :] <= query_pos[:, None]
        return (scores, visible)

    def sequence_tables(seq):
        key_blocks = all_keys[seq].reshape(block_total, block_rows, kv_heads, head_dim)
        value_blocks = all_values[seq].reshape(block_total, block_rows, kv_heads, head_dim)
        block_index = (
            jnp.zeros((block_total,), jnp.int32)
            .at[all_slots[seq]]
            .set(jnp.arange(block_total, dtype=jnp.int32))
        )
        return (key_blocks, value_blocks, block_index)

    def tile_index(block_index, step):
        return lax.dynamic_slice_in_dim(block_index, step * tile_blocks, tile_blocks)

    def fetch(table, block_index, step):
        return jnp.take(table, tile_index(block_index, step), axis=0).reshape(
            tile_rows, kv_heads, head_dim
        )

    log_totals = []
    attn_parts = []
    seq = 0
    key_blocks, value_blocks, block_index = sequence_tables(seq)
    for which in range(2):
        slot = 2 * seq + which
        query_tile = queries[slot * block_rows : (slot + 1) * block_rows].reshape(
            block_rows, kv_heads, group_size, head_dim
        )
        query_pos = positions[slot * block_rows : (slot + 1) * block_rows]
        tile_count = block_of[seq, which] // tile_blocks + 1

        def max_step(step, carry):
            running_max, running_sum = carry
            scores, visible = tile_scores(
                query_tile, fetch(key_blocks, block_index, step), query_pos, step
            )
            scores = jnp.where(visible, scores, -1e30)
            new_max = jnp.maximum(running_max, jnp.max(scores, axis=-1))
            running_sum = running_sum * jnp.exp(running_max - new_max) + jnp.sum(
                jnp.exp(scores - new_max[..., None]), axis=-1
            )
            return (new_max, running_sum)

        start_max = jnp.full((kv_heads, group_size, block_rows), -1e30, jnp.float32)
        start_sum = jnp.zeros((kv_heads, group_size, block_rows), jnp.float32)
        running_max, running_sum = lax.fori_loop(0, tile_count, max_step, (start_max, start_sum))
        log_total = running_max + jnp.log(running_sum)

        def value_step(step, total):
            scores, visible = tile_scores(
                query_tile, fetch(key_blocks, block_index, step), query_pos, step
            )
            probs = jnp.where(visible, jnp.exp(scores - log_total[..., None]), 0.0)
            return total + jnp.einsum(
                "hgqk,khd->qhgd",
                probs.astype(jnp.bfloat16),
                fetch(value_blocks, block_index, step),
                preferred_element_type=jnp.float32,
            )

        attn_part = lax.fori_loop(
            0,
            tile_count,
            value_step,
            jnp.zeros((block_rows, kv_heads, group_size, head_dim), jnp.float32),
        )
        log_totals.append(log_total)
        attn_parts.append(attn_part)
    attn_full = jnp.concatenate(attn_parts, axis=0)
    attn_bf = attn_full.reshape(flat_rows, q_heads * head_dim).astype(jnp.bfloat16)
    branch = jnp.dot(attn_bf, full_output, preferred_element_type=jnp.float32)
    hidden_mid = residual + branch
    full_post, full_gate, full_up, full_down = (
        lax.all_gather(post_gain, ("ctx", "fsdp"), axis=0, tiled=True),
        lax.all_gather(w_gate, ("ctx", "fsdp"), axis=0, tiled=True),
        lax.all_gather(w_up, ("ctx", "fsdp"), axis=0, tiled=True),
        lax.all_gather(w_down, ("ctx", "fsdp"), axis=0, tiled=True),
    )
    post_scale = lax.rsqrt(jnp.mean(hidden_mid * hidden_mid, axis=-1, keepdims=True) + EPS)
    post_normed = hidden_mid * post_scale
    mlp_in = (post_normed * full_post.astype(jnp.float32)).astype(jnp.bfloat16)
    gate_pre = jnp.dot(mlp_in, full_gate, preferred_element_type=jnp.float32)
    up_pre = jnp.dot(mlp_in, full_up, preferred_element_type=jnp.float32)
    sigmoid_gate = jax.nn.sigmoid(gate_pre)
    activated = gate_pre * sigmoid_gate
    inner = (activated * up_pre).astype(jnp.bfloat16)
    mlp_out = jnp.dot(inner, full_down, preferred_element_type=jnp.float32)
    output = (hidden_mid + mlp_out).astype(jnp.bfloat16)
    full_post, full_gate, full_up, full_down = (
        lax.all_gather(post_gain, ("ctx", "fsdp"), axis=0, tiled=True),
        lax.all_gather(w_gate, ("ctx", "fsdp"), axis=0, tiled=True),
        lax.all_gather(w_up, ("ctx", "fsdp"), axis=0, tiled=True),
        lax.all_gather(w_down, ("ctx", "fsdp"), axis=0, tiled=True),
    )
    grad_out = cotangent.reshape(flat_rows, model_width)
    grad_down = lax.dot_general(inner, grad_out, contract_rows, preferred_element_type=jnp.float32)
    part_down = lax.psum_scatter(grad_down, ("ctx", "fsdp"), scatter_dimension=0, tiled=True)
    grad_inner = lax.dot_general(
        grad_out, full_down, contract_cols, preferred_element_type=jnp.float32
    )
    grad_gate_pre = (
        grad_inner * up_pre * sigmoid_gate * (1.0 + gate_pre * (1.0 - sigmoid_gate))
    ).astype(jnp.bfloat16)
    grad_up_pre = (grad_inner * activated).astype(jnp.bfloat16)
    grad_gate = lax.dot_general(
        mlp_in, grad_gate_pre, contract_rows, preferred_element_type=jnp.float32
    )
    grad_up = lax.dot_general(
        mlp_in, grad_up_pre, contract_rows, preferred_element_type=jnp.float32
    )
    grad_mlp_in = lax.dot_general(
        grad_gate_pre, full_gate, contract_cols, preferred_element_type=jnp.float32
    ) + lax.dot_general(grad_up_pre, full_up, contract_cols, preferred_element_type=jnp.float32)
    grad_post_gain = jnp.sum(grad_mlp_in * post_normed, axis=0)
    grad_mid = grad_out.astype(jnp.float32) + norm_back(
        grad_mlp_in * full_post.astype(jnp.float32), post_normed, post_scale
    )
    part_post, part_gate, part_up = (
        lax.psum_scatter(grad_post_gain, ("ctx", "fsdp"), scatter_dimension=0, tiled=True),
        lax.psum_scatter(grad_gate, ("ctx", "fsdp"), scatter_dimension=0, tiled=True),
        lax.psum_scatter(grad_up, ("ctx", "fsdp"), scatter_dimension=0, tiled=True),
    )
    full_in_gain, full_query, full_key, full_value, full_output = (
        lax.all_gather(in_gain, ("ctx", "fsdp"), axis=0, tiled=True),
        lax.all_gather(w_query, ("ctx", "fsdp"), axis=0, tiled=True),
        lax.all_gather(w_key, ("ctx", "fsdp"), axis=0, tiled=True),
        lax.all_gather(w_value, ("ctx", "fsdp"), axis=0, tiled=True),
        lax.all_gather(w_output, ("ctx", "fsdp"), axis=0, tiled=True),
    )
    grad_branch = grad_mid.astype(jnp.bfloat16)
    grad_output = lax.dot_general(
        attn_bf, grad_branch, contract_rows, preferred_element_type=jnp.float32
    )
    grad_attn = lax.dot_general(
        grad_branch, full_output, contract_cols, preferred_element_type=jnp.float32
    ).astype(jnp.bfloat16)
    grad_attn = grad_attn.reshape(flat_rows, kv_heads, group_size, head_dim)
    query_grads = []
    seq = 0
    key_blocks, value_blocks, block_index = sequence_tables(seq)
    key_grads = jnp.zeros((block_total, block_rows, kv_heads, head_dim), jnp.float32)
    value_grads = jnp.zeros((block_total, block_rows, kv_heads, head_dim), jnp.float32)
    for which in range(2):
        slot = 2 * seq + which
        query_tile = queries[slot * block_rows : (slot + 1) * block_rows].reshape(
            block_rows, kv_heads, group_size, head_dim
        )
        query_pos = positions[slot * block_rows : (slot + 1) * block_rows]
        grad_tile = grad_attn[slot * block_rows : (slot + 1) * block_rows]
        tile_count = block_of[seq, which] // tile_blocks + 1
        delta = jnp.einsum("qhgd,qhgd->hgq", grad_tile.astype(jnp.float32), attn_parts[slot])
        log_total = log_totals[slot]

        def grad_step(step, carry):
            grad_query, keys_acc, values_acc = carry
            key_tile = fetch(key_blocks, block_index, step)
            scores, visible = tile_scores(query_tile, key_tile, query_pos, step)
            probs = jnp.where(visible, jnp.exp(scores - log_total[..., None]), 0.0)
            grad_probs = jnp.einsum(
                "qhgd,khd->hgqk",
                grad_tile,
                fetch(value_blocks, block_index, step),
                preferred_element_type=jnp.float32,
            )
            grad_scores = (probs * (grad_probs - delta[..., None])).astype(jnp.bfloat16)
            grad_query = grad_query + jnp.einsum(
                "hgqk,khd->qhgd", grad_scores, key_tile, preferred_element_type=jnp.float32
            )
            key_part = jnp.einsum(
                "hgqk,qhgd->khd", grad_scores, query_tile, preferred_element_type=jnp.float32
            )
            value_part = jnp.einsum(
                "hgqk,qhgd->khd",
                probs.astype(jnp.bfloat16),
                grad_tile,
                preferred_element_type=jnp.float32,
            )
            places = tile_index(block_index, step)
            keys_acc = keys_acc.at[places].add(
                key_part.reshape(tile_blocks, block_rows, kv_heads, head_dim)
            )
            values_acc = values_acc.at[places].add(
                value_part.reshape(tile_blocks, block_rows, kv_heads, head_dim)
            )
            return (grad_query, keys_acc, values_acc)

        start_query = jnp.zeros((block_rows, kv_heads, group_size, head_dim), jnp.float32)
        grad_query, key_grads, value_grads = lax.fori_loop(
            0, tile_count, grad_step, (start_query, key_grads, value_grads)
        )
        query_grads.append(grad_query)
    key_grad_list = [key_grads.reshape(seq_len, kv_heads * head_dim)]
    value_grad_list = [value_grads.reshape(seq_len, kv_heads * head_dim)]
    grad_keys, grad_values = (
        lax.psum_scatter(
            jnp.stack(key_grad_list, axis=0).astype(jnp.bfloat16),
            "ctx",
            scatter_dimension=1,
            tiled=True,
        ).astype(jnp.float32),
        lax.psum_scatter(
            jnp.stack(value_grad_list, axis=0).astype(jnp.bfloat16),
            "ctx",
            scatter_dimension=1,
            tiled=True,
        ).astype(jnp.float32),
    )
    grad_q_rot = (
        jnp.concatenate(query_grads, axis=0).reshape(flat_rows, q_heads, head_dim) * q_scale
    )
    grad_q_normed = rotate(grad_q_rot, cosine, -sine)
    grad_q_gain = jnp.sum(grad_q_normed * q_unit, axis=(0, 1))
    grad_q_raw = (
        norm_back(grad_q_normed * q_gain.astype(jnp.float32), q_unit, q_rms)
        .astype(jnp.bfloat16)
        .reshape(flat_rows, q_heads * head_dim)
    )
    grad_k_normed = rotate(grad_keys.reshape(flat_rows, kv_heads, head_dim), cosine, -sine)
    grad_k_gain = jnp.sum(grad_k_normed * k_unit, axis=(0, 1))
    grad_k_raw = (
        norm_back(grad_k_normed * k_gain.astype(jnp.float32), k_unit, k_rms)
        .astype(jnp.bfloat16)
        .reshape(flat_rows, kv_heads * head_dim)
    )
    grad_v_local = grad_values.reshape(flat_rows, kv_heads * head_dim).astype(jnp.bfloat16)
    grad_query_w = lax.dot_general(
        attn_in, grad_q_raw, contract_rows, preferred_element_type=jnp.float32
    )
    grad_key_w = lax.dot_general(
        attn_in, grad_k_raw, contract_rows, preferred_element_type=jnp.float32
    )
    grad_value_w = lax.dot_general(
        attn_in, grad_v_local, contract_rows, preferred_element_type=jnp.float32
    )
    grad_attn_in = lax.dot_general(
        grad_q_raw, full_query, contract_cols, preferred_element_type=jnp.float32
    )
    grad_attn_in = grad_attn_in + lax.dot_general(
        grad_k_raw, full_key, contract_cols, preferred_element_type=jnp.float32
    )
    grad_attn_in = grad_attn_in + lax.dot_general(
        grad_v_local, full_value, contract_cols, preferred_element_type=jnp.float32
    )
    grad_in_gain = jnp.sum(grad_attn_in * in_normed, axis=0)
    grad_input = grad_mid + norm_back(
        grad_attn_in * full_in_gain.astype(jnp.float32), in_normed, in_scale
    )
    part_in, part_query, part_key, part_value, part_output = (
        lax.psum_scatter(grad_in_gain, ("ctx", "fsdp"), scatter_dimension=0, tiled=True),
        lax.psum_scatter(grad_query_w, ("ctx", "fsdp"), scatter_dimension=0, tiled=True),
        lax.psum_scatter(grad_key_w, ("ctx", "fsdp"), scatter_dimension=0, tiled=True),
        lax.psum_scatter(grad_value_w, ("ctx", "fsdp"), scatter_dimension=0, tiled=True),
        lax.psum_scatter(grad_output, ("ctx", "fsdp"), scatter_dimension=0, tiled=True),
    )
    sum_q_gain, sum_k_gain = lax.psum((grad_q_gain, grad_k_gain), ("ctx", "fsdp"))
    return (
        output.reshape(seq_count, tok_rows, model_width),
        grad_input.reshape(seq_count, tok_rows, model_width),
        part_in,
        part_query,
        part_key,
        part_value,
        part_output,
        sum_q_gain,
        sum_k_gain,
        part_post,
        part_gate,
        part_up,
        part_down,
    )


MESH = pl.DeviceIdType.MESH
SUBS = 2


def ring_position(index, size):
    column, line = lax.rem(index, 2), lax.div(index, 2)
    return column * (line + 1) + (1 - column) * lax.rem(size - line, size)


def ring_member(position, size):
    late = lax.div(position + size // 2 - 1, size)
    beyond = lax.div(position + size - 1, size)
    return beyond * (1 - late) * (2 * position - 1) + late * 2 * (size - position)


class Ring:
    def __init__(self, size):
        self.size = size
        self.me = lax.axis_index("ctx")
        self.row = lax.axis_index("fsdp")
        self.position = ring_position(self.me, size)

    def member(self, way, steps):
        ahead = self.size - steps if way == 0 else steps
        return ring_member(lax.rem(self.position + ahead, self.size), self.size)

    def target(self, way):
        return (self.member(way, self.size - 1), self.row)

    def barrier(self):
        barrier = pltpu.get_barrier_semaphore()
        for way in range(2):
            pl.semaphore_signal(barrier, inc=1, device_id=self.target(way), device_id_type=MESH)
        pl.semaphore_wait(barrier, 2)


class GatherRing:
    def __init__(self, ring, own, out, send_sems, recv_sems):
        self.ring, self.own, self.out, self.send_sems, self.recv_sems = ring, own, out, send_sems, recv_sems
        self.half = own.shape[0] // 2
        self.sub = self.half // SUBS

    def copy(self, way, step, part, first=False):
        place = pl.ds(way * self.half + part * self.sub, self.sub)
        owner = self.ring.me if first else self.ring.member(way, step)
        source = self.own.at[place] if first else self.out.at[owner, place]
        return pltpu.make_async_remote_copy(
            src_ref=source,
            dst_ref=self.out.at[owner, place],
            send_sem=self.send_sems.at[way, step, part],
            recv_sem=self.recv_sems.at[way, step, part],
            device_id=self.ring.target(way),
            device_id_type=MESH,
        )

    def start(self, way, part):
        self.copy(way, 0, part, first=True).start()

    def step(self, step):
        for part in range(SUBS):
            for way in range(2):
                self.copy(way, step - 1, part).wait_recv()
                self.copy(way, step, part).start()

    def finish(self):
        last = self.ring.size - 2
        for part in range(SUBS):
            for way in range(2):
                self.copy(way, last, part).wait_recv()

        @pl.loop(0, last + 1)
        def _(step):
            for part in range(SUBS):
                for way in range(2):
                    self.copy(way, step, part).wait_send()

    def run(self):
        for way in range(2):
            self.start(way)

        @pl.loop(1, self.ring.size - 1)
        def _(step):
            self.step(step)

        self.finish()


def gather_sems(size):
    return [pltpu.SemaphoreType.DMA((2, size - 1, SUBS)), pltpu.SemaphoreType.DMA((2, size - 1, SUBS))]


class SumRing:
    def __init__(self, ring, compute, terms, outgoing, incoming, send_sems, recv_sems):
        self.ring, self.compute, self.terms = ring, compute, terms
        self.outgoing, self.incoming, self.send_sems, self.recv_sems = outgoing, incoming, send_sems, recv_sems
        self.half = terms.shape[1]
        self.sub = self.half // SUBS

    def copy(self, way, step, part):
        place = pl.ds(part * self.sub, self.sub)
        return pltpu.make_async_remote_copy(
            src_ref=self.outgoing.at[way, lax.rem(step, 2), place],
            dst_ref=self.incoming.at[way, step, place],
            send_sem=self.send_sems.at[way, step, part],
            recv_sem=self.recv_sems.at[way, step, part],
            device_id=self.ring.target(way),
            device_id_type=MESH,
        )

    def terms_of(self, step):
        self.compute([self.ring.member(way, step + 1) for way in range(2)])

    def begin(self):
        self.terms_of(0)
        for part in range(SUBS):
            place = pl.ds(part * self.sub, self.sub)
            for way in range(2):
                self.outgoing[way, 0, place] = self.terms[way, place].astype(jnp.bfloat16)
                self.copy(way, 0, part).start()

    def second(self):
        self.step(1, fresh=True)

    def step(self, step, fresh=False):
        self.terms_of(step)
        for part in range(SUBS):
            place = pl.ds(part * self.sub, self.sub)
            for way in range(2):
                self.copy(way, step - 1, part).wait_recv()
                total = self.terms[way, place] + self.incoming[way, step - 1, place].astype(jnp.float32)
                if not fresh:
                    self.copy(way, step - 2, part).wait_send()
                self.outgoing[way, lax.rem(step, 2), place] = total.astype(jnp.bfloat16)
                self.copy(way, step, part).start()

    def last_terms(self):
        self.compute([self.ring.me, self.ring.me])

    def result(self, way, part):
        last = self.ring.size - 2
        place = pl.ds(part * self.sub, self.sub)
        self.copy(way, last, part).wait_recv()
        return self.terms[way, place] + self.incoming[way, last, place].astype(jnp.float32)

    def parts(self):
        for part in range(SUBS):
            for way in range(2):
                start = way * self.half + part * self.sub
                yield way, part, slice(start, start + self.sub)

    def finish(self):
        for step in (self.ring.size - 3, self.ring.size - 2):
            for part in range(SUBS):
                for way in range(2):
                    self.copy(way, step, part).wait_send()

    def run(self):
        self.begin()
        self.second()

        @pl.loop(2, self.ring.size - 1)
        def _(step):
            self.step(step)

        self.last_terms()


def sum_scratch(size, rows, width):
    half = rows // 2
    return [
        pltpu.VMEM((2, half, width), jnp.float32),
        pltpu.VMEM((2, 2, half, width), jnp.bfloat16),
        pltpu.VMEM((2, size - 1, half, width), jnp.bfloat16),
        pltpu.SemaphoreType.DMA((2, size - 1, SUBS)),
        pltpu.SemaphoreType.DMA((2, size - 1, SUBS)),
    ]


class Square:
    def __init__(self, size):
        self.size = size
        self.me = lax.axis_index("ctx")
        self.row = lax.axis_index("fsdp")
        line, column = lax.div(self.me, 2), lax.rem(self.me, 2)
        half = lax.div(line, 2)
        self.inner = lax.rem(lax.div(line + 1, 2), 2) == 1
        self.outer = lax.rem(lax.div(line + 1, 2), 2) == 0
        self.beside = self.me + 1 - 2 * column
        self.along = self.me + 2 - 4 * lax.rem(line, 2)
        self.across = (3 - line) * 2 + column
        self.diagonal = self.along + 1 - 2 * column
        self.near = (2 - half) * 2 + column
        self.far = 6 * (1 - half) + column
        self.beside_near = (2 - half) * 2 + 1 - column
        self.beside_far = 6 * (1 - half) + 1 - column

    def targets(self):
        return [(member, self.row) for member in (self.beside, self.along, self.across)]


class SquareGather:
    def __init__(self, square, own, out, send_sems, recv_sems):
        self.square, self.own, self.out, self.send_sems, self.recv_sems = square, own, out, send_sems, recv_sems
        self.half = own.shape[0] // 2
        self.sub = self.half // SUBS
        me, rest = square.me, [(square.near, 0), (square.near, 1), (square.far, 0), (square.far, 1)]
        self.sent = [
            [(me, 0), (me, 1), (square.along, 1)] + rest,
            [(me, 0), (me, 1), (square.beside, 0)] + rest,
            [(me, 0), (me, 1), (square.along, 0), (square.along, 1)],
        ]

    def copy(self, link, slot, part):
        member, half = self.sent[link][slot]
        place = pl.ds(half * self.half + part * self.sub, self.sub)
        source = self.own.at[place] if slot < 2 else self.out.at[member, place]
        return remote(
            source,
            self.out.at[member, place],
            self.send_sems.at[link, slot, part],
            self.recv_sems.at[link, slot, part],
            self.square.targets()[link],
        )

    def start(self, half, part):
        for link in range(2):
            self.copy(link, half, part).start()

        @pl.when(self.square.inner)
        def _():
            self.copy(2, half, part).start()

    def relay(self, link, slot, *onward):
        for part in range(SUBS):
            self.copy(link, slot, part).wait_recv()
            for next_link, next_slot in onward:
                self.copy(next_link, next_slot, part).start()

    def first(self):
        @pl.when(self.square.outer)
        def _():
            self.relay(0, 0, (1, 2))
            self.relay(1, 1, (0, 2))

        @pl.when(self.square.inner)
        def _():
            self.relay(1, 0, (2, 2))
            self.relay(2, 0, (1, 3))
            self.relay(1, 1, (2, 3), (0, 2))
            for part in range(SUBS):
                self.copy(0, 3, part).start()

    def second(self):
        @pl.when(self.square.outer)
        def _():
            self.relay(1, 3, (0, 3))
            self.relay(1, 4, (0, 4))

        @pl.when(self.square.inner)
        def _():
            self.relay(2, 1, (1, 4), (0, 4))

    def third(self):
        @pl.when(self.square.outer)
        def _():
            self.relay(1, 5, (0, 5))
            self.relay(1, 6, (0, 6))

        @pl.when(self.square.inner)
        def _():
            self.relay(2, 2, (1, 5), (0, 5))
            self.relay(2, 3, (1, 6), (0, 6))
            self.relay(0, 0, (1, 2))

    def finish(self):
        for slot in range(1, 7):
            self.relay(0, slot)
        self.relay(1, 2)

        @pl.when(self.square.outer)
        def _():
            self.relay(1, 0)

        for part in range(SUBS):
            for slot in range(7):
                self.copy(0, slot, part).wait_send()
            for slot in range(3):
                self.copy(1, slot, part).wait_send()

        @pl.when(self.square.inner)
        def _():
            for part in range(SUBS):
                for slot in range(3, 7):
                    self.copy(1, slot, part).wait_send()
                for slot in range(4):
                    self.copy(2, slot, part).wait_send()


def square_sems():
    return [pltpu.SemaphoreType.DMA((3, 7, SUBS)), pltpu.SemaphoreType.DMA((3, 7, SUBS))]


class SquareSum:
    def __init__(self, square, compute, terms, outgoing, incoming, send_sems, recv_sems):
        self.square, self.compute, self.terms = square, compute, terms
        self.outgoing, self.incoming, self.send_sems, self.recv_sems = outgoing, incoming, send_sems, recv_sems
        self.half = outgoing.shape[1]
        self.sub = self.half // SUBS
        self.first_slot = (0, 7, 14)

    def copy(self, link, slot, part):
        at = self.first_slot[link] + slot
        place = pl.ds(part * self.sub, self.sub)
        return remote(
            self.outgoing.at[at, place],
            self.incoming.at[at, place],
            self.send_sems.at[link, slot, part],
            self.recv_sems.at[link, slot, part],
            self.square.targets()[link],
        )

    def arrived(self, link, slot, part):
        self.copy(link, slot, part).wait_recv()
        at = self.first_slot[link] + slot
        return self.incoming[at, part * self.sub : (part + 1) * self.sub].astype(jnp.float32)

    def term(self, which, half, part):
        start = half * self.half + part * self.sub
        return self.terms[which, start : start + self.sub]

    def send(self, link, slot, which, half, *received):
        at = self.first_slot[link] + slot
        for part in range(SUBS):
            total = self.term(which, half, part)
            for source in received:
                total = total + self.arrived(*source, part)
            self.outgoing[at, part * self.sub : (part + 1) * self.sub] = total.astype(jnp.bfloat16)
            self.copy(link, slot, part).start()

    def begin(self):
        square = self.square
        self.compute(square.beside_far, 0)
        self.send(0, 0, 0, 0)
        self.send(0, 1, 0, 1)
        self.compute(square.beside_near, 1)
        self.send(0, 2, 1, 0)
        self.send(0, 3, 1, 1)
        self.compute(square.diagonal, 2)
        self.send(1, 0, 2, 0)
        self.send(0, 4, 2, 1)
        self.compute(square.far, 0)
        self.compute(square.near, 1)

    def first(self):
        @pl.when(self.square.outer)
        def _():
            self.send(1, 1, 0, 0, (0, 0))
            self.send(1, 2, 0, 1, (0, 1))

        @pl.when(self.square.inner)
        def _():
            self.send(2, 0, 0, 0, (0, 0), (1, 1))

        self.compute(self.square.beside, 3)
        self.send(0, 6, 3, 1)
        self.send(0, 5, 3, 0, (1, 0))
        self.compute(self.square.along, 2)

    def second(self):
        @pl.when(self.square.outer)
        def _():
            self.send(1, 3, 1, 0, (0, 2))
            self.send(1, 4, 1, 1, (0, 3))
            self.send(1, 5, 2, 0)

        @pl.when(self.square.inner)
        def _():
            self.send(2, 1, 0, 1, (0, 1), (1, 2))
            self.send(1, 5, 2, 0, (2, 0))
            self.send(2, 2, 1, 0, (0, 2), (1, 3))

        self.compute(self.square.me, 4)

    def third(self):
        @pl.when(self.square.outer)
        def _():
            self.send(1, 6, 2, 1, (0, 4))

        @pl.when(self.square.inner)
        def _():
            self.send(2, 3, 1, 1, (0, 3), (1, 4))
            self.send(1, 6, 2, 1, (0, 4), (2, 1))
            for half in range(2):
                for part in range(SUBS):
                    start = half * self.half + part * self.sub
                    self.terms[4, start : start + self.sub] = self.term(4, half, part) + self.arrived(2, 2 + half, part)

    def parts(self):
        for half in range(2):
            for part in range(SUBS):
                start = half * self.half + part * self.sub
                yield half, part, slice(start, start + self.sub)

    def result(self, half, part):
        return self.term(4, half, part) + self.arrived(0, 5 + half, part) + self.arrived(1, 5 + half, part)

    def finish(self):
        for part in range(SUBS):
            for slot in range(7):
                self.copy(0, slot, part).wait_send()
            for slot in (0, 5, 6):
                self.copy(1, slot, part).wait_send()

        @pl.when(self.square.outer)
        def _():
            for part in range(SUBS):
                for slot in range(1, 5):
                    self.copy(1, slot, part).wait_send()

        @pl.when(self.square.inner)
        def _():
            for part in range(SUBS):
                for slot in range(4):
                    self.copy(2, slot, part).wait_send()


def square_sum_scratch(rows, width):
    return [
        pltpu.VMEM((5, rows, width), jnp.float32),
        pltpu.VMEM((18, rows // 2, width), jnp.bfloat16),
        pltpu.VMEM((18, rows // 2, width), jnp.bfloat16),
    ] + square_sems()


def block_terms_t(left, weight, terms):
    def compute(member, which):
        @pl.loop(0, weight.shape[0] // TILE)
        def _(tile):
            columns = pl.ds(pl.multiple_of(tile * TILE, TILE), TILE)
            terms[which, :, columns] = lax.dot_general(
                left[member], weight[columns, :], (((1,), (1,)), ((), ())), preferred_element_type=jnp.float32
            )

    return compute


TILE = 512


def row_terms(left, weight, terms):
    half = terms.shape[1]

    def compute(members):
        lines = jnp.concatenate([left[members[way], way * half : (way + 1) * half] for way in range(2)], axis=0)

        @pl.loop(0, weight.shape[1] // TILE)
        def _(tile):
            columns = pl.ds(pl.multiple_of(tile * TILE, TILE), TILE)
            product = jnp.dot(lines, weight[:, columns], preferred_element_type=jnp.float32)
            for way in range(2):
                terms[way, :, columns] = product[way * half : (way + 1) * half]

    return compute


def row_terms_t(left, weight, terms):
    half = terms.shape[1]

    def compute(members):
        lines = jnp.concatenate([left[members[way], way * half : (way + 1) * half] for way in range(2)], axis=0)

        @pl.loop(0, weight.shape[0] // TILE)
        def _(tile):
            columns = pl.ds(pl.multiple_of(tile * TILE, TILE), TILE)
            product = lax.dot_general(
                lines, weight[columns, :], (((1,), (1,)), ((), ())), preferred_element_type=jnp.float32
            )
            for way in range(2):
                terms[way, :, columns] = product[way * half : (way + 1) * half]

    return compute


VMEM_SPEC = pl.BlockSpec(memory_space=pltpu.VMEM)
ANY_SPEC = pl.BlockSpec(memory_space=pl.ANY)


def ctx_peer(ring, ahead):
    return lax.rem(ring.me + ahead, ring.size)


def across(row, n_fsdp):
    return lax.rem(row + n_fsdp // 2, n_fsdp)


def beside(row):
    return row + 1 - 2 * lax.rem(row, 2)


def remote(source, target, send_sem, recv_sem, device):
    return pltpu.make_async_remote_copy(
        src_ref=source,
        dst_ref=target,
        send_sem=send_sem,
        recv_sem=recv_sem,
        device_id=device,
        device_id_type=MESH,
    )


def greet(devices):
    barrier = pltpu.get_barrier_semaphore()
    for device in devices:
        pl.semaphore_signal(barrier, inc=1, device_id=device, device_id_type=MESH)
    pl.semaphore_wait(barrier, len(devices))


def near_devices(ring, n_fsdp):
    return [(ctx_peer(ring, ahead), ring.row) for ahead in range(1, ring.size)] + [
        (ring.me, lax.rem(ring.row + ahead, n_fsdp)) for ahead in range(1, n_fsdp)
    ]


class Spread:
    def __init__(self, ring, n_fsdp, block, out, send_sems, recv_sems):
        self.ring, self.n_fsdp, self.block, self.out = ring, n_fsdp, block, out
        self.send_sems, self.recv_sems = send_sems, recv_sems

    def along_ctx(self, ahead):
        return remote(
            self.block,
            self.out.at[self.ring.row, self.ring.me],
            self.send_sems.at[ahead],
            self.recv_sems.at[ahead],
            (ctx_peer(self.ring, ahead), self.ring.row),
        )

    def along_fsdp(self, ahead):
        line = self.out.at[self.ring.row]
        sem = self.ring.size + ahead
        row = lax.rem(self.ring.row + ahead, self.n_fsdp)
        return remote(line, line, self.send_sems.at[sem], self.recv_sems.at[sem], (self.ring.me, row))

    def begin(self):
        for ahead in range(1, self.ring.size):
            self.along_ctx(ahead).start()
        self.out[self.ring.row, self.ring.me] = self.block[...]

    def collect(self):
        for ahead in range(1, self.ring.size):
            self.along_ctx(ahead).wait_recv()
        for ahead in range(1, self.n_fsdp):
            self.along_fsdp(ahead).start()
        for ahead in range(1, self.n_fsdp):
            self.along_fsdp(ahead).wait_recv()

    def finish(self):
        for ahead in range(1, self.ring.size):
            self.along_ctx(ahead).wait_send()
        for ahead in range(1, self.n_fsdp):
            self.along_fsdp(ahead).wait_send()


class SmallSum:
    def __init__(self, ring, n_fsdp, blocks, by_ctx, part, by_fsdp, send_sems, recv_sems):
        self.ring, self.n_fsdp, self.blocks, self.by_ctx, self.part, self.by_fsdp = (
            ring,
            n_fsdp,
            blocks,
            by_ctx,
            part,
            by_fsdp,
        )
        self.send_sems, self.recv_sems = send_sems, recv_sems

    def along_ctx(self, ahead):
        member = ctx_peer(self.ring, ahead)
        return remote(
            self.blocks.at[member],
            self.by_ctx.at[self.ring.me],
            self.send_sems.at[ahead],
            self.recv_sems.at[ahead],
            (member, self.ring.row),
        )

    def along_fsdp(self, ahead):
        row = lax.rem(self.ring.row + ahead, self.n_fsdp)
        sem = self.ring.size + ahead
        return remote(
            self.part.at[lax.div(row, 2)],
            self.by_fsdp.at[self.ring.row],
            self.send_sems.at[sem],
            self.recv_sems.at[sem],
            (self.ring.me, row),
        )

    def begin(self):
        for ahead in range(1, self.ring.size):
            self.along_ctx(ahead).start()
        self.by_ctx[self.ring.me] = self.blocks[self.ring.me]

    def cross(self):
        for ahead in range(1, self.ring.size):
            self.along_ctx(ahead).wait_recv()
        self.part[...] = jnp.sum(self.by_ctx[...], axis=0)
        for ahead in range(1, self.n_fsdp):
            self.along_fsdp(ahead).start()
        self.by_fsdp[self.ring.row] = self.part[lax.div(self.ring.row, 2)]

    def result(self):
        for ahead in range(1, self.n_fsdp):
            self.along_fsdp(ahead).wait_recv()
        return jnp.sum(self.by_fsdp[...], axis=0)

    def finish(self):
        for ahead in range(1, self.ring.size):
            self.along_ctx(ahead).wait_send()
        for ahead in range(1, self.n_fsdp):
            self.along_fsdp(ahead).wait_send()


def small_sems(size, n_fsdp):
    return [pltpu.SemaphoreType.DMA((size + n_fsdp,)), pltpu.SemaphoreType.DMA((size + n_fsdp,))]


class Rows:
    def __init__(self, ring, n_fsdp, shard, out, send_sems, recv_sems):
        own, far, twin = ring.row, across(ring.row, n_fsdp), beside(ring.row)
        self.keep = pltpu.make_async_copy(shard, out.at[own], send_sems.at[3])
        self.to_far = remote(shard, out.at[own], send_sems.at[0], recv_sems.at[0], (ring.me, far))
        self.to_twin = remote(shard, out.at[own], send_sems.at[1], recv_sems.at[1], (ring.me, twin))
        self.pass_on = remote(out.at[far], out.at[far], send_sems.at[2], recv_sems.at[2], (ring.me, twin))

    def begin(self):
        self.keep.start()
        self.to_far.start()
        self.to_twin.start()

    def relay(self):
        self.to_far.wait_recv()
        self.pass_on.start()

    def finish(self):
        self.keep.wait()
        self.to_far.wait_send()
        self.to_twin.wait()
        self.pass_on.wait()


def rows_sems():
    return [pltpu.SemaphoreType.DMA((4,)), pltpu.SemaphoreType.DMA((3,))]


class Columns:
    def __init__(self, ring, n_fsdp, shard, out, start, send_sems, recv_sems):
        self.ring, self.shard, self.out, self.send_sems, self.recv_sems = ring, shard, out, send_sems, recv_sems
        self.width = shard.shape[1] // ring.size
        self.place = pl.ds(start, self.width)
        far, twin = across(ring.row, n_fsdp), beside(ring.row)
        self.to_far = self.link(0, ring.row, far)
        self.to_twin = self.link(1, ring.row, twin)
        self.pass_on = self.link(2, far, twin)

    def link(self, which, row, target):
        block = self.out.at[:, row, :, self.place]
        sem = self.ring.size + which
        return remote(block, block, self.send_sems.at[sem], self.recv_sems.at[sem], (self.ring.me, target))

    def piece(self, ahead):
        member = ctx_peer(self.ring, ahead)
        source = self.shard.at[:, pl.ds(pl.multiple_of(member * self.width, self.width), self.width)]
        target = self.out.at[self.ring.me, self.ring.row, :, self.place]
        if ahead == 0:
            return pltpu.make_async_copy(source, target, self.send_sems.at[0])
        return remote(source, target, self.send_sems.at[ahead], self.recv_sems.at[ahead], (member, self.ring.row))

    def begin(self):
        for ahead in range(self.ring.size):
            self.piece(ahead).start()

    def spread(self):
        self.piece(0).wait()
        for ahead in range(1, self.ring.size):
            self.piece(ahead).wait_recv()
        self.to_far.start()
        self.to_twin.start()

    def relay(self):
        self.to_far.wait_recv()
        self.pass_on.start()

    def arrive(self):
        self.to_twin.wait_recv()
        self.pass_on.wait_recv()

    def finish(self):
        for ahead in range(1, self.ring.size):
            self.piece(ahead).wait_send()
        self.to_far.wait_send()
        self.to_twin.wait_send()
        self.pass_on.wait_send()


def columns_sems(size):
    return [pltpu.SemaphoreType.DMA((size + 3,)), pltpu.SemaphoreType.DMA((size + 3,))]


class RowGrads:
    def __init__(self, ring, n_fsdp, part, from_twin, to_far, from_far, send_sems, recv_sems):
        own, far, twin = ring.row, across(ring.row, n_fsdp), beside(ring.row)
        self.part, self.from_twin, self.to_far, self.from_far = part, from_twin, to_far, from_far
        self.own, self.far = own, far
        twin_far = across(twin, n_fsdp)
        self.first = [
            remote(part.at[twin], from_twin.at[0], send_sems.at[0], recv_sems.at[0], (ring.me, twin)),
            remote(part.at[twin_far], from_twin.at[1], send_sems.at[1], recv_sems.at[1], (ring.me, twin)),
        ]
        if to_far is None:
            self.to_far = part.at[far]
        self.second = remote(self.to_far, from_far, send_sems.at[2], recv_sems.at[2], (ring.me, far))

    def begin(self):
        self.first[1].start()
        self.first[0].start()

    def cross(self):
        self.first[1].wait_recv()
        self.to_far[...] = (
            self.part[self.far].astype(jnp.float32) + self.from_twin[1].astype(jnp.float32)
        ).astype(jnp.bfloat16)
        self.second.start()

    def result(self):
        self.first[0].wait_recv()
        self.second.wait_recv()
        return (
            self.part[self.own].astype(jnp.float32)
            + self.from_twin[0].astype(jnp.float32)
            + self.from_far[...].astype(jnp.float32)
        )

    def finish(self):
        for copy in self.first + [self.second]:
            copy.wait_send()


def row_grads_sems():
    return [pltpu.SemaphoreType.DMA((3,)), pltpu.SemaphoreType.DMA((3,))]


def row_grads_scratch(shape):
    return [
        pltpu.VMEM((2,) + shape, jnp.bfloat16),
        pltpu.VMEM(shape, jnp.bfloat16),
        pltpu.VMEM(shape, jnp.bfloat16),
    ] + row_grads_sems()


class Deal:
    def __init__(self, ring, total, arrived, send_sems, recv_sems):
        self.ring, self.total, self.arrived = ring, total, arrived
        self.send_sems, self.recv_sems = send_sems, recv_sems

    def piece(self, ahead):
        member = ctx_peer(self.ring, ahead)
        source, target = self.total.at[member], self.arrived.at[self.ring.me]
        if ahead == 0:
            return pltpu.make_async_copy(source, target, self.send_sems.at[0])
        return remote(source, target, self.send_sems.at[ahead], self.recv_sems.at[ahead], (member, self.ring.row))

    def begin(self):
        for ahead in range(self.ring.size):
            self.piece(ahead).start()

    def finish(self):
        for ahead in range(self.ring.size):
            self.piece(ahead).wait()


def deal_sems(size):
    return [pltpu.SemaphoreType.DMA((size,)), pltpu.SemaphoreType.DMA((size,))]


def params(collective_id):
    return pltpu.CompilerParams(
        collective_id=collective_id, has_side_effects=True, vmem_limit_bytes=62 * 1024 * 1024
    )


def head_norm(raw):
    return lax.rsqrt(jnp.mean(raw * raw, axis=-1, keepdims=True) + EPS)


def turn(values, cosine, sine):
    return values * cosine + pltpu.roll(values, values.shape[-1] // 2, 1) * sine


class Places:
    def __init__(self, ring, n_fsdp, all_small, starts, offsets, cosine, sine, places):
        self.ring, self.n_fsdp, self.all_small = ring, n_fsdp, all_small
        self.starts, self.offsets, self.cosine, self.sine, self.places = starts, offsets, cosine, sine, places
        self.block_rows = offsets.shape[1]

    def block(self, member, which):
        return self.all_small[self.ring.row, member, 2:3, which : which + 1]

    def fill(self):
        count = self.starts.shape[1]
        numbers = lax.broadcasted_iota(jnp.int32, (count, 1), 0).astype(jnp.float32)
        offset = lax.broadcasted_iota(jnp.int32, (self.block_rows, self.places.shape[1]), 0).astype(jnp.float32)
        for slot in range(count):
            block = self.block(slot // 2, slot % 2)
            chosen = (numbers == block).astype(jnp.float32)
            cos_start = jnp.sum(chosen * self.starts[0], axis=0, keepdims=True)
            sin_start = jnp.sum(chosen * self.starts[1], axis=0, keepdims=True)
            at = slice(slot * self.block_rows, (slot + 1) * self.block_rows)
            self.cosine[at] = cos_start * self.offsets[0] - sin_start * self.offsets[1]
            self.sine[at] = sin_start * self.offsets[0] + cos_start * self.offsets[1]
            self.places[at] = offset + block * self.block_rows

    def visible(self, member):
        width = self.places.shape[1]
        lane = lax.broadcasted_iota(jnp.int32, (1, width), 1).astype(jnp.float32)
        rows = float(self.block_rows)
        query = lane + jnp.where(lane < rows, self.block(member, 0) * rows, self.block(member, 1) * rows - rows)
        return self.places[...] <= query


def rotation_tables(blocks, block_rows, head):
    inverse = (THETA ** (-(np.arange(head // 2, dtype=np.float32) * np.float32(2.0) / head))).astype(np.float64)

    def both(at):
        angles = at.astype(np.float64)[:, None] * inverse[None, :]
        cosine, sine = np.cos(angles), np.sin(angles)
        return jnp.asarray(
            np.stack(
                [np.concatenate([cosine, cosine], axis=1), np.concatenate([-sine, sine], axis=1)], axis=0
            ).astype(np.float32)
        )

    return both(np.arange(blocks) * block_rows), both(np.arange(block_rows))


def fore_kernel(
    size,
    n_fsdp,
    q_heads,
    blocks,
    in_gain,
    post_gain,
    starts,
    offsets,
    q_gain,
    k_gain,
    hidden,
    w_query,
    w_key,
    w_value,
    w_output,
    w_gate,
    w_up,
    w_down,
    cotangent,
    all_small,
    gains,
    log_totals,
    raw_out,
    queries_out,
    keys_out,
    values_out,
    attn_out,
    attn_in_out,
    w_qkv_out,
    output_out,
    gu_out,
    down_out,
    grad_out,
    small,
    own,
    attn_in,
    w_qkv,
    cosine,
    sine,
    places_ref,
    values_t,
    raw,
    queries,
    keys,
    values,
    attn,
    small_send,
    small_recv,
    local_sems,
    *scratch,
):
    ring = Ring(size)
    head = q_gain.shape[1]
    tokens = hidden.shape[0]
    depth = in_gain.shape[1]
    q_width = q_heads * head
    k_width = w_key.shape[1] // size
    ff = w_gate.shape[1] // size
    columns_q = Columns(ring, n_fsdp, w_query, w_qkv, 0, *scratch[0:2])
    columns_k = Columns(ring, n_fsdp, w_key, w_qkv, q_width, *scratch[2:4])
    columns_v = Columns(ring, n_fsdp, w_value, w_qkv, q_width + k_width, *scratch[4:6])
    columns_gate = Columns(ring, n_fsdp, w_gate, gu_out, 0, *scratch[6:8])
    columns_up = Columns(ring, n_fsdp, w_up, gu_out, ff, *scratch[8:10])
    rows_output = Rows(ring, n_fsdp, w_output, output_out, *scratch[10:12])
    rows_down = Rows(ring, n_fsdp, w_down, down_out, *scratch[12:14])
    square = Square(size)
    gathering = SquareGather(square, own, attn_in, *scratch[14:16])
    gathering_cot = SquareGather(square, cotangent, grad_out, *scratch[16:18])
    places = Places(ring, n_fsdp, all_small, starts, offsets, cosine, sine, places_ref)

    side = lax.rem(ring.row, 2)
    lane = lax.broadcasted_iota(jnp.int32, (1, 2 * depth), 1)
    mine = lax.div(lane, depth) == side
    small[...] = jnp.zeros_like(small)
    for row, part in enumerate((in_gain, post_gain)):
        part_row = part[...].astype(jnp.float32)
        small[row : row + 1] = jnp.where(mine, jnp.concatenate([part_row, part_row], axis=1), 0.0)
    small[2:3] = jnp.where(lane == 0, blocks[0, 0], jnp.where(lane == 1, blocks[0, 1], 0)).astype(jnp.float32)
    greet(near_devices(ring, n_fsdp))
    sharing = Spread(ring, n_fsdp, small, all_small, small_send, small_recv)
    sharing.begin()
    for columns in (columns_q, columns_k, columns_v):
        columns.begin()
    half = tokens // 2
    sharing.collect()
    for pair in range(size * n_fsdp // 2):
        member, chip = pair // (n_fsdp // 2), pair % (n_fsdp // 2)
        gains[:, pair * 128 : (pair + 1) * 128] = all_small[2 * chip, member] + all_small[2 * chip + 1, member]
    for part in range(SUBS):
        for way in range(2):
            start = way * half + part * (half // SUBS)
            place = slice(start, start + half // SUBS)
            rows = hidden[place].astype(jnp.float32)
            scale = lax.rsqrt(jnp.mean(rows * rows, axis=-1, keepdims=True) + EPS)
            own[place] = (rows * scale * gains[0:1]).astype(jnp.bfloat16)
            gathering.start(way, part)
    rows_output.begin()
    rows_down.begin()
    keep = pltpu.make_async_copy(own, attn_in.at[ring.me], local_sems.at[0])
    keep.start()
    keep_cot = pltpu.make_async_copy(cotangent, grad_out.at[ring.me], local_sems.at[1])
    keep_cot.start()
    gathering.first()
    places.fill()
    gathering.second()
    for columns in (columns_q, columns_k, columns_v):
        columns.spread()
    rows_output.relay()
    gathering.third()
    for columns in (columns_q, columns_k, columns_v):
        columns.relay()
    columns_gate.begin()
    columns_up.begin()
    rows_down.relay()
    for columns in (columns_q, columns_k, columns_v):
        columns.arrive()
    gathering.finish()
    keep.wait()
    save_in = pltpu.make_async_copy(attn_in, attn_in_out, local_sems.at[2])
    save_in.start()
    save_qkv = pltpu.make_async_copy(w_qkv, w_qkv_out, local_sems.at[3])
    save_qkv.start()
    width = hidden.shape[1]

    @pl.loop(0, size)
    def _(member):
        at = pl.ds(pl.multiple_of(member * tokens, tokens), tokens)
        product = jnp.dot(
            attn_in[member], w_qkv[...].reshape(width, w_qkv.shape[3]), preferred_element_type=jnp.float32
        )
        raw[at, :] = product[:, : q_width + head]
        for which in range(q_heads + 1):
            values_raw = product[:, which * head : (which + 1) * head]
            gain = q_gain if which < q_heads else k_gain
            turned = turn(values_raw * head_norm(values_raw) * gain[...].astype(jnp.float32), cosine[at, :], sine[at, :])
            if which < q_heads:
                queries[member, which] = (turned * head**-0.5).astype(jnp.bfloat16)
            else:
                keys[at, :] = turned.astype(jnp.bfloat16)
        fresh = product[:, q_width + head :]
        values[at, :] = fresh.astype(jnp.bfloat16)
        values_t[:, at] = fresh.T.astype(jnp.bfloat16)

    @pl.loop(0, size)
    def _(member):
        visible = places.visible(member)
        for which in range(q_heads):
            scores = lax.dot_general(
                keys[...], queries[member, which], (((1,), (1,)), ((), ())), preferred_element_type=jnp.float32
            )
            scores = jnp.where(visible, scores, -1e30)
            peak = jnp.max(scores, axis=0, keepdims=True)
            weights = jnp.exp(scores - peak)
            total = jnp.sum(weights, axis=0, keepdims=True)
            probs = (weights * (1.0 / total)).astype(jnp.bfloat16)
            mixed = jnp.dot(values_t[...], probs, preferred_element_type=jnp.float32)
            attn[member, :, which * head : (which + 1) * head] = mixed.T.astype(jnp.bfloat16)
            log_totals[member, which : which + 1, :] = peak + jnp.log(total)

    saves = [
        pltpu.make_async_copy(source, target, local_sems.at[4 + which])
        for which, (source, target) in enumerate(
            ((raw, raw_out), (queries, queries_out), (keys, keys_out), (values, values_out), (attn, attn_out))
        )
    ]
    for save in saves:
        save.start()
    for part in range(SUBS):
        for way in range(2):
            gathering_cot.start(way, part)
    columns_gate.spread()
    gathering_cot.first()
    columns_up.spread()
    gathering_cot.second()
    gathering_cot.third()
    columns_gate.relay()
    columns_up.relay()
    gathering_cot.finish()
    sharing.finish()
    columns_gate.arrive()
    columns_up.arrive()
    for columns in (columns_q, columns_k, columns_v, columns_gate, columns_up):
        columns.finish()
    rows_output.finish()
    rows_down.finish()
    keep_cot.wait()
    for save in saves + [save_in, save_qkv]:
        save.wait()


def fore(blocks, in_gain, post_gain, tables, q_gain, k_gain, hidden, w_query, w_key, w_value, w_output, w_gate, w_up, w_down, cotangent):
    size, n_fsdp = lax.axis_size("ctx"), lax.axis_size("fsdp")
    rows, width = hidden.shape
    depth = w_query.shape[0]
    head = q_gain.shape[0]
    q_heads = w_query.shape[1] // size // head
    everyone = size * rows
    qkv_share = (w_query.shape[1] + w_key.shape[1] + w_value.shape[1]) // size
    gu_share = (w_gate.shape[1] + w_up.shape[1]) // size
    f32, bf16 = jnp.float32, jnp.bfloat16
    return pl.pallas_call(
        functools.partial(fore_kernel, size, n_fsdp, q_heads),
        out_shape=[
            jax.ShapeDtypeStruct((n_fsdp, size, 8, 2 * depth), f32),
            jax.ShapeDtypeStruct((8, width), f32),
            jax.ShapeDtypeStruct((size, q_heads, rows), f32),
            jax.ShapeDtypeStruct((everyone, (q_heads + 1) * head), f32),
            jax.ShapeDtypeStruct((size, q_heads, rows, head), bf16),
            jax.ShapeDtypeStruct((everyone, head), bf16),
            jax.ShapeDtypeStruct((everyone, head), bf16),
            jax.ShapeDtypeStruct((size, rows, q_heads * head), bf16),
            jax.ShapeDtypeStruct((size, rows, width), bf16),
            jax.ShapeDtypeStruct((size, n_fsdp, depth, qkv_share), bf16),
            jax.ShapeDtypeStruct((n_fsdp,) + w_output.shape, bf16),
            jax.ShapeDtypeStruct((size, n_fsdp, depth, gu_share), bf16),
            jax.ShapeDtypeStruct((n_fsdp,) + w_down.shape, bf16),
            jax.ShapeDtypeStruct((size, rows, width), bf16),
        ],
        in_specs=[pl.BlockSpec(memory_space=pltpu.SMEM)] + [VMEM_SPEC] * 7 + [ANY_SPEC] * 8,
        out_specs=[VMEM_SPEC] * 3 + [ANY_SPEC] * 11,
        scratch_shapes=[
            pltpu.VMEM((8, 2 * depth), f32),
            pltpu.VMEM((rows, width), bf16),
            pltpu.VMEM((size, rows, width), bf16),
            pltpu.VMEM((size, n_fsdp, depth, qkv_share), bf16),
            pltpu.VMEM((everyone, head), f32),
            pltpu.VMEM((everyone, head), f32),
            pltpu.VMEM((everyone, head), f32),
            pltpu.VMEM((head, everyone), bf16),
            pltpu.VMEM((everyone, (q_heads + 1) * head), f32),
            pltpu.VMEM((size, q_heads, rows, head), bf16),
            pltpu.VMEM((everyone, head), bf16),
            pltpu.VMEM((everyone, head), bf16),
            pltpu.VMEM((size, rows, q_heads * head), bf16),
        ]
        + small_sems(size, n_fsdp)
        + [pltpu.SemaphoreType.DMA((9,))]
        + columns_sems(size) * 5
        + rows_sems() * 2
        + square_sems() * 2,
        compiler_params=params(2),
    )(
        blocks,
        in_gain.reshape(1, depth),
        post_gain.reshape(1, depth),
        *tables,
        q_gain.reshape(1, head),
        k_gain.reshape(1, head),
        hidden,
        w_query,
        w_key,
        w_value,
        w_output,
        w_gate,
        w_up,
        w_down,
        cotangent,
    )


def norm_pull(grad_normed, normed, scale):
    return scale * (grad_normed - normed * jnp.mean(grad_normed * normed, axis=-1, keepdims=True))


def feed_forward_kernel(
    size,
    n_fsdp,
    attn,
    w_output,
    hidden,
    gains,
    w_gu_in,
    w_down_in,
    cot_in,
    out_hidden,
    grad_gain,
    grad_mid_out,
    grad_branch,
    gu_total_out,
    down_out,
    w_gu,
    w_down,
    cot,
    load_sems,
    mid,
    own,
    mlp_in,
    inner,
    grad_gu,
    gu_part,
    down_part,
    grad_mid,
    gu_total,
    down_total,
    layer_terms,
    *scratch,
):
    loads = [
        pltpu.make_async_copy(source, target, load_sems.at[which])
        for which, (source, target) in enumerate(((w_gu_in, w_gu), (w_down_in, w_down), (cot_in, cot)))
    ]
    for load in loads:
        load.start()
    ring = Ring(size)
    greet(near_devices(ring, n_fsdp))
    half = own.shape[0] // 2
    ff = w_down.shape[0]
    out_sums, gather_sems_in = scratch[:5], scratch[5:7]
    layer_sums = (layer_terms,) + tuple(scratch[7:11])
    gather_sems_out, keep_sems = scratch[11:13], scratch[13]
    column_scratch = (scratch[14], None, gu_total, scratch[15], scratch[16])
    row_scratch = (scratch[17], None, scratch[18], scratch[19], scratch[20])

    first = SumRing(ring, row_terms(attn, w_output, out_sums[0]), *out_sums)
    first.run()
    gathering = GatherRing(ring, own, mlp_in, *gather_sems_in)
    for way, part, place in first.parts():
        total = first.result(way, part) + hidden[place].astype(jnp.float32)
        mid[place] = total
        scale = lax.rsqrt(jnp.mean(total * total, axis=-1, keepdims=True) + EPS)
        own[place] = (total * scale * gains[1:2]).astype(jnp.bfloat16)
        gathering.start(way, part)
    first.finish()
    keep = pltpu.make_async_copy(own, mlp_in.at[ring.me], keep_sems.at[0])
    keep.start()
    for load in loads:
        load.wait()

    def units(lines, members):
        cot_lines = jnp.concatenate([cot[members[way], way * half : (way + 1) * half] for way in range(2)], axis=0)

        @pl.loop(0, ff // UNITS)
        def _(tile):
            at = pl.multiple_of(tile * UNITS, UNITS)
            here, there = pl.ds(at, UNITS), pl.ds(pl.multiple_of(ff + at, UNITS), UNITS)
            gate = jnp.dot(lines, w_gu[:, here], preferred_element_type=jnp.float32)
            up = jnp.dot(lines, w_gu[:, there], preferred_element_type=jnp.float32)
            pulled = lax.dot_general(
                cot_lines, w_down[here, :], (((1,), (1,)), ((), ())), preferred_element_type=jnp.float32
            )
            sigmoid = 1.0 / (1.0 + jnp.exp(-gate))
            active = gate * sigmoid
            inner_new = (active * up).astype(jnp.bfloat16)
            gate_new = (pulled * up * sigmoid * (1.0 + gate * (1.0 - sigmoid))).astype(jnp.bfloat16)
            up_new = (pulled * active).astype(jnp.bfloat16)
            for way in range(2):
                place = slice(way * half, (way + 1) * half)
                inner[members[way], place, here] = inner_new[place]
                grad_gu[members[way], place, here] = gate_new[place]
                grad_gu[members[way], place, there] = up_new[place]

    def units_of(step):
        members = [ring.member(way, step) for way in range(2)]
        units(
            jnp.concatenate([mlp_in[members[way], way * half : (way + 1) * half] for way in range(2)], axis=0), members
        )

    units(own[...], [ring.me, ring.me])

    @pl.loop(1, size - 1)
    def _(step):
        gathering.step(step)
        units_of(step)

    third = SumRing(ring, row_terms_t(grad_gu, w_gu, out_sums[0]), *out_sums)
    third.begin()
    gathering.finish()
    keep.wait()
    units_of(size - 1)
    rows_all = size * 2 * half
    width = w_gu.shape[0]
    block = width // size

    def gu_tile(member):
        columns = pl.ds(pl.multiple_of(member * block, block), block)
        lines = mlp_in[:, :, columns].reshape(rows_all, block)

        @pl.loop(0, 2 * ff // TILE)
        def _(tile):
            there = pl.ds(pl.multiple_of(tile * TILE, TILE), TILE)
            product = lax.dot_general(
                lines,
                grad_gu[:, :, there].reshape(rows_all, TILE),
                (((0,), (0,)), ((), ())),
                preferred_element_type=jnp.float32,
            ).astype(jnp.bfloat16)
            for row in range(n_fsdp):
                gu_part[row, member, :, there] = product[row * (block // n_fsdp) : (row + 1) * (block // n_fsdp)]

    share = ff // n_fsdp

    def down_tile(tile):
        columns = pl.ds(pl.multiple_of(tile * UNITS, UNITS), UNITS)
        lines = cot[:, :, columns].reshape(rows_all, UNITS)
        product = lax.dot_general(
            inner[...].reshape(rows_all, ff), lines, (((0,), (0,)), ((), ())), preferred_element_type=jnp.float32
        ).astype(jnp.bfloat16)
        for row in range(n_fsdp):
            down_part[row, :, columns] = product[row * share : (row + 1) * share]

    gu_tile(0)
    third.second()
    gu_tile(1)

    @pl.loop(2, size - 1)
    def _(step):
        third.step(step)
        gu_tile(step)

    second = SumRing(ring, row_terms(inner, w_down, layer_sums[0]), *layer_sums)
    second.begin()
    gu_tile(size - 1)
    columns = RowGrads(ring, n_fsdp, gu_part, *column_scratch)
    rows = RowGrads(ring, n_fsdp, down_part, *row_scratch)
    columns.begin()
    third.last_terms()
    gathering = GatherRing(ring, own, grad_branch, *gather_sems_out)
    gain_sum = jnp.zeros_like(grad_gain)
    for way, part, place in third.parts():
        pulled = third.result(way, part)
        values = mid[place]
        scale = lax.rsqrt(jnp.mean(values * values, axis=-1, keepdims=True) + EPS)
        normed = values * scale
        gain_sum = gain_sum + jnp.sum(pulled * normed, axis=0, keepdims=True)
        total = cot[ring.me, place].astype(jnp.float32) + norm_pull(pulled * gains[1:2], normed, scale)
        grad_mid[place] = total
        own[place] = total.astype(jnp.bfloat16)
        gathering.start(way, part)
    grad_gain[...] = gain_sum
    keep = pltpu.make_async_copy(own, grad_branch.at[ring.me], keep_sems.at[1])
    keep.start()
    save_mid = pltpu.make_async_copy(grad_mid, grad_mid_out, keep_sems.at[2])
    save_mid.start()
    third.finish()
    second.second()
    gathering.step(1)
    columns.cross()

    @pl.loop(2, 4)
    def _(step):
        second.step(step)
        gathering.step(step)

        @pl.loop(0, width // UNITS // 2)
        def _(tile):
            down_tile((step - 2) * (width // UNITS // 2) + tile)

    rows.begin()
    second.step(4)
    gathering.step(4)
    rows.cross()

    @pl.loop(5, size - 1)
    def _(step):
        second.step(step)
        gathering.step(step)

    second.last_terms()
    down_total[...] = rows.result()
    save_down = pltpu.make_async_copy(down_total, down_out, keep_sems.at[3])
    save_down.start()
    gu_total[...] = columns.result().astype(jnp.bfloat16)
    save_gu = pltpu.make_async_copy(gu_total, gu_total_out, keep_sems.at[4])
    save_gu.start()
    for way, part, place in second.parts():
        out_hidden[place] = (mid[place] + second.result(way, part)).astype(jnp.bfloat16)
    gathering.finish()
    second.finish()
    columns.finish()
    rows.finish()
    for copy in (keep, save_mid, save_down, save_gu):
        copy.wait()


UNITS = 256


def feed_forward(attn, w_output, hidden, gains, w_gu, w_down, cotangent):
    size, n_fsdp = lax.axis_size("ctx"), lax.axis_size("fsdp")
    rows, width = hidden.shape
    ff = w_down.shape[0]
    depth = width // size // n_fsdp
    sums = sum_scratch(size, rows, width)
    return pl.pallas_call(
        functools.partial(feed_forward_kernel, size, n_fsdp),
        out_shape=[
            jax.ShapeDtypeStruct((rows, width), jnp.bfloat16),
            jax.ShapeDtypeStruct((1, width), jnp.float32),
            jax.ShapeDtypeStruct((rows, width), jnp.float32),
            jax.ShapeDtypeStruct((size, rows, width), jnp.bfloat16),
            jax.ShapeDtypeStruct((size, depth, 2 * ff), jnp.bfloat16),
            jax.ShapeDtypeStruct((ff // n_fsdp, width), jnp.float32),
        ],
        in_specs=[VMEM_SPEC] * 4 + [ANY_SPEC] * 3,
        out_specs=[VMEM_SPEC] * 2 + [ANY_SPEC] * 4,
        scratch_shapes=[
            pltpu.VMEM(w_gu.shape, jnp.bfloat16),
            pltpu.VMEM(w_down.shape, jnp.bfloat16),
            pltpu.VMEM((size, rows, width), jnp.bfloat16),
            pltpu.SemaphoreType.DMA((3,)),
            pltpu.VMEM((rows, width), jnp.float32),
            pltpu.VMEM((rows, width), jnp.bfloat16),
            pltpu.VMEM((size, rows, width), jnp.bfloat16),
            pltpu.VMEM((size, rows, ff), jnp.bfloat16),
            pltpu.VMEM((size, rows, 2 * ff), jnp.bfloat16),
            pltpu.VMEM((n_fsdp, size, depth, 2 * ff), jnp.bfloat16),
            pltpu.VMEM((n_fsdp, ff // n_fsdp, width), jnp.bfloat16),
            pltpu.VMEM((rows, width), jnp.float32),
            pltpu.VMEM((size, depth, 2 * ff), jnp.bfloat16),
            pltpu.VMEM((ff // n_fsdp, width), jnp.float32),
            pltpu.VMEM((2, rows // 2, width), jnp.float32),
        ]
        + sums
        + gather_sems(size)
        + sums[1:]
        + gather_sems(size)
        + [pltpu.SemaphoreType.DMA((5,))]
        + [pltpu.VMEM((2, size, depth, 2 * ff), jnp.bfloat16)]
        + row_grads_sems()
        + [pltpu.VMEM((2, ff // n_fsdp, width), jnp.bfloat16), pltpu.VMEM((ff // n_fsdp, width), jnp.bfloat16)]
        + row_grads_sems(),
        compiler_params=params(5),
    )(
        attn,
        w_output,
        hidden,
        gains,
        w_gu,
        w_down,
        cotangent,
    )


def back_kernel(
    size,
    n_fsdp,
    all_blocks,
    starts,
    offsets,
    q_gain,
    k_gain,
    gains,
    post_sum,
    log_totals,
    *refs,
):
    sources, refs = refs[:11], refs[11:]
    gu_total = refs[0]
    grad_hidden, gains_out, output_out, gu_out, qkv_out = refs[1:6]
    targets, refs = refs[6:17], refs[17:]
    grad_branch, attn, w_output, queries, keys, values, raw, attn_in, w_qkv, hidden, grad_mid = targets
    load_sems, cosine, sine, places_ref, keys_t, grad_keys, grad_values, head_sums, grads, qkv_part, output_part = refs[:11]
    small, small_ctx, small_part, small_fsdp, small_send, small_recv = refs[11:17]
    scratch = refs[17:]
    loads = [
        pltpu.make_async_copy(source, target, load_sems.at[which])
        for which, (source, target) in enumerate(zip(sources, targets))
    ]
    for load in loads:
        load.start()
    sums = scratch[:5]
    ring = Ring(size)
    greet(near_devices(ring, n_fsdp))
    total = scratch[8]
    columns = RowGrads(ring, n_fsdp, qkv_part, scratch[5], None, *scratch[6:8], scratch[9])
    dealing = Deal(ring, total, qkv_out, *scratch[10:12])
    rows = RowGrads(ring, n_fsdp, output_part, scratch[12], None, *scratch[13:16])
    gu_dealing = Deal(ring, gu_total, gu_out, *scratch[16:18])
    gu_dealing.begin()
    places = Places(ring, n_fsdp, all_blocks, starts, offsets, cosine, sine, places_ref)
    places.fill()
    head = q_gain.shape[1]
    q_heads = queries.shape[1]
    tokens = attn_in.shape[1]
    everyone = size * tokens
    width = attn_in.shape[2]
    q_width = q_heads * head
    grad_keys[...] = jnp.zeros_like(grad_keys)
    grad_values[...] = jnp.zeros_like(grad_values)
    head_sums[...] = jnp.zeros_like(head_sums)
    for load in loads[:3]:
        load.wait()

    def through_head(pulled, at, which, gain_here):
        turned = turn(pulled, cosine[at, :], -sine[at, :])
        values_raw = raw[at, which * head : (which + 1) * head]
        scale = head_norm(values_raw)
        unit = values_raw * scale
        kind = 0 if which < q_heads else 1
        head_sums[kind : kind + 1] = head_sums[kind : kind + 1] + jnp.sum(turned * unit, axis=0, keepdims=True)
        return norm_pull(turned * gain_here[...].astype(jnp.float32), unit, scale).astype(jnp.bfloat16)

    def output_tile(tile):
        there = pl.ds(pl.multiple_of(tile * TILE, TILE), TILE)
        product = lax.dot_general(
            attn[...].reshape(everyone, q_width),
            grad_branch[:, :, there].reshape(everyone, TILE),
            (((0,), (0,)), ((), ())),
            preferred_element_type=jnp.float32,
        ).astype(jnp.bfloat16)
        share = q_width // n_fsdp
        for row in range(n_fsdp):
            output_part[row, :, there] = product[row * share : (row + 1) * share]

    @pl.loop(0, width // TILE)
    def _(tile):
        output_tile(tile)

    rows.begin()
    for load in loads[3:]:
        load.wait()
    keys_t[...] = keys[...].astype(jnp.float32).T.astype(jnp.bfloat16)

    @pl.loop(0, size)
    def _(member):
        at = pl.ds(pl.multiple_of(member * tokens, tokens), tokens)
        grad_attn = lax.dot_general(
            grad_branch[member], w_output[...], (((1,), (1,)), ((), ())), preferred_element_type=jnp.float32
        ).astype(jnp.bfloat16)
        visible = places.visible(member)
        for which in range(q_heads):
            lanes = slice(which * head, (which + 1) * head)
            pulled = grad_attn[:, lanes]
            query = queries[member, which]
            scores = lax.dot_general(keys[...], query, (((1,), (1,)), ((), ())), preferred_element_type=jnp.float32)
            probs = jnp.where(visible, jnp.exp(scores - log_totals[member, which : which + 1, :]), 0.0)
            grad_probs = lax.dot_general(
                values[...], pulled, (((1,), (1,)), ((), ())), preferred_element_type=jnp.float32
            )
            delta = jnp.sum(probs * grad_probs, axis=0, keepdims=True)
            grad_scores = (probs * (grad_probs - delta)).astype(jnp.bfloat16)
            grad_keys[...] = grad_keys[...] + jnp.dot(grad_scores, query, preferred_element_type=jnp.float32)
            grad_values[...] = grad_values[...] + jnp.dot(
                probs.astype(jnp.bfloat16), pulled, preferred_element_type=jnp.float32
            )
            grad_query = jnp.dot(keys_t[...], grad_scores, preferred_element_type=jnp.float32).T
            grads[member, :, lanes] = through_head(grad_query * head**-0.5, at, which, q_gain)

    rows.cross()

    @pl.loop(0, size)
    def _(member):
        at = pl.ds(pl.multiple_of(member * tokens, tokens), tokens)
        grads[member, :, q_width : q_width + head] = through_head(grad_keys[at, :], at, q_heads, k_gain)
        grads[member, :, q_width + head :] = grad_values[at, :].astype(jnp.bfloat16)

    block = width // size

    def qkv_tile(member):
        lines = attn_in[:, :, pl.ds(pl.multiple_of(member * block, block), block)].reshape(everyone, block)
        product = lax.dot_general(
            lines,
            grads[...].reshape(everyone, grads.shape[2]),
            (((0,), (0,)), ((), ())),
            preferred_element_type=jnp.float32,
        ).astype(jnp.bfloat16)
        for row in range(n_fsdp):
            qkv_part[row, member] = product[row * (block // n_fsdp) : (row + 1) * (block // n_fsdp)]

    summing = SquareSum(Square(size), block_terms_t(grads, w_qkv, sums[0]), *sums)
    summing.begin()

    @pl.loop(0, size // 2)
    def _(member):
        qkv_tile(member)

    summing.first()

    @pl.loop(size // 2, size)
    def _(member):
        qkv_tile(member)

    columns.begin()
    summing.second()
    columns.cross()
    summing.third()
    total[...] = columns.result().astype(jnp.bfloat16)
    dealing.begin()
    output_out[...] = rows.result()
    gain_sum = jnp.zeros_like(post_sum)
    for way, part, place in summing.parts():
        pulled = summing.result(way, part)
        values_in = hidden[place].astype(jnp.float32)
        scale = lax.rsqrt(jnp.mean(values_in * values_in, axis=-1, keepdims=True) + EPS)
        normed = values_in * scale
        gain_sum = gain_sum + jnp.sum(pulled * normed, axis=0, keepdims=True)
        grad_hidden[place] = grad_mid[place] + norm_pull(pulled * gains[0:1], normed, scale)
    chips = n_fsdp // 2
    for pair in range(size * chips):
        lanes = slice(pair * 128, (pair + 1) * 128)
        small[pair // chips, pair % chips, 0:1] = gain_sum[:, lanes]
        small[pair // chips, pair % chips, 1:2] = post_sum[:, lanes]
        small[pair // chips, pair % chips, 2:4] = head_sums[0:2]
        small[pair // chips, pair % chips, 4:8] = jnp.zeros((4, 128), jnp.float32)
    sharing = SmallSum(ring, n_fsdp, small, small_ctx, small_part, small_fsdp, small_send, small_recv)
    sharing.begin()
    sharing.cross()
    gains_out[...] = sharing.result()
    sharing.finish()
    summing.finish()
    columns.finish()
    rows.finish()
    dealing.finish()
    gu_dealing.finish()


def back(
    all_small,
    tables,
    q_gain,
    k_gain,
    raw,
    queries,
    keys,
    values,
    attn,
    log_totals,
    hidden,
    grad_mid,
    gains,
    post_sum,
    gu_total,
    grad_branch,
    w_output,
    attn_in,
    w_qkv,
):
    size, n_fsdp = lax.axis_size("ctx"), lax.axis_size("fsdp")
    rows, width = hidden.shape
    head = q_gain.shape[0]
    everyone = size * rows
    share = w_qkv.shape[1]
    depth = width // size // n_fsdp
    q_width = attn.shape[2]
    f32, bf16 = jnp.float32, jnp.bfloat16
    loaded = [grad_branch, attn, w_output, queries, keys, values, raw, attn_in, w_qkv, hidden, grad_mid]
    return pl.pallas_call(
        functools.partial(back_kernel, size, n_fsdp),
        out_shape=[
            jax.ShapeDtypeStruct((rows, width), f32),
            jax.ShapeDtypeStruct((8, 128), f32),
            jax.ShapeDtypeStruct((q_width // n_fsdp, width), f32),
            jax.ShapeDtypeStruct(gu_total.shape, bf16),
            jax.ShapeDtypeStruct((size, depth, share), bf16),
        ],
        in_specs=[VMEM_SPEC] * 8 + [ANY_SPEC] * 12,
        out_specs=[VMEM_SPEC] * 3 + [ANY_SPEC] * 2,
        scratch_shapes=[pltpu.VMEM(array.shape, array.dtype) for array in loaded]
        + [
            pltpu.SemaphoreType.DMA((len(loaded),)),
            pltpu.VMEM((everyone, head), f32),
            pltpu.VMEM((everyone, head), f32),
            pltpu.VMEM((everyone, head), f32),
            pltpu.VMEM((head, everyone), bf16),
            pltpu.VMEM((everyone, head), f32),
            pltpu.VMEM((everyone, head), f32),
            pltpu.VMEM((8, head), f32),
            pltpu.VMEM((size, rows, share), bf16),
            pltpu.VMEM((n_fsdp, size, depth, share), bf16),
            pltpu.VMEM((n_fsdp, q_width // n_fsdp, width), bf16),
            pltpu.VMEM((size, n_fsdp // 2, 8, 128), f32),
            pltpu.VMEM((size, n_fsdp // 2, 8, 128), f32),
            pltpu.VMEM((n_fsdp // 2, 8, 128), f32),
            pltpu.VMEM((n_fsdp, 8, 128), f32),
        ]
        + small_sems(size, n_fsdp)
        + square_sum_scratch(rows, width)
        + [
            pltpu.VMEM((2, size, depth, share), bf16),
            pltpu.VMEM((size, depth, share), bf16),
            pltpu.SemaphoreType.DMA((3,)),
            pltpu.VMEM((size, depth, share), bf16),
            pltpu.SemaphoreType.DMA((3,)),
        ]
        + deal_sems(size)
        + [
            pltpu.VMEM((2, q_width // n_fsdp, width), bf16),
            pltpu.VMEM((q_width // n_fsdp, width), bf16),
        ]
        + row_grads_sems()
        + deal_sems(size),
        compiler_params=params(6),
    )(
        all_small,
        *tables,
        q_gain.reshape(1, head),
        k_gain.reshape(1, head),
        gains,
        post_sum,
        log_totals,
        *loaded,
        gu_total,
    )


def finish_kernel(size, gu, qkv, gain_sums, *refs):
    kept, outs, refs = refs[:4], refs[4:9], refs[9:]
    kept_out, gains_out, refs = refs[:4], refs[4:8], refs[8:]
    gu_in, qkv_in, load_sems, wide, save_sems, keep_sems, held = refs[0], refs[1], refs[2], refs[3:8], refs[8], refs[9], refs[10:]
    loads = []
    for member in range(size):
        loads.append(
            (
                pltpu.make_async_copy(gu.at[member], gu_in.at[member], load_sems.at[0, member]),
                pltpu.make_async_copy(qkv.at[member], qkv_in.at[member], load_sems.at[1, member]),
            )
        )
    for pair in loads:
        for load in pair:
            load.start()
    holds = [
        pltpu.make_async_copy(source, target, keep_sems.at[0, which])
        for which, (source, target) in enumerate(zip(kept, held))
    ]
    for hold in holds:
        hold.start()
    side = lax.rem(lax.axis_index("fsdp"), 2)
    depth = gains_out[0].shape[1]
    for row, out in enumerate(gains_out[:2]):
        out[...] = jnp.where(side == 0, gain_sums[row : row + 1, :depth], gain_sums[row : row + 1, depth:])
    for row, out in enumerate(gains_out[2:]):
        out[...] = gain_sums[2 + row : 3 + row]
    saves = []
    for member in range(size):
        for load in loads[member]:
            load.wait()
        which = 0
        for arrived, count in ((gu_in, 2), (qkv_in, 3)):
            start = 0
            for _ in range(count):
                width = wide[which].shape[1] // size
                columns = pl.ds(member * width, width)
                wide[which][:, columns] = arrived[member, :, start : start + width].astype(jnp.float32)
                save = pltpu.make_async_copy(
                    wide[which].at[:, columns], outs[which].at[:, columns], save_sems.at[which, member]
                )
                save.start()
                saves.append(save)
                start += width
                which += 1
    for which, hold in enumerate(holds):
        hold.wait()
        save = pltpu.make_async_copy(held[which], kept_out[which], keep_sems.at[1, which])
        save.start()
        saves.append(save)
    for save in saves:
        save.wait()


def finish(gu, qkv, kept, gain_sums, widths):
    size = lax.axis_size("ctx")
    depth = gu.shape[1]
    f32 = jnp.float32
    wide = [(depth, width) for width in widths]
    return pl.pallas_call(
        functools.partial(finish_kernel, size),
        out_shape=[jax.ShapeDtypeStruct(shape, f32) for shape in wide]
        + [jax.ShapeDtypeStruct(array.shape, array.dtype) for array in kept]
        + [jax.ShapeDtypeStruct((1, depth), f32)] * 2
        + [jax.ShapeDtypeStruct((1, 128), f32)] * 2,
        in_specs=[ANY_SPEC] * 2 + [VMEM_SPEC] + [ANY_SPEC] * len(kept),
        out_specs=[ANY_SPEC] * (len(wide) + len(kept)) + [VMEM_SPEC] * 4,
        scratch_shapes=[
            pltpu.VMEM(gu.shape, gu.dtype),
            pltpu.VMEM(qkv.shape, qkv.dtype),
            pltpu.SemaphoreType.DMA((2, size)),
        ]
        + [pltpu.VMEM(shape, f32) for shape in wide]
        + [pltpu.SemaphoreType.DMA((len(wide), size)), pltpu.SemaphoreType.DMA((2, len(kept)))]
        + [pltpu.VMEM(array.shape, array.dtype) for array in kept],
        compiler_params=pltpu.CompilerParams(vmem_limit_bytes=62 * 1024 * 1024),
    )(gu, qkv, gain_sums, *kept)


def tp_body(
    hidden_in,
    block_of,
    in_gain,
    w_query,
    w_key,
    w_value,
    w_output,
    q_gain,
    k_gain,
    post_gain,
    w_gate,
    w_up,
    w_down,
    cotangent,
):
    seq_count, tok_rows, model_width = hidden_in.shape
    n_ctx = lax.axis_size("ctx")
    block_rows = tok_rows // 2
    rows = seq_count * tok_rows
    head_dim = q_gain.shape[0]
    hidden = hidden_in.reshape(rows, model_width)
    cot_local = cotangent.reshape(rows, model_width)
    depth = w_query.shape[0]

    tables = rotation_tables(2 * n_ctx, block_rows, head_dim)
    (
        all_small,
        gains,
        log_totals,
        raw,
        queries,
        keys,
        values,
        attn,
        attn_in,
        mine_qkv,
        mine_output,
        mine_gu,
        mine_down,
        grad_out,
    ) = fore(
        block_of,
        in_gain,
        post_gain,
        tables,
        q_gain,
        k_gain,
        hidden,
        w_query,
        w_key,
        w_value,
        w_output,
        w_gate,
        w_up,
        w_down,
        cot_local,
    )
    mine_qkv = mine_qkv.reshape(model_width, -1)
    mine_output = mine_output.reshape(-1, model_width)
    output, post_sum, grad_mid, grad_branch, gu_total, part_down = feed_forward(
        attn, mine_output, hidden, gains, mine_gu.reshape(model_width, -1), mine_down.reshape(-1, model_width), grad_out
    )
    grad_hidden, gain_sums, part_output, gu_sums, qkv_sums = back(
        all_small,
        tables,
        q_gain,
        k_gain,
        raw,
        queries,
        keys,
        values,
        attn,
        log_totals,
        hidden,
        grad_mid,
        gains,
        post_sum,
        gu_total,
        grad_branch,
        mine_output,
        attn_in,
        mine_qkv,
    )
    (
        part_gate,
        part_up,
        part_query,
        part_key,
        part_value,
        grad_hidden,
        output,
        part_down,
        part_output,
        part_in,
        part_post,
        sum_q_gain,
        sum_k_gain,
    ) = finish(
        gu_sums,
        qkv_sums,
        (grad_hidden, output, part_down, part_output),
        gain_sums,
        [weight.shape[1] for weight in (w_gate, w_up, w_query, w_key, w_value)],
    )
    return (
        output.reshape(seq_count, tok_rows, model_width),
        grad_hidden.reshape(seq_count, tok_rows, model_width),
        part_in.reshape(-1),
        part_query,
        part_key,
        part_value,
        part_output,
        sum_q_gain.reshape(-1),
        sum_k_gain.reshape(-1),
        part_post.reshape(-1),
        part_gate,
        part_up,
        part_down,
    )


def body(hidden_in, block_of, in_gain, w_query, w_key, w_value, w_output, q_gain, *rest):
    kv_heads = w_key.shape[1] // q_gain.shape[0]
    plan = tp_body if kv_heads == lax.axis_size("ctx") == 8 else gathered_weights_body
    return plan(hidden_in, block_of, in_gain, w_query, w_key, w_value, w_output, q_gain, *rest)


def solution(mesh):
    return jax.shard_map(
        body,
        mesh=mesh,
        in_specs=(
            P("fsdp", "ctx", None),
            P("fsdp", "ctx"),
            P(("ctx", "fsdp")),
            P(("ctx", "fsdp"), None),
            P(("ctx", "fsdp"), None),
            P(("ctx", "fsdp"), None),
            P(("ctx", "fsdp"), None),
            P(),
            P(),
            P(("ctx", "fsdp")),
            P(("ctx", "fsdp"), None),
            P(("ctx", "fsdp"), None),
            P(("ctx", "fsdp"), None),
            P("fsdp", "ctx", None),
        ),
        out_specs=(
            P("fsdp", "ctx", None),
            P("fsdp", "ctx", None),
            P(("ctx", "fsdp")),
            P(("ctx", "fsdp"), None),
            P(("ctx", "fsdp"), None),
            P(("ctx", "fsdp"), None),
            P(("ctx", "fsdp"), None),
            P(),
            P(),
            P(("ctx", "fsdp")),
            P(("ctx", "fsdp"), None),
            P(("ctx", "fsdp"), None),
            P(("ctx", "fsdp"), None),
        ),
        check_vma=False,
    )
```

```python
import functools
import math

import jax
import jax.numpy as jnp
import numpy as np
from jax import lax
from jax.experimental import pallas as pl
from jax.experimental.pallas import tpu as pltpu
from jax.sharding import PartitionSpec as P

EPS = 1e-06
THETA = 1000000.0


def rope_tables(positions, width):
    half_width = width // 2
    inverse = THETA ** (-(jnp.arange(half_width, dtype=jnp.float32) * 2.0 / width))
    angles = positions.astype(jnp.float32)[:, None] * inverse[None, :]
    return (jnp.cos(angles), jnp.sin(angles))


def rotate(values, cosine, sine):
    half_width = values.shape[-1] // 2
    first = values[..., :half_width]
    second = values[..., half_width:]
    cos_wide = cosine[:, None, :]
    sin_wide = sine[:, None, :]
    return jnp.concatenate(
        [first * cos_wide - second * sin_wide, second * cos_wide + first * sin_wide], axis=-1
    )


def norm_back(grad_normed, normed, scale):
    return scale * (grad_normed - normed * jnp.mean(grad_normed * normed, axis=-1, keepdims=True))


def gathered_weights_body(
    hidden_in,
    block_of,
    in_gain,
    w_query,
    w_key,
    w_value,
    w_output,
    q_gain,
    k_gain,
    post_gain,
    w_gate,
    w_up,
    w_down,
    cotangent,
):
    seq_count = hidden_in.shape[0]
    tok_rows = hidden_in.shape[1]
    flat_rows = seq_count * tok_rows
    model_width = hidden_in.shape[2]
    block_rows = tok_rows // 2
    block_total = 2 * lax.axis_size("ctx")
    seq_len = block_total * block_rows
    head_dim = q_gain.shape[0]
    q_heads = w_query.shape[1] // head_dim
    kv_heads = w_key.shape[1] // head_dim
    group_size = q_heads // kv_heads
    tile_blocks = math.gcd(block_total, max(1, 512 // block_rows))
    tile_rows = tile_blocks * block_rows
    q_scale = head_dim ** (-0.5)
    contract_rows = (((0,), (0,)), ((), ()))
    contract_cols = (((1,), (1,)), ((), ()))
    offsets = jnp.arange(block_rows, dtype=jnp.int32)
    positions = (block_of[:, :, None] * block_rows + offsets[None, None, :]).reshape(flat_rows)
    cosine, sine = rope_tables(positions, head_dim)
    residual = hidden_in.reshape(flat_rows, model_width).astype(jnp.float32)
    full_in_gain, full_query, full_key, full_value, full_output = (
        lax.all_gather(in_gain, ("ctx", "fsdp"), axis=0, tiled=True),
        lax.all_gather(w_query, ("ctx", "fsdp"), axis=0, tiled=True),
        lax.all_gather(w_key, ("ctx", "fsdp"), axis=0, tiled=True),
        lax.all_gather(w_value, ("ctx", "fsdp"), axis=0, tiled=True),
        lax.all_gather(w_output, ("ctx", "fsdp"), axis=0, tiled=True),
    )
    in_scale = lax.rsqrt(jnp.mean(residual * residual, axis=-1, keepdims=True) + EPS)
    in_normed = residual * in_scale
    attn_in = (in_normed * full_in_gain.astype(jnp.float32)).astype(jnp.bfloat16)
    q_raw = jnp.dot(attn_in, full_query, preferred_element_type=jnp.float32).reshape(
        flat_rows, q_heads, head_dim
    )
    k_raw = jnp.dot(attn_in, full_key, preferred_element_type=jnp.float32).reshape(
        flat_rows, kv_heads, head_dim
    )
    v_local = jnp.dot(attn_in, full_value, preferred_element_type=jnp.float32).astype(jnp.bfloat16)
    q_rms = lax.rsqrt(jnp.mean(q_raw * q_raw, axis=-1, keepdims=True) + EPS)
    q_unit = q_raw * q_rms
    queries = (rotate(q_unit * q_gain.astype(jnp.float32), cosine, sine) * q_scale).astype(
        jnp.bfloat16
    )
    k_rms = lax.rsqrt(jnp.mean(k_raw * k_raw, axis=-1, keepdims=True) + EPS)
    k_unit = k_raw * k_rms
    keys_local = rotate(k_unit * k_gain.astype(jnp.float32), cosine, sine).astype(jnp.bfloat16)
    all_keys, all_values, all_slots = (
        lax.all_gather(
            keys_local.reshape(seq_count, tok_rows, kv_heads * head_dim), "ctx", axis=1, tiled=True
        ),
        lax.all_gather(
            v_local.reshape(seq_count, tok_rows, kv_heads * head_dim), "ctx", axis=1, tiled=True
        ),
        lax.all_gather(block_of, "ctx", axis=1, tiled=True),
    )

    def tile_scores(query_tile, key_tile, query_pos, step):
        scores = jnp.einsum(
            "qhgd,khd->hgqk", query_tile, key_tile, preferred_element_type=jnp.float32
        )
        key_pos = step * tile_rows + jnp.arange(tile_rows, dtype=jnp.int32)
        visible = key_pos[None, :] <= query_pos[:, None]
        return (scores, visible)

    def sequence_tables(seq):
        key_blocks = all_keys[seq].reshape(block_total, block_rows, kv_heads, head_dim)
        value_blocks = all_values[seq].reshape(block_total, block_rows, kv_heads, head_dim)
        block_index = (
            jnp.zeros((block_total,), jnp.int32)
            .at[all_slots[seq]]
            .set(jnp.arange(block_total, dtype=jnp.int32))
        )
        return (key_blocks, value_blocks, block_index)

    def tile_index(block_index, step):
        return lax.dynamic_slice_in_dim(block_index, step * tile_blocks, tile_blocks)

    def fetch(table, block_index, step):
        return jnp.take(table, tile_index(block_index, step), axis=0).reshape(
            tile_rows, kv_heads, head_dim
        )

    log_totals = []
    attn_parts = []
    seq = 0
    key_blocks, value_blocks, block_index = sequence_tables(seq)
    for which in range(2):
        slot = 2 * seq + which
        query_tile = queries[slot * block_rows : (slot + 1) * block_rows].reshape(
            block_rows, kv_heads, group_size, head_dim
        )
        query_pos = positions[slot * block_rows : (slot + 1) * block_rows]
        tile_count = block_of[seq, which] // tile_blocks + 1

        def max_step(step, carry):
            running_max, running_sum = carry
            scores, visible = tile_scores(
                query_tile, fetch(key_blocks, block_index, step), query_pos, step
            )
            scores = jnp.where(visible, scores, -1e30)
            new_max = jnp.maximum(running_max, jnp.max(scores, axis=-1))
            running_sum = running_sum * jnp.exp(running_max - new_max) + jnp.sum(
                jnp.exp(scores - new_max[..., None]), axis=-1
            )
            return (new_max, running_sum)

        start_max = jnp.full((kv_heads, group_size, block_rows), -1e30, jnp.float32)
        start_sum = jnp.zeros((kv_heads, group_size, block_rows), jnp.float32)
        running_max, running_sum = lax.fori_loop(0, tile_count, max_step, (start_max, start_sum))
        log_total = running_max + jnp.log(running_sum)

        def value_step(step, total):
            scores, visible = tile_scores(
                query_tile, fetch(key_blocks, block_index, step), query_pos, step
            )
            probs = jnp.where(visible, jnp.exp(scores - log_total[..., None]), 0.0)
            return total + jnp.einsum(
                "hgqk,khd->qhgd",
                probs.astype(jnp.bfloat16),
                fetch(value_blocks, block_index, step),
                preferred_element_type=jnp.float32,
            )

        attn_part = lax.fori_loop(
            0,
            tile_count,
            value_step,
            jnp.zeros((block_rows, kv_heads, group_size, head_dim), jnp.float32),
        )
        log_totals.append(log_total)
        attn_parts.append(attn_part)
    attn_full = jnp.concatenate(attn_parts, axis=0)
    attn_bf = attn_full.reshape(flat_rows, q_heads * head_dim).astype(jnp.bfloat16)
    branch = jnp.dot(attn_bf, full_output, preferred_element_type=jnp.float32)
    hidden_mid = residual + branch
    full_post, full_gate, full_up, full_down = (
        lax.all_gather(post_gain, ("ctx", "fsdp"), axis=0, tiled=True),
        lax.all_gather(w_gate, ("ctx", "fsdp"), axis=0, tiled=True),
        lax.all_gather(w_up, ("ctx", "fsdp"), axis=0, tiled=True),
        lax.all_gather(w_down, ("ctx", "fsdp"), axis=0, tiled=True),
    )
    post_scale = lax.rsqrt(jnp.mean(hidden_mid * hidden_mid, axis=-1, keepdims=True) + EPS)
    post_normed = hidden_mid * post_scale
    mlp_in = (post_normed * full_post.astype(jnp.float32)).astype(jnp.bfloat16)
    gate_pre = jnp.dot(mlp_in, full_gate, preferred_element_type=jnp.float32)
    up_pre = jnp.dot(mlp_in, full_up, preferred_element_type=jnp.float32)
    sigmoid_gate = jax.nn.sigmoid(gate_pre)
    activated = gate_pre * sigmoid_gate
    inner = (activated * up_pre).astype(jnp.bfloat16)
    mlp_out = jnp.dot(inner, full_down, preferred_element_type=jnp.float32)
    output = (hidden_mid + mlp_out).astype(jnp.bfloat16)
    full_post, full_gate, full_up, full_down = (
        lax.all_gather(post_gain, ("ctx", "fsdp"), axis=0, tiled=True),
        lax.all_gather(w_gate, ("ctx", "fsdp"), axis=0, tiled=True),
        lax.all_gather(w_up, ("ctx", "fsdp"), axis=0, tiled=True),
        lax.all_gather(w_down, ("ctx", "fsdp"), axis=0, tiled=True),
    )
    grad_out = cotangent.reshape(flat_rows, model_width)
    grad_down = lax.dot_general(inner, grad_out, contract_rows, preferred_element_type=jnp.float32)
    part_down = lax.psum_scatter(grad_down, ("ctx", "fsdp"), scatter_dimension=0, tiled=True)
    grad_inner = lax.dot_general(
        grad_out, full_down, contract_cols, preferred_element_type=jnp.float32
    )
    grad_gate_pre = (
        grad_inner * up_pre * sigmoid_gate * (1.0 + gate_pre * (1.0 - sigmoid_gate))
    ).astype(jnp.bfloat16)
    grad_up_pre = (grad_inner * activated).astype(jnp.bfloat16)
    grad_gate = lax.dot_general(
        mlp_in, grad_gate_pre, contract_rows, preferred_element_type=jnp.float32
    )
    grad_up = lax.dot_general(
        mlp_in, grad_up_pre, contract_rows, preferred_element_type=jnp.float32
    )
    grad_mlp_in = lax.dot_general(
        grad_gate_pre, full_gate, contract_cols, preferred_element_type=jnp.float32
    ) + lax.dot_general(grad_up_pre, full_up, contract_cols, preferred_element_type=jnp.float32)
    grad_post_gain = jnp.sum(grad_mlp_in * post_normed, axis=0)
    grad_mid = grad_out.astype(jnp.float32) + norm_back(
        grad_mlp_in * full_post.astype(jnp.float32), post_normed, post_scale
    )
    part_post, part_gate, part_up = (
        lax.psum_scatter(grad_post_gain, ("ctx", "fsdp"), scatter_dimension=0, tiled=True),
        lax.psum_scatter(grad_gate, ("ctx", "fsdp"), scatter_dimension=0, tiled=True),
        lax.psum_scatter(grad_up, ("ctx", "fsdp"), scatter_dimension=0, tiled=True),
    )
    full_in_gain, full_query, full_key, full_value, full_output = (
        lax.all_gather(in_gain, ("ctx", "fsdp"), axis=0, tiled=True),
        lax.all_gather(w_query, ("ctx", "fsdp"), axis=0, tiled=True),
        lax.all_gather(w_key, ("ctx", "fsdp"), axis=0, tiled=True),
        lax.all_gather(w_value, ("ctx", "fsdp"), axis=0, tiled=True),
        lax.all_gather(w_output, ("ctx", "fsdp"), axis=0, tiled=True),
    )
    grad_branch = grad_mid.astype(jnp.bfloat16)
    grad_output = lax.dot_general(
        attn_bf, grad_branch, contract_rows, preferred_element_type=jnp.float32
    )
    grad_attn = lax.dot_general(
        grad_branch, full_output, contract_cols, preferred_element_type=jnp.float32
    ).astype(jnp.bfloat16)
    grad_attn = grad_attn.reshape(flat_rows, kv_heads, group_size, head_dim)
    query_grads = []
    seq = 0
    key_blocks, value_blocks, block_index = sequence_tables(seq)
    key_grads = jnp.zeros((block_total, block_rows, kv_heads, head_dim), jnp.float32)
    value_grads = jnp.zeros((block_total, block_rows, kv_heads, head_dim), jnp.float32)
    for which in range(2):
        slot = 2 * seq + which
        query_tile = queries[slot * block_rows : (slot + 1) * block_rows].reshape(
            block_rows, kv_heads, group_size, head_dim
        )
        query_pos = positions[slot * block_rows : (slot + 1) * block_rows]
        grad_tile = grad_attn[slot * block_rows : (slot + 1) * block_rows]
        tile_count = block_of[seq, which] // tile_blocks + 1
        delta = jnp.einsum("qhgd,qhgd->hgq", grad_tile.astype(jnp.float32), attn_parts[slot])
        log_total = log_totals[slot]

        def grad_step(step, carry):
            grad_query, keys_acc, values_acc = carry
            key_tile = fetch(key_blocks, block_index, step)
            scores, visible = tile_scores(query_tile, key_tile, query_pos, step)
            probs = jnp.where(visible, jnp.exp(scores - log_total[..., None]), 0.0)
            grad_probs = jnp.einsum(
                "qhgd,khd->hgqk",
                grad_tile,
                fetch(value_blocks, block_index, step),
                preferred_element_type=jnp.float32,
            )
            grad_scores = (probs * (grad_probs - delta[..., None])).astype(jnp.bfloat16)
            grad_query = grad_query + jnp.einsum(
                "hgqk,khd->qhgd", grad_scores, key_tile, preferred_element_type=jnp.float32
            )
            key_part = jnp.einsum(
                "hgqk,qhgd->khd", grad_scores, query_tile, preferred_element_type=jnp.float32
            )
            value_part = jnp.einsum(
                "hgqk,qhgd->khd",
                probs.astype(jnp.bfloat16),
                grad_tile,
                preferred_element_type=jnp.float32,
            )
            places = tile_index(block_index, step)
            keys_acc = keys_acc.at[places].add(
                key_part.reshape(tile_blocks, block_rows, kv_heads, head_dim)
            )
            values_acc = values_acc.at[places].add(
                value_part.reshape(tile_blocks, block_rows, kv_heads, head_dim)
            )
            return (grad_query, keys_acc, values_acc)

        start_query = jnp.zeros((block_rows, kv_heads, group_size, head_dim), jnp.float32)
        grad_query, key_grads, value_grads = lax.fori_loop(
            0, tile_count, grad_step, (start_query, key_grads, value_grads)
        )
        query_grads.append(grad_query)
    key_grad_list = [key_grads.reshape(seq_len, kv_heads * head_dim)]
    value_grad_list = [value_grads.reshape(seq_len, kv_heads * head_dim)]
    grad_keys, grad_values = (
        lax.psum_scatter(
            jnp.stack(key_grad_list, axis=0).astype(jnp.bfloat16),
            "ctx",
            scatter_dimension=1,
            tiled=True,
        ).astype(jnp.float32),
        lax.psum_scatter(
            jnp.stack(value_grad_list, axis=0).astype(jnp.bfloat16),
            "ctx",
            scatter_dimension=1,
            tiled=True,
        ).astype(jnp.float32),
    )
    grad_q_rot = (
        jnp.concatenate(query_grads, axis=0).reshape(flat_rows, q_heads, head_dim) * q_scale
    )
    grad_q_normed = rotate(grad_q_rot, cosine, -sine)
    grad_q_gain = jnp.sum(grad_q_normed * q_unit, axis=(0, 1))
    grad_q_raw = (
        norm_back(grad_q_normed * q_gain.astype(jnp.float32), q_unit, q_rms)
        .astype(jnp.bfloat16)
        .reshape(flat_rows, q_heads * head_dim)
    )
    grad_k_normed = rotate(grad_keys.reshape(flat_rows, kv_heads, head_dim), cosine, -sine)
    grad_k_gain = jnp.sum(grad_k_normed * k_unit, axis=(0, 1))
    grad_k_raw = (
        norm_back(grad_k_normed * k_gain.astype(jnp.float32), k_unit, k_rms)
        .astype(jnp.bfloat16)
        .reshape(flat_rows, kv_heads * head_dim)
    )
    grad_v_local = grad_values.reshape(flat_rows, kv_heads * head_dim).astype(jnp.bfloat16)
    grad_query_w = lax.dot_general(
        attn_in, grad_q_raw, contract_rows, preferred_element_type=jnp.float32
    )
    grad_key_w = lax.dot_general(
        attn_in, grad_k_raw, contract_rows, preferred_element_type=jnp.float32
    )
    grad_value_w = lax.dot_general(
        attn_in, grad_v_local, contract_rows, preferred_element_type=jnp.float32
    )
    grad_attn_in = lax.dot_general(
        grad_q_raw, full_query, contract_cols, preferred_element_type=jnp.float32
    )
    grad_attn_in = grad_attn_in + lax.dot_general(
        grad_k_raw, full_key, contract_cols, preferred_element_type=jnp.float32
    )
    grad_attn_in = grad_attn_in + lax.dot_general(
        grad_v_local, full_value, contract_cols, preferred_element_type=jnp.float32
    )
    grad_in_gain = jnp.sum(grad_attn_in * in_normed, axis=0)
    grad_input = grad_mid + norm_back(
        grad_attn_in * full_in_gain.astype(jnp.float32), in_normed, in_scale
    )
    part_in, part_query, part_key, part_value, part_output = (
        lax.psum_scatter(grad_in_gain, ("ctx", "fsdp"), scatter_dimension=0, tiled=True),
        lax.psum_scatter(grad_query_w, ("ctx", "fsdp"), scatter_dimension=0, tiled=True),
        lax.psum_scatter(grad_key_w, ("ctx", "fsdp"), scatter_dimension=0, tiled=True),
        lax.psum_scatter(grad_value_w, ("ctx", "fsdp"), scatter_dimension=0, tiled=True),
        lax.psum_scatter(grad_output, ("ctx", "fsdp"), scatter_dimension=0, tiled=True),
    )
    sum_q_gain, sum_k_gain = lax.psum((grad_q_gain, grad_k_gain), ("ctx", "fsdp"))
    return (
        output.reshape(seq_count, tok_rows, model_width),
        grad_input.reshape(seq_count, tok_rows, model_width),
        part_in,
        part_query,
        part_key,
        part_value,
        part_output,
        sum_q_gain,
        sum_k_gain,
        part_post,
        part_gate,
        part_up,
        part_down,
    )


MESH = pl.DeviceIdType.MESH
SUBS = 2


def ring_position(index, size):
    column, line = lax.rem(index, 2), lax.div(index, 2)
    return column * (line + 1) + (1 - column) * lax.rem(size - line, size)


def ring_member(position, size):
    late = lax.div(position + size // 2 - 1, size)
    beyond = lax.div(position + size - 1, size)
    return beyond * (1 - late) * (2 * position - 1) + late * 2 * (size - position)


class Ring:
    def __init__(self, size):
        self.size = size
        self.me = lax.axis_index("ctx")
        self.row = lax.axis_index("fsdp")
        self.position = ring_position(self.me, size)

    def member(self, way, steps):
        ahead = self.size - steps if way == 0 else steps
        return ring_member(lax.rem(self.position + ahead, self.size), self.size)

    def target(self, way):
        return (self.member(way, self.size - 1), self.row)

    def barrier(self):
        barrier = pltpu.get_barrier_semaphore()
        for way in range(2):
            pl.semaphore_signal(barrier, inc=1, device_id=self.target(way), device_id_type=MESH)
        pl.semaphore_wait(barrier, 2)


class GatherRing:
    def __init__(self, ring, own, out, send_sems, recv_sems):
        self.ring, self.own, self.out, self.send_sems, self.recv_sems = ring, own, out, send_sems, recv_sems
        self.half = own.shape[0] // 2
        self.sub = self.half // SUBS

    def copy(self, way, step, part, first=False):
        place = pl.ds(way * self.half + part * self.sub, self.sub)
        owner = self.ring.me if first else self.ring.member(way, step)
        source = self.own.at[place] if first else self.out.at[owner, place]
        return pltpu.make_async_remote_copy(
            src_ref=source,
            dst_ref=self.out.at[owner, place],
            send_sem=self.send_sems.at[way, step, part],
            recv_sem=self.recv_sems.at[way, step, part],
            device_id=self.ring.target(way),
            device_id_type=MESH,
        )

    def start(self, way, part):
        self.copy(way, 0, part, first=True).start()

    def step(self, step):
        for part in range(SUBS):
            for way in range(2):
                self.copy(way, step - 1, part).wait_recv()
                self.copy(way, step, part).start()

    def finish(self):
        last = self.ring.size - 2
        for part in range(SUBS):
            for way in range(2):
                self.copy(way, last, part).wait_recv()

        @pl.loop(0, last + 1)
        def _(step):
            for part in range(SUBS):
                for way in range(2):
                    self.copy(way, step, part).wait_send()

    def run(self):
        for way in range(2):
            self.start(way)

        @pl.loop(1, self.ring.size - 1)
        def _(step):
            self.step(step)

        self.finish()


def gather_sems(size):
    return [pltpu.SemaphoreType.DMA((2, size - 1, SUBS)), pltpu.SemaphoreType.DMA((2, size - 1, SUBS))]


class SumRing:
    def __init__(self, ring, compute, terms, outgoing, incoming, send_sems, recv_sems):
        self.ring, self.compute, self.terms = ring, compute, terms
        self.outgoing, self.incoming, self.send_sems, self.recv_sems = outgoing, incoming, send_sems, recv_sems
        self.half = terms.shape[1]
        self.sub = self.half // SUBS

    def copy(self, way, step, part):
        place = pl.ds(part * self.sub, self.sub)
        return pltpu.make_async_remote_copy(
            src_ref=self.outgoing.at[way, lax.rem(step, 2), place],
            dst_ref=self.incoming.at[way, step, place],
            send_sem=self.send_sems.at[way, step, part],
            recv_sem=self.recv_sems.at[way, step, part],
            device_id=self.ring.target(way),
            device_id_type=MESH,
        )

    def terms_of(self, step):
        self.compute([self.ring.member(way, step + 1) for way in range(2)])

    def begin(self):
        self.terms_of(0)
        for part in range(SUBS):
            place = pl.ds(part * self.sub, self.sub)
            for way in range(2):
                self.outgoing[way, 0, place] = self.terms[way, place].astype(jnp.bfloat16)
                self.copy(way, 0, part).start()

    def second(self):
        self.step(1, fresh=True)

    def step(self, step, fresh=False):
        self.terms_of(step)
        for part in range(SUBS):
            place = pl.ds(part * self.sub, self.sub)
            for way in range(2):
                self.copy(way, step - 1, part).wait_recv()
                total = self.terms[way, place] + self.incoming[way, step - 1, place].astype(jnp.float32)
                if not fresh:
                    self.copy(way, step - 2, part).wait_send()
                self.outgoing[way, lax.rem(step, 2), place] = total.astype(jnp.bfloat16)
                self.copy(way, step, part).start()

    def last_terms(self):
        self.compute([self.ring.me, self.ring.me])

    def result(self, way, part):
        last = self.ring.size - 2
        place = pl.ds(part * self.sub, self.sub)
        self.copy(way, last, part).wait_recv()
        return self.terms[way, place] + self.incoming[way, last, place].astype(jnp.float32)

    def parts(self):
        for part in range(SUBS):
            for way in range(2):
                start = way * self.half + part * self.sub
                yield way, part, slice(start, start + self.sub)

    def finish(self):
        for step in (self.ring.size - 3, self.ring.size - 2):
            for part in range(SUBS):
                for way in range(2):
                    self.copy(way, step, part).wait_send()

    def run(self):
        self.begin()
        self.second()

        @pl.loop(2, self.ring.size - 1)
        def _(step):
            self.step(step)

        self.last_terms()


def sum_scratch(size, rows, width):
    half = rows // 2
    return [
        pltpu.VMEM((2, half, width), jnp.float32),
        pltpu.VMEM((2, 2, half, width), jnp.bfloat16),
        pltpu.VMEM((2, size - 1, half, width), jnp.bfloat16),
        pltpu.SemaphoreType.DMA((2, size - 1, SUBS)),
        pltpu.SemaphoreType.DMA((2, size - 1, SUBS)),
    ]


class Square:
    def __init__(self, size):
        self.size = size
        self.me = lax.axis_index("ctx")
        self.row = lax.axis_index("fsdp")
        line, column = lax.div(self.me, 2), lax.rem(self.me, 2)
        half = lax.div(line, 2)
        self.inner = lax.rem(lax.div(line + 1, 2), 2) == 1
        self.outer = lax.rem(lax.div(line + 1, 2), 2) == 0
        self.beside = self.me + 1 - 2 * column
        self.along = self.me + 2 - 4 * lax.rem(line, 2)
        self.across = (3 - line) * 2 + column
        self.diagonal = self.along + 1 - 2 * column
        self.near = (2 - half) * 2 + column
        self.far = 6 * (1 - half) + column
        self.beside_near = (2 - half) * 2 + 1 - column
        self.beside_far = 6 * (1 - half) + 1 - column

    def targets(self):
        return [(member, self.row) for member in (self.beside, self.along, self.across)]


class SquareGather:
    def __init__(self, square, own, out, send_sems, recv_sems):
        self.square, self.own, self.out, self.send_sems, self.recv_sems = square, own, out, send_sems, recv_sems
        self.half = own.shape[0] // 2
        self.sub = self.half // SUBS
        me, rest = square.me, [(square.near, 0), (square.near, 1), (square.far, 0), (square.far, 1)]
        self.sent = [
            [(me, 0), (me, 1), (square.along, 1)] + rest,
            [(me, 0), (me, 1), (square.beside, 0)] + rest,
            [(me, 0), (me, 1), (square.along, 0), (square.along, 1)],
        ]

    def copy(self, link, slot, part):
        member, half = self.sent[link][slot]
        place = pl.ds(half * self.half + part * self.sub, self.sub)
        source = self.own.at[place] if slot < 2 else self.out.at[member, place]
        return remote(
            source,
            self.out.at[member, place],
            self.send_sems.at[link, slot, part],
            self.recv_sems.at[link, slot, part],
            self.square.targets()[link],
        )

    def start(self, half, part):
        for link in range(2):
            self.copy(link, half, part).start()

        @pl.when(self.square.inner)
        def _():
            self.copy(2, half, part).start()

    def relay(self, link, slot, *onward):
        for part in range(SUBS):
            self.copy(link, slot, part).wait_recv()
            for next_link, next_slot in onward:
                self.copy(next_link, next_slot, part).start()

    def first(self):
        @pl.when(self.square.outer)
        def _():
            self.relay(0, 0, (1, 2))
            self.relay(1, 1, (0, 2))

        @pl.when(self.square.inner)
        def _():
            self.relay(1, 0, (2, 2))
            self.relay(2, 0, (1, 3))
            self.relay(1, 1, (2, 3), (0, 2))
            for part in range(SUBS):
                self.copy(0, 3, part).start()

    def second(self):
        @pl.when(self.square.outer)
        def _():
            self.relay(1, 3, (0, 3))
            self.relay(1, 4, (0, 4))

        @pl.when(self.square.inner)
        def _():
            self.relay(2, 1, (1, 4), (0, 4))

    def third(self):
        @pl.when(self.square.outer)
        def _():
            self.relay(1, 5, (0, 5))
            self.relay(1, 6, (0, 6))

        @pl.when(self.square.inner)
        def _():
            self.relay(2, 2, (1, 5), (0, 5))
            self.relay(2, 3, (1, 6), (0, 6))
            self.relay(0, 0, (1, 2))

    def finish(self):
        for slot in range(1, 7):
            self.relay(0, slot)
        self.relay(1, 2)

        @pl.when(self.square.outer)
        def _():
            self.relay(1, 0)

        for part in range(SUBS):
            for slot in range(7):
                self.copy(0, slot, part).wait_send()
            for slot in range(3):
                self.copy(1, slot, part).wait_send()

        @pl.when(self.square.inner)
        def _():
            for part in range(SUBS):
                for slot in range(3, 7):
                    self.copy(1, slot, part).wait_send()
                for slot in range(4):
                    self.copy(2, slot, part).wait_send()


def square_sems():
    return [pltpu.SemaphoreType.DMA((3, 7, SUBS)), pltpu.SemaphoreType.DMA((3, 7, SUBS))]


class SquareSum:
    def __init__(self, square, compute, terms, outgoing, incoming, send_sems, recv_sems):
        self.square, self.compute, self.terms = square, compute, terms
        self.outgoing, self.incoming, self.send_sems, self.recv_sems = outgoing, incoming, send_sems, recv_sems
        self.half = outgoing.shape[1]
        self.sub = self.half // SUBS
        self.first_slot = (0, 7, 14)

    def copy(self, link, slot, part):
        at = self.first_slot[link] + slot
        place = pl.ds(part * self.sub, self.sub)
        return remote(
            self.outgoing.at[at, place],
            self.incoming.at[at, place],
            self.send_sems.at[link, slot, part],
            self.recv_sems.at[link, slot, part],
            self.square.targets()[link],
        )

    def arrived(self, link, slot, part):
        self.copy(link, slot, part).wait_recv()
        at = self.first_slot[link] + slot
        return self.incoming[at, part * self.sub : (part + 1) * self.sub].astype(jnp.float32)

    def term(self, which, half, part):
        start = half * self.half + part * self.sub
        return self.terms[which, start : start + self.sub]

    def send(self, link, slot, which, half, *received):
        at = self.first_slot[link] + slot
        for part in range(SUBS):
            total = self.term(which, half, part)
            for source in received:
                total = total + self.arrived(*source, part)
            self.outgoing[at, part * self.sub : (part + 1) * self.sub] = total.astype(jnp.bfloat16)
            self.copy(link, slot, part).start()

    def begin(self):
        square = self.square
        self.compute(square.beside_far, 0)
        self.send(0, 0, 0, 0)
        self.send(0, 1, 0, 1)
        self.compute(square.beside_near, 1)
        self.send(0, 2, 1, 0)
        self.send(0, 3, 1, 1)
        self.compute(square.diagonal, 2)
        self.send(1, 0, 2, 0)
        self.send(0, 4, 2, 1)
        self.compute(square.far, 0)
        self.compute(square.near, 1)

    def first(self):
        @pl.when(self.square.outer)
        def _():
            self.send(1, 1, 0, 0, (0, 0))
            self.send(1, 2, 0, 1, (0, 1))

        @pl.when(self.square.inner)
        def _():
            self.send(2, 0, 0, 0, (0, 0), (1, 1))

        self.compute(self.square.beside, 3)
        self.send(0, 6, 3, 1)
        self.send(0, 5, 3, 0, (1, 0))
        self.compute(self.square.along, 2)
        self.compute(self.square.me, 4)

    def second(self):
        @pl.when(self.square.outer)
        def _():
            self.send(1, 3, 1, 0, (0, 2))
            self.send(1, 4, 1, 1, (0, 3))
            self.send(1, 5, 2, 0)

        @pl.when(self.square.inner)
        def _():
            self.send(2, 1, 0, 1, (0, 1), (1, 2))
            self.send(1, 5, 2, 0, (2, 0))
            self.send(2, 2, 1, 0, (0, 2), (1, 3))

    def third(self):
        @pl.when(self.square.outer)
        def _():
            self.send(1, 6, 2, 1, (0, 4))

        @pl.when(self.square.inner)
        def _():
            self.send(2, 3, 1, 1, (0, 3), (1, 4))
            self.send(1, 6, 2, 1, (0, 4), (2, 1))
            for half in range(2):
                for part in range(SUBS):
                    start = half * self.half + part * self.sub
                    self.terms[4, start : start + self.sub] = self.term(4, half, part) + self.arrived(2, 2 + half, part)

    def parts(self):
        for half in range(2):
            for part in range(SUBS):
                start = half * self.half + part * self.sub
                yield half, part, slice(start, start + self.sub)

    def result(self, half, part):
        return self.term(4, half, part) + self.arrived(0, 5 + half, part) + self.arrived(1, 5 + half, part)

    def finish(self):
        for part in range(SUBS):
            for slot in range(7):
                self.copy(0, slot, part).wait_send()
            for slot in (0, 5, 6):
                self.copy(1, slot, part).wait_send()

        @pl.when(self.square.outer)
        def _():
            for part in range(SUBS):
                for slot in range(1, 5):
                    self.copy(1, slot, part).wait_send()

        @pl.when(self.square.inner)
        def _():
            for part in range(SUBS):
                for slot in range(4):
                    self.copy(2, slot, part).wait_send()


def square_sum_scratch(rows, width):
    return [
        pltpu.VMEM((5, rows, width), jnp.float32),
        pltpu.VMEM((18, rows // 2, width), jnp.bfloat16),
        pltpu.VMEM((18, rows // 2, width), jnp.bfloat16),
    ] + square_sems()


def block_terms_t(left, weight, terms, factors, product_sum):
    def compute(member, which):
        @pl.loop(0, weight.shape[0] // TILE)
        def _(tile):
            columns = pl.ds(pl.multiple_of(tile * TILE, TILE), TILE)
            terms[which, :, columns] = lax.dot_general(
                left[member], weight[columns, :], (((1,), (1,)), ((), ())), preferred_element_type=jnp.float32
            )
            product_sum[:, columns] = product_sum[:, columns] + jnp.sum(
                terms[which, :, columns] * factors[member, :, columns].astype(jnp.float32), axis=0, keepdims=True
            )

    return compute


TILE = 512


def row_terms(left, weight, terms):
    half = terms.shape[1]

    def compute(members):
        lines = jnp.concatenate([left[members[way], way * half : (way + 1) * half] for way in range(2)], axis=0)

        @pl.loop(0, weight.shape[1] // TILE)
        def _(tile):
            columns = pl.ds(pl.multiple_of(tile * TILE, TILE), TILE)
            product = jnp.dot(lines, weight[:, columns], preferred_element_type=jnp.float32)
            for way in range(2):
                terms[way, :, columns] = product[way * half : (way + 1) * half]

    return compute


def row_terms_t(left, weight, terms):
    half = terms.shape[1]

    def compute(members):
        lines = jnp.concatenate([left[members[way], way * half : (way + 1) * half] for way in range(2)], axis=0)

        @pl.loop(0, weight.shape[0] // TILE)
        def _(tile):
            columns = pl.ds(pl.multiple_of(tile * TILE, TILE), TILE)
            product = lax.dot_general(
                lines, weight[columns, :], (((1,), (1,)), ((), ())), preferred_element_type=jnp.float32
            )
            for way in range(2):
                terms[way, :, columns] = product[way * half : (way + 1) * half]

    return compute


VMEM_SPEC = pl.BlockSpec(memory_space=pltpu.VMEM)
ANY_SPEC = pl.BlockSpec(memory_space=pl.ANY)


def ctx_peer(ring, ahead):
    return lax.rem(ring.me + ahead, ring.size)


def across(row, n_fsdp):
    return lax.rem(row + n_fsdp // 2, n_fsdp)


def beside(row):
    return row + 1 - 2 * lax.rem(row, 2)


def remote(source, target, send_sem, recv_sem, device):
    return pltpu.make_async_remote_copy(
        src_ref=source,
        dst_ref=target,
        send_sem=send_sem,
        recv_sem=recv_sem,
        device_id=device,
        device_id_type=MESH,
    )


def greet(devices):
    barrier = pltpu.get_barrier_semaphore()
    for device in devices:
        pl.semaphore_signal(barrier, inc=1, device_id=device, device_id_type=MESH)
    pl.semaphore_wait(barrier, len(devices))


def near_devices(ring, n_fsdp):
    return [(ctx_peer(ring, ahead), ring.row) for ahead in range(1, ring.size)] + [
        (ring.me, lax.rem(ring.row + ahead, n_fsdp)) for ahead in range(1, n_fsdp)
    ]


class Spread:
    def __init__(self, ring, n_fsdp, block, out, send_sems, recv_sems):
        self.ring, self.n_fsdp, self.block, self.out = ring, n_fsdp, block, out
        self.send_sems, self.recv_sems = send_sems, recv_sems

    def along_ctx(self, ahead):
        return remote(
            self.block,
            self.out.at[self.ring.row, self.ring.me],
            self.send_sems.at[ahead],
            self.recv_sems.at[ahead],
            (ctx_peer(self.ring, ahead), self.ring.row),
        )

    def along_fsdp(self, ahead):
        line = self.out.at[self.ring.row]
        sem = self.ring.size + ahead
        row = lax.rem(self.ring.row + ahead, self.n_fsdp)
        return remote(line, line, self.send_sems.at[sem], self.recv_sems.at[sem], (self.ring.me, row))

    def begin(self):
        for ahead in range(1, self.ring.size):
            self.along_ctx(ahead).start()
        self.out[self.ring.row, self.ring.me] = self.block[...]

    def collect(self):
        for ahead in range(1, self.ring.size):
            self.along_ctx(ahead).wait_recv()
        for ahead in range(1, self.n_fsdp):
            self.along_fsdp(ahead).start()
        for ahead in range(1, self.n_fsdp):
            self.along_fsdp(ahead).wait_recv()

    def finish(self):
        for ahead in range(1, self.ring.size):
            self.along_ctx(ahead).wait_send()
        for ahead in range(1, self.n_fsdp):
            self.along_fsdp(ahead).wait_send()


class SmallSum:
    def __init__(self, ring, n_fsdp, blocks, by_ctx, part, by_fsdp, send_sems, recv_sems):
        self.ring, self.n_fsdp, self.blocks, self.by_ctx, self.part, self.by_fsdp = (
            ring,
            n_fsdp,
            blocks,
            by_ctx,
            part,
            by_fsdp,
        )
        self.send_sems, self.recv_sems = send_sems, recv_sems

    def along_ctx(self, ahead):
        member = ctx_peer(self.ring, ahead)
        return remote(
            self.blocks.at[member],
            self.by_ctx.at[self.ring.me],
            self.send_sems.at[ahead],
            self.recv_sems.at[ahead],
            (member, self.ring.row),
        )

    def along_fsdp(self, ahead):
        row = lax.rem(self.ring.row + ahead, self.n_fsdp)
        sem = self.ring.size + ahead
        return remote(
            self.part.at[lax.div(row, 2)],
            self.by_fsdp.at[self.ring.row],
            self.send_sems.at[sem],
            self.recv_sems.at[sem],
            (self.ring.me, row),
        )

    def begin(self):
        for ahead in range(1, self.ring.size):
            self.along_ctx(ahead).start()
        self.by_ctx[self.ring.me] = self.blocks[self.ring.me]

    def cross(self):
        for ahead in range(1, self.ring.size):
            self.along_ctx(ahead).wait_recv()
        self.part[...] = jnp.sum(self.by_ctx[...], axis=0)
        for ahead in range(1, self.n_fsdp):
            self.along_fsdp(ahead).start()
        self.by_fsdp[self.ring.row] = self.part[lax.div(self.ring.row, 2)]

    def result(self):
        for ahead in range(1, self.n_fsdp):
            self.along_fsdp(ahead).wait_recv()
        return jnp.sum(self.by_fsdp[...], axis=0)

    def finish(self):
        for ahead in range(1, self.ring.size):
            self.along_ctx(ahead).wait_send()
        for ahead in range(1, self.n_fsdp):
            self.along_fsdp(ahead).wait_send()


def small_sems(size, n_fsdp):
    return [pltpu.SemaphoreType.DMA((size + n_fsdp,)), pltpu.SemaphoreType.DMA((size + n_fsdp,))]


class Rows:
    def __init__(self, ring, n_fsdp, shard, out, send_sems, recv_sems):
        own, far, twin = ring.row, across(ring.row, n_fsdp), beside(ring.row)
        self.keep = pltpu.make_async_copy(shard, out.at[own], send_sems.at[3])
        self.to_far = remote(shard, out.at[own], send_sems.at[0], recv_sems.at[0], (ring.me, far))
        self.to_twin = remote(shard, out.at[own], send_sems.at[1], recv_sems.at[1], (ring.me, twin))
        self.pass_on = remote(out.at[far], out.at[far], send_sems.at[2], recv_sems.at[2], (ring.me, twin))

    def begin(self):
        self.keep.start()
        self.to_far.start()
        self.to_twin.start()

    def relay(self):
        self.to_far.wait_recv()
        self.pass_on.start()

    def finish(self):
        self.keep.wait()
        self.to_far.wait_send()
        self.to_twin.wait()
        self.pass_on.wait()


def rows_sems():
    return [pltpu.SemaphoreType.DMA((4,)), pltpu.SemaphoreType.DMA((3,))]


class Columns:
    def __init__(self, ring, n_fsdp, shard, out, start, send_sems, recv_sems):
        self.ring, self.shard, self.out, self.send_sems, self.recv_sems = ring, shard, out, send_sems, recv_sems
        self.width = shard.shape[1] // ring.size
        self.place = pl.ds(start, self.width)
        far, twin = across(ring.row, n_fsdp), beside(ring.row)
        self.to_far = self.link(0, ring.row, far)
        self.to_twin = self.link(1, ring.row, twin)
        self.pass_on = self.link(2, far, twin)

    def link(self, which, row, target):
        block = self.out.at[:, row, :, self.place]
        sem = self.ring.size + which
        return remote(block, block, self.send_sems.at[sem], self.recv_sems.at[sem], (self.ring.me, target))

    def piece(self, ahead):
        member = ctx_peer(self.ring, ahead)
        source = self.shard.at[:, pl.ds(pl.multiple_of(member * self.width, self.width), self.width)]
        target = self.out.at[self.ring.me, self.ring.row, :, self.place]
        if ahead == 0:
            return pltpu.make_async_copy(source, target, self.send_sems.at[0])
        return remote(source, target, self.send_sems.at[ahead], self.recv_sems.at[ahead], (member, self.ring.row))

    def begin(self):
        for ahead in range(self.ring.size):
            self.piece(ahead).start()

    def spread(self):
        self.piece(0).wait()
        for ahead in range(1, self.ring.size):
            self.piece(ahead).wait_recv()
        self.to_far.start()
        self.to_twin.start()

    def relay(self):
        self.to_far.wait_recv()
        self.pass_on.start()

    def arrive(self):
        self.to_twin.wait_recv()
        self.pass_on.wait_recv()

    def finish(self):
        for ahead in range(1, self.ring.size):
            self.piece(ahead).wait_send()
        self.to_far.wait_send()
        self.to_twin.wait_send()
        self.pass_on.wait_send()


def columns_sems(size):
    return [pltpu.SemaphoreType.DMA((size + 3,)), pltpu.SemaphoreType.DMA((size + 3,))]


class RowGrads:
    def __init__(self, ring, n_fsdp, part, from_twin, to_far, from_far, send_sems, recv_sems):
        own, far, twin = ring.row, across(ring.row, n_fsdp), beside(ring.row)
        self.part, self.from_twin, self.to_far, self.from_far = part, from_twin, to_far, from_far
        self.own, self.far = own, far
        twin_far = across(twin, n_fsdp)
        self.first = [
            remote(part.at[twin], from_twin.at[0], send_sems.at[0], recv_sems.at[0], (ring.me, twin)),
            remote(part.at[twin_far], from_twin.at[1], send_sems.at[1], recv_sems.at[1], (ring.me, twin)),
        ]
        if to_far is None:
            self.to_far = part.at[far]
        self.second = remote(self.to_far, from_far, send_sems.at[2], recv_sems.at[2], (ring.me, far))

    def begin(self):
        self.first[1].start()
        self.first[0].start()

    def cross(self):
        self.first[1].wait_recv()
        self.to_far[...] = (
            self.part[self.far].astype(jnp.float32) + self.from_twin[1].astype(jnp.float32)
        ).astype(jnp.bfloat16)
        self.second.start()

    def result(self):
        self.first[0].wait_recv()
        self.second.wait_recv()
        return (
            self.part[self.own].astype(jnp.float32)
            + self.from_twin[0].astype(jnp.float32)
            + self.from_far[...].astype(jnp.float32)
        )

    def finish(self):
        for copy in self.first + [self.second]:
            copy.wait_send()


def row_grads_sems():
    return [pltpu.SemaphoreType.DMA((3,)), pltpu.SemaphoreType.DMA((3,))]


def row_grads_scratch(shape):
    return [
        pltpu.VMEM((2,) + shape, jnp.bfloat16),
        pltpu.VMEM(shape, jnp.bfloat16),
        pltpu.VMEM(shape, jnp.bfloat16),
    ] + row_grads_sems()


class Deal:
    def __init__(self, ring, total, arrived, send_sems, recv_sems):
        self.ring, self.total, self.arrived = ring, total, arrived
        self.send_sems, self.recv_sems = send_sems, recv_sems

    def piece(self, ahead):
        member = ctx_peer(self.ring, ahead)
        source, target = self.total.at[member], self.arrived.at[self.ring.me]
        if ahead == 0:
            return pltpu.make_async_copy(source, target, self.send_sems.at[0])
        return remote(source, target, self.send_sems.at[ahead], self.recv_sems.at[ahead], (member, self.ring.row))

    def begin(self):
        for ahead in range(self.ring.size):
            self.piece(ahead).start()

    def finish(self):
        for ahead in range(self.ring.size):
            self.piece(ahead).wait()


def deal_sems(size):
    return [pltpu.SemaphoreType.DMA((size,)), pltpu.SemaphoreType.DMA((size,))]


def params(collective_id):
    return pltpu.CompilerParams(
        collective_id=collective_id, has_side_effects=True, vmem_limit_bytes=62 * 1024 * 1024
    )


def head_norm(raw):
    return lax.rsqrt(jnp.mean(raw * raw, axis=-1, keepdims=True) + EPS)


def turn(values, cosine, sine):
    return values * cosine + pltpu.roll(values, values.shape[-1] // 2, 1) * sine


class Places:
    def __init__(self, ring, n_fsdp, all_small, starts, offsets, cosine, sine, places):
        self.ring, self.n_fsdp, self.all_small = ring, n_fsdp, all_small
        self.starts, self.offsets, self.cosine, self.sine, self.places = starts, offsets, cosine, sine, places
        self.block_rows = offsets.shape[1]

    def block(self, member, which):
        return self.all_small[self.ring.row, member, 2:3, which : which + 1]

    def fill(self):
        count = self.starts.shape[1]
        numbers = lax.broadcasted_iota(jnp.int32, (count, 1), 0).astype(jnp.float32)
        offset = lax.broadcasted_iota(jnp.int32, (self.block_rows, self.places.shape[1]), 0).astype(jnp.float32)
        for slot in range(count):
            block = self.block(slot // 2, slot % 2)
            chosen = (numbers == block).astype(jnp.float32)
            cos_start = jnp.sum(chosen * self.starts[0], axis=0, keepdims=True)
            sin_start = jnp.sum(chosen * self.starts[1], axis=0, keepdims=True)
            at = slice(slot * self.block_rows, (slot + 1) * self.block_rows)
            self.cosine[at] = cos_start * self.offsets[0] - sin_start * self.offsets[1]
            self.sine[at] = sin_start * self.offsets[0] + cos_start * self.offsets[1]
            self.places[at] = offset + block * self.block_rows

    def visible(self, member):
        width = self.places.shape[1]
        lane = lax.broadcasted_iota(jnp.int32, (1, width), 1).astype(jnp.float32)
        rows = float(self.block_rows)
        query = lane + jnp.where(lane < rows, self.block(member, 0) * rows, self.block(member, 1) * rows - rows)
        return self.places[...] <= query


def rotation_tables(blocks, block_rows, head):
    inverse = (THETA ** (-(np.arange(head // 2, dtype=np.float32) * np.float32(2.0) / head))).astype(np.float64)

    def both(at):
        angles = at.astype(np.float64)[:, None] * inverse[None, :]
        cosine, sine = np.cos(angles), np.sin(angles)
        return jnp.asarray(
            np.stack(
                [np.concatenate([cosine, cosine], axis=1), np.concatenate([-sine, sine], axis=1)], axis=0
            ).astype(np.float32)
        )

    return both(np.arange(blocks) * block_rows), both(np.arange(block_rows))


def fore_kernel(
    size,
    n_fsdp,
    q_heads,
    blocks,
    in_gain,
    post_gain,
    starts,
    offsets,
    q_gain,
    k_gain,
    hidden,
    w_query,
    w_key,
    w_value,
    w_output,
    w_gate,
    w_up,
    w_down,
    cotangent,
    all_small,
    gains,
    log_totals,
    raw_out,
    queries_out,
    keys_out,
    values_out,
    attn_out,
    attn_in_out,
    w_qkv_out,
    output_out,
    gu_out,
    down_out,
    grad_out,
    small,
    own,
    attn_in,
    w_qkv,
    cosine,
    sine,
    places_ref,
    values_t,
    raw,
    queries,
    keys,
    values,
    attn,
    small_send,
    small_recv,
    local_sems,
    *scratch,
):
    ring = Ring(size)
    head = q_gain.shape[1]
    tokens = hidden.shape[0]
    depth = in_gain.shape[1]
    q_width = q_heads * head
    k_width = w_key.shape[1] // size
    ff = w_gate.shape[1] // size
    columns_q = Columns(ring, n_fsdp, w_query, w_qkv, 0, *scratch[0:2])
    columns_k = Columns(ring, n_fsdp, w_key, w_qkv, q_width, *scratch[2:4])
    columns_v = Columns(ring, n_fsdp, w_value, w_qkv, q_width + k_width, *scratch[4:6])
    columns_gate = Columns(ring, n_fsdp, w_gate, gu_out, 0, *scratch[6:8])
    columns_up = Columns(ring, n_fsdp, w_up, gu_out, ff, *scratch[8:10])
    rows_output = Rows(ring, n_fsdp, w_output, output_out, *scratch[10:12])
    rows_down = Rows(ring, n_fsdp, w_down, down_out, *scratch[12:14])
    square = Square(size)
    gathering = SquareGather(square, own, attn_in, *scratch[14:16])
    gathering_cot = SquareGather(square, cotangent, grad_out, *scratch[16:18])
    places = Places(ring, n_fsdp, all_small, starts, offsets, cosine, sine, places_ref)

    side = lax.rem(ring.row, 2)
    lane = lax.broadcasted_iota(jnp.int32, (1, 2 * depth), 1)
    mine = lax.div(lane, depth) == side
    small[...] = jnp.zeros_like(small)
    for row, part in enumerate((in_gain, post_gain)):
        part_row = part[...].astype(jnp.float32)
        small[row : row + 1] = jnp.where(mine, jnp.concatenate([part_row, part_row], axis=1), 0.0)
    small[2:3] = jnp.where(lane == 0, blocks[0, 0], jnp.where(lane == 1, blocks[0, 1], 0)).astype(jnp.float32)
    greet(near_devices(ring, n_fsdp))
    sharing = Spread(ring, n_fsdp, small, all_small, small_send, small_recv)
    sharing.begin()
    for columns in (columns_q, columns_k, columns_v):
        columns.begin()
    half = tokens // 2
    sharing.collect()
    for pair in range(size * n_fsdp // 2):
        member, chip = pair // (n_fsdp // 2), pair % (n_fsdp // 2)
        gains[:, pair * 128 : (pair + 1) * 128] = all_small[2 * chip, member] + all_small[2 * chip + 1, member]
    for part in range(SUBS):
        for way in range(2):
            start = way * half + part * (half // SUBS)
            place = slice(start, start + half // SUBS)
            rows = hidden[place].astype(jnp.float32)
            scale = lax.rsqrt(jnp.mean(rows * rows, axis=-1, keepdims=True) + EPS)
            own[place] = (rows * scale * gains[0:1]).astype(jnp.bfloat16)
            gathering.start(way, part)
    rows_output.begin()
    rows_down.begin()
    keep = pltpu.make_async_copy(own, attn_in.at[ring.me], local_sems.at[0])
    keep.start()
    keep_cot = pltpu.make_async_copy(cotangent, grad_out.at[ring.me], local_sems.at[1])
    keep_cot.start()
    gathering.first()
    places.fill()
    gathering.second()
    for columns in (columns_q, columns_k, columns_v):
        columns.spread()
    rows_output.relay()
    gathering.third()
    for columns in (columns_q, columns_k, columns_v):
        columns.relay()
    columns_gate.begin()
    columns_up.begin()
    rows_down.relay()
    for columns in (columns_q, columns_k, columns_v):
        columns.arrive()
    gathering.finish()
    keep.wait()
    save_in = pltpu.make_async_copy(attn_in, attn_in_out, local_sems.at[2])
    save_in.start()
    save_qkv = pltpu.make_async_copy(w_qkv, w_qkv_out, local_sems.at[3])
    save_qkv.start()
    width = hidden.shape[1]

    @pl.loop(0, size)
    def _(member):
        at = pl.ds(pl.multiple_of(member * tokens, tokens), tokens)
        product = jnp.dot(
            attn_in[member], w_qkv[...].reshape(width, w_qkv.shape[3]), preferred_element_type=jnp.float32
        )
        raw[at, :] = product[:, : q_width + head]
        for which in range(q_heads + 1):
            values_raw = product[:, which * head : (which + 1) * head]
            gain = q_gain if which < q_heads else k_gain
            turned = turn(values_raw * head_norm(values_raw) * gain[...].astype(jnp.float32), cosine[at, :], sine[at, :])
            if which < q_heads:
                queries[member, which] = (turned * head**-0.5).astype(jnp.bfloat16)
            else:
                keys[at, :] = turned.astype(jnp.bfloat16)
        fresh = product[:, q_width + head :]
        values[at, :] = fresh.astype(jnp.bfloat16)
        values_t[:, at] = fresh.T.astype(jnp.bfloat16)

    @pl.loop(0, size)
    def _(member):
        visible = places.visible(member)
        for which in range(q_heads):
            scores = lax.dot_general(
                keys[...], queries[member, which], (((1,), (1,)), ((), ())), preferred_element_type=jnp.float32
            )
            scores = jnp.where(visible, scores, -1e30)
            peak = jnp.max(scores, axis=0, keepdims=True)
            weights = jnp.exp(scores - peak)
            total = jnp.sum(weights, axis=0, keepdims=True)
            probs = (weights * (1.0 / total)).astype(jnp.bfloat16)
            mixed = jnp.dot(values_t[...], probs, preferred_element_type=jnp.float32)
            attn[member, :, which * head : (which + 1) * head] = mixed.T.astype(jnp.bfloat16)
            log_totals[member, which : which + 1, :] = peak + jnp.log(total)

    saves = [
        pltpu.make_async_copy(source, target, local_sems.at[4 + which])
        for which, (source, target) in enumerate(
            ((raw, raw_out), (queries, queries_out), (keys, keys_out), (values, values_out), (attn, attn_out))
        )
    ]
    for save in saves:
        save.start()
    for part in range(SUBS):
        for way in range(2):
            gathering_cot.start(way, part)
    columns_gate.spread()
    gathering_cot.first()
    columns_up.spread()
    gathering_cot.second()
    gathering_cot.third()
    columns_gate.relay()
    columns_up.relay()
    gathering_cot.finish()
    sharing.finish()
    columns_gate.arrive()
    columns_up.arrive()
    for columns in (columns_q, columns_k, columns_v, columns_gate, columns_up):
        columns.finish()
    rows_output.finish()
    rows_down.finish()
    keep_cot.wait()
    for save in saves + [save_in, save_qkv]:
        save.wait()


def fore(blocks, in_gain, post_gain, tables, q_gain, k_gain, hidden, w_query, w_key, w_value, w_output, w_gate, w_up, w_down, cotangent):
    size, n_fsdp = lax.axis_size("ctx"), lax.axis_size("fsdp")
    rows, width = hidden.shape
    depth = w_query.shape[0]
    head = q_gain.shape[0]
    q_heads = w_query.shape[1] // size // head
    everyone = size * rows
    qkv_share = (w_query.shape[1] + w_key.shape[1] + w_value.shape[1]) // size
    gu_share = (w_gate.shape[1] + w_up.shape[1]) // size
    f32, bf16 = jnp.float32, jnp.bfloat16
    return pl.pallas_call(
        functools.partial(fore_kernel, size, n_fsdp, q_heads),
        out_shape=[
            jax.ShapeDtypeStruct((n_fsdp, size, 8, 2 * depth), f32),
            jax.ShapeDtypeStruct((8, width), f32),
            jax.ShapeDtypeStruct((size, q_heads, rows), f32),
            jax.ShapeDtypeStruct((everyone, (q_heads + 1) * head), f32),
            jax.ShapeDtypeStruct((size, q_heads, rows, head), bf16),
            jax.ShapeDtypeStruct((everyone, head), bf16),
            jax.ShapeDtypeStruct((everyone, head), bf16),
            jax.ShapeDtypeStruct((size, rows, q_heads * head), bf16),
            jax.ShapeDtypeStruct((size, rows, width), bf16),
            jax.ShapeDtypeStruct((size, n_fsdp, depth, qkv_share), bf16),
            jax.ShapeDtypeStruct((n_fsdp,) + w_output.shape, bf16),
            jax.ShapeDtypeStruct((size, n_fsdp, depth, gu_share), bf16),
            jax.ShapeDtypeStruct((n_fsdp,) + w_down.shape, bf16),
            jax.ShapeDtypeStruct((size, rows, width), bf16),
        ],
        in_specs=[pl.BlockSpec(memory_space=pltpu.SMEM)] + [VMEM_SPEC] * 7 + [ANY_SPEC] * 8,
        out_specs=[VMEM_SPEC] * 3 + [ANY_SPEC] * 11,
        scratch_shapes=[
            pltpu.VMEM((8, 2 * depth), f32),
            pltpu.VMEM((rows, width), bf16),
            pltpu.VMEM((size, rows, width), bf16),
            pltpu.VMEM((size, n_fsdp, depth, qkv_share), bf16),
            pltpu.VMEM((everyone, head), f32),
            pltpu.VMEM((everyone, head), f32),
            pltpu.VMEM((everyone, head), f32),
            pltpu.VMEM((head, everyone), bf16),
            pltpu.VMEM((everyone, (q_heads + 1) * head), f32),
            pltpu.VMEM((size, q_heads, rows, head), bf16),
            pltpu.VMEM((everyone, head), bf16),
            pltpu.VMEM((everyone, head), bf16),
            pltpu.VMEM((size, rows, q_heads * head), bf16),
        ]
        + small_sems(size, n_fsdp)
        + [pltpu.SemaphoreType.DMA((9,))]
        + columns_sems(size) * 5
        + rows_sems() * 2
        + square_sems() * 2,
        compiler_params=params(2),
    )(
        blocks,
        in_gain.reshape(1, depth),
        post_gain.reshape(1, depth),
        *tables,
        q_gain.reshape(1, head),
        k_gain.reshape(1, head),
        hidden,
        w_query,
        w_key,
        w_value,
        w_output,
        w_gate,
        w_up,
        w_down,
        cotangent,
    )


def norm_pull(grad_normed, normed, scale):
    return scale * (grad_normed - normed * jnp.mean(grad_normed * normed, axis=-1, keepdims=True))


def feed_forward_kernel(
    size,
    n_fsdp,
    attn,
    w_output,
    hidden,
    gains,
    w_gu_in,
    w_down_in,
    cot_in,
    out_hidden,
    grad_gain,
    grad_mid_out,
    grad_branch,
    gu_total_out,
    down_out,
    w_gu,
    w_down,
    cot,
    load_sems,
    mid,
    own,
    mlp_in,
    inner,
    grad_gu,
    gu_part,
    down_part,
    grad_mid,
    gu_total,
    down_total,
    layer_terms,
    *scratch,
):
    loads = [
        pltpu.make_async_copy(source, target, load_sems.at[which])
        for which, (source, target) in enumerate(((w_gu_in, w_gu), (w_down_in, w_down), (cot_in, cot)))
    ]
    for load in loads:
        load.start()
    ring = Ring(size)
    greet(near_devices(ring, n_fsdp))
    half = own.shape[0] // 2
    ff = w_down.shape[0]
    out_sums, gather_sems_in = scratch[:5], scratch[5:7]
    layer_sums = (layer_terms,) + tuple(scratch[7:11])
    gather_sems_out, keep_sems = scratch[11:13], scratch[13]
    column_scratch = (scratch[14], None, gu_total, scratch[15], scratch[16])
    row_scratch = (scratch[17], None, scratch[18], scratch[19], scratch[20])

    first = SumRing(ring, row_terms(attn, w_output, out_sums[0]), *out_sums)
    first.run()
    gathering = GatherRing(ring, own, mlp_in, *gather_sems_in)
    for way, part, place in first.parts():
        total = first.result(way, part) + hidden[place].astype(jnp.float32)
        mid[place] = total
        scale = lax.rsqrt(jnp.mean(total * total, axis=-1, keepdims=True) + EPS)
        own[place] = (total * scale * gains[1:2]).astype(jnp.bfloat16)
        gathering.start(way, part)
    first.finish()
    keep = pltpu.make_async_copy(own, mlp_in.at[ring.me], keep_sems.at[0])
    keep.start()
    for load in loads:
        load.wait()

    def units(lines, members):
        cot_lines = jnp.concatenate([cot[members[way], way * half : (way + 1) * half] for way in range(2)], axis=0)

        @pl.loop(0, ff // UNITS)
        def _(tile):
            at = pl.multiple_of(tile * UNITS, UNITS)
            here, there = pl.ds(at, UNITS), pl.ds(pl.multiple_of(ff + at, UNITS), UNITS)
            gate = jnp.dot(lines, w_gu[:, here], preferred_element_type=jnp.float32)
            up = jnp.dot(lines, w_gu[:, there], preferred_element_type=jnp.float32)
            pulled = lax.dot_general(
                cot_lines, w_down[here, :], (((1,), (1,)), ((), ())), preferred_element_type=jnp.float32
            )
            sigmoid = 1.0 / (1.0 + jnp.exp(-gate))
            active = gate * sigmoid
            inner_new = (active * up).astype(jnp.bfloat16)
            gate_new = (pulled * up * sigmoid * (1.0 + gate * (1.0 - sigmoid))).astype(jnp.bfloat16)
            up_new = (pulled * active).astype(jnp.bfloat16)
            for way in range(2):
                place = slice(way * half, (way + 1) * half)
                inner[members[way], place, here] = inner_new[place]
                grad_gu[members[way], place, here] = gate_new[place]
                grad_gu[members[way], place, there] = up_new[place]

    def units_of(step):
        members = [ring.member(way, step) for way in range(2)]
        units(
            jnp.concatenate([mlp_in[members[way], way * half : (way + 1) * half] for way in range(2)], axis=0), members
        )

    units(own[...], [ring.me, ring.me])

    @pl.loop(1, size - 1)
    def _(step):
        gathering.step(step)
        units_of(step)

    third = SumRing(ring, row_terms_t(grad_gu, w_gu, out_sums[0]), *out_sums)
    third.begin()
    gathering.finish()
    keep.wait()
    units_of(size - 1)
    rows_all = size * 2 * half
    width = w_gu.shape[0]
    block = width // size

    def gu_tile(member):
        columns = pl.ds(pl.multiple_of(member * block, block), block)
        lines = mlp_in[:, :, columns].reshape(rows_all, block)

        @pl.loop(0, 2 * ff // TILE)
        def _(tile):
            there = pl.ds(pl.multiple_of(tile * TILE, TILE), TILE)
            product = lax.dot_general(
                lines,
                grad_gu[:, :, there].reshape(rows_all, TILE),
                (((0,), (0,)), ((), ())),
                preferred_element_type=jnp.float32,
            ).astype(jnp.bfloat16)
            for row in range(n_fsdp):
                gu_part[row, member, :, there] = product[row * (block // n_fsdp) : (row + 1) * (block // n_fsdp)]

    share = ff // n_fsdp

    def down_tile(tile):
        columns = pl.ds(pl.multiple_of(tile * UNITS, UNITS), UNITS)
        lines = cot[:, :, columns].reshape(rows_all, UNITS)
        product = lax.dot_general(
            inner[...].reshape(rows_all, ff), lines, (((0,), (0,)), ((), ())), preferred_element_type=jnp.float32
        ).astype(jnp.bfloat16)
        for row in range(n_fsdp):
            down_part[row, :, columns] = product[row * share : (row + 1) * share]

    gu_tile(0)
    third.second()
    gu_tile(1)

    @pl.loop(2, size - 1)
    def _(step):
        third.step(step)
        gu_tile(step)

    second = SumRing(ring, row_terms(inner, w_down, layer_sums[0]), *layer_sums)
    second.begin()
    gu_tile(size - 1)
    columns = RowGrads(ring, n_fsdp, gu_part, *column_scratch)
    rows = RowGrads(ring, n_fsdp, down_part, *row_scratch)
    columns.begin()
    third.last_terms()
    gathering = GatherRing(ring, own, grad_branch, *gather_sems_out)
    gain_sum = jnp.zeros_like(grad_gain)
    for way, part, place in third.parts():
        pulled = third.result(way, part)
        values = mid[place]
        scale = lax.rsqrt(jnp.mean(values * values, axis=-1, keepdims=True) + EPS)
        normed = values * scale
        gain_sum = gain_sum + jnp.sum(pulled * normed, axis=0, keepdims=True)
        total = cot[ring.me, place].astype(jnp.float32) + norm_pull(pulled * gains[1:2], normed, scale)
        grad_mid[place] = total
        own[place] = total.astype(jnp.bfloat16)
        gathering.start(way, part)
    grad_gain[...] = gain_sum
    keep = pltpu.make_async_copy(own, grad_branch.at[ring.me], keep_sems.at[1])
    keep.start()
    save_mid = pltpu.make_async_copy(grad_mid, grad_mid_out, keep_sems.at[2])
    save_mid.start()
    third.finish()
    second.second()
    gathering.step(1)
    columns.cross()

    @pl.loop(2, 4)
    def _(step):
        second.step(step)
        gathering.step(step)

        @pl.loop(0, width // UNITS // 2)
        def _(tile):
            down_tile((step - 2) * (width // UNITS // 2) + tile)

    rows.begin()
    second.step(4)
    gathering.step(4)
    rows.cross()

    @pl.loop(5, size - 1)
    def _(step):
        second.step(step)
        gathering.step(step)

    second.last_terms()
    down_total[...] = rows.result()
    save_down = pltpu.make_async_copy(down_total, down_out, keep_sems.at[3])
    save_down.start()
    gu_total[...] = columns.result().astype(jnp.bfloat16)
    save_gu = pltpu.make_async_copy(gu_total, gu_total_out, keep_sems.at[4])
    save_gu.start()
    for way, part, place in second.parts():
        out_hidden[place] = (mid[place] + second.result(way, part)).astype(jnp.bfloat16)
    gathering.finish()
    second.finish()
    columns.finish()
    rows.finish()
    for copy in (keep, save_mid, save_down, save_gu):
        copy.wait()


UNITS = 256


def feed_forward(attn, w_output, hidden, gains, w_gu, w_down, cotangent):
    size, n_fsdp = lax.axis_size("ctx"), lax.axis_size("fsdp")
    rows, width = hidden.shape
    ff = w_down.shape[0]
    depth = width // size // n_fsdp
    sums = sum_scratch(size, rows, width)
    return pl.pallas_call(
        functools.partial(feed_forward_kernel, size, n_fsdp),
        out_shape=[
            jax.ShapeDtypeStruct((rows, width), jnp.bfloat16),
            jax.ShapeDtypeStruct((1, width), jnp.float32),
            jax.ShapeDtypeStruct((rows, width), jnp.float32),
            jax.ShapeDtypeStruct((size, rows, width), jnp.bfloat16),
            jax.ShapeDtypeStruct((size, depth, 2 * ff), jnp.bfloat16),
            jax.ShapeDtypeStruct((ff // n_fsdp, width), jnp.float32),
        ],
        in_specs=[VMEM_SPEC] * 4 + [ANY_SPEC] * 3,
        out_specs=[VMEM_SPEC] * 2 + [ANY_SPEC] * 4,
        scratch_shapes=[
            pltpu.VMEM(w_gu.shape, jnp.bfloat16),
            pltpu.VMEM(w_down.shape, jnp.bfloat16),
            pltpu.VMEM((size, rows, width), jnp.bfloat16),
            pltpu.SemaphoreType.DMA((3,)),
            pltpu.VMEM((rows, width), jnp.float32),
            pltpu.VMEM((rows, width), jnp.bfloat16),
            pltpu.VMEM((size, rows, width), jnp.bfloat16),
            pltpu.VMEM((size, rows, ff), jnp.bfloat16),
            pltpu.VMEM((size, rows, 2 * ff), jnp.bfloat16),
            pltpu.VMEM((n_fsdp, size, depth, 2 * ff), jnp.bfloat16),
            pltpu.VMEM((n_fsdp, ff // n_fsdp, width), jnp.bfloat16),
            pltpu.VMEM((rows, width), jnp.float32),
            pltpu.VMEM((size, depth, 2 * ff), jnp.bfloat16),
            pltpu.VMEM((ff // n_fsdp, width), jnp.float32),
            pltpu.VMEM((2, rows // 2, width), jnp.float32),
        ]
        + sums
        + gather_sems(size)
        + sums[1:]
        + gather_sems(size)
        + [pltpu.SemaphoreType.DMA((5,))]
        + [pltpu.VMEM((2, size, depth, 2 * ff), jnp.bfloat16)]
        + row_grads_sems()
        + [pltpu.VMEM((2, ff // n_fsdp, width), jnp.bfloat16), pltpu.VMEM((ff // n_fsdp, width), jnp.bfloat16)]
        + row_grads_sems(),
        compiler_params=params(5),
    )(
        attn,
        w_output,
        hidden,
        gains,
        w_gu,
        w_down,
        cotangent,
    )


def back_kernel(
    size,
    n_fsdp,
    all_blocks,
    starts,
    offsets,
    q_gain,
    k_gain,
    gains,
    post_sum,
    log_totals,
    *refs,
):
    sources, refs = refs[:11], refs[11:]
    gu_total = refs[0]
    grad_hidden, gains_out, output_out, gu_out, qkv_out = refs[1:6]
    targets, refs = refs[6:17], refs[17:]
    grad_branch, attn, w_output, queries, keys, values, raw, attn_in, w_qkv, hidden, grad_mid = targets
    load_sems, cosine, sine, places_ref, keys_t, grad_keys, grad_values, head_sums, grads, qkv_part, output_part = refs[:11]
    small, small_ctx, small_part, small_fsdp, small_send, small_recv, in_sum = refs[11:18]
    scratch = refs[18:]
    loads = [
        pltpu.make_async_copy(source, target, load_sems.at[which])
        for which, (source, target) in enumerate(zip(sources, targets))
    ]
    for load in loads:
        load.start()
    sums = scratch[:5]
    ring = Ring(size)
    greet(near_devices(ring, n_fsdp))
    total = scratch[8]
    columns = RowGrads(ring, n_fsdp, qkv_part, scratch[5], None, *scratch[6:8], scratch[9])
    dealing = Deal(ring, total, qkv_out, *scratch[10:12])
    rows = RowGrads(ring, n_fsdp, output_part, scratch[12], None, *scratch[13:16])
    gu_dealing = Deal(ring, gu_total, gu_out, *scratch[16:18])
    gu_dealing.begin()
    places = Places(ring, n_fsdp, all_blocks, starts, offsets, cosine, sine, places_ref)
    places.fill()
    head = q_gain.shape[1]
    q_heads = queries.shape[1]
    tokens = attn_in.shape[1]
    everyone = size * tokens
    width = attn_in.shape[2]
    q_width = q_heads * head
    grad_keys[...] = jnp.zeros_like(grad_keys)
    grad_values[...] = jnp.zeros_like(grad_values)
    head_sums[...] = jnp.zeros_like(head_sums)
    for load in loads[:3]:
        load.wait()

    def through_head(pulled, at, which, gain_here):
        turned = turn(pulled, cosine[at, :], -sine[at, :])
        values_raw = raw[at, which * head : (which + 1) * head]
        scale = head_norm(values_raw)
        unit = values_raw * scale
        kind = 0 if which < q_heads else 1
        head_sums[kind : kind + 1] = head_sums[kind : kind + 1] + jnp.sum(turned * unit, axis=0, keepdims=True)
        return norm_pull(turned * gain_here[...].astype(jnp.float32), unit, scale).astype(jnp.bfloat16)

    def output_tile(tile):
        there = pl.ds(pl.multiple_of(tile * TILE, TILE), TILE)
        product = lax.dot_general(
            attn[...].reshape(everyone, q_width),
            grad_branch[:, :, there].reshape(everyone, TILE),
            (((0,), (0,)), ((), ())),
            preferred_element_type=jnp.float32,
        ).astype(jnp.bfloat16)
        share = q_width // n_fsdp
        for row in range(n_fsdp):
            output_part[row, :, there] = product[row * share : (row + 1) * share]

    @pl.loop(0, width // TILE)
    def _(tile):
        output_tile(tile)

    rows.begin()
    for load in loads[3:]:
        load.wait()
    keys_t[...] = keys[...].astype(jnp.float32).T.astype(jnp.bfloat16)

    @pl.loop(0, size)
    def _(member):
        at = pl.ds(pl.multiple_of(member * tokens, tokens), tokens)
        grad_attn = lax.dot_general(
            grad_branch[member], w_output[...], (((1,), (1,)), ((), ())), preferred_element_type=jnp.float32
        ).astype(jnp.bfloat16)
        visible = places.visible(member)
        for which in range(q_heads):
            lanes = slice(which * head, (which + 1) * head)
            pulled = grad_attn[:, lanes]
            query = queries[member, which]
            scores = lax.dot_general(keys[...], query, (((1,), (1,)), ((), ())), preferred_element_type=jnp.float32)
            probs = jnp.where(visible, jnp.exp(scores - log_totals[member, which : which + 1, :]), 0.0)
            grad_probs = lax.dot_general(
                values[...], pulled, (((1,), (1,)), ((), ())), preferred_element_type=jnp.float32
            )
            delta = jnp.sum(probs * grad_probs, axis=0, keepdims=True)
            grad_scores = (probs * (grad_probs - delta)).astype(jnp.bfloat16)
            grad_keys[...] = grad_keys[...] + jnp.dot(grad_scores, query, preferred_element_type=jnp.float32)
            grad_values[...] = grad_values[...] + jnp.dot(
                probs.astype(jnp.bfloat16), pulled, preferred_element_type=jnp.float32
            )
            grad_query = jnp.dot(keys_t[...], grad_scores, preferred_element_type=jnp.float32).T
            grads[member, :, lanes] = through_head(grad_query * head**-0.5, at, which, q_gain)

    rows.cross()

    @pl.loop(0, size)
    def _(member):
        at = pl.ds(pl.multiple_of(member * tokens, tokens), tokens)
        grads[member, :, q_width : q_width + head] = through_head(grad_keys[at, :], at, q_heads, k_gain)
        grads[member, :, q_width + head :] = grad_values[at, :].astype(jnp.bfloat16)

    block = width // size

    def qkv_tile(member):
        lines = attn_in[:, :, pl.ds(pl.multiple_of(member * block, block), block)].reshape(everyone, block)
        product = lax.dot_general(
            lines,
            grads[...].reshape(everyone, grads.shape[2]),
            (((0,), (0,)), ((), ())),
            preferred_element_type=jnp.float32,
        ).astype(jnp.bfloat16)
        for row in range(n_fsdp):
            qkv_part[row, member] = product[row * (block // n_fsdp) : (row + 1) * (block // n_fsdp)]

    in_sum[...] = jnp.zeros_like(in_sum)
    summing = SquareSum(Square(size), block_terms_t(grads, w_qkv, sums[0], attn_in, in_sum), *sums)
    summing.begin()

    @pl.loop(0, size // 2)
    def _(member):
        qkv_tile(member)

    summing.first()

    @pl.loop(size // 2, size)
    def _(member):
        qkv_tile(member)

    columns.begin()
    chips = n_fsdp // 2
    for pair in range(size * chips):
        lanes = slice(pair * 128, (pair + 1) * 128)
        small[pair // chips, pair % chips, 0:1] = in_sum[:, lanes] / gains[0:1, lanes]
        small[pair // chips, pair % chips, 1:2] = post_sum[:, lanes]
        small[pair // chips, pair % chips, 2:4] = head_sums[0:2]
        small[pair // chips, pair % chips, 4:8] = jnp.zeros((4, 128), jnp.float32)
    sharing = SmallSum(ring, n_fsdp, small, small_ctx, small_part, small_fsdp, small_send, small_recv)
    sharing.begin()
    summing.second()
    columns.cross()
    summing.third()
    total[...] = columns.result().astype(jnp.bfloat16)
    dealing.begin()
    output_out[...] = rows.result()
    sharing.cross()
    for way, part, place in summing.parts():
        pulled = summing.result(way, part)
        values_in = hidden[place].astype(jnp.float32)
        scale = lax.rsqrt(jnp.mean(values_in * values_in, axis=-1, keepdims=True) + EPS)
        normed = values_in * scale
        grad_hidden[place] = grad_mid[place] + norm_pull(pulled * gains[0:1], normed, scale)
    gains_out[...] = sharing.result()
    sharing.finish()
    summing.finish()
    columns.finish()
    rows.finish()
    dealing.finish()
    gu_dealing.finish()


def back(
    all_small,
    tables,
    q_gain,
    k_gain,
    raw,
    queries,
    keys,
    values,
    attn,
    log_totals,
    hidden,
    grad_mid,
    gains,
    post_sum,
    gu_total,
    grad_branch,
    w_output,
    attn_in,
    w_qkv,
):
    size, n_fsdp = lax.axis_size("ctx"), lax.axis_size("fsdp")
    rows, width = hidden.shape
    head = q_gain.shape[0]
    everyone = size * rows
    share = w_qkv.shape[1]
    depth = width // size // n_fsdp
    q_width = attn.shape[2]
    f32, bf16 = jnp.float32, jnp.bfloat16
    loaded = [grad_branch, attn, w_output, queries, keys, values, raw, attn_in, w_qkv, hidden, grad_mid]
    return pl.pallas_call(
        functools.partial(back_kernel, size, n_fsdp),
        out_shape=[
            jax.ShapeDtypeStruct((rows, width), f32),
            jax.ShapeDtypeStruct((8, 128), f32),
            jax.ShapeDtypeStruct((q_width // n_fsdp, width), f32),
            jax.ShapeDtypeStruct(gu_total.shape, bf16),
            jax.ShapeDtypeStruct((size, depth, share), bf16),
        ],
        in_specs=[VMEM_SPEC] * 8 + [ANY_SPEC] * 12,
        out_specs=[VMEM_SPEC] * 3 + [ANY_SPEC] * 2,
        scratch_shapes=[pltpu.VMEM(array.shape, array.dtype) for array in loaded]
        + [
            pltpu.SemaphoreType.DMA((len(loaded),)),
            pltpu.VMEM((everyone, head), f32),
            pltpu.VMEM((everyone, head), f32),
            pltpu.VMEM((everyone, head), f32),
            pltpu.VMEM((head, everyone), bf16),
            pltpu.VMEM((everyone, head), f32),
            pltpu.VMEM((everyone, head), f32),
            pltpu.VMEM((8, head), f32),
            pltpu.VMEM((size, rows, share), bf16),
            pltpu.VMEM((n_fsdp, size, depth, share), bf16),
            pltpu.VMEM((n_fsdp, q_width // n_fsdp, width), bf16),
            pltpu.VMEM((size, n_fsdp // 2, 8, 128), f32),
            pltpu.VMEM((size, n_fsdp // 2, 8, 128), f32),
            pltpu.VMEM((n_fsdp // 2, 8, 128), f32),
            pltpu.VMEM((n_fsdp, 8, 128), f32),
        ]
        + small_sems(size, n_fsdp)
        + [pltpu.VMEM((1, width), f32)]
        + square_sum_scratch(rows, width)
        + [
            pltpu.VMEM((2, size, depth, share), bf16),
            pltpu.VMEM((size, depth, share), bf16),
            pltpu.SemaphoreType.DMA((3,)),
            pltpu.VMEM((size, depth, share), bf16),
            pltpu.SemaphoreType.DMA((3,)),
        ]
        + deal_sems(size)
        + [
            pltpu.VMEM((2, q_width // n_fsdp, width), bf16),
            pltpu.VMEM((q_width // n_fsdp, width), bf16),
        ]
        + row_grads_sems()
        + deal_sems(size),
        compiler_params=params(6),
    )(
        all_small,
        *tables,
        q_gain.reshape(1, head),
        k_gain.reshape(1, head),
        gains,
        post_sum,
        log_totals,
        *loaded,
        gu_total,
    )


def finish_kernel(size, gu, qkv, gain_sums, *refs):
    kept, outs, refs = refs[:4], refs[4:9], refs[9:]
    kept_out, gains_out, refs = refs[:4], refs[4:8], refs[8:]
    gu_in, qkv_in, load_sems, wide, save_sems, keep_sems, held = refs[0], refs[1], refs[2], refs[3:8], refs[8], refs[9], refs[10:]
    share = size // 2
    loads = []
    for part in range(2):
        members = pl.ds(part * share, share)
        loads.append(
            (
                pltpu.make_async_copy(gu.at[members], gu_in.at[members], load_sems.at[0, part]),
                pltpu.make_async_copy(qkv.at[members], qkv_in.at[members], load_sems.at[1, part]),
            )
        )
    for pair in loads:
        for load in pair:
            load.start()
    holds = [
        pltpu.make_async_copy(source, target, keep_sems.at[0, which])
        for which, (source, target) in enumerate(zip(kept, held))
    ]
    for hold in holds:
        hold.start()
    side = lax.rem(lax.axis_index("fsdp"), 2)
    depth = gains_out[0].shape[1]
    for row, out in enumerate(gains_out[:2]):
        out[...] = jnp.where(side == 0, gain_sums[row : row + 1, :depth], gain_sums[row : row + 1, depth:])
    for row, out in enumerate(gains_out[2:]):
        out[...] = gain_sums[2 + row : 3 + row]
    saves = []
    for part in range(2):
        for load in loads[part]:
            load.wait()
        which = 0
        for arrived, count in ((gu_in, 2), (qkv_in, 3)):
            start = 0
            for _ in range(count):
                width = wide[which].shape[1] // size
                for member in range(part * share, (part + 1) * share):
                    wide[which][:, member * width : (member + 1) * width] = arrived[
                        member, :, start : start + width
                    ].astype(jnp.float32)
                columns = pl.ds(part * share * width, share * width)
                save = pltpu.make_async_copy(
                    wide[which].at[:, columns], outs[which].at[:, columns], save_sems.at[which, part]
                )
                save.start()
                saves.append(save)
                start += width
                which += 1
    for which, hold in enumerate(holds):
        hold.wait()
        save = pltpu.make_async_copy(held[which], kept_out[which], keep_sems.at[1, which])
        save.start()
        saves.append(save)
    for save in saves:
        save.wait()


def finish(gu, qkv, kept, gain_sums, widths):
    size = lax.axis_size("ctx")
    depth = gu.shape[1]
    f32 = jnp.float32
    wide = [(depth, width) for width in widths]
    return pl.pallas_call(
        functools.partial(finish_kernel, size),
        out_shape=[jax.ShapeDtypeStruct(shape, f32) for shape in wide]
        + [jax.ShapeDtypeStruct(array.shape, array.dtype) for array in kept]
        + [jax.ShapeDtypeStruct((1, depth), f32)] * 2
        + [jax.ShapeDtypeStruct((1, 128), f32)] * 2,
        in_specs=[ANY_SPEC] * 2 + [VMEM_SPEC] + [ANY_SPEC] * len(kept),
        out_specs=[ANY_SPEC] * (len(wide) + len(kept)) + [VMEM_SPEC] * 4,
        scratch_shapes=[
            pltpu.VMEM(gu.shape, gu.dtype),
            pltpu.VMEM(qkv.shape, qkv.dtype),
            pltpu.SemaphoreType.DMA((2, 2)),
        ]
        + [pltpu.VMEM(shape, f32) for shape in wide]
        + [pltpu.SemaphoreType.DMA((len(wide), 2)), pltpu.SemaphoreType.DMA((2, len(kept)))]
        + [pltpu.VMEM(array.shape, array.dtype) for array in kept],
        compiler_params=pltpu.CompilerParams(vmem_limit_bytes=62 * 1024 * 1024),
    )(gu, qkv, gain_sums, *kept)


def tp_body(
    hidden_in,
    block_of,
    in_gain,
    w_query,
    w_key,
    w_value,
    w_output,
    q_gain,
    k_gain,
    post_gain,
    w_gate,
    w_up,
    w_down,
    cotangent,
):
    seq_count, tok_rows, model_width = hidden_in.shape
    n_ctx = lax.axis_size("ctx")
    block_rows = tok_rows // 2
    rows = seq_count * tok_rows
    head_dim = q_gain.shape[0]
    hidden = hidden_in.reshape(rows, model_width)
    cot_local = cotangent.reshape(rows, model_width)
    depth = w_query.shape[0]

    tables = rotation_tables(2 * n_ctx, block_rows, head_dim)
    (
        all_small,
        gains,
        log_totals,
        raw,
        queries,
        keys,
        values,
        attn,
        attn_in,
        mine_qkv,
        mine_output,
        mine_gu,
        mine_down,
        grad_out,
    ) = fore(
        block_of,
        in_gain,
        post_gain,
        tables,
        q_gain,
        k_gain,
        hidden,
        w_query,
        w_key,
        w_value,
        w_output,
        w_gate,
        w_up,
        w_down,
        cot_local,
    )
    mine_qkv = mine_qkv.reshape(model_width, -1)
    mine_output = mine_output.reshape(-1, model_width)
    output, post_sum, grad_mid, grad_branch, gu_total, part_down = feed_forward(
        attn, mine_output, hidden, gains, mine_gu.reshape(model_width, -1), mine_down.reshape(-1, model_width), grad_out
    )
    grad_hidden, gain_sums, part_output, gu_sums, qkv_sums = back(
        all_small,
        tables,
        q_gain,
        k_gain,
        raw,
        queries,
        keys,
        values,
        attn,
        log_totals,
        hidden,
        grad_mid,
        gains,
        post_sum,
        gu_total,
        grad_branch,
        mine_output,
        attn_in,
        mine_qkv,
    )
    (
        part_gate,
        part_up,
        part_query,
        part_key,
        part_value,
        grad_hidden,
        output,
        part_down,
        part_output,
        part_in,
        part_post,
        sum_q_gain,
        sum_k_gain,
    ) = finish(
        gu_sums,
        qkv_sums,
        (grad_hidden, output, part_down, part_output),
        gain_sums,
        [weight.shape[1] for weight in (w_gate, w_up, w_query, w_key, w_value)],
    )
    return (
        output.reshape(seq_count, tok_rows, model_width),
        grad_hidden.reshape(seq_count, tok_rows, model_width),
        part_in.reshape(-1),
        part_query,
        part_key,
        part_value,
        part_output,
        sum_q_gain.reshape(-1),
        sum_k_gain.reshape(-1),
        part_post.reshape(-1),
        part_gate,
        part_up,
        part_down,
    )


def body(hidden_in, block_of, in_gain, w_query, w_key, w_value, w_output, q_gain, *rest):
    kv_heads = w_key.shape[1] // q_gain.shape[0]
    plan = tp_body if kv_heads == lax.axis_size("ctx") == 8 else gathered_weights_body
    return plan(hidden_in, block_of, in_gain, w_query, w_key, w_value, w_output, q_gain, *rest)


def solution(mesh):
    return jax.shard_map(
        body,
        mesh=mesh,
        in_specs=(
            P("fsdp", "ctx", None),
            P("fsdp", "ctx"),
            P(("ctx", "fsdp")),
            P(("ctx", "fsdp"), None),
            P(("ctx", "fsdp"), None),
            P(("ctx", "fsdp"), None),
            P(("ctx", "fsdp"), None),
            P(),
            P(),
            P(("ctx", "fsdp")),
            P(("ctx", "fsdp"), None),
            P(("ctx", "fsdp"), None),
            P(("ctx", "fsdp"), None),
            P("fsdp", "ctx", None),
        ),
        out_specs=(
            P("fsdp", "ctx", None),
            P("fsdp", "ctx", None),
            P(("ctx", "fsdp")),
            P(("ctx", "fsdp"), None),
            P(("ctx", "fsdp"), None),
            P(("ctx", "fsdp"), None),
            P(("ctx", "fsdp"), None),
            P(),
            P(),
            P(("ctx", "fsdp")),
            P(("ctx", "fsdp"), None),
            P(("ctx", "fsdp"), None),
            P(("ctx", "fsdp"), None),
        ),
        check_vma=False,
    )
```

```python
import functools
import math

import jax
import jax.numpy as jnp
import numpy as np
from jax import lax
from jax.experimental import pallas as pl
from jax.experimental.pallas import tpu as pltpu
from jax.sharding import PartitionSpec as P

EPS = 1e-06
THETA = 1000000.0


def rope_tables(positions, width):
    half_width = width // 2
    inverse = THETA ** (-(jnp.arange(half_width, dtype=jnp.float32) * 2.0 / width))
    angles = positions.astype(jnp.float32)[:, None] * inverse[None, :]
    return (jnp.cos(angles), jnp.sin(angles))


def rotate(values, cosine, sine):
    half_width = values.shape[-1] // 2
    first = values[..., :half_width]
    second = values[..., half_width:]
    cos_wide = cosine[:, None, :]
    sin_wide = sine[:, None, :]
    return jnp.concatenate(
        [first * cos_wide - second * sin_wide, second * cos_wide + first * sin_wide], axis=-1
    )


def norm_back(grad_normed, normed, scale):
    return scale * (grad_normed - normed * jnp.mean(grad_normed * normed, axis=-1, keepdims=True))


def gathered_weights_body(
    hidden_in,
    block_of,
    in_gain,
    w_query,
    w_key,
    w_value,
    w_output,
    q_gain,
    k_gain,
    post_gain,
    w_gate,
    w_up,
    w_down,
    cotangent,
):
    seq_count = hidden_in.shape[0]
    tok_rows = hidden_in.shape[1]
    flat_rows = seq_count * tok_rows
    model_width = hidden_in.shape[2]
    block_rows = tok_rows // 2
    block_total = 2 * lax.axis_size("ctx")
    seq_len = block_total * block_rows
    head_dim = q_gain.shape[0]
    q_heads = w_query.shape[1] // head_dim
    kv_heads = w_key.shape[1] // head_dim
    group_size = q_heads // kv_heads
    tile_blocks = math.gcd(block_total, max(1, 512 // block_rows))
    tile_rows = tile_blocks * block_rows
    q_scale = head_dim ** (-0.5)
    contract_rows = (((0,), (0,)), ((), ()))
    contract_cols = (((1,), (1,)), ((), ()))
    offsets = jnp.arange(block_rows, dtype=jnp.int32)
    positions = (block_of[:, :, None] * block_rows + offsets[None, None, :]).reshape(flat_rows)
    cosine, sine = rope_tables(positions, head_dim)
    residual = hidden_in.reshape(flat_rows, model_width).astype(jnp.float32)
    full_in_gain, full_query, full_key, full_value, full_output = (
        lax.all_gather(in_gain, ("ctx", "fsdp"), axis=0, tiled=True),
        lax.all_gather(w_query, ("ctx", "fsdp"), axis=0, tiled=True),
        lax.all_gather(w_key, ("ctx", "fsdp"), axis=0, tiled=True),
        lax.all_gather(w_value, ("ctx", "fsdp"), axis=0, tiled=True),
        lax.all_gather(w_output, ("ctx", "fsdp"), axis=0, tiled=True),
    )
    in_scale = lax.rsqrt(jnp.mean(residual * residual, axis=-1, keepdims=True) + EPS)
    in_normed = residual * in_scale
    attn_in = (in_normed * full_in_gain.astype(jnp.float32)).astype(jnp.bfloat16)
    q_raw = jnp.dot(attn_in, full_query, preferred_element_type=jnp.float32).reshape(
        flat_rows, q_heads, head_dim
    )
    k_raw = jnp.dot(attn_in, full_key, preferred_element_type=jnp.float32).reshape(
        flat_rows, kv_heads, head_dim
    )
    v_local = jnp.dot(attn_in, full_value, preferred_element_type=jnp.float32).astype(jnp.bfloat16)
    q_rms = lax.rsqrt(jnp.mean(q_raw * q_raw, axis=-1, keepdims=True) + EPS)
    q_unit = q_raw * q_rms
    queries = (rotate(q_unit * q_gain.astype(jnp.float32), cosine, sine) * q_scale).astype(
        jnp.bfloat16
    )
    k_rms = lax.rsqrt(jnp.mean(k_raw * k_raw, axis=-1, keepdims=True) + EPS)
    k_unit = k_raw * k_rms
    keys_local = rotate(k_unit * k_gain.astype(jnp.float32), cosine, sine).astype(jnp.bfloat16)
    all_keys, all_values, all_slots = (
        lax.all_gather(
            keys_local.reshape(seq_count, tok_rows, kv_heads * head_dim), "ctx", axis=1, tiled=True
        ),
        lax.all_gather(
            v_local.reshape(seq_count, tok_rows, kv_heads * head_dim), "ctx", axis=1, tiled=True
        ),
        lax.all_gather(block_of, "ctx", axis=1, tiled=True),
    )

    def tile_scores(query_tile, key_tile, query_pos, step):
        scores = jnp.einsum(
            "qhgd,khd->hgqk", query_tile, key_tile, preferred_element_type=jnp.float32
        )
        key_pos = step * tile_rows + jnp.arange(tile_rows, dtype=jnp.int32)
        visible = key_pos[None, :] <= query_pos[:, None]
        return (scores, visible)

    def sequence_tables(seq):
        key_blocks = all_keys[seq].reshape(block_total, block_rows, kv_heads, head_dim)
        value_blocks = all_values[seq].reshape(block_total, block_rows, kv_heads, head_dim)
        block_index = (
            jnp.zeros((block_total,), jnp.int32)
            .at[all_slots[seq]]
            .set(jnp.arange(block_total, dtype=jnp.int32))
        )
        return (key_blocks, value_blocks, block_index)

    def tile_index(block_index, step):
        return lax.dynamic_slice_in_dim(block_index, step * tile_blocks, tile_blocks)

    def fetch(table, block_index, step):
        return jnp.take(table, tile_index(block_index, step), axis=0).reshape(
            tile_rows, kv_heads, head_dim
        )

    log_totals = []
    attn_parts = []
    seq = 0
    key_blocks, value_blocks, block_index = sequence_tables(seq)
    for which in range(2):
        slot = 2 * seq + which
        query_tile = queries[slot * block_rows : (slot + 1) * block_rows].reshape(
            block_rows, kv_heads, group_size, head_dim
        )
        query_pos = positions[slot * block_rows : (slot + 1) * block_rows]
        tile_count = block_of[seq, which] // tile_blocks + 1

        def max_step(step, carry):
            running_max, running_sum = carry
            scores, visible = tile_scores(
                query_tile, fetch(key_blocks, block_index, step), query_pos, step
            )
            scores = jnp.where(visible, scores, -1e30)
            new_max = jnp.maximum(running_max, jnp.max(scores, axis=-1))
            running_sum = running_sum * jnp.exp(running_max - new_max) + jnp.sum(
                jnp.exp(scores - new_max[..., None]), axis=-1
            )
            return (new_max, running_sum)

        start_max = jnp.full((kv_heads, group_size, block_rows), -1e30, jnp.float32)
        start_sum = jnp.zeros((kv_heads, group_size, block_rows), jnp.float32)
        running_max, running_sum = lax.fori_loop(0, tile_count, max_step, (start_max, start_sum))
        log_total = running_max + jnp.log(running_sum)

        def value_step(step, total):
            scores, visible = tile_scores(
                query_tile, fetch(key_blocks, block_index, step), query_pos, step
            )
            probs = jnp.where(visible, jnp.exp(scores - log_total[..., None]), 0.0)
            return total + jnp.einsum(
                "hgqk,khd->qhgd",
                probs.astype(jnp.bfloat16),
                fetch(value_blocks, block_index, step),
                preferred_element_type=jnp.float32,
            )

        attn_part = lax.fori_loop(
            0,
            tile_count,
            value_step,
            jnp.zeros((block_rows, kv_heads, group_size, head_dim), jnp.float32),
        )
        log_totals.append(log_total)
        attn_parts.append(attn_part)
    attn_full = jnp.concatenate(attn_parts, axis=0)
    attn_bf = attn_full.reshape(flat_rows, q_heads * head_dim).astype(jnp.bfloat16)
    branch = jnp.dot(attn_bf, full_output, preferred_element_type=jnp.float32)
    hidden_mid = residual + branch
    full_post, full_gate, full_up, full_down = (
        lax.all_gather(post_gain, ("ctx", "fsdp"), axis=0, tiled=True),
        lax.all_gather(w_gate, ("ctx", "fsdp"), axis=0, tiled=True),
        lax.all_gather(w_up, ("ctx", "fsdp"), axis=0, tiled=True),
        lax.all_gather(w_down, ("ctx", "fsdp"), axis=0, tiled=True),
    )
    post_scale = lax.rsqrt(jnp.mean(hidden_mid * hidden_mid, axis=-1, keepdims=True) + EPS)
    post_normed = hidden_mid * post_scale
    mlp_in = (post_normed * full_post.astype(jnp.float32)).astype(jnp.bfloat16)
    gate_pre = jnp.dot(mlp_in, full_gate, preferred_element_type=jnp.float32)
    up_pre = jnp.dot(mlp_in, full_up, preferred_element_type=jnp.float32)
    sigmoid_gate = jax.nn.sigmoid(gate_pre)
    activated = gate_pre * sigmoid_gate
    inner = (activated * up_pre).astype(jnp.bfloat16)
    mlp_out = jnp.dot(inner, full_down, preferred_element_type=jnp.float32)
    output = (hidden_mid + mlp_out).astype(jnp.bfloat16)
    full_post, full_gate, full_up, full_down = (
        lax.all_gather(post_gain, ("ctx", "fsdp"), axis=0, tiled=True),
        lax.all_gather(w_gate, ("ctx", "fsdp"), axis=0, tiled=True),
        lax.all_gather(w_up, ("ctx", "fsdp"), axis=0, tiled=True),
        lax.all_gather(w_down, ("ctx", "fsdp"), axis=0, tiled=True),
    )
    grad_out = cotangent.reshape(flat_rows, model_width)
    grad_down = lax.dot_general(inner, grad_out, contract_rows, preferred_element_type=jnp.float32)
    part_down = lax.psum_scatter(grad_down, ("ctx", "fsdp"), scatter_dimension=0, tiled=True)
    grad_inner = lax.dot_general(
        grad_out, full_down, contract_cols, preferred_element_type=jnp.float32
    )
    grad_gate_pre = (
        grad_inner * up_pre * sigmoid_gate * (1.0 + gate_pre * (1.0 - sigmoid_gate))
    ).astype(jnp.bfloat16)
    grad_up_pre = (grad_inner * activated).astype(jnp.bfloat16)
    grad_gate = lax.dot_general(
        mlp_in, grad_gate_pre, contract_rows, preferred_element_type=jnp.float32
    )
    grad_up = lax.dot_general(
        mlp_in, grad_up_pre, contract_rows, preferred_element_type=jnp.float32
    )
    grad_mlp_in = lax.dot_general(
        grad_gate_pre, full_gate, contract_cols, preferred_element_type=jnp.float32
    ) + lax.dot_general(grad_up_pre, full_up, contract_cols, preferred_element_type=jnp.float32)
    grad_post_gain = jnp.sum(grad_mlp_in * post_normed, axis=0)
    grad_mid = grad_out.astype(jnp.float32) + norm_back(
        grad_mlp_in * full_post.astype(jnp.float32), post_normed, post_scale
    )
    part_post, part_gate, part_up = (
        lax.psum_scatter(grad_post_gain, ("ctx", "fsdp"), scatter_dimension=0, tiled=True),
        lax.psum_scatter(grad_gate, ("ctx", "fsdp"), scatter_dimension=0, tiled=True),
        lax.psum_scatter(grad_up, ("ctx", "fsdp"), scatter_dimension=0, tiled=True),
    )
    full_in_gain, full_query, full_key, full_value, full_output = (
        lax.all_gather(in_gain, ("ctx", "fsdp"), axis=0, tiled=True),
        lax.all_gather(w_query, ("ctx", "fsdp"), axis=0, tiled=True),
        lax.all_gather(w_key, ("ctx", "fsdp"), axis=0, tiled=True),
        lax.all_gather(w_value, ("ctx", "fsdp"), axis=0, tiled=True),
        lax.all_gather(w_output, ("ctx", "fsdp"), axis=0, tiled=True),
    )
    grad_branch = grad_mid.astype(jnp.bfloat16)
    grad_output = lax.dot_general(
        attn_bf, grad_branch, contract_rows, preferred_element_type=jnp.float32
    )
    grad_attn = lax.dot_general(
        grad_branch, full_output, contract_cols, preferred_element_type=jnp.float32
    ).astype(jnp.bfloat16)
    grad_attn = grad_attn.reshape(flat_rows, kv_heads, group_size, head_dim)
    query_grads = []
    seq = 0
    key_blocks, value_blocks, block_index = sequence_tables(seq)
    key_grads = jnp.zeros((block_total, block_rows, kv_heads, head_dim), jnp.float32)
    value_grads = jnp.zeros((block_total, block_rows, kv_heads, head_dim), jnp.float32)
    for which in range(2):
        slot = 2 * seq + which
        query_tile = queries[slot * block_rows : (slot + 1) * block_rows].reshape(
            block_rows, kv_heads, group_size, head_dim
        )
        query_pos = positions[slot * block_rows : (slot + 1) * block_rows]
        grad_tile = grad_attn[slot * block_rows : (slot + 1) * block_rows]
        tile_count = block_of[seq, which] // tile_blocks + 1
        delta = jnp.einsum("qhgd,qhgd->hgq", grad_tile.astype(jnp.float32), attn_parts[slot])
        log_total = log_totals[slot]

        def grad_step(step, carry):
            grad_query, keys_acc, values_acc = carry
            key_tile = fetch(key_blocks, block_index, step)
            scores, visible = tile_scores(query_tile, key_tile, query_pos, step)
            probs = jnp.where(visible, jnp.exp(scores - log_total[..., None]), 0.0)
            grad_probs = jnp.einsum(
                "qhgd,khd->hgqk",
                grad_tile,
                fetch(value_blocks, block_index, step),
                preferred_element_type=jnp.float32,
            )
            grad_scores = (probs * (grad_probs - delta[..., None])).astype(jnp.bfloat16)
            grad_query = grad_query + jnp.einsum(
                "hgqk,khd->qhgd", grad_scores, key_tile, preferred_element_type=jnp.float32
            )
            key_part = jnp.einsum(
                "hgqk,qhgd->khd", grad_scores, query_tile, preferred_element_type=jnp.float32
            )
            value_part = jnp.einsum(
                "hgqk,qhgd->khd",
                probs.astype(jnp.bfloat16),
                grad_tile,
                preferred_element_type=jnp.float32,
            )
            places = tile_index(block_index, step)
            keys_acc = keys_acc.at[places].add(
                key_part.reshape(tile_blocks, block_rows, kv_heads, head_dim)
            )
            values_acc = values_acc.at[places].add(
                value_part.reshape(tile_blocks, block_rows, kv_heads, head_dim)
            )
            return (grad_query, keys_acc, values_acc)

        start_query = jnp.zeros((block_rows, kv_heads, group_size, head_dim), jnp.float32)
        grad_query, key_grads, value_grads = lax.fori_loop(
            0, tile_count, grad_step, (start_query, key_grads, value_grads)
        )
        query_grads.append(grad_query)
    key_grad_list = [key_grads.reshape(seq_len, kv_heads * head_dim)]
    value_grad_list = [value_grads.reshape(seq_len, kv_heads * head_dim)]
    grad_keys, grad_values = (
        lax.psum_scatter(
            jnp.stack(key_grad_list, axis=0).astype(jnp.bfloat16),
            "ctx",
            scatter_dimension=1,
            tiled=True,
        ).astype(jnp.float32),
        lax.psum_scatter(
            jnp.stack(value_grad_list, axis=0).astype(jnp.bfloat16),
            "ctx",
            scatter_dimension=1,
            tiled=True,
        ).astype(jnp.float32),
    )
    grad_q_rot = (
        jnp.concatenate(query_grads, axis=0).reshape(flat_rows, q_heads, head_dim) * q_scale
    )
    grad_q_normed = rotate(grad_q_rot, cosine, -sine)
    grad_q_gain = jnp.sum(grad_q_normed * q_unit, axis=(0, 1))
    grad_q_raw = (
        norm_back(grad_q_normed * q_gain.astype(jnp.float32), q_unit, q_rms)
        .astype(jnp.bfloat16)
        .reshape(flat_rows, q_heads * head_dim)
    )
    grad_k_normed = rotate(grad_keys.reshape(flat_rows, kv_heads, head_dim), cosine, -sine)
    grad_k_gain = jnp.sum(grad_k_normed * k_unit, axis=(0, 1))
    grad_k_raw = (
        norm_back(grad_k_normed * k_gain.astype(jnp.float32), k_unit, k_rms)
        .astype(jnp.bfloat16)
        .reshape(flat_rows, kv_heads * head_dim)
    )
    grad_v_local = grad_values.reshape(flat_rows, kv_heads * head_dim).astype(jnp.bfloat16)
    grad_query_w = lax.dot_general(
        attn_in, grad_q_raw, contract_rows, preferred_element_type=jnp.float32
    )
    grad_key_w = lax.dot_general(
        attn_in, grad_k_raw, contract_rows, preferred_element_type=jnp.float32
    )
    grad_value_w = lax.dot_general(
        attn_in, grad_v_local, contract_rows, preferred_element_type=jnp.float32
    )
    grad_attn_in = lax.dot_general(
        grad_q_raw, full_query, contract_cols, preferred_element_type=jnp.float32
    )
    grad_attn_in = grad_attn_in + lax.dot_general(
        grad_k_raw, full_key, contract_cols, preferred_element_type=jnp.float32
    )
    grad_attn_in = grad_attn_in + lax.dot_general(
        grad_v_local, full_value, contract_cols, preferred_element_type=jnp.float32
    )
    grad_in_gain = jnp.sum(grad_attn_in * in_normed, axis=0)
    grad_input = grad_mid + norm_back(
        grad_attn_in * full_in_gain.astype(jnp.float32), in_normed, in_scale
    )
    part_in, part_query, part_key, part_value, part_output = (
        lax.psum_scatter(grad_in_gain, ("ctx", "fsdp"), scatter_dimension=0, tiled=True),
        lax.psum_scatter(grad_query_w, ("ctx", "fsdp"), scatter_dimension=0, tiled=True),
        lax.psum_scatter(grad_key_w, ("ctx", "fsdp"), scatter_dimension=0, tiled=True),
        lax.psum_scatter(grad_value_w, ("ctx", "fsdp"), scatter_dimension=0, tiled=True),
        lax.psum_scatter(grad_output, ("ctx", "fsdp"), scatter_dimension=0, tiled=True),
    )
    sum_q_gain, sum_k_gain = lax.psum((grad_q_gain, grad_k_gain), ("ctx", "fsdp"))
    return (
        output.reshape(seq_count, tok_rows, model_width),
        grad_input.reshape(seq_count, tok_rows, model_width),
        part_in,
        part_query,
        part_key,
        part_value,
        part_output,
        sum_q_gain,
        sum_k_gain,
        part_post,
        part_gate,
        part_up,
        part_down,
    )


MESH = pl.DeviceIdType.MESH
SUBS = 2


def ring_position(index, size):
    column, line = lax.rem(index, 2), lax.div(index, 2)
    return column * (line + 1) + (1 - column) * lax.rem(size - line, size)


def ring_member(position, size):
    late = lax.div(position + size // 2 - 1, size)
    beyond = lax.div(position + size - 1, size)
    return beyond * (1 - late) * (2 * position - 1) + late * 2 * (size - position)


class Ring:
    def __init__(self, size):
        self.size = size
        self.me = lax.axis_index("ctx")
        self.row = lax.axis_index("fsdp")
        self.position = ring_position(self.me, size)

    def member(self, way, steps):
        ahead = self.size - steps if way == 0 else steps
        return ring_member(lax.rem(self.position + ahead, self.size), self.size)

    def target(self, way):
        return (self.member(way, self.size - 1), self.row)

    def barrier(self):
        barrier = pltpu.get_barrier_semaphore()
        for way in range(2):
            pl.semaphore_signal(barrier, inc=1, device_id=self.target(way), device_id_type=MESH)
        pl.semaphore_wait(barrier, 2)


class GatherRing:
    def __init__(self, ring, own, out, send_sems, recv_sems):
        self.ring, self.own, self.out, self.send_sems, self.recv_sems = ring, own, out, send_sems, recv_sems
        self.half = own.shape[0] // 2
        self.sub = self.half // SUBS

    def copy(self, way, step, part, first=False):
        place = pl.ds(way * self.half + part * self.sub, self.sub)
        owner = self.ring.me if first else self.ring.member(way, step)
        source = self.own.at[place] if first else self.out.at[owner, place]
        return pltpu.make_async_remote_copy(
            src_ref=source,
            dst_ref=self.out.at[owner, place],
            send_sem=self.send_sems.at[way, step, part],
            recv_sem=self.recv_sems.at[way, step, part],
            device_id=self.ring.target(way),
            device_id_type=MESH,
        )

    def start(self, way, part):
        self.copy(way, 0, part, first=True).start()

    def step(self, step):
        for part in range(SUBS):
            for way in range(2):
                self.copy(way, step - 1, part).wait_recv()
                self.copy(way, step, part).start()

    def finish(self):
        last = self.ring.size - 2
        for part in range(SUBS):
            for way in range(2):
                self.copy(way, last, part).wait_recv()

        @pl.loop(0, last + 1)
        def _(step):
            for part in range(SUBS):
                for way in range(2):
                    self.copy(way, step, part).wait_send()

    def run(self):
        for way in range(2):
            self.start(way)

        @pl.loop(1, self.ring.size - 1)
        def _(step):
            self.step(step)

        self.finish()


def gather_sems(size):
    return [pltpu.SemaphoreType.DMA((2, size - 1, SUBS)), pltpu.SemaphoreType.DMA((2, size - 1, SUBS))]


class SumRing:
    def __init__(self, ring, compute, terms, outgoing, incoming, send_sems, recv_sems):
        self.ring, self.compute, self.terms = ring, compute, terms
        self.outgoing, self.incoming, self.send_sems, self.recv_sems = outgoing, incoming, send_sems, recv_sems
        self.half = terms.shape[1]
        self.sub = self.half // SUBS

    def copy(self, way, step, part):
        place = pl.ds(part * self.sub, self.sub)
        return pltpu.make_async_remote_copy(
            src_ref=self.outgoing.at[way, lax.rem(step, 2), place],
            dst_ref=self.incoming.at[way, step, place],
            send_sem=self.send_sems.at[way, step, part],
            recv_sem=self.recv_sems.at[way, step, part],
            device_id=self.ring.target(way),
            device_id_type=MESH,
        )

    def terms_of(self, step):
        self.compute([self.ring.member(way, step + 1) for way in range(2)])

    def begin(self):
        self.terms_of(0)
        for part in range(SUBS):
            place = pl.ds(part * self.sub, self.sub)
            for way in range(2):
                self.outgoing[way, 0, place] = self.terms[way, place].astype(jnp.bfloat16)
                self.copy(way, 0, part).start()

    def second(self):
        self.step(1, fresh=True)

    def step(self, step, fresh=False):
        self.terms_of(step)
        for part in range(SUBS):
            place = pl.ds(part * self.sub, self.sub)
            for way in range(2):
                self.copy(way, step - 1, part).wait_recv()
                total = self.terms[way, place] + self.incoming[way, step - 1, place].astype(jnp.float32)
                if not fresh:
                    self.copy(way, step - 2, part).wait_send()
                self.outgoing[way, lax.rem(step, 2), place] = total.astype(jnp.bfloat16)
                self.copy(way, step, part).start()

    def last_terms(self):
        self.compute([self.ring.me, self.ring.me])

    def result(self, way, part):
        last = self.ring.size - 2
        place = pl.ds(part * self.sub, self.sub)
        self.copy(way, last, part).wait_recv()
        return self.terms[way, place] + self.incoming[way, last, place].astype(jnp.float32)

    def parts(self):
        for part in range(SUBS):
            for way in range(2):
                start = way * self.half + part * self.sub
                yield way, part, slice(start, start + self.sub)

    def finish(self):
        for step in (self.ring.size - 3, self.ring.size - 2):
            for part in range(SUBS):
                for way in range(2):
                    self.copy(way, step, part).wait_send()

    def run(self):
        self.begin()
        self.second()

        @pl.loop(2, self.ring.size - 1)
        def _(step):
            self.step(step)

        self.last_terms()


def sum_scratch(size, rows, width):
    half = rows // 2
    return [
        pltpu.VMEM((2, half, width), jnp.float32),
        pltpu.VMEM((2, 2, half, width), jnp.bfloat16),
        pltpu.VMEM((2, size - 1, half, width), jnp.bfloat16),
        pltpu.SemaphoreType.DMA((2, size - 1, SUBS)),
        pltpu.SemaphoreType.DMA((2, size - 1, SUBS)),
    ]


class Square:
    def __init__(self, size):
        self.size = size
        self.me = lax.axis_index("ctx")
        self.row = lax.axis_index("fsdp")
        line, column = lax.div(self.me, 2), lax.rem(self.me, 2)
        half = lax.div(line, 2)
        self.inner = lax.rem(lax.div(line + 1, 2), 2) == 1
        self.outer = lax.rem(lax.div(line + 1, 2), 2) == 0
        self.beside = self.me + 1 - 2 * column
        self.along = self.me + 2 - 4 * lax.rem(line, 2)
        self.across = (3 - line) * 2 + column
        self.diagonal = self.along + 1 - 2 * column
        self.near = (2 - half) * 2 + column
        self.far = 6 * (1 - half) + column
        self.beside_near = (2 - half) * 2 + 1 - column
        self.beside_far = 6 * (1 - half) + 1 - column

    def targets(self):
        return [(member, self.row) for member in (self.beside, self.along, self.across)]


LED, KEPT = range(SUBS // 2), range(SUBS // 2, SUBS)


class SquareGather:
    def __init__(self, square, own, out, send_sems, recv_sems):
        self.square, self.own, self.out, self.send_sems, self.recv_sems = square, own, out, send_sems, recv_sems
        self.half = own.shape[0] // 2
        self.sub = self.half // SUBS
        me, rest = square.me, [(square.near, 0), (square.near, 1), (square.far, 0), (square.far, 1)]
        self.sent = [
            [(me, 0), (me, 1), (square.along, 1)] + rest + [(square.along, 0)],
            [(me, 0), (me, 1), (square.beside, 0)] + rest,
            [(me, 0), (me, 1), (square.along, 0), (square.along, 1)],
        ]

    def copy(self, link, slot, part):
        member, half = self.sent[link][slot]
        place = pl.ds(half * self.half + part * self.sub, self.sub)
        source = self.own.at[place] if slot < 2 else self.out.at[member, place]
        return remote(
            source,
            self.out.at[member, place],
            self.send_sems.at[link, slot, part],
            self.recv_sems.at[link, slot, part],
            self.square.targets()[link],
        )

    def start(self, half, part):
        for link in range(2):
            self.copy(link, half, part).start()

        @pl.when(self.square.inner)
        def _():
            self.copy(2, half, part).start()

    def relay(self, link, slot, *onward, parts=range(SUBS)):
        for part in parts:
            self.copy(link, slot, part).wait_recv()
            for next_link, next_slot in onward:
                self.copy(next_link, next_slot, part).start()

    def first(self):
        @pl.when(self.square.outer)
        def _():
            self.relay(0, 0, (1, 2))
            self.relay(1, 1, (0, 2))
            self.relay(1, 0, (0, 7), parts=LED)
            self.relay(1, 0, parts=KEPT)

        @pl.when(self.square.inner)
        def _():
            self.relay(1, 0, (2, 2))
            self.relay(2, 0, (1, 3))
            self.relay(1, 1, (2, 3), (0, 2))
            for part in range(SUBS):
                self.copy(0, 3, part).start()

    def second(self):
        @pl.when(self.square.outer)
        def _():
            self.relay(1, 3, (0, 3))
            self.relay(1, 4, (0, 4))

        @pl.when(self.square.inner)
        def _():
            self.relay(2, 1, (1, 4), (0, 4))

    def third(self):
        @pl.when(self.square.outer)
        def _():
            self.relay(1, 5, (0, 5))
            self.relay(1, 6, (0, 6))

        @pl.when(self.square.inner)
        def _():
            self.relay(2, 2, (1, 5), (0, 5))
            self.relay(2, 3, (1, 6), (0, 6))
            self.relay(0, 0, parts=LED)
            self.relay(0, 0, (1, 2), parts=KEPT)

    def finish(self):
        for slot in range(1, 7):
            self.relay(0, slot)
        self.relay(1, 2, parts=KEPT)
        for part in range(SUBS):
            for slot in range(7):
                self.copy(0, slot, part).wait_send()
            for slot in range(2):
                self.copy(1, slot, part).wait_send()
        for part in KEPT:
            self.copy(1, 2, part).wait_send()

        @pl.when(self.square.outer)
        def _():
            self.relay(0, 7, parts=LED)
            for part in LED:
                self.copy(0, 7, part).wait_send()
                self.copy(1, 2, part).wait_send()

        @pl.when(self.square.inner)
        def _():
            self.relay(1, 2, parts=LED)
            for part in range(SUBS):
                for slot in range(3, 7):
                    self.copy(1, slot, part).wait_send()
                for slot in range(4):
                    self.copy(2, slot, part).wait_send()


def square_sems():
    return [pltpu.SemaphoreType.DMA((3, 8, SUBS)), pltpu.SemaphoreType.DMA((3, 8, SUBS))]


class SquareSum:
    def __init__(self, square, compute, terms, outgoing, incoming, send_sems, recv_sems):
        self.square, self.compute, self.terms = square, compute, terms
        self.outgoing, self.incoming, self.send_sems, self.recv_sems = outgoing, incoming, send_sems, recv_sems
        self.half = outgoing.shape[1]
        self.sub = self.half // SUBS
        self.first_slot = (0, 8, 15)

    def copy(self, link, slot, part):
        at = self.first_slot[link] + slot
        place = pl.ds(part * self.sub, self.sub)
        return remote(
            self.outgoing.at[at, place],
            self.incoming.at[at, place],
            self.send_sems.at[link, slot, part],
            self.recv_sems.at[link, slot, part],
            self.square.targets()[link],
        )

    def arrived(self, link, slot, part):
        self.copy(link, slot, part).wait_recv()
        at = self.first_slot[link] + slot
        return self.incoming[at, part * self.sub : (part + 1) * self.sub].astype(jnp.float32)

    def term(self, which, half, part):
        start = half * self.half + part * self.sub
        return self.terms[which, start : start + self.sub]

    def send(self, link, slot, which, half, *received, parts=range(SUBS)):
        at = self.first_slot[link] + slot
        for part in parts:
            total = self.term(which, half, part)
            for source in received:
                total = total + self.arrived(*source, part)
            self.outgoing[at, part * self.sub : (part + 1) * self.sub] = total.astype(jnp.bfloat16)
            self.copy(link, slot, part).start()

    def begin(self):
        square = self.square
        self.compute(square.beside_far, 0)
        self.send(0, 0, 0, 0)
        self.send(0, 1, 0, 1)
        self.compute(square.beside_near, 1)
        self.send(0, 2, 1, 0)
        self.send(0, 3, 1, 1)
        self.compute(square.diagonal, 2)
        self.send(1, 0, 2, 0, parts=KEPT)

        @pl.when(square.outer)
        def _():
            self.send(0, 7, 2, 0, parts=LED)

        @pl.when(square.inner)
        def _():
            self.send(1, 0, 2, 0, parts=LED)

        self.send(0, 4, 2, 1)
        self.compute(square.far, 0)
        self.compute(square.near, 1)

    def first(self):
        @pl.when(self.square.outer)
        def _():
            self.send(1, 1, 0, 0, (0, 0))
            self.send(1, 2, 0, 1, (0, 1))

        @pl.when(self.square.inner)
        def _():
            self.send(2, 0, 0, 0, (0, 0), (1, 1))

        self.compute(self.square.beside, 3)
        self.send(0, 6, 3, 1)
        self.send(0, 5, 3, 0, (1, 0), parts=KEPT)

        @pl.when(self.square.outer)
        def _():
            self.send(0, 5, 3, 0, (1, 0), parts=LED)

        @pl.when(self.square.inner)
        def _():
            self.send(0, 5, 3, 0, parts=LED)

        self.compute(self.square.along, 2)
        self.compute(self.square.me, 4)

    def second(self):
        @pl.when(self.square.outer)
        def _():
            self.send(1, 3, 1, 0, (0, 2))
            self.send(1, 4, 1, 1, (0, 3))
            self.send(1, 5, 2, 0, (0, 7), parts=LED)
            self.send(1, 5, 2, 0, parts=KEPT)

        @pl.when(self.square.inner)
        def _():
            self.send(2, 1, 0, 1, (0, 1), (1, 2))
            self.send(1, 5, 2, 0, (2, 0))
            self.send(2, 2, 1, 0, (0, 2), (1, 3))

    def third(self):
        @pl.when(self.square.outer)
        def _():
            self.send(1, 6, 2, 1, (0, 4))

        @pl.when(self.square.inner)
        def _():
            self.send(2, 3, 1, 1, (0, 3), (1, 4))
            self.send(1, 6, 2, 1, (0, 4), (2, 1))
            for half in range(2):
                for part in range(SUBS):
                    start = half * self.half + part * self.sub
                    self.terms[4, start : start + self.sub] = self.term(4, half, part) + self.arrived(2, 2 + half, part)

    def parts(self):
        for half in range(2):
            for part in range(SUBS):
                start = half * self.half + part * self.sub
                yield half, part, slice(start, start + self.sub)

    def result(self, half, part):
        return self.term(4, half, part) + self.arrived(0, 5 + half, part) + self.arrived(1, 5 + half, part)

    def finish(self):
        for part in range(SUBS):
            for slot in range(7):
                self.copy(0, slot, part).wait_send()
            for slot in (5, 6):
                self.copy(1, slot, part).wait_send()
        for part in KEPT:
            self.copy(1, 0, part).wait_send()

        @pl.when(self.square.outer)
        def _():
            for part in LED:
                self.copy(0, 7, part).wait_send()
            for part in range(SUBS):
                for slot in range(1, 5):
                    self.copy(1, slot, part).wait_send()

        @pl.when(self.square.inner)
        def _():
            for part in LED:
                self.copy(1, 0, part).wait_send()
            for part in range(SUBS):
                for slot in range(4):
                    self.copy(2, slot, part).wait_send()


def square_sum_scratch(rows, width):
    return [
        pltpu.VMEM((5, rows, width), jnp.float32),
        pltpu.VMEM((19, rows // 2, width), jnp.bfloat16),
        pltpu.VMEM((19, rows // 2, width), jnp.bfloat16),
    ] + square_sems()


def block_terms_t(left, weight, terms, factors, product_sum):
    def compute(member, which):
        @pl.loop(0, weight.shape[0] // TILE)
        def _(tile):
            columns = pl.ds(pl.multiple_of(tile * TILE, TILE), TILE)
            terms[which, :, columns] = lax.dot_general(
                left[member], weight[columns, :], (((1,), (1,)), ((), ())), preferred_element_type=jnp.float32
            )
            product_sum[:, columns] = product_sum[:, columns] + jnp.sum(
                terms[which, :, columns] * factors[member, :, columns].astype(jnp.float32), axis=0, keepdims=True
            )

    return compute


TILE = 512


def row_terms(left, weight, terms):
    half = terms.shape[1]

    def compute(members):
        lines = jnp.concatenate([left[members[way], way * half : (way + 1) * half] for way in range(2)], axis=0)

        @pl.loop(0, weight.shape[1] // TILE)
        def _(tile):
            columns = pl.ds(pl.multiple_of(tile * TILE, TILE), TILE)
            product = jnp.dot(lines, weight[:, columns], preferred_element_type=jnp.float32)
            for way in range(2):
                terms[way, :, columns] = product[way * half : (way + 1) * half]

    return compute


def row_terms_t(left, weight, terms):
    half = terms.shape[1]
    tile = terms.shape[2] // weight.shape[0]

    def compute(members):
        lines = jnp.concatenate([left[members[way], way * half : (way + 1) * half] for way in range(2)], axis=0)

        @pl.loop(0, weight.shape[0])
        def _(block):
            columns = pl.ds(pl.multiple_of(block * tile, tile), tile)
            product = lax.dot_general(
                lines,
                weight[block].reshape(tile, weight.shape[-1]),
                (((1,), (1,)), ((), ())),
                preferred_element_type=jnp.float32,
            )
            for way in range(2):
                terms[way, :, columns] = product[way * half : (way + 1) * half]

    return compute


VMEM_SPEC = pl.BlockSpec(memory_space=pltpu.VMEM)
ANY_SPEC = pl.BlockSpec(memory_space=pl.ANY)


def ctx_peer(ring, ahead):
    return lax.rem(ring.me + ahead, ring.size)


def across(row, n_fsdp):
    return lax.rem(row + n_fsdp // 2, n_fsdp)


def beside(row):
    return row + 1 - 2 * lax.rem(row, 2)


def remote(source, target, send_sem, recv_sem, device):
    return pltpu.make_async_remote_copy(
        src_ref=source,
        dst_ref=target,
        send_sem=send_sem,
        recv_sem=recv_sem,
        device_id=device,
        device_id_type=MESH,
    )


def greet(devices):
    barrier = pltpu.get_barrier_semaphore()
    for device in devices:
        pl.semaphore_signal(barrier, inc=1, device_id=device, device_id_type=MESH)
    pl.semaphore_wait(barrier, len(devices))


def near_devices(ring, n_fsdp):
    return [(ctx_peer(ring, ahead), ring.row) for ahead in range(1, ring.size)] + [
        (ring.me, lax.rem(ring.row + ahead, n_fsdp)) for ahead in range(1, n_fsdp)
    ]


class Spread:
    def __init__(self, ring, n_fsdp, block, out, send_sems, recv_sems):
        self.ring, self.n_fsdp, self.block, self.out = ring, n_fsdp, block, out
        self.send_sems, self.recv_sems = send_sems, recv_sems

    def along_ctx(self, ahead):
        return remote(
            self.block,
            self.out.at[self.ring.row, self.ring.me],
            self.send_sems.at[ahead],
            self.recv_sems.at[ahead],
            (ctx_peer(self.ring, ahead), self.ring.row),
        )

    def along_fsdp(self, ahead):
        line = self.out.at[self.ring.row]
        sem = self.ring.size + ahead
        row = lax.rem(self.ring.row + ahead, self.n_fsdp)
        return remote(line, line, self.send_sems.at[sem], self.recv_sems.at[sem], (self.ring.me, row))

    def begin(self):
        for ahead in range(1, self.ring.size):
            self.along_ctx(ahead).start()
        self.out[self.ring.row, self.ring.me] = self.block[...]

    def collect(self):
        for ahead in range(1, self.ring.size):
            self.along_ctx(ahead).wait_recv()
        for ahead in range(1, self.n_fsdp):
            self.along_fsdp(ahead).start()
        for ahead in range(1, self.n_fsdp):
            self.along_fsdp(ahead).wait_recv()

    def finish(self):
        for ahead in range(1, self.ring.size):
            self.along_ctx(ahead).wait_send()
        for ahead in range(1, self.n_fsdp):
            self.along_fsdp(ahead).wait_send()


class SmallSum:
    def __init__(self, ring, n_fsdp, blocks, by_ctx, part, by_fsdp, send_sems, recv_sems):
        self.ring, self.n_fsdp, self.blocks, self.by_ctx, self.part, self.by_fsdp = (
            ring,
            n_fsdp,
            blocks,
            by_ctx,
            part,
            by_fsdp,
        )
        self.send_sems, self.recv_sems = send_sems, recv_sems

    def along_ctx(self, ahead):
        member = ctx_peer(self.ring, ahead)
        return remote(
            self.blocks.at[member],
            self.by_ctx.at[self.ring.me],
            self.send_sems.at[ahead],
            self.recv_sems.at[ahead],
            (member, self.ring.row),
        )

    def along_fsdp(self, ahead):
        row = lax.rem(self.ring.row + ahead, self.n_fsdp)
        sem = self.ring.size + ahead
        return remote(
            self.part.at[lax.div(row, 2)],
            self.by_fsdp.at[self.ring.row],
            self.send_sems.at[sem],
            self.recv_sems.at[sem],
            (self.ring.me, row),
        )

    def begin(self):
        for ahead in range(1, self.ring.size):
            self.along_ctx(ahead).start()
        self.by_ctx[self.ring.me] = self.blocks[self.ring.me]

    def cross(self):
        for ahead in range(1, self.ring.size):
            self.along_ctx(ahead).wait_recv()
        self.part[...] = jnp.sum(self.by_ctx[...], axis=0)
        for ahead in range(1, self.n_fsdp):
            self.along_fsdp(ahead).start()
        self.by_fsdp[self.ring.row] = self.part[lax.div(self.ring.row, 2)]

    def result(self):
        for ahead in range(1, self.n_fsdp):
            self.along_fsdp(ahead).wait_recv()
        return jnp.sum(self.by_fsdp[...], axis=0)

    def finish(self):
        for ahead in range(1, self.ring.size):
            self.along_ctx(ahead).wait_send()
        for ahead in range(1, self.n_fsdp):
            self.along_fsdp(ahead).wait_send()


def small_sems(size, n_fsdp):
    return [pltpu.SemaphoreType.DMA((size + n_fsdp,)), pltpu.SemaphoreType.DMA((size + n_fsdp,))]


class Rows:
    def __init__(self, ring, n_fsdp, shard, out, send_sems, recv_sems):
        own, far, twin = ring.row, across(ring.row, n_fsdp), beside(ring.row)
        self.keep = pltpu.make_async_copy(shard, out.at[own], send_sems.at[3])
        self.to_far = remote(shard, out.at[own], send_sems.at[0], recv_sems.at[0], (ring.me, far))
        self.to_twin = remote(shard, out.at[own], send_sems.at[1], recv_sems.at[1], (ring.me, twin))
        self.pass_on = remote(out.at[far], out.at[far], send_sems.at[2], recv_sems.at[2], (ring.me, twin))

    def begin(self):
        self.keep.start()
        self.to_far.start()
        self.to_twin.start()

    def relay(self):
        self.to_far.wait_recv()
        self.pass_on.start()

    def finish(self):
        self.keep.wait()
        self.to_far.wait_send()
        self.to_twin.wait()
        self.pass_on.wait()


def rows_sems():
    return [pltpu.SemaphoreType.DMA((4,)), pltpu.SemaphoreType.DMA((3,))]


class Links:
    def __init__(self, ring, n_fsdp, out, place, send_sems, recv_sems):
        self.ring, self.out, self.place, self.send_sems, self.recv_sems = ring, out, place, send_sems, recv_sems
        far, twin = across(ring.row, n_fsdp), beside(ring.row)
        self.to_far = self.link(0, ring.row, far)
        self.to_twin = self.link(1, ring.row, twin)
        self.pass_on = self.link(2, far, twin)

    def link(self, which, row, target):
        block = self.out.at[:, row, :, self.place]
        return remote(block, block, self.send_sems.at[which], self.recv_sems.at[which], (self.ring.me, target))

    def begin(self):
        self.to_far.start()
        self.to_twin.start()

    def relay(self):
        self.to_far.wait_recv()
        self.pass_on.start()

    def arrive(self):
        self.to_twin.wait_recv()
        self.pass_on.wait_recv()

    def finish(self):
        self.to_far.wait_send()
        self.to_twin.wait_send()
        self.pass_on.wait_send()


def links_sems():
    return [pltpu.SemaphoreType.DMA((3,)), pltpu.SemaphoreType.DMA((3,))]


class Pieces:
    def __init__(self, ring, shard, out, start, send_sems, recv_sems):
        self.ring, self.shard, self.out, self.send_sems, self.recv_sems = ring, shard, out, send_sems, recv_sems
        self.width = shard.shape[1] // ring.size
        self.place = pl.ds(start, self.width)

    def piece(self, ahead):
        member = ctx_peer(self.ring, ahead)
        source = self.shard.at[:, pl.ds(pl.multiple_of(member * self.width, self.width), self.width)]
        target = self.out.at[self.ring.me, self.ring.row, :, self.place]
        if ahead == 0:
            return pltpu.make_async_copy(source, target, self.send_sems.at[0])
        return remote(source, target, self.send_sems.at[ahead], self.recv_sems.at[ahead], (member, self.ring.row))

    def begin(self):
        for ahead in range(self.ring.size):
            self.piece(ahead).start()

    def arrive(self):
        self.piece(0).wait()
        for ahead in range(1, self.ring.size):
            self.piece(ahead).wait_recv()

    def finish(self):
        for ahead in range(1, self.ring.size):
            self.piece(ahead).wait_send()


class Columns:
    def __init__(self, ring, n_fsdp, shard, out, start, send_sems, recv_sems, link_send, link_recv):
        self.pieces = Pieces(ring, shard, out, start, send_sems, recv_sems)
        self.links = Links(ring, n_fsdp, out, self.pieces.place, link_send, link_recv)
        self.begin, self.relay, self.arrive = self.pieces.begin, self.links.relay, self.links.arrive

    def spread(self):
        self.pieces.arrive()
        self.links.begin()

    def finish(self):
        self.pieces.finish()
        self.links.finish()


def pieces_sems(size):
    return [pltpu.SemaphoreType.DMA((size,)), pltpu.SemaphoreType.DMA((size,))]


class RowGrads:
    def __init__(self, ring, n_fsdp, part, from_twin, to_far, from_far, send_sems, recv_sems):
        own, far, twin = ring.row, across(ring.row, n_fsdp), beside(ring.row)
        self.part, self.from_twin, self.to_far, self.from_far = part, from_twin, to_far, from_far
        self.own, self.far = own, far
        twin_far = across(twin, n_fsdp)
        self.first = [
            remote(part.at[twin], from_twin.at[0], send_sems.at[0], recv_sems.at[0], (ring.me, twin)),
            remote(part.at[twin_far], from_twin.at[1], send_sems.at[1], recv_sems.at[1], (ring.me, twin)),
        ]
        if to_far is None:
            self.to_far = part.at[far]
        self.second = remote(self.to_far, from_far, send_sems.at[2], recv_sems.at[2], (ring.me, far))

    def begin(self):
        self.first[1].start()
        self.first[0].start()

    def cross(self):
        self.first[1].wait_recv()
        self.to_far[...] = (
            self.part[self.far].astype(jnp.float32) + self.from_twin[1].astype(jnp.float32)
        ).astype(jnp.bfloat16)
        self.second.start()

    def result(self):
        self.first[0].wait_recv()
        self.second.wait_recv()
        return (
            self.part[self.own].astype(jnp.float32)
            + self.from_twin[0].astype(jnp.float32)
            + self.from_far[...].astype(jnp.float32)
        )

    def finish(self):
        for copy in self.first + [self.second]:
            copy.wait_send()


def row_grads_sems():
    return [pltpu.SemaphoreType.DMA((3,)), pltpu.SemaphoreType.DMA((3,))]


def row_grads_scratch(shape):
    return [
        pltpu.VMEM((2,) + shape, jnp.bfloat16),
        pltpu.VMEM(shape, jnp.bfloat16),
        pltpu.VMEM(shape, jnp.bfloat16),
    ] + row_grads_sems()


class Deal:
    def __init__(self, ring, total, arrived, send_sems, recv_sems):
        self.ring, self.total, self.arrived = ring, total, arrived
        self.send_sems, self.recv_sems = send_sems, recv_sems

    def piece(self, ahead):
        member = ctx_peer(self.ring, ahead)
        source, target = self.total.at[member], self.arrived.at[self.ring.me]
        if ahead == 0:
            return pltpu.make_async_copy(source, target, self.send_sems.at[0])
        return remote(source, target, self.send_sems.at[ahead], self.recv_sems.at[ahead], (member, self.ring.row))

    def begin(self):
        for ahead in range(self.ring.size):
            self.piece(ahead).start()

    def finish(self):
        for ahead in range(self.ring.size):
            self.piece(ahead).wait()


def deal_sems(size):
    return [pltpu.SemaphoreType.DMA((size,)), pltpu.SemaphoreType.DMA((size,))]


def params(collective_id):
    return pltpu.CompilerParams(
        collective_id=collective_id, has_side_effects=True, vmem_limit_bytes=62 * 1024 * 1024
    )


def head_norm(raw):
    return lax.rsqrt(jnp.mean(raw * raw, axis=-1, keepdims=True) + EPS)


def turn(values, cosine, sine):
    return values * cosine + pltpu.roll(values, values.shape[-1] // 2, 1) * sine


class Places:
    def __init__(self, ring, n_fsdp, all_small, starts, offsets, cosine, sine, places):
        self.ring, self.n_fsdp, self.all_small = ring, n_fsdp, all_small
        self.starts, self.offsets, self.cosine, self.sine, self.places = starts, offsets, cosine, sine, places
        self.block_rows = offsets.shape[1]

    def block(self, member, which):
        return self.all_small[self.ring.row, member, 2:3, which : which + 1]

    def fill(self):
        count = self.starts.shape[1]
        numbers = lax.broadcasted_iota(jnp.int32, (count, 1), 0).astype(jnp.float32)
        offset = lax.broadcasted_iota(jnp.int32, (self.block_rows, self.places.shape[1]), 0).astype(jnp.float32)
        for slot in range(count):
            block = self.block(slot // 2, slot % 2)
            chosen = (numbers == block).astype(jnp.float32)
            cos_start = jnp.sum(chosen * self.starts[0], axis=0, keepdims=True)
            sin_start = jnp.sum(chosen * self.starts[1], axis=0, keepdims=True)
            at = slice(slot * self.block_rows, (slot + 1) * self.block_rows)
            self.cosine[at] = cos_start * self.offsets[0] - sin_start * self.offsets[1]
            self.sine[at] = sin_start * self.offsets[0] + cos_start * self.offsets[1]
            self.places[at] = offset + block * self.block_rows

    def visible(self, member):
        width = self.places.shape[1]
        lane = lax.broadcasted_iota(jnp.int32, (1, width), 1).astype(jnp.float32)
        rows = float(self.block_rows)
        query = lane + jnp.where(lane < rows, self.block(member, 0) * rows, self.block(member, 1) * rows - rows)
        return self.places[...] <= query


def rotation_tables(blocks, block_rows, head):
    inverse = (THETA ** (-(np.arange(head // 2, dtype=np.float32) * np.float32(2.0) / head))).astype(np.float64)

    def both(at):
        angles = at.astype(np.float64)[:, None] * inverse[None, :]
        cosine, sine = np.cos(angles), np.sin(angles)
        return jnp.asarray(
            np.stack(
                [np.concatenate([cosine, cosine], axis=1), np.concatenate([-sine, sine], axis=1)], axis=0
            ).astype(np.float32)
        )

    return both(np.arange(blocks) * block_rows), both(np.arange(block_rows))


def fore_kernel(
    size,
    n_fsdp,
    q_heads,
    blocks,
    in_gain,
    post_gain,
    starts,
    offsets,
    q_gain,
    k_gain,
    hidden,
    w_query,
    w_key,
    w_value,
    w_output,
    w_gate,
    w_up,
    w_down,
    cotangent,
    all_small,
    gains,
    log_totals,
    raw_out,
    queries_out,
    keys_out,
    values_out,
    attn_out,
    attn_in_out,
    w_qkv_out,
    output_out,
    gu_out,
    down_out,
    grad_out,
    small,
    attn_in,
    w_qkv,
    cosine,
    sine,
    places_ref,
    values_t,
    raw,
    queries,
    keys,
    values,
    attn,
    small_send,
    small_recv,
    local_sems,
    *scratch,
):
    ring = Ring(size)
    head = q_gain.shape[1]
    tokens = hidden.shape[0]
    depth = in_gain.shape[1]
    q_width = q_heads * head
    k_width = w_key.shape[1] // size
    ff = w_gate.shape[1] // size
    columns_q = Columns(ring, n_fsdp, w_query, w_qkv, 0, *scratch[0:4])
    columns_k = Columns(ring, n_fsdp, w_key, w_qkv, q_width, *scratch[4:8])
    columns_v = Columns(ring, n_fsdp, w_value, w_qkv, q_width + k_width, *scratch[8:12])
    columns_gate = Columns(ring, n_fsdp, w_gate, gu_out, 0, *scratch[12:16])
    pieces_up = Pieces(ring, w_up, gu_out, ff, *scratch[16:18])
    rows_output = Rows(ring, n_fsdp, w_output, output_out, *scratch[18:20])
    rows_down = Rows(ring, n_fsdp, w_down, down_out, *scratch[20:22])
    square = Square(size)
    gathering = SquareGather(square, hidden, attn_in, *scratch[22:24])
    gathering_cot = SquareGather(square, cotangent, grad_out, *scratch[24:26])
    places = Places(ring, n_fsdp, all_small, starts, offsets, cosine, sine, places_ref)

    side = lax.rem(ring.row, 2)
    lane = lax.broadcasted_iota(jnp.int32, (1, 2 * depth), 1)
    mine = lax.div(lane, depth) == side
    small[...] = jnp.zeros_like(small)
    for row, part in enumerate((in_gain, post_gain)):
        part_row = part[...].astype(jnp.float32)
        small[row : row + 1] = jnp.where(mine, jnp.concatenate([part_row, part_row], axis=1), 0.0)
    small[2:3] = jnp.where(lane == 0, blocks[0, 0], jnp.where(lane == 1, blocks[0, 1], 0)).astype(jnp.float32)
    greet(near_devices(ring, n_fsdp))
    sharing = Spread(ring, n_fsdp, small, all_small, small_send, small_recv)
    sharing.begin()
    for part in range(SUBS):
        for way in range(2):
            gathering.start(way, part)
    for columns in (columns_q, columns_k, columns_v):
        columns.begin()
    keep = pltpu.make_async_copy(hidden, attn_in.at[ring.me], local_sems.at[0])
    keep.start()
    sharing.collect()
    rows_output.begin()
    rows_down.begin()
    for pair in range(size * n_fsdp // 2):
        member, chip = pair // (n_fsdp // 2), pair % (n_fsdp // 2)
        gains[:, pair * 128 : (pair + 1) * 128] = all_small[2 * chip, member] + all_small[2 * chip + 1, member]
    keep_cot = pltpu.make_async_copy(cotangent, grad_out.at[ring.me], local_sems.at[1])
    keep_cot.start()
    gathering.first()
    places.fill()
    gathering.second()
    for columns in (columns_q, columns_k, columns_v):
        columns.spread()
    rows_output.relay()
    gathering.third()
    for columns in (columns_q, columns_k, columns_v):
        columns.relay()
    columns_gate.begin()
    for part in range(SUBS):
        for way in range(2):
            gathering_cot.start(way, part)
    pieces_up.begin()
    rows_down.relay()
    for columns in (columns_q, columns_k, columns_v):
        columns.arrive()
    gathering.finish()
    keep.wait()
    save_qkv = pltpu.make_async_copy(w_qkv, w_qkv_out, local_sems.at[3])
    save_qkv.start()
    width = hidden.shape[1]

    @pl.loop(0, size)
    def _(member):
        at = pl.ds(pl.multiple_of(member * tokens, tokens), tokens)
        rows = attn_in[member].astype(jnp.float32)
        scale = lax.rsqrt(jnp.mean(rows * rows, axis=-1, keepdims=True) + EPS)
        attn_in[member] = (rows * scale * gains[0:1]).astype(jnp.bfloat16)
        product = jnp.dot(
            attn_in[member], w_qkv[...].reshape(width, w_qkv.shape[3]), preferred_element_type=jnp.float32
        )
        raw[at, :] = product[:, : q_width + head]
        for which in range(q_heads + 1):
            values_raw = product[:, which * head : (which + 1) * head]
            gain = q_gain if which < q_heads else k_gain
            turned = turn(values_raw * head_norm(values_raw) * gain[...].astype(jnp.float32), cosine[at, :], sine[at, :])
            if which < q_heads:
                queries[member, which] = (turned * head**-0.5).astype(jnp.bfloat16)
            else:
                keys[at, :] = turned.astype(jnp.bfloat16)
        fresh = product[:, q_width + head :]
        values[at, :] = fresh.astype(jnp.bfloat16)
        values_t[:, at] = fresh.T.astype(jnp.bfloat16)

    @pl.loop(0, size)
    def _(member):
        visible = places.visible(member)
        for which in range(q_heads):
            scores = lax.dot_general(
                keys[...], queries[member, which], (((1,), (1,)), ((), ())), preferred_element_type=jnp.float32
            )
            scores = jnp.where(visible, scores, -1e30)
            peak = jnp.max(scores, axis=0, keepdims=True)
            weights = jnp.exp(scores - peak)
            total = jnp.sum(weights, axis=0, keepdims=True)
            probs = (weights * (1.0 / total)).astype(jnp.bfloat16)
            mixed = jnp.dot(values_t[...], probs, preferred_element_type=jnp.float32)
            attn[member, :, which * head : (which + 1) * head] = mixed.T.astype(jnp.bfloat16)
            log_totals[member, which : which + 1, :] = peak + jnp.log(total)

    save_in = pltpu.make_async_copy(attn_in, attn_in_out, local_sems.at[2])
    save_in.start()
    saves = [
        pltpu.make_async_copy(source, target, local_sems.at[4 + which])
        for which, (source, target) in enumerate(
            ((raw, raw_out), (queries, queries_out), (keys, keys_out), (values, values_out), (attn, attn_out))
        )
    ]
    for save in saves:
        save.start()
    gathering_cot.first()
    columns_gate.spread()
    gathering_cot.second()
    gathering_cot.third()
    columns_gate.relay()
    gathering_cot.finish()
    sharing.finish()
    columns_gate.arrive()
    pieces_up.arrive()
    for columns in (columns_q, columns_k, columns_v, columns_gate, pieces_up):
        columns.finish()
    rows_output.finish()
    rows_down.finish()
    keep_cot.wait()
    for save in saves + [save_in, save_qkv]:
        save.wait()


def fore(blocks, in_gain, post_gain, tables, q_gain, k_gain, hidden, w_query, w_key, w_value, w_output, w_gate, w_up, w_down, cotangent):
    size, n_fsdp = lax.axis_size("ctx"), lax.axis_size("fsdp")
    rows, width = hidden.shape
    depth = w_query.shape[0]
    head = q_gain.shape[0]
    q_heads = w_query.shape[1] // size // head
    everyone = size * rows
    qkv_share = (w_query.shape[1] + w_key.shape[1] + w_value.shape[1]) // size
    gu_share = (w_gate.shape[1] + w_up.shape[1]) // size
    f32, bf16 = jnp.float32, jnp.bfloat16
    return pl.pallas_call(
        functools.partial(fore_kernel, size, n_fsdp, q_heads),
        out_shape=[
            jax.ShapeDtypeStruct((n_fsdp, size, 8, 2 * depth), f32),
            jax.ShapeDtypeStruct((8, width), f32),
            jax.ShapeDtypeStruct((size, q_heads, rows), f32),
            jax.ShapeDtypeStruct((everyone, (q_heads + 1) * head), f32),
            jax.ShapeDtypeStruct((size, q_heads, rows, head), bf16),
            jax.ShapeDtypeStruct((everyone, head), bf16),
            jax.ShapeDtypeStruct((everyone, head), bf16),
            jax.ShapeDtypeStruct((size, rows, q_heads * head), bf16),
            jax.ShapeDtypeStruct((size, rows, width), bf16),
            jax.ShapeDtypeStruct((size, n_fsdp, depth, qkv_share), bf16),
            jax.ShapeDtypeStruct((n_fsdp,) + w_output.shape, bf16),
            jax.ShapeDtypeStruct((size, n_fsdp, depth, gu_share), bf16),
            jax.ShapeDtypeStruct((n_fsdp,) + w_down.shape, bf16),
            jax.ShapeDtypeStruct((size, rows, width), bf16),
        ],
        in_specs=[pl.BlockSpec(memory_space=pltpu.SMEM)] + [VMEM_SPEC] * 7 + [ANY_SPEC] * 8,
        out_specs=[VMEM_SPEC] * 3 + [ANY_SPEC] * 11,
        scratch_shapes=[
            pltpu.VMEM((8, 2 * depth), f32),
            pltpu.VMEM((size, rows, width), bf16),
            pltpu.VMEM((size, n_fsdp, depth, qkv_share), bf16),
            pltpu.VMEM((everyone, head), f32),
            pltpu.VMEM((everyone, head), f32),
            pltpu.VMEM((everyone, head), f32),
            pltpu.VMEM((head, everyone), bf16),
            pltpu.VMEM((everyone, (q_heads + 1) * head), f32),
            pltpu.VMEM((size, q_heads, rows, head), bf16),
            pltpu.VMEM((everyone, head), bf16),
            pltpu.VMEM((everyone, head), bf16),
            pltpu.VMEM((size, rows, q_heads * head), bf16),
        ]
        + small_sems(size, n_fsdp)
        + [pltpu.SemaphoreType.DMA((9,))]
        + (pieces_sems(size) + links_sems()) * 4
        + pieces_sems(size)
        + rows_sems() * 2
        + square_sems() * 2,
        compiler_params=params(2),
    )(
        blocks,
        in_gain.reshape(1, depth),
        post_gain.reshape(1, depth),
        *tables,
        q_gain.reshape(1, head),
        k_gain.reshape(1, head),
        hidden,
        w_query,
        w_key,
        w_value,
        w_output,
        w_gate,
        w_up,
        w_down,
        cotangent,
    )


def norm_pull(grad_normed, normed, scale):
    return scale * (grad_normed - normed * jnp.mean(grad_normed * normed, axis=-1, keepdims=True))


def feed_forward_kernel(
    size,
    n_fsdp,
    attn,
    w_output,
    hidden,
    gains,
    w_gu_in,
    w_down_in,
    cot_in,
    out_hidden,
    grad_gain,
    grad_mid_out,
    grad_branch,
    gu_total_out,
    down_out,
    w_gu,
    w_down,
    cot,
    load_sems,
    mid,
    own,
    mlp_in,
    inner,
    grad_gu,
    gu_part,
    down_part,
    grad_mid,
    gu_total,
    down_total,
    layer_terms,
    *scratch,
):
    ring = Ring(size)
    ff = w_down.shape[0]
    gate_part, up_part = pl.ds(0, ff), pl.ds(ff, ff)
    up_links = Links(ring, n_fsdp, w_gu, up_part, *scratch[21:23])
    loads = [
        pltpu.make_async_copy(source, target, load_sems.at[which])
        for which, (source, target) in enumerate(
            (
                (w_gu_in.at[:, ring.row, :, up_part], w_gu.at[:, ring.row, :, up_part]),
                (w_gu_in.at[:, :, :, gate_part], w_gu.at[:, :, :, gate_part]),
                (w_down_in, w_down),
                (cot_in, cot),
            )
        )
    ]
    for load in loads:
        load.start()
    greet(near_devices(ring, n_fsdp))
    loads[0].wait()
    up_links.begin()
    half = own.shape[0] // 2
    out_sums, gather_sems_in = scratch[:5], scratch[5:7]
    layer_sums = (layer_terms,) + tuple(scratch[7:11])
    gather_sems_out, keep_sems = scratch[11:13], scratch[13]
    column_scratch = (scratch[14], None, gu_total, scratch[15], scratch[16])
    row_scratch = (scratch[17], None, scratch[18], scratch[19], scratch[20])

    first = SumRing(ring, row_terms(attn, w_output, out_sums[0]), *out_sums)
    first.begin()
    first.second()

    @pl.loop(2, size - 2)
    def _(step):
        first.step(step)

    up_links.relay()
    first.step(size - 2)
    first.last_terms()
    gathering = GatherRing(ring, own, mlp_in, *gather_sems_in)
    for way, part, place in first.parts():
        total = first.result(way, part) + hidden[place].astype(jnp.float32)
        mid[place] = total
        scale = lax.rsqrt(jnp.mean(total * total, axis=-1, keepdims=True) + EPS)
        own[place] = (total * scale * gains[1:2]).astype(jnp.bfloat16)
        gathering.start(way, part)
    first.finish()
    keep = pltpu.make_async_copy(own, mlp_in.at[ring.me], keep_sems.at[0])
    keep.start()
    for load in loads[1:]:
        load.wait()
    up_links.arrive()
    width = own.shape[1]

    def units(lines, members):
        cot_lines = jnp.concatenate([cot[members[way], way * half : (way + 1) * half] for way in range(2)], axis=0)

        @pl.loop(0, ff // UNITS)
        def _(tile):
            at = pl.multiple_of(tile * UNITS, UNITS)
            here, there = pl.ds(at, UNITS), pl.ds(pl.multiple_of(ff + at, UNITS), UNITS)
            gate = jnp.dot(lines, w_gu[:, :, :, here].reshape(width, UNITS), preferred_element_type=jnp.float32)
            up = jnp.dot(lines, w_gu[:, :, :, there].reshape(width, UNITS), preferred_element_type=jnp.float32)
            pulled = lax.dot_general(
                cot_lines, w_down[here, :], (((1,), (1,)), ((), ())), preferred_element_type=jnp.float32
            )
            sigmoid = 1.0 / (1.0 + jnp.exp(-gate))
            active = gate * sigmoid
            inner_new = (active * up).astype(jnp.bfloat16)
            gate_new = (pulled * up * sigmoid * (1.0 + gate * (1.0 - sigmoid))).astype(jnp.bfloat16)
            up_new = (pulled * active).astype(jnp.bfloat16)
            for way in range(2):
                place = slice(way * half, (way + 1) * half)
                inner[members[way], place, here] = inner_new[place]
                grad_gu[members[way], place, here] = gate_new[place]
                grad_gu[members[way], place, there] = up_new[place]

    def units_of(step):
        members = [ring.member(way, step) for way in range(2)]
        units(
            jnp.concatenate([mlp_in[members[way], way * half : (way + 1) * half] for way in range(2)], axis=0), members
        )

    units(own[...], [ring.me, ring.me])

    @pl.loop(1, size - 1)
    def _(step):
        gathering.step(step)
        units_of(step)

    third = SumRing(ring, row_terms_t(grad_gu, w_gu, out_sums[0]), *out_sums)
    third.begin()
    gathering.finish()
    keep.wait()
    units_of(size - 1)
    rows_all = size * 2 * half
    block = width // size

    def gu_tile(member):
        columns = pl.ds(pl.multiple_of(member * block, block), block)
        lines = mlp_in[:, :, columns].reshape(rows_all, block)

        @pl.loop(0, 2 * ff // TILE)
        def _(tile):
            there = pl.ds(pl.multiple_of(tile * TILE, TILE), TILE)
            product = lax.dot_general(
                lines,
                grad_gu[:, :, there].reshape(rows_all, TILE),
                (((0,), (0,)), ((), ())),
                preferred_element_type=jnp.float32,
            ).astype(jnp.bfloat16)
            for row in range(n_fsdp):
                gu_part[row, member, :, there] = product[row * (block // n_fsdp) : (row + 1) * (block // n_fsdp)]

    share = ff // n_fsdp

    def down_tile(tile):
        columns = pl.ds(pl.multiple_of(tile * UNITS, UNITS), UNITS)
        lines = cot[:, :, columns].reshape(rows_all, UNITS)
        product = lax.dot_general(
            inner[...].reshape(rows_all, ff), lines, (((0,), (0,)), ((), ())), preferred_element_type=jnp.float32
        ).astype(jnp.bfloat16)
        for row in range(n_fsdp):
            down_part[row, :, columns] = product[row * share : (row + 1) * share]

    gu_tile(0)
    third.second()
    gu_tile(1)

    @pl.loop(2, size - 1)
    def _(step):
        third.step(step)
        gu_tile(step)

    second = SumRing(ring, row_terms(inner, w_down, layer_sums[0]), *layer_sums)
    second.begin()
    gu_tile(size - 1)
    columns = RowGrads(ring, n_fsdp, gu_part, *column_scratch)
    rows = RowGrads(ring, n_fsdp, down_part, *row_scratch)
    columns.begin()
    third.last_terms()
    gathering = GatherRing(ring, own, grad_branch, *gather_sems_out)
    gain_sum = jnp.zeros_like(grad_gain)
    for way, part, place in third.parts():
        pulled = third.result(way, part)
        values = mid[place]
        scale = lax.rsqrt(jnp.mean(values * values, axis=-1, keepdims=True) + EPS)
        normed = values * scale
        gain_sum = gain_sum + jnp.sum(pulled * normed, axis=0, keepdims=True)
        total = cot[ring.me, place].astype(jnp.float32) + norm_pull(pulled * gains[1:2], normed, scale)
        grad_mid[place] = total
        own[place] = total.astype(jnp.bfloat16)
        gathering.start(way, part)
    grad_gain[...] = gain_sum
    keep = pltpu.make_async_copy(own, grad_branch.at[ring.me], keep_sems.at[1])
    keep.start()
    save_mid = pltpu.make_async_copy(grad_mid, grad_mid_out, keep_sems.at[2])
    save_mid.start()
    third.finish()
    second.second()
    gathering.step(1)
    columns.cross()

    @pl.loop(2, 4)
    def _(step):
        second.step(step)
        gathering.step(step)

        @pl.loop(0, width // UNITS // 2)
        def _(tile):
            down_tile((step - 2) * (width // UNITS // 2) + tile)

    rows.begin()
    second.step(4)
    gathering.step(4)
    rows.cross()

    @pl.loop(5, size - 1)
    def _(step):
        second.step(step)
        gathering.step(step)

    second.last_terms()
    down_total[...] = rows.result()
    save_down = pltpu.make_async_copy(down_total, down_out, keep_sems.at[3])
    save_down.start()
    gu_total[...] = columns.result().astype(jnp.bfloat16)
    save_gu = pltpu.make_async_copy(gu_total, gu_total_out, keep_sems.at[4])
    save_gu.start()
    for way, part, place in second.parts():
        out_hidden[place] = (mid[place] + second.result(way, part)).astype(jnp.bfloat16)
    gathering.finish()
    second.finish()
    columns.finish()
    rows.finish()
    up_links.finish()
    for copy in (keep, save_mid, save_down, save_gu):
        copy.wait()


UNITS = 256


def feed_forward(attn, w_output, hidden, gains, w_gu, w_down, cotangent):
    size, n_fsdp = lax.axis_size("ctx"), lax.axis_size("fsdp")
    rows, width = hidden.shape
    ff = w_down.shape[0]
    depth = width // size // n_fsdp
    sums = sum_scratch(size, rows, width)
    return pl.pallas_call(
        functools.partial(feed_forward_kernel, size, n_fsdp),
        out_shape=[
            jax.ShapeDtypeStruct((rows, width), jnp.bfloat16),
            jax.ShapeDtypeStruct((1, width), jnp.float32),
            jax.ShapeDtypeStruct((rows, width), jnp.float32),
            jax.ShapeDtypeStruct((size, rows, width), jnp.bfloat16),
            jax.ShapeDtypeStruct((size, depth, 2 * ff), jnp.bfloat16),
            jax.ShapeDtypeStruct((ff // n_fsdp, width), jnp.float32),
        ],
        in_specs=[VMEM_SPEC] * 4 + [ANY_SPEC] * 3,
        out_specs=[VMEM_SPEC] * 2 + [ANY_SPEC] * 4,
        scratch_shapes=[
            pltpu.VMEM(w_gu.shape, jnp.bfloat16),
            pltpu.VMEM(w_down.shape, jnp.bfloat16),
            pltpu.VMEM((size, rows, width), jnp.bfloat16),
            pltpu.SemaphoreType.DMA((4,)),
            pltpu.VMEM((rows, width), jnp.float32),
            pltpu.VMEM((rows, width), jnp.bfloat16),
            pltpu.VMEM((size, rows, width), jnp.bfloat16),
            pltpu.VMEM((size, rows, ff), jnp.bfloat16),
            pltpu.VMEM((size, rows, 2 * ff), jnp.bfloat16),
            pltpu.VMEM((n_fsdp, size, depth, 2 * ff), jnp.bfloat16),
            pltpu.VMEM((n_fsdp, ff // n_fsdp, width), jnp.bfloat16),
            pltpu.VMEM((rows, width), jnp.float32),
            pltpu.VMEM((size, depth, 2 * ff), jnp.bfloat16),
            pltpu.VMEM((ff // n_fsdp, width), jnp.float32),
            pltpu.VMEM((2, rows // 2, width), jnp.float32),
        ]
        + sums
        + gather_sems(size)
        + sums[1:]
        + gather_sems(size)
        + [pltpu.SemaphoreType.DMA((5,))]
        + [pltpu.VMEM((2, size, depth, 2 * ff), jnp.bfloat16)]
        + row_grads_sems()
        + [pltpu.VMEM((2, ff // n_fsdp, width), jnp.bfloat16), pltpu.VMEM((ff // n_fsdp, width), jnp.bfloat16)]
        + row_grads_sems()
        + links_sems(),
        compiler_params=params(5),
    )(
        attn,
        w_output,
        hidden,
        gains,
        w_gu,
        w_down,
        cotangent,
    )


def back_kernel(
    size,
    n_fsdp,
    all_blocks,
    starts,
    offsets,
    q_gain,
    k_gain,
    gains,
    post_sum,
    log_totals,
    *refs,
):
    sources, refs = refs[:11], refs[11:]
    gu_total = refs[0]
    grad_hidden, gains_out, output_out, gu_out, qkv_out = refs[1:6]
    targets, refs = refs[6:17], refs[17:]
    grad_branch, attn, w_output, queries, keys, values, raw, attn_in, w_qkv, hidden, grad_mid = targets
    load_sems, cosine, sine, places_ref, keys_t, grad_keys, grad_values, head_sums, grads, qkv_part, output_part = refs[:11]
    small, small_ctx, small_part, small_fsdp, small_send, small_recv, in_sum = refs[11:18]
    scratch = refs[18:]
    loads = [
        pltpu.make_async_copy(source, target, load_sems.at[which])
        for which, (source, target) in enumerate(zip(sources, targets))
    ]
    for load in loads:
        load.start()
    sums = scratch[:5]
    ring = Ring(size)
    greet(near_devices(ring, n_fsdp))
    total = scratch[8]
    columns = RowGrads(ring, n_fsdp, qkv_part, scratch[5], None, *scratch[6:8], scratch[9])
    dealing = Deal(ring, total, qkv_out, *scratch[10:12])
    rows = RowGrads(ring, n_fsdp, output_part, scratch[12], None, *scratch[13:16])
    gu_dealing = Deal(ring, gu_total, gu_out, *scratch[16:18])
    gu_dealing.begin()
    places = Places(ring, n_fsdp, all_blocks, starts, offsets, cosine, sine, places_ref)
    places.fill()
    head = q_gain.shape[1]
    q_heads = queries.shape[1]
    tokens = attn_in.shape[1]
    everyone = size * tokens
    width = attn_in.shape[2]
    q_width = q_heads * head
    grad_keys[...] = jnp.zeros_like(grad_keys)
    grad_values[...] = jnp.zeros_like(grad_values)
    head_sums[...] = jnp.zeros_like(head_sums)
    for load in loads[:3]:
        load.wait()

    def through_head(pulled, at, which, gain_here):
        turned = turn(pulled, cosine[at, :], -sine[at, :])
        values_raw = raw[at, which * head : (which + 1) * head]
        scale = head_norm(values_raw)
        unit = values_raw * scale
        kind = 0 if which < q_heads else 1
        head_sums[kind : kind + 1] = head_sums[kind : kind + 1] + jnp.sum(turned * unit, axis=0, keepdims=True)
        return norm_pull(turned * gain_here[...].astype(jnp.float32), unit, scale).astype(jnp.bfloat16)

    def output_tile(tile):
        there = pl.ds(pl.multiple_of(tile * TILE, TILE), TILE)
        product = lax.dot_general(
            attn[...].reshape(everyone, q_width),
            grad_branch[:, :, there].reshape(everyone, TILE),
            (((0,), (0,)), ((), ())),
            preferred_element_type=jnp.float32,
        ).astype(jnp.bfloat16)
        share = q_width // n_fsdp
        for row in range(n_fsdp):
            output_part[row, :, there] = product[row * share : (row + 1) * share]

    @pl.loop(0, width // TILE)
    def _(tile):
        output_tile(tile)

    rows.begin()
    for load in loads[3:]:
        load.wait()
    keys_t[...] = keys[...].astype(jnp.float32).T.astype(jnp.bfloat16)

    @pl.loop(0, size)
    def _(member):
        at = pl.ds(pl.multiple_of(member * tokens, tokens), tokens)
        grad_attn = lax.dot_general(
            grad_branch[member], w_output[...], (((1,), (1,)), ((), ())), preferred_element_type=jnp.float32
        ).astype(jnp.bfloat16)
        visible = places.visible(member)
        for which in range(q_heads):
            lanes = slice(which * head, (which + 1) * head)
            pulled = grad_attn[:, lanes]
            query = queries[member, which]
            scores = lax.dot_general(keys[...], query, (((1,), (1,)), ((), ())), preferred_element_type=jnp.float32)
            probs = jnp.where(visible, jnp.exp(scores - log_totals[member, which : which + 1, :]), 0.0)
            grad_probs = lax.dot_general(
                values[...], pulled, (((1,), (1,)), ((), ())), preferred_element_type=jnp.float32
            )
            delta = jnp.sum(probs * grad_probs, axis=0, keepdims=True)
            grad_scores = (probs * (grad_probs - delta)).astype(jnp.bfloat16)
            grad_keys[...] = grad_keys[...] + jnp.dot(grad_scores, query, preferred_element_type=jnp.float32)
            grad_values[...] = grad_values[...] + jnp.dot(
                probs.astype(jnp.bfloat16), pulled, preferred_element_type=jnp.float32
            )
            grad_query = jnp.dot(keys_t[...], grad_scores, preferred_element_type=jnp.float32).T
            grads[member, :, lanes] = through_head(grad_query * head**-0.5, at, which, q_gain)

    rows.cross()

    @pl.loop(0, size)
    def _(member):
        at = pl.ds(pl.multiple_of(member * tokens, tokens), tokens)
        grads[member, :, q_width : q_width + head] = through_head(grad_keys[at, :], at, q_heads, k_gain)
        grads[member, :, q_width + head :] = grad_values[at, :].astype(jnp.bfloat16)

    block = width // size

    def qkv_tile(member):
        lines = attn_in[:, :, pl.ds(pl.multiple_of(member * block, block), block)].reshape(everyone, block)
        product = lax.dot_general(
            lines,
            grads[...].reshape(everyone, grads.shape[2]),
            (((0,), (0,)), ((), ())),
            preferred_element_type=jnp.float32,
        ).astype(jnp.bfloat16)
        for row in range(n_fsdp):
            qkv_part[row, member] = product[row * (block // n_fsdp) : (row + 1) * (block // n_fsdp)]

    in_sum[...] = jnp.zeros_like(in_sum)
    summing = SquareSum(Square(size), block_terms_t(grads, w_qkv, sums[0], attn_in, in_sum), *sums)
    summing.begin()

    @pl.loop(0, size // 2)
    def _(member):
        qkv_tile(member)

    summing.first()

    @pl.loop(size // 2, size)
    def _(member):
        qkv_tile(member)

    columns.begin()
    chips = n_fsdp // 2
    for pair in range(size * chips):
        lanes = slice(pair * 128, (pair + 1) * 128)
        small[pair // chips, pair % chips, 0:1] = in_sum[:, lanes] / gains[0:1, lanes]
        small[pair // chips, pair % chips, 1:2] = post_sum[:, lanes]
        small[pair // chips, pair % chips, 2:4] = head_sums[0:2]
        small[pair // chips, pair % chips, 4:8] = jnp.zeros((4, 128), jnp.float32)
    sharing = SmallSum(ring, n_fsdp, small, small_ctx, small_part, small_fsdp, small_send, small_recv)
    sharing.begin()
    summing.second()
    columns.cross()
    summing.third()
    total[...] = columns.result().astype(jnp.bfloat16)
    dealing.begin()
    output_out[...] = rows.result()
    sharing.cross()
    for way, part, place in summing.parts():
        pulled = summing.result(way, part)
        values_in = hidden[place].astype(jnp.float32)
        scale = lax.rsqrt(jnp.mean(values_in * values_in, axis=-1, keepdims=True) + EPS)
        normed = values_in * scale
        grad_hidden[place] = grad_mid[place] + norm_pull(pulled * gains[0:1], normed, scale)
    gains_out[...] = sharing.result()
    sharing.finish()
    summing.finish()
    columns.finish()
    rows.finish()
    dealing.finish()
    gu_dealing.finish()


def back(
    all_small,
    tables,
    q_gain,
    k_gain,
    raw,
    queries,
    keys,
    values,
    attn,
    log_totals,
    hidden,
    grad_mid,
    gains,
    post_sum,
    gu_total,
    grad_branch,
    w_output,
    attn_in,
    w_qkv,
):
    size, n_fsdp = lax.axis_size("ctx"), lax.axis_size("fsdp")
    rows, width = hidden.shape
    head = q_gain.shape[0]
    everyone = size * rows
    share = w_qkv.shape[1]
    depth = width // size // n_fsdp
    q_width = attn.shape[2]
    f32, bf16 = jnp.float32, jnp.bfloat16
    loaded = [grad_branch, attn, w_output, queries, keys, values, raw, attn_in, w_qkv, hidden, grad_mid]
    return pl.pallas_call(
        functools.partial(back_kernel, size, n_fsdp),
        out_shape=[
            jax.ShapeDtypeStruct((rows, width), f32),
            jax.ShapeDtypeStruct((8, 128), f32),
            jax.ShapeDtypeStruct((q_width // n_fsdp, width), f32),
            jax.ShapeDtypeStruct(gu_total.shape, bf16),
            jax.ShapeDtypeStruct((size, depth, share), bf16),
        ],
        in_specs=[VMEM_SPEC] * 8 + [ANY_SPEC] * 12,
        out_specs=[VMEM_SPEC] * 3 + [ANY_SPEC] * 2,
        scratch_shapes=[pltpu.VMEM(array.shape, array.dtype) for array in loaded]
        + [
            pltpu.SemaphoreType.DMA((len(loaded),)),
            pltpu.VMEM((everyone, head), f32),
            pltpu.VMEM((everyone, head), f32),
            pltpu.VMEM((everyone, head), f32),
            pltpu.VMEM((head, everyone), bf16),
            pltpu.VMEM((everyone, head), f32),
            pltpu.VMEM((everyone, head), f32),
            pltpu.VMEM((8, head), f32),
            pltpu.VMEM((size, rows, share), bf16),
            pltpu.VMEM((n_fsdp, size, depth, share), bf16),
            pltpu.VMEM((n_fsdp, q_width // n_fsdp, width), bf16),
            pltpu.VMEM((size, n_fsdp // 2, 8, 128), f32),
            pltpu.VMEM((size, n_fsdp // 2, 8, 128), f32),
            pltpu.VMEM((n_fsdp // 2, 8, 128), f32),
            pltpu.VMEM((n_fsdp, 8, 128), f32),
        ]
        + small_sems(size, n_fsdp)
        + [pltpu.VMEM((1, width), f32)]
        + square_sum_scratch(rows, width)
        + [
            pltpu.VMEM((2, size, depth, share), bf16),
            pltpu.VMEM((size, depth, share), bf16),
            pltpu.SemaphoreType.DMA((3,)),
            pltpu.VMEM((size, depth, share), bf16),
            pltpu.SemaphoreType.DMA((3,)),
        ]
        + deal_sems(size)
        + [
            pltpu.VMEM((2, q_width // n_fsdp, width), bf16),
            pltpu.VMEM((q_width // n_fsdp, width), bf16),
        ]
        + row_grads_sems()
        + deal_sems(size),
        compiler_params=params(6),
    )(
        all_small,
        *tables,
        q_gain.reshape(1, head),
        k_gain.reshape(1, head),
        gains,
        post_sum,
        log_totals,
        *loaded,
        gu_total,
    )


def finish_kernel(size, gu, qkv, gain_sums, *refs):
    kept, outs, refs = refs[:4], refs[4:9], refs[9:]
    kept_out, gains_out, refs = refs[:4], refs[4:8], refs[8:]
    gu_in, qkv_in, load_sems, wide, save_sems, keep_sems, held = refs[0], refs[1], refs[2], refs[3:8], refs[8], refs[9], refs[10:]
    share = size // 2
    loads = []
    for part in range(2):
        members = pl.ds(part * share, share)
        loads.append(
            (
                pltpu.make_async_copy(gu.at[members], gu_in.at[members], load_sems.at[0, part]),
                pltpu.make_async_copy(qkv.at[members], qkv_in.at[members], load_sems.at[1, part]),
            )
        )
    for pair in loads:
        for load in pair:
            load.start()
    holds = [
        pltpu.make_async_copy(source, target, keep_sems.at[0, which])
        for which, (source, target) in enumerate(zip(kept, held))
    ]
    for hold in holds:
        hold.start()
    side = lax.rem(lax.axis_index("fsdp"), 2)
    depth = gains_out[0].shape[1]
    for row, out in enumerate(gains_out[:2]):
        out[...] = jnp.where(side == 0, gain_sums[row : row + 1, :depth], gain_sums[row : row + 1, depth:])
    for row, out in enumerate(gains_out[2:]):
        out[...] = gain_sums[2 + row : 3 + row]
    saves = []
    for part in range(2):
        for load in loads[part]:
            load.wait()
        which = 0
        for arrived, count in ((gu_in, 2), (qkv_in, 3)):
            start = 0
            for _ in range(count):
                width = wide[which].shape[1] // size
                for member in range(part * share, (part + 1) * share):
                    wide[which][:, member * width : (member + 1) * width] = arrived[
                        member, :, start : start + width
                    ].astype(jnp.float32)
                columns = pl.ds(part * share * width, share * width)
                save = pltpu.make_async_copy(
                    wide[which].at[:, columns], outs[which].at[:, columns], save_sems.at[which, part]
                )
                save.start()
                saves.append(save)
                start += width
                which += 1
    for which, hold in enumerate(holds):
        hold.wait()
        save = pltpu.make_async_copy(held[which], kept_out[which], keep_sems.at[1, which])
        save.start()
        saves.append(save)
    for save in saves:
        save.wait()


def finish(gu, qkv, kept, gain_sums, widths):
    size = lax.axis_size("ctx")
    depth = gu.shape[1]
    f32 = jnp.float32
    wide = [(depth, width) for width in widths]
    return pl.pallas_call(
        functools.partial(finish_kernel, size),
        out_shape=[jax.ShapeDtypeStruct(shape, f32) for shape in wide]
        + [jax.ShapeDtypeStruct(array.shape, array.dtype) for array in kept]
        + [jax.ShapeDtypeStruct((1, depth), f32)] * 2
        + [jax.ShapeDtypeStruct((1, 128), f32)] * 2,
        in_specs=[ANY_SPEC] * 2 + [VMEM_SPEC] + [ANY_SPEC] * len(kept),
        out_specs=[ANY_SPEC] * (len(wide) + len(kept)) + [VMEM_SPEC] * 4,
        scratch_shapes=[
            pltpu.VMEM(gu.shape, gu.dtype),
            pltpu.VMEM(qkv.shape, qkv.dtype),
            pltpu.SemaphoreType.DMA((2, 2)),
        ]
        + [pltpu.VMEM(shape, f32) for shape in wide]
        + [pltpu.SemaphoreType.DMA((len(wide), 2)), pltpu.SemaphoreType.DMA((2, len(kept)))]
        + [pltpu.VMEM(array.shape, array.dtype) for array in kept],
        compiler_params=pltpu.CompilerParams(vmem_limit_bytes=62 * 1024 * 1024),
    )(gu, qkv, gain_sums, *kept)


def tp_body(
    hidden_in,
    block_of,
    in_gain,
    w_query,
    w_key,
    w_value,
    w_output,
    q_gain,
    k_gain,
    post_gain,
    w_gate,
    w_up,
    w_down,
    cotangent,
):
    seq_count, tok_rows, model_width = hidden_in.shape
    n_ctx = lax.axis_size("ctx")
    block_rows = tok_rows // 2
    rows = seq_count * tok_rows
    head_dim = q_gain.shape[0]
    hidden = hidden_in.reshape(rows, model_width)
    cot_local = cotangent.reshape(rows, model_width)
    depth = w_query.shape[0]

    tables = rotation_tables(2 * n_ctx, block_rows, head_dim)
    (
        all_small,
        gains,
        log_totals,
        raw,
        queries,
        keys,
        values,
        attn,
        attn_in,
        mine_qkv,
        mine_output,
        mine_gu,
        mine_down,
        grad_out,
    ) = fore(
        block_of,
        in_gain,
        post_gain,
        tables,
        q_gain,
        k_gain,
        hidden,
        w_query,
        w_key,
        w_value,
        w_output,
        w_gate,
        w_up,
        w_down,
        cot_local,
    )
    mine_qkv = mine_qkv.reshape(model_width, -1)
    mine_output = mine_output.reshape(-1, model_width)
    output, post_sum, grad_mid, grad_branch, gu_total, part_down = feed_forward(
        attn, mine_output, hidden, gains, mine_gu, mine_down.reshape(-1, model_width), grad_out
    )
    grad_hidden, gain_sums, part_output, gu_sums, qkv_sums = back(
        all_small,
        tables,
        q_gain,
        k_gain,
        raw,
        queries,
        keys,
        values,
        attn,
        log_totals,
        hidden,
        grad_mid,
        gains,
        post_sum,
        gu_total,
        grad_branch,
        mine_output,
        attn_in,
        mine_qkv,
    )
    (
        part_gate,
        part_up,
        part_query,
        part_key,
        part_value,
        grad_hidden,
        output,
        part_down,
        part_output,
        part_in,
        part_post,
        sum_q_gain,
        sum_k_gain,
    ) = finish(
        gu_sums,
        qkv_sums,
        (grad_hidden, output, part_down, part_output),
        gain_sums,
        [weight.shape[1] for weight in (w_gate, w_up, w_query, w_key, w_value)],
    )
    return (
        output.reshape(seq_count, tok_rows, model_width),
        grad_hidden.reshape(seq_count, tok_rows, model_width),
        part_in.reshape(-1),
        part_query,
        part_key,
        part_value,
        part_output,
        sum_q_gain.reshape(-1),
        sum_k_gain.reshape(-1),
        part_post.reshape(-1),
        part_gate,
        part_up,
        part_down,
    )


def body(hidden_in, block_of, in_gain, w_query, w_key, w_value, w_output, q_gain, *rest):
    kv_heads = w_key.shape[1] // q_gain.shape[0]
    plan = tp_body if kv_heads == lax.axis_size("ctx") == 8 else gathered_weights_body
    return plan(hidden_in, block_of, in_gain, w_query, w_key, w_value, w_output, q_gain, *rest)


def solution(mesh):
    return jax.shard_map(
        body,
        mesh=mesh,
        in_specs=(
            P("fsdp", "ctx", None),
            P("fsdp", "ctx"),
            P(("ctx", "fsdp")),
            P(("ctx", "fsdp"), None),
            P(("ctx", "fsdp"), None),
            P(("ctx", "fsdp"), None),
            P(("ctx", "fsdp"), None),
            P(),
            P(),
            P(("ctx", "fsdp")),
            P(("ctx", "fsdp"), None),
            P(("ctx", "fsdp"), None),
            P(("ctx", "fsdp"), None),
            P("fsdp", "ctx", None),
        ),
        out_specs=(
            P("fsdp", "ctx", None),
            P("fsdp", "ctx", None),
            P(("ctx", "fsdp")),
            P(("ctx", "fsdp"), None),
            P(("ctx", "fsdp"), None),
            P(("ctx", "fsdp"), None),
            P(("ctx", "fsdp"), None),
            P(),
            P(),
            P(("ctx", "fsdp")),
            P(("ctx", "fsdp"), None),
            P(("ctx", "fsdp"), None),
            P(("ctx", "fsdp"), None),
        ),
        check_vma=False,
    )
```

```python
import functools
import math

import jax
import jax.numpy as jnp
import numpy as np
from jax import lax
from jax.experimental import pallas as pl
from jax.experimental.pallas import tpu as pltpu
from jax.sharding import PartitionSpec as P

EPS = 1e-06
THETA = 1000000.0


def rope_tables(positions, width):
    half_width = width // 2
    inverse = THETA ** (-(jnp.arange(half_width, dtype=jnp.float32) * 2.0 / width))
    angles = positions.astype(jnp.float32)[:, None] * inverse[None, :]
    return (jnp.cos(angles), jnp.sin(angles))


def rotate(values, cosine, sine):
    half_width = values.shape[-1] // 2
    first = values[..., :half_width]
    second = values[..., half_width:]
    cos_wide = cosine[:, None, :]
    sin_wide = sine[:, None, :]
    return jnp.concatenate(
        [first * cos_wide - second * sin_wide, second * cos_wide + first * sin_wide], axis=-1
    )


def norm_back(grad_normed, normed, scale):
    return scale * (grad_normed - normed * jnp.mean(grad_normed * normed, axis=-1, keepdims=True))


def gathered_weights_body(
    hidden_in,
    block_of,
    in_gain,
    w_query,
    w_key,
    w_value,
    w_output,
    q_gain,
    k_gain,
    post_gain,
    w_gate,
    w_up,
    w_down,
    cotangent,
):
    seq_count = hidden_in.shape[0]
    tok_rows = hidden_in.shape[1]
    flat_rows = seq_count * tok_rows
    model_width = hidden_in.shape[2]
    block_rows = tok_rows // 2
    block_total = 2 * lax.axis_size("ctx")
    seq_len = block_total * block_rows
    head_dim = q_gain.shape[0]
    q_heads = w_query.shape[1] // head_dim
    kv_heads = w_key.shape[1] // head_dim
    group_size = q_heads // kv_heads
    tile_blocks = math.gcd(block_total, max(1, 512 // block_rows))
    tile_rows = tile_blocks * block_rows
    q_scale = head_dim ** (-0.5)
    contract_rows = (((0,), (0,)), ((), ()))
    contract_cols = (((1,), (1,)), ((), ()))
    offsets = jnp.arange(block_rows, dtype=jnp.int32)
    positions = (block_of[:, :, None] * block_rows + offsets[None, None, :]).reshape(flat_rows)
    cosine, sine = rope_tables(positions, head_dim)
    residual = hidden_in.reshape(flat_rows, model_width).astype(jnp.float32)
    full_in_gain, full_query, full_key, full_value, full_output = (
        lax.all_gather(in_gain, ("ctx", "fsdp"), axis=0, tiled=True),
        lax.all_gather(w_query, ("ctx", "fsdp"), axis=0, tiled=True),
        lax.all_gather(w_key, ("ctx", "fsdp"), axis=0, tiled=True),
        lax.all_gather(w_value, ("ctx", "fsdp"), axis=0, tiled=True),
        lax.all_gather(w_output, ("ctx", "fsdp"), axis=0, tiled=True),
    )
    in_scale = lax.rsqrt(jnp.mean(residual * residual, axis=-1, keepdims=True) + EPS)
    in_normed = residual * in_scale
    attn_in = (in_normed * full_in_gain.astype(jnp.float32)).astype(jnp.bfloat16)
    q_raw = jnp.dot(attn_in, full_query, preferred_element_type=jnp.float32).reshape(
        flat_rows, q_heads, head_dim
    )
    k_raw = jnp.dot(attn_in, full_key, preferred_element_type=jnp.float32).reshape(
        flat_rows, kv_heads, head_dim
    )
    v_local = jnp.dot(attn_in, full_value, preferred_element_type=jnp.float32).astype(jnp.bfloat16)
    q_rms = lax.rsqrt(jnp.mean(q_raw * q_raw, axis=-1, keepdims=True) + EPS)
    q_unit = q_raw * q_rms
    queries = (rotate(q_unit * q_gain.astype(jnp.float32), cosine, sine) * q_scale).astype(
        jnp.bfloat16
    )
    k_rms = lax.rsqrt(jnp.mean(k_raw * k_raw, axis=-1, keepdims=True) + EPS)
    k_unit = k_raw * k_rms
    keys_local = rotate(k_unit * k_gain.astype(jnp.float32), cosine, sine).astype(jnp.bfloat16)
    all_keys, all_values, all_slots = (
        lax.all_gather(
            keys_local.reshape(seq_count, tok_rows, kv_heads * head_dim), "ctx", axis=1, tiled=True
        ),
        lax.all_gather(
            v_local.reshape(seq_count, tok_rows, kv_heads * head_dim), "ctx", axis=1, tiled=True
        ),
        lax.all_gather(block_of, "ctx", axis=1, tiled=True),
    )

    def tile_scores(query_tile, key_tile, query_pos, step):
        scores = jnp.einsum(
            "qhgd,khd->hgqk", query_tile, key_tile, preferred_element_type=jnp.float32
        )
        key_pos = step * tile_rows + jnp.arange(tile_rows, dtype=jnp.int32)
        visible = key_pos[None, :] <= query_pos[:, None]
        return (scores, visible)

    def sequence_tables(seq):
        key_blocks = all_keys[seq].reshape(block_total, block_rows, kv_heads, head_dim)
        value_blocks = all_values[seq].reshape(block_total, block_rows, kv_heads, head_dim)
        block_index = (
            jnp.zeros((block_total,), jnp.int32)
            .at[all_slots[seq]]
            .set(jnp.arange(block_total, dtype=jnp.int32))
        )
        return (key_blocks, value_blocks, block_index)

    def tile_index(block_index, step):
        return lax.dynamic_slice_in_dim(block_index, step * tile_blocks, tile_blocks)

    def fetch(table, block_index, step):
        return jnp.take(table, tile_index(block_index, step), axis=0).reshape(
            tile_rows, kv_heads, head_dim
        )

    log_totals = []
    attn_parts = []
    seq = 0
    key_blocks, value_blocks, block_index = sequence_tables(seq)
    for which in range(2):
        slot = 2 * seq + which
        query_tile = queries[slot * block_rows : (slot + 1) * block_rows].reshape(
            block_rows, kv_heads, group_size, head_dim
        )
        query_pos = positions[slot * block_rows : (slot + 1) * block_rows]
        tile_count = block_of[seq, which] // tile_blocks + 1

        def max_step(step, carry):
            running_max, running_sum = carry
            scores, visible = tile_scores(
                query_tile, fetch(key_blocks, block_index, step), query_pos, step
            )
            scores = jnp.where(visible, scores, -1e30)
            new_max = jnp.maximum(running_max, jnp.max(scores, axis=-1))
            running_sum = running_sum * jnp.exp(running_max - new_max) + jnp.sum(
                jnp.exp(scores - new_max[..., None]), axis=-1
            )
            return (new_max, running_sum)

        start_max = jnp.full((kv_heads, group_size, block_rows), -1e30, jnp.float32)
        start_sum = jnp.zeros((kv_heads, group_size, block_rows), jnp.float32)
        running_max, running_sum = lax.fori_loop(0, tile_count, max_step, (start_max, start_sum))
        log_total = running_max + jnp.log(running_sum)

        def value_step(step, total):
            scores, visible = tile_scores(
                query_tile, fetch(key_blocks, block_index, step), query_pos, step
            )
            probs = jnp.where(visible, jnp.exp(scores - log_total[..., None]), 0.0)
            return total + jnp.einsum(
                "hgqk,khd->qhgd",
                probs.astype(jnp.bfloat16),
                fetch(value_blocks, block_index, step),
                preferred_element_type=jnp.float32,
            )

        attn_part = lax.fori_loop(
            0,
            tile_count,
            value_step,
            jnp.zeros((block_rows, kv_heads, group_size, head_dim), jnp.float32),
        )
        log_totals.append(log_total)
        attn_parts.append(attn_part)
    attn_full = jnp.concatenate(attn_parts, axis=0)
    attn_bf = attn_full.reshape(flat_rows, q_heads * head_dim).astype(jnp.bfloat16)
    branch = jnp.dot(attn_bf, full_output, preferred_element_type=jnp.float32)
    hidden_mid = residual + branch
    full_post, full_gate, full_up, full_down = (
        lax.all_gather(post_gain, ("ctx", "fsdp"), axis=0, tiled=True),
        lax.all_gather(w_gate, ("ctx", "fsdp"), axis=0, tiled=True),
        lax.all_gather(w_up, ("ctx", "fsdp"), axis=0, tiled=True),
        lax.all_gather(w_down, ("ctx", "fsdp"), axis=0, tiled=True),
    )
    post_scale = lax.rsqrt(jnp.mean(hidden_mid * hidden_mid, axis=-1, keepdims=True) + EPS)
    post_normed = hidden_mid * post_scale
    mlp_in = (post_normed * full_post.astype(jnp.float32)).astype(jnp.bfloat16)
    gate_pre = jnp.dot(mlp_in, full_gate, preferred_element_type=jnp.float32)
    up_pre = jnp.dot(mlp_in, full_up, preferred_element_type=jnp.float32)
    sigmoid_gate = jax.nn.sigmoid(gate_pre)
    activated = gate_pre * sigmoid_gate
    inner = (activated * up_pre).astype(jnp.bfloat16)
    mlp_out = jnp.dot(inner, full_down, preferred_element_type=jnp.float32)
    output = (hidden_mid + mlp_out).astype(jnp.bfloat16)
    full_post, full_gate, full_up, full_down = (
        lax.all_gather(post_gain, ("ctx", "fsdp"), axis=0, tiled=True),
        lax.all_gather(w_gate, ("ctx", "fsdp"), axis=0, tiled=True),
        lax.all_gather(w_up, ("ctx", "fsdp"), axis=0, tiled=True),
        lax.all_gather(w_down, ("ctx", "fsdp"), axis=0, tiled=True),
    )
    grad_out = cotangent.reshape(flat_rows, model_width)
    grad_down = lax.dot_general(inner, grad_out, contract_rows, preferred_element_type=jnp.float32)
    part_down = lax.psum_scatter(grad_down, ("ctx", "fsdp"), scatter_dimension=0, tiled=True)
    grad_inner = lax.dot_general(
        grad_out, full_down, contract_cols, preferred_element_type=jnp.float32
    )
    grad_gate_pre = (
        grad_inner * up_pre * sigmoid_gate * (1.0 + gate_pre * (1.0 - sigmoid_gate))
    ).astype(jnp.bfloat16)
    grad_up_pre = (grad_inner * activated).astype(jnp.bfloat16)
    grad_gate = lax.dot_general(
        mlp_in, grad_gate_pre, contract_rows, preferred_element_type=jnp.float32
    )
    grad_up = lax.dot_general(
        mlp_in, grad_up_pre, contract_rows, preferred_element_type=jnp.float32
    )
    grad_mlp_in = lax.dot_general(
        grad_gate_pre, full_gate, contract_cols, preferred_element_type=jnp.float32
    ) + lax.dot_general(grad_up_pre, full_up, contract_cols, preferred_element_type=jnp.float32)
    grad_post_gain = jnp.sum(grad_mlp_in * post_normed, axis=0)
    grad_mid = grad_out.astype(jnp.float32) + norm_back(
        grad_mlp_in * full_post.astype(jnp.float32), post_normed, post_scale
    )
    part_post, part_gate, part_up = (
        lax.psum_scatter(grad_post_gain, ("ctx", "fsdp"), scatter_dimension=0, tiled=True),
        lax.psum_scatter(grad_gate, ("ctx", "fsdp"), scatter_dimension=0, tiled=True),
        lax.psum_scatter(grad_up, ("ctx", "fsdp"), scatter_dimension=0, tiled=True),
    )
    full_in_gain, full_query, full_key, full_value, full_output = (
        lax.all_gather(in_gain, ("ctx", "fsdp"), axis=0, tiled=True),
        lax.all_gather(w_query, ("ctx", "fsdp"), axis=0, tiled=True),
        lax.all_gather(w_key, ("ctx", "fsdp"), axis=0, tiled=True),
        lax.all_gather(w_value, ("ctx", "fsdp"), axis=0, tiled=True),
        lax.all_gather(w_output, ("ctx", "fsdp"), axis=0, tiled=True),
    )
    grad_branch = grad_mid.astype(jnp.bfloat16)
    grad_output = lax.dot_general(
        attn_bf, grad_branch, contract_rows, preferred_element_type=jnp.float32
    )
    grad_attn = lax.dot_general(
        grad_branch, full_output, contract_cols, preferred_element_type=jnp.float32
    ).astype(jnp.bfloat16)
    grad_attn = grad_attn.reshape(flat_rows, kv_heads, group_size, head_dim)
    query_grads = []
    seq = 0
    key_blocks, value_blocks, block_index = sequence_tables(seq)
    key_grads = jnp.zeros((block_total, block_rows, kv_heads, head_dim), jnp.float32)
    value_grads = jnp.zeros((block_total, block_rows, kv_heads, head_dim), jnp.float32)
    for which in range(2):
        slot = 2 * seq + which
        query_tile = queries[slot * block_rows : (slot + 1) * block_rows].reshape(
            block_rows, kv_heads, group_size, head_dim
        )
        query_pos = positions[slot * block_rows : (slot + 1) * block_rows]
        grad_tile = grad_attn[slot * block_rows : (slot + 1) * block_rows]
        tile_count = block_of[seq, which] // tile_blocks + 1
        delta = jnp.einsum("qhgd,qhgd->hgq", grad_tile.astype(jnp.float32), attn_parts[slot])
        log_total = log_totals[slot]

        def grad_step(step, carry):
            grad_query, keys_acc, values_acc = carry
            key_tile = fetch(key_blocks, block_index, step)
            scores, visible = tile_scores(query_tile, key_tile, query_pos, step)
            probs = jnp.where(visible, jnp.exp(scores - log_total[..., None]), 0.0)
            grad_probs = jnp.einsum(
                "qhgd,khd->hgqk",
                grad_tile,
                fetch(value_blocks, block_index, step),
                preferred_element_type=jnp.float32,
            )
            grad_scores = (probs * (grad_probs - delta[..., None])).astype(jnp.bfloat16)
            grad_query = grad_query + jnp.einsum(
                "hgqk,khd->qhgd", grad_scores, key_tile, preferred_element_type=jnp.float32
            )
            key_part = jnp.einsum(
                "hgqk,qhgd->khd", grad_scores, query_tile, preferred_element_type=jnp.float32
            )
            value_part = jnp.einsum(
                "hgqk,qhgd->khd",
                probs.astype(jnp.bfloat16),
                grad_tile,
                preferred_element_type=jnp.float32,
            )
            places = tile_index(block_index, step)
            keys_acc = keys_acc.at[places].add(
                key_part.reshape(tile_blocks, block_rows, kv_heads, head_dim)
            )
            values_acc = values_acc.at[places].add(
                value_part.reshape(tile_blocks, block_rows, kv_heads, head_dim)
            )
            return (grad_query, keys_acc, values_acc)

        start_query = jnp.zeros((block_rows, kv_heads, group_size, head_dim), jnp.float32)
        grad_query, key_grads, value_grads = lax.fori_loop(
            0, tile_count, grad_step, (start_query, key_grads, value_grads)
        )
        query_grads.append(grad_query)
    key_grad_list = [key_grads.reshape(seq_len, kv_heads * head_dim)]
    value_grad_list = [value_grads.reshape(seq_len, kv_heads * head_dim)]
    grad_keys, grad_values = (
        lax.psum_scatter(
            jnp.stack(key_grad_list, axis=0).astype(jnp.bfloat16),
            "ctx",
            scatter_dimension=1,
            tiled=True,
        ).astype(jnp.float32),
        lax.psum_scatter(
            jnp.stack(value_grad_list, axis=0).astype(jnp.bfloat16),
            "ctx",
            scatter_dimension=1,
            tiled=True,
        ).astype(jnp.float32),
    )
    grad_q_rot = (
        jnp.concatenate(query_grads, axis=0).reshape(flat_rows, q_heads, head_dim) * q_scale
    )
    grad_q_normed = rotate(grad_q_rot, cosine, -sine)
    grad_q_gain = jnp.sum(grad_q_normed * q_unit, axis=(0, 1))
    grad_q_raw = (
        norm_back(grad_q_normed * q_gain.astype(jnp.float32), q_unit, q_rms)
        .astype(jnp.bfloat16)
        .reshape(flat_rows, q_heads * head_dim)
    )
    grad_k_normed = rotate(grad_keys.reshape(flat_rows, kv_heads, head_dim), cosine, -sine)
    grad_k_gain = jnp.sum(grad_k_normed * k_unit, axis=(0, 1))
    grad_k_raw = (
        norm_back(grad_k_normed * k_gain.astype(jnp.float32), k_unit, k_rms)
        .astype(jnp.bfloat16)
        .reshape(flat_rows, kv_heads * head_dim)
    )
    grad_v_local = grad_values.reshape(flat_rows, kv_heads * head_dim).astype(jnp.bfloat16)
    grad_query_w = lax.dot_general(
        attn_in, grad_q_raw, contract_rows, preferred_element_type=jnp.float32
    )
    grad_key_w = lax.dot_general(
        attn_in, grad_k_raw, contract_rows, preferred_element_type=jnp.float32
    )
    grad_value_w = lax.dot_general(
        attn_in, grad_v_local, contract_rows, preferred_element_type=jnp.float32
    )
    grad_attn_in = lax.dot_general(
        grad_q_raw, full_query, contract_cols, preferred_element_type=jnp.float32
    )
    grad_attn_in = grad_attn_in + lax.dot_general(
        grad_k_raw, full_key, contract_cols, preferred_element_type=jnp.float32
    )
    grad_attn_in = grad_attn_in + lax.dot_general(
        grad_v_local, full_value, contract_cols, preferred_element_type=jnp.float32
    )
    grad_in_gain = jnp.sum(grad_attn_in * in_normed, axis=0)
    grad_input = grad_mid + norm_back(
        grad_attn_in * full_in_gain.astype(jnp.float32), in_normed, in_scale
    )
    part_in, part_query, part_key, part_value, part_output = (
        lax.psum_scatter(grad_in_gain, ("ctx", "fsdp"), scatter_dimension=0, tiled=True),
        lax.psum_scatter(grad_query_w, ("ctx", "fsdp"), scatter_dimension=0, tiled=True),
        lax.psum_scatter(grad_key_w, ("ctx", "fsdp"), scatter_dimension=0, tiled=True),
        lax.psum_scatter(grad_value_w, ("ctx", "fsdp"), scatter_dimension=0, tiled=True),
        lax.psum_scatter(grad_output, ("ctx", "fsdp"), scatter_dimension=0, tiled=True),
    )
    sum_q_gain, sum_k_gain = lax.psum((grad_q_gain, grad_k_gain), ("ctx", "fsdp"))
    return (
        output.reshape(seq_count, tok_rows, model_width),
        grad_input.reshape(seq_count, tok_rows, model_width),
        part_in,
        part_query,
        part_key,
        part_value,
        part_output,
        sum_q_gain,
        sum_k_gain,
        part_post,
        part_gate,
        part_up,
        part_down,
    )


MESH = pl.DeviceIdType.MESH
SUBS = 2


def ring_position(index, size):
    column, line = lax.rem(index, 2), lax.div(index, 2)
    return column * (line + 1) + (1 - column) * lax.rem(size - line, size)


def ring_member(position, size):
    late = lax.div(position + size // 2 - 1, size)
    beyond = lax.div(position + size - 1, size)
    return beyond * (1 - late) * (2 * position - 1) + late * 2 * (size - position)


class Ring:
    def __init__(self, size):
        self.size = size
        self.me = lax.axis_index("ctx")
        self.row = lax.axis_index("fsdp")
        self.position = ring_position(self.me, size)

    def member(self, way, steps):
        ahead = self.size - steps if way == 0 else steps
        return ring_member(lax.rem(self.position + ahead, self.size), self.size)

    def target(self, way):
        return (self.member(way, self.size - 1), self.row)

    def barrier(self):
        barrier = pltpu.get_barrier_semaphore()
        for way in range(2):
            pl.semaphore_signal(barrier, inc=1, device_id=self.target(way), device_id_type=MESH)
        pl.semaphore_wait(barrier, 2)


class GatherRing:
    def __init__(self, ring, own, out, send_sems, recv_sems):
        self.ring, self.own, self.out, self.send_sems, self.recv_sems = ring, own, out, send_sems, recv_sems
        self.half = own.shape[0] // 2
        self.sub = self.half // SUBS

    def copy(self, way, step, part, first=False):
        place = pl.ds(way * self.half + part * self.sub, self.sub)
        owner = self.ring.me if first else self.ring.member(way, step)
        source = self.own.at[place] if first else self.out.at[owner, place]
        return pltpu.make_async_remote_copy(
            src_ref=source,
            dst_ref=self.out.at[owner, place],
            send_sem=self.send_sems.at[way, step, part],
            recv_sem=self.recv_sems.at[way, step, part],
            device_id=self.ring.target(way),
            device_id_type=MESH,
        )

    def start(self, way, part):
        self.copy(way, 0, part, first=True).start()

    def step(self, step):
        for part in range(SUBS):
            for way in range(2):
                self.copy(way, step - 1, part).wait_recv()
                self.copy(way, step, part).start()

    def finish(self):
        last = self.ring.size - 2
        for part in range(SUBS):
            for way in range(2):
                self.copy(way, last, part).wait_recv()

        @pl.loop(0, last + 1)
        def _(step):
            for part in range(SUBS):
                for way in range(2):
                    self.copy(way, step, part).wait_send()

    def run(self):
        for way in range(2):
            self.start(way)

        @pl.loop(1, self.ring.size - 1)
        def _(step):
            self.step(step)

        self.finish()


def gather_sems(size):
    return [pltpu.SemaphoreType.DMA((2, size - 1, SUBS)), pltpu.SemaphoreType.DMA((2, size - 1, SUBS))]


class SumRing:
    def __init__(self, ring, compute, terms, outgoing, incoming, send_sems, recv_sems):
        self.ring, self.compute, self.terms = ring, compute, terms
        self.outgoing, self.incoming, self.send_sems, self.recv_sems = outgoing, incoming, send_sems, recv_sems
        self.half = terms.shape[1]
        self.sub = self.half // SUBS

    def copy(self, way, step, part):
        place = pl.ds(part * self.sub, self.sub)
        return pltpu.make_async_remote_copy(
            src_ref=self.outgoing.at[way, lax.rem(step, 2), place],
            dst_ref=self.incoming.at[way, step, place],
            send_sem=self.send_sems.at[way, step, part],
            recv_sem=self.recv_sems.at[way, step, part],
            device_id=self.ring.target(way),
            device_id_type=MESH,
        )

    def terms_of(self, step):
        self.compute([self.ring.member(way, step + 1) for way in range(2)])

    def begin(self):
        self.terms_of(0)
        for part in range(SUBS):
            place = pl.ds(part * self.sub, self.sub)
            for way in range(2):
                self.outgoing[way, 0, place] = self.terms[way, place].astype(jnp.bfloat16)
                self.copy(way, 0, part).start()

    def second(self):
        self.step(1, fresh=True)

    def step(self, step, fresh=False):
        self.terms_of(step)
        for part in range(SUBS):
            place = pl.ds(part * self.sub, self.sub)
            for way in range(2):
                self.copy(way, step - 1, part).wait_recv()
                total = self.terms[way, place] + self.incoming[way, step - 1, place].astype(jnp.float32)
                if not fresh:
                    self.copy(way, step - 2, part).wait_send()
                self.outgoing[way, lax.rem(step, 2), place] = total.astype(jnp.bfloat16)
                self.copy(way, step, part).start()

    def last_terms(self):
        self.compute([self.ring.me, self.ring.me])

    def result(self, way, part):
        last = self.ring.size - 2
        place = pl.ds(part * self.sub, self.sub)
        self.copy(way, last, part).wait_recv()
        return self.terms[way, place] + self.incoming[way, last, place].astype(jnp.float32)

    def parts(self):
        for part in range(SUBS):
            for way in range(2):
                start = way * self.half + part * self.sub
                yield way, part, slice(start, start + self.sub)

    def finish(self):
        for step in (self.ring.size - 3, self.ring.size - 2):
            for part in range(SUBS):
                for way in range(2):
                    self.copy(way, step, part).wait_send()

    def run(self):
        self.begin()
        self.second()

        @pl.loop(2, self.ring.size - 1)
        def _(step):
            self.step(step)

        self.last_terms()


def sum_scratch(size, rows, width):
    half = rows // 2
    return [
        pltpu.VMEM((2, half, width), jnp.float32),
        pltpu.VMEM((2, 2, half, width), jnp.bfloat16),
        pltpu.VMEM((2, size - 1, half, width), jnp.bfloat16),
        pltpu.SemaphoreType.DMA((2, size - 1, SUBS)),
        pltpu.SemaphoreType.DMA((2, size - 1, SUBS)),
    ]


class Square:
    def __init__(self, size):
        self.size = size
        self.me = lax.axis_index("ctx")
        self.row = lax.axis_index("fsdp")
        line, column = lax.div(self.me, 2), lax.rem(self.me, 2)
        half = lax.div(line, 2)
        self.inner = lax.rem(lax.div(line + 1, 2), 2) == 1
        self.outer = lax.rem(lax.div(line + 1, 2), 2) == 0
        self.beside = self.me + 1 - 2 * column
        self.along = self.me + 2 - 4 * lax.rem(line, 2)
        self.across = (3 - line) * 2 + column
        self.diagonal = self.along + 1 - 2 * column
        self.near = (2 - half) * 2 + column
        self.far = 6 * (1 - half) + column
        self.beside_near = (2 - half) * 2 + 1 - column
        self.beside_far = 6 * (1 - half) + 1 - column

    def targets(self):
        return [(member, self.row) for member in (self.beside, self.along, self.across)]


LED, KEPT = range(SUBS // 2), range(SUBS // 2, SUBS)


class SquareGather:
    def __init__(self, square, own, out, send_sems, recv_sems):
        self.square, self.own, self.out, self.send_sems, self.recv_sems = square, own, out, send_sems, recv_sems
        self.half = own.shape[0] // 2
        self.sub = self.half // SUBS
        me, rest = square.me, [(square.near, 0), (square.near, 1), (square.far, 0), (square.far, 1)]
        self.sent = [
            [(me, 0), (me, 1), (square.along, 1)] + rest + [(square.along, 0)],
            [(me, 0), (me, 1), (square.beside, 0)] + rest,
            [(me, 0), (me, 1), (square.along, 0), (square.along, 1)],
        ]

    def copy(self, link, slot, part):
        member, half = self.sent[link][slot]
        place = pl.ds(half * self.half + part * self.sub, self.sub)
        source = self.own.at[place] if slot < 2 else self.out.at[member, place]
        return remote(
            source,
            self.out.at[member, place],
            self.send_sems.at[link, slot, part],
            self.recv_sems.at[link, slot, part],
            self.square.targets()[link],
        )

    def start(self, half, part):
        for link in range(2):
            self.copy(link, half, part).start()

        @pl.when(self.square.inner)
        def _():
            self.copy(2, half, part).start()

    def relay(self, link, slot, *onward, parts=range(SUBS)):
        for part in parts:
            self.copy(link, slot, part).wait_recv()
            for next_link, next_slot in onward:
                self.copy(next_link, next_slot, part).start()

    def first(self):
        @pl.when(self.square.outer)
        def _():
            self.relay(0, 0, (1, 2))
            self.relay(1, 1, (0, 2))
            self.relay(1, 0, (0, 7), parts=LED)
            self.relay(1, 0, parts=KEPT)

        @pl.when(self.square.inner)
        def _():
            self.relay(1, 0, (2, 2))
            self.relay(2, 0, (1, 3))
            self.relay(1, 1, (2, 3), (0, 2))
            for part in range(SUBS):
                self.copy(0, 3, part).start()

    def second(self):
        @pl.when(self.square.outer)
        def _():
            self.relay(1, 3, (0, 3))
            self.relay(1, 4, (0, 4))

        @pl.when(self.square.inner)
        def _():
            self.relay(2, 1, (1, 4), (0, 4))

    def third(self):
        @pl.when(self.square.outer)
        def _():
            self.relay(1, 5, (0, 5))
            self.relay(1, 6, (0, 6))

        @pl.when(self.square.inner)
        def _():
            self.relay(2, 2, (1, 5), (0, 5))
            self.relay(2, 3, (1, 6), (0, 6))
            self.relay(0, 0, parts=LED)
            self.relay(0, 0, (1, 2), parts=KEPT)

    def finish(self):
        for slot in range(1, 7):
            self.relay(0, slot)
        self.relay(1, 2, parts=KEPT)
        for part in range(SUBS):
            for slot in range(7):
                self.copy(0, slot, part).wait_send()
            for slot in range(2):
                self.copy(1, slot, part).wait_send()
        for part in KEPT:
            self.copy(1, 2, part).wait_send()

        @pl.when(self.square.outer)
        def _():
            self.relay(0, 7, parts=LED)
            for part in LED:
                self.copy(0, 7, part).wait_send()
                self.copy(1, 2, part).wait_send()

        @pl.when(self.square.inner)
        def _():
            self.relay(1, 2, parts=LED)
            for part in range(SUBS):
                for slot in range(3, 7):
                    self.copy(1, slot, part).wait_send()
                for slot in range(4):
                    self.copy(2, slot, part).wait_send()


def square_sems():
    return [pltpu.SemaphoreType.DMA((3, 8, SUBS)), pltpu.SemaphoreType.DMA((3, 8, SUBS))]


class SquareSum:
    def __init__(self, square, compute, terms, outgoing, incoming, send_sems, recv_sems):
        self.square, self.compute, self.terms = square, compute, terms
        self.outgoing, self.incoming, self.send_sems, self.recv_sems = outgoing, incoming, send_sems, recv_sems
        self.half = outgoing.shape[1]
        self.sub = self.half // SUBS
        self.first_slot = (0, 8, 15)

    def copy(self, link, slot, part):
        at = self.first_slot[link] + slot
        place = pl.ds(part * self.sub, self.sub)
        return remote(
            self.outgoing.at[at, place],
            self.incoming.at[at, place],
            self.send_sems.at[link, slot, part],
            self.recv_sems.at[link, slot, part],
            self.square.targets()[link],
        )

    def arrived(self, link, slot, part):
        self.copy(link, slot, part).wait_recv()
        at = self.first_slot[link] + slot
        return self.incoming[at, part * self.sub : (part + 1) * self.sub].astype(jnp.float32)

    def term(self, which, half, part):
        start = half * self.half + part * self.sub
        return self.terms[which, start : start + self.sub]

    def send(self, link, slot, which, half, *received, parts=range(SUBS)):
        at = self.first_slot[link] + slot
        for part in parts:
            total = self.term(which, half, part)
            for source in received:
                total = total + self.arrived(*source, part)
            self.outgoing[at, part * self.sub : (part + 1) * self.sub] = total.astype(jnp.bfloat16)
            self.copy(link, slot, part).start()

    def begin(self):
        square = self.square
        self.compute(square.beside_far, 0)
        self.send(0, 0, 0, 0)
        self.send(0, 1, 0, 1)
        self.compute(square.beside_near, 1)
        self.send(0, 2, 1, 0)
        self.send(0, 3, 1, 1)
        self.compute(square.diagonal, 2)
        self.send(1, 0, 2, 0, parts=KEPT)

        @pl.when(square.outer)
        def _():
            self.send(0, 7, 2, 0, parts=LED)

        @pl.when(square.inner)
        def _():
            self.send(1, 0, 2, 0, parts=LED)

        self.send(0, 4, 2, 1)
        self.compute(square.far, 0)
        self.compute(square.near, 1)

    def first(self):
        @pl.when(self.square.outer)
        def _():
            self.send(1, 1, 0, 0, (0, 0))
            self.send(1, 2, 0, 1, (0, 1))

        @pl.when(self.square.inner)
        def _():
            self.send(2, 0, 0, 0, (0, 0), (1, 1))

        self.compute(self.square.beside, 3)
        self.send(0, 6, 3, 1)
        self.send(0, 5, 3, 0, (1, 0), parts=KEPT)

        @pl.when(self.square.outer)
        def _():
            self.send(0, 5, 3, 0, (1, 0), parts=LED)

        @pl.when(self.square.inner)
        def _():
            self.send(0, 5, 3, 0, parts=LED)

        self.compute(self.square.along, 2)
        self.compute(self.square.me, 4)

    def second(self):
        @pl.when(self.square.outer)
        def _():
            self.send(1, 3, 1, 0, (0, 2))
            self.send(1, 4, 1, 1, (0, 3))
            self.send(1, 5, 2, 0, (0, 7), parts=LED)
            self.send(1, 5, 2, 0, parts=KEPT)

        @pl.when(self.square.inner)
        def _():
            self.send(2, 1, 0, 1, (0, 1), (1, 2))
            self.send(1, 5, 2, 0, (2, 0))
            self.send(2, 2, 1, 0, (0, 2), (1, 3))

    def third(self):
        @pl.when(self.square.outer)
        def _():
            self.send(1, 6, 2, 1, (0, 4))

        @pl.when(self.square.inner)
        def _():
            self.send(2, 3, 1, 1, (0, 3), (1, 4))
            self.send(1, 6, 2, 1, (0, 4), (2, 1))
            for half in range(2):
                for part in range(SUBS):
                    start = half * self.half + part * self.sub
                    self.terms[4, start : start + self.sub] = self.term(4, half, part) + self.arrived(2, 2 + half, part)

    def parts(self):
        for half in range(2):
            for part in range(SUBS):
                start = half * self.half + part * self.sub
                yield half, part, slice(start, start + self.sub)

    def result(self, half, part):
        return self.term(4, half, part) + self.arrived(0, 5 + half, part) + self.arrived(1, 5 + half, part)

    def finish(self):
        for part in range(SUBS):
            for slot in range(7):
                self.copy(0, slot, part).wait_send()
            for slot in (5, 6):
                self.copy(1, slot, part).wait_send()
        for part in KEPT:
            self.copy(1, 0, part).wait_send()

        @pl.when(self.square.outer)
        def _():
            for part in LED:
                self.copy(0, 7, part).wait_send()
            for part in range(SUBS):
                for slot in range(1, 5):
                    self.copy(1, slot, part).wait_send()

        @pl.when(self.square.inner)
        def _():
            for part in LED:
                self.copy(1, 0, part).wait_send()
            for part in range(SUBS):
                for slot in range(4):
                    self.copy(2, slot, part).wait_send()


def square_sum_scratch(rows, width):
    return [
        pltpu.VMEM((5, rows, width), jnp.float32),
        pltpu.VMEM((19, rows // 2, width), jnp.bfloat16),
        pltpu.VMEM((19, rows // 2, width), jnp.bfloat16),
    ] + square_sems()


def block_terms_t(left, weight, terms, factors, product_sum):
    def compute(member, which):
        @pl.loop(0, weight.shape[0] // TILE)
        def _(tile):
            columns = pl.ds(pl.multiple_of(tile * TILE, TILE), TILE)
            terms[which, :, columns] = lax.dot_general(
                left[member], weight[columns, :], (((1,), (1,)), ((), ())), preferred_element_type=jnp.float32
            )
            product_sum[:, columns] = product_sum[:, columns] + jnp.sum(
                terms[which, :, columns] * factors[member, :, columns].astype(jnp.float32), axis=0, keepdims=True
            )

    return compute


TILE = 512


def row_terms(left, weight, terms):
    half = terms.shape[1]

    def compute(members):
        lines = jnp.concatenate([left[members[way], way * half : (way + 1) * half] for way in range(2)], axis=0)

        @pl.loop(0, weight.shape[1] // TILE)
        def _(tile):
            columns = pl.ds(pl.multiple_of(tile * TILE, TILE), TILE)
            product = jnp.dot(lines, weight[:, columns], preferred_element_type=jnp.float32)
            for way in range(2):
                terms[way, :, columns] = product[way * half : (way + 1) * half]

    return compute


def row_terms_t(left, weight, terms):
    half = terms.shape[1]
    tile = terms.shape[2] // weight.shape[0]

    def compute(members):
        lines = jnp.concatenate([left[members[way], way * half : (way + 1) * half] for way in range(2)], axis=0)

        @pl.loop(0, weight.shape[0])
        def _(block):
            columns = pl.ds(pl.multiple_of(block * tile, tile), tile)
            product = lax.dot_general(
                lines,
                weight[block].reshape(tile, weight.shape[-1]),
                (((1,), (1,)), ((), ())),
                preferred_element_type=jnp.float32,
            )
            for way in range(2):
                terms[way, :, columns] = product[way * half : (way + 1) * half]

    return compute


VMEM_SPEC = pl.BlockSpec(memory_space=pltpu.VMEM)
ANY_SPEC = pl.BlockSpec(memory_space=pl.ANY)


def ctx_peer(ring, ahead):
    return lax.rem(ring.me + ahead, ring.size)


def across(row, n_fsdp):
    return lax.rem(row + n_fsdp // 2, n_fsdp)


def beside(row):
    return row + 1 - 2 * lax.rem(row, 2)


def remote(source, target, send_sem, recv_sem, device):
    return pltpu.make_async_remote_copy(
        src_ref=source,
        dst_ref=target,
        send_sem=send_sem,
        recv_sem=recv_sem,
        device_id=device,
        device_id_type=MESH,
    )


def greet(devices):
    barrier = pltpu.get_barrier_semaphore()
    for device in devices:
        pl.semaphore_signal(barrier, inc=1, device_id=device, device_id_type=MESH)
    pl.semaphore_wait(barrier, len(devices))


def near_devices(ring, n_fsdp):
    return [(ctx_peer(ring, ahead), ring.row) for ahead in range(1, ring.size)] + [
        (ring.me, lax.rem(ring.row + ahead, n_fsdp)) for ahead in range(1, n_fsdp)
    ]


class Spread:
    def __init__(self, ring, n_fsdp, block, out, send_sems, recv_sems):
        self.ring, self.n_fsdp, self.block, self.out = ring, n_fsdp, block, out
        self.send_sems, self.recv_sems = send_sems, recv_sems

    def along_ctx(self, ahead):
        return remote(
            self.block,
            self.out.at[self.ring.row, self.ring.me],
            self.send_sems.at[ahead],
            self.recv_sems.at[ahead],
            (ctx_peer(self.ring, ahead), self.ring.row),
        )

    def along_fsdp(self, ahead):
        line = self.out.at[self.ring.row]
        sem = self.ring.size + ahead
        row = lax.rem(self.ring.row + ahead, self.n_fsdp)
        return remote(line, line, self.send_sems.at[sem], self.recv_sems.at[sem], (self.ring.me, row))

    def begin(self):
        for ahead in range(1, self.ring.size):
            self.along_ctx(ahead).start()
        self.out[self.ring.row, self.ring.me] = self.block[...]

    def collect(self):
        for ahead in range(1, self.ring.size):
            self.along_ctx(ahead).wait_recv()
        for ahead in range(1, self.n_fsdp):
            self.along_fsdp(ahead).start()
        for ahead in range(1, self.n_fsdp):
            self.along_fsdp(ahead).wait_recv()

    def finish(self):
        for ahead in range(1, self.ring.size):
            self.along_ctx(ahead).wait_send()
        for ahead in range(1, self.n_fsdp):
            self.along_fsdp(ahead).wait_send()


class SmallSum:
    def __init__(self, ring, n_fsdp, blocks, by_ctx, part, by_fsdp, send_sems, recv_sems):
        self.ring, self.n_fsdp, self.blocks, self.by_ctx, self.part, self.by_fsdp = (
            ring,
            n_fsdp,
            blocks,
            by_ctx,
            part,
            by_fsdp,
        )
        self.send_sems, self.recv_sems = send_sems, recv_sems

    def along_ctx(self, ahead):
        member = ctx_peer(self.ring, ahead)
        return remote(
            self.blocks.at[member],
            self.by_ctx.at[self.ring.me],
            self.send_sems.at[ahead],
            self.recv_sems.at[ahead],
            (member, self.ring.row),
        )

    def along_fsdp(self, ahead):
        row = lax.rem(self.ring.row + ahead, self.n_fsdp)
        sem = self.ring.size + ahead
        return remote(
            self.part.at[lax.div(row, 2)],
            self.by_fsdp.at[self.ring.row],
            self.send_sems.at[sem],
            self.recv_sems.at[sem],
            (self.ring.me, row),
        )

    def begin(self):
        for ahead in range(1, self.ring.size):
            self.along_ctx(ahead).start()
        self.by_ctx[self.ring.me] = self.blocks[self.ring.me]

    def cross(self):
        for ahead in range(1, self.ring.size):
            self.along_ctx(ahead).wait_recv()
        self.part[...] = jnp.sum(self.by_ctx[...], axis=0)
        for ahead in range(1, self.n_fsdp):
            self.along_fsdp(ahead).start()
        self.by_fsdp[self.ring.row] = self.part[lax.div(self.ring.row, 2)]

    def result(self):
        for ahead in range(1, self.n_fsdp):
            self.along_fsdp(ahead).wait_recv()
        return jnp.sum(self.by_fsdp[...], axis=0)

    def finish(self):
        for ahead in range(1, self.ring.size):
            self.along_ctx(ahead).wait_send()
        for ahead in range(1, self.n_fsdp):
            self.along_fsdp(ahead).wait_send()


def small_sems(size, n_fsdp):
    return [pltpu.SemaphoreType.DMA((size + n_fsdp,)), pltpu.SemaphoreType.DMA((size + n_fsdp,))]


class Rows:
    def __init__(self, ring, n_fsdp, shard, out, send_sems, recv_sems):
        own, far, twin = ring.row, across(ring.row, n_fsdp), beside(ring.row)
        self.keep = pltpu.make_async_copy(shard, out.at[own], send_sems.at[3])
        self.to_far = remote(shard, out.at[own], send_sems.at[0], recv_sems.at[0], (ring.me, far))
        self.to_twin = remote(shard, out.at[own], send_sems.at[1], recv_sems.at[1], (ring.me, twin))
        self.pass_on = remote(out.at[far], out.at[far], send_sems.at[2], recv_sems.at[2], (ring.me, twin))

    def begin(self):
        self.keep.start()
        self.to_far.start()
        self.to_twin.start()

    def relay(self):
        self.to_far.wait_recv()
        self.pass_on.start()

    def finish(self):
        self.keep.wait()
        self.to_far.wait_send()
        self.to_twin.wait()
        self.pass_on.wait()


def rows_sems():
    return [pltpu.SemaphoreType.DMA((4,)), pltpu.SemaphoreType.DMA((3,))]


class Links:
    def __init__(self, ring, n_fsdp, out, place, send_sems, recv_sems):
        self.ring, self.out, self.place, self.send_sems, self.recv_sems = ring, out, place, send_sems, recv_sems
        far, twin = across(ring.row, n_fsdp), beside(ring.row)
        self.to_far = self.link(0, ring.row, far)
        self.to_twin = self.link(1, ring.row, twin)
        self.pass_on = self.link(2, far, twin)

    def link(self, which, row, target):
        block = self.out.at[:, row, :, self.place]
        return remote(block, block, self.send_sems.at[which], self.recv_sems.at[which], (self.ring.me, target))

    def begin(self):
        self.to_far.start()
        self.to_twin.start()

    def relay(self):
        self.to_far.wait_recv()
        self.pass_on.start()

    def arrive(self):
        self.to_twin.wait_recv()
        self.pass_on.wait_recv()

    def finish(self):
        self.to_far.wait_send()
        self.to_twin.wait_send()
        self.pass_on.wait_send()


def links_sems():
    return [pltpu.SemaphoreType.DMA((3,)), pltpu.SemaphoreType.DMA((3,))]


class Pieces:
    def __init__(self, ring, shard, out, start, send_sems, recv_sems):
        self.ring, self.shard, self.out, self.send_sems, self.recv_sems = ring, shard, out, send_sems, recv_sems
        self.width = shard.shape[1] // ring.size
        self.place = pl.ds(start, self.width)

    def piece(self, ahead):
        member = ctx_peer(self.ring, ahead)
        source = self.shard.at[:, pl.ds(pl.multiple_of(member * self.width, self.width), self.width)]
        target = self.out.at[self.ring.me, self.ring.row, :, self.place]
        if ahead == 0:
            return pltpu.make_async_copy(source, target, self.send_sems.at[0])
        return remote(source, target, self.send_sems.at[ahead], self.recv_sems.at[ahead], (member, self.ring.row))

    def begin(self):
        for ahead in range(self.ring.size):
            self.piece(ahead).start()

    def arrive(self):
        self.piece(0).wait()
        for ahead in range(1, self.ring.size):
            self.piece(ahead).wait_recv()

    def finish(self):
        for ahead in range(1, self.ring.size):
            self.piece(ahead).wait_send()


class Columns:
    def __init__(self, ring, n_fsdp, shard, out, start, send_sems, recv_sems, link_send, link_recv):
        self.pieces = Pieces(ring, shard, out, start, send_sems, recv_sems)
        self.links = Links(ring, n_fsdp, out, self.pieces.place, link_send, link_recv)
        self.begin, self.relay, self.arrive = self.pieces.begin, self.links.relay, self.links.arrive

    def spread(self):
        self.pieces.arrive()
        self.links.begin()

    def finish(self):
        self.pieces.finish()
        self.links.finish()


def pieces_sems(size):
    return [pltpu.SemaphoreType.DMA((size,)), pltpu.SemaphoreType.DMA((size,))]


class RowGrads:
    def __init__(self, ring, n_fsdp, part, from_twin, to_far, from_far, send_sems, recv_sems):
        own, far, twin = ring.row, across(ring.row, n_fsdp), beside(ring.row)
        self.part, self.from_twin, self.to_far, self.from_far = part, from_twin, to_far, from_far
        self.own, self.far = own, far
        twin_far = across(twin, n_fsdp)
        self.first = [
            remote(part.at[twin], from_twin.at[0], send_sems.at[0], recv_sems.at[0], (ring.me, twin)),
            remote(part.at[twin_far], from_twin.at[1], send_sems.at[1], recv_sems.at[1], (ring.me, twin)),
        ]
        if to_far is None:
            self.to_far = part.at[far]
        self.second = remote(self.to_far, from_far, send_sems.at[2], recv_sems.at[2], (ring.me, far))

    def begin(self):
        self.first[1].start()
        self.first[0].start()

    def cross(self):
        self.first[1].wait_recv()
        self.to_far[...] = (
            self.part[self.far].astype(jnp.float32) + self.from_twin[1].astype(jnp.float32)
        ).astype(jnp.bfloat16)
        self.second.start()

    def result(self):
        self.first[0].wait_recv()
        self.second.wait_recv()
        return (
            self.part[self.own].astype(jnp.float32)
            + self.from_twin[0].astype(jnp.float32)
            + self.from_far[...].astype(jnp.float32)
        )

    def finish(self):
        for copy in self.first + [self.second]:
            copy.wait_send()


def row_grads_sems():
    return [pltpu.SemaphoreType.DMA((3,)), pltpu.SemaphoreType.DMA((3,))]


def row_grads_scratch(shape):
    return [
        pltpu.VMEM((2,) + shape, jnp.bfloat16),
        pltpu.VMEM(shape, jnp.bfloat16),
        pltpu.VMEM(shape, jnp.bfloat16),
    ] + row_grads_sems()


class Deal:
    def __init__(self, ring, total, arrived, send_sems, recv_sems):
        self.ring, self.total, self.arrived = ring, total, arrived
        self.send_sems, self.recv_sems = send_sems, recv_sems

    def piece(self, ahead):
        member = ctx_peer(self.ring, ahead)
        source, target = self.total.at[member], self.arrived.at[self.ring.me]
        if ahead == 0:
            return pltpu.make_async_copy(source, target, self.send_sems.at[0])
        return remote(source, target, self.send_sems.at[ahead], self.recv_sems.at[ahead], (member, self.ring.row))

    def begin(self):
        for ahead in range(self.ring.size):
            self.piece(ahead).start()

    def finish(self):
        for ahead in range(self.ring.size):
            self.piece(ahead).wait()


def deal_sems(size):
    return [pltpu.SemaphoreType.DMA((size,)), pltpu.SemaphoreType.DMA((size,))]


def params(collective_id):
    return pltpu.CompilerParams(
        collective_id=collective_id, has_side_effects=True, vmem_limit_bytes=62 * 1024 * 1024
    )


def head_norm(raw):
    return lax.rsqrt(jnp.mean(raw * raw, axis=-1, keepdims=True) + EPS)


def turn(values, cosine, sine):
    return values * cosine + pltpu.roll(values, values.shape[-1] // 2, 1) * sine


class Places:
    def __init__(self, ring, n_fsdp, all_small, starts, offsets, cosine, sine, places):
        self.ring, self.n_fsdp, self.all_small = ring, n_fsdp, all_small
        self.starts, self.offsets, self.cosine, self.sine, self.places = starts, offsets, cosine, sine, places
        self.block_rows = offsets.shape[1]

    def block(self, member, which):
        return self.all_small[self.ring.row, member, 2:3, which : which + 1]

    def fill(self):
        count = self.starts.shape[1]
        numbers = lax.broadcasted_iota(jnp.int32, (count, 1), 0).astype(jnp.float32)
        offset = lax.broadcasted_iota(jnp.int32, (self.block_rows, self.places.shape[1]), 0).astype(jnp.float32)
        for slot in range(count):
            block = self.block(slot // 2, slot % 2)
            chosen = (numbers == block).astype(jnp.float32)
            cos_start = jnp.sum(chosen * self.starts[0], axis=0, keepdims=True)
            sin_start = jnp.sum(chosen * self.starts[1], axis=0, keepdims=True)
            at = slice(slot * self.block_rows, (slot + 1) * self.block_rows)
            self.cosine[at] = cos_start * self.offsets[0] - sin_start * self.offsets[1]
            self.sine[at] = sin_start * self.offsets[0] + cos_start * self.offsets[1]
            self.places[at] = offset + block * self.block_rows

    def visible(self, member):
        width = self.places.shape[1]
        lane = lax.broadcasted_iota(jnp.int32, (1, width), 1).astype(jnp.float32)
        rows = float(self.block_rows)
        query = lane + jnp.where(lane < rows, self.block(member, 0) * rows, self.block(member, 1) * rows - rows)
        return self.places[...] <= query


def rotation_tables(blocks, block_rows, head):
    inverse = (THETA ** (-(np.arange(head // 2, dtype=np.float32) * np.float32(2.0) / head))).astype(np.float64)

    def both(at):
        angles = at.astype(np.float64)[:, None] * inverse[None, :]
        cosine, sine = np.cos(angles), np.sin(angles)
        return jnp.asarray(
            np.stack(
                [np.concatenate([cosine, cosine], axis=1), np.concatenate([-sine, sine], axis=1)], axis=0
            ).astype(np.float32)
        )

    return both(np.arange(blocks) * block_rows), both(np.arange(block_rows))


def fore_kernel(
    size,
    n_fsdp,
    q_heads,
    blocks,
    in_gain,
    post_gain,
    starts,
    offsets,
    q_gain,
    k_gain,
    hidden,
    w_query,
    w_key,
    w_value,
    w_output,
    w_gate,
    w_up,
    w_down,
    cotangent,
    all_small,
    gains,
    log_totals,
    raw_out,
    queries_out,
    keys_out,
    values_out,
    attn_out,
    attn_in_out,
    w_qkv_out,
    output_out,
    gu_out,
    down_out,
    grad_out,
    small,
    attn_in,
    w_qkv,
    cosine,
    sine,
    places_ref,
    values_t,
    raw,
    queries,
    keys,
    values,
    attn,
    small_send,
    small_recv,
    local_sems,
    *scratch,
):
    ring = Ring(size)
    head = q_gain.shape[1]
    tokens = hidden.shape[0]
    depth = in_gain.shape[1]
    q_width = q_heads * head
    k_width = w_key.shape[1] // size
    ff = w_gate.shape[1] // size
    columns_q = Columns(ring, n_fsdp, w_query, w_qkv, 0, *scratch[0:4])
    columns_k = Columns(ring, n_fsdp, w_key, w_qkv, q_width, *scratch[4:8])
    columns_v = Columns(ring, n_fsdp, w_value, w_qkv, q_width + k_width, *scratch[8:12])
    columns_gate = Columns(ring, n_fsdp, w_gate, gu_out, 0, *scratch[12:16])
    pieces_up = Pieces(ring, w_up, gu_out, ff, *scratch[16:18])
    rows_output = Rows(ring, n_fsdp, w_output, output_out, *scratch[18:20])
    rows_down = Rows(ring, n_fsdp, w_down, down_out, *scratch[20:22])
    square = Square(size)
    gathering = SquareGather(square, hidden, attn_in, *scratch[22:24])
    gathering_cot = SquareGather(square, cotangent, grad_out, *scratch[24:26])
    places = Places(ring, n_fsdp, all_small, starts, offsets, cosine, sine, places_ref)

    side = lax.rem(ring.row, 2)
    lane = lax.broadcasted_iota(jnp.int32, (1, 2 * depth), 1)
    mine = lax.div(lane, depth) == side
    small[...] = jnp.zeros_like(small)
    for row, part in enumerate((in_gain, post_gain)):
        part_row = part[...].astype(jnp.float32)
        small[row : row + 1] = jnp.where(mine, jnp.concatenate([part_row, part_row], axis=1), 0.0)
    small[2:3] = jnp.where(lane == 0, blocks[0, 0], jnp.where(lane == 1, blocks[0, 1], 0)).astype(jnp.float32)
    greet(near_devices(ring, n_fsdp))
    sharing = Spread(ring, n_fsdp, small, all_small, small_send, small_recv)
    sharing.begin()
    for part in range(SUBS):
        for way in range(2):
            gathering.start(way, part)
    for columns in (columns_q, columns_k, columns_v):
        columns.begin()
    keep = pltpu.make_async_copy(hidden, attn_in.at[ring.me], local_sems.at[0])
    keep.start()
    sharing.collect()
    rows_output.begin()
    rows_down.begin()
    for pair in range(size * n_fsdp // 2):
        member, chip = pair // (n_fsdp // 2), pair % (n_fsdp // 2)
        gains[:, pair * 128 : (pair + 1) * 128] = all_small[2 * chip, member] + all_small[2 * chip + 1, member]
    keep_cot = pltpu.make_async_copy(cotangent, grad_out.at[ring.me], local_sems.at[1])
    keep_cot.start()
    gathering.first()
    places.fill()
    gathering.second()
    for columns in (columns_q, columns_k, columns_v):
        columns.spread()
    gathering.third()
    rows_output.relay()
    for columns in (columns_q, columns_k, columns_v):
        columns.relay()
    columns_gate.begin()
    for part in range(SUBS):
        for way in range(2):
            gathering_cot.start(way, part)
    pieces_up.begin()
    for columns in (columns_q, columns_k, columns_v):
        columns.arrive()
    gathering.finish()
    keep.wait()
    save_qkv = pltpu.make_async_copy(w_qkv, w_qkv_out, local_sems.at[3])
    save_qkv.start()
    width = hidden.shape[1]

    @pl.loop(0, size)
    def _(member):
        at = pl.ds(pl.multiple_of(member * tokens, tokens), tokens)
        rows = attn_in[member].astype(jnp.float32)
        scale = lax.rsqrt(jnp.mean(rows * rows, axis=-1, keepdims=True) + EPS)
        attn_in[member] = (rows * scale * gains[0:1]).astype(jnp.bfloat16)
        product = jnp.dot(
            attn_in[member], w_qkv[...].reshape(width, w_qkv.shape[3]), preferred_element_type=jnp.float32
        )
        raw[at, :] = product[:, : q_width + head]
        for which in range(q_heads + 1):
            values_raw = product[:, which * head : (which + 1) * head]
            gain = q_gain if which < q_heads else k_gain
            turned = turn(values_raw * head_norm(values_raw) * gain[...].astype(jnp.float32), cosine[at, :], sine[at, :])
            if which < q_heads:
                queries[member, which] = (turned * head**-0.5).astype(jnp.bfloat16)
            else:
                keys[at, :] = turned.astype(jnp.bfloat16)
        fresh = product[:, q_width + head :]
        values[at, :] = fresh.astype(jnp.bfloat16)
        values_t[:, at] = fresh.T.astype(jnp.bfloat16)

    @pl.loop(0, size)
    def _(member):
        visible = places.visible(member)
        for which in range(q_heads):
            scores = lax.dot_general(
                keys[...], queries[member, which], (((1,), (1,)), ((), ())), preferred_element_type=jnp.float32
            )
            scores = jnp.where(visible, scores, -1e30)
            peak = jnp.max(scores, axis=0, keepdims=True)
            weights = jnp.exp(scores - peak)
            total = jnp.sum(weights, axis=0, keepdims=True)
            probs = (weights * (1.0 / total)).astype(jnp.bfloat16)
            mixed = jnp.dot(values_t[...], probs, preferred_element_type=jnp.float32)
            attn[member, :, which * head : (which + 1) * head] = mixed.T.astype(jnp.bfloat16)
            log_totals[member, which : which + 1, :] = peak + jnp.log(total)

    save_in = pltpu.make_async_copy(attn_in, attn_in_out, local_sems.at[2])
    save_in.start()
    saves = [
        pltpu.make_async_copy(source, target, local_sems.at[4 + which])
        for which, (source, target) in enumerate(
            ((raw, raw_out), (queries, queries_out), (keys, keys_out), (values, values_out), (attn, attn_out))
        )
    ]
    for save in saves:
        save.start()
    gathering_cot.first()
    rows_down.relay()
    columns_gate.spread()
    gathering_cot.second()
    gathering_cot.third()
    columns_gate.relay()
    gathering_cot.finish()
    sharing.finish()
    columns_gate.arrive()
    pieces_up.arrive()
    for columns in (columns_q, columns_k, columns_v, columns_gate, pieces_up):
        columns.finish()
    rows_output.finish()
    rows_down.finish()
    keep_cot.wait()
    for save in saves + [save_in, save_qkv]:
        save.wait()


def fore(blocks, in_gain, post_gain, tables, q_gain, k_gain, hidden, w_query, w_key, w_value, w_output, w_gate, w_up, w_down, cotangent):
    size, n_fsdp = lax.axis_size("ctx"), lax.axis_size("fsdp")
    rows, width = hidden.shape
    depth = w_query.shape[0]
    head = q_gain.shape[0]
    q_heads = w_query.shape[1] // size // head
    everyone = size * rows
    qkv_share = (w_query.shape[1] + w_key.shape[1] + w_value.shape[1]) // size
    gu_share = (w_gate.shape[1] + w_up.shape[1]) // size
    f32, bf16 = jnp.float32, jnp.bfloat16
    return pl.pallas_call(
        functools.partial(fore_kernel, size, n_fsdp, q_heads),
        out_shape=[
            jax.ShapeDtypeStruct((n_fsdp, size, 8, 2 * depth), f32),
            jax.ShapeDtypeStruct((8, width), f32),
            jax.ShapeDtypeStruct((size, q_heads, rows), f32),
            jax.ShapeDtypeStruct((everyone, (q_heads + 1) * head), f32),
            jax.ShapeDtypeStruct((size, q_heads, rows, head), bf16),
            jax.ShapeDtypeStruct((everyone, head), bf16),
            jax.ShapeDtypeStruct((everyone, head), bf16),
            jax.ShapeDtypeStruct((size, rows, q_heads * head), bf16),
            jax.ShapeDtypeStruct((size, rows, width), bf16),
            jax.ShapeDtypeStruct((size, n_fsdp, depth, qkv_share), bf16),
            jax.ShapeDtypeStruct((n_fsdp,) + w_output.shape, bf16),
            jax.ShapeDtypeStruct((size, n_fsdp, depth, gu_share), bf16),
            jax.ShapeDtypeStruct((n_fsdp,) + w_down.shape, bf16),
            jax.ShapeDtypeStruct((size, rows, width), bf16),
        ],
        in_specs=[pl.BlockSpec(memory_space=pltpu.SMEM)] + [VMEM_SPEC] * 7 + [ANY_SPEC] * 8,
        out_specs=[VMEM_SPEC] * 3 + [ANY_SPEC] * 11,
        scratch_shapes=[
            pltpu.VMEM((8, 2 * depth), f32),
            pltpu.VMEM((size, rows, width), bf16),
            pltpu.VMEM((size, n_fsdp, depth, qkv_share), bf16),
            pltpu.VMEM((everyone, head), f32),
            pltpu.VMEM((everyone, head), f32),
            pltpu.VMEM((everyone, head), f32),
            pltpu.VMEM((head, everyone), bf16),
            pltpu.VMEM((everyone, (q_heads + 1) * head), f32),
            pltpu.VMEM((size, q_heads, rows, head), bf16),
            pltpu.VMEM((everyone, head), bf16),
            pltpu.VMEM((everyone, head), bf16),
            pltpu.VMEM((size, rows, q_heads * head), bf16),
        ]
        + small_sems(size, n_fsdp)
        + [pltpu.SemaphoreType.DMA((9,))]
        + (pieces_sems(size) + links_sems()) * 4
        + pieces_sems(size)
        + rows_sems() * 2
        + square_sems() * 2,
        compiler_params=params(2),
    )(
        blocks,
        in_gain.reshape(1, depth),
        post_gain.reshape(1, depth),
        *tables,
        q_gain.reshape(1, head),
        k_gain.reshape(1, head),
        hidden,
        w_query,
        w_key,
        w_value,
        w_output,
        w_gate,
        w_up,
        w_down,
        cotangent,
    )


def norm_pull(grad_normed, normed, scale):
    return scale * (grad_normed - normed * jnp.mean(grad_normed * normed, axis=-1, keepdims=True))


def feed_forward_kernel(
    size,
    n_fsdp,
    attn,
    w_output,
    hidden,
    gains,
    w_gu_in,
    w_down_in,
    cot_in,
    out_hidden,
    grad_gain,
    grad_mid_out,
    grad_branch,
    gu_total_out,
    down_out,
    w_gu,
    w_down,
    cot,
    load_sems,
    mid,
    own,
    mlp_in,
    inner,
    grad_gu,
    gu_part,
    down_part,
    grad_mid,
    gu_total,
    down_total,
    layer_terms,
    *scratch,
):
    ring = Ring(size)
    ff = w_down.shape[0]
    gate_part, up_part = pl.ds(0, ff), pl.ds(ff, ff)
    up_links = Links(ring, n_fsdp, w_gu, up_part, *scratch[21:23])
    loads = [
        pltpu.make_async_copy(source, target, load_sems.at[which])
        for which, (source, target) in enumerate(
            (
                (w_gu_in.at[:, ring.row, :, up_part], w_gu.at[:, ring.row, :, up_part]),
                (w_gu_in.at[:, :, :, gate_part], w_gu.at[:, :, :, gate_part]),
                (w_down_in, w_down),
                (cot_in, cot),
            )
        )
    ]
    for load in loads:
        load.start()
    greet(near_devices(ring, n_fsdp))
    loads[0].wait()
    up_links.begin()
    half = own.shape[0] // 2
    out_sums, gather_sems_in = scratch[:5], scratch[5:7]
    layer_sums = (layer_terms,) + tuple(scratch[7:11])
    gather_sems_out, keep_sems = scratch[11:13], scratch[13]
    column_scratch = (scratch[14], None, gu_total, scratch[15], scratch[16])
    row_scratch = (scratch[17], None, scratch[18], scratch[19], scratch[20])

    first = SumRing(ring, row_terms(attn, w_output, out_sums[0]), *out_sums)
    first.begin()
    first.second()

    @pl.loop(2, size - 2)
    def _(step):
        first.step(step)

    up_links.relay()
    first.step(size - 2)
    first.last_terms()
    gathering = GatherRing(ring, own, mlp_in, *gather_sems_in)
    for way, part, place in first.parts():
        total = first.result(way, part) + hidden[place].astype(jnp.float32)
        mid[place] = total
        scale = lax.rsqrt(jnp.mean(total * total, axis=-1, keepdims=True) + EPS)
        own[place] = (total * scale * gains[1:2]).astype(jnp.bfloat16)
        gathering.start(way, part)
    first.finish()
    keep = pltpu.make_async_copy(own, mlp_in.at[ring.me], keep_sems.at[0])
    keep.start()
    for load in loads[1:]:
        load.wait()
    up_links.arrive()
    width = own.shape[1]

    def units(lines, members):
        cot_lines = jnp.concatenate([cot[members[way], way * half : (way + 1) * half] for way in range(2)], axis=0)

        @pl.loop(0, ff // UNITS)
        def _(tile):
            at = pl.multiple_of(tile * UNITS, UNITS)
            here, there = pl.ds(at, UNITS), pl.ds(pl.multiple_of(ff + at, UNITS), UNITS)
            gate = jnp.dot(lines, w_gu[:, :, :, here].reshape(width, UNITS), preferred_element_type=jnp.float32)
            up = jnp.dot(lines, w_gu[:, :, :, there].reshape(width, UNITS), preferred_element_type=jnp.float32)
            pulled = lax.dot_general(
                cot_lines, w_down[here, :], (((1,), (1,)), ((), ())), preferred_element_type=jnp.float32
            )
            sigmoid = 1.0 / (1.0 + jnp.exp(-gate))
            active = gate * sigmoid
            inner_new = (active * up).astype(jnp.bfloat16)
            gate_new = (pulled * up * sigmoid * (1.0 + gate * (1.0 - sigmoid))).astype(jnp.bfloat16)
            up_new = (pulled * active).astype(jnp.bfloat16)
            for way in range(2):
                place = slice(way * half, (way + 1) * half)
                inner[members[way], place, here] = inner_new[place]
                grad_gu[members[way], place, here] = gate_new[place]
                grad_gu[members[way], place, there] = up_new[place]

    def units_of(step):
        members = [ring.member(way, step) for way in range(2)]
        units(
            jnp.concatenate([mlp_in[members[way], way * half : (way + 1) * half] for way in range(2)], axis=0), members
        )

    units(own[...], [ring.me, ring.me])

    @pl.loop(1, size - 1)
    def _(step):
        gathering.step(step)
        units_of(step)

    third = SumRing(ring, row_terms_t(grad_gu, w_gu, out_sums[0]), *out_sums)
    third.begin()
    gathering.finish()
    keep.wait()
    units_of(size - 1)
    rows_all = size * 2 * half
    block = width // size

    def gu_tile(member):
        columns = pl.ds(pl.multiple_of(member * block, block), block)
        lines = mlp_in[:, :, columns].reshape(rows_all, block)

        @pl.loop(0, 2 * ff // TILE)
        def _(tile):
            there = pl.ds(pl.multiple_of(tile * TILE, TILE), TILE)
            product = lax.dot_general(
                lines,
                grad_gu[:, :, there].reshape(rows_all, TILE),
                (((0,), (0,)), ((), ())),
                preferred_element_type=jnp.float32,
            ).astype(jnp.bfloat16)
            for row in range(n_fsdp):
                gu_part[row, member, :, there] = product[row * (block // n_fsdp) : (row + 1) * (block // n_fsdp)]

    share = ff // n_fsdp

    def down_tile(tile):
        columns = pl.ds(pl.multiple_of(tile * UNITS, UNITS), UNITS)
        lines = cot[:, :, columns].reshape(rows_all, UNITS)
        product = lax.dot_general(
            inner[...].reshape(rows_all, ff), lines, (((0,), (0,)), ((), ())), preferred_element_type=jnp.float32
        ).astype(jnp.bfloat16)
        for row in range(n_fsdp):
            down_part[row, :, columns] = product[row * share : (row + 1) * share]

    gu_tile(0)
    third.second()
    gu_tile(1)

    @pl.loop(2, size - 1)
    def _(step):
        third.step(step)
        gu_tile(step)

    second = SumRing(ring, row_terms(inner, w_down, layer_sums[0]), *layer_sums)
    second.begin()
    gu_tile(size - 1)
    columns = RowGrads(ring, n_fsdp, gu_part, *column_scratch)
    rows = RowGrads(ring, n_fsdp, down_part, *row_scratch)
    columns.begin()
    third.last_terms()
    gathering = GatherRing(ring, own, grad_branch, *gather_sems_out)
    gain_sum = jnp.zeros_like(grad_gain)
    for way, part, place in third.parts():
        pulled = third.result(way, part)
        values = mid[place]
        scale = lax.rsqrt(jnp.mean(values * values, axis=-1, keepdims=True) + EPS)
        normed = values * scale
        gain_sum = gain_sum + jnp.sum(pulled * normed, axis=0, keepdims=True)
        total = cot[ring.me, place].astype(jnp.float32) + norm_pull(pulled * gains[1:2], normed, scale)
        grad_mid[place] = total
        own[place] = total.astype(jnp.bfloat16)
        gathering.start(way, part)
    grad_gain[...] = gain_sum
    keep = pltpu.make_async_copy(own, grad_branch.at[ring.me], keep_sems.at[1])
    keep.start()
    save_mid = pltpu.make_async_copy(grad_mid, grad_mid_out, keep_sems.at[2])
    save_mid.start()
    third.finish()
    second.second()
    gathering.step(1)
    columns.cross()

    @pl.loop(2, 4)
    def _(step):
        second.step(step)
        gathering.step(step)

        @pl.loop(0, width // UNITS // 2)
        def _(tile):
            down_tile((step - 2) * (width // UNITS // 2) + tile)

    rows.begin()
    second.step(4)
    gathering.step(4)
    rows.cross()

    @pl.loop(5, size - 1)
    def _(step):
        second.step(step)
        gathering.step(step)

    second.last_terms()
    down_total[...] = rows.result()
    save_down = pltpu.make_async_copy(down_total, down_out, keep_sems.at[3])
    save_down.start()
    gu_total[...] = columns.result().astype(jnp.bfloat16)
    save_gu = pltpu.make_async_copy(gu_total, gu_total_out, keep_sems.at[4])
    save_gu.start()
    for way, part, place in second.parts():
        out_hidden[place] = (mid[place] + second.result(way, part)).astype(jnp.bfloat16)
    gathering.finish()
    second.finish()
    columns.finish()
    rows.finish()
    up_links.finish()
    for copy in (keep, save_mid, save_down, save_gu):
        copy.wait()


UNITS = 256


def feed_forward(attn, w_output, hidden, gains, w_gu, w_down, cotangent):
    size, n_fsdp = lax.axis_size("ctx"), lax.axis_size("fsdp")
    rows, width = hidden.shape
    ff = w_down.shape[0]
    depth = width // size // n_fsdp
    sums = sum_scratch(size, rows, width)
    return pl.pallas_call(
        functools.partial(feed_forward_kernel, size, n_fsdp),
        out_shape=[
            jax.ShapeDtypeStruct((rows, width), jnp.bfloat16),
            jax.ShapeDtypeStruct((1, width), jnp.float32),
            jax.ShapeDtypeStruct((rows, width), jnp.float32),
            jax.ShapeDtypeStruct((size, rows, width), jnp.bfloat16),
            jax.ShapeDtypeStruct((size, depth, 2 * ff), jnp.bfloat16),
            jax.ShapeDtypeStruct((ff // n_fsdp, width), jnp.float32),
        ],
        in_specs=[VMEM_SPEC] * 4 + [ANY_SPEC] * 3,
        out_specs=[VMEM_SPEC] * 2 + [ANY_SPEC] * 4,
        scratch_shapes=[
            pltpu.VMEM(w_gu.shape, jnp.bfloat16),
            pltpu.VMEM(w_down.shape, jnp.bfloat16),
            pltpu.VMEM((size, rows, width), jnp.bfloat16),
            pltpu.SemaphoreType.DMA((4,)),
            pltpu.VMEM((rows, width), jnp.float32),
            pltpu.VMEM((rows, width), jnp.bfloat16),
            pltpu.VMEM((size, rows, width), jnp.bfloat16),
            pltpu.VMEM((size, rows, ff), jnp.bfloat16),
            pltpu.VMEM((size, rows, 2 * ff), jnp.bfloat16),
            pltpu.VMEM((n_fsdp, size, depth, 2 * ff), jnp.bfloat16),
            pltpu.VMEM((n_fsdp, ff // n_fsdp, width), jnp.bfloat16),
            pltpu.VMEM((rows, width), jnp.float32),
            pltpu.VMEM((size, depth, 2 * ff), jnp.bfloat16),
            pltpu.VMEM((ff // n_fsdp, width), jnp.float32),
            pltpu.VMEM((2, rows // 2, width), jnp.float32),
        ]
        + sums
        + gather_sems(size)
        + sums[1:]
        + gather_sems(size)
        + [pltpu.SemaphoreType.DMA((5,))]
        + [pltpu.VMEM((2, size, depth, 2 * ff), jnp.bfloat16)]
        + row_grads_sems()
        + [pltpu.VMEM((2, ff // n_fsdp, width), jnp.bfloat16), pltpu.VMEM((ff // n_fsdp, width), jnp.bfloat16)]
        + row_grads_sems()
        + links_sems(),
        compiler_params=params(5),
    )(
        attn,
        w_output,
        hidden,
        gains,
        w_gu,
        w_down,
        cotangent,
    )


def back_kernel(
    size,
    n_fsdp,
    all_blocks,
    starts,
    offsets,
    q_gain,
    k_gain,
    gains,
    post_sum,
    log_totals,
    *refs,
):
    sources, refs = refs[:11], refs[11:]
    gu_total = refs[0]
    grad_hidden, gains_out, output_out, gu_out, qkv_out = refs[1:6]
    targets, refs = refs[6:17], refs[17:]
    grad_branch, attn, w_output, queries, keys, values, raw, attn_in, w_qkv, hidden, grad_mid = targets
    load_sems, cosine, sine, places_ref, keys_t, grad_keys, grad_values, head_sums, grads, qkv_part, output_part = refs[:11]
    small, small_ctx, small_part, small_fsdp, small_send, small_recv, in_sum = refs[11:18]
    scratch = refs[18:]
    loads = [
        pltpu.make_async_copy(source, target, load_sems.at[which])
        for which, (source, target) in enumerate(zip(sources, targets))
    ]
    for load in loads:
        load.start()
    sums = scratch[:5]
    ring = Ring(size)
    greet(near_devices(ring, n_fsdp))
    total = scratch[8]
    columns = RowGrads(ring, n_fsdp, qkv_part, scratch[5], None, *scratch[6:8], scratch[9])
    dealing = Deal(ring, total, qkv_out, *scratch[10:12])
    rows = RowGrads(ring, n_fsdp, output_part, scratch[12], None, *scratch[13:16])
    gu_dealing = Deal(ring, gu_total, gu_out, *scratch[16:18])
    gu_dealing.begin()
    places = Places(ring, n_fsdp, all_blocks, starts, offsets, cosine, sine, places_ref)
    places.fill()
    head = q_gain.shape[1]
    q_heads = queries.shape[1]
    tokens = attn_in.shape[1]
    everyone = size * tokens
    width = attn_in.shape[2]
    q_width = q_heads * head
    grad_keys[...] = jnp.zeros_like(grad_keys)
    grad_values[...] = jnp.zeros_like(grad_values)
    head_sums[...] = jnp.zeros_like(head_sums)
    for load in loads[:3]:
        load.wait()

    def through_head(pulled, at, which, gain_here):
        turned = turn(pulled, cosine[at, :], -sine[at, :])
        values_raw = raw[at, which * head : (which + 1) * head]
        scale = head_norm(values_raw)
        unit = values_raw * scale
        kind = 0 if which < q_heads else 1
        head_sums[kind : kind + 1] = head_sums[kind : kind + 1] + jnp.sum(turned * unit, axis=0, keepdims=True)
        return norm_pull(turned * gain_here[...].astype(jnp.float32), unit, scale).astype(jnp.bfloat16)

    def output_tile(tile):
        there = pl.ds(pl.multiple_of(tile * TILE, TILE), TILE)
        product = lax.dot_general(
            attn[...].reshape(everyone, q_width),
            grad_branch[:, :, there].reshape(everyone, TILE),
            (((0,), (0,)), ((), ())),
            preferred_element_type=jnp.float32,
        ).astype(jnp.bfloat16)
        share = q_width // n_fsdp
        for row in range(n_fsdp):
            output_part[row, :, there] = product[row * share : (row + 1) * share]

    for load in loads[3:]:
        load.wait()
    keys_t[...] = keys[...].astype(jnp.float32).T.astype(jnp.bfloat16)

    @pl.loop(0, size)
    def _(member):
        at = pl.ds(pl.multiple_of(member * tokens, tokens), tokens)
        grad_attn = lax.dot_general(
            grad_branch[member], w_output[...], (((1,), (1,)), ((), ())), preferred_element_type=jnp.float32
        ).astype(jnp.bfloat16)
        heads = [slice(which * head, (which + 1) * head) for which in range(q_heads)]
        query = queries[member].reshape(q_heads * tokens, head)
        pulled = jnp.concatenate([grad_attn[:, lanes] for lanes in heads], axis=0)
        log_rows = jnp.concatenate([log_totals[member, which : which + 1, :] for which in range(q_heads)], axis=1)
        visible = jnp.concatenate([places.visible(member)] * q_heads, axis=1)
        scores = lax.dot_general(keys[...], query, (((1,), (1,)), ((), ())), preferred_element_type=jnp.float32)
        probs = jnp.where(visible, jnp.exp(scores - log_rows), 0.0)
        grad_probs = lax.dot_general(values[...], pulled, (((1,), (1,)), ((), ())), preferred_element_type=jnp.float32)
        delta = jnp.sum(probs * grad_probs, axis=0, keepdims=True)
        grad_scores = (probs * (grad_probs - delta)).astype(jnp.bfloat16)
        grad_keys[...] = grad_keys[...] + jnp.dot(grad_scores, query, preferred_element_type=jnp.float32)
        grad_values[...] = grad_values[...] + jnp.dot(
            probs.astype(jnp.bfloat16), pulled, preferred_element_type=jnp.float32
        )
        grad_query = jnp.dot(keys_t[...], grad_scores, preferred_element_type=jnp.float32)
        for which in range(q_heads):
            turned = grad_query[:, which * tokens : (which + 1) * tokens].T
            grads[member, :, heads[which]] = through_head(turned * head**-0.5, at, which, q_gain)

    @pl.loop(0, size)
    def _(member):
        at = pl.ds(pl.multiple_of(member * tokens, tokens), tokens)
        grads[member, :, q_width : q_width + head] = through_head(grad_keys[at, :], at, q_heads, k_gain)
        grads[member, :, q_width + head :] = grad_values[at, :].astype(jnp.bfloat16)

    block = width // size

    def qkv_tile(member):
        lines = attn_in[:, :, pl.ds(pl.multiple_of(member * block, block), block)].reshape(everyone, block)
        product = lax.dot_general(
            lines,
            grads[...].reshape(everyone, grads.shape[2]),
            (((0,), (0,)), ((), ())),
            preferred_element_type=jnp.float32,
        ).astype(jnp.bfloat16)
        for row in range(n_fsdp):
            qkv_part[row, member] = product[row * (block // n_fsdp) : (row + 1) * (block // n_fsdp)]

    in_sum[...] = jnp.zeros_like(in_sum)
    summing = SquareSum(Square(size), block_terms_t(grads, w_qkv, sums[0], attn_in, in_sum), *sums)
    summing.begin()

    @pl.loop(0, width // TILE)
    def _(tile):
        output_tile(tile)

    rows.begin()

    @pl.loop(0, size // 2)
    def _(member):
        qkv_tile(member)

    summing.first()

    @pl.loop(size // 2, size)
    def _(member):
        qkv_tile(member)

    columns.begin()
    chips = n_fsdp // 2
    for pair in range(size * chips):
        lanes = slice(pair * 128, (pair + 1) * 128)
        small[pair // chips, pair % chips, 0:1] = in_sum[:, lanes] / gains[0:1, lanes]
        small[pair // chips, pair % chips, 1:2] = post_sum[:, lanes]
        small[pair // chips, pair % chips, 2:4] = head_sums[0:2]
        small[pair // chips, pair % chips, 4:8] = jnp.zeros((4, 128), jnp.float32)
    sharing = SmallSum(ring, n_fsdp, small, small_ctx, small_part, small_fsdp, small_send, small_recv)
    sharing.begin()
    summing.second()
    columns.cross()
    summing.third()
    rows.cross()
    total[...] = columns.result().astype(jnp.bfloat16)
    dealing.begin()
    output_out[...] = rows.result()
    sharing.cross()
    for way, part, place in summing.parts():
        pulled = summing.result(way, part)
        values_in = hidden[place].astype(jnp.float32)
        scale = lax.rsqrt(jnp.mean(values_in * values_in, axis=-1, keepdims=True) + EPS)
        normed = values_in * scale
        grad_hidden[place] = grad_mid[place] + norm_pull(pulled * gains[0:1], normed, scale)
    gains_out[...] = sharing.result()
    sharing.finish()
    summing.finish()
    columns.finish()
    rows.finish()
    dealing.finish()
    gu_dealing.finish()


def back(
    all_small,
    tables,
    q_gain,
    k_gain,
    raw,
    queries,
    keys,
    values,
    attn,
    log_totals,
    hidden,
    grad_mid,
    gains,
    post_sum,
    gu_total,
    grad_branch,
    w_output,
    attn_in,
    w_qkv,
):
    size, n_fsdp = lax.axis_size("ctx"), lax.axis_size("fsdp")
    rows, width = hidden.shape
    head = q_gain.shape[0]
    everyone = size * rows
    share = w_qkv.shape[1]
    depth = width // size // n_fsdp
    q_width = attn.shape[2]
    f32, bf16 = jnp.float32, jnp.bfloat16
    loaded = [grad_branch, attn, w_output, queries, keys, values, raw, attn_in, w_qkv, hidden, grad_mid]
    return pl.pallas_call(
        functools.partial(back_kernel, size, n_fsdp),
        out_shape=[
            jax.ShapeDtypeStruct((rows, width), f32),
            jax.ShapeDtypeStruct((8, 128), f32),
            jax.ShapeDtypeStruct((q_width // n_fsdp, width), f32),
            jax.ShapeDtypeStruct(gu_total.shape, bf16),
            jax.ShapeDtypeStruct((size, depth, share), bf16),
        ],
        in_specs=[VMEM_SPEC] * 8 + [ANY_SPEC] * 12,
        out_specs=[VMEM_SPEC] * 3 + [ANY_SPEC] * 2,
        scratch_shapes=[pltpu.VMEM(array.shape, array.dtype) for array in loaded]
        + [
            pltpu.SemaphoreType.DMA((len(loaded),)),
            pltpu.VMEM((everyone, head), f32),
            pltpu.VMEM((everyone, head), f32),
            pltpu.VMEM((everyone, head), f32),
            pltpu.VMEM((head, everyone), bf16),
            pltpu.VMEM((everyone, head), f32),
            pltpu.VMEM((everyone, head), f32),
            pltpu.VMEM((8, head), f32),
            pltpu.VMEM((size, rows, share), bf16),
            pltpu.VMEM((n_fsdp, size, depth, share), bf16),
            pltpu.VMEM((n_fsdp, q_width // n_fsdp, width), bf16),
            pltpu.VMEM((size, n_fsdp // 2, 8, 128), f32),
            pltpu.VMEM((size, n_fsdp // 2, 8, 128), f32),
            pltpu.VMEM((n_fsdp // 2, 8, 128), f32),
            pltpu.VMEM((n_fsdp, 8, 128), f32),
        ]
        + small_sems(size, n_fsdp)
        + [pltpu.VMEM((1, width), f32)]
        + square_sum_scratch(rows, width)
        + [
            pltpu.VMEM((2, size, depth, share), bf16),
            pltpu.VMEM((size, depth, share), bf16),
            pltpu.SemaphoreType.DMA((3,)),
            pltpu.VMEM((size, depth, share), bf16),
            pltpu.SemaphoreType.DMA((3,)),
        ]
        + deal_sems(size)
        + [
            pltpu.VMEM((2, q_width // n_fsdp, width), bf16),
            pltpu.VMEM((q_width // n_fsdp, width), bf16),
        ]
        + row_grads_sems()
        + deal_sems(size),
        compiler_params=params(6),
    )(
        all_small,
        *tables,
        q_gain.reshape(1, head),
        k_gain.reshape(1, head),
        gains,
        post_sum,
        log_totals,
        *loaded,
        gu_total,
    )


def finish_kernel(size, gu, qkv, gain_sums, *refs):
    kept, outs, refs = refs[:4], refs[4:9], refs[9:]
    kept_out, gains_out, refs = refs[:4], refs[4:8], refs[8:]
    gu_in, qkv_in, load_sems, wide, save_sems, keep_sems, held = refs[0], refs[1], refs[2], refs[3:8], refs[8], refs[9], refs[10:]
    share = size // 2
    loads = []
    for part in range(2):
        members = pl.ds(part * share, share)
        loads.append(
            (
                pltpu.make_async_copy(gu.at[members], gu_in.at[members], load_sems.at[0, part]),
                pltpu.make_async_copy(qkv.at[members], qkv_in.at[members], load_sems.at[1, part]),
            )
        )
    for pair in loads:
        for load in pair:
            load.start()
    holds = [
        pltpu.make_async_copy(source, target, keep_sems.at[0, which])
        for which, (source, target) in enumerate(zip(kept, held))
    ]
    for hold in holds:
        hold.start()
    side = lax.rem(lax.axis_index("fsdp"), 2)
    depth = gains_out[0].shape[1]
    for row, out in enumerate(gains_out[:2]):
        out[...] = jnp.where(side == 0, gain_sums[row : row + 1, :depth], gain_sums[row : row + 1, depth:])
    for row, out in enumerate(gains_out[2:]):
        out[...] = gain_sums[2 + row : 3 + row]
    saves = []
    for part in range(2):
        for load in loads[part]:
            load.wait()
        which = 0
        for arrived, count in ((gu_in, 2), (qkv_in, 3)):
            start = 0
            for _ in range(count):
                width = wide[which].shape[1] // size
                for member in range(part * share, (part + 1) * share):
                    wide[which][:, member * width : (member + 1) * width] = arrived[
                        member, :, start : start + width
                    ].astype(jnp.float32)
                columns = pl.ds(part * share * width, share * width)
                save = pltpu.make_async_copy(
                    wide[which].at[:, columns], outs[which].at[:, columns], save_sems.at[which, part]
                )
                save.start()
                saves.append(save)
                start += width
                which += 1
    for which, hold in enumerate(holds):
        hold.wait()
        save = pltpu.make_async_copy(held[which], kept_out[which], keep_sems.at[1, which])
        save.start()
        saves.append(save)
    for save in saves:
        save.wait()


def finish(gu, qkv, kept, gain_sums, widths):
    size = lax.axis_size("ctx")
    depth = gu.shape[1]
    f32 = jnp.float32
    wide = [(depth, width) for width in widths]
    return pl.pallas_call(
        functools.partial(finish_kernel, size),
        out_shape=[jax.ShapeDtypeStruct(shape, f32) for shape in wide]
        + [jax.ShapeDtypeStruct(array.shape, array.dtype) for array in kept]
        + [jax.ShapeDtypeStruct((1, depth), f32)] * 2
        + [jax.ShapeDtypeStruct((1, 128), f32)] * 2,
        in_specs=[ANY_SPEC] * 2 + [VMEM_SPEC] + [ANY_SPEC] * len(kept),
        out_specs=[ANY_SPEC] * (len(wide) + len(kept)) + [VMEM_SPEC] * 4,
        scratch_shapes=[
            pltpu.VMEM(gu.shape, gu.dtype),
            pltpu.VMEM(qkv.shape, qkv.dtype),
            pltpu.SemaphoreType.DMA((2, 2)),
        ]
        + [pltpu.VMEM(shape, f32) for shape in wide]
        + [pltpu.SemaphoreType.DMA((len(wide), 2)), pltpu.SemaphoreType.DMA((2, len(kept)))]
        + [pltpu.VMEM(array.shape, array.dtype) for array in kept],
        compiler_params=pltpu.CompilerParams(vmem_limit_bytes=62 * 1024 * 1024),
    )(gu, qkv, gain_sums, *kept)


def tp_body(
    hidden_in,
    block_of,
    in_gain,
    w_query,
    w_key,
    w_value,
    w_output,
    q_gain,
    k_gain,
    post_gain,
    w_gate,
    w_up,
    w_down,
    cotangent,
):
    seq_count, tok_rows, model_width = hidden_in.shape
    n_ctx = lax.axis_size("ctx")
    block_rows = tok_rows // 2
    rows = seq_count * tok_rows
    head_dim = q_gain.shape[0]
    hidden = hidden_in.reshape(rows, model_width)
    cot_local = cotangent.reshape(rows, model_width)
    depth = w_query.shape[0]

    tables = rotation_tables(2 * n_ctx, block_rows, head_dim)
    (
        all_small,
        gains,
        log_totals,
        raw,
        queries,
        keys,
        values,
        attn,
        attn_in,
        mine_qkv,
        mine_output,
        mine_gu,
        mine_down,
        grad_out,
    ) = fore(
        block_of,
        in_gain,
        post_gain,
        tables,
        q_gain,
        k_gain,
        hidden,
        w_query,
        w_key,
        w_value,
        w_output,
        w_gate,
        w_up,
        w_down,
        cot_local,
    )
    mine_qkv = mine_qkv.reshape(model_width, -1)
    mine_output = mine_output.reshape(-1, model_width)
    output, post_sum, grad_mid, grad_branch, gu_total, part_down = feed_forward(
        attn, mine_output, hidden, gains, mine_gu, mine_down.reshape(-1, model_width), grad_out
    )
    grad_hidden, gain_sums, part_output, gu_sums, qkv_sums = back(
        all_small,
        tables,
        q_gain,
        k_gain,
        raw,
        queries,
        keys,
        values,
        attn,
        log_totals,
        hidden,
        grad_mid,
        gains,
        post_sum,
        gu_total,
        grad_branch,
        mine_output,
        attn_in,
        mine_qkv,
    )
    (
        part_gate,
        part_up,
        part_query,
        part_key,
        part_value,
        grad_hidden,
        output,
        part_down,
        part_output,
        part_in,
        part_post,
        sum_q_gain,
        sum_k_gain,
    ) = finish(
        gu_sums,
        qkv_sums,
        (grad_hidden, output, part_down, part_output),
        gain_sums,
        [weight.shape[1] for weight in (w_gate, w_up, w_query, w_key, w_value)],
    )
    return (
        output.reshape(seq_count, tok_rows, model_width),
        grad_hidden.reshape(seq_count, tok_rows, model_width),
        part_in.reshape(-1),
        part_query,
        part_key,
        part_value,
        part_output,
        sum_q_gain.reshape(-1),
        sum_k_gain.reshape(-1),
        part_post.reshape(-1),
        part_gate,
        part_up,
        part_down,
    )


def body(hidden_in, block_of, in_gain, w_query, w_key, w_value, w_output, q_gain, *rest):
    kv_heads = w_key.shape[1] // q_gain.shape[0]
    plan = tp_body if kv_heads == lax.axis_size("ctx") == 8 else gathered_weights_body
    return plan(hidden_in, block_of, in_gain, w_query, w_key, w_value, w_output, q_gain, *rest)


def solution(mesh):
    return jax.shard_map(
        body,
        mesh=mesh,
        in_specs=(
            P("fsdp", "ctx", None),
            P("fsdp", "ctx"),
            P(("ctx", "fsdp")),
            P(("ctx", "fsdp"), None),
            P(("ctx", "fsdp"), None),
            P(("ctx", "fsdp"), None),
            P(("ctx", "fsdp"), None),
            P(),
            P(),
            P(("ctx", "fsdp")),
            P(("ctx", "fsdp"), None),
            P(("ctx", "fsdp"), None),
            P(("ctx", "fsdp"), None),
            P("fsdp", "ctx", None),
        ),
        out_specs=(
            P("fsdp", "ctx", None),
            P("fsdp", "ctx", None),
            P(("ctx", "fsdp")),
            P(("ctx", "fsdp"), None),
            P(("ctx", "fsdp"), None),
            P(("ctx", "fsdp"), None),
            P(("ctx", "fsdp"), None),
            P(),
            P(),
            P(("ctx", "fsdp")),
            P(("ctx", "fsdp"), None),
            P(("ctx", "fsdp"), None),
            P(("ctx", "fsdp"), None),
        ),
        check_vma=False,
    )
```

```python
import functools
import math

import jax
import jax.numpy as jnp
import numpy as np
from jax import lax
from jax.experimental import pallas as pl
from jax.experimental.pallas import tpu as pltpu
from jax.sharding import PartitionSpec as P

EPS = 1e-06
THETA = 1000000.0


def rope_tables(positions, width):
    half_width = width // 2
    inverse = THETA ** (-(jnp.arange(half_width, dtype=jnp.float32) * 2.0 / width))
    angles = positions.astype(jnp.float32)[:, None] * inverse[None, :]
    return (jnp.cos(angles), jnp.sin(angles))


def rotate(values, cosine, sine):
    half_width = values.shape[-1] // 2
    first = values[..., :half_width]
    second = values[..., half_width:]
    cos_wide = cosine[:, None, :]
    sin_wide = sine[:, None, :]
    return jnp.concatenate(
        [first * cos_wide - second * sin_wide, second * cos_wide + first * sin_wide], axis=-1
    )


def norm_back(grad_normed, normed, scale):
    return scale * (grad_normed - normed * jnp.mean(grad_normed * normed, axis=-1, keepdims=True))


def gathered_weights_body(
    hidden_in,
    block_of,
    in_gain,
    w_query,
    w_key,
    w_value,
    w_output,
    q_gain,
    k_gain,
    post_gain,
    w_gate,
    w_up,
    w_down,
    cotangent,
):
    seq_count = hidden_in.shape[0]
    tok_rows = hidden_in.shape[1]
    flat_rows = seq_count * tok_rows
    model_width = hidden_in.shape[2]
    block_rows = tok_rows // 2
    block_total = 2 * lax.axis_size("ctx")
    seq_len = block_total * block_rows
    head_dim = q_gain.shape[0]
    q_heads = w_query.shape[1] // head_dim
    kv_heads = w_key.shape[1] // head_dim
    group_size = q_heads // kv_heads
    tile_blocks = math.gcd(block_total, max(1, 512 // block_rows))
    tile_rows = tile_blocks * block_rows
    q_scale = head_dim ** (-0.5)
    contract_rows = (((0,), (0,)), ((), ()))
    contract_cols = (((1,), (1,)), ((), ()))
    offsets = jnp.arange(block_rows, dtype=jnp.int32)
    positions = (block_of[:, :, None] * block_rows + offsets[None, None, :]).reshape(flat_rows)
    cosine, sine = rope_tables(positions, head_dim)
    residual = hidden_in.reshape(flat_rows, model_width).astype(jnp.float32)
    full_in_gain, full_query, full_key, full_value, full_output = (
        lax.all_gather(in_gain, ("ctx", "fsdp"), axis=0, tiled=True),
        lax.all_gather(w_query, ("ctx", "fsdp"), axis=0, tiled=True),
        lax.all_gather(w_key, ("ctx", "fsdp"), axis=0, tiled=True),
        lax.all_gather(w_value, ("ctx", "fsdp"), axis=0, tiled=True),
        lax.all_gather(w_output, ("ctx", "fsdp"), axis=0, tiled=True),
    )
    in_scale = lax.rsqrt(jnp.mean(residual * residual, axis=-1, keepdims=True) + EPS)
    in_normed = residual * in_scale
    attn_in = (in_normed * full_in_gain.astype(jnp.float32)).astype(jnp.bfloat16)
    q_raw = jnp.dot(attn_in, full_query, preferred_element_type=jnp.float32).reshape(
        flat_rows, q_heads, head_dim
    )
    k_raw = jnp.dot(attn_in, full_key, preferred_element_type=jnp.float32).reshape(
        flat_rows, kv_heads, head_dim
    )
    v_local = jnp.dot(attn_in, full_value, preferred_element_type=jnp.float32).astype(jnp.bfloat16)
    q_rms = lax.rsqrt(jnp.mean(q_raw * q_raw, axis=-1, keepdims=True) + EPS)
    q_unit = q_raw * q_rms
    queries = (rotate(q_unit * q_gain.astype(jnp.float32), cosine, sine) * q_scale).astype(
        jnp.bfloat16
    )
    k_rms = lax.rsqrt(jnp.mean(k_raw * k_raw, axis=-1, keepdims=True) + EPS)
    k_unit = k_raw * k_rms
    keys_local = rotate(k_unit * k_gain.astype(jnp.float32), cosine, sine).astype(jnp.bfloat16)
    all_keys, all_values, all_slots = (
        lax.all_gather(
            keys_local.reshape(seq_count, tok_rows, kv_heads * head_dim), "ctx", axis=1, tiled=True
        ),
        lax.all_gather(
            v_local.reshape(seq_count, tok_rows, kv_heads * head_dim), "ctx", axis=1, tiled=True
        ),
        lax.all_gather(block_of, "ctx", axis=1, tiled=True),
    )

    def tile_scores(query_tile, key_tile, query_pos, step):
        scores = jnp.einsum(
            "qhgd,khd->hgqk", query_tile, key_tile, preferred_element_type=jnp.float32
        )
        key_pos = step * tile_rows + jnp.arange(tile_rows, dtype=jnp.int32)
        visible = key_pos[None, :] <= query_pos[:, None]
        return (scores, visible)

    def sequence_tables(seq):
        key_blocks = all_keys[seq].reshape(block_total, block_rows, kv_heads, head_dim)
        value_blocks = all_values[seq].reshape(block_total, block_rows, kv_heads, head_dim)
        block_index = (
            jnp.zeros((block_total,), jnp.int32)
            .at[all_slots[seq]]
            .set(jnp.arange(block_total, dtype=jnp.int32))
        )
        return (key_blocks, value_blocks, block_index)

    def tile_index(block_index, step):
        return lax.dynamic_slice_in_dim(block_index, step * tile_blocks, tile_blocks)

    def fetch(table, block_index, step):
        return jnp.take(table, tile_index(block_index, step), axis=0).reshape(
            tile_rows, kv_heads, head_dim
        )

    log_totals = []
    attn_parts = []
    seq = 0
    key_blocks, value_blocks, block_index = sequence_tables(seq)
    for which in range(2):
        slot = 2 * seq + which
        query_tile = queries[slot * block_rows : (slot + 1) * block_rows].reshape(
            block_rows, kv_heads, group_size, head_dim
        )
        query_pos = positions[slot * block_rows : (slot + 1) * block_rows]
        tile_count = block_of[seq, which] // tile_blocks + 1

        def max_step(step, carry):
            running_max, running_sum = carry
            scores, visible = tile_scores(
                query_tile, fetch(key_blocks, block_index, step), query_pos, step
            )
            scores = jnp.where(visible, scores, -1e30)
            new_max = jnp.maximum(running_max, jnp.max(scores, axis=-1))
            running_sum = running_sum * jnp.exp(running_max - new_max) + jnp.sum(
                jnp.exp(scores - new_max[..., None]), axis=-1
            )
            return (new_max, running_sum)

        start_max = jnp.full((kv_heads, group_size, block_rows), -1e30, jnp.float32)
        start_sum = jnp.zeros((kv_heads, group_size, block_rows), jnp.float32)
        running_max, running_sum = lax.fori_loop(0, tile_count, max_step, (start_max, start_sum))
        log_total = running_max + jnp.log(running_sum)

        def value_step(step, total):
            scores, visible = tile_scores(
                query_tile, fetch(key_blocks, block_index, step), query_pos, step
            )
            probs = jnp.where(visible, jnp.exp(scores - log_total[..., None]), 0.0)
            return total + jnp.einsum(
                "hgqk,khd->qhgd",
                probs.astype(jnp.bfloat16),
                fetch(value_blocks, block_index, step),
                preferred_element_type=jnp.float32,
            )

        attn_part = lax.fori_loop(
            0,
            tile_count,
            value_step,
            jnp.zeros((block_rows, kv_heads, group_size, head_dim), jnp.float32),
        )
        log_totals.append(log_total)
        attn_parts.append(attn_part)
    attn_full = jnp.concatenate(attn_parts, axis=0)
    attn_bf = attn_full.reshape(flat_rows, q_heads * head_dim).astype(jnp.bfloat16)
    branch = jnp.dot(attn_bf, full_output, preferred_element_type=jnp.float32)
    hidden_mid = residual + branch
    full_post, full_gate, full_up, full_down = (
        lax.all_gather(post_gain, ("ctx", "fsdp"), axis=0, tiled=True),
        lax.all_gather(w_gate, ("ctx", "fsdp"), axis=0, tiled=True),
        lax.all_gather(w_up, ("ctx", "fsdp"), axis=0, tiled=True),
        lax.all_gather(w_down, ("ctx", "fsdp"), axis=0, tiled=True),
    )
    post_scale = lax.rsqrt(jnp.mean(hidden_mid * hidden_mid, axis=-1, keepdims=True) + EPS)
    post_normed = hidden_mid * post_scale
    mlp_in = (post_normed * full_post.astype(jnp.float32)).astype(jnp.bfloat16)
    gate_pre = jnp.dot(mlp_in, full_gate, preferred_element_type=jnp.float32)
    up_pre = jnp.dot(mlp_in, full_up, preferred_element_type=jnp.float32)
    sigmoid_gate = jax.nn.sigmoid(gate_pre)
    activated = gate_pre * sigmoid_gate
    inner = (activated * up_pre).astype(jnp.bfloat16)
    mlp_out = jnp.dot(inner, full_down, preferred_element_type=jnp.float32)
    output = (hidden_mid + mlp_out).astype(jnp.bfloat16)
    full_post, full_gate, full_up, full_down = (
        lax.all_gather(post_gain, ("ctx", "fsdp"), axis=0, tiled=True),
        lax.all_gather(w_gate, ("ctx", "fsdp"), axis=0, tiled=True),
        lax.all_gather(w_up, ("ctx", "fsdp"), axis=0, tiled=True),
        lax.all_gather(w_down, ("ctx", "fsdp"), axis=0, tiled=True),
    )
    grad_out = cotangent.reshape(flat_rows, model_width)
    grad_down = lax.dot_general(inner, grad_out, contract_rows, preferred_element_type=jnp.float32)
    part_down = lax.psum_scatter(grad_down, ("ctx", "fsdp"), scatter_dimension=0, tiled=True)
    grad_inner = lax.dot_general(
        grad_out, full_down, contract_cols, preferred_element_type=jnp.float32
    )
    grad_gate_pre = (
        grad_inner * up_pre * sigmoid_gate * (1.0 + gate_pre * (1.0 - sigmoid_gate))
    ).astype(jnp.bfloat16)
    grad_up_pre = (grad_inner * activated).astype(jnp.bfloat16)
    grad_gate = lax.dot_general(
        mlp_in, grad_gate_pre, contract_rows, preferred_element_type=jnp.float32
    )
    grad_up = lax.dot_general(
        mlp_in, grad_up_pre, contract_rows, preferred_element_type=jnp.float32
    )
    grad_mlp_in = lax.dot_general(
        grad_gate_pre, full_gate, contract_cols, preferred_element_type=jnp.float32
    ) + lax.dot_general(grad_up_pre, full_up, contract_cols, preferred_element_type=jnp.float32)
    grad_post_gain = jnp.sum(grad_mlp_in * post_normed, axis=0)
    grad_mid = grad_out.astype(jnp.float32) + norm_back(
        grad_mlp_in * full_post.astype(jnp.float32), post_normed, post_scale
    )
    part_post, part_gate, part_up = (
        lax.psum_scatter(grad_post_gain, ("ctx", "fsdp"), scatter_dimension=0, tiled=True),
        lax.psum_scatter(grad_gate, ("ctx", "fsdp"), scatter_dimension=0, tiled=True),
        lax.psum_scatter(grad_up, ("ctx", "fsdp"), scatter_dimension=0, tiled=True),
    )
    full_in_gain, full_query, full_key, full_value, full_output = (
        lax.all_gather(in_gain, ("ctx", "fsdp"), axis=0, tiled=True),
        lax.all_gather(w_query, ("ctx", "fsdp"), axis=0, tiled=True),
        lax.all_gather(w_key, ("ctx", "fsdp"), axis=0, tiled=True),
        lax.all_gather(w_value, ("ctx", "fsdp"), axis=0, tiled=True),
        lax.all_gather(w_output, ("ctx", "fsdp"), axis=0, tiled=True),
    )
    grad_branch = grad_mid.astype(jnp.bfloat16)
    grad_output = lax.dot_general(
        attn_bf, grad_branch, contract_rows, preferred_element_type=jnp.float32
    )
    grad_attn = lax.dot_general(
        grad_branch, full_output, contract_cols, preferred_element_type=jnp.float32
    ).astype(jnp.bfloat16)
    grad_attn = grad_attn.reshape(flat_rows, kv_heads, group_size, head_dim)
    query_grads = []
    seq = 0
    key_blocks, value_blocks, block_index = sequence_tables(seq)
    key_grads = jnp.zeros((block_total, block_rows, kv_heads, head_dim), jnp.float32)
    value_grads = jnp.zeros((block_total, block_rows, kv_heads, head_dim), jnp.float32)
    for which in range(2):
        slot = 2 * seq + which
        query_tile = queries[slot * block_rows : (slot + 1) * block_rows].reshape(
            block_rows, kv_heads, group_size, head_dim
        )
        query_pos = positions[slot * block_rows : (slot + 1) * block_rows]
        grad_tile = grad_attn[slot * block_rows : (slot + 1) * block_rows]
        tile_count = block_of[seq, which] // tile_blocks + 1
        delta = jnp.einsum("qhgd,qhgd->hgq", grad_tile.astype(jnp.float32), attn_parts[slot])
        log_total = log_totals[slot]

        def grad_step(step, carry):
            grad_query, keys_acc, values_acc = carry
            key_tile = fetch(key_blocks, block_index, step)
            scores, visible = tile_scores(query_tile, key_tile, query_pos, step)
            probs = jnp.where(visible, jnp.exp(scores - log_total[..., None]), 0.0)
            grad_probs = jnp.einsum(
                "qhgd,khd->hgqk",
                grad_tile,
                fetch(value_blocks, block_index, step),
                preferred_element_type=jnp.float32,
            )
            grad_scores = (probs * (grad_probs - delta[..., None])).astype(jnp.bfloat16)
            grad_query = grad_query + jnp.einsum(
                "hgqk,khd->qhgd", grad_scores, key_tile, preferred_element_type=jnp.float32
            )
            key_part = jnp.einsum(
                "hgqk,qhgd->khd", grad_scores, query_tile, preferred_element_type=jnp.float32
            )
            value_part = jnp.einsum(
                "hgqk,qhgd->khd",
                probs.astype(jnp.bfloat16),
                grad_tile,
                preferred_element_type=jnp.float32,
            )
            places = tile_index(block_index, step)
            keys_acc = keys_acc.at[places].add(
                key_part.reshape(tile_blocks, block_rows, kv_heads, head_dim)
            )
            values_acc = values_acc.at[places].add(
                value_part.reshape(tile_blocks, block_rows, kv_heads, head_dim)
            )
            return (grad_query, keys_acc, values_acc)

        start_query = jnp.zeros((block_rows, kv_heads, group_size, head_dim), jnp.float32)
        grad_query, key_grads, value_grads = lax.fori_loop(
            0, tile_count, grad_step, (start_query, key_grads, value_grads)
        )
        query_grads.append(grad_query)
    key_grad_list = [key_grads.reshape(seq_len, kv_heads * head_dim)]
    value_grad_list = [value_grads.reshape(seq_len, kv_heads * head_dim)]
    grad_keys, grad_values = (
        lax.psum_scatter(
            jnp.stack(key_grad_list, axis=0).astype(jnp.bfloat16),
            "ctx",
            scatter_dimension=1,
            tiled=True,
        ).astype(jnp.float32),
        lax.psum_scatter(
            jnp.stack(value_grad_list, axis=0).astype(jnp.bfloat16),
            "ctx",
            scatter_dimension=1,
            tiled=True,
        ).astype(jnp.float32),
    )
    grad_q_rot = (
        jnp.concatenate(query_grads, axis=0).reshape(flat_rows, q_heads, head_dim) * q_scale
    )
    grad_q_normed = rotate(grad_q_rot, cosine, -sine)
    grad_q_gain = jnp.sum(grad_q_normed * q_unit, axis=(0, 1))
    grad_q_raw = (
        norm_back(grad_q_normed * q_gain.astype(jnp.float32), q_unit, q_rms)
        .astype(jnp.bfloat16)
        .reshape(flat_rows, q_heads * head_dim)
    )
    grad_k_normed = rotate(grad_keys.reshape(flat_rows, kv_heads, head_dim), cosine, -sine)
    grad_k_gain = jnp.sum(grad_k_normed * k_unit, axis=(0, 1))
    grad_k_raw = (
        norm_back(grad_k_normed * k_gain.astype(jnp.float32), k_unit, k_rms)
        .astype(jnp.bfloat16)
        .reshape(flat_rows, kv_heads * head_dim)
    )
    grad_v_local = grad_values.reshape(flat_rows, kv_heads * head_dim).astype(jnp.bfloat16)
    grad_query_w = lax.dot_general(
        attn_in, grad_q_raw, contract_rows, preferred_element_type=jnp.float32
    )
    grad_key_w = lax.dot_general(
        attn_in, grad_k_raw, contract_rows, preferred_element_type=jnp.float32
    )
    grad_value_w = lax.dot_general(
        attn_in, grad_v_local, contract_rows, preferred_element_type=jnp.float32
    )
    grad_attn_in = lax.dot_general(
        grad_q_raw, full_query, contract_cols, preferred_element_type=jnp.float32
    )
    grad_attn_in = grad_attn_in + lax.dot_general(
        grad_k_raw, full_key, contract_cols, preferred_element_type=jnp.float32
    )
    grad_attn_in = grad_attn_in + lax.dot_general(
        grad_v_local, full_value, contract_cols, preferred_element_type=jnp.float32
    )
    grad_in_gain = jnp.sum(grad_attn_in * in_normed, axis=0)
    grad_input = grad_mid + norm_back(
        grad_attn_in * full_in_gain.astype(jnp.float32), in_normed, in_scale
    )
    part_in, part_query, part_key, part_value, part_output = (
        lax.psum_scatter(grad_in_gain, ("ctx", "fsdp"), scatter_dimension=0, tiled=True),
        lax.psum_scatter(grad_query_w, ("ctx", "fsdp"), scatter_dimension=0, tiled=True),
        lax.psum_scatter(grad_key_w, ("ctx", "fsdp"), scatter_dimension=0, tiled=True),
        lax.psum_scatter(grad_value_w, ("ctx", "fsdp"), scatter_dimension=0, tiled=True),
        lax.psum_scatter(grad_output, ("ctx", "fsdp"), scatter_dimension=0, tiled=True),
    )
    sum_q_gain, sum_k_gain = lax.psum((grad_q_gain, grad_k_gain), ("ctx", "fsdp"))
    return (
        output.reshape(seq_count, tok_rows, model_width),
        grad_input.reshape(seq_count, tok_rows, model_width),
        part_in,
        part_query,
        part_key,
        part_value,
        part_output,
        sum_q_gain,
        sum_k_gain,
        part_post,
        part_gate,
        part_up,
        part_down,
    )


MESH = pl.DeviceIdType.MESH
SUBS = 2


def ring_position(index, size):
    column, line = lax.rem(index, 2), lax.div(index, 2)
    return column * (line + 1) + (1 - column) * lax.rem(size - line, size)


def ring_member(position, size):
    late = lax.div(position + size // 2 - 1, size)
    beyond = lax.div(position + size - 1, size)
    return beyond * (1 - late) * (2 * position - 1) + late * 2 * (size - position)


class Ring:
    def __init__(self, size):
        self.size = size
        self.me = lax.axis_index("ctx")
        self.row = lax.axis_index("fsdp")
        self.position = ring_position(self.me, size)

    def member(self, way, steps):
        ahead = self.size - steps if way == 0 else steps
        return ring_member(lax.rem(self.position + ahead, self.size), self.size)

    def target(self, way):
        return (self.member(way, self.size - 1), self.row)

    def barrier(self):
        barrier = pltpu.get_barrier_semaphore()
        for way in range(2):
            pl.semaphore_signal(barrier, inc=1, device_id=self.target(way), device_id_type=MESH)
        pl.semaphore_wait(barrier, 2)


class GatherRing:
    def __init__(self, ring, own, out, send_sems, recv_sems):
        self.ring, self.own, self.out, self.send_sems, self.recv_sems = ring, own, out, send_sems, recv_sems
        self.half = own.shape[0] // 2
        self.sub = self.half // SUBS

    def copy(self, way, step, part, first=False):
        place = pl.ds(way * self.half + part * self.sub, self.sub)
        owner = self.ring.me if first else self.ring.member(way, step)
        source = self.own.at[place] if first else self.out.at[owner, place]
        return pltpu.make_async_remote_copy(
            src_ref=source,
            dst_ref=self.out.at[owner, place],
            send_sem=self.send_sems.at[way, step, part],
            recv_sem=self.recv_sems.at[way, step, part],
            device_id=self.ring.target(way),
            device_id_type=MESH,
        )

    def start(self, way, part):
        self.copy(way, 0, part, first=True).start()

    def step(self, step):
        for part in range(SUBS):
            for way in range(2):
                self.copy(way, step - 1, part).wait_recv()
                self.copy(way, step, part).start()

    def finish(self):
        last = self.ring.size - 2
        for part in range(SUBS):
            for way in range(2):
                self.copy(way, last, part).wait_recv()

        @pl.loop(0, last + 1)
        def _(step):
            for part in range(SUBS):
                for way in range(2):
                    self.copy(way, step, part).wait_send()

    def run(self):
        for way in range(2):
            self.start(way)

        @pl.loop(1, self.ring.size - 1)
        def _(step):
            self.step(step)

        self.finish()


def gather_sems(size):
    return [pltpu.SemaphoreType.DMA((2, size - 1, SUBS)), pltpu.SemaphoreType.DMA((2, size - 1, SUBS))]


class SumRing:
    def __init__(self, ring, compute, terms, outgoing, incoming, send_sems, recv_sems):
        self.ring, self.compute, self.terms = ring, compute, terms
        self.outgoing, self.incoming, self.send_sems, self.recv_sems = outgoing, incoming, send_sems, recv_sems
        self.group = terms.shape[0]
        self.half = terms.shape[2]
        self.sub = self.half // SUBS

    def copy(self, way, step, part):
        place = pl.ds(part * self.sub, self.sub)
        return pltpu.make_async_remote_copy(
            src_ref=self.outgoing.at[way, lax.rem(step, 2), place],
            dst_ref=self.incoming.at[way, step, place],
            send_sem=self.send_sems.at[way, step, part],
            recv_sem=self.recv_sems.at[way, step, part],
            device_id=self.ring.target(way),
            device_id_type=MESH,
        )

    def terms_of(self, step):
        self.compute([[self.ring.member(way, step + 1 + after) for way in range(2)] for after in range(self.group)])

    def begin(self):
        self.terms_of(0)
        for part in range(SUBS):
            place = pl.ds(part * self.sub, self.sub)
            for way in range(2):
                self.outgoing[way, 0, place] = self.terms[0, way, place].astype(jnp.bfloat16)
                self.copy(way, 0, part).start()

    def second(self):
        self.step(1, fresh=True)

    def step(self, step, fresh=False):
        if self.group == 1:
            self.terms_of(step)
        elif not fresh:

            @pl.when(lax.rem(step, self.group) == 0)
            def _():
                self.terms_of(step)

        for part in range(SUBS):
            place = pl.ds(part * self.sub, self.sub)
            for way in range(2):
                self.copy(way, step - 1, part).wait_recv()
                total = self.terms[lax.rem(step, self.group), way, place] + self.incoming[way, step - 1, place].astype(jnp.float32)
                if not fresh:
                    self.copy(way, step - 2, part).wait_send()
                self.outgoing[way, lax.rem(step, 2), place] = total.astype(jnp.bfloat16)
                self.copy(way, step, part).start()

    def last_terms(self):
        if self.group == 1:
            self.terms_of(self.ring.size - 1)

    def result(self, way, part):
        last = self.ring.size - 2
        place = pl.ds(part * self.sub, self.sub)
        self.copy(way, last, part).wait_recv()
        return self.terms[self.group - 1, way, place] + self.incoming[way, last, place].astype(jnp.float32)

    def parts(self):
        for part in range(SUBS):
            for way in range(2):
                start = way * self.half + part * self.sub
                yield way, part, slice(start, start + self.sub)

    def finish(self):
        for step in (self.ring.size - 3, self.ring.size - 2):
            for part in range(SUBS):
                for way in range(2):
                    self.copy(way, step, part).wait_send()


def sum_scratch(size, rows, width):
    half = rows // 2
    return [
        pltpu.VMEM((2, 2, half, width), jnp.float32),
        pltpu.VMEM((2, 2, half, width), jnp.bfloat16),
        pltpu.VMEM((2, size - 1, half, width), jnp.bfloat16),
        pltpu.SemaphoreType.DMA((2, size - 1, SUBS)),
        pltpu.SemaphoreType.DMA((2, size - 1, SUBS)),
    ]


class Square:
    def __init__(self, size):
        self.size = size
        self.me = lax.axis_index("ctx")
        self.row = lax.axis_index("fsdp")
        line, column = lax.div(self.me, 2), lax.rem(self.me, 2)
        half = lax.div(line, 2)
        self.inner = lax.rem(lax.div(line + 1, 2), 2) == 1
        self.outer = lax.rem(lax.div(line + 1, 2), 2) == 0
        self.beside = self.me + 1 - 2 * column
        self.along = self.me + 2 - 4 * lax.rem(line, 2)
        self.across = (3 - line) * 2 + column
        self.diagonal = self.along + 1 - 2 * column
        self.near = (2 - half) * 2 + column
        self.far = 6 * (1 - half) + column
        self.beside_near = (2 - half) * 2 + 1 - column
        self.beside_far = 6 * (1 - half) + 1 - column

    def targets(self):
        return [(member, self.row) for member in (self.beside, self.along, self.across)]


LED, KEPT = range(SUBS // 2), range(SUBS // 2, SUBS)


class SquareGather:
    def __init__(self, square, own, out, send_sems, recv_sems):
        self.square, self.own, self.out, self.send_sems, self.recv_sems = square, own, out, send_sems, recv_sems
        self.half = own.shape[0] // 2
        self.sub = self.half // SUBS
        me, rest = square.me, [(square.near, 0), (square.near, 1), (square.far, 0), (square.far, 1)]
        self.sent = [
            [(me, 0), (me, 1), (square.along, 1)] + rest + [(square.along, 0)],
            [(me, 0), (me, 1), (square.beside, 0)] + rest,
            [(me, 0), (me, 1), (square.along, 0), (square.along, 1)],
        ]

    def copy(self, link, slot, part):
        member, half = self.sent[link][slot]
        place = pl.ds(half * self.half + part * self.sub, self.sub)
        source = self.own.at[place] if slot < 2 else self.out.at[member, place]
        return remote(
            source,
            self.out.at[member, place],
            self.send_sems.at[link, slot, part],
            self.recv_sems.at[link, slot, part],
            self.square.targets()[link],
        )

    def start(self, half, part):
        for link in range(2):
            self.copy(link, half, part).start()

        @pl.when(self.square.inner)
        def _():
            self.copy(2, half, part).start()

    def relay(self, link, slot, *onward, parts=range(SUBS)):
        for part in parts:
            self.copy(link, slot, part).wait_recv()
            for next_link, next_slot in onward:
                self.copy(next_link, next_slot, part).start()

    def first(self):
        @pl.when(self.square.outer)
        def _():
            self.relay(0, 0, (1, 2))
            self.relay(1, 1, (0, 2))
            self.relay(1, 0, (0, 7), parts=LED)
            self.relay(1, 0, parts=KEPT)

        @pl.when(self.square.inner)
        def _():
            self.relay(1, 0, (2, 2))
            self.relay(2, 0, (1, 3))
            self.relay(1, 1, (2, 3), (0, 2))
            for part in range(SUBS):
                self.copy(0, 3, part).start()

    def second(self):
        @pl.when(self.square.outer)
        def _():
            self.relay(1, 3, (0, 3))
            self.relay(1, 4, (0, 4))

        @pl.when(self.square.inner)
        def _():
            self.relay(2, 1, (1, 4), (0, 4))

    def third(self):
        @pl.when(self.square.outer)
        def _():
            self.relay(1, 5, (0, 5))
            self.relay(1, 6, (0, 6))

        @pl.when(self.square.inner)
        def _():
            self.relay(2, 2, (1, 5), (0, 5))
            self.relay(2, 3, (1, 6), (0, 6))
            self.relay(0, 0, parts=LED)
            self.relay(0, 0, (1, 2), parts=KEPT)

    def finish(self):
        for slot in range(1, 7):
            self.relay(0, slot)
        self.relay(1, 2, parts=KEPT)
        for part in range(SUBS):
            for slot in range(7):
                self.copy(0, slot, part).wait_send()
            for slot in range(2):
                self.copy(1, slot, part).wait_send()
        for part in KEPT:
            self.copy(1, 2, part).wait_send()

        @pl.when(self.square.outer)
        def _():
            self.relay(0, 7, parts=LED)
            for part in LED:
                self.copy(0, 7, part).wait_send()
                self.copy(1, 2, part).wait_send()

        @pl.when(self.square.inner)
        def _():
            self.relay(1, 2, parts=LED)
            for part in range(SUBS):
                for slot in range(3, 7):
                    self.copy(1, slot, part).wait_send()
                for slot in range(4):
                    self.copy(2, slot, part).wait_send()


def square_sems():
    return [pltpu.SemaphoreType.DMA((3, 8, SUBS)), pltpu.SemaphoreType.DMA((3, 8, SUBS))]


class SquareSum:
    def __init__(self, square, compute, terms, outgoing, incoming, send_sems, recv_sems):
        self.square, self.compute, self.terms = square, compute, terms
        self.outgoing, self.incoming, self.send_sems, self.recv_sems = outgoing, incoming, send_sems, recv_sems
        self.half = outgoing.shape[1]
        self.sub = self.half // SUBS
        self.first_slot = (0, 8, 15)

    def copy(self, link, slot, part):
        at = self.first_slot[link] + slot
        place = pl.ds(part * self.sub, self.sub)
        return remote(
            self.outgoing.at[at, place],
            self.incoming.at[at, place],
            self.send_sems.at[link, slot, part],
            self.recv_sems.at[link, slot, part],
            self.square.targets()[link],
        )

    def arrived(self, link, slot, part):
        self.copy(link, slot, part).wait_recv()
        at = self.first_slot[link] + slot
        return self.incoming[at, part * self.sub : (part + 1) * self.sub].astype(jnp.float32)

    def term(self, which, half, part):
        start = half * self.half + part * self.sub
        return self.terms[which, start : start + self.sub]

    def send(self, link, slot, which, half, *received, parts=range(SUBS)):
        at = self.first_slot[link] + slot
        for part in parts:
            total = self.term(which, half, part)
            for source in received:
                total = total + self.arrived(*source, part)
            self.outgoing[at, part * self.sub : (part + 1) * self.sub] = total.astype(jnp.bfloat16)
            self.copy(link, slot, part).start()

    def begin(self):
        square = self.square
        self.compute(square.beside_far, 0)
        self.send(0, 0, 0, 0)
        self.send(0, 1, 0, 1)
        self.compute(square.beside_near, 1)
        self.send(0, 2, 1, 0)
        self.send(0, 3, 1, 1)
        self.compute(square.diagonal, 2)
        self.send(1, 0, 2, 0, parts=KEPT)

        @pl.when(square.outer)
        def _():
            self.send(0, 7, 2, 0, parts=LED)

        @pl.when(square.inner)
        def _():
            self.send(1, 0, 2, 0, parts=LED)

        self.send(0, 4, 2, 1)
        self.compute(square.far, 0)
        self.compute(square.near, 1)

    def first(self):
        @pl.when(self.square.outer)
        def _():
            self.send(1, 1, 0, 0, (0, 0))
            self.send(1, 2, 0, 1, (0, 1))

        @pl.when(self.square.inner)
        def _():
            self.send(2, 0, 0, 0, (0, 0), (1, 1))

        self.compute(self.square.beside, 3)
        self.send(0, 6, 3, 1)
        self.send(0, 5, 3, 0, (1, 0), parts=KEPT)

        @pl.when(self.square.outer)
        def _():
            self.send(0, 5, 3, 0, (1, 0), parts=LED)

        @pl.when(self.square.inner)
        def _():
            self.send(0, 5, 3, 0, parts=LED)

        self.compute(self.square.along, 2)
        self.compute(self.square.me, 4)

    def second(self):
        @pl.when(self.square.outer)
        def _():
            self.send(1, 3, 1, 0, (0, 2))
            self.send(1, 4, 1, 1, (0, 3))
            self.send(1, 5, 2, 0, (0, 7), parts=LED)
            self.send(1, 5, 2, 0, parts=KEPT)

        @pl.when(self.square.inner)
        def _():
            self.send(2, 1, 0, 1, (0, 1), (1, 2))
            self.send(1, 5, 2, 0, (2, 0))
            self.send(2, 2, 1, 0, (0, 2), (1, 3))

    def third(self):
        @pl.when(self.square.outer)
        def _():
            self.send(1, 6, 2, 1, (0, 4))

        @pl.when(self.square.inner)
        def _():
            self.send(2, 3, 1, 1, (0, 3), (1, 4))
            self.send(1, 6, 2, 1, (0, 4), (2, 1))
            for half in range(2):
                for part in range(SUBS):
                    start = half * self.half + part * self.sub
                    self.terms[4, start : start + self.sub] = self.term(4, half, part) + self.arrived(2, 2 + half, part)

    def parts(self):
        for half in range(2):
            for part in range(SUBS):
                start = half * self.half + part * self.sub
                yield half, part, slice(start, start + self.sub)

    def result(self, half, part):
        return self.term(4, half, part) + self.arrived(0, 5 + half, part) + self.arrived(1, 5 + half, part)

    def finish(self):
        for part in range(SUBS):
            for slot in range(7):
                self.copy(0, slot, part).wait_send()
            for slot in (5, 6):
                self.copy(1, slot, part).wait_send()
        for part in KEPT:
            self.copy(1, 0, part).wait_send()

        @pl.when(self.square.outer)
        def _():
            for part in LED:
                self.copy(0, 7, part).wait_send()
            for part in range(SUBS):
                for slot in range(1, 5):
                    self.copy(1, slot, part).wait_send()

        @pl.when(self.square.inner)
        def _():
            for part in LED:
                self.copy(1, 0, part).wait_send()
            for part in range(SUBS):
                for slot in range(4):
                    self.copy(2, slot, part).wait_send()


def square_sum_scratch(rows, width):
    return [
        pltpu.VMEM((5, rows, width), jnp.float32),
        pltpu.VMEM((19, rows // 2, width), jnp.bfloat16),
        pltpu.VMEM((19, rows // 2, width), jnp.bfloat16),
    ] + square_sems()


def block_terms_t(left, weight, terms, factors, product_sum):
    def compute(member, which):
        @pl.loop(0, weight.shape[0] // TILE)
        def _(tile):
            columns = pl.ds(pl.multiple_of(tile * TILE, TILE), TILE)
            terms[which, :, columns] = lax.dot_general(
                left[member], weight[columns, :], (((1,), (1,)), ((), ())), preferred_element_type=jnp.float32
            )
            product_sum[:, columns] = product_sum[:, columns] + jnp.sum(
                terms[which, :, columns] * factors[member, :, columns].astype(jnp.float32), axis=0, keepdims=True
            )

    return compute


TILE = 512


def step_lines(left, steps, half):
    return jnp.concatenate(
        [left[members[way], way * half : (way + 1) * half] for members in steps for way in range(2)], axis=0
    )


def keep_terms(terms, product, half, columns):
    for after in range(terms.shape[0]):
        for way in range(2):
            start = (2 * after + way) * half
            terms[after, way, :, columns] = product[start : start + half]


def row_terms(left, weight, terms):
    half = terms.shape[2]

    def compute(steps):
        lines = step_lines(left, steps, half)

        @pl.loop(0, weight.shape[1] // TILE)
        def _(tile):
            columns = pl.ds(pl.multiple_of(tile * TILE, TILE), TILE)
            product = jnp.dot(lines, weight[:, columns], preferred_element_type=jnp.float32)
            keep_terms(terms, product, half, columns)

    return compute


def row_terms_t(left, weight, terms):
    half = terms.shape[2]
    tile = terms.shape[3] // weight.shape[0]

    def compute(steps):
        lines = step_lines(left, steps, half)

        @pl.loop(0, weight.shape[0])
        def _(block):
            columns = pl.ds(pl.multiple_of(block * tile, tile), tile)
            product = lax.dot_general(
                lines,
                weight[block].reshape(tile, weight.shape[-1]),
                (((1,), (1,)), ((), ())),
                preferred_element_type=jnp.float32,
            )
            keep_terms(terms, product, half, columns)

    return compute


VMEM_SPEC = pl.BlockSpec(memory_space=pltpu.VMEM)
ANY_SPEC = pl.BlockSpec(memory_space=pl.ANY)


def ctx_peer(ring, ahead):
    return lax.rem(ring.me + ahead, ring.size)


def across(row, n_fsdp):
    return lax.rem(row + n_fsdp // 2, n_fsdp)


def beside(row):
    return row + 1 - 2 * lax.rem(row, 2)


def remote(source, target, send_sem, recv_sem, device):
    return pltpu.make_async_remote_copy(
        src_ref=source,
        dst_ref=target,
        send_sem=send_sem,
        recv_sem=recv_sem,
        device_id=device,
        device_id_type=MESH,
    )


def greet(devices):
    barrier = pltpu.get_barrier_semaphore()
    for device in devices:
        pl.semaphore_signal(barrier, inc=1, device_id=device, device_id_type=MESH)
    pl.semaphore_wait(barrier, len(devices))


def near_devices(ring, n_fsdp):
    return [(ctx_peer(ring, ahead), ring.row) for ahead in range(1, ring.size)] + [
        (ring.me, lax.rem(ring.row + ahead, n_fsdp)) for ahead in range(1, n_fsdp)
    ]


class Spread:
    def __init__(self, ring, n_fsdp, block, out, send_sems, recv_sems):
        self.ring, self.n_fsdp, self.block, self.out = ring, n_fsdp, block, out
        self.send_sems, self.recv_sems = send_sems, recv_sems

    def along_ctx(self, ahead):
        return remote(
            self.block,
            self.out.at[self.ring.row, self.ring.me],
            self.send_sems.at[ahead],
            self.recv_sems.at[ahead],
            (ctx_peer(self.ring, ahead), self.ring.row),
        )

    def along_fsdp(self, ahead):
        line = self.out.at[self.ring.row]
        sem = self.ring.size + ahead
        row = lax.rem(self.ring.row + ahead, self.n_fsdp)
        return remote(line, line, self.send_sems.at[sem], self.recv_sems.at[sem], (self.ring.me, row))

    def begin(self):
        for ahead in range(1, self.ring.size):
            self.along_ctx(ahead).start()
        self.out[self.ring.row, self.ring.me] = self.block[...]

    def collect(self):
        for ahead in range(1, self.ring.size):
            self.along_ctx(ahead).wait_recv()
        for ahead in range(1, self.n_fsdp):
            self.along_fsdp(ahead).start()
        for ahead in range(1, self.n_fsdp):
            self.along_fsdp(ahead).wait_recv()

    def finish(self):
        for ahead in range(1, self.ring.size):
            self.along_ctx(ahead).wait_send()
        for ahead in range(1, self.n_fsdp):
            self.along_fsdp(ahead).wait_send()


class SmallSum:
    def __init__(self, ring, n_fsdp, blocks, by_ctx, part, by_fsdp, send_sems, recv_sems):
        self.ring, self.n_fsdp, self.blocks, self.by_ctx, self.part, self.by_fsdp = (
            ring,
            n_fsdp,
            blocks,
            by_ctx,
            part,
            by_fsdp,
        )
        self.send_sems, self.recv_sems = send_sems, recv_sems

    def along_ctx(self, ahead):
        member = ctx_peer(self.ring, ahead)
        return remote(
            self.blocks.at[member],
            self.by_ctx.at[self.ring.me],
            self.send_sems.at[ahead],
            self.recv_sems.at[ahead],
            (member, self.ring.row),
        )

    def along_fsdp(self, ahead):
        row = lax.rem(self.ring.row + ahead, self.n_fsdp)
        sem = self.ring.size + ahead
        return remote(
            self.part.at[lax.div(row, 2)],
            self.by_fsdp.at[self.ring.row],
            self.send_sems.at[sem],
            self.recv_sems.at[sem],
            (self.ring.me, row),
        )

    def begin(self):
        for ahead in range(1, self.ring.size):
            self.along_ctx(ahead).start()
        self.by_ctx[self.ring.me] = self.blocks[self.ring.me]

    def cross(self):
        for ahead in range(1, self.ring.size):
            self.along_ctx(ahead).wait_recv()
        self.part[...] = jnp.sum(self.by_ctx[...], axis=0)
        for ahead in range(1, self.n_fsdp):
            self.along_fsdp(ahead).start()
        self.by_fsdp[self.ring.row] = self.part[lax.div(self.ring.row, 2)]

    def result(self):
        for ahead in range(1, self.n_fsdp):
            self.along_fsdp(ahead).wait_recv()
        return jnp.sum(self.by_fsdp[...], axis=0)

    def finish(self):
        for ahead in range(1, self.ring.size):
            self.along_ctx(ahead).wait_send()
        for ahead in range(1, self.n_fsdp):
            self.along_fsdp(ahead).wait_send()


def small_sems(size, n_fsdp):
    return [pltpu.SemaphoreType.DMA((size + n_fsdp,)), pltpu.SemaphoreType.DMA((size + n_fsdp,))]


class Rows:
    def __init__(self, ring, n_fsdp, shard, out, send_sems, recv_sems):
        own, far, twin = ring.row, across(ring.row, n_fsdp), beside(ring.row)
        self.keep = pltpu.make_async_copy(shard, out.at[own], send_sems.at[3])
        self.to_far = remote(shard, out.at[own], send_sems.at[0], recv_sems.at[0], (ring.me, far))
        self.to_twin = remote(shard, out.at[own], send_sems.at[1], recv_sems.at[1], (ring.me, twin))
        self.pass_on = remote(out.at[far], out.at[far], send_sems.at[2], recv_sems.at[2], (ring.me, twin))

    def begin(self):
        self.keep.start()
        self.to_far.start()
        self.to_twin.start()

    def relay(self):
        self.to_far.wait_recv()
        self.pass_on.start()

    def finish(self):
        self.keep.wait()
        self.to_far.wait_send()
        self.to_twin.wait()
        self.pass_on.wait()


def rows_sems():
    return [pltpu.SemaphoreType.DMA((4,)), pltpu.SemaphoreType.DMA((3,))]


class Links:
    def __init__(self, ring, n_fsdp, out, place, send_sems, recv_sems):
        self.ring, self.out, self.place, self.send_sems, self.recv_sems = ring, out, place, send_sems, recv_sems
        far, twin = across(ring.row, n_fsdp), beside(ring.row)
        self.to_far = self.link(0, ring.row, far)
        self.to_twin = self.link(1, ring.row, twin)
        self.pass_on = self.link(2, far, twin)

    def link(self, which, row, target):
        block = self.out.at[:, row, :, self.place]
        return remote(block, block, self.send_sems.at[which], self.recv_sems.at[which], (self.ring.me, target))

    def begin(self):
        self.to_far.start()
        self.to_twin.start()

    def relay(self):
        self.to_far.wait_recv()
        self.pass_on.start()

    def arrive(self):
        self.to_twin.wait_recv()
        self.pass_on.wait_recv()

    def finish(self):
        self.to_far.wait_send()
        self.to_twin.wait_send()
        self.pass_on.wait_send()


def links_sems():
    return [pltpu.SemaphoreType.DMA((3,)), pltpu.SemaphoreType.DMA((3,))]


class Pieces:
    def __init__(self, ring, shard, out, start, send_sems, recv_sems):
        self.ring, self.shard, self.out, self.send_sems, self.recv_sems = ring, shard, out, send_sems, recv_sems
        self.width = shard.shape[1] // ring.size
        self.place = pl.ds(start, self.width)

    def piece(self, ahead):
        member = ctx_peer(self.ring, ahead)
        source = self.shard.at[:, pl.ds(pl.multiple_of(member * self.width, self.width), self.width)]
        target = self.out.at[self.ring.me, self.ring.row, :, self.place]
        if ahead == 0:
            return pltpu.make_async_copy(source, target, self.send_sems.at[0])
        return remote(source, target, self.send_sems.at[ahead], self.recv_sems.at[ahead], (member, self.ring.row))

    def begin(self):
        for ahead in range(self.ring.size):
            self.piece(ahead).start()

    def arrive(self):
        self.piece(0).wait()
        for ahead in range(1, self.ring.size):
            self.piece(ahead).wait_recv()

    def finish(self):
        for ahead in range(1, self.ring.size):
            self.piece(ahead).wait_send()


class Columns:
    def __init__(self, ring, n_fsdp, shard, out, start, send_sems, recv_sems, link_send, link_recv):
        self.pieces = Pieces(ring, shard, out, start, send_sems, recv_sems)
        self.links = Links(ring, n_fsdp, out, self.pieces.place, link_send, link_recv)
        self.begin, self.relay, self.arrive = self.pieces.begin, self.links.relay, self.links.arrive

    def spread(self):
        self.pieces.arrive()
        self.links.begin()

    def finish(self):
        self.pieces.finish()
        self.links.finish()


def pieces_sems(size):
    return [pltpu.SemaphoreType.DMA((size,)), pltpu.SemaphoreType.DMA((size,))]


class RowGrads:
    def __init__(self, ring, n_fsdp, part, from_twin, to_far, from_far, send_sems, recv_sems):
        own, far, twin = ring.row, across(ring.row, n_fsdp), beside(ring.row)
        self.part, self.from_twin, self.to_far, self.from_far = part, from_twin, to_far, from_far
        self.own, self.far = own, far
        twin_far = across(twin, n_fsdp)
        self.first = [
            remote(part.at[twin], from_twin.at[0], send_sems.at[0], recv_sems.at[0], (ring.me, twin)),
            remote(part.at[twin_far], from_twin.at[1], send_sems.at[1], recv_sems.at[1], (ring.me, twin)),
        ]
        if to_far is None:
            self.to_far = part.at[far]
        self.second = remote(self.to_far, from_far, send_sems.at[2], recv_sems.at[2], (ring.me, far))

    def begin(self):
        self.first[1].start()
        self.first[0].start()

    def cross(self):
        self.first[1].wait_recv()
        self.to_far[...] = (
            self.part[self.far].astype(jnp.float32) + self.from_twin[1].astype(jnp.float32)
        ).astype(jnp.bfloat16)
        self.second.start()

    def result(self):
        self.first[0].wait_recv()
        self.second.wait_recv()
        return (
            self.part[self.own].astype(jnp.float32)
            + self.from_twin[0].astype(jnp.float32)
            + self.from_far[...].astype(jnp.float32)
        )

    def finish(self):
        for copy in self.first + [self.second]:
            copy.wait_send()


def row_grads_sems():
    return [pltpu.SemaphoreType.DMA((3,)), pltpu.SemaphoreType.DMA((3,))]


def row_grads_scratch(shape):
    return [
        pltpu.VMEM((2,) + shape, jnp.bfloat16),
        pltpu.VMEM(shape, jnp.bfloat16),
        pltpu.VMEM(shape, jnp.bfloat16),
    ] + row_grads_sems()


class Deal:
    def __init__(self, ring, total, arrived, send_sems, recv_sems):
        self.ring, self.total, self.arrived = ring, total, arrived
        self.send_sems, self.recv_sems = send_sems, recv_sems

    def piece(self, ahead):
        member = ctx_peer(self.ring, ahead)
        source, target = self.total.at[member], self.arrived.at[self.ring.me]
        if ahead == 0:
            return pltpu.make_async_copy(source, target, self.send_sems.at[0])
        return remote(source, target, self.send_sems.at[ahead], self.recv_sems.at[ahead], (member, self.ring.row))

    def begin(self):
        for ahead in range(self.ring.size):
            self.piece(ahead).start()

    def finish(self):
        for ahead in range(self.ring.size):
            self.piece(ahead).wait()


def deal_sems(size):
    return [pltpu.SemaphoreType.DMA((size,)), pltpu.SemaphoreType.DMA((size,))]


def params(collective_id):
    return pltpu.CompilerParams(
        collective_id=collective_id, has_side_effects=True, vmem_limit_bytes=63 * 1024 * 1024
    )


def head_norm(raw):
    return lax.rsqrt(jnp.mean(raw * raw, axis=-1, keepdims=True) + EPS)


def turn(values, cosine, sine):
    return values * cosine + pltpu.roll(values, values.shape[-1] // 2, 1) * sine


class Places:
    def __init__(self, ring, n_fsdp, all_small, starts, offsets, cosine, sine, places):
        self.ring, self.n_fsdp, self.all_small = ring, n_fsdp, all_small
        self.starts, self.offsets, self.cosine, self.sine, self.places = starts, offsets, cosine, sine, places
        self.block_rows = offsets.shape[1]

    def block(self, member, which):
        return self.all_small[self.ring.row, member, 2:3, which : which + 1]

    def fill(self):
        count = self.starts.shape[1]
        numbers = lax.broadcasted_iota(jnp.int32, (count, 1), 0).astype(jnp.float32)
        offset = lax.broadcasted_iota(jnp.int32, (self.block_rows, self.places.shape[1]), 0).astype(jnp.float32)
        for slot in range(count):
            block = self.block(slot // 2, slot % 2)
            chosen = (numbers == block).astype(jnp.float32)
            cos_start = jnp.sum(chosen * self.starts[0], axis=0, keepdims=True)
            sin_start = jnp.sum(chosen * self.starts[1], axis=0, keepdims=True)
            at = slice(slot * self.block_rows, (slot + 1) * self.block_rows)
            self.cosine[at] = cos_start * self.offsets[0] - sin_start * self.offsets[1]
            self.sine[at] = sin_start * self.offsets[0] + cos_start * self.offsets[1]
            self.places[at] = offset + block * self.block_rows

    def visible(self, member):
        width = self.places.shape[1]
        lane = lax.broadcasted_iota(jnp.int32, (1, width), 1).astype(jnp.float32)
        rows = float(self.block_rows)
        query = lane + jnp.where(lane < rows, self.block(member, 0) * rows, self.block(member, 1) * rows - rows)
        return self.places[...] <= query


def rotation_tables(blocks, block_rows, head):
    inverse = (THETA ** (-(np.arange(head // 2, dtype=np.float32) * np.float32(2.0) / head))).astype(np.float64)

    def both(at):
        angles = at.astype(np.float64)[:, None] * inverse[None, :]
        cosine, sine = np.cos(angles), np.sin(angles)
        return jnp.asarray(
            np.stack(
                [np.concatenate([cosine, cosine], axis=1), np.concatenate([-sine, sine], axis=1)], axis=0
            ).astype(np.float32)
        )

    return both(np.arange(blocks) * block_rows), both(np.arange(block_rows))


def fore_kernel(
    size,
    n_fsdp,
    q_heads,
    blocks,
    in_gain,
    post_gain,
    starts,
    offsets,
    q_gain,
    k_gain,
    hidden,
    w_query,
    w_key,
    w_value,
    w_output,
    w_gate,
    w_up,
    w_down,
    cotangent,
    all_small,
    gains,
    log_totals,
    raw_out,
    queries_out,
    keys_out,
    values_out,
    attn_out,
    attn_in_out,
    w_qkv_out,
    output_out,
    gu_out,
    down_out,
    grad_out,
    small,
    attn_in,
    w_qkv,
    cosine,
    sine,
    places_ref,
    values_t,
    raw,
    queries,
    keys,
    values,
    attn,
    small_send,
    small_recv,
    local_sems,
    *scratch,
):
    ring = Ring(size)
    head = q_gain.shape[1]
    tokens = hidden.shape[0]
    depth = in_gain.shape[1]
    q_width = q_heads * head
    k_width = w_key.shape[1] // size
    ff = w_gate.shape[1] // size
    columns_q = Columns(ring, n_fsdp, w_query, w_qkv, 0, *scratch[0:4])
    columns_k = Columns(ring, n_fsdp, w_key, w_qkv, q_width, *scratch[4:8])
    columns_v = Columns(ring, n_fsdp, w_value, w_qkv, q_width + k_width, *scratch[8:12])
    columns_gate = Columns(ring, n_fsdp, w_gate, gu_out, 0, *scratch[12:16])
    pieces_up = Pieces(ring, w_up, gu_out, ff, *scratch[16:18])
    rows_output = Rows(ring, n_fsdp, w_output, output_out, *scratch[18:20])
    rows_down = Rows(ring, n_fsdp, w_down, down_out, *scratch[20:22])
    square = Square(size)
    gathering = SquareGather(square, hidden, attn_in, *scratch[22:24])
    gathering_cot = SquareGather(square, cotangent, grad_out, *scratch[24:26])
    places = Places(ring, n_fsdp, all_small, starts, offsets, cosine, sine, places_ref)

    side = lax.rem(ring.row, 2)
    lane = lax.broadcasted_iota(jnp.int32, (1, 2 * depth), 1)
    mine = lax.div(lane, depth) == side
    small[...] = jnp.zeros_like(small)
    for row, part in enumerate((in_gain, post_gain)):
        part_row = part[...].astype(jnp.float32)
        small[row : row + 1] = jnp.where(mine, jnp.concatenate([part_row, part_row], axis=1), 0.0)
    small[2:3] = jnp.where(lane == 0, blocks[0, 0], jnp.where(lane == 1, blocks[0, 1], 0)).astype(jnp.float32)
    greet(near_devices(ring, n_fsdp))
    sharing = Spread(ring, n_fsdp, small, all_small, small_send, small_recv)
    sharing.begin()
    for part in range(SUBS):
        for way in range(2):
            gathering.start(way, part)
    for columns in (columns_q, columns_k, columns_v):
        columns.begin()
    keep = pltpu.make_async_copy(hidden, attn_in.at[ring.me], local_sems.at[0])
    keep.start()
    sharing.collect()
    rows_output.begin()
    rows_down.begin()
    for pair in range(size * n_fsdp // 2):
        member, chip = pair // (n_fsdp // 2), pair % (n_fsdp // 2)
        gains[:, pair * 128 : (pair + 1) * 128] = all_small[2 * chip, member] + all_small[2 * chip + 1, member]
    keep_cot = pltpu.make_async_copy(cotangent, grad_out.at[ring.me], local_sems.at[1])
    keep_cot.start()
    gathering.first()
    places.fill()
    gathering.second()
    for columns in (columns_q, columns_k, columns_v):
        columns.spread()
    gathering.third()
    rows_output.relay()
    for columns in (columns_q, columns_k, columns_v):
        columns.relay()
    columns_gate.begin()
    for part in range(SUBS):
        for way in range(2):
            gathering_cot.start(way, part)
    pieces_up.begin()
    for columns in (columns_q, columns_k, columns_v):
        columns.arrive()
    gathering.finish()
    keep.wait()
    save_qkv = pltpu.make_async_copy(w_qkv, w_qkv_out, local_sems.at[3])
    save_qkv.start()
    width = hidden.shape[1]

    @pl.loop(0, size)
    def _(member):
        at = pl.ds(pl.multiple_of(member * tokens, tokens), tokens)
        rows = attn_in[member].astype(jnp.float32)
        scale = lax.rsqrt(jnp.mean(rows * rows, axis=-1, keepdims=True) + EPS)
        attn_in[member] = (rows * scale * gains[0:1]).astype(jnp.bfloat16)
        product = jnp.dot(
            attn_in[member], w_qkv[...].reshape(width, w_qkv.shape[3]), preferred_element_type=jnp.float32
        )
        raw[at, :] = product[:, : q_width + head]
        for which in range(q_heads + 1):
            values_raw = product[:, which * head : (which + 1) * head]
            gain = q_gain if which < q_heads else k_gain
            turned = turn(values_raw * head_norm(values_raw) * gain[...].astype(jnp.float32), cosine[at, :], sine[at, :])
            if which < q_heads:
                queries[member, which] = (turned * head**-0.5).astype(jnp.bfloat16)
            else:
                keys[at, :] = turned.astype(jnp.bfloat16)
        fresh = product[:, q_width + head :]
        values[at, :] = fresh.astype(jnp.bfloat16)
        values_t[:, at] = fresh.T.astype(jnp.bfloat16)

    @pl.loop(0, size)
    def _(member):
        visible = places.visible(member)
        for which in range(q_heads):
            scores = lax.dot_general(
                keys[...], queries[member, which], (((1,), (1,)), ((), ())), preferred_element_type=jnp.float32
            )
            scores = jnp.where(visible, scores, -1e30)
            peak = jnp.max(scores, axis=0, keepdims=True)
            weights = jnp.exp(scores - peak)
            total = jnp.sum(weights, axis=0, keepdims=True)
            probs = (weights * (1.0 / total)).astype(jnp.bfloat16)
            mixed = jnp.dot(values_t[...], probs, preferred_element_type=jnp.float32)
            attn[member, :, which * head : (which + 1) * head] = mixed.T.astype(jnp.bfloat16)
            log_totals[member, which : which + 1, :] = peak + jnp.log(total)

    save_in = pltpu.make_async_copy(attn_in, attn_in_out, local_sems.at[2])
    save_in.start()
    saves = [
        pltpu.make_async_copy(source, target, local_sems.at[4 + which])
        for which, (source, target) in enumerate(
            ((raw, raw_out), (queries, queries_out), (keys, keys_out), (values, values_out), (attn, attn_out))
        )
    ]
    for save in saves:
        save.start()
    gathering_cot.first()
    rows_down.relay()
    columns_gate.spread()
    gathering_cot.second()
    gathering_cot.third()
    columns_gate.relay()
    gathering_cot.finish()
    sharing.finish()
    columns_gate.arrive()
    pieces_up.arrive()
    for columns in (columns_q, columns_k, columns_v, columns_gate, pieces_up):
        columns.finish()
    rows_output.finish()
    rows_down.finish()
    keep_cot.wait()
    for save in saves + [save_in, save_qkv]:
        save.wait()


def fore(blocks, in_gain, post_gain, tables, q_gain, k_gain, hidden, w_query, w_key, w_value, w_output, w_gate, w_up, w_down, cotangent):
    size, n_fsdp = lax.axis_size("ctx"), lax.axis_size("fsdp")
    rows, width = hidden.shape
    depth = w_query.shape[0]
    head = q_gain.shape[0]
    q_heads = w_query.shape[1] // size // head
    everyone = size * rows
    qkv_share = (w_query.shape[1] + w_key.shape[1] + w_value.shape[1]) // size
    gu_share = (w_gate.shape[1] + w_up.shape[1]) // size
    f32, bf16 = jnp.float32, jnp.bfloat16
    return pl.pallas_call(
        functools.partial(fore_kernel, size, n_fsdp, q_heads),
        out_shape=[
            jax.ShapeDtypeStruct((n_fsdp, size, 8, 2 * depth), f32),
            jax.ShapeDtypeStruct((8, width), f32),
            jax.ShapeDtypeStruct((size, q_heads, rows), f32),
            jax.ShapeDtypeStruct((everyone, (q_heads + 1) * head), f32),
            jax.ShapeDtypeStruct((size, q_heads, rows, head), bf16),
            jax.ShapeDtypeStruct((everyone, head), bf16),
            jax.ShapeDtypeStruct((everyone, head), bf16),
            jax.ShapeDtypeStruct((size, rows, q_heads * head), bf16),
            jax.ShapeDtypeStruct((size, rows, width), bf16),
            jax.ShapeDtypeStruct((size, n_fsdp, depth, qkv_share), bf16),
            jax.ShapeDtypeStruct((n_fsdp,) + w_output.shape, bf16),
            jax.ShapeDtypeStruct((size, n_fsdp, depth, gu_share), bf16),
            jax.ShapeDtypeStruct((n_fsdp,) + w_down.shape, bf16),
            jax.ShapeDtypeStruct((size, rows, width), bf16),
        ],
        in_specs=[pl.BlockSpec(memory_space=pltpu.SMEM)] + [VMEM_SPEC] * 7 + [ANY_SPEC] * 8,
        out_specs=[VMEM_SPEC] * 3 + [ANY_SPEC] * 11,
        scratch_shapes=[
            pltpu.VMEM((8, 2 * depth), f32),
            pltpu.VMEM((size, rows, width), bf16),
            pltpu.VMEM((size, n_fsdp, depth, qkv_share), bf16),
            pltpu.VMEM((everyone, head), f32),
            pltpu.VMEM((everyone, head), f32),
            pltpu.VMEM((everyone, head), f32),
            pltpu.VMEM((head, everyone), bf16),
            pltpu.VMEM((everyone, (q_heads + 1) * head), f32),
            pltpu.VMEM((size, q_heads, rows, head), bf16),
            pltpu.VMEM((everyone, head), bf16),
            pltpu.VMEM((everyone, head), bf16),
            pltpu.VMEM((size, rows, q_heads * head), bf16),
        ]
        + small_sems(size, n_fsdp)
        + [pltpu.SemaphoreType.DMA((9,))]
        + (pieces_sems(size) + links_sems()) * 4
        + pieces_sems(size)
        + rows_sems() * 2
        + square_sems() * 2,
        compiler_params=params(2),
    )(
        blocks,
        in_gain.reshape(1, depth),
        post_gain.reshape(1, depth),
        *tables,
        q_gain.reshape(1, head),
        k_gain.reshape(1, head),
        hidden,
        w_query,
        w_key,
        w_value,
        w_output,
        w_gate,
        w_up,
        w_down,
        cotangent,
    )


def norm_pull(grad_normed, normed, scale):
    return scale * (grad_normed - normed * jnp.mean(grad_normed * normed, axis=-1, keepdims=True))


def feed_forward_kernel(
    size,
    n_fsdp,
    attn,
    w_output,
    hidden,
    gains,
    w_gu_in,
    w_down_in,
    cot_in,
    out_hidden,
    grad_gain,
    grad_mid_out,
    grad_branch,
    gu_total_out,
    down_out,
    w_gu,
    w_down,
    cot,
    load_sems,
    mid,
    own,
    mlp_in,
    inner,
    grad_gu,
    gu_part,
    down_part,
    grad_mid,
    gu_total,
    down_total,
    layer_terms,
    *scratch,
):
    ring = Ring(size)
    ff = w_down.shape[0]
    gate_part, up_part = pl.ds(0, ff), pl.ds(ff, ff)
    up_links = Links(ring, n_fsdp, w_gu, up_part, *scratch[21:23])
    loads = [
        pltpu.make_async_copy(source, target, load_sems.at[which])
        for which, (source, target) in enumerate(
            (
                (w_gu_in.at[:, ring.row, :, up_part], w_gu.at[:, ring.row, :, up_part]),
                (w_gu_in.at[:, :, :, gate_part], w_gu.at[:, :, :, gate_part]),
                (w_down_in, w_down),
                (cot_in, cot),
            )
        )
    ]
    for load in loads:
        load.start()
    greet(near_devices(ring, n_fsdp))
    loads[0].wait()
    up_links.begin()
    half = own.shape[0] // 2
    out_sums, gather_sems_in = scratch[:5], scratch[5:7]
    layer_sums = (layer_terms,) + tuple(scratch[7:11])
    gather_sems_out, keep_sems = scratch[11:13], scratch[13]
    column_scratch = (scratch[14], None, gu_total, scratch[15], scratch[16])
    row_scratch = (scratch[17], None, scratch[18], scratch[19], scratch[20])

    first = SumRing(ring, row_terms(attn, w_output, out_sums[0]), *out_sums)
    first.begin()
    first.second()

    @pl.loop(2, size - 2)
    def _(step):
        first.step(step)

    up_links.relay()
    first.step(size - 2)
    gathering = GatherRing(ring, own, mlp_in, *gather_sems_in)
    for way, part, place in first.parts():
        total = first.result(way, part) + hidden[place].astype(jnp.float32)
        mid[place] = total
        scale = lax.rsqrt(jnp.mean(total * total, axis=-1, keepdims=True) + EPS)
        own[place] = (total * scale * gains[1:2]).astype(jnp.bfloat16)
        gathering.start(way, part)
    first.finish()
    keep = pltpu.make_async_copy(own, mlp_in.at[ring.me], keep_sems.at[0])
    keep.start()
    for load in loads[1:]:
        load.wait()
    up_links.arrive()
    width = own.shape[1]

    def units(lines, members):
        cot_lines = jnp.concatenate([cot[members[way], way * half : (way + 1) * half] for way in range(2)], axis=0)

        @pl.loop(0, ff // UNITS)
        def _(tile):
            at = pl.multiple_of(tile * UNITS, UNITS)
            here, there = pl.ds(at, UNITS), pl.ds(pl.multiple_of(ff + at, UNITS), UNITS)
            gate = jnp.dot(lines, w_gu[:, :, :, here].reshape(width, UNITS), preferred_element_type=jnp.float32)
            up = jnp.dot(lines, w_gu[:, :, :, there].reshape(width, UNITS), preferred_element_type=jnp.float32)
            pulled = lax.dot_general(
                cot_lines, w_down[here, :], (((1,), (1,)), ((), ())), preferred_element_type=jnp.float32
            )
            sigmoid = 1.0 / (1.0 + jnp.exp(-gate))
            active = gate * sigmoid
            inner_new = (active * up).astype(jnp.bfloat16)
            gate_new = (pulled * up * sigmoid * (1.0 + gate * (1.0 - sigmoid))).astype(jnp.bfloat16)
            up_new = (pulled * active).astype(jnp.bfloat16)
            for way in range(2):
                place = slice(way * half, (way + 1) * half)
                inner[members[way], place, here] = inner_new[place]
                grad_gu[members[way], place, here] = gate_new[place]
                grad_gu[members[way], place, there] = up_new[place]

    def units_of(step):
        members = [ring.member(way, step) for way in range(2)]
        units(
            jnp.concatenate([mlp_in[members[way], way * half : (way + 1) * half] for way in range(2)], axis=0), members
        )

    units(own[...], [ring.me, ring.me])

    @pl.loop(1, size - 1)
    def _(step):
        gathering.step(step)
        units_of(step)

    third = SumRing(ring, row_terms_t(grad_gu, w_gu, out_sums[0]), *out_sums)
    third.begin()
    gathering.finish()
    keep.wait()
    units_of(size - 1)
    rows_all = size * 2 * half
    block = width // size

    def gu_tile(member):
        columns = pl.ds(pl.multiple_of(member * block, block), block)
        lines = mlp_in[:, :, columns].reshape(rows_all, block)

        @pl.loop(0, 2 * ff // TILE)
        def _(tile):
            there = pl.ds(pl.multiple_of(tile * TILE, TILE), TILE)
            product = lax.dot_general(
                lines,
                grad_gu[:, :, there].reshape(rows_all, TILE),
                (((0,), (0,)), ((), ())),
                preferred_element_type=jnp.float32,
            ).astype(jnp.bfloat16)
            for row in range(n_fsdp):
                gu_part[row, member, :, there] = product[row * (block // n_fsdp) : (row + 1) * (block // n_fsdp)]

    share = ff // n_fsdp

    def down_tile(tile):
        columns = pl.ds(pl.multiple_of(tile * UNITS, UNITS), UNITS)
        lines = cot[:, :, columns].reshape(rows_all, UNITS)
        product = lax.dot_general(
            inner[...].reshape(rows_all, ff), lines, (((0,), (0,)), ((), ())), preferred_element_type=jnp.float32
        ).astype(jnp.bfloat16)
        for row in range(n_fsdp):
            down_part[row, :, columns] = product[row * share : (row + 1) * share]

    gu_tile(0)
    third.second()
    gu_tile(1)

    @pl.loop(2, size - 1)
    def _(step):
        third.step(step)
        gu_tile(step)

    second = SumRing(ring, row_terms(inner, w_down, layer_sums[0]), *layer_sums)
    second.begin()
    gu_tile(size - 1)
    columns = RowGrads(ring, n_fsdp, gu_part, *column_scratch)
    rows = RowGrads(ring, n_fsdp, down_part, *row_scratch)
    columns.begin()
    gathering = GatherRing(ring, own, grad_branch, *gather_sems_out)
    gain_sum = jnp.zeros_like(grad_gain)
    for way, part, place in third.parts():
        pulled = third.result(way, part)
        values = mid[place]
        scale = lax.rsqrt(jnp.mean(values * values, axis=-1, keepdims=True) + EPS)
        normed = values * scale
        gain_sum = gain_sum + jnp.sum(pulled * normed, axis=0, keepdims=True)
        total = cot[ring.me, place].astype(jnp.float32) + norm_pull(pulled * gains[1:2], normed, scale)
        grad_mid[place] = total
        own[place] = total.astype(jnp.bfloat16)
        gathering.start(way, part)
    grad_gain[...] = gain_sum
    keep = pltpu.make_async_copy(own, grad_branch.at[ring.me], keep_sems.at[1])
    keep.start()
    save_mid = pltpu.make_async_copy(grad_mid, grad_mid_out, keep_sems.at[2])
    save_mid.start()
    third.finish()
    second.second()
    gathering.step(1)
    columns.cross()

    @pl.loop(2, 4)
    def _(step):
        second.step(step)
        gathering.step(step)

        @pl.loop(0, width // UNITS // 2)
        def _(tile):
            down_tile((step - 2) * (width // UNITS // 2) + tile)

    rows.begin()
    second.step(4)
    gathering.step(4)
    rows.cross()

    @pl.loop(5, size - 1)
    def _(step):
        second.step(step)
        gathering.step(step)

    second.last_terms()
    down_total[...] = rows.result()
    save_down = pltpu.make_async_copy(down_total, down_out, keep_sems.at[3])
    save_down.start()
    gu_total[...] = columns.result().astype(jnp.bfloat16)
    save_gu = pltpu.make_async_copy(gu_total, gu_total_out, keep_sems.at[4])
    save_gu.start()
    for way, part, place in second.parts():
        out_hidden[place] = (mid[place] + second.result(way, part)).astype(jnp.bfloat16)
    gathering.finish()
    second.finish()
    columns.finish()
    rows.finish()
    up_links.finish()
    for copy in (keep, save_mid, save_down, save_gu):
        copy.wait()


UNITS = 256


def feed_forward(attn, w_output, hidden, gains, w_gu, w_down, cotangent):
    size, n_fsdp = lax.axis_size("ctx"), lax.axis_size("fsdp")
    rows, width = hidden.shape
    ff = w_down.shape[0]
    depth = width // size // n_fsdp
    sums = sum_scratch(size, rows, width)
    return pl.pallas_call(
        functools.partial(feed_forward_kernel, size, n_fsdp),
        out_shape=[
            jax.ShapeDtypeStruct((rows, width), jnp.bfloat16),
            jax.ShapeDtypeStruct((1, width), jnp.float32),
            jax.ShapeDtypeStruct((rows, width), jnp.float32),
            jax.ShapeDtypeStruct((size, rows, width), jnp.bfloat16),
            jax.ShapeDtypeStruct((size, depth, 2 * ff), jnp.bfloat16),
            jax.ShapeDtypeStruct((ff // n_fsdp, width), jnp.float32),
        ],
        in_specs=[VMEM_SPEC] * 4 + [ANY_SPEC] * 3,
        out_specs=[VMEM_SPEC] * 2 + [ANY_SPEC] * 4,
        scratch_shapes=[
            pltpu.VMEM(w_gu.shape, jnp.bfloat16),
            pltpu.VMEM(w_down.shape, jnp.bfloat16),
            pltpu.VMEM((size, rows, width), jnp.bfloat16),
            pltpu.SemaphoreType.DMA((4,)),
            pltpu.VMEM((rows, width), jnp.float32),
            pltpu.VMEM((rows, width), jnp.bfloat16),
            pltpu.VMEM((size, rows, width), jnp.bfloat16),
            pltpu.VMEM((size, rows, ff), jnp.bfloat16),
            pltpu.VMEM((size, rows, 2 * ff), jnp.bfloat16),
            pltpu.VMEM((n_fsdp, size, depth, 2 * ff), jnp.bfloat16),
            pltpu.VMEM((n_fsdp, ff // n_fsdp, width), jnp.bfloat16),
            pltpu.VMEM((rows, width), jnp.float32),
            pltpu.VMEM((size, depth, 2 * ff), jnp.bfloat16),
            pltpu.VMEM((ff // n_fsdp, width), jnp.float32),
            pltpu.VMEM((1, 2, rows // 2, width), jnp.float32),
        ]
        + sums
        + gather_sems(size)
        + sums[1:]
        + gather_sems(size)
        + [pltpu.SemaphoreType.DMA((5,))]
        + [pltpu.VMEM((2, size, depth, 2 * ff), jnp.bfloat16)]
        + row_grads_sems()
        + [pltpu.VMEM((2, ff // n_fsdp, width), jnp.bfloat16), pltpu.VMEM((ff // n_fsdp, width), jnp.bfloat16)]
        + row_grads_sems()
        + links_sems(),
        compiler_params=params(5),
    )(
        attn,
        w_output,
        hidden,
        gains,
        w_gu,
        w_down,
        cotangent,
    )


def back_kernel(
    size,
    n_fsdp,
    all_blocks,
    starts,
    offsets,
    q_gain,
    k_gain,
    gains,
    post_sum,
    log_totals,
    *refs,
):
    sources, refs = refs[:11], refs[11:]
    gu_total = refs[0]
    grad_hidden, gains_out, output_out, gu_out, qkv_out = refs[1:6]
    targets, refs = refs[6:17], refs[17:]
    grad_branch, attn, w_output, queries, keys, values, raw, attn_in, w_qkv, hidden, grad_mid = targets
    load_sems, cosine, sine, places_ref, keys_t, grad_keys, grad_values, head_sums, grads, qkv_part, output_part = refs[:11]
    small, small_ctx, small_part, small_fsdp, small_send, small_recv, in_sum = refs[11:18]
    scratch = refs[18:]
    loads = [
        pltpu.make_async_copy(source, target, load_sems.at[which])
        for which, (source, target) in enumerate(zip(sources, targets))
    ]
    for load in loads:
        load.start()
    sums = scratch[:5]
    ring = Ring(size)
    greet(near_devices(ring, n_fsdp))
    total = scratch[8]
    columns = RowGrads(ring, n_fsdp, qkv_part, scratch[5], None, *scratch[6:8], scratch[9])
    dealing = Deal(ring, total, qkv_out, *scratch[10:12])
    rows = RowGrads(ring, n_fsdp, output_part, scratch[12], None, *scratch[13:16])
    gu_dealing = Deal(ring, gu_total, gu_out, *scratch[16:18])
    gu_dealing.begin()
    places = Places(ring, n_fsdp, all_blocks, starts, offsets, cosine, sine, places_ref)
    places.fill()
    head = q_gain.shape[1]
    q_heads = queries.shape[1]
    tokens = attn_in.shape[1]
    everyone = size * tokens
    width = attn_in.shape[2]
    q_width = q_heads * head
    grad_keys[...] = jnp.zeros_like(grad_keys)
    grad_values[...] = jnp.zeros_like(grad_values)
    head_sums[...] = jnp.zeros_like(head_sums)
    for load in loads[:3]:
        load.wait()

    def through_head(pulled, at, which, gain_here):
        turned = turn(pulled, cosine[at, :], -sine[at, :])
        values_raw = raw[at, which * head : (which + 1) * head]
        scale = head_norm(values_raw)
        unit = values_raw * scale
        kind = 0 if which < q_heads else 1
        head_sums[kind : kind + 1] = head_sums[kind : kind + 1] + jnp.sum(turned * unit, axis=0, keepdims=True)
        return norm_pull(turned * gain_here[...].astype(jnp.float32), unit, scale).astype(jnp.bfloat16)

    def output_tile(tile):
        there = pl.ds(pl.multiple_of(tile * TILE, TILE), TILE)
        product = lax.dot_general(
            attn[...].reshape(everyone, q_width),
            grad_branch[:, :, there].reshape(everyone, TILE),
            (((0,), (0,)), ((), ())),
            preferred_element_type=jnp.float32,
        ).astype(jnp.bfloat16)
        share = q_width // n_fsdp
        for row in range(n_fsdp):
            output_part[row, :, there] = product[row * share : (row + 1) * share]

    for load in loads[3:]:
        load.wait()
    keys_t[...] = keys[...].astype(jnp.float32).T.astype(jnp.bfloat16)

    @pl.loop(0, size)
    def _(member):
        at = pl.ds(pl.multiple_of(member * tokens, tokens), tokens)
        grad_attn = lax.dot_general(
            grad_branch[member], w_output[...], (((1,), (1,)), ((), ())), preferred_element_type=jnp.float32
        ).astype(jnp.bfloat16)
        heads = [slice(which * head, (which + 1) * head) for which in range(q_heads)]
        query = queries[member].reshape(q_heads * tokens, head)
        pulled = jnp.concatenate([grad_attn[:, lanes] for lanes in heads], axis=0)
        log_rows = jnp.concatenate([log_totals[member, which : which + 1, :] for which in range(q_heads)], axis=1)
        visible = jnp.concatenate([places.visible(member)] * q_heads, axis=1)
        scores = lax.dot_general(keys[...], query, (((1,), (1,)), ((), ())), preferred_element_type=jnp.float32)
        probs = jnp.where(visible, jnp.exp(scores - log_rows), 0.0)
        grad_probs = lax.dot_general(values[...], pulled, (((1,), (1,)), ((), ())), preferred_element_type=jnp.float32)
        delta = jnp.sum(probs * grad_probs, axis=0, keepdims=True)
        grad_scores = (probs * (grad_probs - delta)).astype(jnp.bfloat16)
        grad_keys[...] = grad_keys[...] + jnp.dot(grad_scores, query, preferred_element_type=jnp.float32)
        grad_values[...] = grad_values[...] + jnp.dot(
            probs.astype(jnp.bfloat16), pulled, preferred_element_type=jnp.float32
        )
        grad_query = jnp.dot(keys_t[...], grad_scores, preferred_element_type=jnp.float32)
        for which in range(q_heads):
            turned = grad_query[:, which * tokens : (which + 1) * tokens].T
            grads[member, :, heads[which]] = through_head(turned * head**-0.5, at, which, q_gain)

    @pl.loop(0, size)
    def _(member):
        at = pl.ds(pl.multiple_of(member * tokens, tokens), tokens)
        grads[member, :, q_width : q_width + head] = through_head(grad_keys[at, :], at, q_heads, k_gain)
        grads[member, :, q_width + head :] = grad_values[at, :].astype(jnp.bfloat16)

    block = width // size

    def qkv_tile(member):
        lines = attn_in[:, :, pl.ds(pl.multiple_of(member * block, block), block)].reshape(everyone, block)
        product = lax.dot_general(
            lines,
            grads[...].reshape(everyone, grads.shape[2]),
            (((0,), (0,)), ((), ())),
            preferred_element_type=jnp.float32,
        ).astype(jnp.bfloat16)
        for row in range(n_fsdp):
            qkv_part[row, member] = product[row * (block // n_fsdp) : (row + 1) * (block // n_fsdp)]

    in_sum[...] = jnp.zeros_like(in_sum)
    summing = SquareSum(Square(size), block_terms_t(grads, w_qkv, sums[0], attn_in, in_sum), *sums)
    summing.begin()

    @pl.loop(0, width // TILE)
    def _(tile):
        output_tile(tile)

    rows.begin()

    @pl.loop(0, size // 2)
    def _(member):
        qkv_tile(member)

    summing.first()

    @pl.loop(size // 2, size)
    def _(member):
        qkv_tile(member)

    columns.begin()
    chips = n_fsdp // 2
    for pair in range(size * chips):
        lanes = slice(pair * 128, (pair + 1) * 128)
        small[pair // chips, pair % chips, 0:1] = in_sum[:, lanes] / gains[0:1, lanes]
        small[pair // chips, pair % chips, 1:2] = post_sum[:, lanes]
        small[pair // chips, pair % chips, 2:4] = head_sums[0:2]
        small[pair // chips, pair % chips, 4:8] = jnp.zeros((4, 128), jnp.float32)
    sharing = SmallSum(ring, n_fsdp, small, small_ctx, small_part, small_fsdp, small_send, small_recv)
    sharing.begin()
    summing.second()
    columns.cross()
    summing.third()
    rows.cross()
    total[...] = columns.result().astype(jnp.bfloat16)
    dealing.begin()
    output_out[...] = rows.result()
    sharing.cross()
    for way, part, place in summing.parts():
        pulled = summing.result(way, part)
        values_in = hidden[place].astype(jnp.float32)
        scale = lax.rsqrt(jnp.mean(values_in * values_in, axis=-1, keepdims=True) + EPS)
        normed = values_in * scale
        grad_hidden[place] = grad_mid[place] + norm_pull(pulled * gains[0:1], normed, scale)
    gains_out[...] = sharing.result()
    sharing.finish()
    summing.finish()
    columns.finish()
    rows.finish()
    dealing.finish()
    gu_dealing.finish()


def back(
    all_small,
    tables,
    q_gain,
    k_gain,
    raw,
    queries,
    keys,
    values,
    attn,
    log_totals,
    hidden,
    grad_mid,
    gains,
    post_sum,
    gu_total,
    grad_branch,
    w_output,
    attn_in,
    w_qkv,
):
    size, n_fsdp = lax.axis_size("ctx"), lax.axis_size("fsdp")
    rows, width = hidden.shape
    head = q_gain.shape[0]
    everyone = size * rows
    share = w_qkv.shape[1]
    depth = width // size // n_fsdp
    q_width = attn.shape[2]
    f32, bf16 = jnp.float32, jnp.bfloat16
    loaded = [grad_branch, attn, w_output, queries, keys, values, raw, attn_in, w_qkv, hidden, grad_mid]
    return pl.pallas_call(
        functools.partial(back_kernel, size, n_fsdp),
        out_shape=[
            jax.ShapeDtypeStruct((rows, width), f32),
            jax.ShapeDtypeStruct((8, 128), f32),
            jax.ShapeDtypeStruct((q_width // n_fsdp, width), f32),
            jax.ShapeDtypeStruct(gu_total.shape, bf16),
            jax.ShapeDtypeStruct((size, depth, share), bf16),
        ],
        in_specs=[VMEM_SPEC] * 8 + [ANY_SPEC] * 12,
        out_specs=[VMEM_SPEC] * 3 + [ANY_SPEC] * 2,
        scratch_shapes=[pltpu.VMEM(array.shape, array.dtype) for array in loaded]
        + [
            pltpu.SemaphoreType.DMA((len(loaded),)),
            pltpu.VMEM((everyone, head), f32),
            pltpu.VMEM((everyone, head), f32),
            pltpu.VMEM((everyone, head), f32),
            pltpu.VMEM((head, everyone), bf16),
            pltpu.VMEM((everyone, head), f32),
            pltpu.VMEM((everyone, head), f32),
            pltpu.VMEM((8, head), f32),
            pltpu.VMEM((size, rows, share), bf16),
            pltpu.VMEM((n_fsdp, size, depth, share), bf16),
            pltpu.VMEM((n_fsdp, q_width // n_fsdp, width), bf16),
            pltpu.VMEM((size, n_fsdp // 2, 8, 128), f32),
            pltpu.VMEM((size, n_fsdp // 2, 8, 128), f32),
            pltpu.VMEM((n_fsdp // 2, 8, 128), f32),
            pltpu.VMEM((n_fsdp, 8, 128), f32),
        ]
        + small_sems(size, n_fsdp)
        + [pltpu.VMEM((1, width), f32)]
        + square_sum_scratch(rows, width)
        + [
            pltpu.VMEM((2, size, depth, share), bf16),
            pltpu.VMEM((size, depth, share), bf16),
            pltpu.SemaphoreType.DMA((3,)),
            pltpu.VMEM((size, depth, share), bf16),
            pltpu.SemaphoreType.DMA((3,)),
        ]
        + deal_sems(size)
        + [
            pltpu.VMEM((2, q_width // n_fsdp, width), bf16),
            pltpu.VMEM((q_width // n_fsdp, width), bf16),
        ]
        + row_grads_sems()
        + deal_sems(size),
        compiler_params=params(6),
    )(
        all_small,
        *tables,
        q_gain.reshape(1, head),
        k_gain.reshape(1, head),
        gains,
        post_sum,
        log_totals,
        *loaded,
        gu_total,
    )


def finish_kernel(size, gu, qkv, gain_sums, *refs):
    kept, outs, refs = refs[:4], refs[4:9], refs[9:]
    kept_out, gains_out, refs = refs[:4], refs[4:8], refs[8:]
    gu_in, qkv_in, load_sems, wide, save_sems, keep_sems, held = refs[0], refs[1], refs[2], refs[3:8], refs[8], refs[9], refs[10:]
    share = size // 2
    loads = []
    for part in range(2):
        members = pl.ds(part * share, share)
        loads.append(
            (
                pltpu.make_async_copy(gu.at[members], gu_in.at[members], load_sems.at[0, part]),
                pltpu.make_async_copy(qkv.at[members], qkv_in.at[members], load_sems.at[1, part]),
            )
        )
    for pair in loads:
        for load in pair:
            load.start()
    holds = [
        pltpu.make_async_copy(source, target, keep_sems.at[0, which])
        for which, (source, target) in enumerate(zip(kept, held))
    ]
    for hold in holds:
        hold.start()
    side = lax.rem(lax.axis_index("fsdp"), 2)
    depth = gains_out[0].shape[1]
    for row, out in enumerate(gains_out[:2]):
        out[...] = jnp.where(side == 0, gain_sums[row : row + 1, :depth], gain_sums[row : row + 1, depth:])
    for row, out in enumerate(gains_out[2:]):
        out[...] = gain_sums[2 + row : 3 + row]
    saves = []
    for part in range(2):
        for load in loads[part]:
            load.wait()
        which = 0
        for arrived, count in ((gu_in, 2), (qkv_in, 3)):
            start = 0
            for _ in range(count):
                width = wide[which].shape[1] // size
                for member in range(part * share, (part + 1) * share):
                    wide[which][:, member * width : (member + 1) * width] = arrived[
                        member, :, start : start + width
                    ].astype(jnp.float32)
                columns = pl.ds(part * share * width, share * width)
                save = pltpu.make_async_copy(
                    wide[which].at[:, columns], outs[which].at[:, columns], save_sems.at[which, part]
                )
                save.start()
                saves.append(save)
                start += width
                which += 1
    for which, hold in enumerate(holds):
        hold.wait()
        save = pltpu.make_async_copy(held[which], kept_out[which], keep_sems.at[1, which])
        save.start()
        saves.append(save)
    for save in saves:
        save.wait()


def finish(gu, qkv, kept, gain_sums, widths):
    size = lax.axis_size("ctx")
    depth = gu.shape[1]
    f32 = jnp.float32
    wide = [(depth, width) for width in widths]
    return pl.pallas_call(
        functools.partial(finish_kernel, size),
        out_shape=[jax.ShapeDtypeStruct(shape, f32) for shape in wide]
        + [jax.ShapeDtypeStruct(array.shape, array.dtype) for array in kept]
        + [jax.ShapeDtypeStruct((1, depth), f32)] * 2
        + [jax.ShapeDtypeStruct((1, 128), f32)] * 2,
        in_specs=[ANY_SPEC] * 2 + [VMEM_SPEC] + [ANY_SPEC] * len(kept),
        out_specs=[ANY_SPEC] * (len(wide) + len(kept)) + [VMEM_SPEC] * 4,
        scratch_shapes=[
            pltpu.VMEM(gu.shape, gu.dtype),
            pltpu.VMEM(qkv.shape, qkv.dtype),
            pltpu.SemaphoreType.DMA((2, 2)),
        ]
        + [pltpu.VMEM(shape, f32) for shape in wide]
        + [pltpu.SemaphoreType.DMA((len(wide), 2)), pltpu.SemaphoreType.DMA((2, len(kept)))]
        + [pltpu.VMEM(array.shape, array.dtype) for array in kept],
        compiler_params=pltpu.CompilerParams(vmem_limit_bytes=62 * 1024 * 1024),
    )(gu, qkv, gain_sums, *kept)


def tp_body(
    hidden_in,
    block_of,
    in_gain,
    w_query,
    w_key,
    w_value,
    w_output,
    q_gain,
    k_gain,
    post_gain,
    w_gate,
    w_up,
    w_down,
    cotangent,
):
    seq_count, tok_rows, model_width = hidden_in.shape
    n_ctx = lax.axis_size("ctx")
    block_rows = tok_rows // 2
    rows = seq_count * tok_rows
    head_dim = q_gain.shape[0]
    hidden = hidden_in.reshape(rows, model_width)
    cot_local = cotangent.reshape(rows, model_width)
    depth = w_query.shape[0]

    tables = rotation_tables(2 * n_ctx, block_rows, head_dim)
    (
        all_small,
        gains,
        log_totals,
        raw,
        queries,
        keys,
        values,
        attn,
        attn_in,
        mine_qkv,
        mine_output,
        mine_gu,
        mine_down,
        grad_out,
    ) = fore(
        block_of,
        in_gain,
        post_gain,
        tables,
        q_gain,
        k_gain,
        hidden,
        w_query,
        w_key,
        w_value,
        w_output,
        w_gate,
        w_up,
        w_down,
        cot_local,
    )
    mine_qkv = mine_qkv.reshape(model_width, -1)
    mine_output = mine_output.reshape(-1, model_width)
    output, post_sum, grad_mid, grad_branch, gu_total, part_down = feed_forward(
        attn, mine_output, hidden, gains, mine_gu, mine_down.reshape(-1, model_width), grad_out
    )
    grad_hidden, gain_sums, part_output, gu_sums, qkv_sums = back(
        all_small,
        tables,
        q_gain,
        k_gain,
        raw,
        queries,
        keys,
        values,
        attn,
        log_totals,
        hidden,
        grad_mid,
        gains,
        post_sum,
        gu_total,
        grad_branch,
        mine_output,
        attn_in,
        mine_qkv,
    )
    (
        part_gate,
        part_up,
        part_query,
        part_key,
        part_value,
        grad_hidden,
        output,
        part_down,
        part_output,
        part_in,
        part_post,
        sum_q_gain,
        sum_k_gain,
    ) = finish(
        gu_sums,
        qkv_sums,
        (grad_hidden, output, part_down, part_output),
        gain_sums,
        [weight.shape[1] for weight in (w_gate, w_up, w_query, w_key, w_value)],
    )
    return (
        output.reshape(seq_count, tok_rows, model_width),
        grad_hidden.reshape(seq_count, tok_rows, model_width),
        part_in.reshape(-1),
        part_query,
        part_key,
        part_value,
        part_output,
        sum_q_gain.reshape(-1),
        sum_k_gain.reshape(-1),
        part_post.reshape(-1),
        part_gate,
        part_up,
        part_down,
    )


def body(hidden_in, block_of, in_gain, w_query, w_key, w_value, w_output, q_gain, *rest):
    kv_heads = w_key.shape[1] // q_gain.shape[0]
    plan = tp_body if kv_heads == lax.axis_size("ctx") == 8 else gathered_weights_body
    return plan(hidden_in, block_of, in_gain, w_query, w_key, w_value, w_output, q_gain, *rest)


def solution(mesh):
    return jax.shard_map(
        body,
        mesh=mesh,
        in_specs=(
            P("fsdp", "ctx", None),
            P("fsdp", "ctx"),
            P(("ctx", "fsdp")),
            P(("ctx", "fsdp"), None),
            P(("ctx", "fsdp"), None),
            P(("ctx", "fsdp"), None),
            P(("ctx", "fsdp"), None),
            P(),
            P(),
            P(("ctx", "fsdp")),
            P(("ctx", "fsdp"), None),
            P(("ctx", "fsdp"), None),
            P(("ctx", "fsdp"), None),
            P("fsdp", "ctx", None),
        ),
        out_specs=(
            P("fsdp", "ctx", None),
            P("fsdp", "ctx", None),
            P(("ctx", "fsdp")),
            P(("ctx", "fsdp"), None),
            P(("ctx", "fsdp"), None),
            P(("ctx", "fsdp"), None),
            P(("ctx", "fsdp"), None),
            P(),
            P(),
            P(("ctx", "fsdp")),
            P(("ctx", "fsdp"), None),
            P(("ctx", "fsdp"), None),
            P(("ctx", "fsdp"), None),
        ),
        check_vma=False,
    )
```
